32 devices in a mesh: dp: 4 (over x, core), fsdp: 8 (over z, y).
Axes of the slice: x: 2, y: 2, z: 4, core: 2. Of those that a mesh axis runs over, the one named last changes fastest.
Arguments:
- source_tokens: bfloat16 [32, 384, 512], P(('dp', 'fsdp')), may hold values from -6 to 6
- target_tokens: bfloat16 [32, 384, 512], P(('dp', 'fsdp')), may hold values from -6 to 6
- source_segments: int32 [32, 384], P(('dp', 'fsdp')), may hold values from 0 to 3, never falling along the last dimension, each value on 1 to 192 neighbouring positions
- target_segments: int32 [32, 384], P(('dp', 'fsdp')), may hold values from 0 to 3, never falling along the last dimension, each value on 1 to 192 neighbouring positions
- output_grad: bfloat16 [32, 384, 512], P(('dp', 'fsdp')), may hold values from -6 to 6
- attention_weight: float32 [12, 512, 512], P(None, ('dp', 'fsdp')), may hold values from -0.79549513 to 0.79549513
- up_weight: float32 [2, 512, 2048], P(None, ('dp', 'fsdp')), may hold values from -0.25 to 0.25
- down_weight: float32 [2, 2048, 512], P(None, ('dp', 'fsdp')), may hold values from -0.125 to 0.125
- vectors: float32 [21, 512], P(None, ('dp', 'fsdp')), may hold values from -0.5 to 1.3
- hidden_bias: float32 [2, 2048], P(None, ('dp', 'fsdp')), may hold values from -2.5 to 2.5
- attention_first: float32 [12, 512, 512], P(None, ('dp', 'fsdp')), may hold values from -36.580914 to 36.580914
- up_first: float32 [2, 512, 2048], P(None, ('dp', 'fsdp')), may hold values from -36.580914 to 36.580914
- down_first: float32 [2, 2048, 512], P(None, ('dp', 'fsdp')), may hold values from -36.580914 to 36.580914
- vectors_first: float32 [21, 512], P(None, ('dp', 'fsdp')), may hold values from -36.580914 to 36.580914
- hidden_first: float32 [2, 2048], P(None, ('dp', 'fsdp')), may hold values from -36.580914 to 36.580914
- attention_second: float32 [12, 512, 512], P(None, ('dp', 'fsdp')), may hold values from 3.072 to 12.288
- up_second: float32 [2, 512, 2048], P(None, ('dp', 'fsdp')), may hold values from 3.072 to 12.288
- down_second: float32 [2, 2048, 512], P(None, ('dp', 'fsdp')), may hold values from 3.072 to 12.288
- vectors_second: float32 [21, 512], P(None, ('dp', 'fsdp')), may hold values from 3.072 to 12.288
- hidden_second: float32 [2, 2048], P(None, ('dp', 'fsdp')), may hold values from 3.072 to 12.288
Outputs:
- encoder_out: float32 [32, 384, 512], P(('dp', 'fsdp'))
- decoder_out: float32 [32, 384, 512], P(('dp', 'fsdp'))
- source_grad: float32 [32, 384, 512], P(('dp', 'fsdp'))
- target_grad: float32 [32, 384, 512], P(('dp', 'fsdp'))
- attention_next: float32 [12, 512, 512], P(None, ('dp', 'fsdp'))
- up_next: float32 [2, 512, 2048], P(None, ('dp', 'fsdp'))
- down_next: float32 [2, 2048, 512], P(None, ('dp', 'fsdp'))
- vectors_next: float32 [21, 512], P(None, ('dp', 'fsdp'))
- hidden_next: float32 [2, 2048], P(None, ('dp', 'fsdp'))
- attention_mean: float32 [12, 512, 512], P(None, ('dp', 'fsdp'))
- up_mean: float32 [2, 512, 2048], P(None, ('dp', 'fsdp'))
- down_mean: float32 [2, 2048, 512], P(None, ('dp', 'fsdp'))
- vectors_mean: float32 [21, 512], P(None, ('dp', 'fsdp'))
- hidden_mean: float32 [2, 2048], P(None, ('dp', 'fsdp'))
- attention_square: float32 [12, 512, 512], P(None, ('dp', 'fsdp'))
- up_square: float32 [2, 512, 2048], P(None, ('dp', 'fsdp'))
- down_square: float32 [2, 2048, 512], P(None, ('dp', 'fsdp'))
- vectors_square: float32 [21, 512], P(None, ('dp', 'fsdp'))
- hidden_square: float32 [2, 2048], P(None, ('dp', 'fsdp'))
- attention_copy: bfloat16 [12, 512, 512], P(None, ('dp', 'fsdp'))
- up_copy: bfloat16 [2, 512, 2048], P(None, ('dp', 'fsdp'))
- down_copy: bfloat16 [2, 2048, 512], P(None, ('dp', 'fsdp'))
- vectors_copy: bfloat16 [21, 512], P(None, ('dp', 'fsdp'))
- hidden_copy: bfloat16 [2, 2048], P(None, ('dp', 'fsdp'))
The draws below stay inside these ranges and needn't reach their ends.
Inputs may be any that keep to these rules, and one draw needn't show every extreme that they name: `source_segments`: in each row the ids never fall, each of 0 to 3 occurs, and a sentence holds at most 192 tokens. `target_segments`: in each row the ids never fall, each of 0 to 3 occurs, and a sentence holds at most 192 tokens.
All inputs are finite; a program needn't handle non-finite values.
Results may differ from the reference program's by a relative error of at most 0.018.
Values may be sent and summed in bfloat16 or wider, within the bound.
No kernel may reach another device: no remote copies, remote signals or barrier semaphores. Data moves between devices by JAX's collectives and lax.ppermute only.
A program may use at most 192 MiB of HBM per device.

```python
import math
import jax
import jax.numpy as jnp
import numpy as np
from jax import lax

D = 512
FF = 2048
HEADS = 8
HEAD_DIM = 64
LEN = 384
SEGS = 4
STEP = 10
ROWS = 32
TOK_ALL = 12288


def draw_attention_weight(key, part):
    key = jax.random.fold_in(key, 11)
    normal_draw = jnp.clip(jax.random.normal(key, (12, D, D), jnp.float32), -6.0, 6.0)
    matrix_slot = lax.iota(jnp.int32, 12) % 4
    factor = jnp.where(matrix_slot == 3, 3.0, 1.0) * D ** (-0.5)
    return normal_draw * factor[:, None, None]


def draw_vectors(key, part):
    key = jax.random.fold_in(key, 23)
    uniform_draw = jax.random.uniform(key, (21, D), jnp.float32, -1.0, 1.0)
    row_index = lax.iota(jnp.int32, 21)
    is_gain = (row_index == 3) | (row_index == 6) | (row_index == 11) | (row_index == 16) | (row_index == 19)
    return jnp.where(is_gain[:, None], 1.0 + 0.3 * uniform_draw, 0.5 * uniform_draw)


def levels(stream_key, shape, pieces, low, top_value):
    def one(dim, shards_of):
        steps = jax.random.uniform(jax.random.fold_in(jax.random.fold_in(stream_key, 6), dim), (shards_of,), jnp.float32, low / len(pieces), top_value / len(pieces))
        return jnp.repeat(jnp.exp(steps), shape[dim] // shards_of).reshape((-1,) + (1,) * (len(shape) - dim - 1))

    loudness = one(*pieces[0])
    for cut in pieces[1:]:
        loudness = loudness * one(*cut)
    return loudness


def profile(number_of, total, limit, skew):
    weights = [(1 << 20) // math.isqrt(rank ** skew) + 1 for rank in range(2, number_of + 1)]
    spare, counts = total - limit - (number_of - 1), [1] * (number_of - 1)
    while spare > 0:
        movable = [i for i in range(number_of - 1) if counts[i] < limit]
        pool, remaining = sum([weights[i] for i in movable]), spare
        for i in movable:
            addition = min(limit - counts[i], max(1, remaining * weights[i] // pool), spare)
            counts[i] = counts[i] + addition
            spare = spare - addition
    return np.array([limit] + counts)


def uneven(key, count, total, bound, lean):
    if count == 2:
        one = jax.random.randint(key, (), max(1, total - bound), min(bound, total - 1) + 1)
        return jnp.stack([one, total - one])
    lengths = jnp.asarray(profile(count, total, bound, lean), jnp.int32)
    pairs = (count - 1) // 2
    giver, receiver = lengths[1:1 + 2 * pairs:2], lengths[2:2 + 2 * pairs:2]
    slack = jnp.minimum(giver - 1, bound - receiver)
    shifted = jax.random.randint(jax.random.fold_in(key, 1), (pairs,), 0, 1 << 20) % (slack + 1)
    lengths = lengths.at[1:1 + 2 * pairs:2].set(giver - shifted).at[2:2 + 2 * pairs:2].set(receiver + shifted)
    return lengths[jax.random.permutation(jax.random.fold_in(key, 2), count)]


def scatter_about(rng, shape, deviation, limit, shards=(), held_as=jnp.bfloat16):
    factor_of = levels(rng, shape, shards, -0.22, 0.18) if shards else 1.0
    values = jax.random.normal(rng, shape, jnp.float32) * deviation * factor_of
    return jnp.minimum(jnp.maximum(values, -limit), limit).astype(held_as)


def setup_inputs(seed: int = 0) -> dict:
    splits = jax.random.split(jax.random.key(seed), 21)
    return {
        "source_tokens": scatter_about(splits[0], (ROWS, LEN, D), 1.0, 6.0, ((0, 32),)),
        "target_tokens": scatter_about(splits[1], (ROWS, LEN, D), 1.0, 6.0, ((0, 32),)),
        "source_segments": jax.vmap(lambda own: jnp.searchsorted(jnp.cumsum(uneven(own, SEGS, LEN, LEN // 2, 1)), jnp.arange(LEN), side="right"))(jax.random.split(splits[2], ROWS)).reshape((ROWS, LEN)).astype(jnp.int32),
        "target_segments": jax.vmap(lambda own: jnp.searchsorted(jnp.cumsum(uneven(own, SEGS, LEN, LEN // 2, 1)), jnp.arange(LEN), side="right"))(jax.random.split(splits[3], ROWS)).reshape((ROWS, LEN)).astype(jnp.int32),
        "output_grad": scatter_about(splits[4], (ROWS, LEN, D), 1.0, 6.0, ((0, 32),)),
        "attention_weight": draw_attention_weight(jax.random.fold_in(splits[20], 71), 0),
        "up_weight": scatter_about(splits[6], (2, D, FF), D ** -0.5, 0.25, ((1, 32),), jnp.float32),
        "down_weight": scatter_about(splits[7], (2, FF, D), FF ** -0.5, 0.125, ((1, 32),), jnp.float32),
        "vectors": draw_vectors(jax.random.fold_in(splits[20], 71), 0),
        "hidden_bias": scatter_about(splits[9], (2, FF), 0.3, 2.5, ((1, 32),), jnp.float32),
        "attention_first": scatter_about(splits[10], (12, D, D), (0.055 * TOK_ALL ** 0.5), 36.580914, ((1, 32),), jnp.float32),
        "up_first": scatter_about(splits[11], (2, D, FF), (0.055 * TOK_ALL ** 0.5), 36.580914, ((1, 32),), jnp.float32),
        "down_first": scatter_about(splits[12], (2, FF, D), (0.055 * TOK_ALL ** 0.5), 36.580914, ((1, 32),), jnp.float32),
        "vectors_first": scatter_about(splits[13], (21, D), (0.055 * TOK_ALL ** 0.5), 36.580914, ((1, 32),), jnp.float32),
        "hidden_first": scatter_about(splits[14], (2, FF), (0.055 * TOK_ALL ** 0.5), 36.580914, ((1, 32),), jnp.float32),
        "attention_second": jnp.clip(jnp.exp(math.log(12.288) - 1.3862944 * jax.random.uniform(splits[15], (12, D, D), jnp.float32) ** levels(splits[15], (12, D, D), ((1, 32),), -0.2, 0.2)), 3.072, 12.288),
        "up_second": jnp.clip(jnp.exp(math.log(12.288) - 1.3862944 * jax.random.uniform(splits[16], (2, D, FF), jnp.float32) ** levels(splits[16], (2, D, FF), ((1, 32),), -0.2, 0.2)), 3.072, 12.288),
        "down_second": jnp.clip(jnp.exp(math.log(12.288) - 1.3862944 * jax.random.uniform(splits[17], (2, FF, D), jnp.float32) ** levels(splits[17], (2, FF, D), ((1, 32),), -0.2, 0.2)), 3.072, 12.288),
        "vectors_second": jnp.clip(jnp.exp(math.log(12.288) - 1.3862944 * jax.random.uniform(splits[18], (21, D), jnp.float32) ** levels(splits[18], (21, D), ((1, 32),), -0.2, 0.2)), 3.072, 12.288),
        "hidden_second": jnp.clip(jnp.exp(math.log(12.288) - 1.3862944 * jax.random.uniform(splits[19], (2, FF), jnp.float32) ** levels(splits[19], (2, FF), ((1, 32),), -0.2, 0.2)), 3.072, 12.288),
    }


@jax.custom_vjp
def low(v):
    return lax.optimization_barrier(v.astype(jnp.bfloat16)).astype(jnp.float32)

@jax.custom_vjp
def low_back(v):
    return v

def low_keep(v):
    return (low(v), None)

def low_pass(kept, grad):
    return (grad,)

def back_keep(v):
    return (v, None)

def back_low(kept, grad):
    return (low(grad),)
low.defvjp(low_keep, low_pass)
low_back.defvjp(back_keep, back_low)
EPS_NORM = 1e-05
EPS_ADAM = 1e-08
BETA_ONE = 0.9
BETA_TWO = 0.999
LOWEST = -1e+30
RATES = (0.05, 0.05, 0.05, 0.3, 0.3)
DECAYS = (0.01, 0.01, 0.01, 0.0, 0.0)

def rounded(value_in):
    return low(low_back(value_in))

def matmul_high(left_rows, right_cols):
    return jnp.dot(left_rows, right_cols, precision=lax.Precision.HIGHEST)

def layer_norm(pre_norm, norm_gain, norm_shift):
    row_mean = lax.optimization_barrier(jnp.mean(pre_norm, axis=-1, keepdims=True))
    centred = pre_norm - row_mean
    spread = lax.optimization_barrier(jnp.mean(centred * centred, axis=-1, keepdims=True))
    return centred * lax.rsqrt(spread + EPS_NORM) * norm_gain + norm_shift

def attend(query_in, key_in, weights, biases, allowed):
    length = query_in.shape[0]
    key_count = key_in.shape[0]
    query_vecs = rounded(matmul_high(query_in, weights[0]) + biases[0]).reshape(length, HEADS, HEAD_DIM)
    key_vecs = rounded(matmul_high(key_in, weights[1])).reshape(key_count, HEADS, HEAD_DIM)
    value_vecs = rounded(matmul_high(key_in, weights[2]) + biases[1]).reshape(key_count, HEADS, HEAD_DIM)
    scores = jnp.einsum('qhe,khe->hqk', query_vecs, key_vecs, precision=lax.Precision.HIGHEST)
    scores = low_back(scores * HEAD_DIM ** (-0.5))
    scores = jnp.where(allowed[None], scores, LOWEST)
    largest = lax.optimization_barrier(jnp.max(scores, axis=-1, keepdims=True))
    exponent = jnp.exp(scores - largest)
    attention = low(exponent / lax.optimization_barrier(jnp.sum(exponent, axis=-1, keepdims=True)))
    combined = jnp.einsum('hqk,khe->qhe', attention, value_vecs, precision=lax.Precision.HIGHEST)
    combined = rounded(combined.reshape(length, HEADS * HEAD_DIM))
    return low_back(matmul_high(combined, weights[3]) + biases[2])

def feed_forward(inputs, weight_in, bias_in, weight_out, bias_out):
    hidden = low_back(matmul_high(inputs, weight_in) + bias_in)
    active = low(jax.nn.gelu(hidden, approximate=True))
    return low_back(matmul_high(active, weight_out) + bias_out)

def encode(source, source_segment, projections, weight_in, weight_out, vector_rows, hidden_rows):
    allowed = source_segment[:, None] == source_segment[None, :]
    attended = attend(source, source, projections, vector_rows[0:3], allowed)
    first_norm = layer_norm(source + attended, vector_rows[3], vector_rows[4])
    branch = feed_forward(low(first_norm), weight_in, hidden_rows, weight_out, vector_rows[5])
    return layer_norm(first_norm + branch, vector_rows[6], vector_rows[7])

def decode(target, memory, target_segment, source_segment, projections, weight_in, weight_out, vector_rows, hidden_rows):
    length = target.shape[0]
    places = jnp.arange(length)
    causal = (target_segment[:, None] == target_segment[None, :]) & (places[:, None] >= places[None, :])
    crossing = target_segment[:, None] == source_segment[None, :]
    attended = attend(target, target, projections[0:4], vector_rows[0:3], causal)
    first_norm = layer_norm(target + attended, vector_rows[3], vector_rows[4])
    crossed = attend(low(first_norm), low(memory), projections[4:8], vector_rows[5:8], crossing)
    second_norm = layer_norm(first_norm + crossed, vector_rows[8], vector_rows[9])
    branch = feed_forward(low(second_norm), weight_in, hidden_rows, weight_out, vector_rows[10])
    return layer_norm(second_norm + branch, vector_rows[11], vector_rows[12])

def forward(params, sources, targets, source_segments, target_segments):
    copies = tuple((low(param) for param in params))
    projections, weight_in, weight_out, vector_rows, hidden_rows = copies

    def one_row(row_data):
        source, target, source_segment, target_segment = row_data
        memory = encode(source, source_segment, projections[0:4], weight_in[0], weight_out[0], vector_rows[0:8], hidden_rows[0])
        result = decode(target, memory, target_segment, source_segment, projections[4:12], weight_in[1], weight_out[1], vector_rows[8:21], hidden_rows[1])
        return (memory, result)
    return lax.map(jax.checkpoint(one_row), (sources, targets, source_segments, target_segments))

def adam_update(weight, gradient, first, second, rate, decay):
    first_new = BETA_ONE * first + (1.0 - BETA_ONE) * gradient
    second_new = BETA_TWO * second + (1.0 - BETA_TWO) * gradient * gradient
    first_hat = first_new / (1.0 - BETA_ONE ** STEP)
    second_hat = second_new / (1.0 - BETA_TWO ** STEP)
    weight_new = weight - rate * (first_hat / (jnp.sqrt(second_hat) + EPS_ADAM) + decay * weight)
    return (weight_new, first_new, second_new, weight_new.astype(jnp.bfloat16))

def reference(source_tokens, target_tokens, source_segments, target_segments, output_grad, attention_weight, up_weight, down_weight, vectors, hidden_bias, attention_first, up_first, down_first, vectors_first, hidden_first, attention_second, up_second, down_second, vectors_second, hidden_second):
    params = (attention_weight, up_weight, down_weight, vectors, hidden_bias)
    firsts = (attention_first, up_first, down_first, vectors_first, hidden_first)
    seconds = (attention_second, up_second, down_second, vectors_second, hidden_second)
    sources = source_tokens.astype(jnp.float32)
    targets = target_tokens.astype(jnp.float32)

    def run(param_set, source_rows, target_rows):
        return forward(param_set, source_rows, target_rows, source_segments, target_segments)
    (memory, result), pullback = jax.vjp(run, params, sources, targets)
    grads, source_grad, target_grad = pullback((jnp.zeros_like(memory), output_grad.astype(jnp.float32)))
    updated = [adam_update(params[slot], grads[slot], firsts[slot], seconds[slot], RATES[slot], DECAYS[slot]) for slot in range(5)]
    return (memory, result, source_grad, target_grad, updated[0][0], updated[1][0], updated[2][0], updated[3][0], updated[4][0], updated[0][1], updated[1][1], updated[2][1], updated[3][1], updated[4][1], updated[0][2], updated[1][2], updated[2][2], updated[3][2], updated[4][2], updated[0][3], updated[1][3], updated[2][3], updated[3][3], updated[4][3])
```

```python
import functools
import math

import jax
import jax.numpy as jnp
from jax import lax
from jax.sharding import PartitionSpec as P

HEADS = 8
STEP = 10


EPS_NORM = 1e-05
EPS_ADAM = 1e-08
BETA_ONE = 0.9
BETA_TWO = 0.999
LOWEST = -1e30
PAIRED = 2
RATES = (0.05, 0.05, 0.05, 0.3, 0.3)
DECAYS = (0.01, 0.01, 0.01, 0.0, 0.0)


def layer_norm(pre_norm, norm_gain, norm_shift):
    row_mean = jnp.mean(pre_norm, axis=-1, keepdims=True)
    centred = pre_norm - row_mean
    spread = jnp.mean(centred * centred, axis=-1, keepdims=True)
    return centred * lax.rsqrt(spread + EPS_NORM) * norm_gain + norm_shift


def gelu_tanh(pre_act):
    return jax.nn.gelu(pre_act, approximate=True)


def project(inputs, weight):
    return jnp.dot(inputs, weight, preferred_element_type=jnp.float32)


def weight_grad(inputs, gradient):
    return jnp.einsum("ld,le->de", inputs, gradient, preferred_element_type=jnp.float32)


def back_project(gradient, weight):
    return jnp.einsum("le,de->ld", gradient, weight, preferred_element_type=jnp.float32)


def column_sum(gradient):
    return jnp.sum(gradient, axis=0, dtype=jnp.float32)


def split_heads(row_block):
    return row_block.reshape(row_block.shape[0], HEADS, row_block.shape[1] // HEADS)


def masked_scores(query_heads, key_heads, head_start, allowed, inv_root):
    head_pick = slice(head_start, head_start + PAIRED)
    scores = (
        jnp.einsum(
            "qhe,khe->hqk",
            query_heads[:, head_pick],
            key_heads[:, head_pick],
            preferred_element_type=jnp.float32,
        )
        * inv_root
    )
    return jnp.where(allowed[None], scores, LOWEST)


def attend_forward(query_rows, key_rows, weights, biases, allowed):
    model_width = query_rows.shape[1]
    inv_root = (model_width // HEADS) ** (-0.5)
    query_vecs = (project(query_rows, weights[0]) + biases[0]).astype(jnp.bfloat16)
    key_vecs = project(key_rows, weights[1]).astype(jnp.bfloat16)
    value_vecs = (project(key_rows, weights[2]) + biases[1]).astype(jnp.bfloat16)
    query_heads = split_heads(query_vecs)
    key_heads = split_heads(key_vecs)
    value_heads = split_heads(value_vecs)
    mixed_parts = []
    log_parts = []
    for head_start in range(0, HEADS, PAIRED):
        scores = masked_scores(query_heads, key_heads, head_start, allowed, inv_root)
        largest = jnp.max(scores, axis=-1, keepdims=True)
        exponent = jnp.exp(scores - largest)
        row_total = jnp.sum(exponent, axis=-1, keepdims=True)
        attention = (exponent / row_total).astype(jnp.bfloat16)
        mixed_parts.append(
            jnp.einsum(
                "hqk,khe->qhe",
                attention,
                value_heads[:, head_start : head_start + PAIRED],
                preferred_element_type=jnp.float32,
            )
        )
        log_parts.append(largest + jnp.log(row_total))
    combined = (
        jnp.concatenate(mixed_parts, axis=1)
        .reshape(query_rows.shape[0], model_width)
        .astype(jnp.bfloat16)
    )
    result = project(combined, weights[3]) + biases[2]
    return (
        result,
        (query_vecs, key_vecs, value_vecs, jnp.concatenate(log_parts, axis=0), combined),
    )


def attend_backward(grad_out, query_rows, key_rows, weights, allowed, kept):
    query_vecs, key_vecs, value_vecs, log_totals, combined = kept
    inv_root = (query_rows.shape[1] // HEADS) ** (-0.5)
    out_low = grad_out.astype(jnp.bfloat16)
    output_weight = weight_grad(combined, out_low)
    output_bias = column_sum(out_low)
    combined_grad = back_project(out_low, weights[3]).astype(jnp.bfloat16)
    query_heads = split_heads(query_vecs)
    key_heads = split_heads(key_vecs)
    value_heads = split_heads(value_vecs)
    grad_heads = split_heads(combined_grad)
    query_parts = []
    key_parts = []
    value_parts = []
    for head_start in range(0, HEADS, PAIRED):
        head_pick = slice(head_start, head_start + PAIRED)
        scores = masked_scores(query_heads, key_heads, head_start, allowed, inv_root)
        attention = jnp.exp(scores - log_totals[head_pick])
        attention_low = attention.astype(jnp.bfloat16)
        value_parts.append(
            jnp.einsum(
                "hqk,qhe->khe",
                attention_low,
                grad_heads[:, head_pick],
                preferred_element_type=jnp.float32,
            )
        )
        prob_grad = jnp.einsum(
            "qhe,khe->hqk",
            grad_heads[:, head_pick],
            value_heads[:, head_pick],
            preferred_element_type=jnp.float32,
        )
        row_dot = jnp.sum(prob_grad * attention, axis=-1, keepdims=True)
        score_low = (attention * (prob_grad - row_dot)).astype(jnp.bfloat16)
        query_parts.append(
            jnp.einsum(
                "hqk,khe->qhe",
                score_low,
                key_heads[:, head_pick],
                preferred_element_type=jnp.float32,
            )
            * inv_root
        )
        key_parts.append(
            jnp.einsum(
                "hqk,qhe->khe",
                score_low,
                query_heads[:, head_pick],
                preferred_element_type=jnp.float32,
            )
            * inv_root
        )
    query_grad = jnp.concatenate(query_parts, axis=1).reshape(query_vecs.shape).astype(jnp.bfloat16)
    key_grad = jnp.concatenate(key_parts, axis=1).reshape(key_vecs.shape).astype(jnp.bfloat16)
    value_grad = jnp.concatenate(value_parts, axis=1).reshape(value_vecs.shape).astype(jnp.bfloat16)
    stacked = jnp.stack(
        [
            weight_grad(query_rows, query_grad),
            weight_grad(key_rows, key_grad),
            weight_grad(key_rows, value_grad),
            output_weight,
        ]
    )
    bias_grads = jnp.stack([column_sum(query_grad), column_sum(value_grad), output_bias])
    query_back = back_project(query_grad, weights[0])
    key_back = back_project(key_grad, weights[1]) + back_project(value_grad, weights[2])
    return (stacked, bias_grads, query_back, key_back)


def feed_forward(inputs, weight_in, bias_in, weight_out, bias_out):
    hidden, gelu_pull = jax.vjp(gelu_tanh, project(inputs, weight_in) + bias_in)
    active = hidden.astype(jnp.bfloat16)
    return (project(active, weight_out) + bias_out, (gelu_pull, active))


def feed_backward(grad_in, inputs, weight_in, weight_out, kept):
    gelu_pull, active = kept
    grad_low = grad_in.astype(jnp.bfloat16)
    out_weight = weight_grad(active, grad_low)
    out_bias = column_sum(grad_low)
    (hidden_grad,) = gelu_pull(back_project(grad_low, weight_out))
    hidden_low = hidden_grad.astype(jnp.bfloat16)
    return (
        back_project(hidden_low, weight_in),
        weight_grad(inputs, hidden_low),
        column_sum(hidden_low),
        out_weight,
        out_bias,
    )


def encode_forward(source, source_segment, weights):
    projections, weight_in, weight_out, vector_low, hidden_low = weights
    vector_rows = vector_low.astype(jnp.float32)
    hidden_rows = hidden_low.astype(jnp.float32)
    allowed = source_segment[:, None] == source_segment[None, :]
    attended, attend_kept = attend_forward(source, source, projections, vector_rows[0:3], allowed)
    first_norm, first_pull = jax.vjp(
        layer_norm, source.astype(jnp.float32) + attended, vector_rows[3], vector_rows[4]
    )
    first_low = first_norm.astype(jnp.bfloat16)
    branch, branch_kept = feed_forward(
        first_low, weight_in[0], hidden_rows[0], weight_out[0], vector_rows[5]
    )
    output, second_pull = jax.vjp(layer_norm, first_norm + branch, vector_rows[6], vector_rows[7])
    return (output, (allowed, attend_kept, first_pull, first_low, branch_kept, second_pull))


def encode_backward(grad_in, source, weights, kept):
    projections, weight_in, weight_out = (weights[0], weights[1], weights[2])
    allowed, attend_kept, first_pull, first_low, branch_kept, second_pull = kept
    second_grad, gain_two, shift_two = second_pull(grad_in)
    rows_back, in_weight, in_bias, out_weight, out_bias = feed_backward(
        second_grad, first_low, weight_in[0], weight_out[0], branch_kept
    )
    first_grad, gain_one, shift_one = first_pull(second_grad + rows_back)
    stacked, bias_grads, query_back, key_back = attend_backward(
        first_grad, source, source, projections, allowed, attend_kept
    )
    source_grad = first_grad + query_back + key_back
    vector_grads = jnp.concatenate(
        [bias_grads, jnp.stack([gain_one, shift_one, out_bias, gain_two, shift_two])], axis=0
    )
    return (source_grad, (stacked, in_weight[None], out_weight[None], vector_grads, in_bias[None]))


def decode_forward(target, memory, target_segment, source_segment, weights):
    projections, weight_in, weight_out, vector_low, hidden_low = weights
    vector_rows = vector_low.astype(jnp.float32)
    hidden_rows = hidden_low.astype(jnp.float32)
    places = lax.iota(jnp.int32, target.shape[0])
    causal = (target_segment[:, None] == target_segment[None, :]) & (
        places[:, None] >= places[None, :]
    )
    crossing = target_segment[:, None] == source_segment[None, :]
    attended, self_kept = attend_forward(target, target, projections[0:4], vector_rows[0:3], causal)
    first_norm, first_pull = jax.vjp(
        layer_norm, target.astype(jnp.float32) + attended, vector_rows[3], vector_rows[4]
    )
    first_low = first_norm.astype(jnp.bfloat16)
    memory_low = memory.astype(jnp.bfloat16)
    crossed, cross_kept = attend_forward(
        first_low, memory_low, projections[4:8], vector_rows[5:8], crossing
    )
    second_norm, second_pull = jax.vjp(
        layer_norm, first_norm + crossed, vector_rows[8], vector_rows[9]
    )
    second_low = second_norm.astype(jnp.bfloat16)
    branch, branch_kept = feed_forward(
        second_low, weight_in[0], hidden_rows[0], weight_out[0], vector_rows[10]
    )
    output, third_pull = jax.vjp(layer_norm, second_norm + branch, vector_rows[11], vector_rows[12])
    return (
        output,
        (
            causal,
            self_kept,
            first_pull,
            first_low,
            memory_low,
            crossing,
            cross_kept,
            second_pull,
            second_low,
            branch_kept,
            third_pull,
        ),
    )


def decode_backward(grad_in, target, weights, kept):
    projections, weight_in, weight_out = (weights[0], weights[1], weights[2])
    (
        causal,
        self_kept,
        first_pull,
        first_low,
        memory_low,
        crossing,
        cross_kept,
        second_pull,
        second_low,
        branch_kept,
        third_pull,
    ) = kept
    third_grad, gain_three, shift_three = third_pull(grad_in)
    rows_back, in_weight, in_bias, out_weight, out_bias = feed_backward(
        third_grad, second_low, weight_in[0], weight_out[0], branch_kept
    )
    second_grad, gain_two, shift_two = second_pull(third_grad + rows_back)
    cross_stack, cross_bias, cross_query, memory_grad = attend_backward(
        second_grad, first_low, memory_low, projections[4:8], crossing, cross_kept
    )
    first_grad, gain_one, shift_one = first_pull(second_grad + cross_query)
    self_stack, self_bias, self_query, self_key = attend_backward(
        first_grad, target, target, projections[0:4], causal, self_kept
    )
    target_grad = first_grad + self_query + self_key
    vector_grads = jnp.concatenate(
        [
            self_bias,
            jnp.stack([gain_one, shift_one]),
            cross_bias,
            jnp.stack([gain_two, shift_two, out_bias, gain_three, shift_three]),
        ],
        axis=0,
    )
    stacked = jnp.concatenate([self_stack, cross_stack], axis=0)
    return (
        target_grad,
        memory_grad,
        (stacked, in_weight[None], out_weight[None], vector_grads, in_bias[None]),
    )


def adam_update(weight, gradient, first, second, rate, decay):
    first_new = BETA_ONE * first + (1.0 - BETA_ONE) * gradient
    second_new = BETA_TWO * second + (1.0 - BETA_TWO) * gradient * gradient
    first_hat = first_new / (1.0 - BETA_ONE**STEP)
    second_hat = second_new / (1.0 - BETA_TWO**STEP)
    weight_new = weight - rate * (first_hat / (jnp.sqrt(second_hat) + EPS_ADAM) + decay * weight)
    return (weight_new, first_new, second_new, weight_new.astype(jnp.bfloat16))


AXES = ("dp", "fsdp")


def small_rows(pieces):
    wide = pieces[0].shape[2]
    flat = pieces[3].size + pieces[4].size
    return -(-flat // (16 * wide)) * 16


def pack(pieces):
    wide = pieces[0].shape[2]
    rows = pieces[1].shape[1]
    up = pieces[1].reshape(-1, rows, pieces[1].shape[2] // wide, wide)
    up = up.transpose(0, 2, 1, 3).reshape(-1, wide)
    small = jnp.concatenate([pieces[3].reshape(-1), pieces[4].reshape(-1)])
    lines = small_rows(pieces)
    small = jnp.pad(small, (0, lines * wide - small.shape[0])).reshape(lines, wide)
    return jnp.concatenate(
        [pieces[0].reshape(-1, wide), up, pieces[2].reshape(-1, wide), small], axis=0
    )


def unpack(packed, pieces):
    count = packed.shape[0]
    wide = packed.shape[2]
    outs = []
    at = 0
    for slot in range(3):
        number, rows, columns = pieces[slot].shape
        lines = number * rows * (columns // wide)
        part = packed[:, at : at + lines].reshape(count, number, columns // wide, rows, wide)
        outs.append(part.transpose(1, 0, 3, 2, 4).reshape(number, count * rows, columns))
        at += lines
    small = packed[:, at:].reshape(count, -1)
    at = 0
    for slot in (3, 4):
        number, rows = pieces[slot].shape
        part = small[:, at : at + number * rows].reshape(count, number, rows)
        outs.append(part.transpose(1, 0, 2).reshape(number, count * rows))
        at += number * rows
    return tuple(outs)


def gather_packed(pieces):
    return unpack(lax.all_gather(pack(pieces), AXES, axis=0, tiled=False), pieces)


def exchange(send, bit, count):
    pairs = [(place, place ^ (1 << bit)) for place in range(count)]
    return lax.ppermute(send, AXES, pairs)


def scatter_packed(grads, pieces, axis_sizes):
    outer, inner = axis_sizes
    count = outer * inner
    wide = pieces[0].shape[2]
    parts = []
    for slot in range(3):
        number, rows, columns = pieces[slot].shape
        part = grads[slot].reshape(number, count, rows, columns // wide, wide)
        parts.append(part.transpose(1, 0, 3, 2, 4).reshape(count, -1, wide))
    small = []
    for slot in (3, 4):
        number, rows = pieces[slot].shape
        small.append(grads[slot].reshape(number, count, rows).transpose(1, 0, 2).reshape(count, -1))
    lines = small_rows(pieces)
    small = jnp.concatenate(small, axis=1)
    small = jnp.pad(small, ((0, 0), (0, lines * wide - small.shape[1]))).reshape(count, lines, wide)
    packed = jnp.concatenate(parts + [small], axis=1).astype(jnp.bfloat16)
    bits = int(math.log2(count))
    inner_bits = int(math.log2(inner))
    first = inner_bits
    outer_rest = list(range(inner_bits + 1, bits))
    inner_list = list(range(inner_bits))
    orders = (
        [first] + outer_rest + inner_list,
        [first] + inner_list[:1] + outer_rest + inner_list[1:],
    )
    total = packed.shape[1]
    cut = total // 32 * 16
    place = lax.axis_index(AXES)
    streams = []
    for order, piece in zip(orders, (packed[:, :cut], packed[:, cut:])):
        streams.append([piece.reshape((2,) * bits + piece.shape[1:]), list(range(bits))[::-1]])
    for step in range(bits):
        for index, order in enumerate(orders):
            held, left = streams[index]
            bit = order[step]
            axis = left.index(bit)
            mine = (place >> bit) & 1
            send = lax.dynamic_index_in_dim(held, 1 - mine, axis, keepdims=False)
            keep = lax.dynamic_index_in_dim(held, mine, axis, keepdims=False)
            arrived = exchange(send.astype(jnp.bfloat16), bit, count)
            added = keep.astype(jnp.float32) + arrived.astype(jnp.float32)
            if step < bits - 1:
                added = added.astype(jnp.bfloat16)
            streams[index] = [added, left[:axis] + left[axis + 1 :]]
    share = jnp.concatenate([streams[0][0], streams[1][0]], axis=0)[None]
    return unpack(share, pieces)


def per_device(
    axis_sizes,
    source_tokens,
    target_tokens,
    source_segments,
    target_segments,
    output_grad,
    attention_weight,
    up_weight,
    down_weight,
    vectors,
    hidden_bias,
    attention_first,
    up_first,
    down_first,
    vectors_first,
    hidden_first,
    attention_second,
    up_second,
    down_second,
    vectors_second,
    hidden_second,
):
    masters = (attention_weight, up_weight, down_weight, vectors, hidden_bias)
    firsts = (attention_first, up_first, down_first, vectors_first, hidden_first)
    seconds = (attention_second, up_second, down_second, vectors_second, hidden_second)
    halves = [master.astype(jnp.bfloat16) for master in masters]
    encoder_pieces = [halves[0][0:4], halves[1][0:1], halves[2][0:1], halves[3][0:8], halves[4][0:1]]
    decoder_pieces = [halves[0][4:12], halves[1][1:2], halves[2][1:2], halves[3][8:21], halves[4][1:2]]
    source = source_tokens[0]
    target = target_tokens[0]
    source_segment = source_segments[0]
    target_segment = target_segments[0]
    encoder_weights = gather_packed(encoder_pieces)
    decoder_weights = gather_packed(decoder_pieces)
    memory, encoder_kept = encode_forward(source, source_segment, encoder_weights)
    result, decoder_kept = decode_forward(
        target, memory, target_segment, source_segment, decoder_weights
    )
    target_grad, memory_grad, decoder_grads = decode_backward(
        output_grad[0].astype(jnp.float32), target, decoder_weights, decoder_kept
    )
    decoder_shares = scatter_packed(decoder_grads, decoder_pieces, axis_sizes)
    source_grad, encoder_grads = encode_backward(memory_grad, source, encoder_weights, encoder_kept)
    encoder_shares = scatter_packed(encoder_grads, encoder_pieces, axis_sizes)
    grad_list = [
        jnp.concatenate([encoder_shares[slot_index], decoder_shares[slot_index]], axis=0)
        for slot_index in range(5)
    ]
    updated = []
    for slot_index in range(5):
        updated.append(
            adam_update(
                masters[slot_index],
                grad_list[slot_index],
                firsts[slot_index],
                seconds[slot_index],
                RATES[slot_index],
                DECAYS[slot_index],
            )
        )
    return (
        memory[None],
        result[None],
        source_grad[None],
        target_grad[None],
        updated[0][0],
        updated[1][0],
        updated[2][0],
        updated[3][0],
        updated[4][0],
        updated[0][1],
        updated[1][1],
        updated[2][1],
        updated[3][1],
        updated[4][1],
        updated[0][2],
        updated[1][2],
        updated[2][2],
        updated[3][2],
        updated[4][2],
        updated[0][3],
        updated[1][3],
        updated[2][3],
        updated[3][3],
        updated[4][3],
    )


def solution(mesh):
    placed = (
        P(("dp", "fsdp"), None, None),
        P(("dp", "fsdp"), None, None),
        P(("dp", "fsdp"), None),
        P(("dp", "fsdp"), None),
        P(("dp", "fsdp"), None, None),
        P(None, ("dp", "fsdp"), None),
        P(None, ("dp", "fsdp"), None),
        P(None, ("dp", "fsdp"), None),
        P(None, ("dp", "fsdp")),
        P(None, ("dp", "fsdp")),
        P(None, ("dp", "fsdp"), None),
        P(None, ("dp", "fsdp"), None),
        P(None, ("dp", "fsdp"), None),
        P(None, ("dp", "fsdp")),
        P(None, ("dp", "fsdp")),
        P(None, ("dp", "fsdp"), None),
        P(None, ("dp", "fsdp"), None),
        P(None, ("dp", "fsdp"), None),
        P(None, ("dp", "fsdp")),
        P(None, ("dp", "fsdp")),
    )
    return jax.shard_map(
        functools.partial(per_device, (mesh.shape["dp"], mesh.shape["fsdp"])),
        mesh=mesh,
        in_specs=placed,
        out_specs=(
            P(("dp", "fsdp"), None, None),
            P(("dp", "fsdp"), None, None),
            P(("dp", "fsdp"), None, None),
            P(("dp", "fsdp"), None, None),
            P(None, ("dp", "fsdp"), None),
            P(None, ("dp", "fsdp"), None),
            P(None, ("dp", "fsdp"), None),
            P(None, ("dp", "fsdp")),
            P(None, ("dp", "fsdp")),
            P(None, ("dp", "fsdp"), None),
            P(None, ("dp", "fsdp"), None),
            P(None, ("dp", "fsdp"), None),
            P(None, ("dp", "fsdp")),
            P(None, ("dp", "fsdp")),
            P(None, ("dp", "fsdp"), None),
            P(None, ("dp", "fsdp"), None),
            P(None, ("dp", "fsdp"), None),
            P(None, ("dp", "fsdp")),
            P(None, ("dp", "fsdp")),
            P(None, ("dp", "fsdp"), None),
            P(None, ("dp", "fsdp"), None),
            P(None, ("dp", "fsdp"), None),
            P(None, ("dp", "fsdp")),
            P(None, ("dp", "fsdp")),
        ),
        check_vma=False,
    )
```

```python
import functools

import jax
import jax.numpy as jnp
from jax import lax
from jax.experimental import pallas as pl
from jax.experimental.pallas import tpu as pltpu
from jax.sharding import PartitionSpec as P

HEADS = 8
STEP = 10
EPS_NORM = 1e-05
EPS_ADAM = 1e-08
BETA_ONE = 0.9
BETA_TWO = 0.999
LOWEST = -1e30
RATES = (0.05, 0.05, 0.05, 0.3, 0.3)
DECAYS = (0.01, 0.01, 0.01, 0.0, 0.0)
AXES = ("dp", "fsdp")
QUAD = 4
BLOCK = 16
LANES = 128
SMALL_ROWS = 32
HIDDEN_ROW = 21
BF = jnp.bfloat16
F32 = jnp.float32
VMEM = pl.BlockSpec(memory_space=pltpu.VMEM)
SMEM = pl.BlockSpec(memory_space=pltpu.SMEM)
ANY = pl.BlockSpec(memory_space=pl.ANY)
ROOT_TWO_PI = 0.7978845608028654
CUBIC = 0.044715


def dot(left, right):
    return jnp.dot(left, right, preferred_element_type=F32)


def dot_nt(left, right):
    return lax.dot_general(left, right, (((1,), (1,)), ((), ())), preferred_element_type=F32)


def load_start(table, near, far, place, sems):
    half = near.shape[0]
    for index in range(half):
        pltpu.make_async_copy(near.at[index], place(table[index]), sems.at[0]).start()
        pltpu.make_async_copy(far.at[index], place(table[half + index]), sems.at[1]).start()


def load_wait(near, far, sems):
    pltpu.make_async_copy(near, near, sems.at[0]).wait()
    pltpu.make_async_copy(far, far, sems.at[1]).wait()


def store_start(table, keep, send, place, sems):
    half = keep.shape[0]
    for index in range(half):
        pltpu.make_async_copy(place(table[half + index]), send.at[index], sems.at[1]).start()
        pltpu.make_async_copy(place(table[index]), keep.at[index], sems.at[0]).start()


def row_place(scratch, low, high):
    def place(block):
        start = pl.multiple_of(block * BLOCK, BLOCK)
        return scratch.at[low:high, pl.ds(start, BLOCK), :]

    return place


def block_place(scratch):
    return lambda block: scratch.at[block]


def norm_forward(pre, gain, shift, out_ref, hat_ref, rstd_ref):
    mean = jnp.mean(pre, axis=-1, keepdims=True)
    centred = pre - mean
    spread = jnp.mean(centred * centred, axis=-1, keepdims=True)
    rstd = lax.rsqrt(spread + EPS_NORM)
    hat = centred * rstd
    hat_ref[...] = hat
    rstd_ref[...] = jnp.broadcast_to(rstd, rstd_ref.shape)
    out_ref[...] = hat * gain + shift


def norm_backward(grad, hat, rstd, gain):
    gain_grad = jnp.sum(grad * hat, axis=0, keepdims=True)
    shift_grad = jnp.sum(grad, axis=0, keepdims=True)
    scaled = grad * gain
    one = jnp.mean(scaled, axis=-1, keepdims=True)
    two = jnp.mean(scaled * hat, axis=-1, keepdims=True)
    return rstd * (scaled - one - hat * two), gain_grad, shift_grad


def lane_mask(rows):
    return lax.broadcasted_iota(jnp.int32, (rows, LANES), 1) < LANES // 2


def stacked_pair(block):
    first = lane_mask(block.shape[0])
    zero = jnp.zeros_like(block)
    return jnp.concatenate([jnp.where(first, block, zero), jnp.where(first, zero, block)], axis=0)


def merged_pair(stacked):
    rows = stacked.shape[0] // 2
    return jnp.where(lane_mask(rows), stacked[:rows], stacked[rows:])


def mask_fill(bias_ref, column_seg, row_seg, causal, transposed):
    length = bias_ref.shape[0]
    column = jnp.broadcast_to(column_seg, (LANES, length)).T
    for at in range(0, length, LANES):
        same = column == row_seg[:, at : at + LANES]
        if causal:
            down = lax.broadcasted_iota(jnp.int32, (length, LANES), 0)
            along = lax.broadcasted_iota(jnp.int32, (length, LANES), 1) + at
            order = (down <= along) if transposed else (along <= down)
            same = same & order
        bias_ref[:, at : at + LANES] = jnp.where(same, 0.0, LOWEST)


def attend_forward_kernel(parts, cross, causal, base, *refs):
    refs = list(refs)
    tables = [refs.pop(0) for _ in range(parts)]
    query_seg = refs.pop(0)
    key_seg = refs.pop(0)
    small = refs.pop(0)
    rows_ref = refs.pop(0)
    memory_ref = refs.pop(0) if cross else None
    near_far = [(refs.pop(0), refs.pop(0)) for _ in range(parts)]
    out_ref, hat_ref, rstd_ref, q_ref, k_ref, v_ref, o_ref, lse_ref = refs[:8]
    w_ref, bias_ref, sems = refs[8:]
    step = QUAD // parts
    for part in range(parts):
        near, far = near_far[part]
        place = row_place(w_ref, part * step, (part + 1) * step)
        load_start(tables[part], near, far, place, sems.at[part])
    length, width = rows_ref.shape
    mask_fill(bias_ref, query_seg[...], key_seg[...], causal, False)
    rows = rows_ref[...].astype(BF)
    keys = memory_ref[...].astype(BF) if cross else rows
    for part in range(parts):
        near, far = near_far[part]
        load_wait(near, far, sems.at[part])
    scale = (width // HEADS) ** (-0.5)
    q_ref[...] = (dot(rows, w_ref[0]) + small[base : base + 1]).astype(BF) * jnp.asarray(scale, BF)
    k_ref[...] = dot(keys, w_ref[1]).astype(BF)
    v_ref[...] = (dot(keys, w_ref[2]) + small[base + 1 : base + 2]).astype(BF)
    lane = lax.broadcasted_iota(jnp.int32, (LANES, LANES), 1)
    for at in range(0, length, LANES):
        reach = at + LANES if causal else length
        logs = jnp.zeros((LANES, LANES), F32)
        for pair in range(HEADS // 2):
            lanes = slice(pair * LANES, (pair + 1) * LANES)
            stacked = stacked_pair(q_ref[at : at + LANES, lanes])
            scores = dot_nt(stacked, k_ref[:reach, lanes])
            bias = bias_ref[at : at + LANES, :reach]
            scores = scores + jnp.concatenate([bias, bias], axis=0)
            largest = jnp.max(scores, axis=-1, keepdims=True)
            exponent = jnp.exp(scores - largest).astype(BF)
            values = jnp.concatenate([v_ref[:reach, lanes], jnp.ones((reach, LANES), BF)], axis=1)
            mixed = dot(exponent, values)
            total = mixed[:, LANES:]
            o_ref[at : at + LANES, lanes] = merged_pair(mixed[:, :LANES] / total).astype(BF)
            log_total = largest + jnp.log(total)
            logs = jnp.where(lane == 2 * pair, log_total[:LANES], logs)
            logs = jnp.where(lane == 2 * pair + 1, log_total[LANES:], logs)
        lse_ref[:, at : at + LANES] = logs.T[:HEADS]
    attended = dot(o_ref[...], w_ref[3]) + small[base + 2 : base + 3]
    pre = rows_ref[...].astype(F32) + attended
    norm_forward(pre, small[base + 3 : base + 4], small[base + 4 : base + 5], out_ref, hat_ref, rstd_ref)


def attend_backward_kernel(parts, cross, causal, base, *refs):
    refs = list(refs)
    tables = [refs.pop(0) for _ in range(parts)]
    query_seg = refs.pop(0)
    key_seg = refs.pop(0)
    small = refs.pop(0)
    grad_ref = refs.pop(0)
    hat_ref, rstd_ref = refs.pop(0), refs.pop(0)
    rows_ref = refs.pop(0)
    memory_ref = refs.pop(0) if cross else None
    q_ref, k_ref, v_ref, o_ref, lse_ref = [refs.pop(0) for _ in range(5)]
    near_far = [(refs.pop(0), refs.pop(0)) for _ in range(parts)]
    rows_out = refs.pop(0)
    memory_out = refs.pop(0) if cross else None
    small_out = refs.pop(0)
    keep_send = [(refs.pop(0), refs.pop(0)) for _ in range(parts)]
    w_ref, dw_ref, bias_ref, dout_ref, dq_t_ref, dk_ref, dv_ref, kt_ref, sems = refs
    step = QUAD // parts
    for part in range(parts):
        near, far = near_far[part]
        place = row_place(w_ref, part * step, (part + 1) * step)
        load_start(tables[part], near, far, place, sems.at[part])
    length, width = rows_ref.shape
    head = width // HEADS
    scale = head ** (-0.5)
    mask_fill(bias_ref, key_seg[...], query_seg[...], causal, True)
    kt_ref[...] = k_ref[...].T
    pre_grad, gain_grad, shift_grad = norm_backward(
        grad_ref[...], hat_ref[...], rstd_ref[:, :1], small[base + 3 : base + 4]
    )
    rows_out[...] = pre_grad
    low = pre_grad.astype(BF)
    for part in range(parts):
        near, far = near_far[part]
        load_wait(near, far, sems.at[part])
    dout_ref[...] = dot_nt(low, w_ref[3]).astype(BF)
    dw_ref[3] = dot(o_ref[...].T, low).astype(BF)
    out_bias = jnp.sum(low.astype(F32), axis=0, keepdims=True)
    product = dout_ref[...].astype(F32) * o_ref[...].astype(F32)
    high = product.astype(BF)
    rest = (product - high.astype(F32)).astype(BF)
    picker = lax.broadcasted_iota(jnp.int32, (BLOCK, width), 1) // head
    picker = (picker == lax.broadcasted_iota(jnp.int32, (BLOCK, width), 0)).astype(BF)
    row_dots = dot_nt(picker, high) + dot_nt(picker, rest)
    for pair in range(HEADS // 2):
        lanes = slice(pair * LANES, (pair + 1) * LANES)
        for at in range(0, length, LANES):
            begin = at if causal else 0
            query = q_ref[begin:, lanes]
            dout = dout_ref[begin:, lanes]
            scores = dot_nt(stacked_pair(k_ref[at : at + LANES, lanes]), query)
            prob_grad = dot_nt(stacked_pair(v_ref[at : at + LANES, lanes]), dout)
            bias = bias_ref[at : at + LANES, begin:]
            probs = []
            score_grads = []
            for part in range(2):
                which = 2 * pair + part
                half = slice(part * LANES, (part + 1) * LANES)
                prob = jnp.exp(scores[half] + (bias - lse_ref[which : which + 1, begin:]))
                probs.append(prob.astype(BF))
                row_dot = row_dots[which : which + 1, begin:]
                score_grads.append((prob * (prob_grad[half] - row_dot)).astype(BF))
                at_t = pair * LANES + part * head
                back = dot(kt_ref[at_t : at_t + head, at : at + LANES], score_grads[part])
                if at == 0:
                    dq_t_ref[at_t : at_t + head, :] = back
                else:
                    dq_t_ref[at_t : at_t + head, begin:] += back
            value_back = dot(jnp.concatenate(probs, axis=0), dout)
            dv_ref[at : at + LANES, lanes] = merged_pair(value_back).astype(BF)
            key_back = dot(jnp.concatenate(score_grads, axis=0), query)
            dk_ref[at : at + LANES, lanes] = merged_pair(key_back).astype(BF)
    query_grad = (dq_t_ref[...] * scale).T.astype(BF)
    key_grad = dk_ref[...]
    value_grad = dv_ref[...]
    turned = rows_ref[...].astype(BF).T
    dw_ref[0] = dot(turned, query_grad).astype(BF)
    if cross:
        turned = memory_ref[...].astype(BF).T
    dw_ref[1] = dot(turned, key_grad).astype(BF)
    dw_ref[2] = dot(turned, value_grad).astype(BF)
    for part in range(parts):
        keep, send = keep_send[part]
        place = row_place(dw_ref, part * step, (part + 1) * step)
        store_start(tables[part], keep, send, place, sems.at[part])
    rows_back = rows_out[...] + dot_nt(query_grad, w_ref[0])
    memory_back = dot_nt(key_grad, w_ref[1]) + dot_nt(value_grad, w_ref[2])
    if cross:
        rows_out[...] = rows_back
        memory_out[...] = memory_back
    else:
        rows_out[...] = rows_back + memory_back
    query_bias = jnp.sum(query_grad.astype(F32), axis=0, keepdims=True)
    value_bias = jnp.sum(value_grad.astype(F32), axis=0, keepdims=True)
    spare = jnp.zeros((3, width), F32)
    small_out[...] = jnp.concatenate(
        [query_bias, value_bias, out_bias, gain_grad, shift_grad, spare], axis=0
    )
    for part in range(parts):
        keep, send = keep_send[part]
        load_wait(keep, send, sems.at[part])


def gelu_parts(pre):
    inner = ROOT_TWO_PI * (pre + CUBIC * pre * pre * pre)
    curve = jnp.tanh(inner)
    return curve, 0.5 * pre * (1.0 + curve)


def gelu_slope(pre, curve):
    bend = ROOT_TWO_PI * (1.0 + 3.0 * CUBIC * pre * pre)
    return 0.5 * (1.0 + curve) + 0.5 * pre * (1.0 - curve * curve) * bend


def chunk_of(ref, index):
    number = ref.shape[0] // QUAD
    part = ref[index * number : (index + 1) * number]
    return part.reshape(number * ref.shape[1] * ref.shape[2], ref.shape[3])


def feed_forward_steps(small, base, hidden_at, rows_ref, up_ref, down_ref, pre_ref):
    rows = rows_ref[...].astype(BF)
    total = rows_ref[...] + small[base : base + 1]
    for index in range(QUAD):
        at = hidden_at + index
        pre = dot(rows, up_ref[index]) + small[at : at + 1]
        pre_ref[index] = pre
        active = gelu_parts(pre)[1].astype(BF)
        total = total + dot(active, chunk_of(down_ref, index))
    return total


def feed_backward_steps(pre_grad, rows_ref, up_ref, down_ref, pre_ref, dup_ref, ddown_ref, rows_out):
    low = pre_grad.astype(BF)
    turned = rows_ref[...].astype(BF).T
    total = pre_grad
    hidden_grads = []
    number = ddown_ref.shape[0] // QUAD
    for index in range(QUAD):
        pre = pre_ref[index]
        curve, active = gelu_parts(pre)
        down_grad = dot(active.astype(BF).T, low).astype(BF)
        ddown_ref[index * number : (index + 1) * number] = down_grad.reshape(
            (number,) + ddown_ref.shape[1:]
        )
        back = dot_nt(low, chunk_of(down_ref, index))
        hidden = (back * gelu_slope(pre, curve)).astype(BF)
        hidden_grads.append(jnp.sum(hidden.astype(F32), axis=0, keepdims=True))
        dup_ref[index] = dot(turned, hidden).astype(BF)
        total = total + dot_nt(hidden, up_ref[index])
    rows_out[...] = total
    out_bias = jnp.sum(low.astype(F32), axis=0, keepdims=True)
    return out_bias, hidden_grads


def load_feed(tables, near_far, up_ref, down_ref, sems):
    load_start(tables[0], *near_far[0], row_place(up_ref, 0, QUAD), sems.at[0])
    load_start(tables[1], *near_far[1], block_place(down_ref), sems.at[1])
    return [functools.partial(load_wait, *near_far[i], sems.at[i]) for i in range(2)]


def store_feed(tables, keep_send, dup_ref, ddown_ref, sems):
    store_start(tables[1], *keep_send[1], block_place(ddown_ref), sems.at[1])
    store_start(tables[0], *keep_send[0], row_place(dup_ref, 0, QUAD), sems.at[0])
    return [functools.partial(load_wait, *keep_send[i], sems.at[i]) for i in range(2)]


def feed_forward_kernel(base, hidden_at, *refs):
    table_a, table_b, small, rows_ref, near_a, far_a, near_b, far_b = refs[:8]
    out_ref, hat_ref, rstd_ref, pre_ref = refs[8:12]
    up_ref, down_ref, sems = refs[12:]
    for wait in load_feed((table_a, table_b), ((near_a, far_a), (near_b, far_b)), up_ref, down_ref, sems):
        wait()
    pre = feed_forward_steps(small, base, hidden_at, rows_ref, up_ref, down_ref, pre_ref)
    norm_forward(pre, small[base + 1 : base + 2], small[base + 2 : base + 3], out_ref, hat_ref, rstd_ref)


def feed_backward_kernel(base, *refs):
    table_a, table_b, small, grad_ref, hat_ref, rstd_ref, rows_ref, pre_ref = refs[:8]
    near_far = (refs[8:10], refs[10:12])
    rows_out, small_out = refs[12:14]
    keep_send = (refs[14:16], refs[16:18])
    up_ref, down_ref, dup_ref, ddown_ref, sems = refs[18:]
    tables = (table_a, table_b)
    waits = load_feed(tables, near_far, up_ref, down_ref, sems)
    pre_grad, gain_grad, shift_grad = norm_backward(
        grad_ref[...], hat_ref[...], rstd_ref[:, :1], small[base + 1 : base + 2]
    )
    for wait in waits:
        wait()
    out_bias, hidden_grads = feed_backward_steps(
        pre_grad, rows_ref, up_ref, down_ref, pre_ref, dup_ref, ddown_ref, rows_out
    )
    waits = store_feed(tables, keep_send, dup_ref, ddown_ref, sems)
    spare = jnp.zeros_like(out_bias)
    small_out[...] = jnp.concatenate(
        [out_bias, gain_grad, shift_grad] + hidden_grads + [spare], axis=0
    )
    for wait in waits:
        wait()


def feed_both_kernel(base, hidden_at, *refs):
    table_a, table_b, small, rows_ref, grad_ref = refs[:5]
    near_far = (refs[5:7], refs[7:9])
    out_ref, rows_out, small_out = refs[9:12]
    keep_send = (refs[12:14], refs[14:16])
    up_ref, down_ref, dup_ref, ddown_ref, pre_ref, hat_ref, rstd_ref, sems = refs[16:]
    tables = (table_a, table_b)
    for wait in load_feed(tables, near_far, up_ref, down_ref, sems):
        wait()
    pre = feed_forward_steps(small, base, hidden_at, rows_ref, up_ref, down_ref, pre_ref)
    gain = small[base + 1 : base + 2]
    norm_forward(pre, gain, small[base + 2 : base + 3], out_ref, hat_ref, rstd_ref)
    pre_grad, gain_grad, shift_grad = norm_backward(
        grad_ref[...].astype(F32), hat_ref[...], rstd_ref[:, :1], gain
    )
    out_bias, hidden_grads = feed_backward_steps(
        pre_grad, rows_ref, up_ref, down_ref, pre_ref, dup_ref, ddown_ref, rows_out
    )
    waits = store_feed(tables, keep_send, dup_ref, ddown_ref, sems)
    spare = jnp.zeros_like(out_bias)
    small_out[...] = jnp.concatenate(
        [out_bias, gain_grad, shift_grad] + hidden_grads + [spare], axis=0
    )
    for wait in waits:
        wait()


def shaped(shape, dtype=F32):
    return jax.ShapeDtypeStruct(shape, dtype)


def call(kernel, ins, specs, outs, out_specs, scratch, flops, moved):
    return pl.pallas_call(
        kernel,
        out_shape=outs,
        in_specs=specs,
        out_specs=out_specs,
        scratch_shapes=scratch,
        cost_estimate=pl.CostEstimate(flops=flops, bytes_accessed=moved, transcendentals=0),
        compiler_params=pltpu.CompilerParams(vmem_limit_bytes=40 * 1024 * 1024),
    )(*ins)


def half_shapes(weights):
    return [shaped(array.shape, BF) for pair in weights for array in pair]


def attend_forward(tables, segments, small, base, rows, memory, weights, causal):
    length, width = rows.shape
    parts = len(weights)
    cross = memory is not None
    ins = list(tables) + list(segments) + [small, rows] + ([memory] if cross else [])
    specs = [SMEM] * parts + [VMEM] * (len(ins) - parts)
    ins += [array for pair in weights for array in pair]
    specs += [ANY] * (2 * parts)
    outs = [shaped((length, width)), shaped((length, width)), shaped((length, LANES))]
    outs += [shaped((length, width), BF)] * 4 + [shaped((HEADS, length))]
    scratch = [
        pltpu.VMEM((QUAD, width, width), BF),
        pltpu.VMEM((length, length), F32),
        pltpu.SemaphoreType.DMA((parts, 2)),
    ]
    kernel = functools.partial(attend_forward_kernel, parts, cross, causal, base)
    flops = 8 * length * width * width + 16 * length * length * width
    return call(kernel, ins, specs, outs, [VMEM] * len(outs), scratch, flops, 8_000_000)


def attend_backward(tables, segments, small, base, grad, kept, rows, memory, weights, causal):
    length, width = rows.shape
    parts = len(weights)
    cross = memory is not None
    out, hat, rstd, q, k, v, o, lse = kept
    ins = list(tables) + list(segments) + [small, grad, hat, rstd, rows]
    ins += ([memory] if cross else []) + [q, k, v, o, lse]
    specs = [SMEM] * parts + [VMEM] * (len(ins) - parts)
    ins += [array for pair in weights for array in pair]
    specs += [ANY] * (2 * parts)
    outs = [shaped((length, width))] * (2 if cross else 1) + [shaped((8, width))]
    out_specs = [VMEM] * len(outs) + [ANY] * (2 * parts)
    outs += half_shapes(weights)
    scratch = [
        pltpu.VMEM((QUAD, width, width), BF),
        pltpu.VMEM((QUAD, width, width), BF),
        pltpu.VMEM((length, length), F32),
        pltpu.VMEM((length, width), BF),
        pltpu.VMEM((width, length), F32),
        pltpu.VMEM((length, width), BF),
        pltpu.VMEM((length, width), BF),
        pltpu.VMEM((width, length), BF),
        pltpu.SemaphoreType.DMA((parts, 2)),
    ]
    kernel = functools.partial(attend_backward_kernel, parts, cross, causal, base)
    flops = 16 * length * width * width + 40 * length * length * width
    results = call(kernel, ins, specs, outs, out_specs, scratch, flops, 12_000_000)
    results = list(results)
    rows_grad = results.pop(0)
    memory_grad = results.pop(0) if cross else None
    small_grad = results.pop(0)
    return rows_grad, memory_grad, small_grad, [results[2 * i : 2 * i + 2] for i in range(parts)]


def feed_scratch(width, grads):
    number = width // BLOCK
    once = [pltpu.VMEM((QUAD, width, width), BF), pltpu.VMEM((number, QUAD, BLOCK, width), BF)]
    return once * (2 if grads else 1)


def feed_forward(tables, small, base, hidden_at, rows, weights):
    length, width = rows.shape
    ins = list(tables) + [small, rows] + [array for pair in weights for array in pair]
    specs = [SMEM] * 2 + [VMEM] * 2 + [ANY] * 4
    outs = [shaped((length, width)), shaped((length, width)), shaped((length, LANES))]
    outs += [shaped((QUAD, length, width))]
    scratch = feed_scratch(width, False) + [pltpu.SemaphoreType.DMA((2, 2))]
    kernel = functools.partial(feed_forward_kernel, base, hidden_at)
    flops = 16 * length * width * width
    return call(kernel, ins, specs, outs, [VMEM] * len(outs), scratch, flops, 10_000_000)


def feed_backward(tables, small, base, grad, kept, rows, weights):
    length, width = rows.shape
    _, hat, rstd, pre = kept
    ins = list(tables) + [small, grad, hat, rstd, rows, pre]
    ins += [array for pair in weights for array in pair]
    specs = [SMEM] * 2 + [VMEM] * 6 + [ANY] * 4
    outs = [shaped((length, width)), shaped((8, width))] + half_shapes(weights)
    out_specs = [VMEM] * 2 + [ANY] * 4
    scratch = feed_scratch(width, True) + [pltpu.SemaphoreType.DMA((2, 2))]
    kernel = functools.partial(feed_backward_kernel, base)
    flops = 32 * length * width * width
    results = call(kernel, ins, specs, outs, out_specs, scratch, flops, 14_000_000)
    return results[0], results[1], [results[2:4], results[4:6]]


def feed_both(tables, small, base, hidden_at, rows, grad, weights):
    length, width = rows.shape
    ins = list(tables) + [small, rows, grad] + [array for pair in weights for array in pair]
    specs = [SMEM] * 2 + [VMEM] * 3 + [ANY] * 4
    outs = [shaped((length, width)), shaped((length, width)), shaped((8, width))]
    outs += half_shapes(weights)
    out_specs = [VMEM] * 3 + [ANY] * 4
    scratch = feed_scratch(width, True) + [
        pltpu.VMEM((QUAD, length, width), F32),
        pltpu.VMEM((length, width), F32),
        pltpu.VMEM((length, LANES), F32),
        pltpu.SemaphoreType.DMA((2, 2)),
    ]
    kernel = functools.partial(feed_both_kernel, base, hidden_at)
    flops = 48 * length * width * width
    results = call(kernel, ins, specs, outs, out_specs, scratch, flops, 12_000_000)
    return results[0], results[1], results[2], [results[3:5], results[5:7]]


def hop(array, bit, count):
    return lax.ppermute(array, AXES, [(place, place ^ (1 << bit)) for place in range(count)])


class Direct:
    def __init__(self, axis_sizes):
        outer, inner = axis_sizes
        self.count = outer * inner
        inner_bits = inner.bit_length() - 1
        bits = self.count.bit_length() - 1
        self.core = inner_bits
        across = list(range(inner_bits + 1, bits))
        up = [0]
        along = list(range(1, inner_bits))
        self.orders = ([self.core] + across + up + along, [self.core] + up + across + along)
        self.tail = len(along)
        self.place = lax.axis_index(AXES)

    def tables(self):
        made = []
        for order in self.orders:
            index = jnp.arange(self.count, dtype=jnp.int32)
            block = jnp.zeros_like(index)
            for at, bit in enumerate(order):
                block = block | (((index >> (len(order) - 1 - at)) & 1) << bit)
            made.append(block ^ self.place)
        return made

    def gather_tail(self, array):
        for bit in self.orders[0][::-1][: self.tail]:
            array = jnp.concatenate([array, hop(array, bit, self.count)], axis=0)
        return array

    def gather_rest(self, array, which):
        for bit in self.orders[which][1:][::-1][self.tail :]:
            array = jnp.concatenate([array, hop(array, bit, self.count)], axis=0)
        return array, hop(array, self.core, self.count)

    def halve(self, keep, send, bit):
        total = keep.astype(F32) + hop(send, bit, self.count).astype(F32)
        half = total.shape[0] // 2
        if half == 0:
            return total
        return total[:half].astype(BF), total[half:].astype(BF)

    def scatter_rest(self, keep, send, which):
        for bit in self.orders[which][: len(self.orders[which]) - self.tail]:
            keep, send = self.halve(keep, send, bit)
        return keep, send

    def scatter_tail(self, pairs):
        keep = jnp.concatenate([pair[0] for pair in pairs], axis=1)
        send = jnp.concatenate([pair[1] for pair in pairs], axis=1)
        for bit in self.orders[0][-self.tail : -1]:
            keep, send = self.halve(keep, send, bit)
        return self.halve(keep, send, self.orders[0][-1])[0]


def sum_all(array, count):
    for bit in range(count.bit_length() - 1):
        array = array + hop(array, bit, count)
    return array


def adam_update(weight, gradient, first, second, rate, decay):
    first_new = BETA_ONE * first + (1.0 - BETA_ONE) * gradient
    second_new = BETA_TWO * second + (1.0 - BETA_TWO) * gradient * gradient
    first_hat = first_new / (1.0 - BETA_ONE**STEP)
    second_hat = second_new / (1.0 - BETA_TWO**STEP)
    weight_new = weight - rate * (first_hat / (jnp.sqrt(second_hat) + EPS_ADAM) + decay * weight)
    return (weight_new, first_new, second_new, weight_new.astype(BF))


def spread(piece, place, count):
    rows, lanes = piece.shape
    lane = lax.broadcasted_iota(jnp.int32, (rows, lanes * count), 1) // lanes
    return jnp.where(lane == place, jnp.tile(piece, (1, count)), jnp.zeros((), piece.dtype))


def gather_small(vectors, hidden, place, count, width):
    whole = spread(vectors.astype(BF), place, count)
    deep = spread(hidden.astype(BF), place, count).reshape(-1, width)
    spare = jnp.zeros((SMALL_ROWS - whole.shape[0] - deep.shape[0], width), BF)
    return sum_all(jnp.concatenate([whole, deep, spare], axis=0), count).astype(F32)


def scatter_small(grads, vectors, hidden, place, count):
    enc_attend, enc_feed, self_attend, cross_attend, dec_feed = grads
    whole = jnp.concatenate(
        [
            enc_attend[:5],
            enc_feed[:3],
            self_attend[:5],
            cross_attend[:5],
            dec_feed[:3],
            enc_feed[3:7],
            dec_feed[3:7],
            enc_feed[7:],
            dec_feed[7:],
            dec_feed[7:],
        ],
        axis=0,
    )
    whole = sum_all(whole, count)
    rows, lanes = vectors.shape
    first = lax.dynamic_slice_in_dim(whole[:rows], place * lanes, lanes, axis=1)
    layers, lanes = hidden.shape
    deep = whole[rows : rows + 2 * QUAD].reshape(layers, -1)
    return first, lax.dynamic_slice_in_dim(deep, place * lanes, lanes, axis=1)


def gather_whole(attention, up, down):
    width = attention.shape[2]
    number = width // BLOCK
    square = lax.all_gather(attention, AXES, axis=1, tiled=True)
    square = square.reshape(-1, QUAD, number, BLOCK, width).transpose(0, 2, 1, 3, 4)
    tall = lax.all_gather(up, AXES, axis=1, tiled=True)
    tall = tall.reshape(2, number, BLOCK, QUAD, width).transpose(0, 1, 3, 2, 4)
    deep = lax.all_gather(down, AXES, axis=1, tiled=True).reshape(2, number, QUAD, BLOCK, width)
    half = number // 2
    quads = [square[0], tall[0], deep[0], square[1], square[2], tall[1], deep[1]]
    return [(quad[:half], quad[half:]) for quad in quads]


def scatter_whole(quads):
    joined = [jnp.concatenate(pair, axis=0).astype(F32) for pair in quads]
    number, _, _, width = joined[0].shape
    square = jnp.stack([joined[0], joined[3], joined[4]])
    square = square.transpose(0, 2, 1, 3, 4).reshape(3 * QUAD, width, width)
    tall = jnp.stack([joined[1], joined[5]]).transpose(0, 1, 3, 2, 4)
    tall = tall.reshape(2, width, QUAD * width)
    deep = jnp.stack([joined[2], joined[6]]).reshape(2, QUAD * width, width)
    return [
        lax.psum_scatter(part, AXES, scatter_dimension=1, tiled=True)
        for part in (square, tall, deep)
    ]


def per_device(
    axis_sizes,
    source_tokens,
    target_tokens,
    source_segments,
    target_segments,
    output_grad,
    attention_weight,
    up_weight,
    down_weight,
    vectors,
    hidden_bias,
    *moments,
):
    masters = (attention_weight, up_weight, down_weight, vectors, hidden_bias)
    firsts = moments[:5]
    seconds = moments[5:]
    source = source_tokens[0]
    target = target_tokens[0]
    width = source.shape[1]
    count = axis_sizes[0] * axis_sizes[1]
    place = lax.axis_index(AXES)
    direct = count * BLOCK == width
    small = gather_small(vectors, hidden_bias, place, count, width)
    attention = attention_weight.astype(BF)
    up = up_weight.astype(BF)
    down = down_weight.astype(BF)
    if direct:
        net = Direct(axis_sizes)
        table_a, table_b = net.tables()
        square = attention.reshape(3, 1, QUAD, BLOCK, width)
        tall = up.reshape(2, 1, BLOCK, QUAD, width).transpose(0, 1, 3, 2, 4)
        deep = down.reshape(2, 1, QUAD, BLOCK, width)
        first = net.gather_tail(square[0])
        cut = QUAD // 2
        enc_attend_w = [net.gather_rest(first[:, :cut], 0), net.gather_rest(first[:, cut:], 1)]
        second = net.gather_tail(jnp.concatenate([tall[0], deep[0]], axis=1))
        enc_feed_w = [net.gather_rest(second[:, :QUAD], 0), net.gather_rest(second[:, QUAD:], 1)]
        third = net.gather_tail(jnp.concatenate([square[1], square[2]], axis=1))
        self_w = [net.gather_rest(third[:, :QUAD], 0)]
        cross_w = [net.gather_rest(third[:, QUAD:], 1)]
        fourth = net.gather_tail(jnp.concatenate([tall[1], deep[1]], axis=1))
        dec_feed_w = [net.gather_rest(fourth[:, :QUAD], 0), net.gather_rest(fourth[:, QUAD:], 1)]
    else:
        quads = gather_whole(attention, up, down)
        table_a = table_b = jnp.arange(width // BLOCK, dtype=jnp.int32)
        enc_attend_w, self_w, cross_w = [quads[0]], [quads[3]], [quads[4]]
        enc_feed_w, dec_feed_w = quads[1:3], quads[5:7]
    both = (table_a, table_b)
    enc_tables = both[: len(enc_attend_w)]
    source_pair = (source_segments, source_segments)
    target_pair = (target_segments, target_segments)
    cross_pair = (target_segments, source_segments)

    enc_kept = attend_forward(enc_tables, source_pair, small, 0, source, None, enc_attend_w, False)
    enc_mid = enc_kept[0]
    enc_feed_kept = feed_forward(both, small, 5, HIDDEN_ROW, enc_mid, enc_feed_w)
    memory = enc_feed_kept[0]
    self_kept = attend_forward((table_a,), target_pair, small, 8, target, None, self_w, True)
    dec_one = self_kept[0]
    cross_kept = attend_forward((table_b,), cross_pair, small, 13, dec_one, memory, cross_w, False)
    dec_two = cross_kept[0]
    result, two_grad, dec_feed_small, dec_feed_q = feed_both(
        both, small, 18, HIDDEN_ROW + QUAD, dec_two, output_grad[0], dec_feed_w
    )
    one_grad, memory_grad, cross_small, cross_q = attend_backward(
        (table_b,), cross_pair, small, 13, two_grad, cross_kept, dec_one, memory, cross_w, False
    )
    target_grad, _, self_small, self_q = attend_backward(
        (table_a,), target_pair, small, 8, one_grad, self_kept, target, None, self_w, True
    )
    mid_grad, enc_feed_small, enc_feed_q = feed_backward(
        both, small, 5, memory_grad, enc_feed_kept, enc_mid, enc_feed_w
    )
    source_grad, _, enc_small, enc_q = attend_backward(
        enc_tables, source_pair, small, 0, mid_grad, enc_kept, source, None, enc_attend_w, False
    )

    if direct:
        dec_feed_s = [net.scatter_rest(*dec_feed_q[1], 1), net.scatter_rest(*dec_feed_q[0], 0)]
        down_dec, up_dec = jnp.split(net.scatter_tail(dec_feed_s), 2, axis=0)
        attend_s = [net.scatter_rest(*cross_q[0], 1), net.scatter_rest(*self_q[0], 0)]
        cross_g, self_g = jnp.split(net.scatter_tail(attend_s), 2, axis=0)
        enc_feed_s = [net.scatter_rest(*enc_feed_q[1], 1), net.scatter_rest(*enc_feed_q[0], 0)]
        down_enc, up_enc = jnp.split(net.scatter_tail(enc_feed_s), 2, axis=0)
        enc_s = [net.scatter_rest(*enc_q[0], 0), net.scatter_rest(*enc_q[1], 1)]
        enc_g = net.scatter_tail(enc_s)
        square_g = jnp.concatenate([enc_g, self_g, cross_g], axis=0)
        tall_g = jnp.stack([up_enc, up_dec]).transpose(0, 2, 1, 3).reshape(up_weight.shape)
        deep_g = jnp.stack([down_enc, down_dec]).reshape(down_weight.shape)
    else:
        quads = [enc_q[0], enc_feed_q[0], enc_feed_q[1], self_q[0], cross_q[0]] + dec_feed_q
        square_g, tall_g, deep_g = scatter_whole(quads)
    small_grads = (enc_small, enc_feed_small, self_small, cross_small, dec_feed_small)
    vector_g, hidden_g = scatter_small(small_grads, vectors, hidden_bias, place, count)

    grads = (square_g, tall_g, deep_g, vector_g, hidden_g)
    updated = [
        adam_update(
            masters[slot], grads[slot], firsts[slot], seconds[slot], RATES[slot], DECAYS[slot]
        )
        for slot in range(5)
    ]
    tokens = (memory[None], result[None], source_grad[None], target_grad[None])
    return tokens + tuple(updated[slot][kind] for kind in range(4) for slot in range(5))


def solution(mesh):
    rows = P(AXES, None, None)
    line = P(AXES, None)
    matrix = P(None, AXES, None)
    vector = P(None, AXES)
    state = (matrix, matrix, matrix, vector, vector)
    return jax.shard_map(
        functools.partial(per_device, (mesh.shape["dp"], mesh.shape["fsdp"])),
        mesh=mesh,
        in_specs=(rows, rows, line, line, rows) + state * 3,
        out_specs=(rows,) * 4 + state * 4,
        check_vma=False,
    )
```

```python
import functools

import jax
import jax.numpy as jnp
from jax import lax
from jax.experimental import pallas as pl
from jax.experimental.pallas import tpu as pltpu
from jax.sharding import PartitionSpec as P

HEADS = 8
STEP = 10
EPS_NORM = 1e-05
EPS_ADAM = 1e-08
BETA_ONE = 0.9
BETA_TWO = 0.999
LOWEST = -1e30
RATES = (0.05, 0.05, 0.05, 0.3, 0.3)
DECAYS = (0.01, 0.01, 0.01, 0.0, 0.0)
AXES = ("dp", "fsdp")
QUAD = 4
BLOCK = 16
LANES = 128
SMALL_ROWS = 32
HIDDEN_ROW = 21
BF = jnp.bfloat16
F32 = jnp.float32
VMEM = pl.BlockSpec(memory_space=pltpu.VMEM)
SMEM = pl.BlockSpec(memory_space=pltpu.SMEM)
ANY = pl.BlockSpec(memory_space=pl.ANY)
ROOT_TWO_PI = 0.7978845608028654
CUBIC = 0.044715


def dot(left, right):
    return jnp.dot(left, right, preferred_element_type=F32)


def dot_nt(left, right):
    return lax.dot_general(left, right, (((1,), (1,)), ((), ())), preferred_element_type=F32)


def load_start(table, near, far, place, sems):
    half = near.shape[0]
    for index in range(half):
        pltpu.make_async_copy(near.at[index], place(table[index]), sems.at[0]).start()
        pltpu.make_async_copy(far.at[index], place(table[half + index]), sems.at[1]).start()


def load_wait(near, far, sems):
    pltpu.make_async_copy(near, near, sems.at[0]).wait()
    pltpu.make_async_copy(far, far, sems.at[1]).wait()


def store_start(table, keep, send, place, sems):
    half = keep.shape[0]
    for index in range(half):
        pltpu.make_async_copy(place(table[half + index]), send.at[index], sems.at[1]).start()
        pltpu.make_async_copy(place(table[index]), keep.at[index], sems.at[0]).start()


def row_place(scratch, low, high):
    def place(block):
        start = pl.multiple_of(block * BLOCK, BLOCK)
        return scratch.at[low:high, pl.ds(start, BLOCK), :]

    return place


def block_place(scratch):
    return lambda block: scratch.at[block]


def norm_forward(pre, gain, shift, out_ref, hat_ref, rstd_ref):
    mean = jnp.mean(pre, axis=-1, keepdims=True)
    centred = pre - mean
    spread = jnp.mean(centred * centred, axis=-1, keepdims=True)
    rstd = lax.rsqrt(spread + EPS_NORM)
    hat = centred * rstd
    hat_ref[...] = hat
    rstd_ref[...] = jnp.broadcast_to(rstd, rstd_ref.shape)
    out_ref[...] = hat * gain + shift


def norm_backward(grad, hat, rstd, gain):
    gain_grad = jnp.sum(grad * hat, axis=0, keepdims=True)
    shift_grad = jnp.sum(grad, axis=0, keepdims=True)
    scaled = grad * gain
    one = jnp.mean(scaled, axis=-1, keepdims=True)
    two = jnp.mean(scaled * hat, axis=-1, keepdims=True)
    return rstd * (scaled - one - hat * two), gain_grad, shift_grad


def lane_mask(rows):
    return lax.broadcasted_iota(jnp.int32, (rows, LANES), 1) < LANES // 2


def stacked_pair(block):
    first = lane_mask(block.shape[0])
    zero = jnp.zeros_like(block)
    return jnp.concatenate([jnp.where(first, block, zero), jnp.where(first, zero, block)], axis=0)


def merged_pair(stacked):
    rows = stacked.shape[0] // 2
    return jnp.where(lane_mask(rows), stacked[:rows], stacked[rows:])


def mask_fill(bias_ref, column_seg, row_seg, causal, transposed):
    length = bias_ref.shape[0]
    column = jnp.broadcast_to(column_seg, (LANES, length)).T
    for at in range(0, length, LANES):
        same = column == row_seg[:, at : at + LANES]
        if causal:
            down = lax.broadcasted_iota(jnp.int32, (length, LANES), 0)
            along = lax.broadcasted_iota(jnp.int32, (length, LANES), 1) + at
            order = (down <= along) if transposed else (along <= down)
            same = same & order
        bias_ref[:, at : at + LANES] = jnp.where(same, 0.0, LOWEST)


def attend_forward_kernel(parts, cross, causal, base, *refs):
    refs = list(refs)
    tables = [refs.pop(0) for _ in range(parts)]
    query_seg = refs.pop(0)
    key_seg = refs.pop(0)
    small = refs.pop(0)
    rows_ref = refs.pop(0)
    memory_ref = refs.pop(0) if cross else None
    near_far = [(refs.pop(0), refs.pop(0)) for _ in range(parts)]
    out_ref, hat_ref, rstd_ref, q_ref, k_ref, v_ref, o_ref, lse_ref = refs[:8]
    w_ref, bias_ref, sems = refs[8:]
    step = QUAD // parts
    for part in range(parts):
        near, far = near_far[part]
        place = row_place(w_ref, part * step, (part + 1) * step)
        load_start(tables[part], near, far, place, sems.at[part])
    length, width = rows_ref.shape
    mask_fill(bias_ref, query_seg[...], key_seg[...], causal, False)
    rows = rows_ref[...].astype(BF)
    keys = memory_ref[...].astype(BF) if cross else rows
    for part in range(parts):
        near, far = near_far[part]
        load_wait(near, far, sems.at[part])
    scale = (width // HEADS) ** (-0.5)
    q_ref[...] = (dot(rows, w_ref[0]) + small[base : base + 1]).astype(BF) * jnp.asarray(scale, BF)
    k_ref[...] = dot(keys, w_ref[1]).astype(BF)
    v_ref[...] = (dot(keys, w_ref[2]) + small[base + 1 : base + 2]).astype(BF)
    lane = lax.broadcasted_iota(jnp.int32, (LANES, LANES), 1)
    for at in range(0, length, LANES):
        reach = at + LANES if causal else length
        logs = jnp.zeros((LANES, LANES), F32)
        for pair in range(HEADS // 2):
            lanes = slice(pair * LANES, (pair + 1) * LANES)
            stacked = stacked_pair(q_ref[at : at + LANES, lanes])
            scores = dot_nt(stacked, k_ref[:reach, lanes])
            bias = bias_ref[at : at + LANES, :reach]
            scores = scores + jnp.concatenate([bias, bias], axis=0)
            largest = jnp.max(scores, axis=-1, keepdims=True)
            exponent = jnp.exp(scores - largest).astype(BF)
            values = jnp.concatenate([v_ref[:reach, lanes], jnp.ones((reach, LANES), BF)], axis=1)
            mixed = dot(exponent, values)
            total = mixed[:, LANES:]
            o_ref[at : at + LANES, lanes] = merged_pair(mixed[:, :LANES] / total).astype(BF)
            log_total = largest + jnp.log(total)
            logs = jnp.where(lane == 2 * pair, log_total[:LANES], logs)
            logs = jnp.where(lane == 2 * pair + 1, log_total[LANES:], logs)
        lse_ref[:, at : at + LANES] = logs.T[:HEADS]
    attended = dot(o_ref[...], w_ref[3]) + small[base + 2 : base + 3]
    pre = rows_ref[...].astype(F32) + attended
    norm_forward(pre, small[base + 3 : base + 4], small[base + 4 : base + 5], out_ref, hat_ref, rstd_ref)


def attend_backward_kernel(parts, cross, causal, base, *refs):
    refs = list(refs)
    tables = [refs.pop(0) for _ in range(parts)]
    query_seg = refs.pop(0)
    key_seg = refs.pop(0)
    small = refs.pop(0)
    grad_ref = refs.pop(0)
    hat_ref, rstd_ref = refs.pop(0), refs.pop(0)
    rows_ref = refs.pop(0)
    memory_ref = refs.pop(0) if cross else None
    q_ref, k_ref, v_ref, o_ref, lse_ref = [refs.pop(0) for _ in range(5)]
    near_far = [(refs.pop(0), refs.pop(0)) for _ in range(parts)]
    rows_out = refs.pop(0)
    memory_out = refs.pop(0) if cross else None
    small_out = refs.pop(0)
    keep_send = [(refs.pop(0), refs.pop(0)) for _ in range(parts)]
    w_ref, dw_ref, bias_ref, dout_ref, dq_t_ref, dk_ref, dv_ref, kt_ref, sems = refs
    step = QUAD // parts
    for part in range(parts):
        near, far = near_far[part]
        place = row_place(w_ref, part * step, (part + 1) * step)
        load_start(tables[part], near, far, place, sems.at[part])
    length, width = rows_ref.shape
    head = width // HEADS
    scale = head ** (-0.5)
    mask_fill(bias_ref, key_seg[...], query_seg[...], causal, True)
    kt_ref[...] = k_ref[...].T
    pre_grad, gain_grad, shift_grad = norm_backward(
        grad_ref[...], hat_ref[...], rstd_ref[:, :1], small[base + 3 : base + 4]
    )
    rows_out[...] = pre_grad
    low = pre_grad.astype(BF)
    for part in range(parts):
        near, far = near_far[part]
        load_wait(near, far, sems.at[part])
    dout_ref[...] = dot_nt(low, w_ref[3]).astype(BF)
    dw_ref[3] = dot(o_ref[...].T, low).astype(BF)
    out_bias = jnp.sum(low.astype(F32), axis=0, keepdims=True)
    product = dout_ref[...].astype(F32) * o_ref[...].astype(F32)
    high = product.astype(BF)
    rest = (product - high.astype(F32)).astype(BF)
    picker = lax.broadcasted_iota(jnp.int32, (BLOCK, width), 1) // head
    picker = (picker == lax.broadcasted_iota(jnp.int32, (BLOCK, width), 0)).astype(BF)
    row_dots = dot_nt(picker, high) + dot_nt(picker, rest)
    for pair in range(HEADS // 2):
        lanes = slice(pair * LANES, (pair + 1) * LANES)
        for at in range(0, length, LANES):
            begin = at if causal else 0
            query = q_ref[begin:, lanes]
            dout = dout_ref[begin:, lanes]
            scores = dot_nt(stacked_pair(k_ref[at : at + LANES, lanes]), query)
            prob_grad = dot_nt(stacked_pair(v_ref[at : at + LANES, lanes]), dout)
            bias = bias_ref[at : at + LANES, begin:]
            probs = []
            score_grads = []
            for part in range(2):
                which = 2 * pair + part
                half = slice(part * LANES, (part + 1) * LANES)
                prob = jnp.exp(scores[half] + (bias - lse_ref[which : which + 1, begin:]))
                probs.append(prob.astype(BF))
                row_dot = row_dots[which : which + 1, begin:]
                score_grads.append((prob * (prob_grad[half] - row_dot)).astype(BF))
                at_t = pair * LANES + part * head
                back = dot(kt_ref[at_t : at_t + head, at : at + LANES], score_grads[part])
                if at == 0:
                    dq_t_ref[at_t : at_t + head, :] = back
                else:
                    dq_t_ref[at_t : at_t + head, begin:] += back
            value_back = dot(jnp.concatenate(probs, axis=0), dout)
            dv_ref[at : at + LANES, lanes] = merged_pair(value_back).astype(BF)
            key_back = dot(jnp.concatenate(score_grads, axis=0), query)
            dk_ref[at : at + LANES, lanes] = merged_pair(key_back).astype(BF)
    query_grad = (dq_t_ref[...] * scale).T.astype(BF)
    key_grad = dk_ref[...]
    value_grad = dv_ref[...]
    turned = rows_ref[...].astype(BF).T
    dw_ref[0] = dot(turned, query_grad).astype(BF)
    if cross:
        turned = memory_ref[...].astype(BF).T
    dw_ref[1] = dot(turned, key_grad).astype(BF)
    dw_ref[2] = dot(turned, value_grad).astype(BF)
    for part in range(parts):
        keep, send = keep_send[part]
        place = row_place(dw_ref, part * step, (part + 1) * step)
        store_start(tables[part], keep, send, place, sems.at[part])
    rows_back = rows_out[...] + dot_nt(query_grad, w_ref[0])
    memory_back = dot_nt(key_grad, w_ref[1]) + dot_nt(value_grad, w_ref[2])
    if cross:
        rows_out[...] = rows_back
        memory_out[...] = memory_back
    else:
        rows_out[...] = rows_back + memory_back
    query_bias = jnp.sum(query_grad.astype(F32), axis=0, keepdims=True)
    value_bias = jnp.sum(value_grad.astype(F32), axis=0, keepdims=True)
    spare = jnp.zeros((3, width), F32)
    small_out[...] = jnp.concatenate(
        [query_bias, value_bias, out_bias, gain_grad, shift_grad, spare], axis=0
    )
    for part in range(parts):
        keep, send = keep_send[part]
        load_wait(keep, send, sems.at[part])


def gelu_parts(pre):
    inner = ROOT_TWO_PI * (pre + CUBIC * pre * pre * pre)
    curve = jnp.tanh(inner)
    return curve, 0.5 * pre * (1.0 + curve)


def gelu_slope(pre, curve):
    bend = ROOT_TWO_PI * (1.0 + 3.0 * CUBIC * pre * pre)
    return 0.5 * (1.0 + curve) + 0.5 * pre * (1.0 - curve * curve) * bend


def chunk_of(ref, index):
    number = ref.shape[0] // QUAD
    part = ref[index * number : (index + 1) * number]
    return part.reshape(number * ref.shape[1] * ref.shape[2], ref.shape[3])


def feed_forward_steps(small, base, hidden_at, rows_ref, up_ref, down_ref, pre_ref):
    rows = rows_ref[...].astype(BF)
    total = rows_ref[...] + small[base : base + 1]
    for index in range(QUAD):
        at = hidden_at + index
        pre = dot(rows, up_ref[index]) + small[at : at + 1]
        pre_ref[index] = pre
        active = gelu_parts(pre)[1].astype(BF)
        total = total + dot(active, chunk_of(down_ref, index))
    return total


def feed_backward_steps(pre_grad, rows_ref, up_ref, down_ref, pre_ref, dup_ref, ddown_ref, rows_out):
    low = pre_grad.astype(BF)
    turned = rows_ref[...].astype(BF).T
    total = pre_grad
    hidden_grads = []
    number = ddown_ref.shape[0] // QUAD
    for index in range(QUAD):
        pre = pre_ref[index]
        curve, active = gelu_parts(pre)
        down_grad = dot(active.astype(BF).T, low).astype(BF)
        ddown_ref[index * number : (index + 1) * number] = down_grad.reshape(
            (number,) + ddown_ref.shape[1:]
        )
        back = dot_nt(low, chunk_of(down_ref, index))
        hidden = (back * gelu_slope(pre, curve)).astype(BF)
        hidden_grads.append(jnp.sum(hidden.astype(F32), axis=0, keepdims=True))
        dup_ref[index] = dot(turned, hidden).astype(BF)
        total = total + dot_nt(hidden, up_ref[index])
    rows_out[...] = total
    out_bias = jnp.sum(low.astype(F32), axis=0, keepdims=True)
    return out_bias, hidden_grads


def load_feed(tables, near_far, up_ref, down_ref, sems):
    load_start(tables[0], *near_far[0], row_place(up_ref, 0, QUAD), sems.at[0])
    load_start(tables[1], *near_far[1], block_place(down_ref), sems.at[1])
    return [functools.partial(load_wait, *near_far[i], sems.at[i]) for i in range(2)]


def store_feed(tables, keep_send, dup_ref, ddown_ref, sems):
    store_start(tables[1], *keep_send[1], block_place(ddown_ref), sems.at[1])
    store_start(tables[0], *keep_send[0], row_place(dup_ref, 0, QUAD), sems.at[0])
    return [functools.partial(load_wait, *keep_send[i], sems.at[i]) for i in range(2)]


def feed_forward_kernel(base, hidden_at, *refs):
    table_a, table_b, small, rows_ref, near_a, far_a, near_b, far_b = refs[:8]
    out_ref, hat_ref, rstd_ref, pre_ref = refs[8:12]
    up_ref, down_ref, sems = refs[12:]
    for wait in load_feed((table_a, table_b), ((near_a, far_a), (near_b, far_b)), up_ref, down_ref, sems):
        wait()
    pre = feed_forward_steps(small, base, hidden_at, rows_ref, up_ref, down_ref, pre_ref)
    norm_forward(pre, small[base + 1 : base + 2], small[base + 2 : base + 3], out_ref, hat_ref, rstd_ref)


def feed_backward_kernel(base, *refs):
    tables, out_tables, refs = refs[:2], refs[2:4], refs[4:]
    small, grad_ref, hat_ref, rstd_ref, rows_ref, pre_ref = refs[:6]
    near_far = (refs[6:8], refs[8:10])
    rows_out, small_out = refs[10:12]
    keep_send = (refs[12:14], refs[14:16])
    up_ref, down_ref, dup_ref, ddown_ref, sems = refs[16:]
    waits = load_feed(tables, near_far, up_ref, down_ref, sems)
    pre_grad, gain_grad, shift_grad = norm_backward(
        grad_ref[...], hat_ref[...], rstd_ref[:, :1], small[base + 1 : base + 2]
    )
    for wait in waits:
        wait()
    out_bias, hidden_grads = feed_backward_steps(
        pre_grad, rows_ref, up_ref, down_ref, pre_ref, dup_ref, ddown_ref, rows_out
    )
    waits = store_feed(out_tables, keep_send, dup_ref, ddown_ref, sems)
    spare = jnp.zeros_like(out_bias)
    small_out[...] = jnp.concatenate(
        [out_bias, gain_grad, shift_grad] + hidden_grads + [spare], axis=0
    )
    for wait in waits:
        wait()


def feed_both_kernel(base, hidden_at, *refs):
    tables, out_tables, refs = refs[:2], refs[2:4], refs[4:]
    small, rows_ref, grad_ref = refs[:3]
    near_far = (refs[3:5], refs[5:7])
    out_ref, rows_out, small_out = refs[7:10]
    keep_send = (refs[10:12], refs[12:14])
    up_ref, down_ref, dup_ref, ddown_ref, pre_ref, hat_ref, rstd_ref, sems = refs[14:]
    for wait in load_feed(tables, near_far, up_ref, down_ref, sems):
        wait()
    pre = feed_forward_steps(small, base, hidden_at, rows_ref, up_ref, down_ref, pre_ref)
    gain = small[base + 1 : base + 2]
    norm_forward(pre, gain, small[base + 2 : base + 3], out_ref, hat_ref, rstd_ref)
    pre_grad, gain_grad, shift_grad = norm_backward(
        grad_ref[...].astype(F32), hat_ref[...], rstd_ref[:, :1], gain
    )
    out_bias, hidden_grads = feed_backward_steps(
        pre_grad, rows_ref, up_ref, down_ref, pre_ref, dup_ref, ddown_ref, rows_out
    )
    waits = store_feed(out_tables, keep_send, dup_ref, ddown_ref, sems)
    spare = jnp.zeros_like(out_bias)
    small_out[...] = jnp.concatenate(
        [out_bias, gain_grad, shift_grad] + hidden_grads + [spare], axis=0
    )
    for wait in waits:
        wait()


def shaped(shape, dtype=F32):
    return jax.ShapeDtypeStruct(shape, dtype)


def call(kernel, ins, specs, outs, out_specs, scratch, flops, moved):
    return pl.pallas_call(
        kernel,
        out_shape=outs,
        in_specs=specs,
        out_specs=out_specs,
        scratch_shapes=scratch,
        cost_estimate=pl.CostEstimate(flops=flops, bytes_accessed=moved, transcendentals=0),
        compiler_params=pltpu.CompilerParams(vmem_limit_bytes=40 * 1024 * 1024),
    )(*ins)


def half_shapes(weights):
    return [shaped(array.shape, BF) for pair in weights for array in pair]


def attend_forward(tables, segments, small, base, rows, memory, weights, causal):
    length, width = rows.shape
    parts = len(weights)
    cross = memory is not None
    ins = list(tables) + list(segments) + [small, rows] + ([memory] if cross else [])
    specs = [SMEM] * parts + [VMEM] * (len(ins) - parts)
    ins += [array for pair in weights for array in pair]
    specs += [ANY] * (2 * parts)
    outs = [shaped((length, width)), shaped((length, width)), shaped((length, LANES))]
    outs += [shaped((length, width), BF)] * 4 + [shaped((HEADS, length))]
    scratch = [
        pltpu.VMEM((QUAD, width, width), BF),
        pltpu.VMEM((length, length), F32),
        pltpu.SemaphoreType.DMA((parts, 2)),
    ]
    kernel = functools.partial(attend_forward_kernel, parts, cross, causal, base)
    flops = 8 * length * width * width + 16 * length * length * width
    return call(kernel, ins, specs, outs, [VMEM] * len(outs), scratch, flops, 8_000_000)


def attend_backward(tables, segments, small, base, grad, kept, rows, memory, weights, causal):
    length, width = rows.shape
    parts = len(weights)
    cross = memory is not None
    out, hat, rstd, q, k, v, o, lse = kept
    ins = list(tables) + list(segments) + [small, grad, hat, rstd, rows]
    ins += ([memory] if cross else []) + [q, k, v, o, lse]
    specs = [SMEM] * parts + [VMEM] * (len(ins) - parts)
    ins += [array for pair in weights for array in pair]
    specs += [ANY] * (2 * parts)
    outs = [shaped((length, width))] * (2 if cross else 1) + [shaped((8, width))]
    out_specs = [VMEM] * len(outs) + [ANY] * (2 * parts)
    outs += half_shapes(weights)
    scratch = [
        pltpu.VMEM((QUAD, width, width), BF),
        pltpu.VMEM((QUAD, width, width), BF),
        pltpu.VMEM((length, length), F32),
        pltpu.VMEM((length, width), BF),
        pltpu.VMEM((width, length), F32),
        pltpu.VMEM((length, width), BF),
        pltpu.VMEM((length, width), BF),
        pltpu.VMEM((width, length), BF),
        pltpu.SemaphoreType.DMA((parts, 2)),
    ]
    kernel = functools.partial(attend_backward_kernel, parts, cross, causal, base)
    flops = 16 * length * width * width + 40 * length * length * width
    results = call(kernel, ins, specs, outs, out_specs, scratch, flops, 12_000_000)
    results = list(results)
    rows_grad = results.pop(0)
    memory_grad = results.pop(0) if cross else None
    small_grad = results.pop(0)
    return rows_grad, memory_grad, small_grad, [results[2 * i : 2 * i + 2] for i in range(parts)]


def feed_scratch(width, grads):
    number = width // BLOCK
    once = [pltpu.VMEM((QUAD, width, width), BF), pltpu.VMEM((number, QUAD, BLOCK, width), BF)]
    return once * (2 if grads else 1)


def feed_forward(tables, small, base, hidden_at, rows, weights):
    length, width = rows.shape
    ins = list(tables) + [small, rows] + [array for pair in weights for array in pair]
    specs = [SMEM] * 2 + [VMEM] * 2 + [ANY] * 4
    outs = [shaped((length, width)), shaped((length, width)), shaped((length, LANES))]
    outs += [shaped((QUAD, length, width))]
    scratch = feed_scratch(width, False) + [pltpu.SemaphoreType.DMA((2, 2))]
    kernel = functools.partial(feed_forward_kernel, base, hidden_at)
    flops = 16 * length * width * width
    return call(kernel, ins, specs, outs, [VMEM] * len(outs), scratch, flops, 10_000_000)


def feed_backward(tables, out_tables, small, base, grad, kept, rows, weights):
    length, width = rows.shape
    _, hat, rstd, pre = kept
    ins = list(tables) + list(out_tables) + [small, grad, hat, rstd, rows, pre]
    ins += [array for pair in weights for array in pair]
    specs = [SMEM] * 4 + [VMEM] * 6 + [ANY] * 4
    outs = [shaped((length, width)), shaped((8, width))] + half_shapes(weights)
    out_specs = [VMEM] * 2 + [ANY] * 4
    scratch = feed_scratch(width, True) + [pltpu.SemaphoreType.DMA((2, 2))]
    kernel = functools.partial(feed_backward_kernel, base)
    flops = 32 * length * width * width
    results = call(kernel, ins, specs, outs, out_specs, scratch, flops, 14_000_000)
    return results[0], results[1], [results[2:4], results[4:6]]


def feed_both(tables, out_tables, small, base, hidden_at, rows, grad, weights):
    length, width = rows.shape
    ins = list(tables) + list(out_tables) + [small, rows, grad] + [array for pair in weights for array in pair]
    specs = [SMEM] * 4 + [VMEM] * 3 + [ANY] * 4
    outs = [shaped((length, width)), shaped((length, width)), shaped((8, width))]
    outs += half_shapes(weights)
    out_specs = [VMEM] * 3 + [ANY] * 4
    scratch = feed_scratch(width, True) + [
        pltpu.VMEM((QUAD, length, width), F32),
        pltpu.VMEM((length, width), F32),
        pltpu.VMEM((length, LANES), F32),
        pltpu.SemaphoreType.DMA((2, 2)),
    ]
    kernel = functools.partial(feed_both_kernel, base, hidden_at)
    flops = 48 * length * width * width
    results = call(kernel, ins, specs, outs, out_specs, scratch, flops, 12_000_000)
    return results[0], results[1], results[2], [results[3:5], results[5:7]]


def tie(*arrays):
    return lax.optimization_barrier(arrays)


class Direct:
    def __init__(self, axis_sizes):
        outer, inner = axis_sizes
        self.count = outer * inner
        inner_bits = inner.bit_length() - 1
        bits = self.count.bit_length() - 1
        core = [inner_bits]
        across = list(range(inner_bits + 1, bits))
        up = [0]
        along = list(range(1, inner_bits))
        self.orders = {
            "a": core + across + up + along,
            "b": core + up + across + along,
            "c": core + along[:1] + across + up + along[1:],
            "d": core + along[:1] + up + across + along[1:],
        }
        self.place = lax.axis_index(AXES)

    def hop(self, array, bit):
        return lax.ppermute(array, AXES, [(at, at ^ (1 << bit)) for at in range(self.count)])

    def table(self, name):
        order = self.orders[name]
        index = jnp.arange(self.count, dtype=jnp.int32)
        block = jnp.zeros_like(index)
        for at, bit in enumerate(order):
            block = block | (((index >> (len(order) - 1 - at)) & 1) << bit)
        return block ^ self.place

    def grow(self, array, name, first, steps):
        for bit in self.orders[name][::-1][first : first + steps]:
            array = jnp.concatenate([array, self.hop(array, bit)], axis=0)
        return array

    def finish(self, array, name):
        return array, self.hop(array, self.orders[name][0])


class Sum:
    def __init__(self, net, name, keep, send):
        self.net = net
        self.order = net.orders[name]
        self.pieces = [keep]
        self.send = send
        self.done = 0

    def part(self, low, high):
        total = self.pieces[0][low:high].astype(F32)
        for piece in self.pieces[1:]:
            total = total + piece[low:high].astype(F32)
        return total

    def step(self):
        arrived = self.net.hop(self.send, self.order[self.done])
        self.done += 1
        self.pieces.append(arrived)
        number = arrived.shape[0]
        if number > 1:
            self.send = self.part(number // 2, number).astype(BF)
        return self

    def steps(self, number):
        for _ in range(number):
            self.step()
        return self

    def total(self):
        return self.part(0, 1)[0]


def tie_sums(array, *sums):
    tied = tie(array, *[item.pieces[-1] for item in sums])
    for item, piece in zip(sums, tied[1:]):
        item.pieces[-1] = piece
        number = piece.shape[0]
        item.send = item.part(number // 2, number).astype(BF)
    return tied[0]


def sum_all(array, count):
    for bit in range(count.bit_length() - 1):
        pairs = [(at, at ^ (1 << bit)) for at in range(count)]
        array = array + lax.ppermute(array, AXES, pairs)
    return array


def adam_update(weight, gradient, first, second, rate, decay):
    first_new = BETA_ONE * first + (1.0 - BETA_ONE) * gradient
    second_new = BETA_TWO * second + (1.0 - BETA_TWO) * gradient * gradient
    first_hat = first_new / (1.0 - BETA_ONE**STEP)
    second_hat = second_new / (1.0 - BETA_TWO**STEP)
    weight_new = weight - rate * (first_hat / (jnp.sqrt(second_hat) + EPS_ADAM) + decay * weight)
    return (weight_new, first_new, second_new, weight_new.astype(BF))


def spread(piece, place, count):
    rows, lanes = piece.shape
    lane = lax.broadcasted_iota(jnp.int32, (rows, lanes * count), 1) // lanes
    return jnp.where(lane == place, jnp.tile(piece, (1, count)), jnp.zeros((), piece.dtype))


def gather_small(vectors, hidden, place, count, width):
    whole = spread(vectors.astype(BF), place, count)
    deep = spread(hidden.astype(BF), place, count).reshape(-1, width)
    spare = jnp.zeros((SMALL_ROWS - whole.shape[0] - deep.shape[0], width), BF)
    return sum_all(jnp.concatenate([whole, deep, spare], axis=0), count).astype(F32)


def scatter_small(grads, vectors, hidden, place, count):
    enc_attend, enc_feed, self_attend, cross_attend, dec_feed = grads
    whole = jnp.concatenate(
        [
            enc_attend[:5],
            enc_feed[:3],
            self_attend[:5],
            cross_attend[:5],
            dec_feed[:3],
            enc_feed[3:7],
            dec_feed[3:7],
            enc_feed[7:],
            dec_feed[7:],
            dec_feed[7:],
        ],
        axis=0,
    )
    whole = sum_all(whole, count)
    rows, lanes = vectors.shape
    first = lax.dynamic_slice_in_dim(whole[:rows], place * lanes, lanes, axis=1)
    layers, lanes = hidden.shape
    deep = whole[rows : rows + 2 * QUAD].reshape(layers, -1)
    return first, lax.dynamic_slice_in_dim(deep, place * lanes, lanes, axis=1)


def gather_whole(attention, up, down):
    width = attention.shape[2]
    number = width // BLOCK
    square = lax.all_gather(attention, AXES, axis=1, tiled=True)
    square = square.reshape(-1, QUAD, number, BLOCK, width).transpose(0, 2, 1, 3, 4)
    tall = lax.all_gather(up, AXES, axis=1, tiled=True)
    tall = tall.reshape(2, number, BLOCK, QUAD, width).transpose(0, 1, 3, 2, 4)
    deep = lax.all_gather(down, AXES, axis=1, tiled=True).reshape(2, number, QUAD, BLOCK, width)
    half = number // 2
    quads = [square[0], tall[0], deep[0], square[1], square[2], tall[1], deep[1]]
    return [(quad[:half], quad[half:]) for quad in quads]


def scatter_whole(quads):
    joined = [jnp.concatenate(pair, axis=0).astype(F32) for pair in quads]
    number, _, _, width = joined[0].shape
    square = jnp.stack([joined[0], joined[3], joined[4]])
    square = square.transpose(0, 2, 1, 3, 4).reshape(3 * QUAD, width, width)
    tall = jnp.stack([joined[1], joined[5]]).transpose(0, 1, 3, 2, 4)
    tall = tall.reshape(2, width, QUAD * width)
    deep = jnp.stack([joined[2], joined[6]]).reshape(2, QUAD * width, width)
    return [
        lax.psum_scatter(part, AXES, scatter_dimension=1, tiled=True)
        for part in (square, tall, deep)
    ]


def direct_step(net, small, pairs, source, target, grad, attention, up, down):
    source_pair, target_pair, cross_pair = pairs
    width = source.shape[1]
    square = attention.reshape(3, 1, QUAD, BLOCK, width)
    tall = up.reshape(2, 1, BLOCK, QUAD, width).transpose(0, 1, 3, 2, 4)
    deep = down.reshape(2, 1, QUAD, BLOCK, width)
    table = {name: net.table(name) for name in net.orders}
    ab = (table["a"], table["b"])
    cd = (table["c"], table["d"])
    cut = QUAD // 2

    first = net.grow(square[0], "a", 0, 1)
    second = net.grow(jnp.concatenate([tall[0], deep[0]], axis=1), "a", 0, 1)
    third = jnp.concatenate([square[1], square[2]], axis=1)
    third, first = tie(third, first)
    third = net.grow(third, "a", 0, 1)
    fourth = jnp.concatenate([tall[1], deep[1]], axis=1)
    fourth, second = tie(fourth, second)
    fourth = net.grow(fourth, "c", 0, 1)
    first = net.grow(first, "a", 1, 1)
    second = net.grow(second, "a", 1, 1)
    third = net.grow(third, "a", 1, 1)
    query_key = net.grow(first[:, :cut], "a", 2, 1)
    value_out = net.grow(first[:, cut:], "b", 2, 1)
    up_one = net.grow(second[:, :QUAD], "a", 2, 1)
    down_one = net.grow(second[:, QUAD:], "b", 2, 1)
    third, query_key, value_out = tie(third, query_key, value_out)
    self_w = net.grow(third[:, :QUAD], "a", 2, 1)
    cross_w = net.grow(third[:, QUAD:], "b", 2, 1)
    query_key = net.grow(query_key, "a", 3, 1)
    value_out = net.grow(value_out, "b", 3, 1)
    fourth, query_key, value_out = tie(fourth, query_key, value_out)
    up_two = net.grow(fourth[:, :QUAD], "c", 1, 1)
    down_two = net.grow(fourth[:, QUAD:], "d", 1, 1)
    enc_attend_w = [net.finish(query_key, "a"), net.finish(value_out, "b")]
    source, up_one, down_one = tie(source, up_one, down_one)
    up_one = net.grow(up_one, "a", 3, 1)
    down_one = net.grow(down_one, "b", 3, 1)

    enc_kept = attend_forward(ab, source_pair, small, 0, source, None, enc_attend_w, False)
    enc_mid, up_one, down_one, self_w, cross_w = tie(enc_kept[0], up_one, down_one, self_w, cross_w)
    self_w = net.grow(self_w, "a", 3, 1)
    cross_w = net.grow(cross_w, "b", 3, 1)
    up_two = net.grow(up_two, "c", 2, 1)
    down_two = net.grow(down_two, "d", 2, 1)
    enc_feed_w = [net.finish(up_one, "a"), net.finish(down_one, "b")]
    enc_feed_kept = feed_forward(ab, small, 5, HIDDEN_ROW, enc_mid, enc_feed_w)
    memory, self_w, cross_w = tie(enc_feed_kept[0], self_w, cross_w)
    up_two = net.grow(up_two, "c", 3, 1)
    down_two = net.grow(down_two, "d", 3, 1)
    self_w = [net.finish(self_w, "a")]
    cross_w = [net.finish(cross_w, "b")]
    self_kept = attend_forward(ab[:1], target_pair, small, 8, target, None, self_w, True)
    dec_one, up_two, down_two = tie(self_kept[0], up_two, down_two)
    dec_feed_w = [net.finish(up_two, "c"), net.finish(down_two, "d")]
    cross_kept = attend_forward(ab[1:], cross_pair, small, 13, dec_one, memory, cross_w, False)
    dec_two = cross_kept[0]
    result, two_grad, dec_feed_small, dec_feed_q = feed_both(
        cd, ab, small, 18, HIDDEN_ROW + QUAD, dec_two, grad, dec_feed_w
    )

    feed_two = [Sum(net, "b", *dec_feed_q[1]).step(), Sum(net, "a", *dec_feed_q[0]).step()]
    one_grad, memory_grad, cross_small, cross_q = attend_backward(
        ab[1:], cross_pair, small, 13, two_grad, cross_kept, dec_one, memory, cross_w, False
    )
    memory_grad = tie_sums(memory_grad, *feed_two)
    for item in feed_two:
        item.step()
    cross_s = Sum(net, "b", *cross_q[0]).step()
    mid_grad, enc_feed_small, enc_feed_q = feed_backward(
        ab, cd, small, 5, memory_grad, enc_feed_kept, enc_mid, enc_feed_w
    )
    one_grad, mid_grad = tie(one_grad, mid_grad)
    one_grad = tie_sums(one_grad, *feed_two, cross_s)
    for item in feed_two:
        item.step()
    cross_s.step()
    feed_one = [Sum(net, "d", *enc_feed_q[1]).step(), Sum(net, "c", *enc_feed_q[0]).step()]
    target_grad, _, self_small, self_q = attend_backward(
        ab[:1], target_pair, small, 8, one_grad, self_kept, target, None, self_w, True
    )
    mid_grad, target_grad = tie(mid_grad, target_grad)
    mid_grad = tie_sums(mid_grad, *feed_two, cross_s, *feed_one)
    cross_s.step()
    for item in feed_one:
        item.step()
    self_s = Sum(net, "a", *self_q[0]).step()
    feed_two = joined(feed_two, "a").step()
    source_grad, _, enc_small, enc_q = attend_backward(
        ab, source_pair, small, 0, mid_grad, enc_kept, source, None, enc_attend_w, False
    )
    enc_s = [Sum(net, "a", *enc_q[0]).steps(3), Sum(net, "b", *enc_q[1]).steps(3)]
    enc_s = joined(enc_s, "a").steps(2)
    feed_two.step()
    cross_s.steps(2)
    self_s.steps(4)
    for item in feed_one:
        item.steps(2)
    feed_one = joined(feed_one, "c").step()
    down_dec, up_dec = jnp.split(feed_two.total(), 2, axis=0)
    down_enc, up_enc = jnp.split(feed_one.total(), 2, axis=0)
    square_g = jnp.concatenate([enc_s.total(), self_s.total(), cross_s.total()], axis=0)
    tall_g = jnp.stack([up_enc, up_dec]).transpose(0, 2, 1, 3).reshape(up.shape)
    deep_g = jnp.stack([down_enc, down_dec]).reshape(down.shape)
    tokens = (memory, result, source_grad, target_grad)
    smalls = (enc_small, enc_feed_small, self_small, cross_small, dec_feed_small)
    return tokens, smalls, (square_g, tall_g, deep_g)


def whole_step(small, pairs, source, target, grad, attention, up, down):
    source_pair, target_pair, cross_pair = pairs
    quads = gather_whole(attention, up, down)
    one = (jnp.arange(source.shape[1] // BLOCK, dtype=jnp.int32),)
    two = one * 2
    enc_attend_w, self_w, cross_w = [quads[0]], [quads[3]], [quads[4]]
    enc_feed_w, dec_feed_w = quads[1:3], quads[5:7]
    enc_kept = attend_forward(one, source_pair, small, 0, source, None, enc_attend_w, False)
    enc_mid = enc_kept[0]
    enc_feed_kept = feed_forward(two, small, 5, HIDDEN_ROW, enc_mid, enc_feed_w)
    memory = enc_feed_kept[0]
    self_kept = attend_forward(one, target_pair, small, 8, target, None, self_w, True)
    dec_one = self_kept[0]
    cross_kept = attend_forward(one, cross_pair, small, 13, dec_one, memory, cross_w, False)
    dec_two = cross_kept[0]
    result, two_grad, dec_feed_small, dec_feed_q = feed_both(
        two, two, small, 18, HIDDEN_ROW + QUAD, dec_two, grad, dec_feed_w
    )
    one_grad, memory_grad, cross_small, cross_q = attend_backward(
        one, cross_pair, small, 13, two_grad, cross_kept, dec_one, memory, cross_w, False
    )
    target_grad, _, self_small, self_q = attend_backward(
        one, target_pair, small, 8, one_grad, self_kept, target, None, self_w, True
    )
    mid_grad, enc_feed_small, enc_feed_q = feed_backward(
        two, two, small, 5, memory_grad, enc_feed_kept, enc_mid, enc_feed_w
    )
    source_grad, _, enc_small, enc_q = attend_backward(
        one, source_pair, small, 0, mid_grad, enc_kept, source, None, enc_attend_w, False
    )
    tokens = (memory, result, source_grad, target_grad)
    smalls = (enc_small, enc_feed_small, self_small, cross_small, dec_feed_small)
    quads = [enc_q[0], enc_feed_q[0], enc_feed_q[1], self_q[0], cross_q[0]] + dec_feed_q
    return tokens, smalls, scatter_whole(quads)


def joined(sums, name):
    item = Sum(sums[0].net, name, None, jnp.concatenate([each.send for each in sums], axis=1))
    item.done = sums[0].done
    half = item.send.shape[0]
    item.pieces = [jnp.concatenate([each.part(0, half) for each in sums], axis=1)]
    return item


def per_device(
    axis_sizes,
    source_tokens,
    target_tokens,
    source_segments,
    target_segments,
    output_grad,
    attention_weight,
    up_weight,
    down_weight,
    vectors,
    hidden_bias,
    *moments,
):
    masters = (attention_weight, up_weight, down_weight, vectors, hidden_bias)
    firsts = moments[:5]
    seconds = moments[5:]
    source = source_tokens[0]
    target = target_tokens[0]
    width = source.shape[1]
    count = axis_sizes[0] * axis_sizes[1]
    place = lax.axis_index(AXES)
    direct = count * BLOCK == width
    small = gather_small(vectors, hidden_bias, place, count, width)
    attention = attention_weight.astype(BF)
    up = up_weight.astype(BF)
    down = down_weight.astype(BF)
    pairs = (
        (source_segments, source_segments),
        (target_segments, target_segments),
        (target_segments, source_segments),
    )
    grad = output_grad[0]
    if direct:
        net = Direct(axis_sizes)
        tokens, small_grads, shares = direct_step(
            net, small, pairs, source, target, grad, attention, up, down
        )
    else:
        tokens, small_grads, shares = whole_step(
            small, pairs, source, target, grad, attention, up, down
        )
    square_g, tall_g, deep_g = shares
    memory, result, source_grad, target_grad = tokens
    vector_g, hidden_g = scatter_small(small_grads, vectors, hidden_bias, place, count)

    grads = (square_g, tall_g, deep_g, vector_g, hidden_g)
    updated = [
        adam_update(
            masters[slot], grads[slot], firsts[slot], seconds[slot], RATES[slot], DECAYS[slot]
        )
        for slot in range(5)
    ]
    tokens = (memory[None], result[None], source_grad[None], target_grad[None])
    return tokens + tuple(updated[slot][kind] for kind in range(4) for slot in range(5))


def solution(mesh):
    rows = P(AXES, None, None)
    line = P(AXES, None)
    matrix = P(None, AXES, None)
    vector = P(None, AXES)
    state = (matrix, matrix, matrix, vector, vector)
    return jax.shard_map(
        functools.partial(per_device, (mesh.shape["dp"], mesh.shape["fsdp"])),
        mesh=mesh,
        in_specs=(rows, rows, line, line, rows) + state * 3,
        out_specs=(rows,) * 4 + state * 4,
        check_vma=False,
    )
```

```python
import functools

import jax
import jax.numpy as jnp
from jax import lax
from jax.experimental import pallas as pl
from jax.experimental.pallas import tpu as pltpu
from jax.sharding import PartitionSpec as P

HEADS = 8
STEP = 10
EPS_NORM = 1e-05
EPS_ADAM = 1e-08
BETA_ONE = 0.9
BETA_TWO = 0.999
LOWEST = -1e30
RATES = (0.05, 0.05, 0.05, 0.3, 0.3)
DECAYS = (0.01, 0.01, 0.01, 0.0, 0.0)
AXES = ("dp", "fsdp")
QUAD = 4
BLOCK = 16
LANES = 128
SMALL_ROWS = 32
HIDDEN_ROW = 24
BF = jnp.bfloat16
F32 = jnp.float32
VMEM = pl.BlockSpec(memory_space=pltpu.VMEM)
SMEM = pl.BlockSpec(memory_space=pltpu.SMEM)
ANY = pl.BlockSpec(memory_space=pl.ANY)
ROOT_TWO_PI = 0.7978845608028654
CUBIC = 0.044715


def dot(left, right):
    return jnp.dot(left, right, preferred_element_type=F32)


def dot_nt(left, right):
    return lax.dot_general(left, right, (((1,), (1,)), ((), ())), preferred_element_type=F32)


def load_start(part, place, sems):
    table, arrays, low, number = part
    at = 0
    for slot, array in enumerate(arrays):
        for index in range(array.shape[0]):
            source = array.at[index, low : low + number]
            pltpu.make_async_copy(source, place(table[at]), sems.at[slot]).start()
            at += 1


def load_wait(part, sems):
    table, arrays, low, number = part
    for slot, array in enumerate(arrays):
        whole = array.at[:, low : low + number]
        pltpu.make_async_copy(whole, whole, sems.at[slot]).wait()


def store_start(part, place, sems):
    table, arrays, low, number = part
    half = arrays[0].shape[0]
    for index in range(half):
        for slot in (1, 0):
            target = arrays[slot].at[index, low : low + number]
            source = place(table[slot * half + index])
            pltpu.make_async_copy(source, target, sems.at[slot]).start()


def row_place(scratch, low, high):
    def place(block):
        start = pl.multiple_of(block * BLOCK, BLOCK)
        return scratch.at[low:high, pl.ds(start, BLOCK), :]

    return place


def block_place(scratch):
    return lambda block: scratch.at[block]


def norm_forward(pre, gain, shift, out_ref, hat_ref, rstd_ref):
    mean = jnp.mean(pre, axis=-1, keepdims=True)
    centred = pre - mean
    spread = jnp.mean(centred * centred, axis=-1, keepdims=True)
    rstd = lax.rsqrt(spread + EPS_NORM)
    hat = centred * rstd
    hat_ref[...] = hat
    rstd_ref[...] = jnp.broadcast_to(rstd, rstd_ref.shape)
    out_ref[...] = hat * gain + shift


def norm_backward(grad, hat, rstd, gain):
    gain_grad = jnp.sum(grad * hat, axis=0, keepdims=True)
    shift_grad = jnp.sum(grad, axis=0, keepdims=True)
    scaled = grad * gain
    one = jnp.mean(scaled, axis=-1, keepdims=True)
    two = jnp.mean(scaled * hat, axis=-1, keepdims=True)
    return rstd * (scaled - one - hat * two), gain_grad, shift_grad


def lane_mask(rows):
    return lax.broadcasted_iota(jnp.int32, (rows, LANES), 1) < LANES // 2


def stacked_pair(block):
    first = lane_mask(block.shape[0])
    zero = jnp.zeros_like(block)
    return jnp.concatenate([jnp.where(first, block, zero), jnp.where(first, zero, block)], axis=0)


def merged_pair(stacked):
    rows = stacked.shape[0] // 2
    return jnp.where(lane_mask(rows), stacked[:rows], stacked[rows:])


def mask_fill(bias_ref, column_seg, row_seg, causal, transposed):
    length = bias_ref.shape[0]
    column = jnp.broadcast_to(column_seg, (LANES, length)).T
    for at in range(0, length, LANES):
        same = column == row_seg[:, at : at + LANES]
        if causal:
            down = lax.broadcasted_iota(jnp.int32, (length, LANES), 0)
            along = lax.broadcasted_iota(jnp.int32, (length, LANES), 1) + at
            order = (down <= along) if transposed else (along <= down)
            same = same & order
        bias_ref[:, at : at + LANES] = jnp.where(same, 0.0, LOWEST)


def take_parts(refs, layout, tables):
    parts = []
    for slot, (arrays, low, number) in enumerate(layout):
        parts.append((tables[slot], [refs.pop(0) for _ in range(arrays)], low, number))
    return parts


def small_part(part):
    table, arrays, low, number = part
    return table, arrays, low + number, 1


def small_join(blocks_ref):
    count = blocks_ref.shape[0]
    groups = blocks_ref.shape[3] // LANES
    per = count // groups
    vectors = []
    hidden = [[], []]
    for group in range(groups):
        total = blocks_ref[group * per, 0, :8].astype(F32)
        for at in range(group * per + 1, (group + 1) * per):
            total = total + blocks_ref[at, 0, :8].astype(F32)
        columns = [total[:, at : at + LANES] for at in range(0, 4 * LANES, LANES)]
        vectors.append(jnp.concatenate(columns[:3], axis=0))
        for layer in range(2):
            rows = [columns[3][4 * layer + at : 4 * layer + at + 1] for at in range(4)]
            hidden[layer].append(jnp.concatenate(rows, axis=1))
    return jnp.concatenate([jnp.concatenate(vectors, axis=1)] + hidden[0] + hidden[1], axis=0)


def small_split(whole, group):
    lanes = slice(group * LANES, (group + 1) * LANES)
    columns = [whole[at : at + 8, lanes] for at in (0, 8, 16)]
    rows = []
    for layer in range(2):
        row = whole[24 + 4 * layer + group : 25 + 4 * layer + group]
        rows += [row[:, at : at + LANES] for at in range(0, 4 * LANES, LANES)]
    columns.append(jnp.concatenate(rows, axis=0))
    block = jnp.concatenate(columns, axis=1)
    return jnp.concatenate([block, jnp.zeros_like(block)], axis=0).astype(BF)


def attend_forward_kernel(layout, cross, causal, base, joins, *refs):
    refs = list(refs)
    tables = [refs.pop(0) for _ in layout]
    query_seg = refs.pop(0)
    key_seg = refs.pop(0)
    small = None if joins else refs.pop(0)
    rows_ref = refs.pop(0)
    memory_ref = refs.pop(0) if cross else None
    parts = take_parts(refs, layout, tables)
    out_ref, hat_ref, rstd_ref, q_ref, k_ref, v_ref, o_ref, lse_ref = [refs.pop(0) for _ in range(8)]
    if joins:
        small = refs.pop(0)
        blocks_ref = refs.pop()
        extra = small_part(parts[-1])
    w_ref, bias_ref, sems = refs
    first = 0
    if joins:
        load_start(extra, lambda block: blocks_ref.at[block], sems.at[len(parts)])
    for slot, part in enumerate(parts):
        load_start(part, row_place(w_ref, first, first + part[3]), sems.at[slot])
        first += part[3]
    length, width = rows_ref.shape
    mask_fill(bias_ref, query_seg[...], key_seg[...], causal, False)
    rows = rows_ref[...].astype(BF)
    keys = memory_ref[...].astype(BF) if cross else rows
    if joins:
        load_wait(extra, sems.at[len(parts)])
        small[...] = small_join(blocks_ref)
    for slot, part in enumerate(parts):
        load_wait(part, sems.at[slot])
    scale = (width // HEADS) ** (-0.5)
    q_ref[...] = (dot(rows, w_ref[0]) + small[base : base + 1]).astype(BF) * jnp.asarray(scale, BF)
    k_ref[...] = dot(keys, w_ref[1]).astype(BF)
    v_ref[...] = (dot(keys, w_ref[2]) + small[base + 1 : base + 2]).astype(BF)
    lane = lax.broadcasted_iota(jnp.int32, (LANES, LANES), 1)
    for at in range(0, length, LANES):
        reach = at + LANES if causal else length
        logs = jnp.zeros((LANES, LANES), F32)
        for pair in range(HEADS // 2):
            lanes = slice(pair * LANES, (pair + 1) * LANES)
            stacked = stacked_pair(q_ref[at : at + LANES, lanes])
            scores = dot_nt(stacked, k_ref[:reach, lanes])
            bias = bias_ref[at : at + LANES, :reach]
            scores = scores + jnp.concatenate([bias, bias], axis=0)
            largest = jnp.max(scores, axis=-1, keepdims=True)
            exponent = jnp.exp(scores - largest).astype(BF)
            values = jnp.concatenate([v_ref[:reach, lanes], jnp.ones((reach, LANES), BF)], axis=1)
            mixed = dot(exponent, values)
            total = mixed[:, LANES:]
            o_ref[at : at + LANES, lanes] = merged_pair(mixed[:, :LANES] / total).astype(BF)
            log_total = largest + jnp.log(total)
            logs = jnp.where(lane == 2 * pair, log_total[:LANES], logs)
            logs = jnp.where(lane == 2 * pair + 1, log_total[LANES:], logs)
        lse_ref[:, at : at + LANES] = logs.T[:HEADS]
    attended = dot(o_ref[...], w_ref[3]) + small[base + 2 : base + 3]
    pre = rows_ref[...].astype(F32) + attended
    norm_forward(pre, small[base + 3 : base + 4], small[base + 4 : base + 5], out_ref, hat_ref, rstd_ref)


def attend_backward_kernel(layout, cross, causal, base, splits, *refs):
    refs = list(refs)
    tables = [refs.pop(0) for _ in layout]
    out_tables = [refs.pop(0) for _ in layout]
    query_seg = refs.pop(0)
    key_seg = refs.pop(0)
    small = refs.pop(0)
    grad_ref = refs.pop(0)
    hat_ref, rstd_ref = refs.pop(0), refs.pop(0)
    rows_ref = refs.pop(0)
    memory_ref = refs.pop(0) if cross else None
    q_ref, k_ref, v_ref, o_ref, lse_ref = [refs.pop(0) for _ in range(5)]
    others = [refs.pop(0) for _ in range(4)] if splits else None
    parts = take_parts(refs, layout, tables)
    rows_out = refs.pop(0)
    memory_out = refs.pop(0) if cross else None
    small_out = None if splits else refs.pop(0)
    outs = take_parts(refs, [(2, 0, number) for _, _, number in layout], out_tables)
    blocks_ref = refs.pop() if splits else None
    w_ref, dw_ref, bias_ref, dout_ref, dq_t_ref, dk_ref, dv_ref, kt_ref, sems = refs
    first = 0
    for slot, part in enumerate(parts):
        load_start(part, row_place(w_ref, first, first + part[3]), sems.at[slot])
        first += part[3]
    length, width = rows_ref.shape
    head = width // HEADS
    scale = head ** (-0.5)
    mask_fill(bias_ref, key_seg[...], query_seg[...], causal, True)
    kt_ref[...] = k_ref[...].T
    pre_grad, gain_grad, shift_grad = norm_backward(
        grad_ref[...], hat_ref[...], rstd_ref[:, :1], small[base + 3 : base + 4]
    )
    rows_out[...] = pre_grad
    low = pre_grad.astype(BF)
    for slot, part in enumerate(parts):
        load_wait(part, sems.at[slot])
    dout_ref[...] = dot_nt(low, w_ref[3]).astype(BF)
    dw_ref[3] = dot(o_ref[...].T, low).astype(BF)
    out_bias = jnp.sum(low.astype(F32), axis=0, keepdims=True)
    product = dout_ref[...].astype(F32) * o_ref[...].astype(F32)
    high = product.astype(BF)
    rest = (product - high.astype(F32)).astype(BF)
    picker = lax.broadcasted_iota(jnp.int32, (BLOCK, width), 1) // head
    picker = (picker == lax.broadcasted_iota(jnp.int32, (BLOCK, width), 0)).astype(BF)
    row_dots = dot_nt(picker, high) + dot_nt(picker, rest)
    for pair in range(HEADS // 2):
        lanes = slice(pair * LANES, (pair + 1) * LANES)
        for at in range(0, length, LANES):
            begin = at if causal else 0
            query = q_ref[begin:, lanes]
            dout = dout_ref[begin:, lanes]
            scores = dot_nt(stacked_pair(k_ref[at : at + LANES, lanes]), query)
            prob_grad = dot_nt(stacked_pair(v_ref[at : at + LANES, lanes]), dout)
            bias = bias_ref[at : at + LANES, begin:]
            probs = []
            score_grads = []
            for part in range(2):
                which = 2 * pair + part
                half = slice(part * LANES, (part + 1) * LANES)
                prob = jnp.exp(scores[half] + (bias - lse_ref[which : which + 1, begin:]))
                probs.append(prob.astype(BF))
                row_dot = row_dots[which : which + 1, begin:]
                score_grads.append((prob * (prob_grad[half] - row_dot)).astype(BF))
                at_t = pair * LANES + part * head
                back = dot(kt_ref[at_t : at_t + head, at : at + LANES], score_grads[part])
                if at == 0:
                    dq_t_ref[at_t : at_t + head, :] = back
                else:
                    dq_t_ref[at_t : at_t + head, begin:] += back
            value_back = dot(jnp.concatenate(probs, axis=0), dout)
            dv_ref[at : at + LANES, lanes] = merged_pair(value_back).astype(BF)
            key_back = dot(jnp.concatenate(score_grads, axis=0), query)
            dk_ref[at : at + LANES, lanes] = merged_pair(key_back).astype(BF)
    query_grad = (dq_t_ref[...] * scale).T.astype(BF)
    key_grad = dk_ref[...]
    value_grad = dv_ref[...]
    turned = rows_ref[...].astype(BF).T
    dw_ref[0] = dot(turned, query_grad).astype(BF)
    if cross:
        turned = memory_ref[...].astype(BF).T
    dw_ref[1] = dot(turned, key_grad).astype(BF)
    dw_ref[2] = dot(turned, value_grad).astype(BF)
    first = 0
    for slot, part in enumerate(outs):
        store_start(part, row_place(dw_ref, first, first + part[3]), sems.at[slot])
        first += part[3]
    rows_back = rows_out[...] + dot_nt(query_grad, w_ref[0])
    memory_back = dot_nt(key_grad, w_ref[1]) + dot_nt(value_grad, w_ref[2])
    if cross:
        rows_out[...] = rows_back
        memory_out[...] = memory_back
    else:
        rows_out[...] = rows_back + memory_back
    query_bias = jnp.sum(query_grad.astype(F32), axis=0, keepdims=True)
    value_bias = jnp.sum(value_grad.astype(F32), axis=0, keepdims=True)
    spare = jnp.zeros((3, width), F32)
    own = jnp.concatenate(
        [query_bias, value_bias, out_bias, gain_grad, shift_grad, spare], axis=0
    )
    if splits:
        enc_feed, self_attend, cross_attend, dec_feed = [other[...] for other in others]
        whole = small_rows(own, enc_feed, self_attend, cross_attend, dec_feed)
        groups = blocks_ref.shape[0]
        for group in range(groups):
            blocks_ref[group, 0] = small_split(whole, group)
        extra = small_part(outs[-1])
        per = 2 * extra[1][0].shape[0] // groups
        store_start(extra, lambda block: blocks_ref.at[block // per], sems.at[len(parts)])
        load_wait(extra, sems.at[len(parts)])
    else:
        small_out[...] = own
    for slot, part in enumerate(outs):
        load_wait(part, sems.at[slot])


def small_rows(enc_attend, enc_feed, self_attend, cross_attend, dec_feed):
    return jnp.concatenate(
        [
            enc_attend[:5],
            enc_feed[:3],
            self_attend[:5],
            cross_attend[:5],
            dec_feed[:3],
            dec_feed[7:],
            dec_feed[7:],
            dec_feed[7:],
            enc_feed[3:7],
            dec_feed[3:7],
        ],
        axis=0,
    )


def gelu_parts(pre):
    inner = ROOT_TWO_PI * (pre + CUBIC * pre * pre * pre)
    curve = jnp.tanh(inner)
    return curve, 0.5 * pre * (1.0 + curve)


def gelu_slope(pre, curve):
    bend = ROOT_TWO_PI * (1.0 + 3.0 * CUBIC * pre * pre)
    return 0.5 * (1.0 + curve) + 0.5 * pre * (1.0 - curve * curve) * bend


def chunk_of(ref, index):
    number = ref.shape[0] // QUAD
    part = ref[index * number : (index + 1) * number]
    return part.reshape(number * ref.shape[1] * ref.shape[2], ref.shape[3])


def feed_forward_steps(small, base, hidden_at, rows_ref, up_ref, down_ref, pre_ref):
    rows = rows_ref[...].astype(BF)
    total = rows_ref[...] + small[base : base + 1]
    for index in range(QUAD):
        at = hidden_at + index
        pre = dot(rows, up_ref[index]) + small[at : at + 1]
        pre_ref[index] = pre
        active = gelu_parts(pre)[1].astype(BF)
        total = total + dot(active, chunk_of(down_ref, index))
    return total


def feed_backward_steps(pre_grad, rows_ref, up_ref, down_ref, pre_ref, dup_ref, ddown_ref, rows_out):
    low = pre_grad.astype(BF)
    turned = rows_ref[...].astype(BF).T
    total = pre_grad
    hidden_grads = []
    number = ddown_ref.shape[0] // QUAD
    for index in range(QUAD):
        pre = pre_ref[index]
        curve, active = gelu_parts(pre)
        down_grad = dot(active.astype(BF).T, low).astype(BF)
        ddown_ref[index * number : (index + 1) * number] = down_grad.reshape(
            (number,) + ddown_ref.shape[1:]
        )
        back = dot_nt(low, chunk_of(down_ref, index))
        hidden = (back * gelu_slope(pre, curve)).astype(BF)
        hidden_grads.append(jnp.sum(hidden.astype(F32), axis=0, keepdims=True))
        dup_ref[index] = dot(turned, hidden).astype(BF)
        total = total + dot_nt(hidden, up_ref[index])
    rows_out[...] = total
    out_bias = jnp.sum(low.astype(F32), axis=0, keepdims=True)
    return out_bias, hidden_grads


def load_feed(parts, up_ref, down_ref, sems):
    load_start(parts[0], row_place(up_ref, 0, QUAD), sems.at[0])
    load_start(parts[1], block_place(down_ref), sems.at[1])


def store_feed(outs, dup_ref, ddown_ref, sems):
    store_start(outs[1], block_place(ddown_ref), sems.at[1])
    store_start(outs[0], row_place(dup_ref, 0, QUAD), sems.at[0])


def wait_feed(parts, sems):
    for slot, part in enumerate(parts):
        load_wait(part, sems.at[slot])


def feed_outs(refs, tables):
    arrays = [refs.pop(0), refs.pop(0)]
    return [(tables[slot], arrays, slot * QUAD, QUAD) for slot in range(2)]


def feed_small(out_bias, gain_grad, shift_grad, hidden_grads):
    spare = jnp.zeros_like(out_bias)
    return jnp.concatenate([out_bias, gain_grad, shift_grad] + hidden_grads + [spare], axis=0)


def feed_forward_kernel(layout, base, hidden_at, *refs):
    refs = list(refs)
    tables = [refs.pop(0), refs.pop(0)]
    small, rows_ref = refs.pop(0), refs.pop(0)
    parts = take_parts(refs, layout, tables)
    out_ref, hat_ref, rstd_ref, pre_ref, up_ref, down_ref, sems = refs
    load_feed(parts, up_ref, down_ref, sems)
    wait_feed(parts, sems)
    pre = feed_forward_steps(small, base, hidden_at, rows_ref, up_ref, down_ref, pre_ref)
    norm_forward(pre, small[base + 1 : base + 2], small[base + 2 : base + 3], out_ref, hat_ref, rstd_ref)


def feed_backward_kernel(layout, base, *refs):
    refs = list(refs)
    tables = [refs.pop(0), refs.pop(0)]
    out_tables = [refs.pop(0), refs.pop(0)]
    small, grad_ref, hat_ref, rstd_ref, rows_ref, pre_ref = [refs.pop(0) for _ in range(6)]
    parts = take_parts(refs, layout, tables)
    rows_out, small_out = refs.pop(0), refs.pop(0)
    outs = feed_outs(refs, out_tables)
    up_ref, down_ref, dup_ref, ddown_ref, sems, out_sems = refs
    load_feed(parts, up_ref, down_ref, sems)
    pre_grad, gain_grad, shift_grad = norm_backward(
        grad_ref[...], hat_ref[...], rstd_ref[:, :1], small[base + 1 : base + 2]
    )
    wait_feed(parts, sems)
    out_bias, hidden_grads = feed_backward_steps(
        pre_grad, rows_ref, up_ref, down_ref, pre_ref, dup_ref, ddown_ref, rows_out
    )
    store_feed(outs, dup_ref, ddown_ref, out_sems)
    small_out[...] = feed_small(out_bias, gain_grad, shift_grad, hidden_grads)
    wait_feed(outs, out_sems)


def feed_both_kernel(layout, base, hidden_at, *refs):
    refs = list(refs)
    tables = [refs.pop(0), refs.pop(0)]
    out_tables = [refs.pop(0), refs.pop(0)]
    small, rows_ref, grad_ref = [refs.pop(0) for _ in range(3)]
    parts = take_parts(refs, layout, tables)
    out_ref, rows_out, small_out = [refs.pop(0) for _ in range(3)]
    outs = feed_outs(refs, out_tables)
    up_ref, down_ref, dup_ref, ddown_ref, pre_ref, hat_ref, rstd_ref, sems, out_sems = refs
    load_feed(parts, up_ref, down_ref, sems)
    wait_feed(parts, sems)
    pre = feed_forward_steps(small, base, hidden_at, rows_ref, up_ref, down_ref, pre_ref)
    gain = small[base + 1 : base + 2]
    norm_forward(pre, gain, small[base + 2 : base + 3], out_ref, hat_ref, rstd_ref)
    pre_grad, gain_grad, shift_grad = norm_backward(
        grad_ref[...].astype(F32), hat_ref[...], rstd_ref[:, :1], gain
    )
    out_bias, hidden_grads = feed_backward_steps(
        pre_grad, rows_ref, up_ref, down_ref, pre_ref, dup_ref, ddown_ref, rows_out
    )
    store_feed(outs, dup_ref, ddown_ref, out_sems)
    small_out[...] = feed_small(out_bias, gain_grad, shift_grad, hidden_grads)
    wait_feed(outs, out_sems)


def shaped(shape, dtype=F32):
    return jax.ShapeDtypeStruct(shape, dtype)


def call(kernel, ins, specs, outs, out_specs, scratch, flops, moved):
    return pl.pallas_call(
        kernel,
        out_shape=outs,
        in_specs=specs,
        out_specs=out_specs,
        scratch_shapes=scratch,
        cost_estimate=pl.CostEstimate(flops=flops, bytes_accessed=moved, transcendentals=0),
        compiler_params=pltpu.CompilerParams(vmem_limit_bytes=40 * 1024 * 1024),
    )(*ins)


def layout_of(parts):
    return [(len(arrays), low, number) for _, arrays, low, number in parts]


def arrays_of(parts):
    return [array for part in parts for array in part[1]]


def most(parts):
    return max(len(part[1]) for part in parts)


def halves(width, number):
    return [shaped((width // BLOCK // 2, number, BLOCK, width), BF)] * 2


def attend_forward(segments, small, base, rows, memory, parts, causal):
    length, width = rows.shape
    cross = memory is not None
    joins = small is None
    ins = [part[0] for part in parts] + list(segments) + ([] if joins else [small]) + [rows]
    ins += [memory] if cross else []
    specs = [SMEM] * len(parts) + [VMEM] * (len(ins) - len(parts))
    arrays = arrays_of(parts)
    ins += arrays
    specs += [ANY] * len(arrays)
    outs = [shaped((length, width)), shaped((length, width)), shaped((length, LANES))]
    outs += [shaped((length, width), BF)] * 4 + [shaped((HEADS, length))]
    outs += [shaped((SMALL_ROWS, width))] if joins else []
    scratch = [
        pltpu.VMEM((QUAD, width, width), BF),
        pltpu.VMEM((length, length), F32),
        pltpu.SemaphoreType.DMA((len(parts) + 1, most(parts))),
    ]
    scratch += [pltpu.VMEM((width // BLOCK, 1, BLOCK, width), BF)] if joins else []
    kernel = functools.partial(attend_forward_kernel, layout_of(parts), cross, causal, base, joins)
    flops = 8 * length * width * width + 16 * length * length * width
    return call(kernel, ins, specs, outs, [VMEM] * len(outs), scratch, flops, 8_000_000)


def attend_backward(
    out_tables, segments, small, base, grad, kept, rows, memory, parts, causal, others
):
    length, width = rows.shape
    cross = memory is not None
    splits = others is not None
    hat, rstd, q, k, v, o, lse = kept[1:8]
    ins = [part[0] for part in parts] + list(out_tables)
    specs = [SMEM] * len(ins)
    ins += list(segments) + [small, grad, hat, rstd, rows]
    ins += ([memory] if cross else []) + [q, k, v, o, lse] + list(others or ())
    specs += [VMEM] * (len(ins) - len(specs))
    arrays = arrays_of(parts)
    ins += arrays
    specs += [ANY] * len(arrays)
    outs = [shaped((length, width))] * (2 if cross else 1)
    outs += [] if splits else [shaped((8, width))]
    out_specs = [VMEM] * len(outs) + [ANY] * (2 * len(parts))
    for slot, part in enumerate(parts):
        outs += halves(width, part[3] + (1 if splits and slot == len(parts) - 1 else 0))
    scratch = [
        pltpu.VMEM((QUAD, width, width), BF),
        pltpu.VMEM((QUAD, width, width), BF),
        pltpu.VMEM((length, length), F32),
        pltpu.VMEM((length, width), BF),
        pltpu.VMEM((width, length), F32),
        pltpu.VMEM((length, width), BF),
        pltpu.VMEM((length, width), BF),
        pltpu.VMEM((width, length), BF),
        pltpu.SemaphoreType.DMA((len(parts) + 1, 2)),
    ]
    scratch += [pltpu.VMEM((width // LANES, 1, BLOCK, width), BF)] if splits else []
    kernel = functools.partial(
        attend_backward_kernel, layout_of(parts), cross, causal, base, splits
    )
    flops = 16 * length * width * width + 40 * length * length * width
    results = list(call(kernel, ins, specs, outs, out_specs, scratch, flops, 12_000_000))
    rows_grad = results.pop(0)
    memory_grad = results.pop(0) if cross else None
    small_grad = None if splits else results.pop(0)
    return rows_grad, memory_grad, small_grad, [results[2 * i : 2 * i + 2] for i in range(len(parts))]


def feed_scratch(width, grads):
    number = width // BLOCK
    once = [pltpu.VMEM((QUAD, width, width), BF), pltpu.VMEM((number, QUAD, BLOCK, width), BF)]
    return once * (2 if grads else 1)


def feed_forward(small, base, hidden_at, rows, parts):
    length, width = rows.shape
    arrays = arrays_of(parts)
    ins = [part[0] for part in parts] + [small, rows] + arrays
    specs = [SMEM] * 2 + [VMEM] * 2 + [ANY] * len(arrays)
    outs = [shaped((length, width)), shaped((length, width)), shaped((length, LANES))]
    outs += [shaped((QUAD, length, width))]
    scratch = feed_scratch(width, False) + [pltpu.SemaphoreType.DMA((2, most(parts)))]
    kernel = functools.partial(feed_forward_kernel, layout_of(parts), base, hidden_at)
    flops = 16 * length * width * width
    return call(kernel, ins, specs, outs, [VMEM] * len(outs), scratch, flops, 10_000_000)


def feed_backward(out_tables, small, base, grad, kept, rows, parts):
    length, width = rows.shape
    _, hat, rstd, pre = kept
    arrays = arrays_of(parts)
    ins = [part[0] for part in parts] + list(out_tables) + [small, grad, hat, rstd, rows, pre]
    ins += arrays
    specs = [SMEM] * 4 + [VMEM] * 6 + [ANY] * len(arrays)
    outs = [shaped((length, width)), shaped((8, width))] + halves(width, 2 * QUAD)
    out_specs = [VMEM] * 2 + [ANY] * 2
    scratch = feed_scratch(width, True)
    scratch += [pltpu.SemaphoreType.DMA((2, most(parts))), pltpu.SemaphoreType.DMA((2, 2))]
    kernel = functools.partial(feed_backward_kernel, layout_of(parts), base)
    flops = 32 * length * width * width
    results = call(kernel, ins, specs, outs, out_specs, scratch, flops, 14_000_000)
    return results[0], results[1], results[2:4]


def feed_both(out_tables, small, base, hidden_at, rows, grad, parts):
    length, width = rows.shape
    arrays = arrays_of(parts)
    ins = [part[0] for part in parts] + list(out_tables) + [small, rows, grad] + arrays
    specs = [SMEM] * 4 + [VMEM] * 3 + [ANY] * len(arrays)
    outs = [shaped((length, width)), shaped((length, width)), shaped((8, width))]
    outs += halves(width, 2 * QUAD)
    out_specs = [VMEM] * 3 + [ANY] * 2
    scratch = feed_scratch(width, True) + [
        pltpu.VMEM((QUAD, length, width), F32),
        pltpu.VMEM((length, width), F32),
        pltpu.VMEM((length, LANES), F32),
        pltpu.SemaphoreType.DMA((2, most(parts))),
        pltpu.SemaphoreType.DMA((2, 2)),
    ]
    kernel = functools.partial(feed_both_kernel, layout_of(parts), base, hidden_at)
    flops = 48 * length * width * width
    results = call(kernel, ins, specs, outs, out_specs, scratch, flops, 12_000_000)
    return results[0], results[1], results[2], results[3:5]


def tie(*arrays):
    return lax.optimization_barrier(arrays)


class Direct:
    def __init__(self, axis_sizes):
        outer, inner = axis_sizes
        self.count = outer * inner
        inner_bits = inner.bit_length() - 1
        bits = self.count.bit_length() - 1
        core = [inner_bits]
        across = list(range(inner_bits + 1, bits))
        up = [0]
        along = list(range(1, inner_bits))
        self.orders = {
            "a": core + across + up + along,
            "b": core + up + across + along,
        }
        self.place = lax.axis_index(AXES)

    def hop(self, array, bit):
        return lax.ppermute(array, AXES, [(at, at ^ (1 << bit)) for at in range(self.count)])

    def table(self, name):
        order = self.orders[name]
        index = jnp.arange(self.count, dtype=jnp.int32)
        block = jnp.zeros_like(index)
        for at, bit in enumerate(order):
            block = block | (((index >> (len(order) - 1 - at)) & 1) << bit)
        return block ^ self.place

    def grow(self, array, name, first, steps):
        for bit in self.orders[name][::-1][first : first + steps]:
            array = jnp.concatenate([array, self.hop(array, bit)], axis=0)
        return array

    def finish(self, array, name):
        return [array, self.hop(array, self.orders[name][0])]


class Sum:
    def __init__(self, net, name, keep, send):
        self.net = net
        self.order = net.orders[name]
        self.pieces = [keep]
        self.send = send
        self.done = 0

    def part(self, low, high):
        total = self.pieces[0][low:high].astype(F32)
        for piece in self.pieces[1:]:
            total = total + piece[low:high].astype(F32)
        return total

    def step(self):
        self.pieces.append(self.net.hop(self.send, self.order[self.done]))
        self.done += 1
        self.ready()
        return self

    def ready(self):
        number = self.pieces[-1].shape[0]
        if number > 1:
            self.send = self.part(number // 2, number).astype(BF)

    def steps(self, number):
        for _ in range(number):
            self.step()
        return self

    def total(self):
        return self.part(0, 1)[0]

    def split(self, names, cuts):
        made = []
        for name, (low, high) in zip(names, cuts):
            item = Sum(self.net, name, None, None)
            item.pieces = [piece[:, low:high] for piece in self.pieces]
            item.done = self.done
            item.ready()
            made.append(item)
        return made


def joined(sums, name):
    item = Sum(sums[0].net, name, None, jnp.concatenate([each.send for each in sums], axis=1))
    item.done = sums[0].done
    half = item.send.shape[0]
    item.pieces = [jnp.concatenate([each.part(0, half) for each in sums], axis=1)]
    return item


def tie_sums(array, *sums):
    tied = tie(array, *[item.send for item in sums])
    for item, send in zip(sums, tied[1:]):
        item.send = send
    return tied[0]


def adam_update(weight, gradient, first, second, rate, decay):
    first_new = BETA_ONE * first + (1.0 - BETA_ONE) * gradient
    second_new = BETA_TWO * second + (1.0 - BETA_TWO) * gradient * gradient
    first_hat = first_new / (1.0 - BETA_ONE**STEP)
    second_hat = second_new / (1.0 - BETA_TWO**STEP)
    weight_new = weight - rate * (first_hat / (jnp.sqrt(second_hat) + EPS_ADAM) + decay * weight)
    return (weight_new, first_new, second_new, weight_new.astype(BF))


def small_block(vectors, hidden, place, count, width):
    groups = width // LANES
    per = count // groups
    at = place % per
    rows = 3 * 8
    lane = lax.broadcasted_iota(jnp.int32, (rows, LANES), 1) // vectors.shape[1]
    upright = jnp.pad(vectors.astype(BF), ((0, rows - vectors.shape[0]), (0, 0)))
    upright = jnp.where(lane == at, jnp.tile(upright, (1, per)), jnp.zeros((), BF))
    lane = lax.broadcasted_iota(jnp.int32, (2, width), 1) // hidden.shape[1]
    level = jnp.where(lane == at, jnp.tile(hidden.astype(BF), (1, per)), jnp.zeros((), BF))
    columns = [upright[low : low + 8] for low in (0, 8, 16)] + [level.reshape(8, LANES)]
    return jnp.pad(jnp.concatenate(columns, axis=1), ((0, BLOCK - 8), (0, 0)))


def small_share(total, vectors, hidden, place, count):
    width = total.shape[1]
    per = count // (width // LANES)
    at = place % per
    upright = jnp.concatenate([total[:8, low : low + LANES] for low in (0, LANES, 2 * LANES)], axis=0)
    rows, lanes = vectors.shape
    first = lax.dynamic_slice_in_dim(upright[:rows], at * lanes, lanes, axis=1)
    level = total[:8, 3 * LANES :].reshape(2, width)
    lanes = hidden.shape[1]
    return first, lax.dynamic_slice_in_dim(level, at * lanes, lanes, axis=1)


def gather_small(vectors, hidden):
    whole = lax.all_gather(vectors.astype(BF), AXES, axis=1, tiled=True)
    deep = lax.all_gather(hidden.astype(BF), AXES, axis=1, tiled=True)
    whole = jnp.pad(whole, ((0, HIDDEN_ROW - whole.shape[0]), (0, 0)))
    return jnp.concatenate([whole, deep.reshape(-1, whole.shape[1])], axis=0).astype(F32)


def scatter_small(grads, vectors, hidden, place, count):
    whole = lax.psum(small_rows(*grads), AXES)
    rows, lanes = vectors.shape
    first = lax.dynamic_slice_in_dim(whole[:rows], place * lanes, lanes, axis=1)
    layers, lanes = hidden.shape
    deep = whole[HIDDEN_ROW:].reshape(layers, -1)
    return first, lax.dynamic_slice_in_dim(deep, place * lanes, lanes, axis=1)


def gather_whole(attention, up, down):
    width = attention.shape[2]
    number = width // BLOCK
    square = lax.all_gather(attention, AXES, axis=1, tiled=True)
    square = square.reshape(-1, QUAD, number, BLOCK, width).transpose(0, 2, 1, 3, 4)
    tall = lax.all_gather(up, AXES, axis=1, tiled=True)
    tall = tall.reshape(2, number, BLOCK, QUAD, width).transpose(0, 1, 3, 2, 4)
    deep = lax.all_gather(down, AXES, axis=1, tiled=True).reshape(2, number, QUAD, BLOCK, width)
    half = number // 2
    quads = [square[0], tall[0], deep[0], square[1], square[2], tall[1], deep[1]]
    return [(quad[:half], quad[half:]) for quad in quads]


def scatter_whole(quads):
    joined = [jnp.concatenate(pair, axis=0).astype(F32) for pair in quads]
    number, _, _, width = joined[0].shape
    square = jnp.stack([joined[0], joined[3], joined[4]])
    square = square.transpose(0, 2, 1, 3, 4).reshape(3 * QUAD, width, width)
    tall = jnp.stack([joined[1], joined[5]]).transpose(0, 1, 3, 2, 4)
    tall = tall.reshape(2, width, QUAD * width)
    deep = jnp.stack([joined[2], joined[6]]).reshape(2, QUAD * width, width)
    return [
        lax.psum_scatter(part, AXES, scatter_dimension=1, tiled=True)
        for part in (square, tall, deep)
    ]


def direct_step(pairs, source, target, grad, attention, up, down, vectors, hidden, axis_sizes):
    net = Direct(axis_sizes)
    source_pair, target_pair, cross_pair = pairs
    width = source.shape[1]
    tall = up.reshape(2, BLOCK, QUAD, width).transpose(0, 2, 1, 3)
    deep = down.reshape(2, QUAD, BLOCK, width)
    a, b = net.table("a"), net.table("b")
    plain = jnp.arange(net.count, dtype=jnp.int32)
    cut = QUAD // 2

    later = jnp.concatenate([attention[QUAD:], tall[1], deep[1]], axis=0)
    later = lax.all_gather(later, AXES, axis=0, tiled=False)
    small = small_block(vectors, hidden, net.place, net.count, width)
    first = jnp.concatenate([attention[:QUAD], small[None]], axis=0)[None]
    second = jnp.concatenate([tall[0], deep[0]], axis=0)[None]
    first = net.grow(first, "a", 0, 1)
    second = net.grow(second, "a", 0, 1)
    first = net.grow(first, "a", 1, 1)
    second = net.grow(second, "a", 1, 1)
    query_key = net.grow(first[:, :cut], "a", 2, 1)
    value_out = net.grow(first[:, cut:], "b", 2, 1)
    up_one = net.grow(second[:, :QUAD], "a", 2, 1)
    down_one = net.grow(second[:, QUAD:], "b", 2, 1)
    query_key = net.grow(query_key, "a", 3, 1)
    value_out = net.grow(value_out, "b", 3, 1)
    enc_attend_w = [
        (a, net.finish(query_key, "a"), 0, cut),
        (b, net.finish(value_out, "b"), 0, cut),
    ]
    source, up_one, down_one = tie(source, up_one, down_one)
    up_one = net.grow(up_one, "a", 3, 1)
    down_one = net.grow(down_one, "b", 3, 1)
    enc_kept = attend_forward(source_pair, None, 0, source, None, enc_attend_w, False)
    small = enc_kept[8]
    enc_mid, up_one, down_one = tie(enc_kept[0], up_one, down_one)
    enc_feed_w = [
        (a, net.finish(up_one, "a"), 0, QUAD),
        (b, net.finish(down_one, "b"), 0, QUAD),
    ]
    enc_feed_kept = feed_forward(small, 5, HIDDEN_ROW, enc_mid, enc_feed_w)
    memory, later = tie(enc_feed_kept[0], later)
    self_w, cross_w, up_two, down_two = [
        (plain, [later], QUAD * slot, QUAD) for slot in range(4)
    ]
    self_kept = attend_forward(target_pair, small, 8, target, None, [self_w], True)
    dec_one = self_kept[0]
    cross_kept = attend_forward(cross_pair, small, 13, dec_one, memory, [cross_w], False)
    dec_two = cross_kept[0]
    result, two_grad, dec_feed_small, feed_two = feed_both(
        (a, b), small, 18, HIDDEN_ROW + QUAD, dec_two, grad, [up_two, down_two]
    )

    names, cuts = ("a", "b"), ((0, QUAD), (QUAD, 2 * QUAD))
    feed_two = Sum(net, "a", *feed_two).step()
    one_grad, memory_grad, cross_small, cross_q = attend_backward(
        (b,), cross_pair, small, 13, two_grad, cross_kept, dec_one, memory, [cross_w], False, None
    )
    feed_two = feed_two.split(names, cuts)
    memory_grad = tie_sums(memory_grad, *feed_two)
    feed_two = [item.step() for item in feed_two]
    cross_s = Sum(net, "b", *cross_q[0]).step()
    mid_grad, enc_feed_small, feed_one = feed_backward(
        (a, b), small, 5, memory_grad, enc_feed_kept, enc_mid, enc_feed_w
    )
    one_grad, mid_grad = tie(one_grad, mid_grad)
    one_grad = tie_sums(one_grad, *feed_two, cross_s)
    feed_two = [item.step() for item in feed_two]
    cross_s.step()
    feed_one = Sum(net, "a", *feed_one).step()
    target_grad, _, self_small, self_q = attend_backward(
        (a,), target_pair, small, 8, one_grad, self_kept, target, None, [self_w], True, None
    )
    mid_grad, target_grad = tie(mid_grad, target_grad)
    feed_one = feed_one.split(names, cuts)
    mid_grad = tie_sums(mid_grad, *feed_two, cross_s, *feed_one)
    cross_s.step()
    feed_one = [item.step() for item in feed_one]
    self_s = Sum(net, "a", *self_q[0]).step()
    others = (enc_feed_small, self_small, cross_small, dec_feed_small)
    source_grad, _, _, enc_q = attend_backward(
        (a, b), source_pair, small, 0, mid_grad, enc_kept, source, None, enc_attend_w, False, others
    )
    enc_s = [Sum(net, "a", *enc_q[0]).step(), Sum(net, "b", *enc_q[1]).step()]
    self_s.step()
    feed_one = [item.step() for item in feed_one]
    decoder = joined(feed_two + [cross_s], "a").steps(2)
    self_s.step()
    enc_s = [item.steps(2) for item in enc_s]
    encoder = joined(enc_s + [self_s] + feed_one, "a").steps(2)
    up_dec, down_dec, cross_g = jnp.split(decoder.total(), 3, axis=0)
    encoder = encoder.total()
    enc_g = jnp.concatenate([encoder[:QUAD], encoder[QUAD + 1 : 2 * QUAD + 1]], axis=0)
    up_enc, down_enc = encoder[2 * QUAD + 1 : 3 * QUAD + 1], encoder[3 * QUAD + 1 :]
    square_g = jnp.concatenate([enc_g, cross_g], axis=0)
    tall_g = jnp.stack([up_enc, up_dec]).transpose(0, 2, 1, 3).reshape(up.shape)
    deep_g = jnp.stack([down_enc, down_dec]).reshape(down.shape)
    small_g = small_share(encoder[QUAD], vectors, hidden, net.place, net.count)
    return (memory, result, source_grad, target_grad), (square_g, tall_g, deep_g) + small_g


def whole_step(pairs, source, target, grad, attention, up, down, vectors, hidden, axis_sizes):
    source_pair, target_pair, cross_pair = pairs
    small = gather_small(vectors, hidden)
    quads = gather_whole(attention, up, down)
    table = jnp.arange(source.shape[1] // BLOCK, dtype=jnp.int32)
    two = (table, table)
    parts = [(table, list(quad), 0, QUAD) for quad in quads]
    enc_kept = attend_forward(source_pair, small, 0, source, None, parts[:1], False)
    enc_mid = enc_kept[0]
    enc_feed_kept = feed_forward(small, 5, HIDDEN_ROW, enc_mid, parts[1:3])
    memory = enc_feed_kept[0]
    self_kept = attend_forward(target_pair, small, 8, target, None, parts[3:4], True)
    dec_one = self_kept[0]
    cross_kept = attend_forward(cross_pair, small, 13, dec_one, memory, parts[4:5], False)
    dec_two = cross_kept[0]
    result, two_grad, dec_feed_small, feed_two = feed_both(
        two, small, 18, HIDDEN_ROW + QUAD, dec_two, grad, parts[5:7]
    )
    one_grad, memory_grad, cross_small, cross_q = attend_backward(
        two[:1], cross_pair, small, 13, two_grad, cross_kept, dec_one, memory, parts[4:5], False, None
    )
    target_grad, _, self_small, self_q = attend_backward(
        two[:1], target_pair, small, 8, one_grad, self_kept, target, None, parts[3:4], True, None
    )
    mid_grad, enc_feed_small, feed_one = feed_backward(
        two, small, 5, memory_grad, enc_feed_kept, enc_mid, parts[1:3]
    )
    source_grad, _, enc_small, enc_q = attend_backward(
        two[:1], source_pair, small, 0, mid_grad, enc_kept, source, None, parts[:1], False, None
    )
    quads = [enc_q[0]]
    quads += [[half[:, low : low + QUAD] for half in feed_one] for low in (0, QUAD)]
    quads += [self_q[0], cross_q[0]]
    quads += [[half[:, low : low + QUAD] for half in feed_two] for low in (0, QUAD)]
    smalls = (enc_small, enc_feed_small, self_small, cross_small, dec_feed_small)
    count = axis_sizes[0] * axis_sizes[1]
    shares = scatter_small(smalls, vectors, hidden, lax.axis_index(AXES), count)
    return (memory, result, source_grad, target_grad), tuple(scatter_whole(quads)) + shares


def per_device(
    axis_sizes,
    source_tokens,
    target_tokens,
    source_segments,
    target_segments,
    output_grad,
    attention_weight,
    up_weight,
    down_weight,
    vectors,
    hidden_bias,
    *moments,
):
    masters = (attention_weight, up_weight, down_weight, vectors, hidden_bias)
    firsts = moments[:5]
    seconds = moments[5:]
    width = source_tokens.shape[2]
    pairs = (
        (source_segments, source_segments),
        (target_segments, target_segments),
        (target_segments, source_segments),
    )
    direct = axis_sizes[0] * axis_sizes[1] * BLOCK == width
    (memory, result, source_grad, target_grad), grads = (direct_step if direct else whole_step)(
        pairs,
        source_tokens[0],
        target_tokens[0],
        output_grad[0],
        attention_weight.astype(BF),
        up_weight.astype(BF),
        down_weight.astype(BF),
        vectors,
        hidden_bias,
        axis_sizes,
    )
    updated = [
        adam_update(
            masters[slot], grads[slot], firsts[slot], seconds[slot], RATES[slot], DECAYS[slot]
        )
        for slot in range(5)
    ]
    tokens = (memory[None], result[None], source_grad[None], target_grad[None])
    return tokens + tuple(updated[slot][kind] for kind in range(4) for slot in range(5))


def solution(mesh):
    rows = P(AXES, None, None)
    line = P(AXES, None)
    matrix = P(None, AXES, None)
    vector = P(None, AXES)
    state = (matrix, matrix, matrix, vector, vector)
    return jax.shard_map(
        functools.partial(per_device, (mesh.shape["dp"], mesh.shape["fsdp"])),
        mesh=mesh,
        in_specs=(rows, rows, line, line, rows) + state * 3,
        out_specs=(rows,) * 4 + state * 4,
        check_vma=False,
    )
```

```python
import functools

import jax
import jax.numpy as jnp
from jax import lax
from jax.experimental import pallas as pl
from jax.experimental.pallas import tpu as pltpu
from jax.sharding import PartitionSpec as P

HEADS = 8
STEP = 10
EPS_NORM = 1e-05
EPS_ADAM = 1e-08
BETA_ONE = 0.9
BETA_TWO = 0.999
LOWEST = -1e30
RATES = (0.05, 0.05, 0.05, 0.3, 0.3)
DECAYS = (0.01, 0.01, 0.01, 0.0, 0.0)
AXES = ("dp", "fsdp")
QUAD = 4
BLOCK = 16
LANES = 128
SMALL_ROWS = 32
HIDDEN_ROW = 24
BF = jnp.bfloat16
F32 = jnp.float32
VMEM = pl.BlockSpec(memory_space=pltpu.VMEM)
SMEM = pl.BlockSpec(memory_space=pltpu.SMEM)
ANY = pl.BlockSpec(memory_space=pl.ANY)
ROOT_TWO_PI = 0.7978845608028654
CUBIC = 0.044715


def dot(left, right):
    return jnp.dot(left, right, preferred_element_type=F32)


def dot_nt(left, right):
    return lax.dot_general(left, right, (((1,), (1,)), ((), ())), preferred_element_type=F32)


def load_start(part, place, sems):
    table, arrays, low, number = part
    at = 0
    for slot, array in enumerate(arrays):
        for index in range(array.shape[0]):
            source = array.at[index, low : low + number]
            pltpu.make_async_copy(source, place(table[at]), sems.at[slot]).start()
            at += 1


def load_wait(part, sems):
    table, arrays, low, number = part
    for slot, array in enumerate(arrays):
        whole = array.at[:, low : low + number]
        pltpu.make_async_copy(whole, whole, sems.at[slot]).wait()


def store_start(part, place, sems):
    table, arrays, low, number = part
    half = arrays[0].shape[0]
    for index in range(half):
        for slot in (1, 0):
            target = arrays[slot].at[index, low : low + number]
            source = place(table[slot * half + index])
            pltpu.make_async_copy(source, target, sems.at[slot]).start()


def row_place(scratch, low, high):
    def place(block):
        start = pl.multiple_of(block * BLOCK, BLOCK)
        return scratch.at[low:high, pl.ds(start, BLOCK), :]

    return place


def block_place(scratch):
    return lambda block: scratch.at[block]


def norm_forward(pre, gain, shift, out_ref, hat_ref, rstd_ref):
    mean = jnp.mean(pre, axis=-1, keepdims=True)
    centred = pre - mean
    spread = jnp.mean(centred * centred, axis=-1, keepdims=True)
    rstd = lax.rsqrt(spread + EPS_NORM)
    hat = centred * rstd
    hat_ref[...] = hat
    rstd_ref[...] = jnp.broadcast_to(rstd, rstd_ref.shape)
    out_ref[...] = hat * gain + shift


def norm_backward(grad, hat, rstd, gain):
    gain_grad = jnp.sum(grad * hat, axis=0, keepdims=True)
    shift_grad = jnp.sum(grad, axis=0, keepdims=True)
    scaled = grad * gain
    one = jnp.mean(scaled, axis=-1, keepdims=True)
    two = jnp.mean(scaled * hat, axis=-1, keepdims=True)
    return rstd * (scaled - one - hat * two), gain_grad, shift_grad


def lane_mask(rows):
    return lax.broadcasted_iota(jnp.int32, (rows, LANES), 1) < LANES // 2


def stacked_pair(block):
    first = lane_mask(block.shape[0])
    zero = jnp.zeros_like(block)
    return jnp.concatenate([jnp.where(first, block, zero), jnp.where(first, zero, block)], axis=0)


def merged_pair(stacked):
    rows = stacked.shape[0] // 2
    return jnp.where(lane_mask(rows), stacked[:rows], stacked[rows:])


def mask_fill(bias_ref, column_seg, row_seg, causal, transposed):
    length = bias_ref.shape[0]
    column = jnp.broadcast_to(column_seg, (LANES, length)).T
    for at in range(0, length, LANES):
        same = column == row_seg[:, at : at + LANES]
        if causal:
            down = lax.broadcasted_iota(jnp.int32, (length, LANES), 0)
            along = lax.broadcasted_iota(jnp.int32, (length, LANES), 1) + at
            order = (down <= along) if transposed else (along <= down)
            same = same & order
        bias_ref[:, at : at + LANES] = jnp.where(same, 0.0, LOWEST)


def take_parts(refs, layout, tables):
    parts = []
    for slot, (arrays, low, number) in enumerate(layout):
        parts.append((tables[slot], [refs.pop(0) for _ in range(arrays)], low, number))
    return parts


def small_part(part):
    table, arrays, low, number = part
    return table, arrays, low + number, 1


def small_join(blocks_ref):
    count = blocks_ref.shape[0]
    groups = blocks_ref.shape[3] // LANES
    per = count // groups
    vectors = []
    hidden = [[], []]
    for group in range(groups):
        total = blocks_ref[group * per, 0, :8].astype(F32)
        for at in range(group * per + 1, (group + 1) * per):
            total = total + blocks_ref[at, 0, :8].astype(F32)
        columns = [total[:, at : at + LANES] for at in range(0, 4 * LANES, LANES)]
        vectors.append(jnp.concatenate(columns[:3], axis=0))
        for layer in range(2):
            rows = [columns[3][4 * layer + at : 4 * layer + at + 1] for at in range(4)]
            hidden[layer].append(jnp.concatenate(rows, axis=1))
    return jnp.concatenate([jnp.concatenate(vectors, axis=1)] + hidden[0] + hidden[1], axis=0)


def small_split(whole, group):
    lanes = slice(group * LANES, (group + 1) * LANES)
    columns = [whole[at : at + 8, lanes] for at in (0, 8, 16)]
    rows = []
    for layer in range(2):
        row = whole[24 + 4 * layer + group : 25 + 4 * layer + group]
        rows += [row[:, at : at + LANES] for at in range(0, 4 * LANES, LANES)]
    columns.append(jnp.concatenate(rows, axis=0))
    block = jnp.concatenate(columns, axis=1)
    return jnp.concatenate([block, jnp.zeros_like(block)], axis=0).astype(BF)


def attend_forward_kernel(layout, cross, causal, base, joins, *refs):
    refs = list(refs)
    tables = [refs.pop(0) for _ in layout]
    query_seg = refs.pop(0)
    key_seg = refs.pop(0)
    small = None if joins else refs.pop(0)
    rows_ref = refs.pop(0)
    memory_ref = refs.pop(0) if cross else None
    parts = take_parts(refs, layout, tables)
    out_ref, hat_ref, rstd_ref, q_ref, k_ref, v_ref, o_ref, lse_ref = [refs.pop(0) for _ in range(8)]
    if joins:
        small = refs.pop(0)
        blocks_ref = refs.pop()
        extra = small_part(parts[-1])
    w_ref, bias_ref, sems = refs
    first = 0
    if joins:
        load_start(extra, lambda block: blocks_ref.at[block], sems.at[len(parts)])
    for slot, part in enumerate(parts):
        load_start(part, row_place(w_ref, first, first + part[3]), sems.at[slot])
        first += part[3]
    length, width = rows_ref.shape
    mask_fill(bias_ref, query_seg[...], key_seg[...], causal, False)
    rows = rows_ref[...].astype(BF)
    keys = memory_ref[...].astype(BF) if cross else rows
    if joins:
        load_wait(extra, sems.at[len(parts)])
        small[...] = small_join(blocks_ref)
    for slot, part in enumerate(parts):
        load_wait(part, sems.at[slot])
    scale = (width // HEADS) ** (-0.5)
    q_ref[...] = (dot(rows, w_ref[0]) + small[base : base + 1]).astype(BF) * jnp.asarray(scale, BF)
    k_ref[...] = dot(keys, w_ref[1]).astype(BF)
    v_ref[...] = (dot(keys, w_ref[2]) + small[base + 1 : base + 2]).astype(BF)
    lane = lax.broadcasted_iota(jnp.int32, (LANES, LANES), 1)
    for at in range(0, length, LANES):
        reach = at + LANES if causal else length
        logs = jnp.zeros((LANES, LANES), F32)
        for pair in range(HEADS // 2):
            lanes = slice(pair * LANES, (pair + 1) * LANES)
            stacked = stacked_pair(q_ref[at : at + LANES, lanes])
            scores = dot_nt(stacked, k_ref[:reach, lanes])
            bias = bias_ref[at : at + LANES, :reach]
            scores = scores + jnp.concatenate([bias, bias], axis=0)
            largest = jnp.max(scores, axis=-1, keepdims=True)
            exponent = jnp.exp(scores - largest).astype(BF)
            values = jnp.concatenate([v_ref[:reach, lanes], jnp.ones((reach, LANES), BF)], axis=1)
            mixed = dot(exponent, values)
            total = mixed[:, LANES:]
            o_ref[at : at + LANES, lanes] = merged_pair(mixed[:, :LANES] / total).astype(BF)
            log_total = largest + jnp.log(total)
            logs = jnp.where(lane == 2 * pair, log_total[:LANES], logs)
            logs = jnp.where(lane == 2 * pair + 1, log_total[LANES:], logs)
        lse_ref[:, at : at + LANES] = logs.T[:HEADS]
    attended = dot(o_ref[...], w_ref[3]) + small[base + 2 : base + 3]
    pre = rows_ref[...].astype(F32) + attended
    norm_forward(pre, small[base + 3 : base + 4], small[base + 4 : base + 5], out_ref, hat_ref, rstd_ref)


def attend_backward_kernel(layout, cross, causal, base, splits, *refs):
    refs = list(refs)
    tables = [refs.pop(0) for _ in layout]
    out_tables = [refs.pop(0) for _ in layout]
    query_seg = refs.pop(0)
    key_seg = refs.pop(0)
    small = refs.pop(0)
    grad_ref = refs.pop(0)
    hat_ref, rstd_ref = refs.pop(0), refs.pop(0)
    rows_ref = refs.pop(0)
    memory_ref = refs.pop(0) if cross else None
    q_ref, k_ref, v_ref, o_ref, lse_ref = [refs.pop(0) for _ in range(5)]
    others = [refs.pop(0) for _ in range(4)] if splits else None
    parts = take_parts(refs, layout, tables)
    rows_out = refs.pop(0)
    memory_out = refs.pop(0) if cross else None
    small_out = None if splits else refs.pop(0)
    outs = take_parts(refs, [(2, 0, number) for _, _, number in layout], out_tables)
    blocks_ref = refs.pop() if splits else None
    w_ref, dw_ref, bias_ref, dout_ref, dq_t_ref, dk_ref, dv_ref, kt_ref, sems = refs
    first = 0
    for slot, part in enumerate(parts):
        load_start(part, row_place(w_ref, first, first + part[3]), sems.at[slot])
        first += part[3]
    length, width = rows_ref.shape
    head = width // HEADS
    scale = head ** (-0.5)
    mask_fill(bias_ref, key_seg[...], query_seg[...], causal, True)
    kt_ref[...] = k_ref[...].T
    pre_grad, gain_grad, shift_grad = norm_backward(
        grad_ref[...], hat_ref[...], rstd_ref[:, :1], small[base + 3 : base + 4]
    )
    rows_out[...] = pre_grad
    low = pre_grad.astype(BF)
    for slot, part in enumerate(parts):
        load_wait(part, sems.at[slot])
    dout_ref[...] = dot_nt(low, w_ref[3]).astype(BF)
    dw_ref[3] = dot(o_ref[...].T, low).astype(BF)
    out_bias = jnp.sum(low.astype(F32), axis=0, keepdims=True)
    product = dout_ref[...].astype(F32) * o_ref[...].astype(F32)
    high = product.astype(BF)
    rest = (product - high.astype(F32)).astype(BF)
    picker = lax.broadcasted_iota(jnp.int32, (BLOCK, width), 1) // head
    picker = (picker == lax.broadcasted_iota(jnp.int32, (BLOCK, width), 0)).astype(BF)
    row_dots = dot_nt(picker, high) + dot_nt(picker, rest)
    for pair in range(HEADS // 2):
        lanes = slice(pair * LANES, (pair + 1) * LANES)
        for at in range(0, length, LANES):
            begin = at if causal else 0
            query = q_ref[begin:, lanes]
            dout = dout_ref[begin:, lanes]
            scores = dot_nt(stacked_pair(k_ref[at : at + LANES, lanes]), query)
            prob_grad = dot_nt(stacked_pair(v_ref[at : at + LANES, lanes]), dout)
            bias = bias_ref[at : at + LANES, begin:]
            probs = []
            score_grads = []
            for part in range(2):
                which = 2 * pair + part
                half = slice(part * LANES, (part + 1) * LANES)
                prob = jnp.exp(scores[half] + (bias - lse_ref[which : which + 1, begin:]))
                probs.append(prob.astype(BF))
                row_dot = row_dots[which : which + 1, begin:]
                score_grads.append((prob * (prob_grad[half] - row_dot)).astype(BF))
                at_t = pair * LANES + part * head
                back = dot(kt_ref[at_t : at_t + head, at : at + LANES], score_grads[part])
                if at == 0:
                    dq_t_ref[at_t : at_t + head, :] = back
                else:
                    dq_t_ref[at_t : at_t + head, begin:] += back
            value_back = dot(jnp.concatenate(probs, axis=0), dout)
            dv_ref[at : at + LANES, lanes] = merged_pair(value_back).astype(BF)
            key_back = dot(jnp.concatenate(score_grads, axis=0), query)
            dk_ref[at : at + LANES, lanes] = merged_pair(key_back).astype(BF)
    query_grad = (dq_t_ref[...] * scale).T.astype(BF)
    key_grad = dk_ref[...]
    value_grad = dv_ref[...]
    turned = rows_ref[...].astype(BF).T
    dw_ref[0] = dot(turned, query_grad).astype(BF)
    if cross:
        turned = memory_ref[...].astype(BF).T
    dw_ref[1] = dot(turned, key_grad).astype(BF)
    dw_ref[2] = dot(turned, value_grad).astype(BF)
    first = 0
    for slot, part in enumerate(outs):
        store_start(part, row_place(dw_ref, first, first + part[3]), sems.at[slot])
        first += part[3]
    rows_back = rows_out[...] + dot_nt(query_grad, w_ref[0])
    memory_back = dot_nt(key_grad, w_ref[1]) + dot_nt(value_grad, w_ref[2])
    if cross:
        rows_out[...] = rows_back
        memory_out[...] = memory_back
    else:
        rows_out[...] = rows_back + memory_back
    query_bias = jnp.sum(query_grad.astype(F32), axis=0, keepdims=True)
    value_bias = jnp.sum(value_grad.astype(F32), axis=0, keepdims=True)
    spare = jnp.zeros((3, width), F32)
    own = jnp.concatenate(
        [query_bias, value_bias, out_bias, gain_grad, shift_grad, spare], axis=0
    )
    if splits:
        enc_feed, self_attend, cross_attend, dec_feed = [other[...] for other in others]
        whole = small_rows(own, enc_feed, self_attend, cross_attend, dec_feed)
        groups = blocks_ref.shape[0]
        for group in range(groups):
            blocks_ref[group, 0] = small_split(whole, group)
        extra = small_part(outs[-1])
        per = 2 * extra[1][0].shape[0] // groups
        store_start(extra, lambda block: blocks_ref.at[block // per], sems.at[len(parts)])
        load_wait(extra, sems.at[len(parts)])
    else:
        small_out[...] = own
    for slot, part in enumerate(outs):
        load_wait(part, sems.at[slot])


def small_rows(enc_attend, enc_feed, self_attend, cross_attend, dec_feed):
    return jnp.concatenate(
        [
            enc_attend[:5],
            enc_feed[:3],
            self_attend[:5],
            cross_attend[:5],
            dec_feed[:3],
            dec_feed[7:],
            dec_feed[7:],
            dec_feed[7:],
            enc_feed[3:7],
            dec_feed[3:7],
        ],
        axis=0,
    )


def gelu_parts(pre):
    inner = ROOT_TWO_PI * (pre + CUBIC * pre * pre * pre)
    curve = jnp.tanh(inner)
    return curve, 0.5 * pre * (1.0 + curve)


def gelu_slope(pre, curve):
    bend = ROOT_TWO_PI * (1.0 + 3.0 * CUBIC * pre * pre)
    return 0.5 * (1.0 + curve) + 0.5 * pre * (1.0 - curve * curve) * bend


def chunk_of(ref, index):
    number = ref.shape[0] // QUAD
    part = ref[index * number : (index + 1) * number]
    return part.reshape(number * ref.shape[1] * ref.shape[2], ref.shape[3])


def feed_forward_steps(small, base, hidden_at, rows_ref, up_ref, down_ref, pre_ref):
    rows = rows_ref[...].astype(BF)
    total = rows_ref[...] + small[base : base + 1]
    for index in range(QUAD):
        at = hidden_at + index
        pre = dot(rows, up_ref[index]) + small[at : at + 1]
        pre_ref[index] = pre
        active = gelu_parts(pre)[1].astype(BF)
        total = total + dot(active, chunk_of(down_ref, index))
    return total


def feed_backward_steps(pre_grad, rows_ref, up_ref, down_ref, pre_ref, dup_ref, ddown_ref, rows_out):
    low = pre_grad.astype(BF)
    turned = rows_ref[...].astype(BF).T
    total = pre_grad
    hidden_grads = []
    number = ddown_ref.shape[0] // QUAD
    for index in range(QUAD):
        pre = pre_ref[index]
        curve, active = gelu_parts(pre)
        down_grad = dot(active.astype(BF).T, low).astype(BF)
        ddown_ref[index * number : (index + 1) * number] = down_grad.reshape(
            (number,) + ddown_ref.shape[1:]
        )
        back = dot_nt(low, chunk_of(down_ref, index))
        hidden = (back * gelu_slope(pre, curve)).astype(BF)
        hidden_grads.append(jnp.sum(hidden.astype(F32), axis=0, keepdims=True))
        dup_ref[index] = dot(turned, hidden).astype(BF)
        total = total + dot_nt(hidden, up_ref[index])
    rows_out[...] = total
    out_bias = jnp.sum(low.astype(F32), axis=0, keepdims=True)
    return out_bias, hidden_grads


def load_feed(parts, up_ref, down_ref, sems):
    load_start(parts[0], row_place(up_ref, 0, QUAD), sems.at[0])
    load_start(parts[1], block_place(down_ref), sems.at[1])


def store_feed(outs, dup_ref, ddown_ref, sems):
    store_start(outs[1], block_place(ddown_ref), sems.at[1])
    store_start(outs[0], row_place(dup_ref, 0, QUAD), sems.at[0])


def wait_feed(parts, sems):
    for slot, part in enumerate(parts):
        load_wait(part, sems.at[slot])


def feed_outs(refs, tables):
    arrays = [refs.pop(0), refs.pop(0)]
    return [(tables[slot], arrays, slot * QUAD, QUAD) for slot in range(2)]


def feed_small(out_bias, gain_grad, shift_grad, hidden_grads):
    spare = jnp.zeros_like(out_bias)
    return jnp.concatenate([out_bias, gain_grad, shift_grad] + hidden_grads + [spare], axis=0)


def feed_forward_kernel(layout, base, hidden_at, *refs):
    refs = list(refs)
    tables = [refs.pop(0), refs.pop(0)]
    small, rows_ref = refs.pop(0), refs.pop(0)
    parts = take_parts(refs, layout, tables)
    out_ref, hat_ref, rstd_ref, pre_ref, up_ref, down_ref, sems = refs
    load_feed(parts, up_ref, down_ref, sems)
    wait_feed(parts, sems)
    pre = feed_forward_steps(small, base, hidden_at, rows_ref, up_ref, down_ref, pre_ref)
    norm_forward(pre, small[base + 1 : base + 2], small[base + 2 : base + 3], out_ref, hat_ref, rstd_ref)


def feed_backward_kernel(layout, base, *refs):
    refs = list(refs)
    tables = [refs.pop(0), refs.pop(0)]
    out_tables = [refs.pop(0), refs.pop(0)]
    small, grad_ref, hat_ref, rstd_ref, rows_ref, pre_ref = [refs.pop(0) for _ in range(6)]
    parts = take_parts(refs, layout, tables)
    rows_out, small_out = refs.pop(0), refs.pop(0)
    outs = feed_outs(refs, out_tables)
    up_ref, down_ref, dup_ref, ddown_ref, sems, out_sems = refs
    load_feed(parts, up_ref, down_ref, sems)
    pre_grad, gain_grad, shift_grad = norm_backward(
        grad_ref[...], hat_ref[...], rstd_ref[:, :1], small[base + 1 : base + 2]
    )
    wait_feed(parts, sems)
    out_bias, hidden_grads = feed_backward_steps(
        pre_grad, rows_ref, up_ref, down_ref, pre_ref, dup_ref, ddown_ref, rows_out
    )
    store_feed(outs, dup_ref, ddown_ref, out_sems)
    small_out[...] = feed_small(out_bias, gain_grad, shift_grad, hidden_grads)
    wait_feed(outs, out_sems)


def feed_both_kernel(layout, base, hidden_at, *refs):
    refs = list(refs)
    tables = [refs.pop(0), refs.pop(0)]
    out_tables = [refs.pop(0), refs.pop(0)]
    small, rows_ref, grad_ref = [refs.pop(0) for _ in range(3)]
    parts = take_parts(refs, layout, tables)
    out_ref, rows_out, small_out = [refs.pop(0) for _ in range(3)]
    outs = feed_outs(refs, out_tables)
    up_ref, down_ref, dup_ref, ddown_ref, pre_ref, hat_ref, rstd_ref, sems, out_sems = refs
    load_feed(parts, up_ref, down_ref, sems)
    wait_feed(parts, sems)
    pre = feed_forward_steps(small, base, hidden_at, rows_ref, up_ref, down_ref, pre_ref)
    gain = small[base + 1 : base + 2]
    norm_forward(pre, gain, small[base + 2 : base + 3], out_ref, hat_ref, rstd_ref)
    pre_grad, gain_grad, shift_grad = norm_backward(
        grad_ref[...].astype(F32), hat_ref[...], rstd_ref[:, :1], gain
    )
    out_bias, hidden_grads = feed_backward_steps(
        pre_grad, rows_ref, up_ref, down_ref, pre_ref, dup_ref, ddown_ref, rows_out
    )
    store_feed(outs, dup_ref, ddown_ref, out_sems)
    small_out[...] = feed_small(out_bias, gain_grad, shift_grad, hidden_grads)
    wait_feed(outs, out_sems)


def shaped(shape, dtype=F32):
    return jax.ShapeDtypeStruct(shape, dtype)


def call(kernel, ins, specs, outs, out_specs, scratch, flops, moved):
    return pl.pallas_call(
        kernel,
        out_shape=outs,
        in_specs=specs,
        out_specs=out_specs,
        scratch_shapes=scratch,
        cost_estimate=pl.CostEstimate(flops=flops, bytes_accessed=moved, transcendentals=0),
        compiler_params=pltpu.CompilerParams(vmem_limit_bytes=40 * 1024 * 1024),
    )(*ins)


def layout_of(parts):
    return [(len(arrays), low, number) for _, arrays, low, number in parts]


def arrays_of(parts):
    return [array for part in parts for array in part[1]]


def most(parts):
    return max(len(part[1]) for part in parts)


def halves(width, number):
    return [shaped((width // BLOCK // 2, number, BLOCK, width), BF)] * 2


def attend_forward(segments, small, base, rows, memory, parts, causal):
    length, width = rows.shape
    cross = memory is not None
    joins = small is None
    ins = [part[0] for part in parts] + list(segments) + ([] if joins else [small]) + [rows]
    ins += [memory] if cross else []
    specs = [SMEM] * len(parts) + [VMEM] * (len(ins) - len(parts))
    arrays = arrays_of(parts)
    ins += arrays
    specs += [ANY] * len(arrays)
    outs = [shaped((length, width)), shaped((length, width)), shaped((length, LANES))]
    outs += [shaped((length, width), BF)] * 4 + [shaped((HEADS, length))]
    outs += [shaped((SMALL_ROWS, width))] if joins else []
    scratch = [
        pltpu.VMEM((QUAD, width, width), BF),
        pltpu.VMEM((length, length), F32),
        pltpu.SemaphoreType.DMA((len(parts) + 1, most(parts))),
    ]
    scratch += [pltpu.VMEM((width // BLOCK, 1, BLOCK, width), BF)] if joins else []
    kernel = functools.partial(attend_forward_kernel, layout_of(parts), cross, causal, base, joins)
    flops = 8 * length * width * width + 16 * length * length * width
    return call(kernel, ins, specs, outs, [VMEM] * len(outs), scratch, flops, 8_000_000)


def attend_backward(
    out_tables, segments, small, base, grad, kept, rows, memory, parts, causal, others
):
    length, width = rows.shape
    cross = memory is not None
    splits = others is not None
    hat, rstd, q, k, v, o, lse = kept[1:8]
    ins = [part[0] for part in parts] + list(out_tables)
    specs = [SMEM] * len(ins)
    ins += list(segments) + [small, grad, hat, rstd, rows]
    ins += ([memory] if cross else []) + [q, k, v, o, lse] + list(others or ())
    specs += [VMEM] * (len(ins) - len(specs))
    arrays = arrays_of(parts)
    ins += arrays
    specs += [ANY] * len(arrays)
    outs = [shaped((length, width))] * (2 if cross else 1)
    outs += [] if splits else [shaped((8, width))]
    out_specs = [VMEM] * len(outs) + [ANY] * (2 * len(parts))
    for slot, part in enumerate(parts):
        outs += halves(width, part[3] + (1 if splits and slot == len(parts) - 1 else 0))
    scratch = [
        pltpu.VMEM((QUAD, width, width), BF),
        pltpu.VMEM((QUAD, width, width), BF),
        pltpu.VMEM((length, length), F32),
        pltpu.VMEM((length, width), BF),
        pltpu.VMEM((width, length), F32),
        pltpu.VMEM((length, width), BF),
        pltpu.VMEM((length, width), BF),
        pltpu.VMEM((width, length), BF),
        pltpu.SemaphoreType.DMA((len(parts) + 1, 2)),
    ]
    scratch += [pltpu.VMEM((width // LANES, 1, BLOCK, width), BF)] if splits else []
    kernel = functools.partial(
        attend_backward_kernel, layout_of(parts), cross, causal, base, splits
    )
    flops = 16 * length * width * width + 40 * length * length * width
    results = list(call(kernel, ins, specs, outs, out_specs, scratch, flops, 12_000_000))
    rows_grad = results.pop(0)
    memory_grad = results.pop(0) if cross else None
    small_grad = None if splits else results.pop(0)
    return rows_grad, memory_grad, small_grad, [results[2 * i : 2 * i + 2] for i in range(len(parts))]


def feed_scratch(width, grads):
    number = width // BLOCK
    once = [pltpu.VMEM((QUAD, width, width), BF), pltpu.VMEM((number, QUAD, BLOCK, width), BF)]
    return once * (2 if grads else 1)


def feed_forward(small, base, hidden_at, rows, parts):
    length, width = rows.shape
    arrays = arrays_of(parts)
    ins = [part[0] for part in parts] + [small, rows] + arrays
    specs = [SMEM] * 2 + [VMEM] * 2 + [ANY] * len(arrays)
    outs = [shaped((length, width)), shaped((length, width)), shaped((length, LANES))]
    outs += [shaped((QUAD, length, width))]
    scratch = feed_scratch(width, False) + [pltpu.SemaphoreType.DMA((2, most(parts)))]
    kernel = functools.partial(feed_forward_kernel, layout_of(parts), base, hidden_at)
    flops = 16 * length * width * width
    return call(kernel, ins, specs, outs, [VMEM] * len(outs), scratch, flops, 10_000_000)


def feed_backward(out_tables, small, base, grad, kept, rows, parts):
    length, width = rows.shape
    _, hat, rstd, pre = kept
    arrays = arrays_of(parts)
    ins = [part[0] for part in parts] + list(out_tables) + [small, grad, hat, rstd, rows, pre]
    ins += arrays
    specs = [SMEM] * 4 + [VMEM] * 6 + [ANY] * len(arrays)
    outs = [shaped((length, width)), shaped((8, width))] + halves(width, 2 * QUAD)
    out_specs = [VMEM] * 2 + [ANY] * 2
    scratch = feed_scratch(width, True)
    scratch += [pltpu.SemaphoreType.DMA((2, most(parts))), pltpu.SemaphoreType.DMA((2, 2))]
    kernel = functools.partial(feed_backward_kernel, layout_of(parts), base)
    flops = 32 * length * width * width
    results = call(kernel, ins, specs, outs, out_specs, scratch, flops, 14_000_000)
    return results[0], results[1], results[2:4]


def feed_both(out_tables, small, base, hidden_at, rows, grad, parts):
    length, width = rows.shape
    arrays = arrays_of(parts)
    ins = [part[0] for part in parts] + list(out_tables) + [small, rows, grad] + arrays
    specs = [SMEM] * 4 + [VMEM] * 3 + [ANY] * len(arrays)
    outs = [shaped((length, width)), shaped((length, width)), shaped((8, width))]
    outs += halves(width, 2 * QUAD)
    out_specs = [VMEM] * 3 + [ANY] * 2
    scratch = feed_scratch(width, True) + [
        pltpu.VMEM((QUAD, length, width), F32),
        pltpu.VMEM((length, width), F32),
        pltpu.VMEM((length, LANES), F32),
        pltpu.SemaphoreType.DMA((2, most(parts))),
        pltpu.SemaphoreType.DMA((2, 2)),
    ]
    kernel = functools.partial(feed_both_kernel, layout_of(parts), base, hidden_at)
    flops = 48 * length * width * width
    results = call(kernel, ins, specs, outs, out_specs, scratch, flops, 12_000_000)
    return results[0], results[1], results[2], results[3:5]


def tie(*arrays):
    return lax.optimization_barrier(arrays)


class Direct:
    def __init__(self, axis_sizes):
        outer, inner = axis_sizes
        self.count = outer * inner
        inner_bits = inner.bit_length() - 1
        bits = self.count.bit_length() - 1
        core = [inner_bits]
        across = list(range(inner_bits + 1, bits))
        up = [0]
        along = list(range(1, inner_bits))
        self.orders = {
            "a": core + across + up + along,
            "b": core + up + across + along,
        }
        self.place = lax.axis_index(AXES)

    def hop(self, array, bit):
        return lax.ppermute(array, AXES, [(at, at ^ (1 << bit)) for at in range(self.count)])

    def table(self, name):
        order = self.orders[name]
        index = jnp.arange(self.count, dtype=jnp.int32)
        block = jnp.zeros_like(index)
        for at, bit in enumerate(order):
            block = block | (((index >> (len(order) - 1 - at)) & 1) << bit)
        return block ^ self.place

    def grow(self, array, name, step, *tokens):
        arrived = self.hop(array, self.orders[name][::-1][step])
        if tokens:
            arrived = tie(arrived, *tokens)[0]
        return jnp.concatenate([array, arrived], axis=0)

    def finish(self, array, name):
        return [array, self.hop(array, self.orders[name][0])]


class Sum:
    def __init__(self, net, name, segments, send, done):
        self.net = net
        self.name = name
        self.segments = segments
        self.send = send
        self.done = done

    def step(self):
        arrived = self.net.hop(self.send, self.net.orders[self.name][self.done])
        self.done += 1
        low = 0
        made = []
        for width, pieces in self.segments:
            made.append((width, pieces + [(arrived, low)]))
            low += width
        self.segments = made
        return self

    def number(self):
        return self.segments[0][1][-1][0].shape[0]

    def split(self, names):
        return [
            Sum(self.net, name, [segment], None, self.done)
            for name, segment in zip(names, self.segments)
        ]


def sum_of(net, name, keep, send, widths):
    low = 0
    segments = []
    for width in widths:
        segments.append((width, [(keep, low)]))
        low += width
    return Sum(net, name, segments, send, 0)


def joined(sums):
    segments = [segment for item in sums for segment in item.segments]
    return Sum(sums[0].net, sums[0].name, segments, None, sums[0].done)


def combine_kernel(plan, count, *refs):
    arrays, outs, buffers, sems = refs[:count], refs[count:-2], refs[-2], refs[-1]
    at = 0
    starts = []
    for _, number, _, width, pieces in plan:
        for index, low in pieces:
            source = arrays[index].at[number : 2 * number, low : low + width]
            target = buffers.at[at, :number, :width]
            copy = pltpu.make_async_copy(source, target, sems.at[len(starts)])
            copy.start()
            starts.append(copy)
            at += 1
    at = 0
    for slot, number, first, width, pieces in plan:
        for index in range(len(pieces)):
            starts[at + index].wait()
        begin = at

        def body(block, carry, begin=begin, slot=slot, first=first, width=width, pieces=pieces):
            value = buffers[begin, block, :width].astype(F32)
            for index in range(1, len(pieces)):
                value = value + buffers[begin + index, block, :width].astype(F32)
            outs[slot][block, first : first + width] = value.astype(BF)
            return carry

        lax.fori_loop(0, number, body, 0)
        at += len(pieces)


def settle(sums, *tokens):
    arrays = []
    plan = []
    shapes = []
    for slot, item in enumerate(sums):
        number = item.number() // 2
        first = 0
        for width, pieces in item.segments:
            entry = []
            for array, low in pieces:
                found = [at for at, other in enumerate(arrays) if other is array]
                if not found:
                    arrays.append(array)
                entry.append((found[0] if found else len(arrays) - 1, low))
            plan.append((slot, number, first, width, entry))
            first += width
        block = item.segments[0][1][0][0].shape[2:]
        shapes.append(shaped((number, first) + block, BF))
    tied = list(tie(*arrays, *tokens))[: len(arrays)] if tokens else arrays
    buffers = sum(len(entry[4]) for entry in plan)
    size = (max(entry[1] for entry in plan), max(entry[3] for entry in plan)) + shapes[0].shape[2:]
    moved = sum(entry[1] * entry[3] * (len(entry[4]) + 1) for entry in plan) * 16384
    sends = pl.pallas_call(
        functools.partial(combine_kernel, plan, len(tied)),
        out_shape=shapes,
        in_specs=[ANY] * len(tied),
        out_specs=[VMEM] * len(shapes),
        scratch_shapes=[pltpu.VMEM((buffers,) + size, BF), pltpu.SemaphoreType.DMA((buffers,))],
        cost_estimate=pl.CostEstimate(flops=0, bytes_accessed=moved, transcendentals=0),
        compiler_params=pltpu.CompilerParams(vmem_limit_bytes=32 * 1024 * 1024),
    )(*tied)
    for item, send in zip(sums, sends):
        item.send = send


def total(item):
    made = []
    for width, pieces in item.segments:
        value = pieces[0][0][0, pieces[0][1] : pieces[0][1] + width].astype(F32)
        for array, low in pieces[1:]:
            value = value + array[0, low : low + width].astype(F32)
        made.append(value)
    return made


def tie_sums(array, *sums):
    tied = tie(array, *[item.send for item in sums])
    for item, send in zip(sums, tied[1:]):
        item.send = send
    return tied[0]


def adam_update(weight, gradient, first, second, rate, decay):
    first_new = BETA_ONE * first + (1.0 - BETA_ONE) * gradient
    second_new = BETA_TWO * second + (1.0 - BETA_TWO) * gradient * gradient
    first_hat = first_new / (1.0 - BETA_ONE**STEP)
    second_hat = second_new / (1.0 - BETA_TWO**STEP)
    weight_new = weight - rate * (first_hat / (jnp.sqrt(second_hat) + EPS_ADAM) + decay * weight)
    return (weight_new, first_new, second_new, weight_new.astype(BF))


def small_block(vectors, hidden, place, count, width):
    groups = width // LANES
    per = count // groups
    at = place % per
    rows = 3 * 8
    lane = lax.broadcasted_iota(jnp.int32, (rows, LANES), 1) // vectors.shape[1]
    upright = jnp.pad(vectors.astype(BF), ((0, rows - vectors.shape[0]), (0, 0)))
    upright = jnp.where(lane == at, jnp.tile(upright, (1, per)), jnp.zeros((), BF))
    lane = lax.broadcasted_iota(jnp.int32, (2, width), 1) // hidden.shape[1]
    level = jnp.where(lane == at, jnp.tile(hidden.astype(BF), (1, per)), jnp.zeros((), BF))
    columns = [upright[low : low + 8] for low in (0, 8, 16)] + [level.reshape(8, LANES)]
    return jnp.pad(jnp.concatenate(columns, axis=1), ((0, BLOCK - 8), (0, 0)))


def small_share(total, vectors, hidden, place, count):
    width = total.shape[1]
    per = count // (width // LANES)
    at = place % per
    upright = jnp.concatenate([total[:8, low : low + LANES] for low in (0, LANES, 2 * LANES)], axis=0)
    rows, lanes = vectors.shape
    first = lax.dynamic_slice_in_dim(upright[:rows], at * lanes, lanes, axis=1)
    level = total[:8, 3 * LANES :].reshape(2, width)
    lanes = hidden.shape[1]
    return first, lax.dynamic_slice_in_dim(level, at * lanes, lanes, axis=1)


def gather_small(vectors, hidden):
    whole = lax.all_gather(vectors.astype(BF), AXES, axis=1, tiled=True)
    deep = lax.all_gather(hidden.astype(BF), AXES, axis=1, tiled=True)
    whole = jnp.pad(whole, ((0, HIDDEN_ROW - whole.shape[0]), (0, 0)))
    return jnp.concatenate([whole, deep.reshape(-1, whole.shape[1])], axis=0).astype(F32)


def scatter_small(grads, vectors, hidden, place, count):
    whole = lax.psum(small_rows(*grads), AXES)
    rows, lanes = vectors.shape
    first = lax.dynamic_slice_in_dim(whole[:rows], place * lanes, lanes, axis=1)
    layers, lanes = hidden.shape
    deep = whole[HIDDEN_ROW:].reshape(layers, -1)
    return first, lax.dynamic_slice_in_dim(deep, place * lanes, lanes, axis=1)


def gather_whole(attention, up, down):
    width = attention.shape[2]
    number = width // BLOCK
    square = lax.all_gather(attention, AXES, axis=1, tiled=True)
    square = square.reshape(-1, QUAD, number, BLOCK, width).transpose(0, 2, 1, 3, 4)
    tall = lax.all_gather(up, AXES, axis=1, tiled=True)
    tall = tall.reshape(2, number, BLOCK, QUAD, width).transpose(0, 1, 3, 2, 4)
    deep = lax.all_gather(down, AXES, axis=1, tiled=True).reshape(2, number, QUAD, BLOCK, width)
    half = number // 2
    quads = [square[0], tall[0], deep[0], square[1], square[2], tall[1], deep[1]]
    return [(quad[:half], quad[half:]) for quad in quads]


def scatter_whole(quads):
    joined = [jnp.concatenate(pair, axis=0).astype(F32) for pair in quads]
    number, _, _, width = joined[0].shape
    square = jnp.stack([joined[0], joined[3], joined[4]])
    square = square.transpose(0, 2, 1, 3, 4).reshape(3 * QUAD, width, width)
    tall = jnp.stack([joined[1], joined[5]]).transpose(0, 1, 3, 2, 4)
    tall = tall.reshape(2, width, QUAD * width)
    deep = jnp.stack([joined[2], joined[6]]).reshape(2, QUAD * width, width)
    return [
        lax.psum_scatter(part, AXES, scatter_dimension=1, tiled=True)
        for part in (square, tall, deep)
    ]


def direct_step(pairs, source, target, grad, attention, up, down, vectors, hidden, axis_sizes):
    net = Direct(axis_sizes)
    source_pair, target_pair, cross_pair = pairs
    width = source.shape[1]
    tall = up.reshape(2, BLOCK, QUAD, width).transpose(0, 2, 1, 3)
    deep = down.reshape(2, QUAD, BLOCK, width)
    a, b = net.table("a"), net.table("b")
    plain = jnp.arange(net.count, dtype=jnp.int32)
    cut = QUAD // 2

    later = jnp.concatenate([attention[2 * QUAD :], tall[1], deep[1]], axis=0)
    later = lax.all_gather(later, AXES, axis=0, tiled=False)
    small = small_block(vectors, hidden, net.place, net.count, width)
    first = jnp.concatenate([attention[:QUAD], small[None]], axis=0)[None]
    middle = QUAD + cut
    second = jnp.concatenate(
        [tall[0], attention[QUAD:middle], deep[0], attention[middle : 2 * QUAD]], axis=0
    )[None]
    first = net.grow(first, "a", 0)
    second, first = tie(second, first)
    second = net.grow(second, "a", 0)
    first = net.grow(first, "a", 1)
    second, first = tie(second, first)
    second = net.grow(second, "a", 1)
    query_key = net.grow(first[:, :cut], "a", 2)
    value_out = net.grow(first[:, cut:], "b", 2)
    second, query_key, value_out = tie(second, query_key, value_out)
    up_one = net.grow(second[:, :middle], "a", 2)
    down_one = net.grow(second[:, middle:], "b", 2)
    query_key = net.grow(query_key, "a", 3)
    value_out = net.grow(value_out, "b", 3)
    up_one, down_one, query_key, value_out = tie(up_one, down_one, query_key, value_out)
    query_key = net.finish(query_key, "a")
    value_out = net.finish(value_out, "b")
    enc_attend_w = [(a, query_key, 0, cut), (b, value_out, 0, cut)]
    source, up_one, down_one = tie(source, up_one, down_one)
    enc_kept = attend_forward(source_pair, None, 0, source, None, enc_attend_w, False)
    enc_mid, small = enc_kept[0], enc_kept[8]
    up_one = net.grow(up_one, "a", 3, enc_mid)
    down_one = net.grow(down_one, "b", 3, enc_mid)
    up_one = net.finish(up_one, "a")
    down_one = net.finish(down_one, "b")
    enc_feed_w = [(a, up_one, 0, QUAD), (b, down_one, 0, QUAD)]
    self_w = [(a, up_one, QUAD, cut), (b, down_one, QUAD, cut)]
    enc_feed_kept = feed_forward(small, 5, HIDDEN_ROW, enc_mid, enc_feed_w)
    memory = enc_feed_kept[0]
    self_kept = attend_forward(target_pair, small, 8, target, None, self_w, True)
    dec_one = self_kept[0]
    later, memory, dec_one = tie(later, memory, dec_one)
    cross_w, up_two, down_two = [(plain, [later], QUAD * slot, QUAD) for slot in range(3)]
    cross_kept = attend_forward(cross_pair, small, 13, dec_one, memory, [cross_w], False)
    dec_two = cross_kept[0]
    result, two_grad, dec_feed_small, feed_two = feed_both(
        (a, b), small, 18, HIDDEN_ROW + QUAD, dec_two, grad, [up_two, down_two]
    )

    names = ("a", "b")
    feed_two = sum_of(net, "a", *feed_two, (QUAD, QUAD)).step()
    one_grad, memory_grad, cross_small, cross_q = attend_backward(
        (b,), cross_pair, small, 13, two_grad, cross_kept, dec_one, memory, [cross_w], False, None
    )
    cross_s = sum_of(net, "b", *cross_q[0], (QUAD,))
    feed_two = feed_two.split(names)
    settle(feed_two, cross_small)
    memory_grad = tie_sums(memory_grad, *feed_two, cross_s)
    cross_s.step()
    feed_two = [item.step() for item in feed_two]
    mid_grad, enc_feed_small, feed_one = feed_backward(
        (a, b), small, 5, memory_grad, enc_feed_kept, enc_mid, enc_feed_w
    )
    feed_one = sum_of(net, "a", *feed_one, (QUAD, QUAD))
    settle(feed_two + [cross_s], enc_feed_small)
    one_grad = tie_sums(one_grad, *feed_two, cross_s, feed_one)
    feed_one.step()
    feed_two = [item.step() for item in feed_two]
    cross_s.step()
    target_grad, _, self_small, self_q = attend_backward(
        (a, b), target_pair, small, 8, one_grad, self_kept, target, None, self_w, True, None
    )
    self_s = [sum_of(net, name, *pair, (cut,)) for name, pair in zip(names, self_q)]
    feed_two = joined(feed_two)
    feed_one = feed_one.split(names)
    settle([feed_two, cross_s] + feed_one, self_small)
    mid_grad = tie_sums(mid_grad, feed_two, cross_s, *feed_one, *self_s)
    self_s = [item.step() for item in self_s]
    feed_two.step()
    cross_s.step()
    feed_one = [item.step() for item in feed_one]
    others = (enc_feed_small, self_small, cross_small, dec_feed_small)
    source_grad, _, _, enc_q = attend_backward(
        (a, b), source_pair, small, 0, mid_grad, enc_kept, source, None, enc_attend_w, False, others
    )
    enc_s = [
        sum_of(net, name, *pair, (pair[0].shape[1],)) for name, pair in zip(names, enc_q)
    ]
    settle(self_s + feed_one, source_grad)
    feed_one[0].send = tie_sums(feed_one[0].send, *self_s, *enc_s)
    enc_s = [item.step() for item in enc_s]
    self_s = [item.step() for item in self_s]
    feed_one = [item.step() for item in feed_one]
    settle(enc_s + [feed_two], *[item.send for item in self_s])
    enc_s = [item.step() for item in enc_s]
    feed_two.step()
    settle(enc_s + self_s)
    enc_s = [item.step() for item in enc_s]
    self_s = [item.step() for item in self_s]
    ending = joined(enc_s + self_s + feed_one + [cross_s])
    settle([ending])
    ending.step()
    settle([ending])
    ending.step()
    query_key, value_out, self_one, self_two, up_enc, down_enc, cross_g = total(ending)
    up_dec, down_dec = total(feed_two)
    square_g = jnp.concatenate([query_key, value_out[:cut], self_one, self_two, cross_g], axis=0)
    tall_g = jnp.stack([up_enc, up_dec]).transpose(0, 2, 1, 3).reshape(up.shape)
    deep_g = jnp.stack([down_enc, down_dec]).reshape(down.shape)
    vectors, hidden = tie(vectors, hidden, source_grad)[:2]
    small_g = small_share(value_out[cut], vectors, hidden, net.place, net.count)
    return (memory, result, source_grad, target_grad), (square_g, tall_g, deep_g) + small_g


def whole_step(pairs, source, target, grad, attention, up, down, vectors, hidden, axis_sizes):
    source_pair, target_pair, cross_pair = pairs
    small = gather_small(vectors, hidden)
    quads = gather_whole(attention, up, down)
    table = jnp.arange(source.shape[1] // BLOCK, dtype=jnp.int32)
    two = (table, table)
    parts = [(table, list(quad), 0, QUAD) for quad in quads]
    enc_kept = attend_forward(source_pair, small, 0, source, None, parts[:1], False)
    enc_mid = enc_kept[0]
    enc_feed_kept = feed_forward(small, 5, HIDDEN_ROW, enc_mid, parts[1:3])
    memory = enc_feed_kept[0]
    self_kept = attend_forward(target_pair, small, 8, target, None, parts[3:4], True)
    dec_one = self_kept[0]
    cross_kept = attend_forward(cross_pair, small, 13, dec_one, memory, parts[4:5], False)
    dec_two = cross_kept[0]
    result, two_grad, dec_feed_small, feed_two = feed_both(
        two, small, 18, HIDDEN_ROW + QUAD, dec_two, grad, parts[5:7]
    )
    one_grad, memory_grad, cross_small, cross_q = attend_backward(
        two[:1], cross_pair, small, 13, two_grad, cross_kept, dec_one, memory, parts[4:5], False, None
    )
    target_grad, _, self_small, self_q = attend_backward(
        two[:1], target_pair, small, 8, one_grad, self_kept, target, None, parts[3:4], True, None
    )
    mid_grad, enc_feed_small, feed_one = feed_backward(
        two, small, 5, memory_grad, enc_feed_kept, enc_mid, parts[1:3]
    )
    source_grad, _, enc_small, enc_q = attend_backward(
        two[:1], source_pair, small, 0, mid_grad, enc_kept, source, None, parts[:1], False, None
    )
    quads = [enc_q[0]]
    quads += [[half[:, low : low + QUAD] for half in feed_one] for low in (0, QUAD)]
    quads += [self_q[0], cross_q[0]]
    quads += [[half[:, low : low + QUAD] for half in feed_two] for low in (0, QUAD)]
    smalls = (enc_small, enc_feed_small, self_small, cross_small, dec_feed_small)
    count = axis_sizes[0] * axis_sizes[1]
    shares = scatter_small(smalls, vectors, hidden, lax.axis_index(AXES), count)
    return (memory, result, source_grad, target_grad), tuple(scatter_whole(quads)) + shares


def per_device(
    axis_sizes,
    source_tokens,
    target_tokens,
    source_segments,
    target_segments,
    output_grad,
    attention_weight,
    up_weight,
    down_weight,
    vectors,
    hidden_bias,
    *moments,
):
    masters = (attention_weight, up_weight, down_weight, vectors, hidden_bias)
    firsts = moments[:5]
    seconds = moments[5:]
    width = source_tokens.shape[2]
    pairs = (
        (source_segments, source_segments),
        (target_segments, target_segments),
        (target_segments, source_segments),
    )
    direct = axis_sizes[0] * axis_sizes[1] * BLOCK == width
    (memory, result, source_grad, target_grad), grads = (direct_step if direct else whole_step)(
        pairs,
        source_tokens[0],
        target_tokens[0],
        output_grad[0],
        attention_weight.astype(BF),
        up_weight.astype(BF),
        down_weight.astype(BF),
        vectors,
        hidden_bias,
        axis_sizes,
    )
    updated = [
        adam_update(
            masters[slot], grads[slot], firsts[slot], seconds[slot], RATES[slot], DECAYS[slot]
        )
        for slot in range(5)
    ]
    tokens = (memory[None], result[None], source_grad[None], target_grad[None])
    return tokens + tuple(updated[slot][kind] for kind in range(4) for slot in range(5))


def solution(mesh):
    rows = P(AXES, None, None)
    line = P(AXES, None)
    matrix = P(None, AXES, None)
    vector = P(None, AXES)
    state = (matrix, matrix, matrix, vector, vector)
    return jax.shard_map(
        functools.partial(per_device, (mesh.shape["dp"], mesh.shape["fsdp"])),
        mesh=mesh,
        in_specs=(rows, rows, line, line, rows) + state * 3,
        out_specs=(rows,) * 4 + state * 4,
        check_vma=False,
    )
```

```python
import functools

import jax
import jax.numpy as jnp
from jax import lax
from jax.experimental import pallas as pl
from jax.experimental.pallas import tpu as pltpu
from jax.sharding import PartitionSpec as P

HEADS = 8
STEP = 10
EPS_NORM = 1e-05
EPS_ADAM = 1e-08
BETA_ONE = 0.9
BETA_TWO = 0.999
LOWEST = -1e30
RATES = (0.05, 0.05, 0.05, 0.3, 0.3)
DECAYS = (0.01, 0.01, 0.01, 0.0, 0.0)
AXES = ("dp", "fsdp")
QUAD = 4
BLOCK = 16
LANES = 128
SMALL_ROWS = 32
HIDDEN_ROW = 24
BF = jnp.bfloat16
F32 = jnp.float32
VMEM = pl.BlockSpec(memory_space=pltpu.VMEM)
SMEM = pl.BlockSpec(memory_space=pltpu.SMEM)
ANY = pl.BlockSpec(memory_space=pl.ANY)
ROOT_TWO_PI = 0.7978845608028654
CUBIC = 0.044715


def dot(left, right):
    return jnp.dot(left, right, preferred_element_type=F32)


def dot_nt(left, right):
    return lax.dot_general(left, right, (((1,), (1,)), ((), ())), preferred_element_type=F32)


def load_start(part, place, sems):
    table, arrays, low, number = part
    at = 0
    for slot, array in enumerate(arrays):
        for index in range(array.shape[0]):
            source = array.at[index, low : low + number]
            pltpu.make_async_copy(source, place(table[at]), sems.at[slot]).start()
            at += 1


def load_wait(part, sems):
    table, arrays, low, number = part
    for slot, array in enumerate(arrays):
        whole = array.at[:, low : low + number]
        pltpu.make_async_copy(whole, whole, sems.at[slot]).wait()


def store_start(part, place, sems):
    table, arrays, low, number = part
    half = arrays[0].shape[0]
    for index in range(half):
        for slot in (1, 0):
            target = arrays[slot].at[index, low : low + number]
            source = place(table[slot * half + index])
            pltpu.make_async_copy(source, target, sems.at[slot]).start()


def row_place(scratch, low, high):
    def place(block):
        start = pl.multiple_of(block * BLOCK, BLOCK)
        return scratch.at[low:high, pl.ds(start, BLOCK), :]

    return place


def block_place(scratch):
    return lambda block: scratch.at[block]


def norm_forward(pre, gain, shift, out_ref, hat_ref, rstd_ref):
    mean = jnp.mean(pre, axis=-1, keepdims=True)
    centred = pre - mean
    spread = jnp.mean(centred * centred, axis=-1, keepdims=True)
    rstd = lax.rsqrt(spread + EPS_NORM)
    hat = centred * rstd
    hat_ref[...] = hat
    rstd_ref[...] = jnp.broadcast_to(rstd, rstd_ref.shape)
    out_ref[...] = hat * gain + shift


def norm_backward(grad, hat, rstd, gain):
    gain_grad = jnp.sum(grad * hat, axis=0, keepdims=True)
    shift_grad = jnp.sum(grad, axis=0, keepdims=True)
    scaled = grad * gain
    one = jnp.mean(scaled, axis=-1, keepdims=True)
    two = jnp.mean(scaled * hat, axis=-1, keepdims=True)
    return rstd * (scaled - one - hat * two), gain_grad, shift_grad


def lane_mask(rows):
    return lax.broadcasted_iota(jnp.int32, (rows, LANES), 1) < LANES // 2


def stacked_pair(block):
    first = lane_mask(block.shape[0])
    zero = jnp.zeros_like(block)
    return jnp.concatenate([jnp.where(first, block, zero), jnp.where(first, zero, block)], axis=0)


def merged_pair(stacked):
    rows = stacked.shape[0] // 2
    return jnp.where(lane_mask(rows), stacked[:rows], stacked[rows:])


def mask_fill(bias_ref, column_seg, row_seg, causal, transposed):
    length = bias_ref.shape[0]
    column = jnp.broadcast_to(column_seg, (LANES, length)).T
    for at in range(0, length, LANES):
        same = column == row_seg[:, at : at + LANES]
        if causal:
            down = lax.broadcasted_iota(jnp.int32, (length, LANES), 0)
            along = lax.broadcasted_iota(jnp.int32, (length, LANES), 1) + at
            order = (down <= along) if transposed else (along <= down)
            same = same & order
        bias_ref[:, at : at + LANES] = jnp.where(same, 0.0, LOWEST)


def take_parts(refs, layout, tables):
    parts = []
    for slot, (arrays, low, number) in enumerate(layout):
        parts.append((tables[slot], [refs.pop(0) for _ in range(arrays)], low, number))
    return parts


def small_part(part):
    table, arrays, low, number = part
    return table, arrays, low + number, 1


def small_join(blocks_ref):
    count = blocks_ref.shape[0]
    groups = blocks_ref.shape[3] // LANES
    per = count // groups
    vectors = []
    hidden = [[], []]
    for group in range(groups):
        total = blocks_ref[group * per, 0, :8].astype(F32)
        for at in range(group * per + 1, (group + 1) * per):
            total = total + blocks_ref[at, 0, :8].astype(F32)
        columns = [total[:, at : at + LANES] for at in range(0, 4 * LANES, LANES)]
        vectors.append(jnp.concatenate(columns[:3], axis=0))
        for layer in range(2):
            rows = [columns[3][4 * layer + at : 4 * layer + at + 1] for at in range(4)]
            hidden[layer].append(jnp.concatenate(rows, axis=1))
    return jnp.concatenate([jnp.concatenate(vectors, axis=1)] + hidden[0] + hidden[1], axis=0)


def small_split(whole, group):
    lanes = slice(group * LANES, (group + 1) * LANES)
    columns = [whole[at : at + 8, lanes] for at in (0, 8, 16)]
    rows = []
    for layer in range(2):
        row = whole[24 + 4 * layer + group : 25 + 4 * layer + group]
        rows += [row[:, at : at + LANES] for at in range(0, 4 * LANES, LANES)]
    columns.append(jnp.concatenate(rows, axis=0))
    block = jnp.concatenate(columns, axis=1)
    return jnp.concatenate([block, jnp.zeros_like(block)], axis=0).astype(BF)


def attend_forward_kernel(layout, cross, causal, base, joins, *refs):
    refs = list(refs)
    tables = [refs.pop(0) for _ in layout]
    query_seg = refs.pop(0)
    key_seg = refs.pop(0)
    small = None if joins else refs.pop(0)
    rows_ref = refs.pop(0)
    memory_ref = refs.pop(0) if cross else None
    parts = take_parts(refs, layout, tables)
    out_ref, hat_ref, rstd_ref, q_ref, k_ref, v_ref, o_ref, lse_ref = [refs.pop(0) for _ in range(8)]
    if joins:
        small = refs.pop(0)
        blocks_ref = refs.pop()
        extra = small_part(parts[-1])
    w_ref, bias_ref, sems = refs
    first = 0
    if joins:
        load_start(extra, lambda block: blocks_ref.at[block], sems.at[len(parts)])
    for slot, part in enumerate(parts):
        load_start(part, row_place(w_ref, first, first + part[3]), sems.at[slot])
        first += part[3]
    length, width = rows_ref.shape
    mask_fill(bias_ref, query_seg[...], key_seg[...], causal, False)
    rows = rows_ref[...].astype(BF)
    keys = memory_ref[...].astype(BF) if cross else rows
    if joins:
        load_wait(extra, sems.at[len(parts)])
        small[...] = small_join(blocks_ref)
    for slot, part in enumerate(parts):
        load_wait(part, sems.at[slot])
    scale = (width // HEADS) ** (-0.5)
    q_ref[...] = (dot(rows, w_ref[0]) + small[base : base + 1]).astype(BF) * jnp.asarray(scale, BF)
    k_ref[...] = dot(keys, w_ref[1]).astype(BF)
    v_ref[...] = (dot(keys, w_ref[2]) + small[base + 1 : base + 2]).astype(BF)
    lane = lax.broadcasted_iota(jnp.int32, (LANES, LANES), 1)
    for at in range(0, length, LANES):
        reach = at + LANES if causal else length
        logs = jnp.zeros((LANES, LANES), F32)
        for pair in range(HEADS // 2):
            lanes = slice(pair * LANES, (pair + 1) * LANES)
            stacked = stacked_pair(q_ref[at : at + LANES, lanes])
            scores = dot_nt(stacked, k_ref[:reach, lanes])
            bias = bias_ref[at : at + LANES, :reach]
            scores = scores + jnp.concatenate([bias, bias], axis=0)
            largest = jnp.max(scores, axis=-1, keepdims=True)
            exponent = jnp.exp(scores - largest).astype(BF)
            values = jnp.concatenate([v_ref[:reach, lanes], jnp.ones((reach, LANES), BF)], axis=1)
            mixed = dot(exponent, values)
            total = mixed[:, LANES:]
            o_ref[at : at + LANES, lanes] = merged_pair(mixed[:, :LANES] / total).astype(BF)
            log_total = largest + jnp.log(total)
            logs = jnp.where(lane == 2 * pair, log_total[:LANES], logs)
            logs = jnp.where(lane == 2 * pair + 1, log_total[LANES:], logs)
        lse_ref[:, at : at + LANES] = logs.T[:HEADS]
    attended = dot(o_ref[...], w_ref[3]) + small[base + 2 : base + 3]
    pre = rows_ref[...].astype(F32) + attended
    norm_forward(pre, small[base + 3 : base + 4], small[base + 4 : base + 5], out_ref, hat_ref, rstd_ref)


def attend_backward_kernel(layout, cross, causal, base, splits, *refs):
    refs = list(refs)
    tables = [refs.pop(0) for _ in layout]
    out_tables = [refs.pop(0) for _ in layout]
    query_seg = refs.pop(0)
    key_seg = refs.pop(0)
    small = refs.pop(0)
    grad_ref = refs.pop(0)
    hat_ref, rstd_ref = refs.pop(0), refs.pop(0)
    rows_ref = refs.pop(0)
    memory_ref = refs.pop(0) if cross else None
    q_ref, k_ref, v_ref, o_ref, lse_ref = [refs.pop(0) for _ in range(5)]
    others = [refs.pop(0) for _ in range(4)] if splits else None
    parts = take_parts(refs, layout, tables)
    rows_out = refs.pop(0)
    memory_out = refs.pop(0) if cross else None
    small_out = None if splits else refs.pop(0)
    targets = [refs.pop(0), refs.pop(0)]
    outs = []
    for table, (_, _, number) in zip(out_tables, layout):
        outs.append((table, targets, sum(part[3] for part in outs), number))
    blocks_ref = refs.pop() if splits else None
    w_ref, dw_ref, bias_ref, dout_ref, dq_t_ref, dk_ref, dv_ref, kt_ref, sems = refs
    first = 0
    for slot, part in enumerate(parts):
        load_start(part, row_place(w_ref, first, first + part[3]), sems.at[slot])
        first += part[3]
    length, width = rows_ref.shape
    head = width // HEADS
    scale = head ** (-0.5)
    mask_fill(bias_ref, key_seg[...], query_seg[...], causal, True)
    kt_ref[...] = k_ref[...].T
    pre_grad, gain_grad, shift_grad = norm_backward(
        grad_ref[...], hat_ref[...], rstd_ref[:, :1], small[base + 3 : base + 4]
    )
    rows_out[...] = pre_grad
    low = pre_grad.astype(BF)
    for slot, part in enumerate(parts):
        load_wait(part, sems.at[slot])
    dout_ref[...] = dot_nt(low, w_ref[3]).astype(BF)
    dw_ref[3] = dot(o_ref[...].T, low).astype(BF)
    out_bias = jnp.sum(low.astype(F32), axis=0, keepdims=True)
    product = dout_ref[...].astype(F32) * o_ref[...].astype(F32)
    high = product.astype(BF)
    rest = (product - high.astype(F32)).astype(BF)
    picker = lax.broadcasted_iota(jnp.int32, (BLOCK, width), 1) // head
    picker = (picker == lax.broadcasted_iota(jnp.int32, (BLOCK, width), 0)).astype(BF)
    row_dots = dot_nt(picker, high) + dot_nt(picker, rest)
    for pair in range(HEADS // 2):
        lanes = slice(pair * LANES, (pair + 1) * LANES)
        for at in range(0, length, LANES):
            begin = at if causal else 0
            query = q_ref[begin:, lanes]
            dout = dout_ref[begin:, lanes]
            scores = dot_nt(stacked_pair(k_ref[at : at + LANES, lanes]), query)
            prob_grad = dot_nt(stacked_pair(v_ref[at : at + LANES, lanes]), dout)
            bias = bias_ref[at : at + LANES, begin:]
            probs = []
            score_grads = []
            for part in range(2):
                which = 2 * pair + part
                half = slice(part * LANES, (part + 1) * LANES)
                prob = jnp.exp(scores[half] + (bias - lse_ref[which : which + 1, begin:]))
                probs.append(prob.astype(BF))
                row_dot = row_dots[which : which + 1, begin:]
                score_grads.append((prob * (prob_grad[half] - row_dot)).astype(BF))
                at_t = pair * LANES + part * head
                back = dot(kt_ref[at_t : at_t + head, at : at + LANES], score_grads[part])
                if at == 0:
                    dq_t_ref[at_t : at_t + head, :] = back
                else:
                    dq_t_ref[at_t : at_t + head, begin:] += back
            value_back = dot(jnp.concatenate(probs, axis=0), dout)
            dv_ref[at : at + LANES, lanes] = merged_pair(value_back).astype(BF)
            key_back = dot(jnp.concatenate(score_grads, axis=0), query)
            dk_ref[at : at + LANES, lanes] = merged_pair(key_back).astype(BF)
    query_grad = (dq_t_ref[...] * scale).T.astype(BF)
    key_grad = dk_ref[...]
    value_grad = dv_ref[...]
    turned = rows_ref[...].astype(BF).T
    dw_ref[0] = dot(turned, query_grad).astype(BF)
    if cross:
        turned = memory_ref[...].astype(BF).T
    dw_ref[1] = dot(turned, key_grad).astype(BF)
    dw_ref[2] = dot(turned, value_grad).astype(BF)
    first = 0
    for slot, part in enumerate(outs):
        store_start(part, row_place(dw_ref, first, first + part[3]), sems.at[slot])
        first += part[3]
    rows_back = rows_out[...] + dot_nt(query_grad, w_ref[0])
    memory_back = dot_nt(key_grad, w_ref[1]) + dot_nt(value_grad, w_ref[2])
    if cross:
        rows_out[...] = rows_back
        memory_out[...] = memory_back
    else:
        rows_out[...] = rows_back + memory_back
    query_bias = jnp.sum(query_grad.astype(F32), axis=0, keepdims=True)
    value_bias = jnp.sum(value_grad.astype(F32), axis=0, keepdims=True)
    spare = jnp.zeros((3, width), F32)
    own = jnp.concatenate(
        [query_bias, value_bias, out_bias, gain_grad, shift_grad, spare], axis=0
    )
    if splits:
        enc_feed, self_attend, cross_attend, dec_feed = [other[...] for other in others]
        whole = small_rows(own, enc_feed, self_attend, cross_attend, dec_feed)
        groups = blocks_ref.shape[0]
        for group in range(groups):
            blocks_ref[group, 0] = small_split(whole, group)
        extra = small_part(outs[-1])
        per = 2 * extra[1][0].shape[0] // groups
        store_start(extra, lambda block: blocks_ref.at[block // per], sems.at[len(parts)])
        load_wait(extra, sems.at[len(parts)])
    else:
        small_out[...] = own
    for slot, part in enumerate(outs):
        load_wait(part, sems.at[slot])


def small_rows(enc_attend, enc_feed, self_attend, cross_attend, dec_feed):
    return jnp.concatenate(
        [
            enc_attend[:5],
            enc_feed[:3],
            self_attend[:5],
            cross_attend[:5],
            dec_feed[:3],
            dec_feed[7:],
            dec_feed[7:],
            dec_feed[7:],
            enc_feed[3:7],
            dec_feed[3:7],
        ],
        axis=0,
    )


def gelu_parts(pre):
    inner = ROOT_TWO_PI * (pre + CUBIC * pre * pre * pre)
    curve = jnp.tanh(inner)
    return curve, 0.5 * pre * (1.0 + curve)


def gelu_slope(pre, curve):
    bend = ROOT_TWO_PI * (1.0 + 3.0 * CUBIC * pre * pre)
    return 0.5 * (1.0 + curve) + 0.5 * pre * (1.0 - curve * curve) * bend


def chunk_of(ref, index):
    number = ref.shape[0] // QUAD
    part = ref[index * number : (index + 1) * number]
    return part.reshape(number * ref.shape[1] * ref.shape[2], ref.shape[3])


def feed_forward_steps(small, base, hidden_at, rows_ref, up_ref, down_ref, pre_ref):
    rows = rows_ref[...].astype(BF)
    total = rows_ref[...] + small[base : base + 1]
    for index in range(QUAD):
        at = hidden_at + index
        pre = dot(rows, up_ref[index]) + small[at : at + 1]
        pre_ref[index] = pre
        active = gelu_parts(pre)[1].astype(BF)
        total = total + dot(active, chunk_of(down_ref, index))
    return total


def feed_backward_steps(pre_grad, rows_ref, up_ref, down_ref, pre_ref, dup_ref, ddown_ref, rows_out):
    low = pre_grad.astype(BF)
    turned = rows_ref[...].astype(BF).T
    total = pre_grad
    hidden_grads = []
    number = ddown_ref.shape[0] // QUAD
    for index in range(QUAD):
        pre = pre_ref[index]
        curve, active = gelu_parts(pre)
        down_grad = dot(active.astype(BF).T, low).astype(BF)
        ddown_ref[index * number : (index + 1) * number] = down_grad.reshape(
            (number,) + ddown_ref.shape[1:]
        )
        back = dot_nt(low, chunk_of(down_ref, index))
        hidden = (back * gelu_slope(pre, curve)).astype(BF)
        hidden_grads.append(jnp.sum(hidden.astype(F32), axis=0, keepdims=True))
        dup_ref[index] = dot(turned, hidden).astype(BF)
        total = total + dot_nt(hidden, up_ref[index])
    rows_out[...] = total
    out_bias = jnp.sum(low.astype(F32), axis=0, keepdims=True)
    return out_bias, hidden_grads


def load_feed(parts, up_ref, down_ref, sems):
    load_start(parts[0], row_place(up_ref, 0, QUAD), sems.at[0])
    load_start(parts[1], block_place(down_ref), sems.at[1])


def store_feed(outs, dup_ref, ddown_ref, sems):
    store_start(outs[1], block_place(ddown_ref), sems.at[1])
    store_start(outs[0], row_place(dup_ref, 0, QUAD), sems.at[0])


def wait_feed(parts, sems):
    for slot, part in enumerate(parts):
        load_wait(part, sems.at[slot])


def feed_outs(refs, tables):
    arrays = [refs.pop(0), refs.pop(0)]
    return [(tables[slot], arrays, slot * QUAD, QUAD) for slot in range(2)]


def feed_small(out_bias, gain_grad, shift_grad, hidden_grads):
    spare = jnp.zeros_like(out_bias)
    return jnp.concatenate([out_bias, gain_grad, shift_grad] + hidden_grads + [spare], axis=0)


def feed_forward_kernel(layout, base, hidden_at, *refs):
    refs = list(refs)
    tables = [refs.pop(0), refs.pop(0)]
    small, rows_ref = refs.pop(0), refs.pop(0)
    parts = take_parts(refs, layout, tables)
    out_ref, hat_ref, rstd_ref, pre_ref, up_ref, down_ref, sems = refs
    load_feed(parts, up_ref, down_ref, sems)
    wait_feed(parts, sems)
    pre = feed_forward_steps(small, base, hidden_at, rows_ref, up_ref, down_ref, pre_ref)
    norm_forward(pre, small[base + 1 : base + 2], small[base + 2 : base + 3], out_ref, hat_ref, rstd_ref)


def feed_backward_kernel(layout, base, *refs):
    refs = list(refs)
    tables = [refs.pop(0), refs.pop(0)]
    out_tables = [refs.pop(0), refs.pop(0)]
    small, grad_ref, hat_ref, rstd_ref, rows_ref, pre_ref = [refs.pop(0) for _ in range(6)]
    parts = take_parts(refs, layout, tables)
    rows_out, small_out = refs.pop(0), refs.pop(0)
    outs = feed_outs(refs, out_tables)
    up_ref, down_ref, dup_ref, ddown_ref, sems, out_sems = refs
    load_feed(parts, up_ref, down_ref, sems)
    pre_grad, gain_grad, shift_grad = norm_backward(
        grad_ref[...], hat_ref[...], rstd_ref[:, :1], small[base + 1 : base + 2]
    )
    wait_feed(parts, sems)
    out_bias, hidden_grads = feed_backward_steps(
        pre_grad, rows_ref, up_ref, down_ref, pre_ref, dup_ref, ddown_ref, rows_out
    )
    store_feed(outs, dup_ref, ddown_ref, out_sems)
    small_out[...] = feed_small(out_bias, gain_grad, shift_grad, hidden_grads)
    wait_feed(outs, out_sems)


def feed_both_kernel(layout, base, hidden_at, *refs):
    refs = list(refs)
    tables = [refs.pop(0), refs.pop(0)]
    out_tables = [refs.pop(0), refs.pop(0)]
    small, rows_ref, grad_ref = [refs.pop(0) for _ in range(3)]
    parts = take_parts(refs, layout, tables)
    out_ref, rows_out, small_out = [refs.pop(0) for _ in range(3)]
    outs = feed_outs(refs, out_tables)
    up_ref, down_ref, dup_ref, ddown_ref, pre_ref, hat_ref, rstd_ref, sems, out_sems = refs
    load_feed(parts, up_ref, down_ref, sems)
    wait_feed(parts, sems)
    pre = feed_forward_steps(small, base, hidden_at, rows_ref, up_ref, down_ref, pre_ref)
    gain = small[base + 1 : base + 2]
    norm_forward(pre, gain, small[base + 2 : base + 3], out_ref, hat_ref, rstd_ref)
    pre_grad, gain_grad, shift_grad = norm_backward(
        grad_ref[...].astype(F32), hat_ref[...], rstd_ref[:, :1], gain
    )
    out_bias, hidden_grads = feed_backward_steps(
        pre_grad, rows_ref, up_ref, down_ref, pre_ref, dup_ref, ddown_ref, rows_out
    )
    store_feed(outs, dup_ref, ddown_ref, out_sems)
    small_out[...] = feed_small(out_bias, gain_grad, shift_grad, hidden_grads)
    wait_feed(outs, out_sems)


def shaped(shape, dtype=F32):
    return jax.ShapeDtypeStruct(shape, dtype)


def call(kernel, ins, specs, outs, out_specs, scratch, flops, moved):
    return pl.pallas_call(
        kernel,
        out_shape=outs,
        in_specs=specs,
        out_specs=out_specs,
        scratch_shapes=scratch,
        cost_estimate=pl.CostEstimate(flops=flops, bytes_accessed=moved, transcendentals=0),
        compiler_params=pltpu.CompilerParams(vmem_limit_bytes=40 * 1024 * 1024),
    )(*ins)


def layout_of(parts):
    return [(len(arrays), low, number) for _, arrays, low, number in parts]


def arrays_of(parts):
    return [array for part in parts for array in part[1]]


def most(parts):
    return max(len(part[1]) for part in parts)


def halves(width, number):
    return [shaped((width // BLOCK // 2, number, BLOCK, width), BF)] * 2


def attend_forward(segments, small, base, rows, memory, parts, causal):
    length, width = rows.shape
    cross = memory is not None
    joins = small is None
    ins = [part[0] for part in parts] + list(segments) + ([] if joins else [small]) + [rows]
    ins += [memory] if cross else []
    specs = [SMEM] * len(parts) + [VMEM] * (len(ins) - len(parts))
    arrays = arrays_of(parts)
    ins += arrays
    specs += [ANY] * len(arrays)
    outs = [shaped((length, width)), shaped((length, width)), shaped((length, LANES))]
    outs += [shaped((length, width), BF)] * 4 + [shaped((HEADS, length))]
    outs += [shaped((SMALL_ROWS, width))] if joins else []
    scratch = [
        pltpu.VMEM((QUAD, width, width), BF),
        pltpu.VMEM((length, length), F32),
        pltpu.SemaphoreType.DMA((len(parts) + 1, most(parts))),
    ]
    scratch += [pltpu.VMEM((width // BLOCK, 1, BLOCK, width), BF)] if joins else []
    kernel = functools.partial(attend_forward_kernel, layout_of(parts), cross, causal, base, joins)
    flops = 8 * length * width * width + 16 * length * length * width
    return call(kernel, ins, specs, outs, [VMEM] * len(outs), scratch, flops, 8_000_000)


def attend_backward(
    out_tables, segments, small, base, grad, kept, rows, memory, parts, causal, others
):
    length, width = rows.shape
    cross = memory is not None
    splits = others is not None
    hat, rstd, q, k, v, o, lse = kept[1:8]
    ins = [part[0] for part in parts] + list(out_tables)
    specs = [SMEM] * len(ins)
    ins += list(segments) + [small, grad, hat, rstd, rows]
    ins += ([memory] if cross else []) + [q, k, v, o, lse] + list(others or ())
    specs += [VMEM] * (len(ins) - len(specs))
    arrays = arrays_of(parts)
    ins += arrays
    specs += [ANY] * len(arrays)
    outs = [shaped((length, width))] * (2 if cross else 1)
    outs += [] if splits else [shaped((8, width))]
    out_specs = [VMEM] * len(outs) + [ANY] * 2
    outs += halves(width, QUAD + (1 if splits else 0))
    scratch = [
        pltpu.VMEM((QUAD, width, width), BF),
        pltpu.VMEM((QUAD, width, width), BF),
        pltpu.VMEM((length, length), F32),
        pltpu.VMEM((length, width), BF),
        pltpu.VMEM((width, length), F32),
        pltpu.VMEM((length, width), BF),
        pltpu.VMEM((length, width), BF),
        pltpu.VMEM((width, length), BF),
        pltpu.SemaphoreType.DMA((len(parts) + 1, 2)),
    ]
    scratch += [pltpu.VMEM((width // LANES, 1, BLOCK, width), BF)] if splits else []
    kernel = functools.partial(
        attend_backward_kernel, layout_of(parts), cross, causal, base, splits
    )
    flops = 16 * length * width * width + 40 * length * length * width
    results = list(call(kernel, ins, specs, outs, out_specs, scratch, flops, 12_000_000))
    rows_grad = results.pop(0)
    memory_grad = results.pop(0) if cross else None
    small_grad = None if splits else results.pop(0)
    return rows_grad, memory_grad, small_grad, results


def feed_scratch(width, grads):
    number = width // BLOCK
    once = [pltpu.VMEM((QUAD, width, width), BF), pltpu.VMEM((number, QUAD, BLOCK, width), BF)]
    return once * (2 if grads else 1)


def feed_forward(small, base, hidden_at, rows, parts):
    length, width = rows.shape
    arrays = arrays_of(parts)
    ins = [part[0] for part in parts] + [small, rows] + arrays
    specs = [SMEM] * 2 + [VMEM] * 2 + [ANY] * len(arrays)
    outs = [shaped((length, width)), shaped((length, width)), shaped((length, LANES))]
    outs += [shaped((QUAD, length, width))]
    scratch = feed_scratch(width, False) + [pltpu.SemaphoreType.DMA((2, most(parts)))]
    kernel = functools.partial(feed_forward_kernel, layout_of(parts), base, hidden_at)
    flops = 16 * length * width * width
    return call(kernel, ins, specs, outs, [VMEM] * len(outs), scratch, flops, 10_000_000)


def feed_backward(out_tables, small, base, grad, kept, rows, parts):
    length, width = rows.shape
    _, hat, rstd, pre = kept
    arrays = arrays_of(parts)
    ins = [part[0] for part in parts] + list(out_tables) + [small, grad, hat, rstd, rows, pre]
    ins += arrays
    specs = [SMEM] * 4 + [VMEM] * 6 + [ANY] * len(arrays)
    outs = [shaped((length, width)), shaped((8, width))] + halves(width, 2 * QUAD)
    out_specs = [VMEM] * 2 + [ANY] * 2
    scratch = feed_scratch(width, True)
    scratch += [pltpu.SemaphoreType.DMA((2, most(parts))), pltpu.SemaphoreType.DMA((2, 2))]
    kernel = functools.partial(feed_backward_kernel, layout_of(parts), base)
    flops = 32 * length * width * width
    results = call(kernel, ins, specs, outs, out_specs, scratch, flops, 14_000_000)
    return results[0], results[1], results[2:4]


def feed_both(out_tables, small, base, hidden_at, rows, grad, parts):
    length, width = rows.shape
    arrays = arrays_of(parts)
    ins = [part[0] for part in parts] + list(out_tables) + [small, rows, grad] + arrays
    specs = [SMEM] * 4 + [VMEM] * 3 + [ANY] * len(arrays)
    outs = [shaped((length, width)), shaped((length, width)), shaped((8, width))]
    outs += halves(width, 2 * QUAD)
    out_specs = [VMEM] * 3 + [ANY] * 2
    scratch = feed_scratch(width, True) + [
        pltpu.VMEM((QUAD, length, width), F32),
        pltpu.VMEM((length, width), F32),
        pltpu.VMEM((length, LANES), F32),
        pltpu.SemaphoreType.DMA((2, most(parts))),
        pltpu.SemaphoreType.DMA((2, 2)),
    ]
    kernel = functools.partial(feed_both_kernel, layout_of(parts), base, hidden_at)
    flops = 48 * length * width * width
    results = call(kernel, ins, specs, outs, out_specs, scratch, flops, 12_000_000)
    return results[0], results[1], results[2], results[3:5]


def first_kernel(at_ref, square_ref, tall_ref, deep_ref, vector_ref, hidden_ref, own_ref, later_ref, turn_ref, line_ref):
    at = at_ref[0]
    width = square_ref.shape[2]
    cut = QUAD // 2
    turn_ref[...] = jnp.zeros_like(turn_ref)
    lanes, rows = vector_ref.shape
    turn_ref[pl.ds(pl.multiple_of(at * lanes, lanes), lanes), :rows] = vector_ref[...]
    upright = turn_ref[...].T
    line_ref[...] = jnp.zeros_like(line_ref)
    layers, lanes = hidden_ref.shape
    per = LANES // lanes
    for layer in range(layers):
        row = jnp.concatenate([hidden_ref[layer : layer + 1]] * per, axis=1)
        lane = lax.broadcasted_iota(jnp.int32, row.shape, 1) // lanes
        row = jnp.where(lane == at % per, row, 0.0)
        line_ref[pl.ds(4 * layer + at // per, 1), :] = row
    columns = [upright[low : low + 8] for low in (0, 8, 16)] + [line_ref[...]]
    block = jnp.concatenate(columns, axis=1)
    small = jnp.concatenate([block, jnp.zeros_like(block)], axis=0)
    first = list(range(cut)) + list(range(QUAD, QUAD + cut))
    second = list(range(cut, QUAD)) + [None] + list(range(QUAD + cut, 2 * QUAD))
    for slot, index in enumerate(first + second):
        own_ref[0, slot] = (small if index is None else square_ref[index]).astype(BF)
    for index in range(QUAD):
        later_ref[index] = square_ref[2 * QUAD + index].astype(BF)
    for layer in range(2):
        for index in range(QUAD):
            lanes = slice(index * width, (index + 1) * width)
            later_ref[(2 * layer + 1) * QUAD + index] = tall_ref[layer, :, lanes].astype(BF)
            rows = slice(index * BLOCK, (index + 1) * BLOCK)
            later_ref[(2 * layer + 2) * QUAD + index] = deep_ref[layer, rows].astype(BF)


def first_arrays(at, square, tall, deep, vectors, hidden):
    width = square.shape[2]
    return pl.pallas_call(
        first_kernel,
        out_shape=[
            shaped((1, 2 * QUAD + 1, BLOCK, width), BF),
            shaped((5 * QUAD, BLOCK, width), BF),
        ],
        in_specs=[SMEM] + [VMEM] * 5,
        out_specs=[VMEM] * 2,
        scratch_shapes=[pltpu.VMEM((LANES, LANES), F32), pltpu.VMEM((8, LANES), F32)],
    )(at, square, tall, deep, vectors.T, hidden)


def last_kernel(plan, count, at_ref, *refs):
    arrays, refs = refs[:count], refs[count:]
    masters, firsts, seconds = refs[:5], refs[5:10], refs[10:15]
    outs, refs = [refs[15 + 5 * kind : 20 + 5 * kind] for kind in range(4)], refs[35:]
    buffers, turn_ref, line_ref, sems = refs
    at = at_ref[0]
    starts = []
    for width, pieces, _ in plan:
        for index, low in pieces:
            source = arrays[index].at[0, low : low + width]
            copy = pltpu.make_async_copy(source, buffers.at[len(starts), :width], sems.at[len(starts)])
            copy.start()
            starts.append(copy)

    def update(slot, where, gradient):
        results = adam_update(
            masters[slot][where],
            gradient,
            firsts[slot][where],
            seconds[slot][where],
            RATES[slot],
            DECAYS[slot],
        )
        for kind in range(4):
            outs[kind][slot][where] = results[kind]

    begin = 0
    for width, pieces, targets in plan:
        for index in range(len(pieces)):
            starts[begin + index].wait()
        for sub, (slot, where) in enumerate(targets):
            gradient = buffers[begin, sub].astype(F32)
            for index in range(1, len(pieces)):
                gradient = gradient + buffers[begin + index, sub].astype(F32)
            if slot < 3:
                update(slot, where, gradient)
                continue
            turn_ref[...] = jnp.zeros_like(turn_ref)
            for column in range(3):
                lanes = slice(column * LANES, (column + 1) * LANES)
                turn_ref[8 * column : 8 * column + 8, :] = gradient[:8, lanes]
            turn_ref[...] = turn_ref[...].T
            lanes, rows = masters[3].shape
            share = turn_ref[pl.ds(pl.multiple_of(at * lanes, lanes), lanes), :][:, :rows]
            update(3, slice(None), share)
            line_ref[...] = gradient[:8, 3 * LANES :]
            layers, lanes = masters[4].shape
            per = LANES // lanes
            for layer in range(layers):
                row = line_ref[pl.ds(4 * layer + at // per, 1), :]
                share = row[:, :lanes]
                for part in range(1, per):
                    other = row[:, part * lanes : (part + 1) * lanes]
                    share = jnp.where(at % per == part, other, share)
                update(4, slice(layer, layer + 1), share)
        begin += len(pieces)


def last_update(at, segments, masters, firsts, seconds):
    arrays = []
    plan = []
    for width, pieces, targets in segments:
        entry = []
        for array, low in pieces:
            found = [place for place, other in enumerate(arrays) if other is array]
            if not found:
                arrays.append(array)
            entry.append((found[0] if found else len(arrays) - 1, low))
        plan.append((width, entry, targets))
    params = [list(group) for group in (masters, firsts, seconds)]
    for group in params:
        group[3] = group[3].T
    flat = params[0] + params[1] + params[2]
    outs = [shaped(array.shape) for array in params[0]] * 3
    outs += [shaped(array.shape, BF) for array in params[0]]
    pieces = sum(len(entry[1]) for entry in plan)
    block = arrays[0].shape[2:]
    results = pl.pallas_call(
        functools.partial(last_kernel, plan, len(arrays)),
        out_shape=outs,
        in_specs=[SMEM] + [ANY] * len(arrays) + [VMEM] * len(flat),
        out_specs=[VMEM] * len(outs),
        scratch_shapes=[
            pltpu.VMEM((pieces, max(entry[0] for entry in plan)) + block, BF),
            pltpu.VMEM((LANES, LANES), F32),
            pltpu.VMEM((8, LANES), F32),
            pltpu.SemaphoreType.DMA((pieces,)),
        ],
        compiler_params=pltpu.CompilerParams(vmem_limit_bytes=40 * 1024 * 1024),
    )(at, *arrays, *flat)
    results = list(results)
    for kind in range(4):
        results[5 * kind + 3] = results[5 * kind + 3].T
    return results


def tie(*arrays):
    return lax.optimization_barrier(arrays)


class Direct:
    def __init__(self, axis_sizes):
        outer, inner = axis_sizes
        self.count = outer * inner
        inner_bits = inner.bit_length() - 1
        bits = self.count.bit_length() - 1
        core = [inner_bits]
        across = list(range(inner_bits + 1, bits))
        up = [0]
        along = list(range(1, inner_bits))
        self.orders = {
            "a": core + across + up + along,
            "b": core + up + across + along,
        }
        self.place = lax.axis_index(AXES)

    def hop(self, array, bit):
        return lax.ppermute(array, AXES, [(at, at ^ (1 << bit)) for at in range(self.count)])

    def table(self, name):
        order = self.orders[name]
        index = jnp.arange(self.count, dtype=jnp.int32)
        block = jnp.zeros_like(index)
        for at, bit in enumerate(order):
            block = block | (((index >> (len(order) - 1 - at)) & 1) << bit)
        return block ^ self.place

    def grow(self, arrays, names, step):
        arrived = []
        for array, name in zip(arrays, names):
            arrived.append(self.hop(array, self.orders[name][::-1][step]))
        pairs = zip(arrays, tie(*arrived))
        return [jnp.concatenate(pair, axis=0) for pair in pairs]

    def finish(self, array, name):
        return [array, self.hop(array, self.orders[name][0])]


class Sum:
    def __init__(self, net, name, segments, send, done):
        self.net = net
        self.name = name
        self.segments = segments
        self.send = send
        self.done = done

    def step(self):
        arrived = self.net.hop(self.send, self.net.orders[self.name][self.done])
        self.done += 1
        low = 0
        made = []
        for width, pieces in self.segments:
            made.append((width, pieces + [(arrived, low)]))
            low += width
        self.segments = made
        return self

    def last(self):
        return [self.segments[0][1][-1][0]]

    def number(self):
        return self.segments[0][1][-1][0].shape[0]

    def split(self, names):
        return [
            Sum(self.net, name, [segment], None, self.done)
            for name, segment in zip(names, self.segments)
        ]


def step_all(sums):
    for item in sums:
        item.step()


def sum_of(net, name, keep, send, widths):
    low = 0
    segments = []
    for width in widths:
        segments.append((width, [(keep, low)]))
        low += width
    return Sum(net, name, segments, send, 0)


def joined(sums):
    segments = [segment for item in sums for segment in item.segments]
    return Sum(sums[0].net, sums[0].name, segments, None, sums[0].done)


def combine_kernel(plan, count, *refs):
    arrays, outs, buffers, sems = refs[:count], refs[count:-2], refs[-2], refs[-1]
    at = 0
    starts = []
    for _, number, _, width, pieces in plan:
        for index, low in pieces:
            source = arrays[index].at[number : 2 * number, low : low + width]
            target = buffers.at[at, :number, :width]
            copy = pltpu.make_async_copy(source, target, sems.at[len(starts)])
            copy.start()
            starts.append(copy)
            at += 1
    at = 0
    for slot, number, first, width, pieces in plan:
        for index in range(len(pieces)):
            starts[at + index].wait()
        begin = at

        def body(block, carry, begin=begin, slot=slot, first=first, width=width, pieces=pieces):
            value = buffers[begin, block, :width].astype(F32)
            for index in range(1, len(pieces)):
                value = value + buffers[begin + index, block, :width].astype(F32)
            outs[slot][block, first : first + width] = value.astype(BF)
            return carry

        lax.fori_loop(0, number, body, 0)
        at += len(pieces)


def settle(sums, *tokens):
    arrays = []
    plan = []
    shapes = []
    for slot, item in enumerate(sums):
        number = item.number() // 2
        first = 0
        for width, pieces in item.segments:
            entry = []
            for array, low in pieces:
                found = [at for at, other in enumerate(arrays) if other is array]
                if not found:
                    arrays.append(array)
                entry.append((found[0] if found else len(arrays) - 1, low))
            plan.append((slot, number, first, width, entry))
            first += width
        block = item.segments[0][1][0][0].shape[2:]
        shapes.append(shaped((number, first) + block, BF))
    tied = list(tie(*arrays, *tokens))[: len(arrays)] if tokens else arrays
    buffers = sum(len(entry[4]) for entry in plan)
    size = (max(entry[1] for entry in plan), max(entry[3] for entry in plan)) + shapes[0].shape[2:]
    moved = sum(entry[1] * entry[3] * (len(entry[4]) + 1) for entry in plan) * 16384
    sends = pl.pallas_call(
        functools.partial(combine_kernel, plan, len(tied)),
        out_shape=shapes,
        in_specs=[ANY] * len(tied),
        out_specs=[VMEM] * len(shapes),
        scratch_shapes=[pltpu.VMEM((buffers,) + size, BF), pltpu.SemaphoreType.DMA((buffers,))],
        cost_estimate=pl.CostEstimate(flops=0, bytes_accessed=moved, transcendentals=0),
        compiler_params=pltpu.CompilerParams(vmem_limit_bytes=32 * 1024 * 1024),
    )(*tied)
    for item, send in zip(sums, sends):
        item.send = send


def tie_sums(array, *sums):
    tied = tie(array, *[item.send for item in sums])
    for item, send in zip(sums, tied[1:]):
        item.send = send
    return tied[0]


def adam_update(weight, gradient, first, second, rate, decay):
    first_new = BETA_ONE * first + (1.0 - BETA_ONE) * gradient
    second_new = BETA_TWO * second + (1.0 - BETA_TWO) * gradient * gradient
    first_hat = first_new / (1.0 - BETA_ONE**STEP)
    second_hat = second_new / (1.0 - BETA_TWO**STEP)
    weight_new = weight - rate * (first_hat / (jnp.sqrt(second_hat) + EPS_ADAM) + decay * weight)
    return (weight_new, first_new, second_new, weight_new.astype(BF))


def gather_small(vectors, hidden):
    whole = lax.all_gather(vectors.astype(BF), AXES, axis=1, tiled=True)
    deep = lax.all_gather(hidden.astype(BF), AXES, axis=1, tiled=True)
    whole = jnp.pad(whole, ((0, HIDDEN_ROW - whole.shape[0]), (0, 0)))
    return jnp.concatenate([whole, deep.reshape(-1, whole.shape[1])], axis=0).astype(F32)


def scatter_small(grads, vectors, hidden, place, count):
    whole = lax.psum(small_rows(*grads), AXES)
    rows, lanes = vectors.shape
    first = lax.dynamic_slice_in_dim(whole[:rows], place * lanes, lanes, axis=1)
    layers, lanes = hidden.shape
    deep = whole[HIDDEN_ROW:].reshape(layers, -1)
    return first, lax.dynamic_slice_in_dim(deep, place * lanes, lanes, axis=1)


def gather_whole(attention, up, down):
    width = attention.shape[2]
    number = width // BLOCK
    square = lax.all_gather(attention, AXES, axis=1, tiled=True)
    square = square.reshape(-1, QUAD, number, BLOCK, width).transpose(0, 2, 1, 3, 4)
    tall = lax.all_gather(up, AXES, axis=1, tiled=True)
    tall = tall.reshape(2, number, BLOCK, QUAD, width).transpose(0, 1, 3, 2, 4)
    deep = lax.all_gather(down, AXES, axis=1, tiled=True).reshape(2, number, QUAD, BLOCK, width)
    half = number // 2
    quads = [square[0], tall[0], deep[0], square[1], square[2], tall[1], deep[1]]
    return [(quad[:half], quad[half:]) for quad in quads]


def scatter_whole(quads):
    joined = [jnp.concatenate(pair, axis=0).astype(F32) for pair in quads]
    number, _, _, width = joined[0].shape
    square = jnp.stack([joined[0], joined[3], joined[4]])
    square = square.transpose(0, 2, 1, 3, 4).reshape(3 * QUAD, width, width)
    tall = jnp.stack([joined[1], joined[5]]).transpose(0, 1, 3, 2, 4)
    tall = tall.reshape(2, width, QUAD * width)
    deep = jnp.stack([joined[2], joined[6]]).reshape(2, QUAD * width, width)
    return [
        lax.psum_scatter(part, AXES, scatter_dimension=1, tiled=True)
        for part in (square, tall, deep)
    ]


def direct_step(pairs, source, target, grad, masters, firsts, seconds, axis_sizes):
    net = Direct(axis_sizes)
    source_pair, target_pair, cross_pair = pairs
    a, b = net.table("a"), net.table("b")
    plain = jnp.arange(net.count, dtype=jnp.int32)
    cut = QUAD // 2
    at = (net.place % (net.count * LANES // source.shape[1])).astype(jnp.int32).reshape(1)

    first, later = first_arrays(at, *masters)
    later = lax.all_gather(later, AXES, axis=0, tiled=False)
    names = ("a", "b")
    first = net.grow(net.grow([first], names, 0), names, 1)[0]
    left, right = net.grow(net.grow([first[:, :QUAD], first[:, QUAD:]], names, 2), names, 3)
    left = net.finish(left, "a")
    right = net.finish(right, "b")
    enc_attend_w = [(a, left, 0, cut), (b, right, 0, cut)]
    self_w = [(a, left, cut, cut), (b, right, cut + 1, cut)]
    enc_kept = attend_forward(source_pair, None, 0, source, None, enc_attend_w, False)
    enc_mid, small = enc_kept[0], enc_kept[8]
    self_kept = attend_forward(target_pair, small, 8, target, None, self_w, True)
    dec_one = self_kept[0]
    later, enc_mid, dec_one = tie(later, enc_mid, dec_one)
    cross_w, up_one, down_one, up_two, down_two = [
        (plain, [later], QUAD * slot, QUAD) for slot in range(5)
    ]
    enc_feed_w = [up_one, down_one]
    enc_feed_kept = feed_forward(small, 5, HIDDEN_ROW, enc_mid, enc_feed_w)
    memory = enc_feed_kept[0]
    cross_w = [(plain, [later], 0, cut), (plain, [later], cut, cut)]
    cross_kept = attend_forward(cross_pair, small, 13, dec_one, memory, cross_w, False)
    dec_two = cross_kept[0]
    result, two_grad, dec_feed_small, feed_two = feed_both(
        (a, b), small, 18, HIDDEN_ROW + QUAD, dec_two, grad, [up_two, down_two]
    )

    feed_two = sum_of(net, "a", *feed_two, (QUAD, QUAD)).step()
    one_grad, memory_grad, cross_small, cross_q = attend_backward(
        (a, b), cross_pair, small, 13, two_grad, cross_kept, dec_one, memory, cross_w, False, None
    )
    cross_s = sum_of(net, "a", *cross_q, (cut, cut))
    feed_two = feed_two.split(names)
    settle(feed_two, cross_small)
    memory_grad = tie_sums(memory_grad, *feed_two, cross_s)
    step_all(feed_two + [cross_s])
    mid_grad, enc_feed_small, feed_one = feed_backward(
        (a, b), small, 5, memory_grad, enc_feed_kept, enc_mid, enc_feed_w
    )
    feed_one = sum_of(net, "a", *feed_one, (QUAD, QUAD))
    cross_s = cross_s.split(names)
    settle(feed_two + cross_s, enc_feed_small)
    one_grad = tie_sums(one_grad, *feed_two, *cross_s, feed_one)
    step_all(feed_two + cross_s + [feed_one])
    target_grad, _, self_small, self_q = attend_backward(
        (a, b), target_pair, small, 8, one_grad, self_kept, target, None, self_w, True, None
    )
    self_s = sum_of(net, "a", *self_q, (cut, cut))
    feed_one = feed_one.split(names)
    settle(cross_s + feed_one, self_small, *[array for item in feed_two for array in item.last()])
    mid_grad = tie_sums(mid_grad, *cross_s, *feed_one, self_s)
    step_all(cross_s + feed_one + [self_s])
    others = (enc_feed_small, self_small, cross_small, dec_feed_small)
    source_grad, _, _, enc_q = attend_backward(
        (a, b), source_pair, small, 0, mid_grad, enc_kept, source, None, enc_attend_w, False, others
    )
    enc_s = sum_of(net, "a", *enc_q, (cut, cut + 1))
    self_s = self_s.split(names)
    settle(self_s + feed_one, source_grad, *[array for item in cross_s for array in item.last()])
    enc_s.send = tie_sums(enc_s.send, *self_s, *feed_one)
    step_all([enc_s] + self_s + feed_one)
    enc_s = enc_s.split(names)
    decoder = joined(feed_two + cross_s)
    settle(enc_s + self_s + [decoder], *[array for item in feed_one for array in item.last()])
    step_all(enc_s + self_s + [decoder])
    encoder = joined(self_s + feed_one)
    settle(enc_s + [encoder, decoder])
    step_all(enc_s + [encoder, decoder])
    ending = joined(enc_s)
    settle([ending, encoder], *decoder.last())
    step_all([ending, encoder])
    settle([ending], *encoder.last())
    ending.step()

    square = [(0, index) for index in range(3 * QUAD)]
    tall, deep = [], []
    for layer in range(2):
        for index in range(QUAD):
            lanes = slice(index * source.shape[1], (index + 1) * source.shape[1])
            tall.append((1, (layer, slice(None), lanes)))
            deep.append((2, (layer, slice(index * BLOCK, (index + 1) * BLOCK))))
    targets = [square[:cut], square[cut:QUAD] + [(3, None)]]
    targets += [square[QUAD : QUAD + cut], square[QUAD + cut : 2 * QUAD], tall[:QUAD], deep[:QUAD]]
    targets += [tall[QUAD:], deep[QUAD:]]
    targets += [square[2 * QUAD : 2 * QUAD + cut], square[2 * QUAD + cut :]]
    segments = ending.segments + encoder.segments + decoder.segments
    segments = [segment + (target,) for segment, target in zip(segments, targets)]
    updated = last_update(at, segments, masters, firsts, seconds)
    return (memory, result, source_grad, target_grad), updated


def whole_step(pairs, source, target, grad, masters, firsts, seconds, axis_sizes):
    attention, up, down = [master.astype(BF) for master in masters[:3]]
    vectors, hidden = masters[3:]
    source_pair, target_pair, cross_pair = pairs
    small = gather_small(vectors, hidden)
    quads = gather_whole(attention, up, down)
    table = jnp.arange(source.shape[1] // BLOCK, dtype=jnp.int32)
    two = (table, table)
    parts = [(table, list(quad), 0, QUAD) for quad in quads]
    enc_kept = attend_forward(source_pair, small, 0, source, None, parts[:1], False)
    enc_mid = enc_kept[0]
    enc_feed_kept = feed_forward(small, 5, HIDDEN_ROW, enc_mid, parts[1:3])
    memory = enc_feed_kept[0]
    self_kept = attend_forward(target_pair, small, 8, target, None, parts[3:4], True)
    dec_one = self_kept[0]
    cross_kept = attend_forward(cross_pair, small, 13, dec_one, memory, parts[4:5], False)
    dec_two = cross_kept[0]
    result, two_grad, dec_feed_small, feed_two = feed_both(
        two, small, 18, HIDDEN_ROW + QUAD, dec_two, grad, parts[5:7]
    )
    one_grad, memory_grad, cross_small, cross_q = attend_backward(
        two[:1], cross_pair, small, 13, two_grad, cross_kept, dec_one, memory, parts[4:5], False, None
    )
    target_grad, _, self_small, self_q = attend_backward(
        two[:1], target_pair, small, 8, one_grad, self_kept, target, None, parts[3:4], True, None
    )
    mid_grad, enc_feed_small, feed_one = feed_backward(
        two, small, 5, memory_grad, enc_feed_kept, enc_mid, parts[1:3]
    )
    source_grad, _, enc_small, enc_q = attend_backward(
        two[:1], source_pair, small, 0, mid_grad, enc_kept, source, None, parts[:1], False, None
    )
    quads = [enc_q]
    quads += [[half[:, low : low + QUAD] for half in feed_one] for low in (0, QUAD)]
    quads += [self_q, cross_q]
    quads += [[half[:, low : low + QUAD] for half in feed_two] for low in (0, QUAD)]
    smalls = (enc_small, enc_feed_small, self_small, cross_small, dec_feed_small)
    count = axis_sizes[0] * axis_sizes[1]
    shares = scatter_small(smalls, vectors, hidden, lax.axis_index(AXES), count)
    grads = tuple(scatter_whole(quads)) + shares
    updated = [
        adam_update(
            masters[slot], grads[slot], firsts[slot], seconds[slot], RATES[slot], DECAYS[slot]
        )
        for slot in range(5)
    ]
    flat = [updated[slot][kind] for kind in range(4) for slot in range(5)]
    return (memory, result, source_grad, target_grad), flat


def per_device(
    axis_sizes,
    source_tokens,
    target_tokens,
    source_segments,
    target_segments,
    output_grad,
    attention_weight,
    up_weight,
    down_weight,
    vectors,
    hidden_bias,
    *moments,
):
    masters = (attention_weight, up_weight, down_weight, vectors, hidden_bias)
    firsts = moments[:5]
    seconds = moments[5:]
    width = source_tokens.shape[2]
    pairs = (
        (source_segments, source_segments),
        (target_segments, target_segments),
        (target_segments, source_segments),
    )
    direct = axis_sizes[0] * axis_sizes[1] * BLOCK == width
    tokens, updated = (direct_step if direct else whole_step)(
        pairs,
        source_tokens[0],
        target_tokens[0],
        output_grad[0],
        masters,
        firsts,
        seconds,
        axis_sizes,
    )
    return tuple(array[None] for array in tokens) + tuple(updated)


def solution(mesh):
    rows = P(AXES, None, None)
    line = P(AXES, None)
    matrix = P(None, AXES, None)
    vector = P(None, AXES)
    state = (matrix, matrix, matrix, vector, vector)
    return jax.shard_map(
        functools.partial(per_device, (mesh.shape["dp"], mesh.shape["fsdp"])),
        mesh=mesh,
        in_specs=(rows, rows, line, line, rows) + state * 3,
        out_specs=(rows,) * 4 + state * 4,
        check_vma=False,
    )
```

```python
import functools

import jax
import jax.numpy as jnp
from jax import lax
from jax.experimental import pallas as pl
from jax.experimental.pallas import tpu as pltpu
from jax.sharding import PartitionSpec as P

HEADS = 8
STEP = 10
EPS_NORM = 1e-05
EPS_ADAM = 1e-08
BETA_ONE = 0.9
BETA_TWO = 0.999
LOWEST = -1e30
RATES = (0.05, 0.05, 0.05, 0.3, 0.3)
DECAYS = (0.01, 0.01, 0.01, 0.0, 0.0)
AXES = ("dp", "fsdp")
QUAD = 4
BLOCK = 16
LANES = 128
SMALL_ROWS = 32
VMEM_BYTES = 60 * 1024 * 1024
HIDDEN_ROW = 24
BF = jnp.bfloat16
F32 = jnp.float32
VMEM = pl.BlockSpec(memory_space=pltpu.VMEM)
SMEM = pl.BlockSpec(memory_space=pltpu.SMEM)
ANY = pl.BlockSpec(memory_space=pl.ANY)
ROOT_TWO_PI = 0.7978845608028654
CUBIC = 0.044715


def dot(left, right):
    return jnp.dot(left, right, preferred_element_type=F32)


def dot_nt(left, right):
    return lax.dot_general(left, right, (((1,), (1,)), ((), ())), preferred_element_type=F32)


def load_start(part, place, sems):
    table, arrays, low, number = part
    at = 0
    for slot, array in enumerate(arrays):
        for index in range(array.shape[0]):
            source = array.at[index, low : low + number]
            pltpu.make_async_copy(source, place(table[at]), sems.at[slot]).start()
            at += 1


def load_wait(part, sems):
    table, arrays, low, number = part
    for slot, array in enumerate(arrays):
        whole = array.at[:, low : low + number]
        pltpu.make_async_copy(whole, whole, sems.at[slot]).wait()


def store_start(part, place, sems):
    table, arrays, low, number = part
    half = arrays[0].shape[0]
    for index in range(half):
        for slot in (1, 0):
            target = arrays[slot].at[index, low : low + number]
            source = place(table[slot * half + index])
            pltpu.make_async_copy(source, target, sems.at[slot]).start()


def row_place(scratch, low, high):
    def place(block):
        start = pl.multiple_of(block * BLOCK, BLOCK)
        return scratch.at[low:high, pl.ds(start, BLOCK), :]

    return place


def block_place(scratch):
    return lambda block: scratch.at[block]


def norm_forward(pre, gain, shift, out_ref, hat_ref, rstd_ref):
    mean = jnp.mean(pre, axis=-1, keepdims=True)
    centred = pre - mean
    spread = jnp.mean(centred * centred, axis=-1, keepdims=True)
    rstd = lax.rsqrt(spread + EPS_NORM)
    hat = centred * rstd
    hat_ref[...] = hat
    rstd_ref[...] = jnp.broadcast_to(rstd, rstd_ref.shape)
    out_ref[...] = hat * gain + shift


def norm_backward(grad, hat, rstd, gain):
    gain_grad = jnp.sum(grad * hat, axis=0, keepdims=True)
    shift_grad = jnp.sum(grad, axis=0, keepdims=True)
    scaled = grad * gain
    one = jnp.mean(scaled, axis=-1, keepdims=True)
    two = jnp.mean(scaled * hat, axis=-1, keepdims=True)
    return rstd * (scaled - one - hat * two), gain_grad, shift_grad


def lane_mask(rows):
    return lax.broadcasted_iota(jnp.int32, (rows, LANES), 1) < LANES // 2


def stacked_pair(block):
    first = lane_mask(block.shape[0])
    zero = jnp.zeros_like(block)
    return jnp.concatenate([jnp.where(first, block, zero), jnp.where(first, zero, block)], axis=0)


def merged_pair(stacked):
    rows = stacked.shape[0] // 2
    return jnp.where(lane_mask(rows), stacked[:rows], stacked[rows:])


def mask_fill(bias_ref, column_seg, row_seg, causal, transposed):
    length = bias_ref.shape[0]
    column = jnp.broadcast_to(column_seg, (LANES, length)).T
    for at in range(0, length, LANES):
        same = column == row_seg[:, at : at + LANES]
        if causal:
            down = lax.broadcasted_iota(jnp.int32, (length, LANES), 0)
            along = lax.broadcasted_iota(jnp.int32, (length, LANES), 1) + at
            order = (down <= along) if transposed else (along <= down)
            same = same & order
        bias_ref[:, at : at + LANES] = jnp.where(same, 0.0, LOWEST)


def take_parts(refs, layout, tables):
    parts = []
    for slot, (arrays, low, number) in enumerate(layout):
        parts.append((tables[slot], [refs.pop(0) for _ in range(arrays)], low, number))
    return parts


def small_part(part):
    table, arrays, low, number = part
    return table, arrays, low + number, 1


def small_join(blocks_ref):
    count = blocks_ref.shape[0]
    groups = blocks_ref.shape[3] // LANES
    per = count // groups
    vectors = []
    hidden = [[], []]
    for group in range(groups):
        total = blocks_ref[group * per, 0, :8].astype(F32)
        for at in range(group * per + 1, (group + 1) * per):
            total = total + blocks_ref[at, 0, :8].astype(F32)
        columns = [total[:, at : at + LANES] for at in range(0, 4 * LANES, LANES)]
        vectors.append(jnp.concatenate(columns[:3], axis=0))
        for layer in range(2):
            rows = [columns[3][4 * layer + at : 4 * layer + at + 1] for at in range(4)]
            hidden[layer].append(jnp.concatenate(rows, axis=1))
    return jnp.concatenate([jnp.concatenate(vectors, axis=1)] + hidden[0] + hidden[1], axis=0)


def small_split(whole, group):
    lanes = slice(group * LANES, (group + 1) * LANES)
    columns = [whole[at : at + 8, lanes] for at in (0, 8, 16)]
    rows = []
    for layer in range(2):
        row = whole[24 + 4 * layer + group : 25 + 4 * layer + group]
        rows += [row[:, at : at + LANES] for at in range(0, 4 * LANES, LANES)]
    columns.append(jnp.concatenate(rows, axis=0))
    block = jnp.concatenate(columns, axis=1)
    return jnp.concatenate([block, jnp.zeros_like(block)], axis=0).astype(BF)


def attend_forward_kernel(layout, cross, causal, base, joins, *refs):
    refs = list(refs)
    tables = [refs.pop(0) for _ in layout]
    query_seg = refs.pop(0)
    key_seg = refs.pop(0)
    small = None if joins else refs.pop(0)
    rows_ref = refs.pop(0)
    memory_ref = refs.pop(0) if cross else None
    parts = take_parts(refs, layout, tables)
    out_ref, hat_ref, rstd_ref, q_ref, k_ref, v_ref, o_ref, lse_ref = [refs.pop(0) for _ in range(8)]
    if joins:
        small = refs.pop(0)
        blocks_ref = refs.pop()
        extra = small_part(parts[-1])
    w_ref, bias_ref, sems = refs
    first = 0
    if joins:
        load_start(extra, lambda block: blocks_ref.at[block], sems.at[len(parts)])
    for slot, part in enumerate(parts):
        load_start(part, row_place(w_ref, first, first + part[3]), sems.at[slot])
        first += part[3]
    length, width = rows_ref.shape
    mask_fill(bias_ref, query_seg[...], key_seg[...], causal, False)
    rows = rows_ref[...].astype(BF)
    keys = memory_ref[...].astype(BF) if cross else rows
    if joins:
        load_wait(extra, sems.at[len(parts)])
        small[...] = small_join(blocks_ref)
    for slot, part in enumerate(parts):
        load_wait(part, sems.at[slot])
    scale = (width // HEADS) ** (-0.5)
    q_ref[...] = (dot(rows, w_ref[0]) + small[base : base + 1]).astype(BF) * jnp.asarray(scale, BF)
    k_ref[...] = dot(keys, w_ref[1]).astype(BF)
    v_ref[...] = (dot(keys, w_ref[2]) + small[base + 1 : base + 2]).astype(BF)
    lane = lax.broadcasted_iota(jnp.int32, (LANES, LANES), 1)
    for at in range(0, length, LANES):
        reach = at + LANES if causal else length
        logs = jnp.zeros((LANES, LANES), F32)
        for pair in range(HEADS // 2):
            lanes = slice(pair * LANES, (pair + 1) * LANES)
            stacked = stacked_pair(q_ref[at : at + LANES, lanes])
            scores = dot_nt(stacked, k_ref[:reach, lanes])
            bias = bias_ref[at : at + LANES, :reach]
            scores = scores + jnp.concatenate([bias, bias], axis=0)
            largest = jnp.max(scores, axis=-1, keepdims=True)
            exponent = jnp.exp(scores - largest).astype(BF)
            values = jnp.concatenate([v_ref[:reach, lanes], jnp.ones((reach, LANES), BF)], axis=1)
            mixed = dot(exponent, values)
            total = mixed[:, LANES:]
            o_ref[at : at + LANES, lanes] = merged_pair(mixed[:, :LANES] / total).astype(BF)
            log_total = largest + jnp.log(total)
            logs = jnp.where(lane == 2 * pair, log_total[:LANES], logs)
            logs = jnp.where(lane == 2 * pair + 1, log_total[LANES:], logs)
        lse_ref[:, at : at + LANES] = logs.T[:HEADS]
    attended = dot(o_ref[...], w_ref[3]) + small[base + 2 : base + 3]
    pre = rows_ref[...].astype(F32) + attended
    norm_forward(pre, small[base + 3 : base + 4], small[base + 4 : base + 5], out_ref, hat_ref, rstd_ref)


def attend_backward_kernel(layout, cross, causal, base, splits, *refs):
    refs = list(refs)
    tables = [refs.pop(0) for _ in layout]
    out_tables = [refs.pop(0), refs.pop(0)]
    query_seg = refs.pop(0)
    key_seg = refs.pop(0)
    small = refs.pop(0)
    grad_ref = refs.pop(0)
    hat_ref, rstd_ref = refs.pop(0), refs.pop(0)
    rows_ref = refs.pop(0)
    memory_ref = refs.pop(0) if cross else None
    q_ref, k_ref, v_ref, o_ref, lse_ref = [refs.pop(0) for _ in range(5)]
    others = [refs.pop(0) for _ in range(4)] if splits else None
    parts = take_parts(refs, layout, tables)
    rows_out = refs.pop(0)
    memory_out = refs.pop(0) if cross else None
    small_out = None if splits else refs.pop(0)
    targets = [refs.pop(0), refs.pop(0)]
    outs = []
    for slot, table in enumerate(out_tables):
        outs.append((table, targets, slot * QUAD // 2, QUAD // 2))
    blocks_ref = refs.pop() if splits else None
    w_ref, dw_ref, bias_ref, dout_ref, dq_t_ref, dk_ref, dv_ref, kt_ref, sems = refs
    first = 0
    for slot, part in enumerate(parts):
        load_start(part, row_place(w_ref, first, first + part[3]), sems.at[slot])
        first += part[3]
    length, width = rows_ref.shape
    head = width // HEADS
    scale = head ** (-0.5)
    mask_fill(bias_ref, key_seg[...], query_seg[...], causal, True)
    kt_ref[...] = k_ref[...].T
    pre_grad, gain_grad, shift_grad = norm_backward(
        grad_ref[...], hat_ref[...], rstd_ref[:, :1], small[base + 3 : base + 4]
    )
    rows_out[...] = pre_grad
    low = pre_grad.astype(BF)
    for slot, part in enumerate(parts):
        load_wait(part, sems.at[slot])
    dout_ref[...] = dot_nt(low, w_ref[3]).astype(BF)
    dw_ref[3] = dot(o_ref[...].T, low).astype(BF)
    out_bias = jnp.sum(low.astype(F32), axis=0, keepdims=True)
    product = dout_ref[...].astype(F32) * o_ref[...].astype(F32)
    high = product.astype(BF)
    rest = (product - high.astype(F32)).astype(BF)
    picker = lax.broadcasted_iota(jnp.int32, (BLOCK, width), 1) // head
    picker = (picker == lax.broadcasted_iota(jnp.int32, (BLOCK, width), 0)).astype(BF)
    row_dots = dot_nt(picker, high) + dot_nt(picker, rest)
    for pair in range(HEADS // 2):
        lanes = slice(pair * LANES, (pair + 1) * LANES)
        for at in range(0, length, LANES):
            begin = at if causal else 0
            query = q_ref[begin:, lanes]
            dout = dout_ref[begin:, lanes]
            scores = dot_nt(stacked_pair(k_ref[at : at + LANES, lanes]), query)
            prob_grad = dot_nt(stacked_pair(v_ref[at : at + LANES, lanes]), dout)
            bias = bias_ref[at : at + LANES, begin:]
            probs = []
            score_grads = []
            for part in range(2):
                which = 2 * pair + part
                half = slice(part * LANES, (part + 1) * LANES)
                prob = jnp.exp(scores[half] + (bias - lse_ref[which : which + 1, begin:]))
                probs.append(prob.astype(BF))
                row_dot = row_dots[which : which + 1, begin:]
                score_grads.append((prob * (prob_grad[half] - row_dot)).astype(BF))
                at_t = pair * LANES + part * head
                back = dot(kt_ref[at_t : at_t + head, at : at + LANES], score_grads[part])
                if at == 0:
                    dq_t_ref[at_t : at_t + head, :] = back
                else:
                    dq_t_ref[at_t : at_t + head, begin:] += back
            value_back = dot(jnp.concatenate(probs, axis=0), dout)
            dv_ref[at : at + LANES, lanes] = merged_pair(value_back).astype(BF)
            key_back = dot(jnp.concatenate(score_grads, axis=0), query)
            dk_ref[at : at + LANES, lanes] = merged_pair(key_back).astype(BF)
    query_grad = (dq_t_ref[...] * scale).T.astype(BF)
    key_grad = dk_ref[...]
    value_grad = dv_ref[...]
    turned = rows_ref[...].astype(BF).T
    dw_ref[0] = dot(turned, query_grad).astype(BF)
    if cross:
        turned = memory_ref[...].astype(BF).T
    dw_ref[1] = dot(turned, key_grad).astype(BF)
    dw_ref[2] = dot(turned, value_grad).astype(BF)
    first = 0
    for slot, part in enumerate(outs):
        store_start(part, row_place(dw_ref, first, first + part[3]), sems.at[slot])
        first += part[3]
    rows_back = rows_out[...] + dot_nt(query_grad, w_ref[0])
    memory_back = dot_nt(key_grad, w_ref[1]) + dot_nt(value_grad, w_ref[2])
    if cross:
        rows_out[...] = rows_back
        memory_out[...] = memory_back
    else:
        rows_out[...] = rows_back + memory_back
    query_bias = jnp.sum(query_grad.astype(F32), axis=0, keepdims=True)
    value_bias = jnp.sum(value_grad.astype(F32), axis=0, keepdims=True)
    spare = jnp.zeros((3, width), F32)
    own = jnp.concatenate(
        [query_bias, value_bias, out_bias, gain_grad, shift_grad, spare], axis=0
    )
    if splits:
        enc_feed, self_attend, cross_attend, dec_feed = [other[...] for other in others]
        whole = small_rows(own, enc_feed, self_attend, cross_attend, dec_feed)
        groups = blocks_ref.shape[0]
        for group in range(groups):
            blocks_ref[group, 0] = small_split(whole, group)
        extra = small_part(outs[-1])
        per = 2 * extra[1][0].shape[0] // groups
        store_start(extra, lambda block: blocks_ref.at[block // per], sems.at[2])
        load_wait(extra, sems.at[2])
    else:
        small_out[...] = own
    for slot, part in enumerate(outs):
        load_wait(part, sems.at[slot])


def small_rows(enc_attend, enc_feed, self_attend, cross_attend, dec_feed):
    return jnp.concatenate(
        [
            enc_attend[:5],
            enc_feed[:3],
            self_attend[:5],
            cross_attend[:5],
            dec_feed[:3],
            dec_feed[7:],
            dec_feed[7:],
            dec_feed[7:],
            enc_feed[3:7],
            dec_feed[3:7],
        ],
        axis=0,
    )


def gelu_parts(pre):
    square = pre * pre
    curve = jnp.tanh(ROOT_TWO_PI * pre * (1.0 + CUBIC * square))
    half = 0.5 * pre
    rise = 0.5 + 0.5 * curve
    bend = ROOT_TWO_PI * (1.0 + 3.0 * CUBIC * square)
    return pre * rise, rise + half * (1.0 - curve * curve) * bend


def chunk_of(ref, index):
    number = ref.shape[0] // QUAD
    part = ref[index * number : (index + 1) * number]
    return part.reshape(number * ref.shape[1] * ref.shape[2], ref.shape[3])


def feed_forward_steps(small, base, hidden_at, rows_ref, up_ref, down_ref, active_ref, slope_ref):
    rows = rows_ref[...].astype(BF)
    total = rows_ref[...] + small[base : base + 1]
    for index in range(QUAD):
        at = hidden_at + index
        pre = dot(rows, up_ref[index]) + small[at : at + 1]
        active, slope = gelu_parts(pre)
        active = active.astype(BF)
        active_ref[index] = active
        slope_ref[index] = slope
        total = total + dot(active, chunk_of(down_ref, index))
    return total


def feed_backward_steps(
    pre_grad, rows_ref, up_ref, down_ref, active_ref, slope_ref, dup_ref, ddown_ref, rows_out
):
    low = pre_grad.astype(BF)
    turned = rows_ref[...].astype(BF).T
    total = pre_grad
    hidden_grads = []
    number = ddown_ref.shape[0] // QUAD
    for index in range(QUAD):
        down_grad = dot(active_ref[index].T, low).astype(BF)
        ddown_ref[index * number : (index + 1) * number] = down_grad.reshape(
            (number,) + ddown_ref.shape[1:]
        )
        back = dot_nt(low, chunk_of(down_ref, index))
        hidden = (back * slope_ref[index]).astype(BF)
        hidden_grads.append(jnp.sum(hidden.astype(F32), axis=0, keepdims=True))
        dup_ref[index] = dot(turned, hidden).astype(BF)
        total = total + dot_nt(hidden, up_ref[index])
    rows_out[...] = total
    out_bias = jnp.sum(low.astype(F32), axis=0, keepdims=True)
    return out_bias, hidden_grads


def load_feed(parts, up_ref, down_ref, sems):
    load_start(parts[0], row_place(up_ref, 0, QUAD), sems.at[0])
    load_start(parts[1], block_place(down_ref), sems.at[1])


def store_feed(outs, dup_ref, ddown_ref, sems):
    store_start(outs[1], block_place(ddown_ref), sems.at[1])
    store_start(outs[0], row_place(dup_ref, 0, QUAD), sems.at[0])


def wait_feed(parts, sems):
    for slot, part in enumerate(parts):
        load_wait(part, sems.at[slot])


def feed_outs(refs, tables):
    arrays = [refs.pop(0), refs.pop(0)]
    return [(tables[slot], arrays, slot * QUAD, QUAD) for slot in range(2)]


def feed_small(out_bias, gain_grad, shift_grad, hidden_grads):
    spare = jnp.zeros_like(out_bias)
    return jnp.concatenate([out_bias, gain_grad, shift_grad] + hidden_grads + [spare], axis=0)


def feed_forward_kernel(layout, base, hidden_at, *refs):
    refs = list(refs)
    tables = [refs.pop(0), refs.pop(0)]
    small, rows_ref = refs.pop(0), refs.pop(0)
    parts = take_parts(refs, layout, tables)
    out_ref, hat_ref, rstd_ref, active_ref, slope_ref, up_ref, down_ref, sems = refs
    load_feed(parts, up_ref, down_ref, sems)
    wait_feed(parts, sems)
    pre = feed_forward_steps(
        small, base, hidden_at, rows_ref, up_ref, down_ref, active_ref, slope_ref
    )
    norm_forward(pre, small[base + 1 : base + 2], small[base + 2 : base + 3], out_ref, hat_ref, rstd_ref)


def feed_backward_kernel(layout, base, *refs):
    refs = list(refs)
    tables = [refs.pop(0), refs.pop(0)]
    out_tables = [refs.pop(0), refs.pop(0)]
    small, grad_ref, hat_ref, rstd_ref, rows_ref = [refs.pop(0) for _ in range(5)]
    active_ref, slope_ref = refs.pop(0), refs.pop(0)
    parts = take_parts(refs, layout, tables)
    rows_out, small_out = refs.pop(0), refs.pop(0)
    outs = feed_outs(refs, out_tables)
    up_ref, down_ref, dup_ref, ddown_ref, sems, out_sems = refs
    load_feed(parts, up_ref, down_ref, sems)
    pre_grad, gain_grad, shift_grad = norm_backward(
        grad_ref[...], hat_ref[...], rstd_ref[:, :1], small[base + 1 : base + 2]
    )
    wait_feed(parts, sems)
    out_bias, hidden_grads = feed_backward_steps(
        pre_grad, rows_ref, up_ref, down_ref, active_ref, slope_ref, dup_ref, ddown_ref, rows_out
    )
    store_feed(outs, dup_ref, ddown_ref, out_sems)
    small_out[...] = feed_small(out_bias, gain_grad, shift_grad, hidden_grads)
    wait_feed(outs, out_sems)


def feed_both_kernel(layout, base, hidden_at, *refs):
    refs = list(refs)
    tables = [refs.pop(0), refs.pop(0)]
    out_tables = [refs.pop(0), refs.pop(0)]
    small, rows_ref, grad_ref = [refs.pop(0) for _ in range(3)]
    parts = take_parts(refs, layout, tables)
    out_ref, rows_out, small_out = [refs.pop(0) for _ in range(3)]
    outs = feed_outs(refs, out_tables)
    up_ref, down_ref, dup_ref, ddown_ref, active_ref, slope_ref, hat_ref, rstd_ref = refs[:8]
    sems, out_sems = refs[8:]
    load_feed(parts, up_ref, down_ref, sems)
    wait_feed(parts, sems)
    pre = feed_forward_steps(
        small, base, hidden_at, rows_ref, up_ref, down_ref, active_ref, slope_ref
    )
    gain = small[base + 1 : base + 2]
    norm_forward(pre, gain, small[base + 2 : base + 3], out_ref, hat_ref, rstd_ref)
    pre_grad, gain_grad, shift_grad = norm_backward(
        grad_ref[...].astype(F32), hat_ref[...], rstd_ref[:, :1], gain
    )
    out_bias, hidden_grads = feed_backward_steps(
        pre_grad, rows_ref, up_ref, down_ref, active_ref, slope_ref, dup_ref, ddown_ref, rows_out
    )
    store_feed(outs, dup_ref, ddown_ref, out_sems)
    small_out[...] = feed_small(out_bias, gain_grad, shift_grad, hidden_grads)
    wait_feed(outs, out_sems)


def shaped(shape, dtype=F32):
    return jax.ShapeDtypeStruct(shape, dtype)


def call(kernel, ins, specs, outs, out_specs, scratch, flops, moved):
    return pl.pallas_call(
        kernel,
        out_shape=outs,
        in_specs=specs,
        out_specs=out_specs,
        scratch_shapes=scratch,
        cost_estimate=pl.CostEstimate(flops=flops, bytes_accessed=moved, transcendentals=0),
        compiler_params=pltpu.CompilerParams(vmem_limit_bytes=VMEM_BYTES),
    )(*ins)


def layout_of(parts):
    return [(len(arrays), low, number) for _, arrays, low, number in parts]


def arrays_of(parts):
    return [array for part in parts for array in part[1]]


def most(parts):
    return max(len(part[1]) for part in parts)


def halves(width, number):
    return [shaped((width // BLOCK // 2, number, BLOCK, width), BF)] * 2


def attend_forward(segments, small, base, rows, memory, parts, causal):
    length, width = rows.shape
    cross = memory is not None
    joins = small is None
    ins = [part[0] for part in parts] + list(segments) + ([] if joins else [small]) + [rows]
    ins += [memory] if cross else []
    specs = [SMEM] * len(parts) + [VMEM] * (len(ins) - len(parts))
    arrays = arrays_of(parts)
    ins += arrays
    specs += [ANY] * len(arrays)
    outs = [shaped((length, width)), shaped((length, width)), shaped((length, LANES))]
    outs += [shaped((length, width), BF)] * 4 + [shaped((HEADS, length))]
    outs += [shaped((SMALL_ROWS, width))] if joins else []
    scratch = [
        pltpu.VMEM((QUAD, width, width), BF),
        pltpu.VMEM((length, length), F32),
        pltpu.SemaphoreType.DMA((len(parts) + 1, most(parts))),
    ]
    scratch += [pltpu.VMEM((width // BLOCK, 1, BLOCK, width), BF)] if joins else []
    kernel = functools.partial(attend_forward_kernel, layout_of(parts), cross, causal, base, joins)
    flops = 8 * length * width * width + 16 * length * length * width
    return call(kernel, ins, specs, outs, [VMEM] * len(outs), scratch, flops, 8_000_000)


def attend_backward(
    out_tables, segments, small, base, grad, kept, rows, memory, parts, causal, others
):
    length, width = rows.shape
    cross = memory is not None
    splits = others is not None
    hat, rstd, q, k, v, o, lse = kept[1:8]
    ins = [part[0] for part in parts] + list(out_tables)
    specs = [SMEM] * len(ins)
    ins += list(segments) + [small, grad, hat, rstd, rows]
    ins += ([memory] if cross else []) + [q, k, v, o, lse] + list(others or ())
    specs += [VMEM] * (len(ins) - len(specs))
    arrays = arrays_of(parts)
    ins += arrays
    specs += [ANY] * len(arrays)
    outs = [shaped((length, width))] * (2 if cross else 1)
    outs += [] if splits else [shaped((8, width))]
    out_specs = [VMEM] * len(outs) + [ANY] * 2
    outs += halves(width, QUAD + (1 if splits else 0))
    scratch = [
        pltpu.VMEM((QUAD, width, width), BF),
        pltpu.VMEM((QUAD, width, width), BF),
        pltpu.VMEM((length, length), F32),
        pltpu.VMEM((length, width), BF),
        pltpu.VMEM((width, length), F32),
        pltpu.VMEM((length, width), BF),
        pltpu.VMEM((length, width), BF),
        pltpu.VMEM((width, length), BF),
        pltpu.SemaphoreType.DMA((3, 2)),
    ]
    scratch += [pltpu.VMEM((width // LANES, 1, BLOCK, width), BF)] if splits else []
    kernel = functools.partial(
        attend_backward_kernel, layout_of(parts), cross, causal, base, splits
    )
    flops = 16 * length * width * width + 40 * length * length * width
    results = list(call(kernel, ins, specs, outs, out_specs, scratch, flops, 12_000_000))
    rows_grad = results.pop(0)
    memory_grad = results.pop(0) if cross else None
    small_grad = None if splits else results.pop(0)
    return rows_grad, memory_grad, small_grad, results


def feed_scratch(width, grads):
    number = width // BLOCK
    once = [pltpu.VMEM((QUAD, width, width), BF), pltpu.VMEM((number, QUAD, BLOCK, width), BF)]
    return once * (2 if grads else 1)


def feed_forward(small, base, hidden_at, rows, parts):
    length, width = rows.shape
    arrays = arrays_of(parts)
    ins = [part[0] for part in parts] + [small, rows] + arrays
    specs = [SMEM] * 2 + [VMEM] * 2 + [ANY] * len(arrays)
    outs = [shaped((length, width)), shaped((length, width)), shaped((length, LANES))]
    outs += [shaped((QUAD, length, width), BF), shaped((QUAD, length, width))]
    scratch = feed_scratch(width, False) + [pltpu.SemaphoreType.DMA((2, most(parts)))]
    kernel = functools.partial(feed_forward_kernel, layout_of(parts), base, hidden_at)
    flops = 16 * length * width * width
    return call(kernel, ins, specs, outs, [VMEM] * len(outs), scratch, flops, 10_000_000)


def feed_backward(out_tables, small, base, grad, kept, rows, parts):
    length, width = rows.shape
    hat, rstd, active, slope = kept[1:]
    arrays = arrays_of(parts)
    ins = [part[0] for part in parts] + list(out_tables) + [small, grad, hat, rstd, rows, active, slope]
    ins += arrays
    specs = [SMEM] * 4 + [VMEM] * 7 + [ANY] * len(arrays)
    outs = [shaped((length, width)), shaped((8, width))] + halves(width, 2 * QUAD)
    out_specs = [VMEM] * 2 + [ANY] * 2
    scratch = feed_scratch(width, True)
    scratch += [pltpu.SemaphoreType.DMA((2, most(parts))), pltpu.SemaphoreType.DMA((2, 2))]
    kernel = functools.partial(feed_backward_kernel, layout_of(parts), base)
    flops = 32 * length * width * width
    results = call(kernel, ins, specs, outs, out_specs, scratch, flops, 14_000_000)
    return results[0], results[1], results[2:4]


def feed_both(out_tables, small, base, hidden_at, rows, grad, parts):
    length, width = rows.shape
    arrays = arrays_of(parts)
    ins = [part[0] for part in parts] + list(out_tables) + [small, rows, grad] + arrays
    specs = [SMEM] * 4 + [VMEM] * 3 + [ANY] * len(arrays)
    outs = [shaped((length, width)), shaped((length, width)), shaped((8, width))]
    outs += halves(width, 2 * QUAD)
    out_specs = [VMEM] * 3 + [ANY] * 2
    scratch = feed_scratch(width, True) + [
        pltpu.VMEM((QUAD, length, width), BF),
        pltpu.VMEM((QUAD, length, width), F32),
        pltpu.VMEM((length, width), F32),
        pltpu.VMEM((length, LANES), F32),
        pltpu.SemaphoreType.DMA((2, most(parts))),
        pltpu.SemaphoreType.DMA((2, 2)),
    ]
    kernel = functools.partial(feed_both_kernel, layout_of(parts), base, hidden_at)
    flops = 48 * length * width * width
    results = call(kernel, ins, specs, outs, out_specs, scratch, flops, 12_000_000)
    return results[0], results[1], results[2], results[3:5]


def first_kernel(at_ref, square_ref, tall_ref, deep_ref, vector_ref, hidden_ref, one_ref, two_ref, rest_ref, turn_ref, line_ref):
    at = at_ref[0]
    width = square_ref.shape[2]
    turn_ref[...] = jnp.zeros_like(turn_ref)
    lanes, rows = vector_ref.shape
    turn_ref[pl.ds(pl.multiple_of(at * lanes, lanes), lanes), :rows] = vector_ref[...]
    upright = turn_ref[...].T
    line_ref[...] = jnp.zeros_like(line_ref)
    layers, lanes = hidden_ref.shape
    per = LANES // lanes
    for layer in range(layers):
        row = jnp.concatenate([hidden_ref[layer : layer + 1]] * per, axis=1)
        lane = lax.broadcasted_iota(jnp.int32, row.shape, 1) // lanes
        row = jnp.where(lane == at % per, row, 0.0)
        line_ref[pl.ds(4 * layer + at // per, 1), :] = row
    columns = [upright[low : low + 8] for low in (0, 8, 16)] + [line_ref[...]]
    block = jnp.concatenate(columns, axis=1)
    small = jnp.concatenate([block, jnp.zeros_like(block)], axis=0)
    tall = []
    deep = []
    for layer in range(2):
        for index in range(QUAD):
            lanes = slice(index * width, (index + 1) * width)
            tall.append(tall_ref[layer, :, lanes])
            deep.append(deep_ref[layer, index * BLOCK : (index + 1) * BLOCK])
    square = [square_ref[index] for index in range(3 * QUAD)]
    groups = [
        square[:QUAD] + [small],
        tall[:QUAD] + deep[:QUAD],
        square[QUAD : 2 * QUAD] + tall[QUAD:] + square[2 * QUAD :] + deep[QUAD:],
    ]
    for out_ref, group in zip((one_ref, two_ref, rest_ref), groups):
        for slot, block in enumerate(group):
            out_ref[0, slot] = block.astype(BF)


def first_arrays(at, square, tall, deep, vectors, hidden):
    width = square.shape[2]
    return pl.pallas_call(
        first_kernel,
        out_shape=[
            shaped((1, QUAD + 1, BLOCK, width), BF),
            shaped((1, 2 * QUAD, BLOCK, width), BF),
            shaped((1, 4 * QUAD, BLOCK, width), BF),
        ],
        in_specs=[SMEM] + [VMEM] * 5,
        out_specs=[VMEM] * 3,
        scratch_shapes=[pltpu.VMEM((LANES, LANES), F32), pltpu.VMEM((8, LANES), F32)],
        compiler_params=pltpu.CompilerParams(vmem_limit_bytes=VMEM_BYTES // 3),
    )(at, square, tall, deep, vectors.T, hidden)


def last_kernel(plan, count, at_ref, *refs):
    arrays, refs = refs[:count], refs[count:]
    masters, firsts, seconds = refs[:5], refs[5:10], refs[10:15]
    outs, refs = [refs[15 + 5 * kind : 20 + 5 * kind] for kind in range(4)], refs[35:]
    buffers, turn_ref, line_ref, sems = refs
    at = at_ref[0]
    starts = []
    for width, pieces, _ in plan:
        for index, low in pieces:
            source = arrays[index].at[0, low : low + width]
            copy = pltpu.make_async_copy(source, buffers.at[len(starts), :width], sems.at[len(starts)])
            copy.start()
            starts.append(copy)

    def update(slot, where, gradient):
        results = adam_update(
            masters[slot][where],
            gradient,
            firsts[slot][where],
            seconds[slot][where],
            RATES[slot],
            DECAYS[slot],
        )
        for kind in range(4):
            outs[kind][slot][where] = results[kind]

    begin = 0
    for width, pieces, targets in plan:
        for index in range(len(pieces)):
            starts[begin + index].wait()
        for sub, (slot, where) in enumerate(targets):
            gradient = buffers[begin, sub].astype(F32)
            for index in range(1, len(pieces)):
                gradient = gradient + buffers[begin + index, sub].astype(F32)
            if slot < 3:
                update(slot, where, gradient)
                continue
            turn_ref[...] = jnp.zeros_like(turn_ref)
            for column in range(3):
                lanes = slice(column * LANES, (column + 1) * LANES)
                turn_ref[8 * column : 8 * column + 8, :] = gradient[:8, lanes]
            turn_ref[...] = turn_ref[...].T
            lanes, rows = masters[3].shape
            share = turn_ref[pl.ds(pl.multiple_of(at * lanes, lanes), lanes), :][:, :rows]
            update(3, slice(None), share)
            line_ref[...] = gradient[:8, 3 * LANES :]
            layers, lanes = masters[4].shape
            per = LANES // lanes
            for layer in range(layers):
                row = line_ref[pl.ds(4 * layer + at // per, 1), :]
                share = row[:, :lanes]
                for part in range(1, per):
                    other = row[:, part * lanes : (part + 1) * lanes]
                    share = jnp.where(at % per == part, other, share)
                update(4, slice(layer, layer + 1), share)
        begin += len(pieces)


def last_update(at, segments, masters, firsts, seconds):
    arrays = []
    plan = []
    for width, pieces, targets in segments:
        entry = []
        for array, low in pieces:
            found = [place for place, other in enumerate(arrays) if other is array]
            if not found:
                arrays.append(array)
            entry.append((found[0] if found else len(arrays) - 1, low))
        plan.append((width, entry, targets))
    params = [list(group) for group in (masters, firsts, seconds)]
    for group in params:
        group[3] = group[3].T
    flat = params[0] + params[1] + params[2]
    outs = [shaped(array.shape) for array in params[0]] * 3
    outs += [shaped(array.shape, BF) for array in params[0]]
    pieces = sum(len(entry[1]) for entry in plan)
    block = arrays[0].shape[2:]
    results = pl.pallas_call(
        functools.partial(last_kernel, plan, len(arrays)),
        out_shape=outs,
        in_specs=[SMEM] + [ANY] * len(arrays) + [VMEM] * len(flat),
        out_specs=[VMEM] * len(outs),
        scratch_shapes=[
            pltpu.VMEM((pieces, max(entry[0] for entry in plan)) + block, BF),
            pltpu.VMEM((LANES, LANES), F32),
            pltpu.VMEM((8, LANES), F32),
            pltpu.SemaphoreType.DMA((pieces,)),
        ],
        compiler_params=pltpu.CompilerParams(vmem_limit_bytes=VMEM_BYTES // 3),
    )(at, *arrays, *flat)
    results = list(results)
    for kind in range(4):
        results[5 * kind + 3] = results[5 * kind + 3].T
    return results


def tie(*arrays):
    return lax.optimization_barrier(arrays)


class Direct:
    def __init__(self, axis_sizes):
        outer, inner = axis_sizes
        self.count = outer * inner
        inner_bits = inner.bit_length() - 1
        bits = self.count.bit_length() - 1
        core = [inner_bits]
        across = list(range(inner_bits + 1, bits))
        up = [0]
        along = list(range(1, inner_bits))
        self.orders = {
            "a": core + across + up + along,
            "b": core + up + across + along,
        }
        self.place = lax.axis_index(AXES)

    def hop(self, array, bit):
        return lax.ppermute(array, AXES, [(at, at ^ (1 << bit)) for at in range(self.count)])

    def table(self, name):
        order = self.orders[name]
        index = jnp.arange(self.count, dtype=jnp.int32)
        block = jnp.zeros_like(index)
        for at, bit in enumerate(order):
            block = block | (((index >> (len(order) - 1 - at)) & 1) << bit)
        return block ^ self.place

    def arrive(self, array, name, step):
        return self.hop(array, self.orders[name][::-1][step])

    def finish(self, array, name):
        return [array, self.hop(array, self.orders[name][0])]


def grown(arrays, arrivals):
    return [jnp.concatenate(pair, axis=0) for pair in zip(arrays, arrivals)]


class Sum:
    def __init__(self, net, name, segments, send, done):
        self.net = net
        self.name = name
        self.segments = segments
        self.send = send
        self.done = done

    def step(self):
        arrived = self.net.hop(self.send, self.net.orders[self.name][self.done])
        self.done += 1
        low = 0
        made = []
        for width, pieces in self.segments:
            made.append((width, pieces + [(arrived, low)]))
            low += width
        self.segments = made
        return self

    def last(self):
        return [self.segments[0][1][-1][0]]

    def number(self):
        return self.segments[0][1][-1][0].shape[0]

    def split(self, names):
        return [
            Sum(self.net, name, [segment], None, self.done)
            for name, segment in zip(names, self.segments)
        ]


def step_all(sums):
    for item in sums:
        item.step()


def sum_of(net, name, keep, send, widths):
    low = 0
    segments = []
    for width in widths:
        segments.append((width, [(keep, low)]))
        low += width
    return Sum(net, name, segments, send, 0)


def joined(sums):
    segments = [segment for item in sums for segment in item.segments]
    return Sum(sums[0].net, sums[0].name, segments, None, sums[0].done)


def combine_kernel(plan, count, *refs):
    arrays, outs, buffers, sems = refs[:count], refs[count:-2], refs[-2], refs[-1]
    at = 0
    starts = []
    for _, number, _, width, pieces in plan:
        for index, low in pieces:
            source = arrays[index].at[number : 2 * number, low : low + width]
            target = buffers.at[at, :number, :width]
            copy = pltpu.make_async_copy(source, target, sems.at[len(starts)])
            copy.start()
            starts.append(copy)
            at += 1
    at = 0
    for slot, number, first, width, pieces in plan:
        for index in range(len(pieces)):
            starts[at + index].wait()
        begin = at

        def body(block, carry, begin=begin, slot=slot, first=first, width=width, pieces=pieces):
            value = buffers[begin, block, :width].astype(F32)
            for index in range(1, len(pieces)):
                value = value + buffers[begin + index, block, :width].astype(F32)
            outs[slot][block, first : first + width] = value.astype(BF)
            return carry

        lax.fori_loop(0, number, body, 0)
        at += len(pieces)


def settle(sums, *tokens):
    arrays = []
    plan = []
    shapes = []
    for slot, item in enumerate(sums):
        number = item.number() // 2
        first = 0
        for width, pieces in item.segments:
            entry = []
            for array, low in pieces:
                found = [at for at, other in enumerate(arrays) if other is array]
                if not found:
                    arrays.append(array)
                entry.append((found[0] if found else len(arrays) - 1, low))
            plan.append((slot, number, first, width, entry))
            first += width
        block = item.segments[0][1][0][0].shape[2:]
        shapes.append(shaped((number, first) + block, BF))
    tied = list(tie(*arrays, *tokens))[: len(arrays)] if tokens else arrays
    buffers = sum(len(entry[4]) for entry in plan)
    size = (max(entry[1] for entry in plan), max(entry[3] for entry in plan)) + shapes[0].shape[2:]
    moved = sum(entry[1] * entry[3] * (len(entry[4]) + 1) for entry in plan) * 16384
    sends = pl.pallas_call(
        functools.partial(combine_kernel, plan, len(tied)),
        out_shape=shapes,
        in_specs=[ANY] * len(tied),
        out_specs=[VMEM] * len(shapes),
        scratch_shapes=[pltpu.VMEM((buffers,) + size, BF), pltpu.SemaphoreType.DMA((buffers,))],
        cost_estimate=pl.CostEstimate(flops=0, bytes_accessed=moved, transcendentals=0),
        compiler_params=pltpu.CompilerParams(vmem_limit_bytes=VMEM_BYTES // 3),
    )(*tied)
    for item, send in zip(sums, sends):
        item.send = send


def tie_sums(array, *sums):
    tied = tie(array, *[item.send for item in sums])
    for item, send in zip(sums, tied[1:]):
        item.send = send
    return tied[0]


def adam_update(weight, gradient, first, second, rate, decay):
    first_new = BETA_ONE * first + (1.0 - BETA_ONE) * gradient
    second_new = BETA_TWO * second + (1.0 - BETA_TWO) * gradient * gradient
    first_hat = first_new / (1.0 - BETA_ONE**STEP)
    second_hat = second_new / (1.0 - BETA_TWO**STEP)
    weight_new = weight - rate * (first_hat / (jnp.sqrt(second_hat) + EPS_ADAM) + decay * weight)
    return (weight_new, first_new, second_new, weight_new.astype(BF))


def gather_small(vectors, hidden):
    whole = lax.all_gather(vectors.astype(BF), AXES, axis=1, tiled=True)
    deep = lax.all_gather(hidden.astype(BF), AXES, axis=1, tiled=True)
    whole = jnp.pad(whole, ((0, HIDDEN_ROW - whole.shape[0]), (0, 0)))
    return jnp.concatenate([whole, deep.reshape(-1, whole.shape[1])], axis=0).astype(F32)


def scatter_small(grads, vectors, hidden, place, count):
    whole = lax.psum(small_rows(*grads), AXES)
    rows, lanes = vectors.shape
    first = lax.dynamic_slice_in_dim(whole[:rows], place * lanes, lanes, axis=1)
    layers, lanes = hidden.shape
    deep = whole[HIDDEN_ROW:].reshape(layers, -1)
    return first, lax.dynamic_slice_in_dim(deep, place * lanes, lanes, axis=1)


def gather_whole(attention, up, down):
    width = attention.shape[2]
    number = width // BLOCK
    square = lax.all_gather(attention, AXES, axis=1, tiled=True)
    square = square.reshape(-1, QUAD, number, BLOCK, width).transpose(0, 2, 1, 3, 4)
    tall = lax.all_gather(up, AXES, axis=1, tiled=True)
    tall = tall.reshape(2, number, BLOCK, QUAD, width).transpose(0, 1, 3, 2, 4)
    deep = lax.all_gather(down, AXES, axis=1, tiled=True).reshape(2, number, QUAD, BLOCK, width)
    half = number // 2
    quads = [square[0], tall[0], deep[0], square[1], square[2], tall[1], deep[1]]
    return [(quad[:half], quad[half:]) for quad in quads]


def scatter_whole(quads):
    joined = [jnp.concatenate(pair, axis=0).astype(F32) for pair in quads]
    number, _, _, width = joined[0].shape
    square = jnp.stack([joined[0], joined[3], joined[4]])
    square = square.transpose(0, 2, 1, 3, 4).reshape(3 * QUAD, width, width)
    tall = jnp.stack([joined[1], joined[5]]).transpose(0, 1, 3, 2, 4)
    tall = tall.reshape(2, width, QUAD * width)
    deep = jnp.stack([joined[2], joined[6]]).reshape(2, QUAD * width, width)
    return [
        lax.psum_scatter(part, AXES, scatter_dimension=1, tiled=True)
        for part in (square, tall, deep)
    ]


def direct_step(pairs, source, target, grad, masters, firsts, seconds, axis_sizes):
    net = Direct(axis_sizes)
    source_pair, target_pair, cross_pair = pairs
    a, b = net.table("a"), net.table("b")
    cut = QUAD // 2
    at = (net.place % (net.count * LANES // source.shape[1])).astype(jnp.int32).reshape(1)

    one, two, rest = first_arrays(at, *masters)
    one, two = grown((one, two), tie(net.arrive(one, "a", 0), net.arrive(two, "a", 0)))
    rest, two = tie(rest, two)
    rest_more = net.arrive(rest, "a", 0)
    one, two = grown((one, two), tie(net.arrive(one, "a", 1), net.arrive(two, "a", 1)))
    streams = [one[:, :cut], one[:, cut:], two[:, :QUAD], two[:, QUAD:]]
    names = ("a", "b", "a", "b")
    more = [net.arrive(array, name, 2) for array, name in zip(streams, names)]
    left, right, up_one, down_one, rest = grown(streams + [rest], tie(*more, rest_more))
    more = [net.arrive(left, "a", 3), net.arrive(right, "b", 3), net.arrive(rest, "a", 1)]
    left, right, rest = grown((left, right, rest), tie(*more))
    left = net.finish(left, "a")
    right = net.finish(right, "b")
    self_w, up_two = rest[:, :QUAD], rest[:, QUAD : 2 * QUAD]
    cross_w, down_two = rest[:, 2 * QUAD : 3 * QUAD], rest[:, 3 * QUAD :]
    streams = [up_one, down_one, self_w, cross_w]
    streams = list(tie(source, *streams))
    source = streams.pop(0)
    more = [net.arrive(*item) for item in zip(streams, names, (3, 3, 2, 2))]
    enc_attend_w = [(a, left, 0, cut), (b, right, 0, cut)]
    enc_kept = attend_forward(source_pair, None, 0, source, None, enc_attend_w, False)
    enc_mid, small = enc_kept[0], enc_kept[8]
    up_one, down_one = grown((up_one, down_one), tie(*more[:2], small)[:2])
    self_w, cross_w = grown((self_w, cross_w), tie(*more[2:], up_one, down_one)[:2])
    up_one = net.finish(up_one, "a")
    down_one = net.finish(down_one, "b")
    streams = [self_w, cross_w, up_two, down_two]
    streams = list(tie(enc_mid, *streams))
    enc_mid = streams.pop(0)
    self_w, cross_w, up_two, down_two = streams
    more = [net.arrive(*item) for item in zip(streams, names, (3, 3, 2, 2))]
    enc_feed_w = [(a, up_one, 0, QUAD), (b, down_one, 0, QUAD)]
    enc_feed_kept = feed_forward(small, 5, HIDDEN_ROW, enc_mid, enc_feed_w)
    memory = enc_feed_kept[0]
    self_w, cross_w = grown((self_w, cross_w), tie(*more[:2], memory)[:2])
    up_two, down_two = grown((up_two, down_two), tie(*more[2:], self_w, cross_w)[:2])
    self_w = net.finish(self_w, "a")
    cross_w = net.finish(cross_w, "b")
    target, up_two, down_two = tie(target, up_two, down_two)
    more = [net.arrive(up_two, "a", 3), net.arrive(down_two, "b", 3)]
    self_w = [(a, self_w, 0, QUAD)]
    cross_w = [(b, cross_w, 0, QUAD)]
    self_kept = attend_forward(target_pair, small, 8, target, None, self_w, True)
    dec_one = self_kept[0]
    cross_kept = attend_forward(cross_pair, small, 13, dec_one, memory, cross_w, False)
    dec_two = cross_kept[0]
    up_two, down_two = grown((up_two, down_two), tie(*more, dec_two)[:2])
    dec_feed_w = [(a, net.finish(up_two, "a"), 0, QUAD), (b, net.finish(down_two, "b"), 0, QUAD)]
    result, two_grad, dec_feed_small, feed_two = feed_both(
        (a, b), small, 18, HIDDEN_ROW + QUAD, dec_two, grad, dec_feed_w
    )

    names = names[:2]
    feed_two = sum_of(net, "a", *feed_two, (QUAD, QUAD)).step()
    one_grad, memory_grad, cross_small, cross_q = attend_backward(
        (a, b), cross_pair, small, 13, two_grad, cross_kept, dec_one, memory, cross_w, False, None
    )
    cross_s = sum_of(net, "a", *cross_q, (cut, cut))
    feed_two = feed_two.split(names)
    settle(feed_two, cross_small)
    memory_grad = tie_sums(memory_grad, *feed_two, cross_s)
    step_all(feed_two + [cross_s])
    mid_grad, enc_feed_small, feed_one = feed_backward(
        (a, b), small, 5, memory_grad, enc_feed_kept, enc_mid, enc_feed_w
    )
    feed_one = sum_of(net, "a", *feed_one, (QUAD, QUAD))
    cross_s = cross_s.split(names)
    settle(feed_two + cross_s, enc_feed_small)
    one_grad = tie_sums(one_grad, *feed_two, *cross_s, feed_one)
    step_all(feed_two + cross_s + [feed_one])
    target_grad, _, self_small, self_q = attend_backward(
        (a, b), target_pair, small, 8, one_grad, self_kept, target, None, self_w, True, None
    )
    self_s = sum_of(net, "a", *self_q, (cut, cut))
    feed_one = feed_one.split(names)
    settle(cross_s + feed_one, self_small, *[array for item in feed_two for array in item.last()])
    mid_grad = tie_sums(mid_grad, *cross_s, *feed_one, self_s)
    step_all(cross_s + feed_one + [self_s])
    others = (enc_feed_small, self_small, cross_small, dec_feed_small)
    source_grad, _, _, enc_q = attend_backward(
        (a, b), source_pair, small, 0, mid_grad, enc_kept, source, None, enc_attend_w, False, others
    )
    enc_s = sum_of(net, "a", *enc_q, (cut, cut + 1))
    self_s = self_s.split(names)
    settle(self_s + feed_one, source_grad, *[array for item in cross_s for array in item.last()])
    enc_s.send = tie_sums(enc_s.send, *self_s, *feed_one)
    step_all([enc_s] + self_s + feed_one)
    enc_s = enc_s.split(names)
    decoder = joined(feed_two + cross_s)
    settle(enc_s + self_s + [decoder], *[array for item in feed_one for array in item.last()])
    step_all(enc_s + self_s + [decoder])
    encoder = joined(self_s + feed_one)
    settle(enc_s + [encoder, decoder])
    step_all(enc_s + [encoder, decoder])
    ending = joined(enc_s)
    settle([ending, encoder], *decoder.last())
    step_all([ending, encoder])
    settle([ending], *encoder.last())
    ending.step()

    square = [(0, index) for index in range(3 * QUAD)]
    tall, deep = [], []
    for layer in range(2):
        for index in range(QUAD):
            lanes = slice(index * source.shape[1], (index + 1) * source.shape[1])
            tall.append((1, (layer, slice(None), lanes)))
            deep.append((2, (layer, slice(index * BLOCK, (index + 1) * BLOCK))))
    targets = [square[:cut], square[cut:QUAD] + [(3, None)]]
    targets += [square[QUAD : QUAD + cut], square[QUAD + cut : 2 * QUAD], tall[:QUAD], deep[:QUAD]]
    targets += [tall[QUAD:], deep[QUAD:]]
    targets += [square[2 * QUAD : 2 * QUAD + cut], square[2 * QUAD + cut :]]
    segments = ending.segments + encoder.segments + decoder.segments
    segments = [segment + (target,) for segment, target in zip(segments, targets)]
    updated = last_update(at, segments, masters, firsts, seconds)
    return (memory, result, source_grad, target_grad), updated


def whole_step(pairs, source, target, grad, masters, firsts, seconds, axis_sizes):
    attention, up, down = [master.astype(BF) for master in masters[:3]]
    vectors, hidden = masters[3:]
    source_pair, target_pair, cross_pair = pairs
    small = gather_small(vectors, hidden)
    quads = gather_whole(attention, up, down)
    table = jnp.arange(source.shape[1] // BLOCK, dtype=jnp.int32)
    two = (table, table)
    parts = [(table, list(quad), 0, QUAD) for quad in quads]
    enc_kept = attend_forward(source_pair, small, 0, source, None, parts[:1], False)
    enc_mid = enc_kept[0]
    enc_feed_kept = feed_forward(small, 5, HIDDEN_ROW, enc_mid, parts[1:3])
    memory = enc_feed_kept[0]
    self_kept = attend_forward(target_pair, small, 8, target, None, parts[3:4], True)
    dec_one = self_kept[0]
    cross_kept = attend_forward(cross_pair, small, 13, dec_one, memory, parts[4:5], False)
    dec_two = cross_kept[0]
    result, two_grad, dec_feed_small, feed_two = feed_both(
        two, small, 18, HIDDEN_ROW + QUAD, dec_two, grad, parts[5:7]
    )
    one_grad, memory_grad, cross_small, cross_q = attend_backward(
        two, cross_pair, small, 13, two_grad, cross_kept, dec_one, memory, parts[4:5], False, None
    )
    target_grad, _, self_small, self_q = attend_backward(
        two, target_pair, small, 8, one_grad, self_kept, target, None, parts[3:4], True, None
    )
    mid_grad, enc_feed_small, feed_one = feed_backward(
        two, small, 5, memory_grad, enc_feed_kept, enc_mid, parts[1:3]
    )
    source_grad, _, enc_small, enc_q = attend_backward(
        two, source_pair, small, 0, mid_grad, enc_kept, source, None, parts[:1], False, None
    )
    quads = [enc_q]
    quads += [[half[:, low : low + QUAD] for half in feed_one] for low in (0, QUAD)]
    quads += [self_q, cross_q]
    quads += [[half[:, low : low + QUAD] for half in feed_two] for low in (0, QUAD)]
    smalls = (enc_small, enc_feed_small, self_small, cross_small, dec_feed_small)
    count = axis_sizes[0] * axis_sizes[1]
    shares = scatter_small(smalls, vectors, hidden, lax.axis_index(AXES), count)
    grads = tuple(scatter_whole(quads)) + shares
    updated = [
        adam_update(
            masters[slot], grads[slot], firsts[slot], seconds[slot], RATES[slot], DECAYS[slot]
        )
        for slot in range(5)
    ]
    flat = [updated[slot][kind] for kind in range(4) for slot in range(5)]
    return (memory, result, source_grad, target_grad), flat


def per_device(
    axis_sizes,
    source_tokens,
    target_tokens,
    source_segments,
    target_segments,
    output_grad,
    attention_weight,
    up_weight,
    down_weight,
    vectors,
    hidden_bias,
    *moments,
):
    masters = (attention_weight, up_weight, down_weight, vectors, hidden_bias)
    firsts = moments[:5]
    seconds = moments[5:]
    width = source_tokens.shape[2]
    pairs = (
        (source_segments, source_segments),
        (target_segments, target_segments),
        (target_segments, source_segments),
    )
    direct = axis_sizes[0] * axis_sizes[1] * BLOCK == width
    tokens, updated = (direct_step if direct else whole_step)(
        pairs,
        source_tokens[0],
        target_tokens[0],
        output_grad[0],
        masters,
        firsts,
        seconds,
        axis_sizes,
    )
    return tuple(array[None] for array in tokens) + tuple(updated)


def solution(mesh):
    rows = P(AXES, None, None)
    line = P(AXES, None)
    matrix = P(None, AXES, None)
    vector = P(None, AXES)
    state = (matrix, matrix, matrix, vector, vector)
    return jax.shard_map(
        functools.partial(per_device, (mesh.shape["dp"], mesh.shape["fsdp"])),
        mesh=mesh,
        in_specs=(rows, rows, line, line, rows) + state * 3,
        out_specs=(rows,) * 4 + state * 4,
        check_vma=False,
    )
```

```python
import functools

import jax
import jax.numpy as jnp
from jax import lax
from jax.experimental import pallas as pl
from jax.experimental.pallas import tpu as pltpu
from jax.sharding import PartitionSpec as P

HEADS = 8
STEP = 10
EPS_NORM = 1e-05
EPS_ADAM = 1e-08
BETA_ONE = 0.9
BETA_TWO = 0.999
LOWEST = -1e30
RATES = (0.05, 0.05, 0.05, 0.3, 0.3)
DECAYS = (0.01, 0.01, 0.01, 0.0, 0.0)
AXES = ("dp", "fsdp")
QUAD = 4
BLOCK = 16
LANES = 128
SMALL_ROWS = 32
VMEM_BYTES = 60 * 1024 * 1024
HIDDEN_ROW = 24
BF = jnp.bfloat16
F32 = jnp.float32
VMEM = pl.BlockSpec(memory_space=pltpu.VMEM)
SMEM = pl.BlockSpec(memory_space=pltpu.SMEM)
ANY = pl.BlockSpec(memory_space=pl.ANY)
ROOT_TWO_PI = 0.7978845608028654
CUBIC = 0.044715


def dot(left, right):
    return jnp.dot(left, right, preferred_element_type=F32)


def dot_nt(left, right):
    return lax.dot_general(left, right, (((1,), (1,)), ((), ())), preferred_element_type=F32)


def load_start(part, place, sems):
    table, arrays, low, number = part
    at = 0
    for slot, array in enumerate(arrays):
        for index in range(array.shape[0]):
            source = array.at[index, low : low + number]
            pltpu.make_async_copy(source, place(table[at]), sems.at[slot]).start()
            at += 1


def load_wait(part, sems):
    table, arrays, low, number = part
    for slot, array in enumerate(arrays):
        whole = array.at[:, low : low + number]
        pltpu.make_async_copy(whole, whole, sems.at[slot]).wait()


def store_start(part, place, sems):
    table, arrays, low, number = part
    half = arrays[0].shape[0]
    for index in range(half):
        for slot in (1, 0):
            target = arrays[slot].at[index, low : low + number]
            source = place(table[slot * half + index])
            pltpu.make_async_copy(source, target, sems.at[slot]).start()


def row_place(scratch, low, high):
    def place(block):
        start = pl.multiple_of(block * BLOCK, BLOCK)
        return scratch.at[low:high, pl.ds(start, BLOCK), :]

    return place


def block_place(scratch):
    return lambda block: scratch.at[block]


def norm_forward(pre, gain, shift, out_ref, hat_ref, rstd_ref):
    mean = jnp.mean(pre, axis=-1, keepdims=True)
    centred = pre - mean
    spread = jnp.mean(centred * centred, axis=-1, keepdims=True)
    rstd = lax.rsqrt(spread + EPS_NORM)
    hat = centred * rstd
    hat_ref[...] = hat
    rstd_ref[...] = jnp.broadcast_to(rstd, rstd_ref.shape)
    out_ref[...] = hat * gain + shift


def norm_backward(grad, hat, rstd, gain):
    gain_grad = jnp.sum(grad * hat, axis=0, keepdims=True)
    shift_grad = jnp.sum(grad, axis=0, keepdims=True)
    scaled = grad * gain
    one = jnp.mean(scaled, axis=-1, keepdims=True)
    two = jnp.mean(scaled * hat, axis=-1, keepdims=True)
    return rstd * (scaled - one - hat * two), gain_grad, shift_grad


def lane_mask(rows):
    return lax.broadcasted_iota(jnp.int32, (rows, LANES), 1) < LANES // 2


def stacked_pair(block):
    first = lane_mask(block.shape[0])
    zero = jnp.zeros_like(block)
    return jnp.concatenate([jnp.where(first, block, zero), jnp.where(first, zero, block)], axis=0)


def merged_pair(stacked):
    rows = stacked.shape[0] // 2
    return jnp.where(lane_mask(rows), stacked[:rows], stacked[rows:])


def mask_fill(bias_ref, column_seg, row_seg, causal, transposed):
    length = bias_ref.shape[0]
    column = jnp.broadcast_to(column_seg, (LANES, length)).T
    for at in range(0, length, LANES):
        same = column == row_seg[:, at : at + LANES]
        if causal:
            down = lax.broadcasted_iota(jnp.int32, (length, LANES), 0)
            along = lax.broadcasted_iota(jnp.int32, (length, LANES), 1) + at
            order = (down <= along) if transposed else (along <= down)
            same = same & order
        bias_ref[:, at : at + LANES] = jnp.where(same, 0.0, LOWEST)


def take_parts(refs, layout, tables):
    parts = []
    for slot, (arrays, low, number) in enumerate(layout):
        parts.append((tables[slot], [refs.pop(0) for _ in range(arrays)], low, number))
    return parts


def small_part(part):
    table, arrays, low, number = part
    return table, arrays, low + number, 1


def small_join(blocks_ref):
    count = blocks_ref.shape[0]
    groups = blocks_ref.shape[3] // LANES
    per = count // groups
    vectors = []
    hidden = [[], []]
    for group in range(groups):
        total = blocks_ref[group * per, 0, :8].astype(F32)
        for at in range(group * per + 1, (group + 1) * per):
            total = total + blocks_ref[at, 0, :8].astype(F32)
        columns = [total[:, at : at + LANES] for at in range(0, 4 * LANES, LANES)]
        vectors.append(jnp.concatenate(columns[:3], axis=0))
        for layer in range(2):
            rows = [columns[3][4 * layer + at : 4 * layer + at + 1] for at in range(4)]
            hidden[layer].append(jnp.concatenate(rows, axis=1))
    return jnp.concatenate([jnp.concatenate(vectors, axis=1)] + hidden[0] + hidden[1], axis=0)


def small_split(whole, group):
    lanes = slice(group * LANES, (group + 1) * LANES)
    columns = [whole[at : at + 8, lanes] for at in (0, 8, 16)]
    rows = []
    for layer in range(2):
        row = whole[24 + 4 * layer + group : 25 + 4 * layer + group]
        rows += [row[:, at : at + LANES] for at in range(0, 4 * LANES, LANES)]
    columns.append(jnp.concatenate(rows, axis=0))
    block = jnp.concatenate(columns, axis=1)
    return jnp.concatenate([block, jnp.zeros_like(block)], axis=0).astype(BF)


def attend_forward_kernel(layout, cross, causal, base, joins, *refs):
    refs = list(refs)
    tables = [refs.pop(0) for _ in layout]
    query_seg = refs.pop(0)
    key_seg = refs.pop(0)
    small = None if joins else refs.pop(0)
    rows_ref = refs.pop(0)
    memory_ref = refs.pop(0) if cross else None
    parts = take_parts(refs, layout, tables)
    out_ref, hat_ref, rstd_ref, q_ref, k_ref, v_ref, o_ref, lse_ref = [refs.pop(0) for _ in range(8)]
    if joins:
        small = refs.pop(0)
        blocks_ref = refs.pop()
        extra = small_part(parts[-1])
    w_ref, bias_ref, sems = refs
    first = 0
    if joins:
        load_start(extra, lambda block: blocks_ref.at[block], sems.at[len(parts)])
    for slot, part in enumerate(parts):
        load_start(part, row_place(w_ref, first, first + part[3]), sems.at[slot])
        first += part[3]
    length, width = rows_ref.shape
    mask_fill(bias_ref, query_seg[...], key_seg[...], causal, False)
    rows = rows_ref[...].astype(BF)
    keys = memory_ref[...].astype(BF) if cross else rows
    if joins:
        load_wait(extra, sems.at[len(parts)])
        small[...] = small_join(blocks_ref)
    for slot, part in enumerate(parts):
        load_wait(part, sems.at[slot])
    scale = (width // HEADS) ** (-0.5)
    q_ref[...] = (dot(rows, w_ref[0]) + small[base : base + 1]).astype(BF) * jnp.asarray(scale, BF)
    k_ref[...] = dot(keys, w_ref[1]).astype(BF)
    v_ref[...] = (dot(keys, w_ref[2]) + small[base + 1 : base + 2]).astype(BF)
    lane = lax.broadcasted_iota(jnp.int32, (LANES, LANES), 1)
    for at in range(0, length, LANES):
        reach = at + LANES if causal else length
        logs = jnp.zeros((LANES, LANES), F32)
        for pair in range(HEADS // 2):
            lanes = slice(pair * LANES, (pair + 1) * LANES)
            stacked = stacked_pair(q_ref[at : at + LANES, lanes])
            scores = dot_nt(stacked, k_ref[:reach, lanes])
            bias = bias_ref[at : at + LANES, :reach]
            scores = scores + jnp.concatenate([bias, bias], axis=0)
            largest = jnp.max(scores, axis=-1, keepdims=True)
            exponent = jnp.exp(scores - largest).astype(BF)
            values = jnp.concatenate([v_ref[:reach, lanes], jnp.ones((reach, LANES), BF)], axis=1)
            mixed = dot(exponent, values)
            total = mixed[:, LANES:]
            o_ref[at : at + LANES, lanes] = merged_pair(mixed[:, :LANES] / total).astype(BF)
            log_total = largest + jnp.log(total)
            logs = jnp.where(lane == 2 * pair, log_total[:LANES], logs)
            logs = jnp.where(lane == 2 * pair + 1, log_total[LANES:], logs)
        lse_ref[:, at : at + LANES] = logs.T[:HEADS]
    attended = dot(o_ref[...], w_ref[3]) + small[base + 2 : base + 3]
    pre = rows_ref[...].astype(F32) + attended
    norm_forward(pre, small[base + 3 : base + 4], small[base + 4 : base + 5], out_ref, hat_ref, rstd_ref)


def attend_backward_kernel(layout, cross, causal, base, splits, *refs):
    refs = list(refs)
    tables = [refs.pop(0) for _ in layout]
    out_tables = [refs.pop(0), refs.pop(0)]
    query_seg = refs.pop(0)
    key_seg = refs.pop(0)
    small = refs.pop(0)
    grad_ref = refs.pop(0)
    hat_ref, rstd_ref = refs.pop(0), refs.pop(0)
    rows_ref = refs.pop(0)
    memory_ref = refs.pop(0) if cross else None
    q_ref, k_ref, v_ref, o_ref, lse_ref = [refs.pop(0) for _ in range(5)]
    others = [refs.pop(0) for _ in range(4)] if splits else None
    parts = take_parts(refs, layout, tables)
    rows_out = refs.pop(0)
    memory_out = refs.pop(0) if cross else None
    small_out = None if splits else refs.pop(0)
    targets = [refs.pop(0), refs.pop(0)]
    outs = []
    for slot, table in enumerate(out_tables):
        outs.append((table, targets, slot * QUAD // 2, QUAD // 2))
    blocks_ref = refs.pop() if splits else None
    w_ref, dw_ref, bias_ref, dout_ref, dq_t_ref, dk_ref, dv_ref, kt_ref, sems = refs
    first = 0
    for slot, part in enumerate(parts):
        load_start(part, row_place(w_ref, first, first + part[3]), sems.at[slot])
        first += part[3]
    length, width = rows_ref.shape
    head = width // HEADS
    scale = head ** (-0.5)
    mask_fill(bias_ref, key_seg[...], query_seg[...], causal, True)
    kt_ref[...] = k_ref[...].T
    pre_grad, gain_grad, shift_grad = norm_backward(
        grad_ref[...], hat_ref[...], rstd_ref[:, :1], small[base + 3 : base + 4]
    )
    rows_out[...] = pre_grad
    low = pre_grad.astype(BF)
    for slot, part in enumerate(parts):
        load_wait(part, sems.at[slot])
    dout_ref[...] = dot_nt(low, w_ref[3]).astype(BF)
    dw_ref[3] = dot(o_ref[...].T, low).astype(BF)
    out_bias = jnp.sum(low.astype(F32), axis=0, keepdims=True)
    product = dout_ref[...].astype(F32) * o_ref[...].astype(F32)
    high = product.astype(BF)
    rest = (product - high.astype(F32)).astype(BF)
    picker = lax.broadcasted_iota(jnp.int32, (BLOCK, width), 1) // head
    picker = (picker == lax.broadcasted_iota(jnp.int32, (BLOCK, width), 0)).astype(BF)
    row_dots = dot_nt(picker, high) + dot_nt(picker, rest)
    for pair in range(HEADS // 2):
        lanes = slice(pair * LANES, (pair + 1) * LANES)
        for at in range(0, length, LANES):
            begin = at if causal else 0
            query = q_ref[begin:, lanes]
            dout = dout_ref[begin:, lanes]
            scores = dot_nt(stacked_pair(k_ref[at : at + LANES, lanes]), query)
            prob_grad = dot_nt(stacked_pair(v_ref[at : at + LANES, lanes]), dout)
            bias = bias_ref[at : at + LANES, begin:]
            probs = []
            score_grads = []
            for part in range(2):
                which = 2 * pair + part
                half = slice(part * LANES, (part + 1) * LANES)
                prob = jnp.exp(scores[half] + (bias - lse_ref[which : which + 1, begin:]))
                probs.append(prob.astype(BF))
                row_dot = row_dots[which : which + 1, begin:]
                score_grads.append((prob * (prob_grad[half] - row_dot)).astype(BF))
                at_t = pair * LANES + part * head
                back = dot(kt_ref[at_t : at_t + head, at : at + LANES], score_grads[part])
                if at == 0:
                    dq_t_ref[at_t : at_t + head, :] = back
                else:
                    dq_t_ref[at_t : at_t + head, begin:] += back
            value_back = dot(jnp.concatenate(probs, axis=0), dout)
            dv_ref[at : at + LANES, lanes] = merged_pair(value_back).astype(BF)
            key_back = dot(jnp.concatenate(score_grads, axis=0), query)
            dk_ref[at : at + LANES, lanes] = merged_pair(key_back).astype(BF)
    query_grad = (dq_t_ref[...] * scale).T.astype(BF)
    key_grad = dk_ref[...]
    value_grad = dv_ref[...]
    turned = rows_ref[...].astype(BF).T
    dw_ref[0] = dot(turned, query_grad).astype(BF)
    if cross:
        turned = memory_ref[...].astype(BF).T
    dw_ref[1] = dot(turned, key_grad).astype(BF)
    dw_ref[2] = dot(turned, value_grad).astype(BF)
    first = 0
    for slot, part in enumerate(outs):
        store_start(part, row_place(dw_ref, first, first + part[3]), sems.at[slot])
        first += part[3]
    rows_back = rows_out[...] + dot_nt(query_grad, w_ref[0])
    memory_back = dot_nt(key_grad, w_ref[1]) + dot_nt(value_grad, w_ref[2])
    if cross:
        rows_out[...] = rows_back
        memory_out[...] = memory_back
    else:
        rows_out[...] = rows_back + memory_back
    query_bias = jnp.sum(query_grad.astype(F32), axis=0, keepdims=True)
    value_bias = jnp.sum(value_grad.astype(F32), axis=0, keepdims=True)
    spare = jnp.zeros((3, width), F32)
    own = jnp.concatenate(
        [query_bias, value_bias, out_bias, gain_grad, shift_grad, spare], axis=0
    )
    if splits:
        enc_feed, self_attend, cross_attend, dec_feed = [other[...] for other in others]
        whole = small_rows(own, enc_feed, self_attend, cross_attend, dec_feed)
        groups = blocks_ref.shape[0]
        for group in range(groups):
            blocks_ref[group, 0] = small_split(whole, group)
        extra = small_part(outs[-1])
        per = 2 * extra[1][0].shape[0] // groups
        store_start(extra, lambda block: blocks_ref.at[block // per], sems.at[2])
        load_wait(extra, sems.at[2])
    else:
        small_out[...] = own
    for slot, part in enumerate(outs):
        load_wait(part, sems.at[slot])


def small_rows(enc_attend, enc_feed, self_attend, cross_attend, dec_feed):
    return jnp.concatenate(
        [
            enc_attend[:5],
            enc_feed[:3],
            self_attend[:5],
            cross_attend[:5],
            dec_feed[:3],
            dec_feed[7:],
            dec_feed[7:],
            dec_feed[7:],
            enc_feed[3:7],
            dec_feed[3:7],
        ],
        axis=0,
    )


def gelu_parts(pre):
    square = pre * pre
    curve = jnp.tanh(ROOT_TWO_PI * pre * (1.0 + CUBIC * square))
    half = 0.5 * pre
    rise = 0.5 + 0.5 * curve
    bend = ROOT_TWO_PI * (1.0 + 3.0 * CUBIC * square)
    return pre * rise, rise + half * (1.0 - curve * curve) * bend


def chunk_of(ref, index):
    number = ref.shape[0] // QUAD
    part = ref[index * number : (index + 1) * number]
    return part.reshape(number * ref.shape[1] * ref.shape[2], ref.shape[3])


def feed_forward_steps(small, base, hidden_at, rows_ref, up_ref, down_ref, active_ref, slope_ref):
    rows = rows_ref[...].astype(BF)
    total = rows_ref[...] + small[base : base + 1]
    for index in range(QUAD):
        at = hidden_at + index
        pre = dot(rows, up_ref[index]) + small[at : at + 1]
        active, slope = gelu_parts(pre)
        active = active.astype(BF)
        active_ref[index] = active
        slope_ref[index] = slope
        total = total + dot(active, chunk_of(down_ref, index))
    return total


def feed_backward_steps(
    pre_grad, rows_ref, up_ref, down_ref, active_ref, slope_ref, dup_ref, ddown_ref, rows_out
):
    low = pre_grad.astype(BF)
    turned = rows_ref[...].astype(BF).T
    total = pre_grad
    hidden_grads = []
    number = ddown_ref.shape[0] // QUAD
    for index in range(QUAD):
        down_grad = dot(active_ref[index].T, low).astype(BF)
        ddown_ref[index * number : (index + 1) * number] = down_grad.reshape(
            (number,) + ddown_ref.shape[1:]
        )
        back = dot_nt(low, chunk_of(down_ref, index))
        hidden = (back * slope_ref[index]).astype(BF)
        hidden_grads.append(jnp.sum(hidden.astype(F32), axis=0, keepdims=True))
        dup_ref[index] = dot(turned, hidden).astype(BF)
        total = total + dot_nt(hidden, up_ref[index])
    rows_out[...] = total
    out_bias = jnp.sum(low.astype(F32), axis=0, keepdims=True)
    return out_bias, hidden_grads


def load_feed(parts, up_ref, down_ref, sems):
    load_start(parts[0], row_place(up_ref, 0, QUAD), sems.at[0])
    load_start(parts[1], block_place(down_ref), sems.at[1])


def store_feed(outs, dup_ref, ddown_ref, sems):
    store_start(outs[1], block_place(ddown_ref), sems.at[1])
    store_start(outs[0], row_place(dup_ref, 0, QUAD), sems.at[0])


def wait_feed(parts, sems):
    for slot, part in enumerate(parts):
        load_wait(part, sems.at[slot])


def feed_outs(refs, tables):
    arrays = [refs.pop(0), refs.pop(0)]
    return [(tables[slot], arrays, slot * QUAD, QUAD) for slot in range(2)]


def feed_small(out_bias, gain_grad, shift_grad, hidden_grads):
    spare = jnp.zeros_like(out_bias)
    return jnp.concatenate([out_bias, gain_grad, shift_grad] + hidden_grads + [spare], axis=0)


def feed_forward_kernel(layout, base, hidden_at, *refs):
    refs = list(refs)
    tables = [refs.pop(0), refs.pop(0)]
    small, rows_ref = refs.pop(0), refs.pop(0)
    parts = take_parts(refs, layout, tables)
    out_ref, hat_ref, rstd_ref, active_ref, slope_ref, up_ref, down_ref, sems = refs
    load_feed(parts, up_ref, down_ref, sems)
    wait_feed(parts, sems)
    pre = feed_forward_steps(
        small, base, hidden_at, rows_ref, up_ref, down_ref, active_ref, slope_ref
    )
    norm_forward(pre, small[base + 1 : base + 2], small[base + 2 : base + 3], out_ref, hat_ref, rstd_ref)


def feed_backward_kernel(layout, base, *refs):
    refs = list(refs)
    tables = [refs.pop(0), refs.pop(0)]
    out_tables = [refs.pop(0), refs.pop(0)]
    small, grad_ref, hat_ref, rstd_ref, rows_ref = [refs.pop(0) for _ in range(5)]
    active_ref, slope_ref = refs.pop(0), refs.pop(0)
    parts = take_parts(refs, layout, tables)
    rows_out, small_out = refs.pop(0), refs.pop(0)
    outs = feed_outs(refs, out_tables)
    up_ref, down_ref, dup_ref, ddown_ref, sems, out_sems = refs
    load_feed(parts, up_ref, down_ref, sems)
    pre_grad, gain_grad, shift_grad = norm_backward(
        grad_ref[...], hat_ref[...], rstd_ref[:, :1], small[base + 1 : base + 2]
    )
    wait_feed(parts, sems)
    out_bias, hidden_grads = feed_backward_steps(
        pre_grad, rows_ref, up_ref, down_ref, active_ref, slope_ref, dup_ref, ddown_ref, rows_out
    )
    store_feed(outs, dup_ref, ddown_ref, out_sems)
    small_out[...] = feed_small(out_bias, gain_grad, shift_grad, hidden_grads)
    wait_feed(outs, out_sems)


def feed_both_kernel(layout, base, hidden_at, *refs):
    refs = list(refs)
    tables = [refs.pop(0), refs.pop(0)]
    out_tables = [refs.pop(0), refs.pop(0)]
    small, rows_ref, grad_ref = [refs.pop(0) for _ in range(3)]
    parts = take_parts(refs, layout, tables)
    out_ref, rows_out, small_out = [refs.pop(0) for _ in range(3)]
    outs = feed_outs(refs, out_tables)
    up_ref, down_ref, dup_ref, ddown_ref, active_ref, slope_ref, hat_ref, rstd_ref = refs[:8]
    sems, out_sems = refs[8:]
    load_feed(parts, up_ref, down_ref, sems)
    wait_feed(parts, sems)
    pre = feed_forward_steps(
        small, base, hidden_at, rows_ref, up_ref, down_ref, active_ref, slope_ref
    )
    gain = small[base + 1 : base + 2]
    norm_forward(pre, gain, small[base + 2 : base + 3], out_ref, hat_ref, rstd_ref)
    pre_grad, gain_grad, shift_grad = norm_backward(
        grad_ref[...].astype(F32), hat_ref[...], rstd_ref[:, :1], gain
    )
    out_bias, hidden_grads = feed_backward_steps(
        pre_grad, rows_ref, up_ref, down_ref, active_ref, slope_ref, dup_ref, ddown_ref, rows_out
    )
    store_feed(outs, dup_ref, ddown_ref, out_sems)
    small_out[...] = feed_small(out_bias, gain_grad, shift_grad, hidden_grads)
    wait_feed(outs, out_sems)


def shaped(shape, dtype=F32):
    return jax.ShapeDtypeStruct(shape, dtype)


def call(kernel, ins, specs, outs, out_specs, scratch, flops, moved):
    return pl.pallas_call(
        kernel,
        out_shape=outs,
        in_specs=specs,
        out_specs=out_specs,
        scratch_shapes=scratch,
        cost_estimate=pl.CostEstimate(flops=flops, bytes_accessed=moved, transcendentals=0),
        compiler_params=pltpu.CompilerParams(vmem_limit_bytes=VMEM_BYTES),
    )(*ins)


def layout_of(parts):
    return [(len(arrays), low, number) for _, arrays, low, number in parts]


def arrays_of(parts):
    return [array for part in parts for array in part[1]]


def most(parts):
    return max(len(part[1]) for part in parts)


def halves(width, number):
    return [shaped((width // BLOCK // 2, number, BLOCK, width), BF)] * 2


def attend_forward(segments, small, base, rows, memory, parts, causal):
    length, width = rows.shape
    cross = memory is not None
    joins = small is None
    ins = [part[0] for part in parts] + list(segments) + ([] if joins else [small]) + [rows]
    ins += [memory] if cross else []
    specs = [SMEM] * len(parts) + [VMEM] * (len(ins) - len(parts))
    arrays = arrays_of(parts)
    ins += arrays
    specs += [ANY] * len(arrays)
    outs = [shaped((length, width)), shaped((length, width)), shaped((length, LANES))]
    outs += [shaped((length, width), BF)] * 4 + [shaped((HEADS, length))]
    outs += [shaped((SMALL_ROWS, width))] if joins else []
    scratch = [
        pltpu.VMEM((QUAD, width, width), BF),
        pltpu.VMEM((length, length), F32),
        pltpu.SemaphoreType.DMA((len(parts) + 1, most(parts))),
    ]
    scratch += [pltpu.VMEM((width // BLOCK, 1, BLOCK, width), BF)] if joins else []
    kernel = functools.partial(attend_forward_kernel, layout_of(parts), cross, causal, base, joins)
    flops = 8 * length * width * width + 16 * length * length * width
    return call(kernel, ins, specs, outs, [VMEM] * len(outs), scratch, flops, 8_000_000)


def attend_backward(
    out_tables, segments, small, base, grad, kept, rows, memory, parts, causal, others
):
    length, width = rows.shape
    cross = memory is not None
    splits = others is not None
    hat, rstd, q, k, v, o, lse = kept[1:8]
    ins = [part[0] for part in parts] + list(out_tables)
    specs = [SMEM] * len(ins)
    ins += list(segments) + [small, grad, hat, rstd, rows]
    ins += ([memory] if cross else []) + [q, k, v, o, lse] + list(others or ())
    specs += [VMEM] * (len(ins) - len(specs))
    arrays = arrays_of(parts)
    ins += arrays
    specs += [ANY] * len(arrays)
    outs = [shaped((length, width))] * (2 if cross else 1)
    outs += [] if splits else [shaped((8, width))]
    out_specs = [VMEM] * len(outs) + [ANY] * 2
    outs += halves(width, QUAD + (1 if splits else 0))
    scratch = [
        pltpu.VMEM((QUAD, width, width), BF),
        pltpu.VMEM((QUAD, width, width), BF),
        pltpu.VMEM((length, length), F32),
        pltpu.VMEM((length, width), BF),
        pltpu.VMEM((width, length), F32),
        pltpu.VMEM((length, width), BF),
        pltpu.VMEM((length, width), BF),
        pltpu.VMEM((width, length), BF),
        pltpu.SemaphoreType.DMA((3, 2)),
    ]
    scratch += [pltpu.VMEM((width // LANES, 1, BLOCK, width), BF)] if splits else []
    kernel = functools.partial(
        attend_backward_kernel, layout_of(parts), cross, causal, base, splits
    )
    flops = 16 * length * width * width + 40 * length * length * width
    results = list(call(kernel, ins, specs, outs, out_specs, scratch, flops, 12_000_000))
    rows_grad = results.pop(0)
    memory_grad = results.pop(0) if cross else None
    small_grad = None if splits else results.pop(0)
    return rows_grad, memory_grad, small_grad, results


def feed_scratch(width, grads):
    number = width // BLOCK
    once = [pltpu.VMEM((QUAD, width, width), BF), pltpu.VMEM((number, QUAD, BLOCK, width), BF)]
    return once * (2 if grads else 1)


def feed_forward(small, base, hidden_at, rows, parts):
    length, width = rows.shape
    arrays = arrays_of(parts)
    ins = [part[0] for part in parts] + [small, rows] + arrays
    specs = [SMEM] * 2 + [VMEM] * 2 + [ANY] * len(arrays)
    outs = [shaped((length, width)), shaped((length, width)), shaped((length, LANES))]
    outs += [shaped((QUAD, length, width), BF), shaped((QUAD, length, width))]
    scratch = feed_scratch(width, False) + [pltpu.SemaphoreType.DMA((2, most(parts)))]
    kernel = functools.partial(feed_forward_kernel, layout_of(parts), base, hidden_at)
    flops = 16 * length * width * width
    return call(kernel, ins, specs, outs, [VMEM] * len(outs), scratch, flops, 10_000_000)


def feed_backward(out_tables, small, base, grad, kept, rows, parts):
    length, width = rows.shape
    hat, rstd, active, slope = kept[1:]
    arrays = arrays_of(parts)
    ins = [part[0] for part in parts] + list(out_tables) + [small, grad, hat, rstd, rows, active, slope]
    ins += arrays
    specs = [SMEM] * 4 + [VMEM] * 7 + [ANY] * len(arrays)
    outs = [shaped((length, width)), shaped((8, width))] + halves(width, 2 * QUAD)
    out_specs = [VMEM] * 2 + [ANY] * 2
    scratch = feed_scratch(width, True)
    scratch += [pltpu.SemaphoreType.DMA((2, most(parts))), pltpu.SemaphoreType.DMA((2, 2))]
    kernel = functools.partial(feed_backward_kernel, layout_of(parts), base)
    flops = 32 * length * width * width
    results = call(kernel, ins, specs, outs, out_specs, scratch, flops, 14_000_000)
    return results[0], results[1], results[2:4]


def feed_both(out_tables, small, base, hidden_at, rows, grad, parts):
    length, width = rows.shape
    arrays = arrays_of(parts)
    ins = [part[0] for part in parts] + list(out_tables) + [small, rows, grad] + arrays
    specs = [SMEM] * 4 + [VMEM] * 3 + [ANY] * len(arrays)
    outs = [shaped((length, width)), shaped((length, width)), shaped((8, width))]
    outs += halves(width, 2 * QUAD)
    out_specs = [VMEM] * 3 + [ANY] * 2
    scratch = feed_scratch(width, True) + [
        pltpu.VMEM((QUAD, length, width), BF),
        pltpu.VMEM((QUAD, length, width), F32),
        pltpu.VMEM((length, width), F32),
        pltpu.VMEM((length, LANES), F32),
        pltpu.SemaphoreType.DMA((2, most(parts))),
        pltpu.SemaphoreType.DMA((2, 2)),
    ]
    kernel = functools.partial(feed_both_kernel, layout_of(parts), base, hidden_at)
    flops = 48 * length * width * width
    results = call(kernel, ins, specs, outs, out_specs, scratch, flops, 12_000_000)
    return results[0], results[1], results[2], results[3:5]


def first_kernel(at_ref, square_ref, tall_ref, deep_ref, vector_ref, hidden_ref, one_ref, two_ref, turn_ref, line_ref):
    at = at_ref[0]
    width = square_ref.shape[2]
    turn_ref[...] = jnp.zeros_like(turn_ref)
    lanes, rows = vector_ref.shape
    turn_ref[pl.ds(pl.multiple_of(at * lanes, lanes), lanes), :rows] = vector_ref[...]
    upright = turn_ref[...].T
    line_ref[...] = jnp.zeros_like(line_ref)
    layers, lanes = hidden_ref.shape
    per = LANES // lanes
    for layer in range(layers):
        row = jnp.concatenate([hidden_ref[layer : layer + 1]] * per, axis=1)
        lane = lax.broadcasted_iota(jnp.int32, row.shape, 1) // lanes
        row = jnp.where(lane == at % per, row, 0.0)
        line_ref[pl.ds(4 * layer + at // per, 1), :] = row
    columns = [upright[low : low + 8] for low in (0, 8, 16)] + [line_ref[...]]
    block = jnp.concatenate(columns, axis=1)
    small = jnp.concatenate([block, jnp.zeros_like(block)], axis=0)
    tall = []
    deep = []
    for layer in range(2):
        for index in range(QUAD):
            lanes = slice(index * width, (index + 1) * width)
            tall.append(tall_ref[layer, :, lanes])
            deep.append(deep_ref[layer, index * BLOCK : (index + 1) * BLOCK])
    square = [square_ref[index] for index in range(3 * QUAD)]
    cut = QUAD // 2
    groups = [
        square[:cut] + tall[:QUAD] + square[cut:QUAD] + [small] + deep[:QUAD],
        square[QUAD : 2 * QUAD] + tall[QUAD:] + square[2 * QUAD :] + deep[QUAD:],
    ]
    for out_ref, group in zip((one_ref, two_ref), groups):
        for slot, block in enumerate(group):
            out_ref[0, slot] = block.astype(BF)


def first_arrays(at, square, tall, deep, vectors, hidden):
    width = square.shape[2]
    return pl.pallas_call(
        first_kernel,
        out_shape=[
            shaped((1, 3 * QUAD + 1, BLOCK, width), BF),
            shaped((1, 4 * QUAD, BLOCK, width), BF),
        ],
        in_specs=[SMEM] + [VMEM] * 5,
        out_specs=[VMEM] * 2,
        scratch_shapes=[pltpu.VMEM((LANES, LANES), F32), pltpu.VMEM((8, LANES), F32)],
        compiler_params=pltpu.CompilerParams(vmem_limit_bytes=VMEM_BYTES // 3),
    )(at, square, tall, deep, vectors.T, hidden)


def last_kernel(plan, count, at_ref, *refs):
    arrays, refs = refs[:count], refs[count:]
    masters, firsts, seconds = refs[:5], refs[5:10], refs[10:15]
    outs, refs = [refs[15 + 5 * kind : 20 + 5 * kind] for kind in range(4)], refs[35:]
    buffers, turn_ref, line_ref, sems = refs
    at = at_ref[0]
    starts = []
    for width, pieces, _ in plan:
        for index, low in pieces:
            array = arrays[index]
            array = array if len(array.shape) == 3 else array.at[0]
            source = array.at[low : low + width]
            copy = pltpu.make_async_copy(source, buffers.at[len(starts), :width], sems.at[len(starts)])
            copy.start()
            starts.append(copy)

    def update(slot, where, gradient):
        results = adam_update(
            masters[slot][where],
            gradient,
            firsts[slot][where],
            seconds[slot][where],
            RATES[slot],
            DECAYS[slot],
        )
        for kind in range(4):
            outs[kind][slot][where] = results[kind]

    begin = 0
    for width, pieces, targets in plan:
        for index in range(len(pieces)):
            starts[begin + index].wait()
        for sub, (slot, where) in enumerate(targets):
            gradient = buffers[begin, sub].astype(F32)
            for index in range(1, len(pieces)):
                gradient = gradient + buffers[begin + index, sub].astype(F32)
            if slot < 3:
                update(slot, where, gradient)
                continue
            turn_ref[...] = jnp.zeros_like(turn_ref)
            for column in range(3):
                lanes = slice(column * LANES, (column + 1) * LANES)
                turn_ref[8 * column : 8 * column + 8, :] = gradient[:8, lanes]
            turn_ref[...] = turn_ref[...].T
            lanes, rows = masters[3].shape
            share = turn_ref[pl.ds(pl.multiple_of(at * lanes, lanes), lanes), :][:, :rows]
            update(3, slice(None), share)
            line_ref[...] = gradient[:8, 3 * LANES :]
            layers, lanes = masters[4].shape
            per = LANES // lanes
            for layer in range(layers):
                row = line_ref[pl.ds(4 * layer + at // per, 1), :]
                share = row[:, :lanes]
                for part in range(1, per):
                    other = row[:, part * lanes : (part + 1) * lanes]
                    share = jnp.where(at % per == part, other, share)
                update(4, slice(layer, layer + 1), share)
        begin += len(pieces)


def last_update(at, segments, masters, firsts, seconds):
    arrays = []
    plan = []
    for width, pieces, targets in segments:
        entry = []
        for array, low in pieces:
            found = [place for place, other in enumerate(arrays) if other is array]
            if not found:
                arrays.append(array)
            entry.append((found[0] if found else len(arrays) - 1, low))
        plan.append((width, entry, targets))
    params = [list(group) for group in (masters, firsts, seconds)]
    for group in params:
        group[3] = group[3].T
    flat = params[0] + params[1] + params[2]
    outs = [shaped(array.shape) for array in params[0]] * 3
    outs += [shaped(array.shape, BF) for array in params[0]]
    pieces = sum(len(entry[1]) for entry in plan)
    block = masters[0].shape[1:]
    results = pl.pallas_call(
        functools.partial(last_kernel, plan, len(arrays)),
        out_shape=outs,
        in_specs=[SMEM] + [ANY] * len(arrays) + [VMEM] * len(flat),
        out_specs=[VMEM] * len(outs),
        scratch_shapes=[
            pltpu.VMEM((pieces, max(entry[0] for entry in plan)) + block, BF),
            pltpu.VMEM((LANES, LANES), F32),
            pltpu.VMEM((8, LANES), F32),
            pltpu.SemaphoreType.DMA((pieces,)),
        ],
        compiler_params=pltpu.CompilerParams(vmem_limit_bytes=VMEM_BYTES // 3),
    )(at, *arrays, *flat)
    results = list(results)
    for kind in range(4):
        results[5 * kind + 3] = results[5 * kind + 3].T
    return results


def tie(*arrays):
    return lax.optimization_barrier(arrays)


class Direct:
    def __init__(self, axis_sizes):
        outer, inner = axis_sizes
        self.count = outer * inner
        inner_bits = inner.bit_length() - 1
        bits = self.count.bit_length() - 1
        core = [inner_bits]
        across = list(range(inner_bits + 1, bits))
        up = [0]
        along = list(range(1, inner_bits))
        self.orders = {
            "a": core + across + up + along,
            "b": core + up + across + along,
        }
        self.place = lax.axis_index(AXES)

    def hop(self, array, bit):
        return lax.ppermute(array, AXES, [(at, at ^ (1 << bit)) for at in range(self.count)])

    def table(self, name):
        order = self.orders[name]
        index = jnp.arange(self.count, dtype=jnp.int32)
        block = jnp.zeros_like(index)
        for at, bit in enumerate(order):
            block = block | (((index >> (len(order) - 1 - at)) & 1) << bit)
        return block ^ self.place

    def arrive(self, array, name, step):
        return self.hop(array, self.orders[name][::-1][step])

    def finish(self, array, name):
        return [array, self.hop(array, self.orders[name][0])]


def grown(arrays, arrivals):
    return [jnp.concatenate(pair, axis=0) for pair in zip(arrays, arrivals)]


class Sum:
    def __init__(self, net, name, segments, done, blocks):
        self.net = net
        self.name = name
        self.segments = segments
        self.done = done
        self.blocks = blocks

    def bit(self):
        return self.net.orders[self.name][self.done]

    def split(self, names):
        return [
            Sum(self.net, name, [segment], self.done, self.blocks)
            for name, segment in zip(names, self.segments)
        ]


def core_hop(net, pair, widths):
    keep, send = pair
    arrived = net.hop(send, net.orders["a"][0])
    low = 0
    segments = []
    for width in widths:
        segments.append((width, [(keep, low), (arrived, low)]))
        low += width
    return Sum(net, "a", segments, 1, keep.shape[0])


def combine_kernel(plan, count, outputs, *refs):
    arrays, refs = refs[:count], refs[count:]
    outs, buffers, sems = refs[:outputs], refs[outputs:-1], refs[-1]
    starts = []
    for _, _, number, width, pieces in plan:
        for index, low in pieces:
            array = arrays[index]
            if len(array.shape) == 3:
                source = array.at[low + number * width : low + 2 * number * width]
            else:
                source = array.at[number : 2 * number, low : low + width]
            copy = pltpu.make_async_copy(source, buffers[len(starts)], sems.at[len(starts)])
            copy.start()
            starts.append(copy)
    begin = 0
    for slot, first, number, width, pieces in plan:
        for index in range(begin, begin + len(pieces)):
            starts[index].wait()
        mine = buffers[begin : begin + len(pieces)]

        def body(block, carry, slot=slot, first=first, width=width, mine=mine):
            value = None
            for buffer in mine:
                flat = len(buffer.shape) == 3
                part = buffer[pl.ds(block * width, width)] if flat else buffer[block]
                value = part.astype(F32) if value is None else value + part.astype(F32)
            outs[slot][pl.ds(first + block * width, width)] = value.astype(BF)
            return carry

        lax.fori_loop(0, number, body, 0)
        begin += len(pieces)


class Round:
    def __init__(self, sums, *tokens):
        self.net = sums[0].net
        self.sums = sums
        self.bits = sorted({item.bit() for item in sums})
        arrays = []
        plan = []
        sizes = [0] * len(self.bits)
        self.places = []
        block = None
        for item in sums:
            slot = self.bits.index(item.bit())
            number = item.blocks // 2
            places = []
            for width, pieces in item.segments:
                entry = []
                for array, low in pieces:
                    found = [at for at, other in enumerate(arrays) if other is array]
                    if not found:
                        arrays.append(array)
                    entry.append((found[0] if found else len(arrays) - 1, low))
                    block = array.shape[-2:]
                plan.append((slot, sizes[slot], number, width, entry))
                places.append(sizes[slot])
                sizes[slot] += number * width
            self.places.append((slot, places))
        tied = list(tie(*arrays, *tokens))[: len(arrays)] if tokens else arrays
        scratch = []
        moved = 0
        for _, _, number, width, entry in plan:
            moved += number * width * (len(entry) + 1) * 16384
            for index, _ in entry:
                flat = len(arrays[index].shape) == 3
                shape = (number * width,) if flat else (number, width)
                scratch.append(pltpu.VMEM(shape + block, BF))
        self.sends = pl.pallas_call(
            functools.partial(combine_kernel, plan, len(tied), len(sizes)),
            out_shape=[shaped((size,) + block, BF) for size in sizes],
            in_specs=[ANY] * len(tied),
            out_specs=[VMEM] * len(sizes),
            scratch_shapes=scratch + [pltpu.SemaphoreType.DMA((len(scratch),))],
            cost_estimate=pl.CostEstimate(flops=0, bytes_accessed=moved, transcendentals=0),
            compiler_params=pltpu.CompilerParams(vmem_limit_bytes=VMEM_BYTES // 3),
        )(*tied)

    def before(self, *arrays):
        tied = tie(*arrays, *self.sends)
        self.sends = list(tied[len(arrays) :])
        return tied[: len(arrays)]

    def go(self):
        arrived = [self.net.hop(send, bit) for send, bit in zip(self.sends, self.bits)]
        for item, (slot, places) in zip(self.sums, self.places):
            item.segments = [
                (width, pieces + [(arrived[slot], place)])
                for (width, pieces), place in zip(item.segments, places)
            ]
            item.done += 1
            item.blocks //= 2
        return arrived


def adam_update(weight, gradient, first, second, rate, decay):
    first_new = BETA_ONE * first + (1.0 - BETA_ONE) * gradient
    second_new = BETA_TWO * second + (1.0 - BETA_TWO) * gradient * gradient
    first_hat = first_new / (1.0 - BETA_ONE**STEP)
    second_hat = second_new / (1.0 - BETA_TWO**STEP)
    weight_new = weight - rate * (first_hat / (jnp.sqrt(second_hat) + EPS_ADAM) + decay * weight)
    return (weight_new, first_new, second_new, weight_new.astype(BF))


def gather_small(vectors, hidden):
    whole = lax.all_gather(vectors.astype(BF), AXES, axis=1, tiled=True)
    deep = lax.all_gather(hidden.astype(BF), AXES, axis=1, tiled=True)
    whole = jnp.pad(whole, ((0, HIDDEN_ROW - whole.shape[0]), (0, 0)))
    return jnp.concatenate([whole, deep.reshape(-1, whole.shape[1])], axis=0).astype(F32)


def scatter_small(grads, vectors, hidden, place, count):
    whole = lax.psum(small_rows(*grads), AXES)
    rows, lanes = vectors.shape
    first = lax.dynamic_slice_in_dim(whole[:rows], place * lanes, lanes, axis=1)
    layers, lanes = hidden.shape
    deep = whole[HIDDEN_ROW:].reshape(layers, -1)
    return first, lax.dynamic_slice_in_dim(deep, place * lanes, lanes, axis=1)


def gather_whole(attention, up, down):
    width = attention.shape[2]
    number = width // BLOCK
    square = lax.all_gather(attention, AXES, axis=1, tiled=True)
    square = square.reshape(-1, QUAD, number, BLOCK, width).transpose(0, 2, 1, 3, 4)
    tall = lax.all_gather(up, AXES, axis=1, tiled=True)
    tall = tall.reshape(2, number, BLOCK, QUAD, width).transpose(0, 1, 3, 2, 4)
    deep = lax.all_gather(down, AXES, axis=1, tiled=True).reshape(2, number, QUAD, BLOCK, width)
    half = number // 2
    quads = [square[0], tall[0], deep[0], square[1], square[2], tall[1], deep[1]]
    return [(quad[:half], quad[half:]) for quad in quads]


def scatter_whole(quads):
    joined = [jnp.concatenate(pair, axis=0).astype(F32) for pair in quads]
    number, _, _, width = joined[0].shape
    square = jnp.stack([joined[0], joined[3], joined[4]])
    square = square.transpose(0, 2, 1, 3, 4).reshape(3 * QUAD, width, width)
    tall = jnp.stack([joined[1], joined[5]]).transpose(0, 1, 3, 2, 4)
    tall = tall.reshape(2, width, QUAD * width)
    deep = jnp.stack([joined[2], joined[6]]).reshape(2, QUAD * width, width)
    return [
        lax.psum_scatter(part, AXES, scatter_dimension=1, tiled=True)
        for part in (square, tall, deep)
    ]


def direct_step(pairs, source, target, grad, masters, firsts, seconds, axis_sizes):
    net = Direct(axis_sizes)
    source_pair, target_pair, cross_pair = pairs
    a, b = net.table("a"), net.table("b")
    cut = QUAD // 2
    at = (net.place % (net.count * LANES // source.shape[1])).astype(jnp.int32).reshape(1)

    one, rest = first_arrays(at, *masters)
    (one,) = grown([one], [net.arrive(one, "a", 0)])
    (one,) = grown([one], [net.arrive(one, "a", 1)])
    left, right = one[:, : cut + QUAD], one[:, cut + QUAD :]
    rest, left, right = tie(rest, left, right)
    for step in (2, 3):
        more = tie(
            net.arrive(left, "a", step),
            net.arrive(right, "b", step),
            net.arrive(rest, "a", step - 2),
        )
        left, right, rest = grown((left, right, rest), more)
    self_w, up_two = rest[:, :QUAD], rest[:, QUAD : 2 * QUAD]
    cross_w, down_two = rest[:, 2 * QUAD : 3 * QUAD], rest[:, 3 * QUAD :]
    more = tie(
        net.hop(left, net.orders["a"][0]),
        net.hop(right, net.orders["b"][0]),
        net.arrive(self_w, "a", 2),
        net.arrive(cross_w, "b", 2),
    )
    left, right = [left, more[0]], [right, more[1]]
    self_w, cross_w = grown((self_w, cross_w), more[2:])
    source, self_w, cross_w, up_two, down_two = tie(source, self_w, cross_w, up_two, down_two)
    more = [
        net.arrive(self_w, "a", 3),
        net.arrive(cross_w, "b", 3),
        net.arrive(up_two, "a", 2),
        net.arrive(down_two, "b", 2),
    ]
    enc_attend_w = [(a, left, 0, cut), (b, right, 0, cut)]
    enc_feed_w = [(a, left, cut, QUAD), (b, right, cut + 1, QUAD)]
    enc_kept = attend_forward(source_pair, None, 0, source, None, enc_attend_w, False)
    enc_mid, small = enc_kept[0], enc_kept[8]
    enc_feed_kept = feed_forward(small, 5, HIDDEN_ROW, enc_mid, enc_feed_w)
    memory = enc_feed_kept[0]
    up_two, down_two = grown((up_two, down_two), tie(*more[2:], memory)[:2])
    self_w, cross_w = grown((self_w, cross_w), tie(*more[:2], up_two, down_two)[:2])
    target, up_two, down_two, self_w, cross_w = tie(target, up_two, down_two, self_w, cross_w)
    more = [net.arrive(up_two, "a", 3), net.arrive(down_two, "b", 3)]
    self_w = [(a, net.finish(self_w, "a"), 0, QUAD)]
    cross_w = [(b, net.finish(cross_w, "b"), 0, QUAD)]
    self_kept = attend_forward(target_pair, small, 8, target, None, self_w, True)
    dec_one = self_kept[0]
    cross_kept = attend_forward(cross_pair, small, 13, dec_one, memory, cross_w, False)
    dec_two = cross_kept[0]
    up_two, down_two = grown((up_two, down_two), tie(*more, dec_two)[:2])
    dec_feed_w = [(a, net.finish(up_two, "a"), 0, QUAD), (b, net.finish(down_two, "b"), 0, QUAD)]
    result, two_grad, dec_feed_small, feed_two = feed_both(
        (a, b), small, 18, HIDDEN_ROW + QUAD, dec_two, grad, dec_feed_w
    )

    names = ("a", "b")
    feed_two = core_hop(net, feed_two, (QUAD, QUAD)).split(names)
    one_grad, memory_grad, cross_small, cross_q = attend_backward(
        (a, b), cross_pair, small, 13, two_grad, cross_kept, dec_one, memory, cross_w, False, None
    )
    send = Round(feed_two, cross_small)
    memory_grad, *cross_q = send.before(memory_grad, *cross_q)
    send.go()
    cross_s = core_hop(net, cross_q, (cut, cut)).split(names)
    mid_grad, enc_feed_small, feed_one = feed_backward(
        (a, b), small, 5, memory_grad, enc_feed_kept, enc_mid, enc_feed_w
    )
    send = Round(feed_two + cross_s, enc_feed_small)
    one_grad, *feed_one = send.before(one_grad, *feed_one)
    send.go()
    feed_one = core_hop(net, feed_one, (QUAD, QUAD)).split(names)
    target_grad, _, self_small, self_q = attend_backward(
        (a, b), target_pair, small, 8, one_grad, self_kept, target, None, self_w, True, None
    )
    send = Round(feed_two + cross_s + feed_one, self_small)
    mid_grad, *self_q = send.before(mid_grad, *self_q)
    send.go()
    self_s = core_hop(net, self_q, (cut, cut)).split(names)
    others = (enc_feed_small, self_small, cross_small, dec_feed_small)
    source_grad, _, _, enc_q = attend_backward(
        (a, b), source_pair, small, 0, mid_grad, enc_kept, source, None, enc_attend_w, False, others
    )
    send = Round(feed_two + cross_s + feed_one + self_s, source_grad)
    enc_q = send.before(*enc_q)
    last = send.go()
    enc_s = core_hop(net, enc_q, (cut, cut + 1)).split(names)
    while enc_s[0].blocks > 1:
        send = Round([item for item in cross_s + feed_one + self_s + enc_s if item.blocks > 1], *last)
        last = send.go()

    square = [(0, index) for index in range(3 * QUAD)]
    tall, deep = [], []
    for layer in range(2):
        for index in range(QUAD):
            lanes = slice(index * source.shape[1], (index + 1) * source.shape[1])
            tall.append((1, (layer, slice(None), lanes)))
            deep.append((2, (layer, slice(index * BLOCK, (index + 1) * BLOCK))))
    targets = [square[:cut], square[cut:QUAD] + [(3, None)]]
    targets += [square[QUAD : QUAD + cut], square[QUAD + cut : 2 * QUAD], tall[:QUAD], deep[:QUAD]]
    targets += [tall[QUAD:], deep[QUAD:]]
    targets += [square[2 * QUAD : 2 * QUAD + cut], square[2 * QUAD + cut :]]
    segments = [item.segments[0] for item in enc_s + self_s + feed_one + feed_two + cross_s]
    segments = [segment + (target,) for segment, target in zip(segments, targets)]
    updated = last_update(at, segments, masters, firsts, seconds)
    return (memory, result, source_grad, target_grad), updated


def whole_step(pairs, source, target, grad, masters, firsts, seconds, axis_sizes):
    attention, up, down = [master.astype(BF) for master in masters[:3]]
    vectors, hidden = masters[3:]
    source_pair, target_pair, cross_pair = pairs
    small = gather_small(vectors, hidden)
    quads = gather_whole(attention, up, down)
    table = jnp.arange(source.shape[1] // BLOCK, dtype=jnp.int32)
    two = (table, table)
    parts = [(table, list(quad), 0, QUAD) for quad in quads]
    enc_kept = attend_forward(source_pair, small, 0, source, None, parts[:1], False)
    enc_mid = enc_kept[0]
    enc_feed_kept = feed_forward(small, 5, HIDDEN_ROW, enc_mid, parts[1:3])
    memory = enc_feed_kept[0]
    self_kept = attend_forward(target_pair, small, 8, target, None, parts[3:4], True)
    dec_one = self_kept[0]
    cross_kept = attend_forward(cross_pair, small, 13, dec_one, memory, parts[4:5], False)
    dec_two = cross_kept[0]
    result, two_grad, dec_feed_small, feed_two = feed_both(
        two, small, 18, HIDDEN_ROW + QUAD, dec_two, grad, parts[5:7]
    )
    one_grad, memory_grad, cross_small, cross_q = attend_backward(
        two, cross_pair, small, 13, two_grad, cross_kept, dec_one, memory, parts[4:5], False, None
    )
    target_grad, _, self_small, self_q = attend_backward(
        two, target_pair, small, 8, one_grad, self_kept, target, None, parts[3:4], True, None
    )
    mid_grad, enc_feed_small, feed_one = feed_backward(
        two, small, 5, memory_grad, enc_feed_kept, enc_mid, parts[1:3]
    )
    source_grad, _, enc_small, enc_q = attend_backward(
        two, source_pair, small, 0, mid_grad, enc_kept, source, None, parts[:1], False, None
    )
    quads = [enc_q]
    quads += [[half[:, low : low + QUAD] for half in feed_one] for low in (0, QUAD)]
    quads += [self_q, cross_q]
    quads += [[half[:, low : low + QUAD] for half in feed_two] for low in (0, QUAD)]
    smalls = (enc_small, enc_feed_small, self_small, cross_small, dec_feed_small)
    count = axis_sizes[0] * axis_sizes[1]
    shares = scatter_small(smalls, vectors, hidden, lax.axis_index(AXES), count)
    grads = tuple(scatter_whole(quads)) + shares
    updated = [
        adam_update(
            masters[slot], grads[slot], firsts[slot], seconds[slot], RATES[slot], DECAYS[slot]
        )
        for slot in range(5)
    ]
    flat = [updated[slot][kind] for kind in range(4) for slot in range(5)]
    return (memory, result, source_grad, target_grad), flat


def per_device(
    axis_sizes,
    source_tokens,
    target_tokens,
    source_segments,
    target_segments,
    output_grad,
    attention_weight,
    up_weight,
    down_weight,
    vectors,
    hidden_bias,
    *moments,
):
    masters = (attention_weight, up_weight, down_weight, vectors, hidden_bias)
    firsts = moments[:5]
    seconds = moments[5:]
    width = source_tokens.shape[2]
    pairs = (
        (source_segments, source_segments),
        (target_segments, target_segments),
        (target_segments, source_segments),
    )
    direct = axis_sizes[0] * axis_sizes[1] * BLOCK == width
    tokens, updated = (direct_step if direct else whole_step)(
        pairs,
        source_tokens[0],
        target_tokens[0],
        output_grad[0],
        masters,
        firsts,
        seconds,
        axis_sizes,
    )
    return tuple(array[None] for array in tokens) + tuple(updated)


def solution(mesh):
    rows = P(AXES, None, None)
    line = P(AXES, None)
    matrix = P(None, AXES, None)
    vector = P(None, AXES)
    state = (matrix, matrix, matrix, vector, vector)
    return jax.shard_map(
        functools.partial(per_device, (mesh.shape["dp"], mesh.shape["fsdp"])),
        mesh=mesh,
        in_specs=(rows, rows, line, line, rows) + state * 3,
        out_specs=(rows,) * 4 + state * 4,
        check_vma=False,
    )
```

```python
import functools

import jax
import jax.numpy as jnp
from jax import lax
from jax.experimental import pallas as pl
from jax.experimental.pallas import tpu as pltpu
from jax.sharding import PartitionSpec as P

HEADS = 8
STEP = 10
EPS_NORM = 1e-05
EPS_ADAM = 1e-08
BETA_ONE = 0.9
BETA_TWO = 0.999
LOWEST = -1e30
RATES = (0.05, 0.05, 0.05, 0.3, 0.3)
DECAYS = (0.01, 0.01, 0.01, 0.0, 0.0)
AXES = ("dp", "fsdp")
QUAD = 4
BLOCK = 16
LANES = 128
SMALL_ROWS = 32
VMEM_BYTES = 60 * 1024 * 1024
HIDDEN_ROW = 24
BF = jnp.bfloat16
F32 = jnp.float32
VMEM = pl.BlockSpec(memory_space=pltpu.VMEM)
SMEM = pl.BlockSpec(memory_space=pltpu.SMEM)
ANY = pl.BlockSpec(memory_space=pl.ANY)
ROOT_TWO_PI = 0.7978845608028654
CUBIC = 0.044715


def dot(left, right):
    return jnp.dot(left, right, preferred_element_type=F32)


def dot_nt(left, right):
    return lax.dot_general(left, right, (((1,), (1,)), ((), ())), preferred_element_type=F32)


class Input:
    def __init__(self, array, room, sem):
        self.room = room
        self.shape = room.shape
        self.copy = pltpu.make_async_copy(array, room, sem)
        self.copy.start()
        self.there = False

    def __getitem__(self, where):
        if not self.there:
            self.copy.wait()
            self.there = True
        return self.room[where]


class Output:
    def __init__(self, array, room, sem):
        self.array = array
        self.room = room
        self.shape = room.shape
        self.sem = sem
        self.left = False

    def __getitem__(self, where):
        return self.room[where]

    def __setitem__(self, where, value):
        self.room[where] = value

    def put(self, index=None):
        source = self.room if index is None else self.room.at[index]
        target = self.array if index is None else self.array.at[index]
        pltpu.make_async_copy(source, target, self.sem).start()
        self.left = True

    def finish(self):
        if not self.left:
            self.put()
        pltpu.make_async_copy(self.room, self.array, self.sem).wait()


def staged_kernel(kernel, scalars, inputs, others, outputs, targets, *refs):
    refs = list(refs)
    sems = refs.pop()
    count = inputs + outputs
    rooms = refs[len(refs) - count :]
    refs = refs[: len(refs) - count]
    at = scalars
    for slot in range(inputs):
        refs[at + slot] = Input(refs[at + slot], rooms[slot], sems.at[slot])
    at += inputs + others
    made = []
    for slot in range(inputs, count):
        place = at + slot - inputs
        refs[place] = Output(refs[place], rooms[slot], sems.at[slot])
        made.append(refs[place])
    kernel(*refs)
    for output in made:
        output.finish()


def load_start(part, place, sems):
    table, arrays, low, number = part
    at = 0
    for slot, array in enumerate(arrays):
        for index in range(array.shape[0]):
            source = array.at[index, low : low + number]
            pltpu.make_async_copy(source, place(table[at]), sems.at[slot]).start()
            at += 1


def load_wait(part, sems):
    table, arrays, low, number = part
    for slot, array in enumerate(arrays):
        whole = array.at[:, low : low + number]
        pltpu.make_async_copy(whole, whole, sems.at[slot]).wait()


def store_start(part, place, sems):
    table, arrays, low, number = part
    half = arrays[0].shape[0]
    for index in range(half):
        for slot in (1, 0):
            target = arrays[slot].at[index, low : low + number]
            source = place(table[slot * half + index])
            pltpu.make_async_copy(source, target, sems.at[slot]).start()


def row_place(scratch, low, high):
    def place(block):
        start = pl.multiple_of(block * BLOCK, BLOCK)
        return scratch.at[low:high, pl.ds(start, BLOCK), :]

    return place


def block_place(scratch):
    return lambda block: scratch.at[block]


def norm_forward(pre, gain, shift, out_ref, hat_ref, rstd_ref):
    mean = jnp.mean(pre, axis=-1, keepdims=True)
    centred = pre - mean
    spread = jnp.mean(centred * centred, axis=-1, keepdims=True)
    rstd = lax.rsqrt(spread + EPS_NORM)
    hat = centred * rstd
    hat_ref[...] = hat
    rstd_ref[...] = jnp.broadcast_to(rstd, rstd_ref.shape)
    out_ref[...] = hat * gain + shift
    for ref in (hat_ref, rstd_ref, out_ref):
        if isinstance(ref, Output):
            ref.put()


def norm_backward(grad, hat, rstd, gain):
    gain_grad = jnp.sum(grad * hat, axis=0, keepdims=True)
    shift_grad = jnp.sum(grad, axis=0, keepdims=True)
    scaled = grad * gain
    one = jnp.mean(scaled, axis=-1, keepdims=True)
    two = jnp.mean(scaled * hat, axis=-1, keepdims=True)
    return rstd * (scaled - one - hat * two), gain_grad, shift_grad


def lane_mask(rows):
    return lax.broadcasted_iota(jnp.int32, (rows, LANES), 1) < LANES // 2


def stacked_pair(block):
    first = lane_mask(block.shape[0])
    zero = jnp.zeros_like(block)
    return jnp.concatenate([jnp.where(first, block, zero), jnp.where(first, zero, block)], axis=0)


def merged_pair(stacked):
    rows = stacked.shape[0] // 2
    return jnp.where(lane_mask(rows), stacked[:rows], stacked[rows:])


def mask_fill(bias_ref, column_seg, row_seg, causal, transposed):
    length = bias_ref.shape[0]
    column = jnp.broadcast_to(column_seg, (LANES, length)).T
    for at in range(0, length, LANES):
        same = column == row_seg[:, at : at + LANES]
        if causal:
            down = lax.broadcasted_iota(jnp.int32, (length, LANES), 0)
            along = lax.broadcasted_iota(jnp.int32, (length, LANES), 1) + at
            order = (down <= along) if transposed else (along <= down)
            same = same & order
        bias_ref[:, at : at + LANES] = jnp.where(same, 0.0, LOWEST)


def take_parts(refs, layout, tables):
    parts = []
    for slot, (arrays, low, number) in enumerate(layout):
        parts.append((tables[slot], [refs.pop(0) for _ in range(arrays)], low, number))
    return parts


def small_part(part):
    table, arrays, low, number = part
    return table, arrays, low + number, 1


def small_join(blocks_ref):
    count = blocks_ref.shape[0]
    groups = blocks_ref.shape[3] // LANES
    per = count // groups
    vectors = []
    hidden = [[], []]
    for group in range(groups):
        total = blocks_ref[group * per, 0, :8].astype(F32)
        for at in range(group * per + 1, (group + 1) * per):
            total = total + blocks_ref[at, 0, :8].astype(F32)
        columns = [total[:, at : at + LANES] for at in range(0, 4 * LANES, LANES)]
        vectors.append(jnp.concatenate(columns[:3], axis=0))
        for layer in range(2):
            rows = [columns[3][4 * layer + at : 4 * layer + at + 1] for at in range(4)]
            hidden[layer].append(jnp.concatenate(rows, axis=1))
    return jnp.concatenate([jnp.concatenate(vectors, axis=1)] + hidden[0] + hidden[1], axis=0)


def small_split(whole, group):
    lanes = slice(group * LANES, (group + 1) * LANES)
    columns = [whole[at : at + 8, lanes] for at in (0, 8, 16)]
    rows = []
    for layer in range(2):
        row = whole[24 + 4 * layer + group : 25 + 4 * layer + group]
        rows += [row[:, at : at + LANES] for at in range(0, 4 * LANES, LANES)]
    columns.append(jnp.concatenate(rows, axis=0))
    block = jnp.concatenate(columns, axis=1)
    return jnp.concatenate([block, jnp.zeros_like(block)], axis=0).astype(BF)


def attend_forward_kernel(layout, cross, causal, base, joins, *refs):
    refs = list(refs)
    tables = [refs.pop(0) for _ in layout]
    query_seg = refs.pop(0)
    key_seg = refs.pop(0)
    small = None if joins else refs.pop(0)
    rows_ref = refs.pop(0)
    memory_ref = refs.pop(0) if cross else None
    parts = take_parts(refs, layout, tables)
    q_ref, k_ref, v_ref, o_ref, lse_ref, hat_ref, rstd_ref, out_ref = [refs.pop(0) for _ in range(8)]
    if joins:
        small = refs.pop(0)
        blocks_ref = refs.pop()
        extra = small_part(parts[-1])
    w_ref, bias_ref, sems = refs
    first = 0
    if joins:
        load_start(extra, lambda block: blocks_ref.at[block], sems.at[len(parts)])
    for slot, part in enumerate(parts):
        load_start(part, row_place(w_ref, first, first + part[3]), sems.at[slot])
        first += part[3]
    length, width = rows_ref.shape
    mask_fill(bias_ref, query_seg[...], key_seg[...], causal, False)
    rows = rows_ref[...].astype(BF)
    keys = memory_ref[...].astype(BF) if cross else rows
    if joins:
        load_wait(extra, sems.at[len(parts)])
        small[...] = small_join(blocks_ref)
        small.put()
    for slot, part in enumerate(parts):
        load_wait(part, sems.at[slot])
    scale = (width // HEADS) ** (-0.5)
    q_ref[...] = (dot(rows, w_ref[0]) + small[base : base + 1]).astype(BF) * jnp.asarray(scale, BF)
    k_ref[...] = dot(keys, w_ref[1]).astype(BF)
    v_ref[...] = (dot(keys, w_ref[2]) + small[base + 1 : base + 2]).astype(BF)
    for ref in (q_ref, k_ref, v_ref):
        ref.put()
    lane = lax.broadcasted_iota(jnp.int32, (LANES, LANES), 1)
    for at in range(0, length, LANES):
        reach = at + LANES if causal else length
        logs = jnp.zeros((LANES, LANES), F32)
        for pair in range(HEADS // 2):
            lanes = slice(pair * LANES, (pair + 1) * LANES)
            stacked = stacked_pair(q_ref[at : at + LANES, lanes])
            scores = dot_nt(stacked, k_ref[:reach, lanes])
            bias = bias_ref[at : at + LANES, :reach]
            scores = scores + jnp.concatenate([bias, bias], axis=0)
            largest = jnp.max(scores, axis=-1, keepdims=True)
            exponent = jnp.exp(scores - largest).astype(BF)
            values = jnp.concatenate([v_ref[:reach, lanes], jnp.ones((reach, LANES), BF)], axis=1)
            mixed = dot(exponent, values)
            total = mixed[:, LANES:]
            o_ref[at : at + LANES, lanes] = merged_pair(mixed[:, :LANES] / total).astype(BF)
            log_total = largest + jnp.log(total)
            logs = jnp.where(lane == 2 * pair, log_total[:LANES], logs)
            logs = jnp.where(lane == 2 * pair + 1, log_total[LANES:], logs)
        lse_ref[:, at : at + LANES] = logs.T[:HEADS]
    o_ref.put()
    lse_ref.put()
    attended = dot(o_ref[...], w_ref[3]) + small[base + 2 : base + 3]
    pre = rows_ref[...].astype(F32) + attended
    norm_forward(pre, small[base + 3 : base + 4], small[base + 4 : base + 5], out_ref, hat_ref, rstd_ref)


def attend_backward_kernel(layout, cross, causal, base, splits, *refs):
    refs = list(refs)
    tables = [refs.pop(0) for _ in layout]
    out_tables = [refs.pop(0), refs.pop(0)]
    query_seg = refs.pop(0)
    key_seg = refs.pop(0)
    small = refs.pop(0)
    grad_ref = refs.pop(0)
    hat_ref, rstd_ref = refs.pop(0), refs.pop(0)
    rows_ref = refs.pop(0)
    memory_ref = refs.pop(0) if cross else None
    q_ref, k_ref, v_ref, o_ref, lse_ref = [refs.pop(0) for _ in range(5)]
    others = [refs.pop(0) for _ in range(4)] if splits else None
    parts = take_parts(refs, layout, tables)
    rows_out = refs.pop(0)
    memory_out = refs.pop(0) if cross else None
    small_out = None if splits else refs.pop(0)
    targets = [refs.pop(0), refs.pop(0)]
    outs = []
    for slot, table in enumerate(out_tables):
        outs.append((table, targets, slot * QUAD // 2, QUAD // 2))
    blocks_ref = refs.pop() if splits else None
    w_ref, dw_ref, bias_ref, dout_ref, dq_t_ref, dk_ref, dv_ref, kt_ref, sems = refs
    first = 0
    for slot, part in enumerate(parts):
        load_start(part, row_place(w_ref, first, first + part[3]), sems.at[slot])
        first += part[3]
    length, width = rows_ref.shape
    head = width // HEADS
    scale = head ** (-0.5)
    pre_grad, gain_grad, shift_grad = norm_backward(
        grad_ref[...], hat_ref[...], rstd_ref[:, :1], small[base + 3 : base + 4]
    )
    rows_out[...] = pre_grad
    mask_fill(bias_ref, key_seg[...], query_seg[...], causal, True)
    low = pre_grad.astype(BF)
    for slot, part in enumerate(parts):
        load_wait(part, sems.at[slot])
    dout_ref[...] = dot_nt(low, w_ref[3]).astype(BF)
    dw_ref[3] = dot(o_ref[...].T, low).astype(BF)
    out_bias = jnp.sum(low.astype(F32), axis=0, keepdims=True)
    product = dout_ref[...].astype(F32) * o_ref[...].astype(F32)
    high = product.astype(BF)
    rest = (product - high.astype(F32)).astype(BF)
    picker = lax.broadcasted_iota(jnp.int32, (BLOCK, width), 1) // head
    picker = (picker == lax.broadcasted_iota(jnp.int32, (BLOCK, width), 0)).astype(BF)
    row_dots = dot_nt(picker, high) + dot_nt(picker, rest)
    kt_ref[...] = k_ref[...].T
    for pair in range(HEADS // 2):
        lanes = slice(pair * LANES, (pair + 1) * LANES)
        for at in range(0, length, LANES):
            begin = at if causal else 0
            query = q_ref[begin:, lanes]
            dout = dout_ref[begin:, lanes]
            scores = dot_nt(stacked_pair(k_ref[at : at + LANES, lanes]), query)
            prob_grad = dot_nt(stacked_pair(v_ref[at : at + LANES, lanes]), dout)
            bias = bias_ref[at : at + LANES, begin:]
            probs = []
            score_grads = []
            for part in range(2):
                which = 2 * pair + part
                half = slice(part * LANES, (part + 1) * LANES)
                prob = jnp.exp(scores[half] + (bias - lse_ref[which : which + 1, begin:]))
                probs.append(prob.astype(BF))
                row_dot = row_dots[which : which + 1, begin:]
                score_grads.append((prob * (prob_grad[half] - row_dot)).astype(BF))
                at_t = pair * LANES + part * head
                back = dot(kt_ref[at_t : at_t + head, at : at + LANES], score_grads[part])
                if at == 0:
                    dq_t_ref[at_t : at_t + head, :] = back
                else:
                    dq_t_ref[at_t : at_t + head, begin:] += back
            value_back = dot(jnp.concatenate(probs, axis=0), dout)
            dv_ref[at : at + LANES, lanes] = merged_pair(value_back).astype(BF)
            key_back = dot(jnp.concatenate(score_grads, axis=0), query)
            dk_ref[at : at + LANES, lanes] = merged_pair(key_back).astype(BF)
    query_grad = (dq_t_ref[...] * scale).T.astype(BF)
    key_grad = dk_ref[...]
    value_grad = dv_ref[...]
    turned = rows_ref[...].astype(BF).T
    other = memory_ref[...].astype(BF).T if cross else turned
    dw_ref[2] = dot(other, value_grad).astype(BF)
    store_start(outs[1], row_place(dw_ref, QUAD // 2, QUAD), sems.at[1])
    dw_ref[0] = dot(turned, query_grad).astype(BF)
    dw_ref[1] = dot(other, key_grad).astype(BF)
    store_start(outs[0], row_place(dw_ref, 0, QUAD // 2), sems.at[0])
    rows_back = rows_out[...] + dot_nt(query_grad, w_ref[0])
    memory_back = dot_nt(key_grad, w_ref[1]) + dot_nt(value_grad, w_ref[2])
    if cross:
        rows_out[...] = rows_back
        memory_out[...] = memory_back
        memory_out.put()
    else:
        rows_out[...] = rows_back + memory_back
    rows_out.put()
    query_bias = jnp.sum(query_grad.astype(F32), axis=0, keepdims=True)
    value_bias = jnp.sum(value_grad.astype(F32), axis=0, keepdims=True)
    spare = jnp.zeros((3, width), F32)
    own = jnp.concatenate(
        [query_bias, value_bias, out_bias, gain_grad, shift_grad, spare], axis=0
    )
    if splits:
        enc_feed, self_attend, cross_attend, dec_feed = [other[...] for other in others]
        whole = small_rows(own, enc_feed, self_attend, cross_attend, dec_feed)
        groups = blocks_ref.shape[0]
        for group in range(groups):
            blocks_ref[group, 0] = small_split(whole, group)
        extra = small_part(outs[-1])
        per = 2 * extra[1][0].shape[0] // groups
        store_start(extra, lambda block: blocks_ref.at[block // per], sems.at[2])
        load_wait(extra, sems.at[2])
    else:
        small_out[...] = own
    for slot, part in enumerate(outs):
        load_wait(part, sems.at[slot])


def small_rows(enc_attend, enc_feed, self_attend, cross_attend, dec_feed):
    return jnp.concatenate(
        [
            enc_attend[:5],
            enc_feed[:3],
            self_attend[:5],
            cross_attend[:5],
            dec_feed[:3],
            dec_feed[7:],
            dec_feed[7:],
            dec_feed[7:],
            enc_feed[3:7],
            dec_feed[3:7],
        ],
        axis=0,
    )


def gelu_parts(pre):
    square = pre * pre
    curve = jnp.tanh(ROOT_TWO_PI * pre * (1.0 + CUBIC * square))
    half = 0.5 * pre
    rise = 0.5 + 0.5 * curve
    bend = ROOT_TWO_PI * (1.0 + 3.0 * CUBIC * square)
    return pre * rise, rise + half * (1.0 - curve * curve) * bend


def chunk_of(ref, index):
    number = ref.shape[0] // QUAD
    part = ref[index * number : (index + 1) * number]
    return part.reshape(number * ref.shape[1] * ref.shape[2], ref.shape[3])


def feed_forward_steps(small, base, hidden_at, rows_ref, up_ref, down_ref, active_ref, slope_ref):
    rows = rows_ref[...].astype(BF)
    total = rows_ref[...] + small[base : base + 1]
    for index in range(QUAD):
        at = hidden_at + index
        pre = dot(rows, up_ref[index]) + small[at : at + 1]
        active, slope = gelu_parts(pre)
        active = active.astype(BF)
        active_ref[index] = active
        slope_ref[index] = slope
        for ref in (active_ref, slope_ref):
            if isinstance(ref, Output):
                ref.put(index)
        total = total + dot(active, chunk_of(down_ref, index))
    return total


def feed_backward_steps(
    pre_grad, rows_ref, up_ref, down_ref, active_ref, slope_ref, dup_ref, ddown_ref, rows_out, outs, sems
):
    low = pre_grad.astype(BF)
    number = ddown_ref.shape[0] // QUAD
    for index in range(QUAD):
        down_grad = dot(active_ref[index].T, low).astype(BF)
        ddown_ref[index * number : (index + 1) * number] = down_grad.reshape(
            (number,) + ddown_ref.shape[1:]
        )
    store_start(outs[1], block_place(ddown_ref), sems.at[1])
    turned = rows_ref[...].astype(BF).T
    hiddens = []
    hidden_grads = []
    for index in range(QUAD):
        back = dot_nt(low, chunk_of(down_ref, index))
        hidden = (back * slope_ref[index]).astype(BF)
        hidden_grads.append(jnp.sum(hidden.astype(F32), axis=0, keepdims=True))
        dup_ref[index] = dot(turned, hidden).astype(BF)
        hiddens.append(hidden)
    store_start(outs[0], row_place(dup_ref, 0, QUAD), sems.at[0])
    total = pre_grad
    for index in range(QUAD):
        total = total + dot_nt(hiddens[index], up_ref[index])
    rows_out[...] = total
    rows_out.put()
    out_bias = jnp.sum(low.astype(F32), axis=0, keepdims=True)
    return out_bias, hidden_grads


def load_feed(parts, up_ref, down_ref, sems):
    load_start(parts[0], row_place(up_ref, 0, QUAD), sems.at[0])
    load_start(parts[1], block_place(down_ref), sems.at[1])


def wait_feed(parts, sems):
    for slot, part in enumerate(parts):
        load_wait(part, sems.at[slot])


def feed_outs(refs, tables):
    arrays = [refs.pop(0), refs.pop(0)]
    return [(tables[slot], arrays, slot * QUAD, QUAD) for slot in range(2)]


def feed_small(out_bias, gain_grad, shift_grad, hidden_grads):
    spare = jnp.zeros_like(out_bias)
    return jnp.concatenate([out_bias, gain_grad, shift_grad] + hidden_grads + [spare], axis=0)


def feed_forward_kernel(layout, base, hidden_at, *refs):
    refs = list(refs)
    tables = [refs.pop(0), refs.pop(0)]
    small, rows_ref = refs.pop(0), refs.pop(0)
    parts = take_parts(refs, layout, tables)
    out_ref, hat_ref, rstd_ref, active_ref, slope_ref, up_ref, down_ref, sems = refs
    load_feed(parts, up_ref, down_ref, sems)
    wait_feed(parts, sems)
    pre = feed_forward_steps(
        small, base, hidden_at, rows_ref, up_ref, down_ref, active_ref, slope_ref
    )
    norm_forward(pre, small[base + 1 : base + 2], small[base + 2 : base + 3], out_ref, hat_ref, rstd_ref)


def feed_backward_kernel(layout, base, *refs):
    refs = list(refs)
    tables = [refs.pop(0), refs.pop(0)]
    out_tables = [refs.pop(0), refs.pop(0)]
    small, grad_ref, hat_ref, rstd_ref, rows_ref = [refs.pop(0) for _ in range(5)]
    active_ref, slope_ref = refs.pop(0), refs.pop(0)
    parts = take_parts(refs, layout, tables)
    rows_out, small_out = refs.pop(0), refs.pop(0)
    outs = feed_outs(refs, out_tables)
    up_ref, down_ref, dup_ref, ddown_ref, sems, out_sems = refs
    load_feed(parts, up_ref, down_ref, sems)
    pre_grad, gain_grad, shift_grad = norm_backward(
        grad_ref[...], hat_ref[...], rstd_ref[:, :1], small[base + 1 : base + 2]
    )
    wait_feed(parts, sems)
    out_bias, hidden_grads = feed_backward_steps(
        pre_grad,
        rows_ref,
        up_ref,
        down_ref,
        active_ref,
        slope_ref,
        dup_ref,
        ddown_ref,
        rows_out,
        outs,
        out_sems,
    )
    small_out[...] = feed_small(out_bias, gain_grad, shift_grad, hidden_grads)
    wait_feed(outs, out_sems)


def feed_both_kernel(layout, base, hidden_at, *refs):
    refs = list(refs)
    tables = [refs.pop(0), refs.pop(0)]
    out_tables = [refs.pop(0), refs.pop(0)]
    small, rows_ref, grad_ref = [refs.pop(0) for _ in range(3)]
    parts = take_parts(refs, layout, tables)
    out_ref, rows_out, small_out = [refs.pop(0) for _ in range(3)]
    outs = feed_outs(refs, out_tables)
    up_ref, down_ref, dup_ref, ddown_ref, active_ref, slope_ref, hat_ref, rstd_ref = refs[:8]
    sems, out_sems = refs[8:]
    load_feed(parts, up_ref, down_ref, sems)
    wait_feed(parts, sems)
    pre = feed_forward_steps(
        small, base, hidden_at, rows_ref, up_ref, down_ref, active_ref, slope_ref
    )
    gain = small[base + 1 : base + 2]
    norm_forward(pre, gain, small[base + 2 : base + 3], out_ref, hat_ref, rstd_ref)
    pre_grad, gain_grad, shift_grad = norm_backward(
        grad_ref[...].astype(F32), hat_ref[...], rstd_ref[:, :1], gain
    )
    out_bias, hidden_grads = feed_backward_steps(
        pre_grad,
        rows_ref,
        up_ref,
        down_ref,
        active_ref,
        slope_ref,
        dup_ref,
        ddown_ref,
        rows_out,
        outs,
        out_sems,
    )
    small_out[...] = feed_small(out_bias, gain_grad, shift_grad, hidden_grads)
    wait_feed(outs, out_sems)


def shaped(shape, dtype=F32):
    return jax.ShapeDtypeStruct(shape, dtype)


def call(
    kernel, scalars, inputs, others, outs, targets, scratch, flops, moved, limit=VMEM_BYTES
):
    rooms = [pltpu.VMEM(array.shape, array.dtype) for array in list(inputs) + list(outs)]
    return pl.pallas_call(
        functools.partial(
            staged_kernel, kernel, len(scalars), len(inputs), len(others), len(outs), len(targets)
        ),
        out_shape=list(outs) + list(targets),
        in_specs=[SMEM] * len(scalars) + [ANY] * (len(inputs) + len(others)),
        out_specs=[ANY] * (len(outs) + len(targets)),
        scratch_shapes=scratch + rooms + [pltpu.SemaphoreType.DMA((len(rooms),))],
        cost_estimate=pl.CostEstimate(flops=flops, bytes_accessed=moved, transcendentals=0),
        compiler_params=pltpu.CompilerParams(vmem_limit_bytes=limit),
    )(*scalars, *inputs, *others)


def layout_of(parts):
    return [(len(arrays), low, number) for _, arrays, low, number in parts]


def arrays_of(parts):
    return [array for part in parts for array in part[1]]


def most(parts):
    return max(len(part[1]) for part in parts)


def halves(width, number):
    return [shaped((width // BLOCK // 2, number, BLOCK, width), BF)] * 2


def attend_forward(segments, small, base, rows, memory, parts, causal):
    length, width = rows.shape
    cross = memory is not None
    joins = small is None
    scalars = [part[0] for part in parts]
    inputs = list(segments) + ([] if joins else [small]) + [rows] + ([memory] if cross else [])
    outs = [shaped((length, width), BF)] * 4 + [shaped((HEADS, length))]
    outs += [shaped((length, width)), shaped((length, LANES)), shaped((length, width))]
    outs += [shaped((SMALL_ROWS, width))] if joins else []
    scratch = [
        pltpu.VMEM((QUAD, width, width), BF),
        pltpu.VMEM((length, length), F32),
        pltpu.SemaphoreType.DMA((len(parts) + 1, most(parts))),
    ]
    scratch += [pltpu.VMEM((width // BLOCK, 1, BLOCK, width), BF)] if joins else []
    kernel = functools.partial(attend_forward_kernel, layout_of(parts), cross, causal, base, joins)
    flops = 8 * length * width * width + 16 * length * length * width
    return call(kernel, scalars, inputs, arrays_of(parts), outs, [], scratch, flops, 8_000_000)


def attend_backward(
    out_tables, segments, small, base, grad, kept, rows, memory, parts, causal, others
):
    length, width = rows.shape
    cross = memory is not None
    splits = others is not None
    q, k, v, o, lse, hat, rstd = kept[:7]
    scalars = [part[0] for part in parts] + list(out_tables)
    inputs = list(segments) + [small, grad, hat, rstd, rows]
    inputs += ([memory] if cross else []) + [q, k, v, o, lse] + list(others or ())
    outs = [shaped((length, width))] * (2 if cross else 1)
    outs += [] if splits else [shaped((8, width))]
    targets = halves(width, QUAD + (1 if splits else 0))
    scratch = [
        pltpu.VMEM((QUAD, width, width), BF),
        pltpu.VMEM((QUAD, width, width), BF),
        pltpu.VMEM((length, length), F32),
        pltpu.VMEM((length, width), BF),
        pltpu.VMEM((width, length), F32),
        pltpu.VMEM((length, width), BF),
        pltpu.VMEM((length, width), BF),
        pltpu.VMEM((width, length), BF),
        pltpu.SemaphoreType.DMA((3, 2)),
    ]
    scratch += [pltpu.VMEM((width // LANES, 1, BLOCK, width), BF)] if splits else []
    kernel = functools.partial(
        attend_backward_kernel, layout_of(parts), cross, causal, base, splits
    )
    flops = 16 * length * width * width + 40 * length * length * width
    arrays = arrays_of(parts)
    results = list(call(kernel, scalars, inputs, arrays, outs, targets, scratch, flops, 12_000_000))
    rows_grad = results.pop(0)
    memory_grad = results.pop(0) if cross else None
    small_grad = None if splits else results.pop(0)
    return rows_grad, memory_grad, small_grad, results


def feed_scratch(width, grads):
    number = width // BLOCK
    once = [pltpu.VMEM((QUAD, width, width), BF), pltpu.VMEM((number, QUAD, BLOCK, width), BF)]
    return once * (2 if grads else 1)


def feed_forward(small, base, hidden_at, rows, parts):
    length, width = rows.shape
    scalars = [part[0] for part in parts]
    outs = [shaped((length, width)), shaped((length, width)), shaped((length, LANES))]
    outs += [shaped((QUAD, length, width), BF), shaped((QUAD, length, width))]
    scratch = feed_scratch(width, False) + [pltpu.SemaphoreType.DMA((2, most(parts)))]
    kernel = functools.partial(feed_forward_kernel, layout_of(parts), base, hidden_at)
    flops = 16 * length * width * width
    arrays = arrays_of(parts)
    return call(kernel, scalars, [small, rows], arrays, outs, [], scratch, flops, 10_000_000)


def feed_backward(out_tables, small, base, grad, kept, rows, parts):
    length, width = rows.shape
    hat, rstd, active, slope = kept[1:]
    scalars = [part[0] for part in parts] + list(out_tables)
    inputs = [small, grad, hat, rstd, rows, active, slope]
    outs = [shaped((length, width)), shaped((8, width))]
    targets = halves(width, 2 * QUAD)
    scratch = feed_scratch(width, True)
    scratch += [pltpu.SemaphoreType.DMA((2, most(parts))), pltpu.SemaphoreType.DMA((2, 2))]
    kernel = functools.partial(feed_backward_kernel, layout_of(parts), base)
    flops = 32 * length * width * width
    arrays = arrays_of(parts)
    results = call(kernel, scalars, inputs, arrays, outs, targets, scratch, flops, 14_000_000)
    return results[0], results[1], results[2:4]


def feed_both(out_tables, small, base, hidden_at, rows, grad, parts):
    length, width = rows.shape
    scalars = [part[0] for part in parts] + list(out_tables)
    outs = [shaped((length, width)), shaped((length, width)), shaped((8, width))]
    targets = halves(width, 2 * QUAD)
    scratch = feed_scratch(width, True) + [
        pltpu.VMEM((QUAD, length, width), BF),
        pltpu.VMEM((QUAD, length, width), F32),
        pltpu.VMEM((length, width), F32),
        pltpu.VMEM((length, LANES), F32),
        pltpu.SemaphoreType.DMA((2, most(parts))),
        pltpu.SemaphoreType.DMA((2, 2)),
    ]
    kernel = functools.partial(feed_both_kernel, layout_of(parts), base, hidden_at)
    flops = 48 * length * width * width
    arrays = arrays_of(parts)
    results = call(kernel, scalars, [small, rows, grad], arrays, outs, targets, scratch, flops, 12_000_000)
    return results[0], results[1], results[2], results[3:5]


def first_kernel(
    at_ref,
    vector_ref,
    hidden_ref,
    square_ref,
    tall_ref,
    deep_ref,
    one_ref,
    two_ref,
    turn_ref,
    line_ref,
):
    at = at_ref[0]
    width = square_ref.shape[2]
    turn_ref[...] = jnp.zeros_like(turn_ref)
    lanes, rows = vector_ref.shape
    turn_ref[pl.ds(pl.multiple_of(at * lanes, lanes), lanes), :rows] = vector_ref[...]
    upright = turn_ref[...].T
    line_ref[...] = jnp.zeros_like(line_ref)
    layers, lanes = hidden_ref.shape
    per = LANES // lanes
    for layer in range(layers):
        row = jnp.concatenate([hidden_ref[layer : layer + 1]] * per, axis=1)
        lane = lax.broadcasted_iota(jnp.int32, row.shape, 1) // lanes
        row = jnp.where(lane == at % per, row, 0.0)
        line_ref[pl.ds(4 * layer + at // per, 1), :] = row
    columns = [upright[low : low + 8] for low in (0, 8, 16)] + [line_ref[...]]
    block = jnp.concatenate(columns, axis=1)
    small = jnp.concatenate([block, jnp.zeros_like(block)], axis=0)
    tall = []
    deep = []
    for layer in range(2):
        for index in range(QUAD):
            lanes = slice(index * width, (index + 1) * width)
            tall.append(tall_ref[layer, :, lanes])
            deep.append(deep_ref[layer, index * BLOCK : (index + 1) * BLOCK])
    square = [square_ref[index] for index in range(3 * QUAD)]
    cut = QUAD // 2
    groups = [
        square[:cut] + tall[:QUAD] + square[cut:QUAD] + [small] + deep[:QUAD],
        square[QUAD : 2 * QUAD] + tall[QUAD:] + square[2 * QUAD :] + deep[QUAD:],
    ]
    for out_ref, group in zip((one_ref, two_ref), groups):
        for slot, block in enumerate(group):
            out_ref[0, slot] = block.astype(BF)
        out_ref.put()


def first_arrays(at, square, tall, deep, vectors, hidden):
    width = square.shape[2]
    outs = [
        shaped((1, 3 * QUAD + 1, BLOCK, width), BF),
        shaped((1, 4 * QUAD, BLOCK, width), BF),
    ]
    scratch = [pltpu.VMEM((LANES, LANES), F32), pltpu.VMEM((8, LANES), F32)]
    inputs = [vectors.T, hidden, square, tall, deep]
    return call(first_kernel, [at], inputs, [], outs, [], scratch, 0, 4_000_000)


def last_kernel(plan, count, at_ref, *refs):
    masters, firsts, seconds = refs[:5], refs[5:10], refs[10:15]
    arrays, refs = refs[15 : 15 + count], refs[15 + count :]
    outs, refs = [refs[5 * kind : 5 * kind + 5] for kind in range(4)], refs[20:]
    buffers, turn_ref, line_ref, sems = refs
    at = at_ref[0]
    starts = []
    for width, pieces, _ in plan:
        for index, low in pieces:
            array = arrays[index]
            array = array if len(array.shape) == 3 else array.at[0]
            source = array.at[low : low + width]
            copy = pltpu.make_async_copy(source, buffers.at[len(starts), :width], sems.at[len(starts)])
            copy.start()
            starts.append(copy)

    def update(slot, where, gradient):
        results = adam_update(
            masters[slot][where],
            gradient,
            firsts[slot][where],
            seconds[slot][where],
            RATES[slot],
            DECAYS[slot],
        )
        for kind in range(4):
            outs[kind][slot][where] = results[kind]

    begin = 0
    left = len(plan)
    for width, pieces, targets in plan:
        for index in range(len(pieces)):
            starts[begin + index].wait()
        for sub, (slot, where) in enumerate(targets):
            gradient = buffers[begin, sub].astype(F32)
            for index in range(1, len(pieces)):
                gradient = gradient + buffers[begin + index, sub].astype(F32)
            if slot < 3:
                update(slot, where, gradient)
                continue
            turn_ref[...] = jnp.zeros_like(turn_ref)
            for column in range(3):
                lanes = slice(column * LANES, (column + 1) * LANES)
                turn_ref[8 * column : 8 * column + 8, :] = gradient[:8, lanes]
            turn_ref[...] = turn_ref[...].T
            lanes, rows = masters[3].shape
            share = turn_ref[pl.ds(pl.multiple_of(at * lanes, lanes), lanes), :][:, :rows]
            update(3, slice(None), share)
            line_ref[...] = gradient[:8, 3 * LANES :]
            layers, lanes = masters[4].shape
            per = LANES // lanes
            for layer in range(layers):
                row = line_ref[pl.ds(4 * layer + at // per, 1), :]
                share = row[:, :lanes]
                for part in range(1, per):
                    other = row[:, part * lanes : (part + 1) * lanes]
                    share = jnp.where(at % per == part, other, share)
                update(4, slice(layer, layer + 1), share)
        begin += len(pieces)
        left -= 1
        for slot in range(5):
            ends = [at for at, (_, _, each) in enumerate(plan) if any(to[0] in used(slot) for to in each)]
            if ends[-1] == len(plan) - 1 - left:
                for kind in range(4):
                    outs[kind][slot].put()


def used(slot):
    return (3,) if slot > 2 else (slot,)


def last_update(at, segments, masters, firsts, seconds):
    arrays = []
    plan = []
    for width, pieces, targets in segments:
        entry = []
        for array, low in pieces:
            found = [place for place, other in enumerate(arrays) if other is array]
            if not found:
                arrays.append(array)
            entry.append((found[0] if found else len(arrays) - 1, low))
        plan.append((width, entry, targets))
    params = [list(group) for group in (masters, firsts, seconds)]
    for group in params:
        group[3] = group[3].T
    flat = params[0] + params[1] + params[2]
    outs = [shaped(array.shape) for array in params[0]] * 3
    outs += [shaped(array.shape, BF) for array in params[0]]
    pieces = sum(len(entry[1]) for entry in plan)
    block = masters[0].shape[1:]
    scratch = [
        pltpu.VMEM((pieces, max(entry[0] for entry in plan)) + block, BF),
        pltpu.VMEM((LANES, LANES), F32),
        pltpu.VMEM((8, LANES), F32),
        pltpu.SemaphoreType.DMA((pieces,)),
    ]
    kernel = functools.partial(last_kernel, plan, len(arrays))
    results = call(
        kernel, [at], flat, arrays, outs, [], scratch, 0, 8_000_000, VMEM_BYTES // 2
    )
    results = list(results)
    for kind in range(4):
        results[5 * kind + 3] = results[5 * kind + 3].T
    return results


def tie(*arrays):
    return lax.optimization_barrier(arrays)


class Direct:
    def __init__(self, axis_sizes):
        outer, inner = axis_sizes
        self.count = outer * inner
        inner_bits = inner.bit_length() - 1
        bits = self.count.bit_length() - 1
        core = [inner_bits]
        across = list(range(inner_bits + 1, bits))
        up = [0]
        along = list(range(1, inner_bits))
        self.orders = {
            "a": core + across + up + along,
            "b": core + up + across + along,
        }
        self.place = lax.axis_index(AXES)

    def hop(self, array, bit):
        return lax.ppermute(array, AXES, [(at, at ^ (1 << bit)) for at in range(self.count)])

    def table(self, name):
        order = self.orders[name]
        index = jnp.arange(self.count, dtype=jnp.int32)
        block = jnp.zeros_like(index)
        for at, bit in enumerate(order):
            block = block | (((index >> (len(order) - 1 - at)) & 1) << bit)
        return block ^ self.place

    def arrive(self, array, name, step):
        return self.hop(array, self.orders[name][::-1][step])

    def finish(self, array, name):
        return [array, self.hop(array, self.orders[name][0])]


def grown(arrays, arrivals):
    return [jnp.concatenate(pair, axis=0) for pair in zip(arrays, arrivals)]


class Sum:
    def __init__(self, net, name, segments, done, blocks):
        self.net = net
        self.name = name
        self.segments = segments
        self.done = done
        self.blocks = blocks

    def bit(self):
        return self.net.orders[self.name][self.done]

    def split(self, names):
        return [
            Sum(self.net, name, [segment], self.done, self.blocks)
            for name, segment in zip(names, self.segments)
        ]


def core_hop(net, pair, widths):
    keep, send = pair
    arrived = net.hop(send, net.orders["a"][0])
    low = 0
    segments = []
    for width in widths:
        segments.append((width, [(keep, low), (arrived, low)]))
        low += width
    return Sum(net, "a", segments, 1, keep.shape[0])


def combine_kernel(plan, count, outputs, *refs):
    arrays, refs = refs[:count], refs[count:]
    outs, buffers, sems = refs[:outputs], refs[outputs:-1], refs[-1]
    starts = []
    for _, _, held, number, width, pieces in plan:
        begin = 0 if held is not None else number
        for index, low in pieces:
            array = arrays[index]
            if len(array.shape) == 3:
                source = array.at[low + begin * width : low + 2 * number * width]
            else:
                source = array.at[begin : 2 * number, low : low + width]
            copy = pltpu.make_async_copy(source, buffers[len(starts)], sems.at[len(starts)])
            copy.start()
            starts.append(copy)
    begin = 0
    for slot, first, held, number, width, pieces in plan:
        for index in range(begin, begin + len(pieces)):
            starts[index].wait()
        mine = buffers[begin : begin + len(pieces)]
        jobs = [(slot, first, 0)] if held is None else [(slot, first, number), (outputs - 1, held, 0)]
        for out, place, skip in jobs:

            def body(block, carry, out=out, place=place, skip=skip, width=width, mine=mine):
                value = None
                for buffer in mine:
                    flat = len(buffer.shape) == 3
                    at = block + skip
                    part = buffer[pl.ds(at * width, width)] if flat else buffer[at]
                    value = part.astype(F32) if value is None else value + part.astype(F32)
                outs[out][pl.ds(place + block * width, width)] = value.astype(BF)
                return carry

            lax.fori_loop(0, number, body, 0)
        begin += len(pieces)


class Round:
    def __init__(self, sums, *tokens, limit=VMEM_BYTES // 3):
        self.net = sums[0].net
        self.sums = sums
        self.bits = sorted({item.bit() for item in sums})
        arrays = []
        plan = []
        sizes = [0] * len(self.bits) + [0]
        self.places = []
        block = None
        for item in sums:
            slot = self.bits.index(item.bit())
            number = item.blocks // 2
            holds = item.done > 1
            places = []
            for width, pieces in item.segments:
                entry = []
                for array, low in pieces:
                    found = [at for at, other in enumerate(arrays) if other is array]
                    if not found:
                        arrays.append(array)
                    entry.append((found[0] if found else len(arrays) - 1, low))
                    block = array.shape[-2:]
                held = sizes[-1] if holds else None
                plan.append((slot, sizes[slot], held, number, width, entry))
                places.append((sizes[slot], held))
                sizes[slot] += number * width
                sizes[-1] += number * width if holds else 0
            self.places.append((slot, places))
        tied = list(tie(*arrays, *tokens))[: len(arrays)] if tokens else arrays
        scratch = []
        moved = 0
        for _, _, held, number, width, entry in plan:
            both = number if held is None else 2 * number
            moved += both * width * (len(entry) + 1) * 16384
            for index, _ in entry:
                flat = len(arrays[index].shape) == 3
                shape = (both * width,) if flat else (both, width)
                scratch.append(pltpu.VMEM(shape + block, BF))
        if not sizes[-1]:
            sizes.pop()
        self.sends = pl.pallas_call(
            functools.partial(combine_kernel, plan, len(tied), len(sizes)),
            out_shape=[shaped((size,) + block, BF) for size in sizes],
            in_specs=[ANY] * len(tied),
            out_specs=[VMEM] * len(sizes),
            scratch_shapes=scratch + [pltpu.SemaphoreType.DMA((len(scratch),))],
            cost_estimate=pl.CostEstimate(flops=0, bytes_accessed=moved, transcendentals=0),
            compiler_params=pltpu.CompilerParams(vmem_limit_bytes=limit),
        )(*tied)

    def before(self, *arrays):
        tied = tie(*arrays, *self.sends)
        self.sends = list(tied[len(arrays) :])
        return tied[: len(arrays)]

    def go(self):
        arrived = [self.net.hop(send, bit) for send, bit in zip(self.sends, self.bits)]
        for item, (slot, places) in zip(self.sums, self.places):
            made = []
            for (width, pieces), (place, held) in zip(item.segments, places):
                stay = pieces if held is None else [(self.sends[-1], held)]
                made.append((width, stay + [(arrived[slot], place)]))
            item.segments = made
            item.done += 1
            item.blocks //= 2
        return arrived


def adam_update(weight, gradient, first, second, rate, decay):
    first_new = BETA_ONE * first + (1.0 - BETA_ONE) * gradient
    second_new = BETA_TWO * second + (1.0 - BETA_TWO) * gradient * gradient
    first_hat = first_new / (1.0 - BETA_ONE**STEP)
    second_hat = second_new / (1.0 - BETA_TWO**STEP)
    weight_new = weight - rate * (first_hat / (jnp.sqrt(second_hat) + EPS_ADAM) + decay * weight)
    return (weight_new, first_new, second_new, weight_new.astype(BF))


def gather_small(vectors, hidden):
    whole = lax.all_gather(vectors.astype(BF), AXES, axis=1, tiled=True)
    deep = lax.all_gather(hidden.astype(BF), AXES, axis=1, tiled=True)
    whole = jnp.pad(whole, ((0, HIDDEN_ROW - whole.shape[0]), (0, 0)))
    return jnp.concatenate([whole, deep.reshape(-1, whole.shape[1])], axis=0).astype(F32)


def scatter_small(grads, vectors, hidden, place, count):
    whole = lax.psum(small_rows(*grads), AXES)
    rows, lanes = vectors.shape
    first = lax.dynamic_slice_in_dim(whole[:rows], place * lanes, lanes, axis=1)
    layers, lanes = hidden.shape
    deep = whole[HIDDEN_ROW:].reshape(layers, -1)
    return first, lax.dynamic_slice_in_dim(deep, place * lanes, lanes, axis=1)


def gather_whole(attention, up, down):
    width = attention.shape[2]
    number = width // BLOCK
    square = lax.all_gather(attention, AXES, axis=1, tiled=True)
    square = square.reshape(-1, QUAD, number, BLOCK, width).transpose(0, 2, 1, 3, 4)
    tall = lax.all_gather(up, AXES, axis=1, tiled=True)
    tall = tall.reshape(2, number, BLOCK, QUAD, width).transpose(0, 1, 3, 2, 4)
    deep = lax.all_gather(down, AXES, axis=1, tiled=True).reshape(2, number, QUAD, BLOCK, width)
    half = number // 2
    quads = [square[0], tall[0], deep[0], square[1], square[2], tall[1], deep[1]]
    return [(quad[:half], quad[half:]) for quad in quads]


def scatter_whole(quads):
    joined = [jnp.concatenate(pair, axis=0).astype(F32) for pair in quads]
    number, _, _, width = joined[0].shape
    square = jnp.stack([joined[0], joined[3], joined[4]])
    square = square.transpose(0, 2, 1, 3, 4).reshape(3 * QUAD, width, width)
    tall = jnp.stack([joined[1], joined[5]]).transpose(0, 1, 3, 2, 4)
    tall = tall.reshape(2, width, QUAD * width)
    deep = jnp.stack([joined[2], joined[6]]).reshape(2, QUAD * width, width)
    return [
        lax.psum_scatter(part, AXES, scatter_dimension=1, tiled=True)
        for part in (square, tall, deep)
    ]


def direct_step(pairs, source, target, grad, masters, firsts, seconds, axis_sizes):
    net = Direct(axis_sizes)
    source_pair, target_pair, cross_pair = pairs
    a, b = net.table("a"), net.table("b")
    cut = QUAD // 2
    at = (net.place % (net.count * LANES // source.shape[1])).astype(jnp.int32).reshape(1)

    one, rest = first_arrays(at, *masters)
    (one,) = grown([one], [net.arrive(one, "a", 0)])
    (one,) = grown([one], [net.arrive(one, "a", 1)])
    left, right = one[:, : cut + QUAD], one[:, cut + QUAD :]
    rest, left, right = tie(rest, left, right)
    for step in (2, 3):
        more = tie(
            net.arrive(left, "a", step),
            net.arrive(right, "b", step),
            net.arrive(rest, "a", step - 2),
        )
        left, right, rest = grown((left, right, rest), more)
    self_w, up_two = rest[:, :QUAD], rest[:, QUAD : 2 * QUAD]
    cross_w, down_two = rest[:, 2 * QUAD : 3 * QUAD], rest[:, 3 * QUAD :]
    more = tie(
        net.hop(left, net.orders["a"][0]),
        net.hop(right, net.orders["b"][0]),
        net.arrive(self_w, "a", 2),
        net.arrive(cross_w, "b", 2),
    )
    left, right = [left, more[0]], [right, more[1]]
    self_w, cross_w = grown((self_w, cross_w), more[2:])
    source, self_w, cross_w, up_two, down_two = tie(source, self_w, cross_w, up_two, down_two)
    more = [
        net.arrive(self_w, "a", 3),
        net.arrive(cross_w, "b", 3),
        net.arrive(up_two, "a", 2),
        net.arrive(down_two, "b", 2),
    ]
    enc_attend_w = [(a, left, 0, cut), (b, right, 0, cut)]
    enc_feed_w = [(a, left, cut, QUAD), (b, right, cut + 1, QUAD)]
    enc_kept = attend_forward(source_pair, None, 0, source, None, enc_attend_w, False)
    enc_mid, small = enc_kept[7], enc_kept[8]
    enc_feed_kept = feed_forward(small, 5, HIDDEN_ROW, enc_mid, enc_feed_w)
    memory = enc_feed_kept[0]
    up_two, down_two = grown((up_two, down_two), tie(*more[2:], memory)[:2])
    self_w, cross_w = grown((self_w, cross_w), tie(*more[:2], up_two, down_two)[:2])
    target, up_two, down_two, self_w, cross_w = tie(target, up_two, down_two, self_w, cross_w)
    more = [net.arrive(up_two, "a", 3), net.arrive(down_two, "b", 3)]
    self_w = [(a, net.finish(self_w, "a"), 0, QUAD)]
    cross_w = [(b, net.finish(cross_w, "b"), 0, QUAD)]
    self_kept = attend_forward(target_pair, small, 8, target, None, self_w, True)
    dec_one = self_kept[7]
    cross_kept = attend_forward(cross_pair, small, 13, dec_one, memory, cross_w, False)
    dec_two = cross_kept[7]
    up_two, down_two = grown((up_two, down_two), tie(*more, dec_two)[:2])
    dec_feed_w = [(a, net.finish(up_two, "a"), 0, QUAD), (b, net.finish(down_two, "b"), 0, QUAD)]
    result, two_grad, dec_feed_small, feed_two = feed_both(
        (a, b), small, 18, HIDDEN_ROW + QUAD, dec_two, grad, dec_feed_w
    )

    names = ("a", "b")
    feed_two = core_hop(net, feed_two, (QUAD, QUAD)).split(names)
    one_grad, memory_grad, cross_small, cross_q = attend_backward(
        (a, b), cross_pair, small, 13, two_grad, cross_kept, dec_one, memory, cross_w, False, None
    )
    send = Round(feed_two, cross_small)
    memory_grad, *cross_q = send.before(memory_grad, *cross_q)
    send.go()
    cross_s = core_hop(net, cross_q, (cut, cut)).split(names)
    mid_grad, enc_feed_small, feed_one = feed_backward(
        (a, b), small, 5, memory_grad, enc_feed_kept, enc_mid, enc_feed_w
    )
    send = Round(feed_two + cross_s, enc_feed_small)
    one_grad, *feed_one = send.before(one_grad, *feed_one)
    send.go()
    feed_one = core_hop(net, feed_one, (QUAD, QUAD)).split(names)
    target_grad, _, self_small, self_q = attend_backward(
        (a, b), target_pair, small, 8, one_grad, self_kept, target, None, self_w, True, None
    )
    send = Round(feed_two + cross_s + feed_one, self_small)
    mid_grad, *self_q = send.before(mid_grad, *self_q)
    send.go()
    self_s = core_hop(net, self_q, (cut, cut)).split(names)
    others = (enc_feed_small, self_small, cross_small, dec_feed_small)
    source_grad, _, _, enc_q = attend_backward(
        (a, b), source_pair, small, 0, mid_grad, enc_kept, source, None, enc_attend_w, False, others
    )
    send = Round(feed_two + cross_s + feed_one + self_s, source_grad)
    enc_q = send.before(*enc_q)
    last = send.go()
    enc_s = core_hop(net, enc_q, (cut, cut + 1)).split(names)
    while enc_s[0].blocks > 1:
        send = Round([item for item in cross_s + feed_one + self_s + enc_s if item.blocks > 1], *last)
        last = send.go()

    square = [(0, index) for index in range(3 * QUAD)]
    tall, deep = [], []
    for layer in range(2):
        for index in range(QUAD):
            lanes = slice(index * source.shape[1], (index + 1) * source.shape[1])
            tall.append((1, (layer, slice(None), lanes)))
            deep.append((2, (layer, slice(index * BLOCK, (index + 1) * BLOCK))))
    targets = [square[:cut], square[cut:QUAD] + [(3, None)]]
    targets += [square[QUAD : QUAD + cut], square[QUAD + cut : 2 * QUAD], tall[:QUAD], deep[:QUAD]]
    targets += [tall[QUAD:], deep[QUAD:]]
    targets += [square[2 * QUAD : 2 * QUAD + cut], square[2 * QUAD + cut :]]
    segments = [item.segments[0] for item in enc_s + self_s + feed_one + feed_two + cross_s]
    segments = [segment + (target,) for segment, target in zip(segments, targets)]
    updated = last_update(at, segments, masters, firsts, seconds)
    return (memory, result, source_grad, target_grad), updated


def whole_step(pairs, source, target, grad, masters, firsts, seconds, axis_sizes):
    attention, up, down = [master.astype(BF) for master in masters[:3]]
    vectors, hidden = masters[3:]
    source_pair, target_pair, cross_pair = pairs
    small = gather_small(vectors, hidden)
    quads = gather_whole(attention, up, down)
    table = jnp.arange(source.shape[1] // BLOCK, dtype=jnp.int32)
    two = (table, table)
    parts = [(table, list(quad), 0, QUAD) for quad in quads]
    enc_kept = attend_forward(source_pair, small, 0, source, None, parts[:1], False)
    enc_mid = enc_kept[7]
    enc_feed_kept = feed_forward(small, 5, HIDDEN_ROW, enc_mid, parts[1:3])
    memory = enc_feed_kept[0]
    self_kept = attend_forward(target_pair, small, 8, target, None, parts[3:4], True)
    dec_one = self_kept[7]
    cross_kept = attend_forward(cross_pair, small, 13, dec_one, memory, parts[4:5], False)
    dec_two = cross_kept[7]
    result, two_grad, dec_feed_small, feed_two = feed_both(
        two, small, 18, HIDDEN_ROW + QUAD, dec_two, grad, parts[5:7]
    )
    one_grad, memory_grad, cross_small, cross_q = attend_backward(
        two, cross_pair, small, 13, two_grad, cross_kept, dec_one, memory, parts[4:5], False, None
    )
    target_grad, _, self_small, self_q = attend_backward(
        two, target_pair, small, 8, one_grad, self_kept, target, None, parts[3:4], True, None
    )
    mid_grad, enc_feed_small, feed_one = feed_backward(
        two, small, 5, memory_grad, enc_feed_kept, enc_mid, parts[1:3]
    )
    source_grad, _, enc_small, enc_q = attend_backward(
        two, source_pair, small, 0, mid_grad, enc_kept, source, None, parts[:1], False, None
    )
    quads = [enc_q]
    quads += [[half[:, low : low + QUAD] for half in feed_one] for low in (0, QUAD)]
    quads += [self_q, cross_q]
    quads += [[half[:, low : low + QUAD] for half in feed_two] for low in (0, QUAD)]
    smalls = (enc_small, enc_feed_small, self_small, cross_small, dec_feed_small)
    count = axis_sizes[0] * axis_sizes[1]
    shares = scatter_small(smalls, vectors, hidden, lax.axis_index(AXES), count)
    grads = tuple(scatter_whole(quads)) + shares
    updated = [
        adam_update(
            masters[slot], grads[slot], firsts[slot], seconds[slot], RATES[slot], DECAYS[slot]
        )
        for slot in range(5)
    ]
    flat = [updated[slot][kind] for kind in range(4) for slot in range(5)]
    return (memory, result, source_grad, target_grad), flat


def per_device(
    axis_sizes,
    source_tokens,
    target_tokens,
    source_segments,
    target_segments,
    output_grad,
    attention_weight,
    up_weight,
    down_weight,
    vectors,
    hidden_bias,
    *moments,
):
    masters = (attention_weight, up_weight, down_weight, vectors, hidden_bias)
    firsts = moments[:5]
    seconds = moments[5:]
    width = source_tokens.shape[2]
    pairs = (
        (source_segments, source_segments),
        (target_segments, target_segments),
        (target_segments, source_segments),
    )
    direct = axis_sizes[0] * axis_sizes[1] * BLOCK == width
    tokens, updated = (direct_step if direct else whole_step)(
        pairs,
        source_tokens[0],
        target_tokens[0],
        output_grad[0],
        masters,
        firsts,
        seconds,
        axis_sizes,
    )
    return tuple(array[None] for array in tokens) + tuple(updated)


def solution(mesh):
    rows = P(AXES, None, None)
    line = P(AXES, None)
    matrix = P(None, AXES, None)
    vector = P(None, AXES)
    state = (matrix, matrix, matrix, vector, vector)
    return jax.shard_map(
        functools.partial(per_device, (mesh.shape["dp"], mesh.shape["fsdp"])),
        mesh=mesh,
        in_specs=(rows, rows, line, line, rows) + state * 3,
        out_specs=(rows,) * 4 + state * 4,
        check_vma=False,
    )
```

```python
import functools

import jax
import jax.numpy as jnp
from jax import lax
from jax.experimental import pallas as pl
from jax.experimental.pallas import tpu as pltpu
from jax.sharding import PartitionSpec as P

HEADS = 8
STEP = 10
EPS_NORM = 1e-05
EPS_ADAM = 1e-08
BETA_ONE = 0.9
BETA_TWO = 0.999
LOWEST = -1e30
RATES = (0.05, 0.05, 0.05, 0.3, 0.3)
DECAYS = (0.01, 0.01, 0.01, 0.0, 0.0)
AXES = ("dp", "fsdp")
QUAD = 4
BLOCK = 16
CHUNK = 64
LANES = 128
SMALL_ROWS = 32
VMEM_BYTES = 60 * 1024 * 1024
HIDDEN_ROW = 24
BF = jnp.bfloat16
F32 = jnp.float32
VMEM = pl.BlockSpec(memory_space=pltpu.VMEM)
SMEM = pl.BlockSpec(memory_space=pltpu.SMEM)
ANY = pl.BlockSpec(memory_space=pl.ANY)
ROOT_TWO_PI = 0.7978845608028654
CUBIC = 0.044715


def dot(left, right):
    return jnp.dot(left, right, preferred_element_type=F32)


def dot_nt(left, right):
    return lax.dot_general(left, right, (((1,), (1,)), ((), ())), preferred_element_type=F32)


class Input:
    def __init__(self, array, room, sem):
        self.room = room
        self.shape = room.shape
        self.copy = pltpu.make_async_copy(array, room, sem)
        self.copy.start()
        self.there = False

    def __getitem__(self, where):
        if not self.there:
            self.copy.wait()
            self.there = True
        return self.room[where]


class Output:
    def __init__(self, array, room, sem):
        self.array = array
        self.room = room
        self.shape = room.shape
        self.sem = sem
        self.left = False

    def __getitem__(self, where):
        return self.room[where]

    def __setitem__(self, where, value):
        self.room[where] = value

    def put(self, index=None):
        source = self.room if index is None else self.room.at[index]
        target = self.array if index is None else self.array.at[index]
        pltpu.make_async_copy(source, target, self.sem).start()
        self.left = True

    def finish(self):
        if not self.left:
            self.put()
        pltpu.make_async_copy(self.room, self.array, self.sem).wait()


def staged_kernel(kernel, scalars, inputs, others, outputs, targets, *refs):
    refs = list(refs)
    sems = refs.pop()
    count = inputs + outputs
    rooms = refs[len(refs) - count :]
    refs = refs[: len(refs) - count]
    at = scalars
    for slot in range(inputs):
        refs[at + slot] = Input(refs[at + slot], rooms[slot], sems.at[slot])
    at += inputs + others
    made = []
    for slot in range(inputs, count):
        place = at + slot - inputs
        refs[place] = Output(refs[place], rooms[slot], sems.at[slot])
        made.append(refs[place])
    kernel(*refs)
    for output in made:
        output.finish()


def load_start(part, place, sems):
    table, arrays, low, number = part
    at = 0
    for slot, array in enumerate(arrays):
        for index in range(array.shape[0]):
            source = array.at[index, low : low + number]
            pltpu.make_async_copy(source, place(table[at]), sems.at[slot]).start()
            at += 1


def load_wait(part, sems):
    table, arrays, low, number = part
    for slot, array in enumerate(arrays):
        whole = array.at[:, low : low + number]
        pltpu.make_async_copy(whole, whole, sems.at[slot]).wait()


def store_start(part, place, sems):
    table, arrays, low, number = part
    half = arrays[0].shape[0]
    for index in range(half):
        for slot in (1, 0):
            target = arrays[slot].at[index, low : low + number]
            source = place(table[slot * half + index])
            pltpu.make_async_copy(source, target, sems.at[slot]).start()


def row_place(scratch, low, high):
    def place(block):
        start = pl.multiple_of(block * BLOCK, BLOCK)
        return scratch.at[low:high, pl.ds(start, BLOCK), :]

    return place


def block_place(scratch):
    return lambda block: scratch.at[block]


def column_sum(values):
    rows, width = values.shape
    return jnp.sum(values.reshape(rows // 8, 8, width), axis=0)


def total_of(sums):
    return jnp.sum(functools.reduce(jnp.add, sums), axis=0, keepdims=True)


def norm_forward(pre_of, length, gain, shift, out_ref, hat_ref, rstd_ref):
    for at in range(0, length, CHUNK):
        rows = slice(at, at + CHUNK)
        pre = pre_of(rows)
        mean = jnp.mean(pre, axis=-1, keepdims=True)
        centred = pre - mean
        spread = jnp.mean(centred * centred, axis=-1, keepdims=True)
        rstd = lax.rsqrt(spread + EPS_NORM)
        hat = centred * rstd
        hat_ref[rows] = hat
        rstd_ref[rows] = jnp.broadcast_to(rstd, (CHUNK, LANES))
        out_ref[rows] = hat * gain + shift
    for ref in (hat_ref, rstd_ref, out_ref):
        if isinstance(ref, Output):
            ref.put()


def norm_backward(grad_ref, hat_ref, rstd_ref, gain, pre_out, low_out):
    length = grad_ref.shape[0]
    sums = ([], [], [])
    for at in range(0, length, CHUNK):
        rows = slice(at, at + CHUNK)
        grad = grad_ref[rows].astype(F32)
        hat = hat_ref[rows]
        sums[0].append(column_sum(grad * hat))
        sums[1].append(column_sum(grad))
        scaled = grad * gain
        one = jnp.mean(scaled, axis=-1, keepdims=True)
        two = jnp.mean(scaled * hat, axis=-1, keepdims=True)
        pre = rstd_ref[rows][:, :1] * (scaled - one - hat * two)
        low = pre.astype(BF)
        pre_out[rows] = pre
        low_out[rows] = low
        sums[2].append(column_sum(low.astype(F32)))
    return [total_of(each) for each in sums]


def lane_mask(rows):
    return lax.broadcasted_iota(jnp.int32, (rows, LANES), 1) < LANES // 2


def stacked_pair(block):
    first = lane_mask(block.shape[0])
    zero = jnp.zeros_like(block)
    return jnp.concatenate([jnp.where(first, block, zero), jnp.where(first, zero, block)], axis=0)


def merged_pair(stacked):
    rows = stacked.shape[0] // 2
    return jnp.where(lane_mask(rows), stacked[:rows], stacked[rows:])


def mask_fill(bias_ref, column_seg, row_seg, causal, transposed):
    length = bias_ref.shape[0]
    column = jnp.broadcast_to(column_seg, (LANES, length)).T
    for at in range(0, length, LANES):
        same = column == row_seg[:, at : at + LANES]
        if causal:
            down = lax.broadcasted_iota(jnp.int32, (length, LANES), 0)
            along = lax.broadcasted_iota(jnp.int32, (length, LANES), 1) + at
            order = (down <= along) if transposed else (along <= down)
            same = same & order
        bias_ref[:, at : at + LANES] = jnp.where(same, 0.0, LOWEST)


def take_parts(refs, layout, tables):
    parts = []
    for slot, (arrays, low, number) in enumerate(layout):
        parts.append((tables[slot], [refs.pop(0) for _ in range(arrays)], low, number))
    return parts


def small_part(part):
    table, arrays, low, number = part
    return table, arrays, low + number, 1


def small_join(blocks_ref):
    count = blocks_ref.shape[0]
    groups = blocks_ref.shape[3] // LANES
    per = count // groups
    vectors = []
    hidden = [[], []]
    for group in range(groups):
        total = blocks_ref[group * per, 0, :8].astype(F32)
        for at in range(group * per + 1, (group + 1) * per):
            total = total + blocks_ref[at, 0, :8].astype(F32)
        columns = [total[:, at : at + LANES] for at in range(0, 4 * LANES, LANES)]
        vectors.append(jnp.concatenate(columns[:3], axis=0))
        for layer in range(2):
            rows = [columns[3][4 * layer + at : 4 * layer + at + 1] for at in range(4)]
            hidden[layer].append(jnp.concatenate(rows, axis=1))
    return jnp.concatenate([jnp.concatenate(vectors, axis=1)] + hidden[0] + hidden[1], axis=0)


def small_split(whole, group):
    lanes = slice(group * LANES, (group + 1) * LANES)
    columns = [whole[at : at + 8, lanes] for at in (0, 8, 16)]
    rows = []
    for layer in range(2):
        row = whole[24 + 4 * layer + group : 25 + 4 * layer + group]
        rows += [row[:, at : at + LANES] for at in range(0, 4 * LANES, LANES)]
    columns.append(jnp.concatenate(rows, axis=0))
    block = jnp.concatenate(columns, axis=1)
    return jnp.concatenate([block, jnp.zeros_like(block)], axis=0).astype(BF)


def attend_forward_kernel(layout, cross, causal, base, joins, *refs):
    refs = list(refs)
    tables = [refs.pop(0) for _ in layout]
    query_seg = refs.pop(0)
    key_seg = refs.pop(0)
    small = None if joins else refs.pop(0)
    rows_ref = refs.pop(0)
    memory_ref = refs.pop(0) if cross else None
    parts = take_parts(refs, layout, tables)
    q_ref, k_ref, v_ref, o_ref, lse_ref, hat_ref, rstd_ref, out_ref = [refs.pop(0) for _ in range(8)]
    if joins:
        small = refs.pop(0)
        blocks_ref = refs.pop()
        extra = small_part(parts[-1])
    w_ref, bias_ref, scores_ref, exponent_ref, largest_ref, mixed_ref, attended_ref, sems = refs
    first = 0
    if joins:
        load_start(extra, lambda block: blocks_ref.at[block], sems.at[len(parts)])
    for slot, part in enumerate(parts):
        load_start(part, row_place(w_ref, first, first + part[3]), sems.at[slot])
        first += part[3]
    length, width = rows_ref.shape
    mask_fill(bias_ref, query_seg[...], key_seg[...], causal, False)
    rows = rows_ref[...].astype(BF)
    keys = memory_ref[...].astype(BF) if cross else rows
    if joins:
        load_wait(extra, sems.at[len(parts)])
        small[...] = small_join(blocks_ref)
        small.put()
    for slot, part in enumerate(parts):
        load_wait(part, sems.at[slot])
    scale = (width // HEADS) ** (-0.5)
    q_ref[...] = (dot(rows, w_ref[0]) + small[base : base + 1]).astype(BF) * jnp.asarray(scale, BF)
    k_ref[...] = dot(keys, w_ref[1]).astype(BF)
    v_ref[...] = (dot(keys, w_ref[2]) + small[base + 1 : base + 2]).astype(BF)
    for ref in (q_ref, k_ref, v_ref):
        ref.put()
    lane = lax.broadcasted_iota(jnp.int32, (LANES, LANES), 1)
    logs = [jnp.zeros((LANES, LANES), F32)] * (length // LANES)
    for pair in range(HEADS // 2):
        lanes = slice(pair * LANES, (pair + 1) * LANES)
        side = pair % 2
        scores_ref[side] = dot_nt(stacked_pair(q_ref[:, lanes]), k_ref[:, lanes])
        for at in range(0, 2 * length, CHUNK):
            chunk = slice(at, at + CHUNK)
            own = slice(at % length, at % length + CHUNK)
            reach = own.start // LANES * LANES + LANES if causal else length
            scores = scores_ref[side, chunk, :reach] + bias_ref[own, :reach]
            largest = jnp.max(scores, axis=-1, keepdims=True)
            exponent_ref[side, chunk, :reach] = jnp.exp(scores - largest).astype(BF)
            if reach < length:
                exponent_ref[side, chunk, reach:] = jnp.zeros((CHUNK, length - reach), BF)
            largest_ref[side, chunk] = jnp.broadcast_to(largest, (CHUNK, LANES))
        values = jnp.concatenate([v_ref[:, lanes], jnp.ones((length, LANES), BF)], axis=1)
        mixed_ref[side] = dot(exponent_ref[side], values)
        for slot, at in enumerate(range(0, length, LANES)):
            outs = []
            for half in range(2):
                chunk = slice(half * length + at, half * length + at + LANES)
                total = mixed_ref[side, chunk, LANES:]
                outs.append(mixed_ref[side, chunk, :LANES] / total)
                log_total = largest_ref[side, chunk] + jnp.log(total)
                logs[slot] = jnp.where(lane == 2 * pair + half, log_total, logs[slot])
            o_ref[at : at + LANES, lanes] = jnp.where(lane_mask(LANES), outs[0], outs[1]).astype(BF)
    for slot, at in enumerate(range(0, length, LANES)):
        lse_ref[:, at : at + LANES] = logs[slot].T[:HEADS]
    o_ref.put()
    lse_ref.put()
    attended_ref[...] = dot(o_ref[...], w_ref[3])
    out_bias = small[base + 2 : base + 3]
    norm_forward(
        lambda rows: rows_ref[rows].astype(F32) + (attended_ref[rows] + out_bias),
        length,
        small[base + 3 : base + 4],
        small[base + 4 : base + 5],
        out_ref,
        hat_ref,
        rstd_ref,
    )


def attend_backward_kernel(layout, cross, causal, base, splits, *refs):
    refs = list(refs)
    tables = [refs.pop(0) for _ in layout]
    out_tables = [refs.pop(0), refs.pop(0)]
    query_seg = refs.pop(0)
    key_seg = refs.pop(0)
    small = refs.pop(0)
    grad_ref = refs.pop(0)
    hat_ref, rstd_ref = refs.pop(0), refs.pop(0)
    rows_ref = refs.pop(0)
    memory_ref = refs.pop(0) if cross else None
    q_ref, k_ref, v_ref, o_ref, lse_ref = [refs.pop(0) for _ in range(5)]
    others = [refs.pop(0) for _ in range(4)] if splits else None
    parts = take_parts(refs, layout, tables)
    rows_out = refs.pop(0)
    memory_out = refs.pop(0) if cross else None
    small_out = None if splits else refs.pop(0)
    targets = [refs.pop(0), refs.pop(0)]
    outs = []
    for slot, table in enumerate(out_tables):
        outs.append((table, targets, slot * QUAD // 2, QUAD // 2))
    blocks_ref = refs.pop() if splits else None
    w_ref, dw_ref, bias_ref, dout_ref, dq_t_ref, dk_ref, dv_ref, kt_ref = refs[:8]
    low_ref, scores_ref, prob_grad_ref, prob_ref, score_grad_ref, sems = refs[8:]
    first = 0
    for slot, part in enumerate(parts):
        load_start(part, row_place(w_ref, first, first + part[3]), sems.at[slot])
        first += part[3]
    length, width = rows_ref.shape
    head = width // HEADS
    scale = head ** (-0.5)
    gain_grad, shift_grad, out_bias = norm_backward(
        grad_ref, hat_ref, rstd_ref, small[base + 3 : base + 4], rows_out, low_ref
    )
    mask_fill(bias_ref, key_seg[...], query_seg[...], causal, True)
    low = low_ref[...]
    for slot, part in enumerate(parts):
        load_wait(part, sems.at[slot])
    dout_ref[...] = dot_nt(low, w_ref[3]).astype(BF)
    dw_ref[3] = dot(o_ref[...].T, low).astype(BF)
    product = dout_ref[...].astype(F32) * o_ref[...].astype(F32)
    high = product.astype(BF)
    rest = (product - high.astype(F32)).astype(BF)
    picker = lax.broadcasted_iota(jnp.int32, (BLOCK, width), 1) // head
    picker = (picker == lax.broadcasted_iota(jnp.int32, (BLOCK, width), 0)).astype(BF)
    row_dots = dot_nt(picker, high) + dot_nt(picker, rest)
    kt_ref[...] = k_ref[...].T
    for pair in range(HEADS // 2):
        lanes = slice(pair * LANES, (pair + 1) * LANES)
        side = pair % 2
        query = q_ref[:, lanes]
        dout = dout_ref[:, lanes]
        scores_ref[side] = dot_nt(stacked_pair(k_ref[:, lanes]), query)
        prob_grad_ref[side] = dot_nt(stacked_pair(v_ref[:, lanes]), dout)
        for at in range(0, 2 * length, CHUNK):
            which = 2 * pair + at // length
            chunk = slice(at, at + CHUNK)
            own = slice(at % length, at % length + CHUNK)
            begin = own.start // LANES * LANES if causal else 0
            shift = bias_ref[own, begin:] - lse_ref[which : which + 1, begin:]
            prob = jnp.exp(scores_ref[side, chunk, begin:] + shift)
            prob_ref[side, chunk, begin:] = prob.astype(BF)
            centred = prob_grad_ref[side, chunk, begin:] - row_dots[which : which + 1, begin:]
            score_grad_ref[side, chunk, begin:] = (prob * centred).astype(BF)
            if begin:
                prob_ref[side, chunk, :begin] = jnp.zeros((CHUNK, begin), BF)
                score_grad_ref[side, chunk, :begin] = jnp.zeros((CHUNK, begin), BF)
        dv_ref[:, lanes] = merged_pair(dot(prob_ref[side], dout)).astype(BF)
        dk_ref[:, lanes] = merged_pair(dot(score_grad_ref[side], query)).astype(BF)
        for half in range(2):
            at = pair * LANES + half * head
            own = slice(half * length, (half + 1) * length)
            dq_t_ref[at : at + head, :] = dot(kt_ref[at : at + head, :], score_grad_ref[side, own])
    query_grad = (dq_t_ref[...] * scale).T.astype(BF)
    key_grad = dk_ref[...]
    value_grad = dv_ref[...]
    turned = rows_ref[...].astype(BF).T
    other = memory_ref[...].astype(BF).T if cross else turned
    dw_ref[2] = dot(other, value_grad).astype(BF)
    store_start(outs[1], row_place(dw_ref, QUAD // 2, QUAD), sems.at[1])
    dw_ref[0] = dot(turned, query_grad).astype(BF)
    dw_ref[1] = dot(other, key_grad).astype(BF)
    store_start(outs[0], row_place(dw_ref, 0, QUAD // 2), sems.at[0])
    rows_back = rows_out[...] + dot_nt(query_grad, w_ref[0])
    memory_back = dot_nt(key_grad, w_ref[1]) + dot_nt(value_grad, w_ref[2])
    if cross:
        rows_out[...] = rows_back
        memory_out[...] = memory_back
        memory_out.put()
    else:
        rows_out[...] = rows_back + memory_back
    rows_out.put()
    query_bias = total_of([column_sum(query_grad.astype(F32))])
    value_bias = total_of([column_sum(value_grad.astype(F32))])
    spare = jnp.zeros((3, width), F32)
    own = jnp.concatenate(
        [query_bias, value_bias, out_bias, gain_grad, shift_grad, spare], axis=0
    )
    if splits:
        enc_feed, self_attend, cross_attend, dec_feed = [other[...] for other in others]
        whole = small_rows(own, enc_feed, self_attend, cross_attend, dec_feed)
        groups = blocks_ref.shape[0]
        for group in range(groups):
            blocks_ref[group, 0] = small_split(whole, group)
        extra = small_part(outs[-1])
        per = 2 * extra[1][0].shape[0] // groups
        store_start(extra, lambda block: blocks_ref.at[block // per], sems.at[2])
        load_wait(extra, sems.at[2])
    else:
        small_out[...] = own
    for slot, part in enumerate(outs):
        load_wait(part, sems.at[slot])


def small_rows(enc_attend, enc_feed, self_attend, cross_attend, dec_feed):
    return jnp.concatenate(
        [
            enc_attend[:5],
            enc_feed[:3],
            self_attend[:5],
            cross_attend[:5],
            dec_feed[:3],
            dec_feed[7:],
            dec_feed[7:],
            dec_feed[7:],
            enc_feed[3:7],
            dec_feed[3:7],
        ],
        axis=0,
    )


def gelu_parts(pre):
    square = pre * pre
    curve = jnp.tanh(ROOT_TWO_PI * pre * (1.0 + CUBIC * square))
    half = 0.5 * pre
    rise = 0.5 + 0.5 * curve
    bend = ROOT_TWO_PI * (1.0 + 3.0 * CUBIC * square)
    return pre * rise, rise + half * (1.0 - curve * curve) * bend


def chunk_of(ref, index):
    number = ref.shape[0] // QUAD
    part = ref[index * number : (index + 1) * number]
    return part.reshape(number * ref.shape[1] * ref.shape[2], ref.shape[3])


def feed_forward_steps(small, base, hidden_at, rows_ref, up_ref, down_ref, active_ref, slope_ref, pre_ref, sum_ref):
    rows = rows_ref[...].astype(BF)
    length = rows.shape[0]
    for index in range(QUAD):
        at = hidden_at + index
        side = index % 2
        pre_ref[side] = dot(rows, up_ref[index])
        bias = small[at : at + 1]
        for at in range(0, length, CHUNK // 2):
            chunk = slice(at, at + CHUNK // 2)
            active, slope = gelu_parts(pre_ref[side, chunk] + bias)
            active_ref[index, chunk] = active.astype(BF)
            slope_ref[index, chunk] = slope
        for ref in (active_ref, slope_ref):
            if isinstance(ref, Output):
                ref.put(index)
    wide = jnp.concatenate([active_ref[index] for index in range(QUAD)], axis=1)
    number, _, _, width = down_ref.shape
    sum_ref[...] = dot(wide, down_ref[...].reshape(QUAD * width, width))
    out_bias = small[base : base + 1]
    return lambda rows: rows_ref[rows] + (sum_ref[rows] + out_bias)


def feed_backward_steps(
    pre_grad, low_ref, rows_ref, up_ref, down_ref, active_ref, slope_ref, dup_ref, ddown_ref, rows_out, back_ref, outs, sems
):
    low = low_ref[...]
    length = low.shape[0]
    number = ddown_ref.shape[0] // QUAD
    for index in range(QUAD):
        down_grad = dot(active_ref[index].T, low).astype(BF)
        ddown_ref[index * number : (index + 1) * number] = down_grad.reshape(
            (number,) + ddown_ref.shape[1:]
        )
    store_start(outs[1], block_place(ddown_ref), sems.at[1])
    turned = rows_ref[...].astype(BF).T
    hidden_grads = []
    hiddens = []
    for index in range(QUAD):
        side = index % 2
        back_ref[side] = dot_nt(low, chunk_of(down_ref, index))
        sums = []
        parts = []
        for at in range(0, length, CHUNK):
            chunk = slice(at, at + CHUNK)
            hidden = (back_ref[side, chunk] * slope_ref[index, chunk]).astype(BF)
            sums.append(column_sum(hidden.astype(F32)))
            parts.append(hidden)
        hidden = jnp.concatenate(parts, axis=0)
        hidden_grads.append(total_of(sums))
        dup_ref[index] = dot(turned, hidden).astype(BF)
        hiddens.append(hidden)
    store_start(outs[0], row_place(dup_ref, 0, QUAD), sems.at[0])
    total = pre_grad[...]
    for index in range(QUAD):
        total = total + dot_nt(hiddens[index], up_ref[index])
    rows_out[...] = total
    rows_out.put()
    return hidden_grads


def load_feed(parts, up_ref, down_ref, sems):
    load_start(parts[0], row_place(up_ref, 0, QUAD), sems.at[0])
    load_start(parts[1], block_place(down_ref), sems.at[1])


def wait_feed(parts, sems):
    for slot, part in enumerate(parts):
        load_wait(part, sems.at[slot])


def feed_outs(refs, tables):
    arrays = [refs.pop(0), refs.pop(0)]
    return [(tables[slot], arrays, slot * QUAD, QUAD) for slot in range(2)]


def feed_small(out_bias, gain_grad, shift_grad, hidden_grads):
    spare = jnp.zeros_like(out_bias)
    return jnp.concatenate([out_bias, gain_grad, shift_grad] + hidden_grads + [spare], axis=0)


def feed_forward_kernel(layout, base, hidden_at, *refs):
    refs = list(refs)
    tables = [refs.pop(0), refs.pop(0)]
    small, rows_ref = refs.pop(0), refs.pop(0)
    parts = take_parts(refs, layout, tables)
    out_ref, hat_ref, rstd_ref, active_ref, slope_ref, up_ref, down_ref = refs[:7]
    pre_ref, sum_ref, sems = refs[7:]
    load_feed(parts, up_ref, down_ref, sems)
    wait_feed(parts, sems)
    pre_of = feed_forward_steps(
        small, base, hidden_at, rows_ref, up_ref, down_ref, active_ref, slope_ref, pre_ref, sum_ref
    )
    gain, shift = small[base + 1 : base + 2], small[base + 2 : base + 3]
    norm_forward(pre_of, rows_ref.shape[0], gain, shift, out_ref, hat_ref, rstd_ref)


def feed_backward_kernel(layout, base, *refs):
    refs = list(refs)
    tables = [refs.pop(0), refs.pop(0)]
    out_tables = [refs.pop(0), refs.pop(0)]
    small, grad_ref, hat_ref, rstd_ref, rows_ref = [refs.pop(0) for _ in range(5)]
    active_ref, slope_ref = refs.pop(0), refs.pop(0)
    parts = take_parts(refs, layout, tables)
    rows_out, small_out = refs.pop(0), refs.pop(0)
    outs = feed_outs(refs, out_tables)
    up_ref, down_ref, dup_ref, ddown_ref, low_ref, back_ref, sems, out_sems = refs
    load_feed(parts, up_ref, down_ref, sems)
    gain_grad, shift_grad, out_bias = norm_backward(
        grad_ref, hat_ref, rstd_ref, small[base + 1 : base + 2], rows_out, low_ref
    )
    wait_feed(parts, sems)
    hidden_grads = feed_backward_steps(
        rows_out,
        low_ref,
        rows_ref,
        up_ref,
        down_ref,
        active_ref,
        slope_ref,
        dup_ref,
        ddown_ref,
        rows_out,
        back_ref,
        outs,
        out_sems,
    )
    small_out[...] = feed_small(out_bias, gain_grad, shift_grad, hidden_grads)
    wait_feed(outs, out_sems)


def feed_both_kernel(layout, base, hidden_at, *refs):
    refs = list(refs)
    tables = [refs.pop(0), refs.pop(0)]
    out_tables = [refs.pop(0), refs.pop(0)]
    small, rows_ref, grad_ref = [refs.pop(0) for _ in range(3)]
    parts = take_parts(refs, layout, tables)
    out_ref, rows_out, small_out = [refs.pop(0) for _ in range(3)]
    outs = feed_outs(refs, out_tables)
    up_ref, down_ref, dup_ref, ddown_ref, low_ref, back_ref, sum_ref = refs[:7]
    active_ref, slope_ref, hat_ref, rstd_ref, sems, out_sems = refs[7:]
    load_feed(parts, up_ref, down_ref, sems)
    wait_feed(parts, sems)
    pre_of = feed_forward_steps(
        small, base, hidden_at, rows_ref, up_ref, down_ref, active_ref, slope_ref, back_ref, sum_ref
    )
    gain, shift = small[base + 1 : base + 2], small[base + 2 : base + 3]
    norm_forward(pre_of, rows_ref.shape[0], gain, shift, out_ref, hat_ref, rstd_ref)
    gain_grad, shift_grad, out_bias = norm_backward(
        grad_ref, hat_ref, rstd_ref, gain, rows_out, low_ref
    )
    hidden_grads = feed_backward_steps(
        rows_out,
        low_ref,
        rows_ref,
        up_ref,
        down_ref,
        active_ref,
        slope_ref,
        dup_ref,
        ddown_ref,
        rows_out,
        back_ref,
        outs,
        out_sems,
    )
    small_out[...] = feed_small(out_bias, gain_grad, shift_grad, hidden_grads)
    wait_feed(outs, out_sems)


def shaped(shape, dtype=F32):
    return jax.ShapeDtypeStruct(shape, dtype)


def call(
    kernel, scalars, inputs, others, outs, targets, scratch, flops, moved, limit=VMEM_BYTES
):
    rooms = [pltpu.VMEM(array.shape, array.dtype) for array in list(inputs) + list(outs)]
    return pl.pallas_call(
        functools.partial(
            staged_kernel, kernel, len(scalars), len(inputs), len(others), len(outs), len(targets)
        ),
        out_shape=list(outs) + list(targets),
        in_specs=[SMEM] * len(scalars) + [ANY] * (len(inputs) + len(others)),
        out_specs=[ANY] * (len(outs) + len(targets)),
        scratch_shapes=scratch + rooms + [pltpu.SemaphoreType.DMA((len(rooms),))],
        cost_estimate=pl.CostEstimate(flops=flops, bytes_accessed=moved, transcendentals=0),
        compiler_params=pltpu.CompilerParams(vmem_limit_bytes=limit),
    )(*scalars, *inputs, *others)


def layout_of(parts):
    return [(len(arrays), low, number) for _, arrays, low, number in parts]


def arrays_of(parts):
    return [array for part in parts for array in part[1]]


def most(parts):
    return max(len(part[1]) for part in parts)


def halves(width, number):
    return [shaped((width // BLOCK // 2, number, BLOCK, width), BF)] * 2


def attend_forward(segments, small, base, rows, memory, parts, causal):
    length, width = rows.shape
    cross = memory is not None
    joins = small is None
    scalars = [part[0] for part in parts]
    inputs = list(segments) + ([] if joins else [small]) + [rows] + ([memory] if cross else [])
    outs = [shaped((length, width), BF)] * 4 + [shaped((HEADS, length))]
    outs += [shaped((length, width)), shaped((length, LANES)), shaped((length, width))]
    outs += [shaped((SMALL_ROWS, width))] if joins else []
    scratch = [
        pltpu.VMEM((QUAD, width, width), BF),
        pltpu.VMEM((length, length), F32),
        pltpu.VMEM((2, 2 * length, length), F32),
        pltpu.VMEM((2, 2 * length, length), BF),
        pltpu.VMEM((2, 2 * length, LANES), F32),
        pltpu.VMEM((2, 2 * length, 2 * LANES), F32),
        pltpu.VMEM((length, width), F32),
        pltpu.SemaphoreType.DMA((len(parts) + 1, most(parts))),
    ]
    scratch += [pltpu.VMEM((width // BLOCK, 1, BLOCK, width), BF)] if joins else []
    kernel = functools.partial(attend_forward_kernel, layout_of(parts), cross, causal, base, joins)
    flops = 8 * length * width * width + 16 * length * length * width
    return call(kernel, scalars, inputs, arrays_of(parts), outs, [], scratch, flops, 8_000_000)


def attend_backward(
    out_tables, segments, small, base, grad, kept, rows, memory, parts, causal, others
):
    length, width = rows.shape
    cross = memory is not None
    splits = others is not None
    q, k, v, o, lse, hat, rstd = kept[:7]
    scalars = [part[0] for part in parts] + list(out_tables)
    inputs = list(segments) + [small, grad, hat, rstd, rows]
    inputs += ([memory] if cross else []) + [q, k, v, o, lse] + list(others or ())
    outs = [shaped((length, width))] * (2 if cross else 1)
    outs += [] if splits else [shaped((8, width))]
    targets = halves(width, QUAD + (1 if splits else 0))
    scratch = [
        pltpu.VMEM((QUAD, width, width), BF),
        pltpu.VMEM((QUAD, width, width), BF),
        pltpu.VMEM((length, length), F32),
        pltpu.VMEM((length, width), BF),
        pltpu.VMEM((width, length), F32),
        pltpu.VMEM((length, width), BF),
        pltpu.VMEM((length, width), BF),
        pltpu.VMEM((width, length), BF),
        pltpu.VMEM((length, width), BF),
        pltpu.VMEM((2, 2 * length, length), F32),
        pltpu.VMEM((2, 2 * length, length), F32),
        pltpu.VMEM((2, 2 * length, length), BF),
        pltpu.VMEM((2, 2 * length, length), BF),
        pltpu.SemaphoreType.DMA((3, 2)),
    ]
    scratch += [pltpu.VMEM((width // LANES, 1, BLOCK, width), BF)] if splits else []
    kernel = functools.partial(
        attend_backward_kernel, layout_of(parts), cross, causal, base, splits
    )
    flops = 16 * length * width * width + 40 * length * length * width
    arrays = arrays_of(parts)
    results = list(call(kernel, scalars, inputs, arrays, outs, targets, scratch, flops, 12_000_000))
    rows_grad = results.pop(0)
    memory_grad = results.pop(0) if cross else None
    small_grad = None if splits else results.pop(0)
    return rows_grad, memory_grad, small_grad, results


def feed_scratch(width, grads):
    number = width // BLOCK
    once = [pltpu.VMEM((QUAD, width, width), BF), pltpu.VMEM((number, QUAD, BLOCK, width), BF)]
    return once * (2 if grads else 1)


def feed_forward(small, base, hidden_at, rows, parts):
    length, width = rows.shape
    scalars = [part[0] for part in parts]
    outs = [shaped((length, width)), shaped((length, width)), shaped((length, LANES))]
    outs += [shaped((QUAD, length, width), BF), shaped((QUAD, length, width))]
    scratch = feed_scratch(width, False)
    scratch += [pltpu.VMEM((2, length, width), F32), pltpu.VMEM((length, width), F32)]
    scratch += [pltpu.SemaphoreType.DMA((2, most(parts)))]
    kernel = functools.partial(feed_forward_kernel, layout_of(parts), base, hidden_at)
    flops = 16 * length * width * width
    arrays = arrays_of(parts)
    return call(kernel, scalars, [small, rows], arrays, outs, [], scratch, flops, 10_000_000)


def feed_backward(out_tables, small, base, grad, kept, rows, parts):
    length, width = rows.shape
    hat, rstd, active, slope = kept[1:]
    scalars = [part[0] for part in parts] + list(out_tables)
    inputs = [small, grad, hat, rstd, rows, active, slope]
    outs = [shaped((length, width)), shaped((8, width))]
    targets = halves(width, 2 * QUAD)
    scratch = feed_scratch(width, True)
    scratch += [pltpu.VMEM((length, width), BF), pltpu.VMEM((2, length, width), F32)]
    scratch += [pltpu.SemaphoreType.DMA((2, most(parts))), pltpu.SemaphoreType.DMA((2, 2))]
    kernel = functools.partial(feed_backward_kernel, layout_of(parts), base)
    flops = 32 * length * width * width
    arrays = arrays_of(parts)
    results = call(kernel, scalars, inputs, arrays, outs, targets, scratch, flops, 14_000_000)
    return results[0], results[1], results[2:4]


def feed_both(out_tables, small, base, hidden_at, rows, grad, parts):
    length, width = rows.shape
    scalars = [part[0] for part in parts] + list(out_tables)
    outs = [shaped((length, width)), shaped((length, width)), shaped((8, width))]
    targets = halves(width, 2 * QUAD)
    scratch = feed_scratch(width, True) + [
        pltpu.VMEM((length, width), BF),
        pltpu.VMEM((2, length, width), F32),
        pltpu.VMEM((length, width), F32),
        pltpu.VMEM((QUAD, length, width), BF),
        pltpu.VMEM((QUAD, length, width), F32),
        pltpu.VMEM((length, width), F32),
        pltpu.VMEM((length, LANES), F32),
        pltpu.SemaphoreType.DMA((2, most(parts))),
        pltpu.SemaphoreType.DMA((2, 2)),
    ]
    kernel = functools.partial(feed_both_kernel, layout_of(parts), base, hidden_at)
    flops = 48 * length * width * width
    arrays = arrays_of(parts)
    results = call(kernel, scalars, [small, rows, grad], arrays, outs, targets, scratch, flops, 12_000_000)
    return results[0], results[1], results[2], results[3:5]


def first_kernel(
    at_ref,
    vector_ref,
    hidden_ref,
    square_ref,
    tall_ref,
    deep_ref,
    one_ref,
    two_ref,
    turn_ref,
    line_ref,
):
    at = at_ref[0]
    width = square_ref.shape[2]
    turn_ref[...] = jnp.zeros_like(turn_ref)
    lanes, rows = vector_ref.shape
    turn_ref[pl.ds(pl.multiple_of(at * lanes, lanes), lanes), :rows] = vector_ref[...]
    upright = turn_ref[...].T
    line_ref[...] = jnp.zeros_like(line_ref)
    layers, lanes = hidden_ref.shape
    per = LANES // lanes
    for layer in range(layers):
        row = jnp.concatenate([hidden_ref[layer : layer + 1]] * per, axis=1)
        lane = lax.broadcasted_iota(jnp.int32, row.shape, 1) // lanes
        row = jnp.where(lane == at % per, row, 0.0)
        line_ref[pl.ds(4 * layer + at // per, 1), :] = row
    columns = [upright[low : low + 8] for low in (0, 8, 16)] + [line_ref[...]]
    block = jnp.concatenate(columns, axis=1)
    small = jnp.concatenate([block, jnp.zeros_like(block)], axis=0)
    tall = []
    deep = []
    for layer in range(2):
        for index in range(QUAD):
            lanes = slice(index * width, (index + 1) * width)
            tall.append(tall_ref[layer, :, lanes])
            deep.append(deep_ref[layer, index * BLOCK : (index + 1) * BLOCK])
    square = [square_ref[index] for index in range(3 * QUAD)]
    cut = QUAD // 2
    groups = [
        square[:cut] + tall[:QUAD] + square[cut:QUAD] + [small] + deep[:QUAD],
        square[QUAD : 2 * QUAD] + tall[QUAD:] + square[2 * QUAD :] + deep[QUAD:],
    ]
    for out_ref, group in zip((one_ref, two_ref), groups):
        for slot, block in enumerate(group):
            out_ref[0, slot] = block.astype(BF)
        out_ref.put()


def first_arrays(at, square, tall, deep, vectors, hidden):
    width = square.shape[2]
    outs = [
        shaped((1, 3 * QUAD + 1, BLOCK, width), BF),
        shaped((1, 4 * QUAD, BLOCK, width), BF),
    ]
    scratch = [pltpu.VMEM((LANES, LANES), F32), pltpu.VMEM((8, LANES), F32)]
    inputs = [vectors.T, hidden, square, tall, deep]
    return call(first_kernel, [at], inputs, [], outs, [], scratch, 0, 4_000_000)


def last_kernel(plan, count, at_ref, *refs):
    masters, firsts, seconds = refs[:5], refs[5:10], refs[10:15]
    arrays, refs = refs[15 : 15 + count], refs[15 + count :]
    outs, refs = [refs[5 * kind : 5 * kind + 5] for kind in range(4)], refs[20:]
    buffers, turn_ref, line_ref, sems = refs
    at = at_ref[0]
    starts = []
    for width, pieces, _ in plan:
        for index, low in pieces:
            array = arrays[index]
            array = array if len(array.shape) == 3 else array.at[0]
            source = array.at[low : low + width]
            copy = pltpu.make_async_copy(source, buffers.at[len(starts), :width], sems.at[len(starts)])
            copy.start()
            starts.append(copy)

    def update(slot, where, gradient):
        results = adam_update(
            masters[slot][where],
            gradient,
            firsts[slot][where],
            seconds[slot][where],
            RATES[slot],
            DECAYS[slot],
        )
        for kind in range(4):
            outs[kind][slot][where] = results[kind]

    begin = 0
    left = len(plan)
    for width, pieces, targets in plan:
        for index in range(len(pieces)):
            starts[begin + index].wait()
        for sub, (slot, where) in enumerate(targets):
            gradient = buffers[begin, sub].astype(F32)
            for index in range(1, len(pieces)):
                gradient = gradient + buffers[begin + index, sub].astype(F32)
            if slot < 3:
                update(slot, where, gradient)
                continue
            turn_ref[...] = jnp.zeros_like(turn_ref)
            for column in range(3):
                lanes = slice(column * LANES, (column + 1) * LANES)
                turn_ref[8 * column : 8 * column + 8, :] = gradient[:8, lanes]
            turn_ref[...] = turn_ref[...].T
            lanes, rows = masters[3].shape
            share = turn_ref[pl.ds(pl.multiple_of(at * lanes, lanes), lanes), :][:, :rows]
            update(3, slice(None), share)
            line_ref[...] = gradient[:8, 3 * LANES :]
            layers, lanes = masters[4].shape
            per = LANES // lanes
            for layer in range(layers):
                row = line_ref[pl.ds(4 * layer + at // per, 1), :]
                share = row[:, :lanes]
                for part in range(1, per):
                    other = row[:, part * lanes : (part + 1) * lanes]
                    share = jnp.where(at % per == part, other, share)
                update(4, slice(layer, layer + 1), share)
        begin += len(pieces)
        left -= 1
        for slot in range(5):
            ends = [at for at, (_, _, each) in enumerate(plan) if any(to[0] in used(slot) for to in each)]
            if ends[-1] == len(plan) - 1 - left:
                for kind in range(4):
                    outs[kind][slot].put()


def used(slot):
    return (3,) if slot > 2 else (slot,)


def last_update(at, segments, masters, firsts, seconds):
    arrays = []
    plan = []
    for width, pieces, targets in segments:
        entry = []
        for array, low in pieces:
            found = [place for place, other in enumerate(arrays) if other is array]
            if not found:
                arrays.append(array)
            entry.append((found[0] if found else len(arrays) - 1, low))
        plan.append((width, entry, targets))
    params = [list(group) for group in (masters, firsts, seconds)]
    for group in params:
        group[3] = group[3].T
    flat = params[0] + params[1] + params[2]
    outs = [shaped(array.shape) for array in params[0]] * 3
    outs += [shaped(array.shape, BF) for array in params[0]]
    pieces = sum(len(entry[1]) for entry in plan)
    block = masters[0].shape[1:]
    scratch = [
        pltpu.VMEM((pieces, max(entry[0] for entry in plan)) + block, BF),
        pltpu.VMEM((LANES, LANES), F32),
        pltpu.VMEM((8, LANES), F32),
        pltpu.SemaphoreType.DMA((pieces,)),
    ]
    kernel = functools.partial(last_kernel, plan, len(arrays))
    results = call(
        kernel, [at], flat, arrays, outs, [], scratch, 0, 8_000_000, VMEM_BYTES // 2
    )
    results = list(results)
    for kind in range(4):
        results[5 * kind + 3] = results[5 * kind + 3].T
    return results


def tie(*arrays):
    return lax.optimization_barrier(arrays)


class Direct:
    def __init__(self, axis_sizes):
        outer, inner = axis_sizes
        self.count = outer * inner
        inner_bits = inner.bit_length() - 1
        bits = self.count.bit_length() - 1
        core = [inner_bits]
        across = list(range(inner_bits + 1, bits))
        up = [0]
        along = list(range(1, inner_bits))
        self.orders = {
            "a": core + across + up + along,
            "b": core + up + across + along,
        }
        self.place = lax.axis_index(AXES)

    def hop(self, array, bit):
        return lax.ppermute(array, AXES, [(at, at ^ (1 << bit)) for at in range(self.count)])

    def table(self, name):
        order = self.orders[name]
        index = jnp.arange(self.count, dtype=jnp.int32)
        block = jnp.zeros_like(index)
        for at, bit in enumerate(order):
            block = block | (((index >> (len(order) - 1 - at)) & 1) << bit)
        return block ^ self.place

    def arrive(self, array, name, step):
        return self.hop(array, self.orders[name][::-1][step])

    def finish(self, array, name):
        return [array, self.hop(array, self.orders[name][0])]


def grown(arrays, arrivals):
    return [jnp.concatenate(pair, axis=0) for pair in zip(arrays, arrivals)]


class Sum:
    def __init__(self, net, name, segments, done, blocks):
        self.net = net
        self.name = name
        self.segments = segments
        self.done = done
        self.blocks = blocks

    def bit(self):
        return self.net.orders[self.name][self.done]

    def split(self, names):
        return [
            Sum(self.net, name, [segment], self.done, self.blocks)
            for name, segment in zip(names, self.segments)
        ]


def core_hop(net, pair, widths):
    keep, send = pair
    arrived = net.hop(send, net.orders["a"][0])
    low = 0
    segments = []
    for width in widths:
        segments.append((width, [(keep, low), (arrived, low)]))
        low += width
    return Sum(net, "a", segments, 1, keep.shape[0])


def combine_kernel(plan, count, outputs, *refs):
    arrays, refs = refs[:count], refs[count:]
    outs, buffers, sems = refs[:outputs], refs[outputs:-1], refs[-1]
    starts = []
    for _, _, held, number, width, pieces in plan:
        begin = 0 if held is not None else number
        for index, low in pieces:
            array = arrays[index]
            if len(array.shape) == 3:
                source = array.at[low + begin * width : low + 2 * number * width]
            else:
                source = array.at[begin : 2 * number, low : low + width]
            copy = pltpu.make_async_copy(source, buffers[len(starts)], sems.at[len(starts)])
            copy.start()
            starts.append(copy)
    begin = 0
    for slot, first, held, number, width, pieces in plan:
        for index in range(begin, begin + len(pieces)):
            starts[index].wait()
        mine = buffers[begin : begin + len(pieces)]
        jobs = [(slot, first, 0)] if held is None else [(slot, first, number), (outputs - 1, held, 0)]
        for out, place, skip in jobs:

            def body(block, carry, out=out, place=place, skip=skip, width=width, mine=mine):
                value = None
                for buffer in mine:
                    flat = len(buffer.shape) == 3
                    at = block + skip
                    part = buffer[pl.ds(at * width, width)] if flat else buffer[at]
                    value = part.astype(F32) if value is None else value + part.astype(F32)
                outs[out][pl.ds(place + block * width, width)] = value.astype(BF)
                return carry

            lax.fori_loop(0, number, body, 0)
        begin += len(pieces)


class Round:
    def __init__(self, sums, *tokens, limit=VMEM_BYTES // 3):
        self.net = sums[0].net
        self.sums = sums
        self.bits = sorted({item.bit() for item in sums})
        arrays = []
        plan = []
        sizes = [0] * len(self.bits) + [0]
        self.places = []
        block = None
        for item in sums:
            slot = self.bits.index(item.bit())
            number = item.blocks // 2
            holds = item.done > 1
            places = []
            for width, pieces in item.segments:
                entry = []
                for array, low in pieces:
                    found = [at for at, other in enumerate(arrays) if other is array]
                    if not found:
                        arrays.append(array)
                    entry.append((found[0] if found else len(arrays) - 1, low))
                    block = array.shape[-2:]
                held = sizes[-1] if holds else None
                plan.append((slot, sizes[slot], held, number, width, entry))
                places.append((sizes[slot], held))
                sizes[slot] += number * width
                sizes[-1] += number * width if holds else 0
            self.places.append((slot, places))
        tied = list(tie(*arrays, *tokens))[: len(arrays)] if tokens else arrays
        scratch = []
        moved = 0
        for _, _, held, number, width, entry in plan:
            both = number if held is None else 2 * number
            moved += both * width * (len(entry) + 1) * 16384
            for index, _ in entry:
                flat = len(arrays[index].shape) == 3
                shape = (both * width,) if flat else (both, width)
                scratch.append(pltpu.VMEM(shape + block, BF))
        if not sizes[-1]:
            sizes.pop()
        self.sends = pl.pallas_call(
            functools.partial(combine_kernel, plan, len(tied), len(sizes)),
            out_shape=[shaped((size,) + block, BF) for size in sizes],
            in_specs=[ANY] * len(tied),
            out_specs=[VMEM] * len(sizes),
            scratch_shapes=scratch + [pltpu.SemaphoreType.DMA((len(scratch),))],
            cost_estimate=pl.CostEstimate(flops=0, bytes_accessed=moved, transcendentals=0),
            compiler_params=pltpu.CompilerParams(vmem_limit_bytes=limit),
        )(*tied)

    def before(self, *arrays):
        tied = tie(*arrays, *self.sends)
        self.sends = list(tied[len(arrays) :])
        return tied[: len(arrays)]

    def go(self):
        arrived = [self.net.hop(send, bit) for send, bit in zip(self.sends, self.bits)]
        for item, (slot, places) in zip(self.sums, self.places):
            made = []
            for (width, pieces), (place, held) in zip(item.segments, places):
                stay = pieces if held is None else [(self.sends[-1], held)]
                made.append((width, stay + [(arrived[slot], place)]))
            item.segments = made
            item.done += 1
            item.blocks //= 2
        return arrived


def adam_update(weight, gradient, first, second, rate, decay):
    first_new = BETA_ONE * first + (1.0 - BETA_ONE) * gradient
    second_new = BETA_TWO * second + (1.0 - BETA_TWO) * gradient * gradient
    first_hat = first_new / (1.0 - BETA_ONE**STEP)
    second_hat = second_new / (1.0 - BETA_TWO**STEP)
    weight_new = weight - rate * (first_hat / (jnp.sqrt(second_hat) + EPS_ADAM) + decay * weight)
    return (weight_new, first_new, second_new, weight_new.astype(BF))


def gather_small(vectors, hidden):
    whole = lax.all_gather(vectors.astype(BF), AXES, axis=1, tiled=True)
    deep = lax.all_gather(hidden.astype(BF), AXES, axis=1, tiled=True)
    whole = jnp.pad(whole, ((0, HIDDEN_ROW - whole.shape[0]), (0, 0)))
    return jnp.concatenate([whole, deep.reshape(-1, whole.shape[1])], axis=0).astype(F32)


def scatter_small(grads, vectors, hidden, place, count):
    whole = lax.psum(small_rows(*grads), AXES)
    rows, lanes = vectors.shape
    first = lax.dynamic_slice_in_dim(whole[:rows], place * lanes, lanes, axis=1)
    layers, lanes = hidden.shape
    deep = whole[HIDDEN_ROW:].reshape(layers, -1)
    return first, lax.dynamic_slice_in_dim(deep, place * lanes, lanes, axis=1)


def gather_whole(attention, up, down):
    width = attention.shape[2]
    number = width // BLOCK
    square = lax.all_gather(attention, AXES, axis=1, tiled=True)
    square = square.reshape(-1, QUAD, number, BLOCK, width).transpose(0, 2, 1, 3, 4)
    tall = lax.all_gather(up, AXES, axis=1, tiled=True)
    tall = tall.reshape(2, number, BLOCK, QUAD, width).transpose(0, 1, 3, 2, 4)
    deep = lax.all_gather(down, AXES, axis=1, tiled=True).reshape(2, number, QUAD, BLOCK, width)
    half = number // 2
    quads = [square[0], tall[0], deep[0], square[1], square[2], tall[1], deep[1]]
    return [(quad[:half], quad[half:]) for quad in quads]


def scatter_whole(quads):
    joined = [jnp.concatenate(pair, axis=0).astype(F32) for pair in quads]
    number, _, _, width = joined[0].shape
    square = jnp.stack([joined[0], joined[3], joined[4]])
    square = square.transpose(0, 2, 1, 3, 4).reshape(3 * QUAD, width, width)
    tall = jnp.stack([joined[1], joined[5]]).transpose(0, 1, 3, 2, 4)
    tall = tall.reshape(2, width, QUAD * width)
    deep = jnp.stack([joined[2], joined[6]]).reshape(2, QUAD * width, width)
    return [
        lax.psum_scatter(part, AXES, scatter_dimension=1, tiled=True)
        for part in (square, tall, deep)
    ]


def direct_step(pairs, source, target, grad, masters, firsts, seconds, axis_sizes):
    net = Direct(axis_sizes)
    source_pair, target_pair, cross_pair = pairs
    a, b = net.table("a"), net.table("b")
    cut = QUAD // 2
    at = (net.place % (net.count * LANES // source.shape[1])).astype(jnp.int32).reshape(1)

    one, rest = first_arrays(at, *masters)
    (one,) = grown([one], [net.arrive(one, "a", 0)])
    (one,) = grown([one], [net.arrive(one, "a", 1)])
    left, right = one[:, : cut + QUAD], one[:, cut + QUAD :]
    rest, left, right = tie(rest, left, right)
    for step in (2, 3):
        more = tie(
            net.arrive(left, "a", step),
            net.arrive(right, "b", step),
            net.arrive(rest, "a", step - 2),
        )
        left, right, rest = grown((left, right, rest), more)
    self_w, up_two = rest[:, :QUAD], rest[:, QUAD : 2 * QUAD]
    cross_w, down_two = rest[:, 2 * QUAD : 3 * QUAD], rest[:, 3 * QUAD :]
    more = tie(
        net.hop(left, net.orders["a"][0]),
        net.hop(right, net.orders["b"][0]),
        net.arrive(self_w, "a", 2),
        net.arrive(cross_w, "b", 2),
    )
    left, right = [left, more[0]], [right, more[1]]
    self_w, cross_w = grown((self_w, cross_w), more[2:])
    source, self_w, cross_w, up_two, down_two = tie(source, self_w, cross_w, up_two, down_two)
    more = [
        net.arrive(self_w, "a", 3),
        net.arrive(cross_w, "b", 3),
        net.arrive(up_two, "a", 2),
        net.arrive(down_two, "b", 2),
    ]
    enc_attend_w = [(a, left, 0, cut), (b, right, 0, cut)]
    enc_feed_w = [(a, left, cut, QUAD), (b, right, cut + 1, QUAD)]
    enc_kept = attend_forward(source_pair, None, 0, source, None, enc_attend_w, False)
    enc_mid, small = enc_kept[7], enc_kept[8]
    enc_feed_kept = feed_forward(small, 5, HIDDEN_ROW, enc_mid, enc_feed_w)
    memory = enc_feed_kept[0]
    up_two, down_two = grown((up_two, down_two), tie(*more[2:], memory)[:2])
    self_w, cross_w = grown((self_w, cross_w), tie(*more[:2], up_two, down_two)[:2])
    target, up_two, down_two, self_w, cross_w = tie(target, up_two, down_two, self_w, cross_w)
    more = [net.arrive(up_two, "a", 3), net.arrive(down_two, "b", 3)]
    self_w = [(a, net.finish(self_w, "a"), 0, QUAD)]
    cross_w = [(b, net.finish(cross_w, "b"), 0, QUAD)]
    self_kept = attend_forward(target_pair, small, 8, target, None, self_w, True)
    dec_one = self_kept[7]
    cross_kept = attend_forward(cross_pair, small, 13, dec_one, memory, cross_w, False)
    dec_two = cross_kept[7]
    up_two, down_two = grown((up_two, down_two), tie(*more, dec_two)[:2])
    dec_feed_w = [(a, net.finish(up_two, "a"), 0, QUAD), (b, net.finish(down_two, "b"), 0, QUAD)]
    result, two_grad, dec_feed_small, feed_two = feed_both(
        (a, b), small, 18, HIDDEN_ROW + QUAD, dec_two, grad, dec_feed_w
    )

    names = ("a", "b")
    feed_two = core_hop(net, feed_two, (QUAD, QUAD)).split(names)
    one_grad, memory_grad, cross_small, cross_q = attend_backward(
        (a, b), cross_pair, small, 13, two_grad, cross_kept, dec_one, memory, cross_w, False, None
    )
    send = Round(feed_two, cross_small)
    memory_grad, *cross_q = send.before(memory_grad, *cross_q)
    send.go()
    cross_s = core_hop(net, cross_q, (cut, cut)).split(names)
    mid_grad, enc_feed_small, feed_one = feed_backward(
        (a, b), small, 5, memory_grad, enc_feed_kept, enc_mid, enc_feed_w
    )
    send = Round(feed_two + cross_s, enc_feed_small)
    one_grad, *feed_one = send.before(one_grad, *feed_one)
    send.go()
    feed_one = core_hop(net, feed_one, (QUAD, QUAD)).split(names)
    target_grad, _, self_small, self_q = attend_backward(
        (a, b), target_pair, small, 8, one_grad, self_kept, target, None, self_w, True, None
    )
    send = Round(feed_two + cross_s + feed_one, self_small)
    mid_grad, *self_q = send.before(mid_grad, *self_q)
    send.go()
    self_s = core_hop(net, self_q, (cut, cut)).split(names)
    others = (enc_feed_small, self_small, cross_small, dec_feed_small)
    source_grad, _, _, enc_q = attend_backward(
        (a, b), source_pair, small, 0, mid_grad, enc_kept, source, None, enc_attend_w, False, others
    )
    send = Round(feed_two + cross_s + feed_one + self_s, source_grad)
    enc_q = send.before(*enc_q)
    last = send.go()
    enc_s = core_hop(net, enc_q, (cut, cut + 1)).split(names)
    while enc_s[0].blocks > 1:
        send = Round([item for item in cross_s + feed_one + self_s + enc_s if item.blocks > 1], *last)
        last = send.go()

    square = [(0, index) for index in range(3 * QUAD)]
    tall, deep = [], []
    for layer in range(2):
        for index in range(QUAD):
            lanes = slice(index * source.shape[1], (index + 1) * source.shape[1])
            tall.append((1, (layer, slice(None), lanes)))
            deep.append((2, (layer, slice(index * BLOCK, (index + 1) * BLOCK))))
    targets = [square[:cut], square[cut:QUAD] + [(3, None)]]
    targets += [square[QUAD : QUAD + cut], square[QUAD + cut : 2 * QUAD], tall[:QUAD], deep[:QUAD]]
    targets += [tall[QUAD:], deep[QUAD:]]
    targets += [square[2 * QUAD : 2 * QUAD + cut], square[2 * QUAD + cut :]]
    segments = [item.segments[0] for item in enc_s + self_s + feed_one + feed_two + cross_s]
    segments = [segment + (target,) for segment, target in zip(segments, targets)]
    updated = last_update(at, segments, masters, firsts, seconds)
    return (memory, result, source_grad, target_grad), updated


def whole_step(pairs, source, target, grad, masters, firsts, seconds, axis_sizes):
    attention, up, down = [master.astype(BF) for master in masters[:3]]
    vectors, hidden = masters[3:]
    source_pair, target_pair, cross_pair = pairs
    small = gather_small(vectors, hidden)
    quads = gather_whole(attention, up, down)
    table = jnp.arange(source.shape[1] // BLOCK, dtype=jnp.int32)
    two = (table, table)
    parts = [(table, list(quad), 0, QUAD) for quad in quads]
    enc_kept = attend_forward(source_pair, small, 0, source, None, parts[:1], False)
    enc_mid = enc_kept[7]
    enc_feed_kept = feed_forward(small, 5, HIDDEN_ROW, enc_mid, parts[1:3])
    memory = enc_feed_kept[0]
    self_kept = attend_forward(target_pair, small, 8, target, None, parts[3:4], True)
    dec_one = self_kept[7]
    cross_kept = attend_forward(cross_pair, small, 13, dec_one, memory, parts[4:5], False)
    dec_two = cross_kept[7]
    result, two_grad, dec_feed_small, feed_two = feed_both(
        two, small, 18, HIDDEN_ROW + QUAD, dec_two, grad, parts[5:7]
    )
    one_grad, memory_grad, cross_small, cross_q = attend_backward(
        two, cross_pair, small, 13, two_grad, cross_kept, dec_one, memory, parts[4:5], False, None
    )
    target_grad, _, self_small, self_q = attend_backward(
        two, target_pair, small, 8, one_grad, self_kept, target, None, parts[3:4], True, None
    )
    mid_grad, enc_feed_small, feed_one = feed_backward(
        two, small, 5, memory_grad, enc_feed_kept, enc_mid, parts[1:3]
    )
    source_grad, _, enc_small, enc_q = attend_backward(
        two, source_pair, small, 0, mid_grad, enc_kept, source, None, parts[:1], False, None
    )
    quads = [enc_q]
    quads += [[half[:, low : low + QUAD] for half in feed_one] for low in (0, QUAD)]
    quads += [self_q, cross_q]
    quads += [[half[:, low : low + QUAD] for half in feed_two] for low in (0, QUAD)]
    smalls = (enc_small, enc_feed_small, self_small, cross_small, dec_feed_small)
    count = axis_sizes[0] * axis_sizes[1]
    shares = scatter_small(smalls, vectors, hidden, lax.axis_index(AXES), count)
    grads = tuple(scatter_whole(quads)) + shares
    updated = [
        adam_update(
            masters[slot], grads[slot], firsts[slot], seconds[slot], RATES[slot], DECAYS[slot]
        )
        for slot in range(5)
    ]
    flat = [updated[slot][kind] for kind in range(4) for slot in range(5)]
    return (memory, result, source_grad, target_grad), flat


def per_device(
    axis_sizes,
    source_tokens,
    target_tokens,
    source_segments,
    target_segments,
    output_grad,
    attention_weight,
    up_weight,
    down_weight,
    vectors,
    hidden_bias,
    *moments,
):
    masters = (attention_weight, up_weight, down_weight, vectors, hidden_bias)
    firsts = moments[:5]
    seconds = moments[5:]
    width = source_tokens.shape[2]
    pairs = (
        (source_segments, source_segments),
        (target_segments, target_segments),
        (target_segments, source_segments),
    )
    direct = axis_sizes[0] * axis_sizes[1] * BLOCK == width
    tokens, updated = (direct_step if direct else whole_step)(
        pairs,
        source_tokens[0],
        target_tokens[0],
        output_grad[0],
        masters,
        firsts,
        seconds,
        axis_sizes,
    )
    return tuple(array[None] for array in tokens) + tuple(updated)


def solution(mesh):
    rows = P(AXES, None, None)
    line = P(AXES, None)
    matrix = P(None, AXES, None)
    vector = P(None, AXES)
    state = (matrix, matrix, matrix, vector, vector)
    return jax.shard_map(
        functools.partial(per_device, (mesh.shape["dp"], mesh.shape["fsdp"])),
        mesh=mesh,
        in_specs=(rows, rows, line, line, rows) + state * 3,
        out_specs=(rows,) * 4 + state * 4,
        check_vma=False,
    )
```

```python
import functools

import jax
import jax.numpy as jnp
from jax import lax
from jax.experimental import pallas as pl
from jax.experimental.pallas import tpu as pltpu
from jax.sharding import PartitionSpec as P

HEADS = 8
STEP = 10
EPS_NORM = 1e-05
EPS_ADAM = 1e-08
BETA_ONE = 0.9
BETA_TWO = 0.999
LOWEST = -1e30
RATES = (0.05, 0.05, 0.05, 0.3, 0.3)
DECAYS = (0.01, 0.01, 0.01, 0.0, 0.0)
AXES = ("dp", "fsdp")
QUAD = 4
BLOCK = 16
CHUNK = 64
LANES = 128
SMALL_ROWS = 32
VMEM_BYTES = 60 * 1024 * 1024
HIDDEN_ROW = 24
BF = jnp.bfloat16
F32 = jnp.float32
VMEM = pl.BlockSpec(memory_space=pltpu.VMEM)
SMEM = pl.BlockSpec(memory_space=pltpu.SMEM)
ANY = pl.BlockSpec(memory_space=pl.ANY)
ROOT_TWO_PI = 0.7978845608028654
CUBIC = 0.044715


def dot(left, right):
    return jnp.dot(left, right, preferred_element_type=F32)


def dot_nt(left, right):
    return lax.dot_general(left, right, (((1,), (1,)), ((), ())), preferred_element_type=F32)


class Input:
    def __init__(self, array, room, sem):
        self.room = room
        self.shape = room.shape
        self.copy = pltpu.make_async_copy(array, room, sem)
        self.copy.start()
        self.there = False

    def __getitem__(self, where):
        if not self.there:
            self.copy.wait()
            self.there = True
        return self.room[where]


class Output:
    def __init__(self, array, room, sem):
        self.array = array
        self.room = room
        self.shape = room.shape
        self.sem = sem
        self.left = False

    def __getitem__(self, where):
        return self.room[where]

    def __setitem__(self, where, value):
        self.room[where] = value

    def put(self, index=None):
        source = self.room if index is None else self.room.at[index]
        target = self.array if index is None else self.array.at[index]
        pltpu.make_async_copy(source, target, self.sem).start()
        self.left = True

    def finish(self):
        if not self.left:
            self.put()
        pltpu.make_async_copy(self.room, self.array, self.sem).wait()


def staged_kernel(kernel, scalars, inputs, others, outputs, targets, *refs):
    refs = list(refs)
    sems = refs.pop()
    count = inputs + outputs
    rooms = refs[len(refs) - count :]
    refs = refs[: len(refs) - count]
    at = scalars
    for slot in range(inputs):
        refs[at + slot] = Input(refs[at + slot], rooms[slot], sems.at[slot])
    at += inputs + others
    made = []
    for slot in range(inputs, count):
        place = at + slot - inputs
        refs[place] = Output(refs[place], rooms[slot], sems.at[slot])
        made.append(refs[place])
    kernel(*refs)
    for output in made:
        output.finish()


def part_copies(part, room, sems):
    _, arrays, low, number = part
    made = []
    first = 0
    for slot, array in enumerate(arrays):
        last = first + array.shape[0]
        made.append((array.at[:, low : low + number], room.at[first:last], sems.at[slot]))
        first = last
    return made


def load_start(part, room, sems):
    for outside, inside, sem in part_copies(part, room, sems):
        pltpu.make_async_copy(outside, inside, sem).start()


def load_wait(part, room, sems):
    for outside, inside, sem in part_copies(part, room, sems):
        pltpu.make_async_copy(outside, inside, sem).wait()


def store_start(part, room, sems):
    for outside, inside, sem in part_copies(part, room, sems)[::-1]:
        pltpu.make_async_copy(inside, outside, sem).start()


def store_wait(part, room, sems):
    for outside, inside, sem in part_copies(part, room, sems):
        pltpu.make_async_copy(inside, outside, sem).wait()


def matrix_of(part, room, index):
    table = part[0]
    return jnp.concatenate([room[table[block], index] for block in range(room.shape[0])], axis=0)


def matrix_put(part, room, index, value):
    table = part[0]
    value = value.astype(BF)
    for block in range(room.shape[0]):
        room[table[block], index] = value[block * BLOCK : (block + 1) * BLOCK]


def deep_of(part, room, index):
    table = part[0]
    number, subs, _, width = room.shape
    blocks = range(index * number // QUAD, (index + 1) * number // QUAD)
    return jnp.concatenate([room[table[block]].reshape(subs * BLOCK, width) for block in blocks], axis=0)


def deep_put(part, room, index, value):
    table = part[0]
    number, subs, _, width = room.shape
    value = value.astype(BF).reshape(number // QUAD, subs, BLOCK, width)
    for at in range(number // QUAD):
        room[table[index * number // QUAD + at]] = value[at]


def column_sum(values):
    rows, width = values.shape
    return jnp.sum(values.reshape(rows // 8, 8, width), axis=0)


def total_of(sums):
    return jnp.sum(functools.reduce(jnp.add, sums), axis=0, keepdims=True)


def norm_forward(pre_of, length, gain, shift, out_ref, hat_ref, rstd_ref):
    for at in range(0, length, CHUNK):
        rows = slice(at, at + CHUNK)
        pre = pre_of(rows)
        mean = jnp.mean(pre, axis=-1, keepdims=True)
        centred = pre - mean
        spread = jnp.mean(centred * centred, axis=-1, keepdims=True)
        rstd = lax.rsqrt(spread + EPS_NORM)
        hat = centred * rstd
        hat_ref[rows] = hat
        rstd_ref[rows] = jnp.broadcast_to(rstd, (CHUNK, LANES))
        out_ref[rows] = hat * gain + shift
    for ref in (hat_ref, rstd_ref, out_ref):
        if isinstance(ref, Output):
            ref.put()


def norm_backward(grad_ref, hat_ref, rstd_ref, gain, pre_out, low_out):
    length = grad_ref.shape[0]
    sums = ([], [], [])
    for at in range(0, length, CHUNK):
        rows = slice(at, at + CHUNK)
        grad = grad_ref[rows].astype(F32)
        hat = hat_ref[rows]
        sums[0].append(column_sum(grad * hat))
        sums[1].append(column_sum(grad))
        scaled = grad * gain
        one = jnp.mean(scaled, axis=-1, keepdims=True)
        two = jnp.mean(scaled * hat, axis=-1, keepdims=True)
        pre = rstd_ref[rows][:, :1] * (scaled - one - hat * two)
        low = pre.astype(BF)
        pre_out[rows] = pre
        low_out[rows] = low
        sums[2].append(column_sum(low.astype(F32)))
    return [total_of(each) for each in sums]


def lane_mask(rows):
    return lax.broadcasted_iota(jnp.int32, (rows, LANES), 1) < LANES // 2


def stacked_pair(block):
    first = lane_mask(block.shape[0])
    zero = jnp.zeros_like(block)
    return jnp.concatenate([jnp.where(first, block, zero), jnp.where(first, zero, block)], axis=0)


def merged_pair(stacked):
    rows = stacked.shape[0] // 2
    return jnp.where(lane_mask(rows), stacked[:rows], stacked[rows:])


def mask_fill(bias_ref, column_seg, row_seg, causal, transposed):
    length = bias_ref.shape[0]
    column = jnp.broadcast_to(column_seg, (LANES, length)).T
    for at in range(0, length, LANES):
        same = column == row_seg[:, at : at + LANES]
        if causal:
            down = lax.broadcasted_iota(jnp.int32, (length, LANES), 0)
            along = lax.broadcasted_iota(jnp.int32, (length, LANES), 1) + at
            order = (down <= along) if transposed else (along <= down)
            same = same & order
        bias_ref[:, at : at + LANES] = jnp.where(same, 0.0, LOWEST)


def take_parts(refs, layout, tables):
    parts = []
    for slot, (arrays, low, number) in enumerate(layout):
        parts.append((tables[slot], [refs.pop(0) for _ in range(arrays)], low, number))
    return parts


def small_part(part):
    table, arrays, low, number = part
    return table, arrays, low + number, 1


def small_join(blocks_ref, table):
    count = blocks_ref.shape[0]
    groups = blocks_ref.shape[3] // LANES
    per = count // groups
    vectors = []
    hidden = [[], []]
    for group in range(groups):
        total = blocks_ref[table[group * per], 0][:8].astype(F32)
        for at in range(group * per + 1, (group + 1) * per):
            total = total + blocks_ref[table[at], 0][:8].astype(F32)
        columns = [total[:, at : at + LANES] for at in range(0, 4 * LANES, LANES)]
        vectors.append(jnp.concatenate(columns[:3], axis=0))
        for layer in range(2):
            rows = [columns[3][4 * layer + at : 4 * layer + at + 1] for at in range(4)]
            hidden[layer].append(jnp.concatenate(rows, axis=1))
    return jnp.concatenate([jnp.concatenate(vectors, axis=1)] + hidden[0] + hidden[1], axis=0)


def small_split(whole, group):
    lanes = slice(group * LANES, (group + 1) * LANES)
    columns = [whole[at : at + 8, lanes] for at in (0, 8, 16)]
    rows = []
    for layer in range(2):
        row = whole[24 + 4 * layer + group : 25 + 4 * layer + group]
        rows += [row[:, at : at + LANES] for at in range(0, 4 * LANES, LANES)]
    columns.append(jnp.concatenate(rows, axis=0))
    block = jnp.concatenate(columns, axis=1)
    return jnp.concatenate([block, jnp.zeros_like(block)], axis=0).astype(BF)


def attend_forward_kernel(layout, cross, causal, base, joins, *refs):
    refs = list(refs)
    tables = [refs.pop(0) for _ in layout]
    query_seg = refs.pop(0)
    key_seg = refs.pop(0)
    small = None if joins else refs.pop(0)
    rows_ref = refs.pop(0)
    memory_ref = refs.pop(0) if cross else None
    parts = take_parts(refs, layout, tables)
    q_ref, k_ref, v_ref, o_ref, lse_ref, hat_ref, rstd_ref, out_ref = [refs.pop(0) for _ in range(8)]
    if joins:
        small = refs.pop(0)
        blocks_ref = refs.pop()
        extra = small_part(parts[-1])
    rooms = [refs.pop(0) for _ in parts]
    bias_ref, scores_ref, exponent_ref, largest_ref, mixed_ref, attended_ref, sems = refs
    if joins:
        load_start(extra, blocks_ref, sems.at[len(parts)])
    where = []
    for slot, part in enumerate(parts):
        load_start(part, rooms[slot], sems.at[slot])
        where += [(part, rooms[slot], index) for index in range(part[3])]
    length, width = rows_ref.shape
    mask_fill(bias_ref, query_seg[...], key_seg[...], causal, False)
    rows = rows_ref[...].astype(BF)
    keys = memory_ref[...].astype(BF) if cross else rows
    if joins:
        load_wait(extra, blocks_ref, sems.at[len(parts)])
        small[...] = small_join(blocks_ref, extra[0])
        small.put()
    for slot, part in enumerate(parts):
        load_wait(part, rooms[slot], sems.at[slot])
    scale = (width // HEADS) ** (-0.5)
    query = dot(rows, matrix_of(*where[0])) + small[base : base + 1]
    q_ref[...] = query.astype(BF) * jnp.asarray(scale, BF)
    k_ref[...] = dot(keys, matrix_of(*where[1])).astype(BF)
    v_ref[...] = (dot(keys, matrix_of(*where[2])) + small[base + 1 : base + 2]).astype(BF)
    for ref in (q_ref, k_ref, v_ref):
        ref.put()
    lane = lax.broadcasted_iota(jnp.int32, (LANES, LANES), 1)
    logs = [jnp.zeros((LANES, LANES), F32)] * (length // LANES)
    for pair in range(HEADS // 2):
        lanes = slice(pair * LANES, (pair + 1) * LANES)
        side = pair % 2
        scores_ref[side] = dot_nt(stacked_pair(q_ref[:, lanes]), k_ref[:, lanes])
        for at in range(0, 2 * length, CHUNK):
            chunk = slice(at, at + CHUNK)
            own = slice(at % length, at % length + CHUNK)
            reach = own.start // LANES * LANES + LANES if causal else length
            scores = scores_ref[side, chunk, :reach] + bias_ref[own, :reach]
            largest = jnp.max(scores, axis=-1, keepdims=True)
            exponent_ref[side, chunk, :reach] = jnp.exp(scores - largest).astype(BF)
            if reach < length:
                exponent_ref[side, chunk, reach:] = jnp.zeros((CHUNK, length - reach), BF)
            largest_ref[side, chunk] = jnp.broadcast_to(largest, (CHUNK, LANES))
        values = jnp.concatenate([v_ref[:, lanes], jnp.ones((length, LANES), BF)], axis=1)
        mixed_ref[side] = dot(exponent_ref[side], values)
        for slot, at in enumerate(range(0, length, LANES)):
            outs = []
            for half in range(2):
                chunk = slice(half * length + at, half * length + at + LANES)
                total = mixed_ref[side, chunk, LANES:]
                outs.append(mixed_ref[side, chunk, :LANES] / total)
                log_total = largest_ref[side, chunk] + jnp.log(total)
                logs[slot] = jnp.where(lane == 2 * pair + half, log_total, logs[slot])
            o_ref[at : at + LANES, lanes] = jnp.where(lane_mask(LANES), outs[0], outs[1]).astype(BF)
    for slot, at in enumerate(range(0, length, LANES)):
        lse_ref[:, at : at + LANES] = logs[slot].T[:HEADS]
    o_ref.put()
    lse_ref.put()
    attended_ref[...] = dot(o_ref[...], matrix_of(*where[3]))
    out_bias = small[base + 2 : base + 3]
    norm_forward(
        lambda rows: rows_ref[rows].astype(F32) + (attended_ref[rows] + out_bias),
        length,
        small[base + 3 : base + 4],
        small[base + 4 : base + 5],
        out_ref,
        hat_ref,
        rstd_ref,
    )


def attend_backward_kernel(layout, cross, causal, base, splits, *refs):
    refs = list(refs)
    tables = [refs.pop(0) for _ in layout]
    out_tables = [refs.pop(0), refs.pop(0)]
    query_seg = refs.pop(0)
    key_seg = refs.pop(0)
    small = refs.pop(0)
    grad_ref = refs.pop(0)
    hat_ref, rstd_ref = refs.pop(0), refs.pop(0)
    rows_ref = refs.pop(0)
    memory_ref = refs.pop(0) if cross else None
    q_ref, k_ref, v_ref, o_ref, lse_ref = [refs.pop(0) for _ in range(5)]
    others = [refs.pop(0) for _ in range(4)] if splits else None
    parts = take_parts(refs, layout, tables)
    rows_out = refs.pop(0)
    memory_out = refs.pop(0) if cross else None
    small_out = None if splits else refs.pop(0)
    targets = [refs.pop(0), refs.pop(0)]
    outs = []
    for slot, table in enumerate(out_tables):
        extra = 1 if splits and slot else 0
        outs.append((table, targets, slot * QUAD // 2, QUAD // 2 + extra))
    rooms = [refs.pop(0) for _ in parts]
    out_rooms = [refs.pop(0), refs.pop(0)]
    bias_ref, dout_ref, dq_t_ref, dk_ref, dv_ref, kt_ref, low_ref = refs[:7]
    scores_ref, prob_grad_ref, prob_ref, score_grad_ref, sems = refs[7:]
    where = []
    for slot, part in enumerate(parts):
        load_start(part, rooms[slot], sems.at[slot])
        where += [(part, rooms[slot], index) for index in range(part[3])]
    length, width = rows_ref.shape
    head = width // HEADS
    scale = head ** (-0.5)
    gain_grad, shift_grad, out_bias = norm_backward(
        grad_ref, hat_ref, rstd_ref, small[base + 3 : base + 4], rows_out, low_ref
    )
    mask_fill(bias_ref, key_seg[...], query_seg[...], causal, True)
    low = low_ref[...]
    for slot, part in enumerate(parts):
        load_wait(part, rooms[slot], sems.at[slot])
    dout_ref[...] = dot_nt(low, matrix_of(*where[3])).astype(BF)
    matrix_put(outs[1], out_rooms[1], 1, dot(o_ref[...].T, low))
    product = dout_ref[...].astype(F32) * o_ref[...].astype(F32)
    high = product.astype(BF)
    rest = (product - high.astype(F32)).astype(BF)
    picker = lax.broadcasted_iota(jnp.int32, (BLOCK, width), 1) // head
    picker = (picker == lax.broadcasted_iota(jnp.int32, (BLOCK, width), 0)).astype(BF)
    row_dots = dot_nt(picker, high) + dot_nt(picker, rest)
    kt_ref[...] = k_ref[...].T
    for pair in range(HEADS // 2):
        lanes = slice(pair * LANES, (pair + 1) * LANES)
        side = pair % 2
        query = q_ref[:, lanes]
        dout = dout_ref[:, lanes]
        scores_ref[side] = dot_nt(stacked_pair(k_ref[:, lanes]), query)
        prob_grad_ref[side] = dot_nt(stacked_pair(v_ref[:, lanes]), dout)
        for at in range(0, 2 * length, CHUNK):
            which = 2 * pair + at // length
            chunk = slice(at, at + CHUNK)
            own = slice(at % length, at % length + CHUNK)
            begin = own.start // LANES * LANES if causal else 0
            shift = bias_ref[own, begin:] - lse_ref[which : which + 1, begin:]
            prob = jnp.exp(scores_ref[side, chunk, begin:] + shift)
            prob_ref[side, chunk, begin:] = prob.astype(BF)
            centred = prob_grad_ref[side, chunk, begin:] - row_dots[which : which + 1, begin:]
            score_grad_ref[side, chunk, begin:] = (prob * centred).astype(BF)
            if begin:
                prob_ref[side, chunk, :begin] = jnp.zeros((CHUNK, begin), BF)
                score_grad_ref[side, chunk, :begin] = jnp.zeros((CHUNK, begin), BF)
        dv_ref[:, lanes] = merged_pair(dot(prob_ref[side], dout)).astype(BF)
        dk_ref[:, lanes] = merged_pair(dot(score_grad_ref[side], query)).astype(BF)
        for half in range(2):
            at = pair * LANES + half * head
            own = slice(half * length, (half + 1) * length)
            dq_t_ref[at : at + head, :] = dot(kt_ref[at : at + head, :], score_grad_ref[side, own])
    query_grad = (dq_t_ref[...] * scale).T.astype(BF)
    key_grad = dk_ref[...]
    value_grad = dv_ref[...]
    turned = rows_ref[...].astype(BF).T
    other = memory_ref[...].astype(BF).T if cross else turned
    query_bias = total_of([column_sum(query_grad.astype(F32))])
    value_bias = total_of([column_sum(value_grad.astype(F32))])
    spare = jnp.zeros((3, width), F32)
    own = jnp.concatenate(
        [query_bias, value_bias, out_bias, gain_grad, shift_grad, spare], axis=0
    )
    if splits:
        enc_feed, self_attend, cross_attend, dec_feed = [other_small[...] for other_small in others]
        whole = small_rows(own, enc_feed, self_attend, cross_attend, dec_feed)
        table, room = outs[1][0], out_rooms[1]
        per = room.shape[0] * LANES // width
        for block in range(room.shape[0]):
            if block % per == 0:
                share = small_split(whole, block // per)
            room[table[block], QUAD // 2] = share
    else:
        small_out[...] = own
    matrix_put(outs[1], out_rooms[1], 0, dot(other, value_grad))
    store_start(outs[1], out_rooms[1], sems.at[1])
    matrix_put(outs[0], out_rooms[0], 0, dot(turned, query_grad))
    matrix_put(outs[0], out_rooms[0], 1, dot(other, key_grad))
    store_start(outs[0], out_rooms[0], sems.at[0])
    rows_back = rows_out[...] + dot_nt(query_grad, matrix_of(*where[0]))
    memory_back = dot_nt(key_grad, matrix_of(*where[1])) + dot_nt(value_grad, matrix_of(*where[2]))
    if cross:
        rows_out[...] = rows_back
        memory_out[...] = memory_back
        memory_out.put()
    else:
        rows_out[...] = rows_back + memory_back
    rows_out.put()
    for slot, part in enumerate(outs):
        store_wait(part, out_rooms[slot], sems.at[slot])


def small_rows(enc_attend, enc_feed, self_attend, cross_attend, dec_feed):
    return jnp.concatenate(
        [
            enc_attend[:5],
            enc_feed[:3],
            self_attend[:5],
            cross_attend[:5],
            dec_feed[:3],
            dec_feed[7:],
            dec_feed[7:],
            dec_feed[7:],
            enc_feed[3:7],
            dec_feed[3:7],
        ],
        axis=0,
    )


def gelu_parts(pre):
    square = pre * pre
    curve = jnp.tanh(ROOT_TWO_PI * pre * (1.0 + CUBIC * square))
    half = 0.5 * pre
    rise = 0.5 + 0.5 * curve
    bend = ROOT_TWO_PI * (1.0 + 3.0 * CUBIC * square)
    return pre * rise, rise + half * (1.0 - curve * curve) * bend


def feed_forward_steps(
    small, base, hidden_at, rows_ref, parts, up_ref, down_ref, active_ref, slope_ref, pre_ref, sum_ref
):
    rows = rows_ref[...].astype(BF)
    length = rows.shape[0]
    for index in range(QUAD):
        at = hidden_at + index
        side = index % 2
        pre_ref[side] = dot(rows, matrix_of(parts[0], up_ref, index))
        bias = small[at : at + 1]
        for at in range(0, length, CHUNK // 2):
            chunk = slice(at, at + CHUNK // 2)
            active, slope = gelu_parts(pre_ref[side, chunk] + bias)
            active_ref[index, chunk] = active.astype(BF)
            slope_ref[index, chunk] = slope
        for ref in (active_ref, slope_ref):
            if isinstance(ref, Output):
                ref.put(index)
    wide = jnp.concatenate([active_ref[index] for index in range(QUAD)], axis=1)
    deep = [deep_of(parts[1], down_ref, index) for index in range(QUAD)]
    sum_ref[...] = dot(wide, jnp.concatenate(deep, axis=0))
    out_bias = small[base : base + 1]
    return lambda rows: rows_ref[rows] + (sum_ref[rows] + out_bias)


def feed_backward_steps(
    low_ref,
    rows_ref,
    parts,
    up_ref,
    down_ref,
    active_ref,
    slope_ref,
    dup_ref,
    ddown_ref,
    rows_out,
    back_ref,
    outs,
    sems,
):
    low = low_ref[...]
    length = low.shape[0]
    for index in range(QUAD):
        deep_put(outs[1], ddown_ref, index, dot(active_ref[index].T, low))
    store_start(outs[1], ddown_ref, sems.at[1])
    turned = rows_ref[...].astype(BF).T
    hidden_grads = []
    hiddens = []
    for index in range(QUAD):
        side = index % 2
        back_ref[side] = dot_nt(low, deep_of(parts[1], down_ref, index))
        sums = []
        pieces = []
        for at in range(0, length, CHUNK):
            chunk = slice(at, at + CHUNK)
            hidden = (back_ref[side, chunk] * slope_ref[index, chunk]).astype(BF)
            sums.append(column_sum(hidden.astype(F32)))
            pieces.append(hidden)
        hidden = jnp.concatenate(pieces, axis=0)
        hidden_grads.append(total_of(sums))
        matrix_put(outs[0], dup_ref, index, dot(turned, hidden))
        hiddens.append(hidden)
    store_start(outs[0], dup_ref, sems.at[0])
    total = rows_out[...]
    for index in range(QUAD):
        total = total + dot_nt(hiddens[index], matrix_of(parts[0], up_ref, index))
    rows_out[...] = total
    rows_out.put()
    return hidden_grads


def load_feed(parts, rooms, sems):
    for slot, part in enumerate(parts):
        load_start(part, rooms[slot], sems.at[slot])


def wait_feed(parts, rooms, sems):
    for slot, part in enumerate(parts):
        load_wait(part, rooms[slot], sems.at[slot])


def end_feed(outs, rooms, sems):
    for slot, part in enumerate(outs):
        store_wait(part, rooms[slot], sems.at[slot])


def feed_outs(refs, tables):
    arrays = [refs.pop(0), refs.pop(0)]
    return [(tables[slot], arrays, slot * QUAD, QUAD) for slot in range(2)]


def feed_small(out_bias, gain_grad, shift_grad, hidden_grads):
    spare = jnp.zeros_like(out_bias)
    return jnp.concatenate([out_bias, gain_grad, shift_grad] + hidden_grads + [spare], axis=0)


def feed_forward_kernel(layout, base, hidden_at, *refs):
    refs = list(refs)
    tables = [refs.pop(0), refs.pop(0)]
    small, rows_ref = refs.pop(0), refs.pop(0)
    parts = take_parts(refs, layout, tables)
    out_ref, hat_ref, rstd_ref, active_ref, slope_ref, up_ref, down_ref = refs[:7]
    pre_ref, sum_ref, sems = refs[7:]
    load_feed(parts, (up_ref, down_ref), sems)
    wait_feed(parts, (up_ref, down_ref), sems)
    pre_of = feed_forward_steps(
        small, base, hidden_at, rows_ref, parts, up_ref, down_ref, active_ref, slope_ref, pre_ref, sum_ref
    )
    gain, shift = small[base + 1 : base + 2], small[base + 2 : base + 3]
    norm_forward(pre_of, rows_ref.shape[0], gain, shift, out_ref, hat_ref, rstd_ref)


def feed_backward_kernel(layout, base, *refs):
    refs = list(refs)
    tables = [refs.pop(0), refs.pop(0)]
    out_tables = [refs.pop(0), refs.pop(0)]
    small, grad_ref, hat_ref, rstd_ref, rows_ref = [refs.pop(0) for _ in range(5)]
    active_ref, slope_ref = refs.pop(0), refs.pop(0)
    parts = take_parts(refs, layout, tables)
    rows_out, small_out = refs.pop(0), refs.pop(0)
    outs = feed_outs(refs, out_tables)
    up_ref, down_ref, dup_ref, ddown_ref, low_ref, back_ref, sems, out_sems = refs
    load_feed(parts, (up_ref, down_ref), sems)
    gain_grad, shift_grad, out_bias = norm_backward(
        grad_ref, hat_ref, rstd_ref, small[base + 1 : base + 2], rows_out, low_ref
    )
    wait_feed(parts, (up_ref, down_ref), sems)
    hidden_grads = feed_backward_steps(
        low_ref,
        rows_ref,
        parts,
        up_ref,
        down_ref,
        active_ref,
        slope_ref,
        dup_ref,
        ddown_ref,
        rows_out,
        back_ref,
        outs,
        out_sems,
    )
    small_out[...] = feed_small(out_bias, gain_grad, shift_grad, hidden_grads)
    end_feed(outs, (dup_ref, ddown_ref), out_sems)


def feed_both_kernel(layout, base, hidden_at, *refs):
    refs = list(refs)
    tables = [refs.pop(0), refs.pop(0)]
    out_tables = [refs.pop(0), refs.pop(0)]
    small, rows_ref, grad_ref = [refs.pop(0) for _ in range(3)]
    parts = take_parts(refs, layout, tables)
    out_ref, rows_out, small_out = [refs.pop(0) for _ in range(3)]
    outs = feed_outs(refs, out_tables)
    up_ref, down_ref, dup_ref, ddown_ref, low_ref, back_ref, sum_ref = refs[:7]
    active_ref, slope_ref, hat_ref, rstd_ref, sems, out_sems = refs[7:]
    load_feed(parts, (up_ref, down_ref), sems)
    wait_feed(parts, (up_ref, down_ref), sems)
    pre_of = feed_forward_steps(
        small, base, hidden_at, rows_ref, parts, up_ref, down_ref, active_ref, slope_ref, back_ref, sum_ref
    )
    gain, shift = small[base + 1 : base + 2], small[base + 2 : base + 3]
    norm_forward(pre_of, rows_ref.shape[0], gain, shift, out_ref, hat_ref, rstd_ref)
    gain_grad, shift_grad, out_bias = norm_backward(
        grad_ref, hat_ref, rstd_ref, gain, rows_out, low_ref
    )
    hidden_grads = feed_backward_steps(
        low_ref,
        rows_ref,
        parts,
        up_ref,
        down_ref,
        active_ref,
        slope_ref,
        dup_ref,
        ddown_ref,
        rows_out,
        back_ref,
        outs,
        out_sems,
    )
    small_out[...] = feed_small(out_bias, gain_grad, shift_grad, hidden_grads)
    end_feed(outs, (dup_ref, ddown_ref), out_sems)


def shaped(shape, dtype=F32):
    return jax.ShapeDtypeStruct(shape, dtype)


def call(
    kernel, scalars, inputs, others, outs, targets, scratch, flops, moved, limit=VMEM_BYTES
):
    rooms = [pltpu.VMEM(array.shape, array.dtype) for array in list(inputs) + list(outs)]
    return pl.pallas_call(
        functools.partial(
            staged_kernel, kernel, len(scalars), len(inputs), len(others), len(outs), len(targets)
        ),
        out_shape=list(outs) + list(targets),
        in_specs=[SMEM] * len(scalars) + [ANY] * (len(inputs) + len(others)),
        out_specs=[ANY] * (len(outs) + len(targets)),
        scratch_shapes=scratch + rooms + [pltpu.SemaphoreType.DMA((len(rooms),))],
        cost_estimate=pl.CostEstimate(flops=flops, bytes_accessed=moved, transcendentals=0),
        compiler_params=pltpu.CompilerParams(vmem_limit_bytes=limit),
    )(*scalars, *inputs, *others)


def layout_of(parts):
    return [(len(arrays), low, number) for _, arrays, low, number in parts]


def arrays_of(parts):
    return [array for part in parts for array in part[1]]


def most(parts):
    return max(len(part[1]) for part in parts)


def halves(width, number):
    return [shaped((width // BLOCK // 2, number, BLOCK, width), BF)] * 2


def attend_forward(segments, small, base, rows, memory, parts, causal):
    length, width = rows.shape
    cross = memory is not None
    joins = small is None
    scalars = [part[0] for part in parts]
    inputs = list(segments) + ([] if joins else [small]) + [rows] + ([memory] if cross else [])
    outs = [shaped((length, width), BF)] * 4 + [shaped((HEADS, length))]
    outs += [shaped((length, width)), shaped((length, LANES)), shaped((length, width))]
    outs += [shaped((SMALL_ROWS, width))] if joins else []
    scratch = [
        pltpu.VMEM((length, length), F32),
        pltpu.VMEM((2, 2 * length, length), F32),
        pltpu.VMEM((2, 2 * length, length), BF),
        pltpu.VMEM((2, 2 * length, LANES), F32),
        pltpu.VMEM((2, 2 * length, 2 * LANES), F32),
        pltpu.VMEM((length, width), F32),
        pltpu.SemaphoreType.DMA((len(parts) + 1, most(parts))),
    ]
    scratch = part_rooms(width, [part[3] for part in parts]) + scratch
    scratch += part_rooms(width, [1]) if joins else []
    kernel = functools.partial(attend_forward_kernel, layout_of(parts), cross, causal, base, joins)
    flops = 8 * length * width * width + 16 * length * length * width
    return call(kernel, scalars, inputs, arrays_of(parts), outs, [], scratch, flops, 8_000_000)


def attend_backward(
    out_tables, segments, small, base, grad, kept, rows, memory, parts, causal, others
):
    length, width = rows.shape
    cross = memory is not None
    splits = others is not None
    q, k, v, o, lse, hat, rstd = kept[:7]
    scalars = [part[0] for part in parts] + list(out_tables)
    inputs = list(segments) + [small, grad, hat, rstd, rows]
    inputs += ([memory] if cross else []) + [q, k, v, o, lse] + list(others or ())
    outs = [shaped((length, width))] * (2 if cross else 1)
    outs += [] if splits else [shaped((8, width))]
    targets = halves(width, QUAD + (1 if splits else 0))
    scratch = [
        pltpu.VMEM((length, length), F32),
        pltpu.VMEM((length, width), BF),
        pltpu.VMEM((width, length), F32),
        pltpu.VMEM((length, width), BF),
        pltpu.VMEM((length, width), BF),
        pltpu.VMEM((width, length), BF),
        pltpu.VMEM((length, width), BF),
        pltpu.VMEM((2, 2 * length, length), F32),
        pltpu.VMEM((2, 2 * length, length), F32),
        pltpu.VMEM((2, 2 * length, length), BF),
        pltpu.VMEM((2, 2 * length, length), BF),
        pltpu.SemaphoreType.DMA((3, 2)),
    ]
    numbers = [part[3] for part in parts] + [QUAD // 2, QUAD // 2 + (1 if splits else 0)]
    scratch = part_rooms(width, numbers) + scratch
    kernel = functools.partial(
        attend_backward_kernel, layout_of(parts), cross, causal, base, splits
    )
    flops = 16 * length * width * width + 40 * length * length * width
    arrays = arrays_of(parts)
    results = list(call(kernel, scalars, inputs, arrays, outs, targets, scratch, flops, 12_000_000))
    rows_grad = results.pop(0)
    memory_grad = results.pop(0) if cross else None
    small_grad = None if splits else results.pop(0)
    return rows_grad, memory_grad, small_grad, results


def part_rooms(width, numbers):
    return [pltpu.VMEM((width // BLOCK, number, BLOCK, width), BF) for number in numbers]


def feed_scratch(width, grads):
    return part_rooms(width, [QUAD] * (4 if grads else 2))


def feed_forward(small, base, hidden_at, rows, parts):
    length, width = rows.shape
    scalars = [part[0] for part in parts]
    outs = [shaped((length, width)), shaped((length, width)), shaped((length, LANES))]
    outs += [shaped((QUAD, length, width), BF), shaped((QUAD, length, width))]
    scratch = feed_scratch(width, False)
    scratch += [pltpu.VMEM((2, length, width), F32), pltpu.VMEM((length, width), F32)]
    scratch += [pltpu.SemaphoreType.DMA((2, most(parts)))]
    kernel = functools.partial(feed_forward_kernel, layout_of(parts), base, hidden_at)
    flops = 16 * length * width * width
    arrays = arrays_of(parts)
    return call(kernel, scalars, [small, rows], arrays, outs, [], scratch, flops, 10_000_000)


def feed_backward(out_tables, small, base, grad, kept, rows, parts):
    length, width = rows.shape
    hat, rstd, active, slope = kept[1:]
    scalars = [part[0] for part in parts] + list(out_tables)
    inputs = [small, grad, hat, rstd, rows, active, slope]
    outs = [shaped((length, width)), shaped((8, width))]
    targets = halves(width, 2 * QUAD)
    scratch = feed_scratch(width, True)
    scratch += [pltpu.VMEM((length, width), BF), pltpu.VMEM((2, length, width), F32)]
    scratch += [pltpu.SemaphoreType.DMA((2, most(parts))), pltpu.SemaphoreType.DMA((2, 2))]
    kernel = functools.partial(feed_backward_kernel, layout_of(parts), base)
    flops = 32 * length * width * width
    arrays = arrays_of(parts)
    results = call(kernel, scalars, inputs, arrays, outs, targets, scratch, flops, 14_000_000)
    return results[0], results[1], results[2:4]


def feed_both(out_tables, small, base, hidden_at, rows, grad, parts):
    length, width = rows.shape
    scalars = [part[0] for part in parts] + list(out_tables)
    outs = [shaped((length, width)), shaped((length, width)), shaped((8, width))]
    targets = halves(width, 2 * QUAD)
    scratch = feed_scratch(width, True) + [
        pltpu.VMEM((length, width), BF),
        pltpu.VMEM((2, length, width), F32),
        pltpu.VMEM((length, width), F32),
        pltpu.VMEM((QUAD, length, width), BF),
        pltpu.VMEM((QUAD, length, width), F32),
        pltpu.VMEM((length, width), F32),
        pltpu.VMEM((length, LANES), F32),
        pltpu.SemaphoreType.DMA((2, most(parts))),
        pltpu.SemaphoreType.DMA((2, 2)),
    ]
    kernel = functools.partial(feed_both_kernel, layout_of(parts), base, hidden_at)
    flops = 48 * length * width * width
    arrays = arrays_of(parts)
    results = call(kernel, scalars, [small, rows, grad], arrays, outs, targets, scratch, flops, 12_000_000)
    return results[0], results[1], results[2], results[3:5]


def first_kernel(
    at_ref,
    vector_ref,
    hidden_ref,
    square_ref,
    tall_ref,
    deep_ref,
    one_ref,
    two_ref,
    turn_ref,
    line_ref,
):
    at = at_ref[0]
    width = square_ref.shape[2]
    turn_ref[...] = jnp.zeros_like(turn_ref)
    lanes, rows = vector_ref.shape
    turn_ref[pl.ds(pl.multiple_of(at * lanes, lanes), lanes), :rows] = vector_ref[...]
    upright = turn_ref[...].T
    line_ref[...] = jnp.zeros_like(line_ref)
    layers, lanes = hidden_ref.shape
    per = LANES // lanes
    for layer in range(layers):
        row = jnp.concatenate([hidden_ref[layer : layer + 1]] * per, axis=1)
        lane = lax.broadcasted_iota(jnp.int32, row.shape, 1) // lanes
        row = jnp.where(lane == at % per, row, 0.0)
        line_ref[pl.ds(4 * layer + at // per, 1), :] = row
    columns = [upright[low : low + 8] for low in (0, 8, 16)] + [line_ref[...]]
    block = jnp.concatenate(columns, axis=1)
    small = jnp.concatenate([block, jnp.zeros_like(block)], axis=0)
    tall = []
    deep = []
    for layer in range(2):
        for index in range(QUAD):
            lanes = slice(index * width, (index + 1) * width)
            tall.append(tall_ref[layer, :, lanes])
            deep.append(deep_ref[layer, index * BLOCK : (index + 1) * BLOCK])
    square = [square_ref[index] for index in range(3 * QUAD)]
    cut = QUAD // 2
    groups = [
        square[:cut] + tall[:QUAD] + square[cut:QUAD] + [small] + deep[:QUAD],
        square[QUAD : 2 * QUAD] + tall[QUAD:] + square[2 * QUAD :] + deep[QUAD:],
    ]
    for out_ref, group in zip((one_ref, two_ref), groups):
        for slot, block in enumerate(group):
            out_ref[0, slot] = block.astype(BF)
        out_ref.put()


def first_arrays(at, square, tall, deep, vectors, hidden):
    width = square.shape[2]
    outs = [
        shaped((1, 3 * QUAD + 1, BLOCK, width), BF),
        shaped((1, 4 * QUAD, BLOCK, width), BF),
    ]
    scratch = [pltpu.VMEM((LANES, LANES), F32), pltpu.VMEM((8, LANES), F32)]
    inputs = [vectors.T, hidden, square, tall, deep]
    return call(first_kernel, [at], inputs, [], outs, [], scratch, 0, 4_000_000)


def last_kernel(plan, count, at_ref, *refs):
    masters, firsts, seconds = refs[:5], refs[5:10], refs[10:15]
    arrays, refs = refs[15 : 15 + count], refs[15 + count :]
    outs, refs = [refs[5 * kind : 5 * kind + 5] for kind in range(4)], refs[20:]
    buffers, turn_ref, line_ref, sems = refs
    at = at_ref[0]
    starts = []
    for width, pieces, _ in plan:
        for index, low in pieces:
            array = arrays[index]
            array = array if len(array.shape) == 3 else array.at[0]
            source = array.at[low : low + width]
            copy = pltpu.make_async_copy(source, buffers.at[len(starts), :width], sems.at[len(starts)])
            copy.start()
            starts.append(copy)

    def update(slot, where, gradient):
        results = adam_update(
            masters[slot][where],
            gradient,
            firsts[slot][where],
            seconds[slot][where],
            RATES[slot],
            DECAYS[slot],
        )
        for kind in range(4):
            outs[kind][slot][where] = results[kind]

    begin = 0
    left = len(plan)
    for width, pieces, targets in plan:
        for index in range(len(pieces)):
            starts[begin + index].wait()
        for sub, (slot, where) in enumerate(targets):
            gradient = buffers[begin, sub].astype(F32)
            for index in range(1, len(pieces)):
                gradient = gradient + buffers[begin + index, sub].astype(F32)
            if slot < 3:
                update(slot, where, gradient)
                continue
            turn_ref[...] = jnp.zeros_like(turn_ref)
            for column in range(3):
                lanes = slice(column * LANES, (column + 1) * LANES)
                turn_ref[8 * column : 8 * column + 8, :] = gradient[:8, lanes]
            turn_ref[...] = turn_ref[...].T
            lanes, rows = masters[3].shape
            share = turn_ref[pl.ds(pl.multiple_of(at * lanes, lanes), lanes), :][:, :rows]
            update(3, slice(None), share)
            line_ref[...] = gradient[:8, 3 * LANES :]
            layers, lanes = masters[4].shape
            per = LANES // lanes
            for layer in range(layers):
                row = line_ref[pl.ds(4 * layer + at // per, 1), :]
                share = row[:, :lanes]
                for part in range(1, per):
                    other = row[:, part * lanes : (part + 1) * lanes]
                    share = jnp.where(at % per == part, other, share)
                update(4, slice(layer, layer + 1), share)
        begin += len(pieces)
        left -= 1
        for slot in range(5):
            ends = [at for at, (_, _, each) in enumerate(plan) if any(to[0] in used(slot) for to in each)]
            if ends[-1] == len(plan) - 1 - left:
                for kind in range(4):
                    outs[kind][slot].put()


def used(slot):
    return (3,) if slot > 2 else (slot,)


def last_update(at, segments, masters, firsts, seconds):
    arrays = []
    plan = []
    for width, pieces, targets in segments:
        entry = []
        for array, low in pieces:
            found = [place for place, other in enumerate(arrays) if other is array]
            if not found:
                arrays.append(array)
            entry.append((found[0] if found else len(arrays) - 1, low))
        plan.append((width, entry, targets))
    params = [list(group) for group in (masters, firsts, seconds)]
    for group in params:
        group[3] = group[3].T
    flat = params[0] + params[1] + params[2]
    outs = [shaped(array.shape) for array in params[0]] * 3
    outs += [shaped(array.shape, BF) for array in params[0]]
    pieces = sum(len(entry[1]) for entry in plan)
    block = masters[0].shape[1:]
    scratch = [
        pltpu.VMEM((pieces, max(entry[0] for entry in plan)) + block, BF),
        pltpu.VMEM((LANES, LANES), F32),
        pltpu.VMEM((8, LANES), F32),
        pltpu.SemaphoreType.DMA((pieces,)),
    ]
    kernel = functools.partial(last_kernel, plan, len(arrays))
    results = call(
        kernel, [at], flat, arrays, outs, [], scratch, 0, 8_000_000, VMEM_BYTES // 2
    )
    results = list(results)
    for kind in range(4):
        results[5 * kind + 3] = results[5 * kind + 3].T
    return results


def tie(*arrays):
    return lax.optimization_barrier(arrays)


class Direct:
    def __init__(self, axis_sizes):
        outer, inner = axis_sizes
        self.count = outer * inner
        inner_bits = inner.bit_length() - 1
        bits = self.count.bit_length() - 1
        core = [inner_bits]
        across = list(range(inner_bits + 1, bits))
        up = [0]
        along = list(range(1, inner_bits))
        self.orders = {
            "a": core + across + up + along,
            "b": core + up + across + along,
        }
        self.place = lax.axis_index(AXES)

    def hop(self, array, bit):
        return lax.ppermute(array, AXES, [(at, at ^ (1 << bit)) for at in range(self.count)])

    def table(self, name):
        order = self.orders[name]
        apart = jnp.arange(self.count, dtype=jnp.int32) ^ self.place
        place = jnp.zeros_like(apart)
        for at, bit in enumerate(order):
            place = place | (((apart >> bit) & 1) << (len(order) - 1 - at))
        return place

    def arrive(self, array, name, step):
        return self.hop(array, self.orders[name][::-1][step])

    def finish(self, array, name):
        return [array, self.hop(array, self.orders[name][0])]


def grown(arrays, arrivals):
    return [jnp.concatenate(pair, axis=0) for pair in zip(arrays, arrivals)]


class Sum:
    def __init__(self, net, name, segments, done, blocks):
        self.net = net
        self.name = name
        self.segments = segments
        self.done = done
        self.blocks = blocks

    def bit(self):
        return self.net.orders[self.name][self.done]

    def split(self, names):
        return [
            Sum(self.net, name, [segment], self.done, self.blocks)
            for name, segment in zip(names, self.segments)
        ]


def core_hop(net, pair, widths):
    keep, send = pair
    arrived = net.hop(send, net.orders["a"][0])
    low = 0
    segments = []
    for width in widths:
        segments.append((width, [(keep, low), (arrived, low)]))
        low += width
    return Sum(net, "a", segments, 1, keep.shape[0])


def combine_kernel(plan, count, outputs, *refs):
    arrays, refs = refs[:count], refs[count:]
    outs, buffers, sems = refs[:outputs], refs[outputs:-1], refs[-1]
    starts = []
    for _, _, held, number, width, pieces in plan:
        begin = 0 if held is not None else number
        for index, low in pieces:
            array = arrays[index]
            if len(array.shape) == 3:
                source = array.at[low + begin * width : low + 2 * number * width]
            else:
                source = array.at[begin : 2 * number, low : low + width]
            copy = pltpu.make_async_copy(source, buffers[len(starts)], sems.at[len(starts)])
            copy.start()
            starts.append(copy)
    begin = 0
    for slot, first, held, number, width, pieces in plan:
        for index in range(begin, begin + len(pieces)):
            starts[index].wait()
        mine = buffers[begin : begin + len(pieces)]
        jobs = [(slot, first, 0)] if held is None else [(slot, first, number), (outputs - 1, held, 0)]
        for out, place, skip in jobs:

            def body(block, carry, out=out, place=place, skip=skip, width=width, mine=mine):
                value = None
                for buffer in mine:
                    flat = len(buffer.shape) == 3
                    at = block + skip
                    part = buffer[pl.ds(at * width, width)] if flat else buffer[at]
                    value = part.astype(F32) if value is None else value + part.astype(F32)
                outs[out][pl.ds(place + block * width, width)] = value.astype(BF)
                return carry

            lax.fori_loop(0, number, body, 0)
        begin += len(pieces)


class Round:
    def __init__(self, sums, *tokens, limit=VMEM_BYTES // 3):
        self.net = sums[0].net
        self.sums = sums
        self.bits = sorted({item.bit() for item in sums})
        arrays = []
        plan = []
        sizes = [0] * len(self.bits) + [0]
        self.places = []
        block = None
        for item in sums:
            slot = self.bits.index(item.bit())
            number = item.blocks // 2
            holds = item.done > 1
            places = []
            for width, pieces in item.segments:
                entry = []
                for array, low in pieces:
                    found = [at for at, other in enumerate(arrays) if other is array]
                    if not found:
                        arrays.append(array)
                    entry.append((found[0] if found else len(arrays) - 1, low))
                    block = array.shape[-2:]
                held = sizes[-1] if holds else None
                plan.append((slot, sizes[slot], held, number, width, entry))
                places.append((sizes[slot], held))
                sizes[slot] += number * width
                sizes[-1] += number * width if holds else 0
            self.places.append((slot, places))
        tied = list(tie(*arrays, *tokens))[: len(arrays)] if tokens else arrays
        scratch = []
        moved = 0
        for _, _, held, number, width, entry in plan:
            both = number if held is None else 2 * number
            moved += both * width * (len(entry) + 1) * 16384
            for index, _ in entry:
                flat = len(arrays[index].shape) == 3
                shape = (both * width,) if flat else (both, width)
                scratch.append(pltpu.VMEM(shape + block, BF))
        if not sizes[-1]:
            sizes.pop()
        self.sends = pl.pallas_call(
            functools.partial(combine_kernel, plan, len(tied), len(sizes)),
            out_shape=[shaped((size,) + block, BF) for size in sizes],
            in_specs=[ANY] * len(tied),
            out_specs=[VMEM] * len(sizes),
            scratch_shapes=scratch + [pltpu.SemaphoreType.DMA((len(scratch),))],
            cost_estimate=pl.CostEstimate(flops=0, bytes_accessed=moved, transcendentals=0),
            compiler_params=pltpu.CompilerParams(vmem_limit_bytes=limit),
        )(*tied)

    def before(self, *arrays):
        tied = tie(*arrays, *self.sends)
        self.sends = list(tied[len(arrays) :])
        return tied[: len(arrays)]

    def go(self):
        arrived = [self.net.hop(send, bit) for send, bit in zip(self.sends, self.bits)]
        for item, (slot, places) in zip(self.sums, self.places):
            made = []
            for (width, pieces), (place, held) in zip(item.segments, places):
                stay = pieces if held is None else [(self.sends[-1], held)]
                made.append((width, stay + [(arrived[slot], place)]))
            item.segments = made
            item.done += 1
            item.blocks //= 2
        return arrived


def adam_update(weight, gradient, first, second, rate, decay):
    first_new = BETA_ONE * first + (1.0 - BETA_ONE) * gradient
    second_new = BETA_TWO * second + (1.0 - BETA_TWO) * gradient * gradient
    first_hat = first_new / (1.0 - BETA_ONE**STEP)
    second_hat = second_new / (1.0 - BETA_TWO**STEP)
    weight_new = weight - rate * (first_hat / (jnp.sqrt(second_hat) + EPS_ADAM) + decay * weight)
    return (weight_new, first_new, second_new, weight_new.astype(BF))


def gather_small(vectors, hidden):
    whole = lax.all_gather(vectors.astype(BF), AXES, axis=1, tiled=True)
    deep = lax.all_gather(hidden.astype(BF), AXES, axis=1, tiled=True)
    whole = jnp.pad(whole, ((0, HIDDEN_ROW - whole.shape[0]), (0, 0)))
    return jnp.concatenate([whole, deep.reshape(-1, whole.shape[1])], axis=0).astype(F32)


def scatter_small(grads, vectors, hidden, place, count):
    whole = lax.psum(small_rows(*grads), AXES)
    rows, lanes = vectors.shape
    first = lax.dynamic_slice_in_dim(whole[:rows], place * lanes, lanes, axis=1)
    layers, lanes = hidden.shape
    deep = whole[HIDDEN_ROW:].reshape(layers, -1)
    return first, lax.dynamic_slice_in_dim(deep, place * lanes, lanes, axis=1)


def gather_whole(attention, up, down):
    width = attention.shape[2]
    number = width // BLOCK
    square = lax.all_gather(attention, AXES, axis=1, tiled=True)
    square = square.reshape(-1, QUAD, number, BLOCK, width).transpose(0, 2, 1, 3, 4)
    tall = lax.all_gather(up, AXES, axis=1, tiled=True)
    tall = tall.reshape(2, number, BLOCK, QUAD, width).transpose(0, 1, 3, 2, 4)
    deep = lax.all_gather(down, AXES, axis=1, tiled=True).reshape(2, number, QUAD, BLOCK, width)
    half = number // 2
    quads = [square[0], tall[0], deep[0], square[1], square[2], tall[1], deep[1]]
    return [(quad[:half], quad[half:]) for quad in quads]


def scatter_whole(quads):
    joined = [jnp.concatenate(pair, axis=0).astype(F32) for pair in quads]
    number, _, _, width = joined[0].shape
    square = jnp.stack([joined[0], joined[3], joined[4]])
    square = square.transpose(0, 2, 1, 3, 4).reshape(3 * QUAD, width, width)
    tall = jnp.stack([joined[1], joined[5]]).transpose(0, 1, 3, 2, 4)
    tall = tall.reshape(2, width, QUAD * width)
    deep = jnp.stack([joined[2], joined[6]]).reshape(2, QUAD * width, width)
    return [
        lax.psum_scatter(part, AXES, scatter_dimension=1, tiled=True)
        for part in (square, tall, deep)
    ]


def direct_step(pairs, source, target, grad, masters, firsts, seconds, axis_sizes):
    net = Direct(axis_sizes)
    source_pair, target_pair, cross_pair = pairs
    a, b = net.table("a"), net.table("b")
    cut = QUAD // 2
    at = (net.place % (net.count * LANES // source.shape[1])).astype(jnp.int32).reshape(1)

    one, rest = first_arrays(at, *masters)
    (one,) = grown([one], [net.arrive(one, "a", 0)])
    (one,) = grown([one], [net.arrive(one, "a", 1)])
    left, right = one[:, : cut + QUAD], one[:, cut + QUAD :]
    rest, left, right = tie(rest, left, right)
    for step in (2, 3):
        more = tie(
            net.arrive(left, "a", step),
            net.arrive(right, "b", step),
            net.arrive(rest, "a", step - 2),
        )
        left, right, rest = grown((left, right, rest), more)
    self_w, up_two = rest[:, :QUAD], rest[:, QUAD : 2 * QUAD]
    cross_w, down_two = rest[:, 2 * QUAD : 3 * QUAD], rest[:, 3 * QUAD :]
    more = tie(
        net.hop(left, net.orders["a"][0]),
        net.hop(right, net.orders["b"][0]),
        net.arrive(self_w, "a", 2),
        net.arrive(cross_w, "b", 2),
    )
    left, right = [left, more[0]], [right, more[1]]
    self_w, cross_w = grown((self_w, cross_w), more[2:])
    source, self_w, cross_w, up_two, down_two = tie(source, self_w, cross_w, up_two, down_two)
    more = [
        net.arrive(self_w, "a", 3),
        net.arrive(cross_w, "b", 3),
        net.arrive(up_two, "a", 2),
        net.arrive(down_two, "b", 2),
    ]
    enc_attend_w = [(a, left, 0, cut), (b, right, 0, cut)]
    enc_feed_w = [(a, left, cut, QUAD), (b, right, cut + 1, QUAD)]
    enc_kept = attend_forward(source_pair, None, 0, source, None, enc_attend_w, False)
    enc_mid, small = enc_kept[7], enc_kept[8]
    enc_feed_kept = feed_forward(small, 5, HIDDEN_ROW, enc_mid, enc_feed_w)
    memory = enc_feed_kept[0]
    up_two, down_two = grown((up_two, down_two), tie(*more[2:], memory)[:2])
    self_w, cross_w = grown((self_w, cross_w), tie(*more[:2], up_two, down_two)[:2])
    target, up_two, down_two, self_w, cross_w = tie(target, up_two, down_two, self_w, cross_w)
    more = [net.arrive(up_two, "a", 3), net.arrive(down_two, "b", 3)]
    self_w = [(a, net.finish(self_w, "a"), 0, QUAD)]
    cross_w = [(b, net.finish(cross_w, "b"), 0, QUAD)]
    self_kept = attend_forward(target_pair, small, 8, target, None, self_w, True)
    dec_one = self_kept[7]
    cross_kept = attend_forward(cross_pair, small, 13, dec_one, memory, cross_w, False)
    dec_two = cross_kept[7]
    up_two, down_two = grown((up_two, down_two), tie(*more, dec_two)[:2])
    dec_feed_w = [(a, net.finish(up_two, "a"), 0, QUAD), (b, net.finish(down_two, "b"), 0, QUAD)]
    result, two_grad, dec_feed_small, feed_two = feed_both(
        (a, b), small, 18, HIDDEN_ROW + QUAD, dec_two, grad, dec_feed_w
    )

    names = ("a", "b")
    feed_two = core_hop(net, feed_two, (QUAD, QUAD)).split(names)
    one_grad, memory_grad, cross_small, cross_q = attend_backward(
        (a, b), cross_pair, small, 13, two_grad, cross_kept, dec_one, memory, cross_w, False, None
    )
    send = Round(feed_two, cross_small)
    memory_grad, *cross_q = send.before(memory_grad, *cross_q)
    send.go()
    cross_s = core_hop(net, cross_q, (cut, cut)).split(names)
    mid_grad, enc_feed_small, feed_one = feed_backward(
        (a, b), small, 5, memory_grad, enc_feed_kept, enc_mid, enc_feed_w
    )
    send = Round(feed_two + cross_s, enc_feed_small)
    one_grad, *feed_one = send.before(one_grad, *feed_one)
    send.go()
    feed_one = core_hop(net, feed_one, (QUAD, QUAD)).split(names)
    target_grad, _, self_small, self_q = attend_backward(
        (a, b), target_pair, small, 8, one_grad, self_kept, target, None, self_w, True, None
    )
    send = Round(feed_two + cross_s + feed_one, self_small)
    mid_grad, *self_q = send.before(mid_grad, *self_q)
    send.go()
    self_s = core_hop(net, self_q, (cut, cut)).split(names)
    others = (enc_feed_small, self_small, cross_small, dec_feed_small)
    source_grad, _, _, enc_q = attend_backward(
        (a, b), source_pair, small, 0, mid_grad, enc_kept, source, None, enc_attend_w, False, others
    )
    send = Round(feed_two + cross_s + feed_one + self_s, source_grad)
    enc_q = send.before(*enc_q)
    last = send.go()
    enc_s = core_hop(net, enc_q, (cut, cut + 1)).split(names)
    while enc_s[0].blocks > 1:
        send = Round([item for item in cross_s + feed_one + self_s + enc_s if item.blocks > 1], *last)
        last = send.go()

    square = [(0, index) for index in range(3 * QUAD)]
    tall, deep = [], []
    for layer in range(2):
        for index in range(QUAD):
            lanes = slice(index * source.shape[1], (index + 1) * source.shape[1])
            tall.append((1, (layer, slice(None), lanes)))
            deep.append((2, (layer, slice(index * BLOCK, (index + 1) * BLOCK))))
    targets = [square[:cut], square[cut:QUAD] + [(3, None)]]
    targets += [square[QUAD : QUAD + cut], square[QUAD + cut : 2 * QUAD], tall[:QUAD], deep[:QUAD]]
    targets += [tall[QUAD:], deep[QUAD:]]
    targets += [square[2 * QUAD : 2 * QUAD + cut], square[2 * QUAD + cut :]]
    segments = [item.segments[0] for item in enc_s + self_s + feed_one + feed_two + cross_s]
    segments = [segment + (target,) for segment, target in zip(segments, targets)]
    updated = last_update(at, segments, masters, firsts, seconds)
    return (memory, result, source_grad, target_grad), updated


def whole_step(pairs, source, target, grad, masters, firsts, seconds, axis_sizes):
    attention, up, down = [master.astype(BF) for master in masters[:3]]
    vectors, hidden = masters[3:]
    source_pair, target_pair, cross_pair = pairs
    small = gather_small(vectors, hidden)
    quads = gather_whole(attention, up, down)
    table = jnp.arange(source.shape[1] // BLOCK, dtype=jnp.int32)
    two = (table, table)
    parts = [(table, list(quad), 0, QUAD) for quad in quads]
    enc_kept = attend_forward(source_pair, small, 0, source, None, parts[:1], False)
    enc_mid = enc_kept[7]
    enc_feed_kept = feed_forward(small, 5, HIDDEN_ROW, enc_mid, parts[1:3])
    memory = enc_feed_kept[0]
    self_kept = attend_forward(target_pair, small, 8, target, None, parts[3:4], True)
    dec_one = self_kept[7]
    cross_kept = attend_forward(cross_pair, small, 13, dec_one, memory, parts[4:5], False)
    dec_two = cross_kept[7]
    result, two_grad, dec_feed_small, feed_two = feed_both(
        two, small, 18, HIDDEN_ROW + QUAD, dec_two, grad, parts[5:7]
    )
    one_grad, memory_grad, cross_small, cross_q = attend_backward(
        two, cross_pair, small, 13, two_grad, cross_kept, dec_one, memory, parts[4:5], False, None
    )
    target_grad, _, self_small, self_q = attend_backward(
        two, target_pair, small, 8, one_grad, self_kept, target, None, parts[3:4], True, None
    )
    mid_grad, enc_feed_small, feed_one = feed_backward(
        two, small, 5, memory_grad, enc_feed_kept, enc_mid, parts[1:3]
    )
    source_grad, _, enc_small, enc_q = attend_backward(
        two, source_pair, small, 0, mid_grad, enc_kept, source, None, parts[:1], False, None
    )
    quads = [enc_q]
    quads += [[half[:, low : low + QUAD] for half in feed_one] for low in (0, QUAD)]
    quads += [self_q, cross_q]
    quads += [[half[:, low : low + QUAD] for half in feed_two] for low in (0, QUAD)]
    smalls = (enc_small, enc_feed_small, self_small, cross_small, dec_feed_small)
    count = axis_sizes[0] * axis_sizes[1]
    shares = scatter_small(smalls, vectors, hidden, lax.axis_index(AXES), count)
    grads = tuple(scatter_whole(quads)) + shares
    updated = [
        adam_update(
            masters[slot], grads[slot], firsts[slot], seconds[slot], RATES[slot], DECAYS[slot]
        )
        for slot in range(5)
    ]
    flat = [updated[slot][kind] for kind in range(4) for slot in range(5)]
    return (memory, result, source_grad, target_grad), flat


def per_device(
    axis_sizes,
    source_tokens,
    target_tokens,
    source_segments,
    target_segments,
    output_grad,
    attention_weight,
    up_weight,
    down_weight,
    vectors,
    hidden_bias,
    *moments,
):
    masters = (attention_weight, up_weight, down_weight, vectors, hidden_bias)
    firsts = moments[:5]
    seconds = moments[5:]
    width = source_tokens.shape[2]
    pairs = (
        (source_segments, source_segments),
        (target_segments, target_segments),
        (target_segments, source_segments),
    )
    direct = axis_sizes[0] * axis_sizes[1] * BLOCK == width
    tokens, updated = (direct_step if direct else whole_step)(
        pairs,
        source_tokens[0],
        target_tokens[0],
        output_grad[0],
        masters,
        firsts,
        seconds,
        axis_sizes,
    )
    return tuple(array[None] for array in tokens) + tuple(updated)


def solution(mesh):
    rows = P(AXES, None, None)
    line = P(AXES, None)
    matrix = P(None, AXES, None)
    vector = P(None, AXES)
    state = (matrix, matrix, matrix, vector, vector)
    return jax.shard_map(
        functools.partial(per_device, (mesh.shape["dp"], mesh.shape["fsdp"])),
        mesh=mesh,
        in_specs=(rows, rows, line, line, rows) + state * 3,
        out_specs=(rows,) * 4 + state * 4,
        check_vma=False,
    )
```

```python
import functools

import jax
import jax.numpy as jnp
from jax import lax
from jax.experimental import pallas as pl
from jax.experimental.pallas import tpu as pltpu
from jax.sharding import PartitionSpec as P

HEADS = 8
STEP = 10
EPS_NORM = 1e-05
EPS_ADAM = 1e-08
BETA_ONE = 0.9
BETA_TWO = 0.999
LOWEST = -1e30
RATES = (0.05, 0.05, 0.05, 0.3, 0.3)
DECAYS = (0.01, 0.01, 0.01, 0.0, 0.0)
AXES = ("dp", "fsdp")
QUAD = 4
BLOCK = 16
CHUNK = 64
LANES = 128
SMALL_ROWS = 32
VMEM_BYTES = 60 * 1024 * 1024
HIDDEN_ROW = 24
BF = jnp.bfloat16
F32 = jnp.float32
VMEM = pl.BlockSpec(memory_space=pltpu.VMEM)
SMEM = pl.BlockSpec(memory_space=pltpu.SMEM)
ANY = pl.BlockSpec(memory_space=pl.ANY)
ROOT_TWO_PI = 0.7978845608028654
CUBIC = 0.044715


def dot(left, right):
    return jnp.dot(left, right, preferred_element_type=F32)


def dot_nt(left, right):
    return lax.dot_general(left, right, (((1,), (1,)), ((), ())), preferred_element_type=F32)


class Input:
    def __init__(self, array, room, sem):
        self.room = room
        self.shape = room.shape
        self.copy = pltpu.make_async_copy(array, room, sem)
        self.copy.start()
        self.there = False

    def wait(self):
        if not self.there:
            self.copy.wait()
            self.there = True

    def __getitem__(self, where):
        self.wait()
        return self.room[where]


class Output:
    def __init__(self, array, room, sem):
        self.array = array
        self.room = room
        self.shape = room.shape
        self.sem = sem
        self.left = False

    def __getitem__(self, where):
        return self.room[where]

    def __setitem__(self, where, value):
        self.room[where] = value

    def put(self, index=None):
        source = self.room if index is None else self.room.at[index]
        target = self.array if index is None else self.array.at[index]
        pltpu.make_async_copy(source, target, self.sem).start()
        self.left = True

    def finish(self):
        if not self.left:
            self.put()
        pltpu.make_async_copy(self.room, self.array, self.sem).wait()


def staged_kernel(kernel, scalars, inputs, others, outputs, targets, *refs):
    refs = list(refs)
    sems = refs.pop()
    count = inputs + outputs
    rooms = refs[len(refs) - count :]
    refs = refs[: len(refs) - count]
    at = scalars
    for slot in range(inputs):
        refs[at + slot] = Input(refs[at + slot], rooms[slot], sems.at[slot])
    at += inputs + others
    made = []
    for slot in range(inputs, count):
        place = at + slot - inputs
        refs[place] = Output(refs[place], rooms[slot], sems.at[slot])
        made.append(refs[place])
    kernel(*refs)
    for output in made:
        output.finish()


def part_copies(part, room, sems):
    _, arrays, low, number = part
    made = []
    first = 0
    for slot, array in enumerate(arrays):
        last = first + array.shape[0]
        made.append((array.at[:, low : low + number], room.at[first:last], sems.at[slot]))
        first = last
    return made


def load_start(part, room, sems):
    for outside, inside, sem in part_copies(part, room, sems):
        pltpu.make_async_copy(outside, inside, sem).start()


def load_wait(part, room, sems):
    for outside, inside, sem in part_copies(part, room, sems):
        pltpu.make_async_copy(outside, inside, sem).wait()


def store_start(part, room, sems):
    for outside, inside, sem in part_copies(part, room, sems)[::-1]:
        pltpu.make_async_copy(inside, outside, sem).start()


def store_wait(part, room, sems):
    for outside, inside, sem in part_copies(part, room, sems):
        pltpu.make_async_copy(inside, outside, sem).wait()


def matrix_of(part, room, index):
    table = part[0]
    return jnp.concatenate([room[table[block], index] for block in range(room.shape[0])], axis=0)


def matrix_put(part, room, index, value):
    table = part[0]
    value = value.astype(BF)
    for block in range(room.shape[0]):
        room[table[block], index] = value[block * BLOCK : (block + 1) * BLOCK]


def deep_of(part, room, index):
    table = part[0]
    number, subs, _, width = room.shape
    first = index * (number // QUAD)
    blocks = [room[table[first + at]] for at in range(number // QUAD)]
    return jnp.concatenate([block.reshape(subs * BLOCK, width) for block in blocks], axis=0)


def deep_put(part, room, index, value):
    table = part[0]
    number, subs, _, width = room.shape
    value = value.astype(BF).reshape(number // QUAD, subs, BLOCK, width)
    for at in range(number // QUAD):
        room[table[index * (number // QUAD) + at]] = value[at]


def column_sum(values):
    rows, width = values.shape
    return jnp.sum(values.reshape(rows // 8, 8, width), axis=0)


def total_of(sums):
    return jnp.sum(functools.reduce(jnp.add, sums), axis=0, keepdims=True)


def chunks(length, body, carry=()):
    def step(index, carry):
        return body(pl.ds(pl.multiple_of(index * CHUNK, CHUNK), CHUNK), carry)

    return lax.fori_loop(0, length // CHUNK, step, carry)


def norm_forward(pre_of, length, gain, shift, out_ref, hat_ref, rstd_ref):
    def body(rows, carry):
        pre = pre_of(rows)
        mean = jnp.mean(pre, axis=-1, keepdims=True)
        centred = pre - mean
        spread = jnp.mean(centred * centred, axis=-1, keepdims=True)
        rstd = lax.rsqrt(spread + EPS_NORM)
        hat = centred * rstd
        hat_ref[rows] = hat
        rstd_ref[rows] = jnp.broadcast_to(rstd, (CHUNK, LANES))
        out_ref[rows] = hat * gain + shift
        return carry

    chunks(length, body)
    for ref in (hat_ref, rstd_ref, out_ref):
        if isinstance(ref, Output):
            ref.put()


def norm_backward(grad_ref, hat_ref, rstd_ref, gain, pre_out, low_out):
    length, width = pre_out.shape
    ready(grad_ref, hat_ref, rstd_ref)

    def body(rows, sums):
        grad = grad_ref[rows].astype(F32)
        hat = hat_ref[rows]
        scaled = grad * gain
        one = jnp.mean(scaled, axis=-1, keepdims=True)
        two = jnp.mean(scaled * hat, axis=-1, keepdims=True)
        pre = rstd_ref[rows][:, :1] * (scaled - one - hat * two)
        low = pre.astype(BF)
        pre_out[rows] = pre
        low_out[rows] = low
        return (
            sums[0] + column_sum(grad * hat),
            sums[1] + column_sum(grad),
            sums[2] + column_sum(low.astype(F32)),
        )

    sums = chunks(length, body, (jnp.zeros((8, width), F32),) * 3)
    return [total_of([each]) for each in sums]


def ready(*refs):
    for ref in refs:
        if isinstance(ref, Input):
            ref.wait()


def lane_mask(rows):
    return lax.broadcasted_iota(jnp.int32, (rows, LANES), 1) < LANES // 2


def stacked_pair(block):
    first = lane_mask(block.shape[0])
    zero = jnp.zeros_like(block)
    return jnp.concatenate([jnp.where(first, block, zero), jnp.where(first, zero, block)], axis=0)


def merged_pair(stacked):
    rows = stacked.shape[0] // 2
    return jnp.where(lane_mask(rows), stacked[:rows], stacked[rows:])


def mask_fill(bias_ref, column_seg, row_seg, causal, transposed):
    length = bias_ref.shape[0]
    column = jnp.broadcast_to(column_seg, (LANES, length)).T
    for at in range(0, length, LANES):
        same = column == row_seg[:, at : at + LANES]
        if causal:
            down = lax.broadcasted_iota(jnp.int32, (length, LANES), 0)
            along = lax.broadcasted_iota(jnp.int32, (length, LANES), 1) + at
            order = (down <= along) if transposed else (along <= down)
            same = same & order
        bias_ref[:, at : at + LANES] = jnp.where(same, 0.0, LOWEST)


def take_parts(refs, layout, tables):
    parts = []
    for slot, (arrays, low, number) in enumerate(layout):
        parts.append((tables[slot], [refs.pop(0) for _ in range(arrays)], low, number))
    return parts


def small_part(part):
    table, arrays, low, number = part
    return table, arrays, low + number, 1


def small_join(blocks_ref, table):
    count = blocks_ref.shape[0]
    groups = blocks_ref.shape[3] // LANES
    per = count // groups
    vectors = []
    hidden = [[], []]
    for group in range(groups):
        total = blocks_ref[table[group * per], 0][:8].astype(F32)
        for at in range(group * per + 1, (group + 1) * per):
            total = total + blocks_ref[table[at], 0][:8].astype(F32)
        columns = [total[:, at : at + LANES] for at in range(0, 4 * LANES, LANES)]
        vectors.append(jnp.concatenate(columns[:3], axis=0))
        for layer in range(2):
            rows = [columns[3][4 * layer + at : 4 * layer + at + 1] for at in range(4)]
            hidden[layer].append(jnp.concatenate(rows, axis=1))
    return jnp.concatenate([jnp.concatenate(vectors, axis=1)] + hidden[0] + hidden[1], axis=0)


def small_split(whole, group):
    lanes = slice(group * LANES, (group + 1) * LANES)
    columns = [whole[at : at + 8, lanes] for at in (0, 8, 16)]
    rows = []
    for layer in range(2):
        row = whole[24 + 4 * layer + group : 25 + 4 * layer + group]
        rows += [row[:, at : at + LANES] for at in range(0, 4 * LANES, LANES)]
    columns.append(jnp.concatenate(rows, axis=0))
    block = jnp.concatenate(columns, axis=1)
    return jnp.concatenate([block, jnp.zeros_like(block)], axis=0).astype(BF)


def attend_forward_kernel(layout, cross, causal, base, joins, *refs):
    refs = list(refs)
    tables = [refs.pop(0) for _ in layout]
    query_seg = refs.pop(0)
    key_seg = refs.pop(0)
    small = None if joins else refs.pop(0)
    rows_ref = refs.pop(0)
    memory_ref = refs.pop(0) if cross else None
    parts = take_parts(refs, layout, tables)
    q_ref, k_ref, v_ref, o_ref, lse_ref, hat_ref, rstd_ref, out_ref = [refs.pop(0) for _ in range(8)]
    if joins:
        small = refs.pop(0)
        blocks_ref = refs.pop()
        extra = small_part(parts[-1])
    rooms = [refs.pop(0) for _ in parts]
    bias_ref, scores_ref, exponent_ref, largest_ref, mixed_ref, attended_ref, logs_ref, sems = refs
    if joins:
        load_start(extra, blocks_ref, sems.at[len(parts)])
    where = []
    for slot, part in enumerate(parts):
        load_start(part, rooms[slot], sems.at[slot])
        where += [(part, rooms[slot], index) for index in range(part[3])]
    length, width = rows_ref.shape
    mask_fill(bias_ref, query_seg[...], key_seg[...], causal, False)
    rows = rows_ref[...].astype(BF)
    keys = memory_ref[...].astype(BF) if cross else rows
    if joins:
        load_wait(extra, blocks_ref, sems.at[len(parts)])
        small[...] = small_join(blocks_ref, extra[0])
        small.put()
    for slot, part in enumerate(parts):
        load_wait(part, rooms[slot], sems.at[slot])
    scale = (width // HEADS) ** (-0.5)
    query = dot(rows, matrix_of(*where[0])) + small[base : base + 1]
    q_ref[...] = query.astype(BF) * jnp.asarray(scale, BF)
    k_ref[...] = dot(keys, matrix_of(*where[1])).astype(BF)
    v_ref[...] = (dot(keys, matrix_of(*where[2])) + small[base + 1 : base + 2]).astype(BF)
    for ref in (q_ref, k_ref, v_ref):
        ref.put()
    lane = lax.broadcasted_iota(jnp.int32, (CHUNK, LANES), 1)
    logs_ref[...] = jnp.zeros_like(logs_ref)

    def pair_body(pair, carry):
        lanes = pl.ds(pl.multiple_of(pair * LANES, LANES), LANES)
        scores_ref[...] = dot_nt(stacked_pair(q_ref[:, lanes]), k_ref[:, lanes])

        def body(index, carry):
            chunk = pl.ds(pl.multiple_of(index * CHUNK, CHUNK), CHUNK)
            own = pl.ds(pl.multiple_of(index * CHUNK % length, CHUNK), CHUNK)
            scores = scores_ref[chunk] + bias_ref[own]
            largest = jnp.max(scores, axis=-1, keepdims=True)
            exponent_ref[chunk] = jnp.exp(scores - largest).astype(BF)
            largest_ref[chunk] = jnp.broadcast_to(largest, (CHUNK, LANES))
            return carry

        lax.fori_loop(0, 2 * length // CHUNK, body, 0)
        values = jnp.concatenate([v_ref[:, lanes], jnp.ones((length, LANES), BF)], axis=1)
        mixed_ref[...] = dot(exponent_ref[...], values)

        def finish(rows, carry):
            outs = []
            logs = logs_ref[rows]
            for half in range(2):
                start = pl.multiple_of(rows.start + half * length, CHUNK)
                total = mixed_ref[pl.ds(start, CHUNK), LANES:]
                outs.append(mixed_ref[pl.ds(start, CHUNK), :LANES] / total)
                log_total = largest_ref[pl.ds(start, CHUNK)] + jnp.log(total)
                logs = jnp.where(lane == 2 * pair + half, log_total, logs)
            logs_ref[rows] = logs
            o_ref[rows, lanes] = jnp.where(lane_mask(CHUNK), outs[0], outs[1]).astype(BF)
            return carry

        chunks(length, finish)
        return carry

    lax.fori_loop(0, HEADS // 2, pair_body, 0)
    lse_ref[...] = logs_ref[...].T[:HEADS]
    o_ref.put()
    lse_ref.put()
    attended_ref[...] = dot(o_ref[...], matrix_of(*where[3]))
    out_bias = small[base + 2 : base + 3]
    norm_forward(
        lambda rows: rows_ref[rows].astype(F32) + (attended_ref[rows] + out_bias),
        length,
        small[base + 3 : base + 4],
        small[base + 4 : base + 5],
        out_ref,
        hat_ref,
        rstd_ref,
    )


def attend_backward_kernel(layout, cross, causal, base, splits, *refs):
    refs = list(refs)
    tables = [refs.pop(0) for _ in layout]
    out_tables = [refs.pop(0), refs.pop(0)]
    query_seg = refs.pop(0)
    key_seg = refs.pop(0)
    small = refs.pop(0)
    grad_ref = refs.pop(0)
    hat_ref, rstd_ref = refs.pop(0), refs.pop(0)
    rows_ref = refs.pop(0)
    memory_ref = refs.pop(0) if cross else None
    q_ref, k_ref, v_ref, o_ref, lse_ref = [refs.pop(0) for _ in range(5)]
    others = [refs.pop(0) for _ in range(4)] if splits else None
    parts = take_parts(refs, layout, tables)
    rows_out = refs.pop(0)
    memory_out = refs.pop(0) if cross else None
    small_out = None if splits else refs.pop(0)
    targets = [refs.pop(0), refs.pop(0)]
    outs = []
    for slot, table in enumerate(out_tables):
        extra = 1 if splits and slot else 0
        outs.append((table, targets, slot * QUAD // 2, QUAD // 2 + extra))
    rooms = [refs.pop(0) for _ in parts]
    out_rooms = [refs.pop(0), refs.pop(0)]
    bias_ref, dout_ref, dq_t_ref, dk_ref, dv_ref, kt_ref, low_ref = refs[:7]
    scores_ref, prob_grad_ref, prob_ref, score_grad_ref, dots_ref, sems = refs[7:]
    where = []
    for slot, part in enumerate(parts):
        load_start(part, rooms[slot], sems.at[slot])
        where += [(part, rooms[slot], index) for index in range(part[3])]
    length, width = rows_ref.shape
    head = width // HEADS
    scale = head ** (-0.5)
    gain_grad, shift_grad, out_bias = norm_backward(
        grad_ref, hat_ref, rstd_ref, small[base + 3 : base + 4], rows_out, low_ref
    )
    mask_fill(bias_ref, key_seg[...], query_seg[...], causal, True)
    low = low_ref[...]
    for slot, part in enumerate(parts):
        load_wait(part, rooms[slot], sems.at[slot])
    dout_ref[...] = dot_nt(low, matrix_of(*where[3])).astype(BF)
    matrix_put(outs[1], out_rooms[1], 1, dot(o_ref[...].T, low))
    product = dout_ref[...].astype(F32) * o_ref[...].astype(F32)
    high = product.astype(BF)
    rest = (product - high.astype(F32)).astype(BF)
    picker = lax.broadcasted_iota(jnp.int32, (BLOCK, width), 1) // head
    picker = (picker == lax.broadcasted_iota(jnp.int32, (BLOCK, width), 0)).astype(BF)
    dots_ref[...] = dot_nt(picker, high) + dot_nt(picker, rest)
    kt_ref[...] = k_ref[...].T
    ready(q_ref, k_ref, v_ref, lse_ref)

    def pair_body(pair, carry):
        lanes = pl.ds(pl.multiple_of(pair * LANES, LANES), LANES)
        query = q_ref[:, lanes]
        dout = dout_ref[:, lanes]
        scores_ref[...] = dot_nt(stacked_pair(k_ref[:, lanes]), query)
        prob_grad_ref[...] = dot_nt(stacked_pair(v_ref[:, lanes]), dout)

        def body(index, carry):
            which = pl.ds(2 * pair + index * CHUNK // length, 1)
            chunk = pl.ds(pl.multiple_of(index * CHUNK, CHUNK), CHUNK)
            own = pl.ds(pl.multiple_of(index * CHUNK % length, CHUNK), CHUNK)
            prob = jnp.exp(scores_ref[chunk] + (bias_ref[own] - lse_ref[which]))
            prob_ref[chunk] = prob.astype(BF)
            centred = prob_grad_ref[chunk] - dots_ref[which]
            score_grad_ref[chunk] = (prob * centred).astype(BF)
            return carry

        lax.fori_loop(0, 2 * length // CHUNK, body, 0)
        dv_ref[:, lanes] = merged_pair(dot(prob_ref[...], dout)).astype(BF)
        dk_ref[:, lanes] = merged_pair(dot(score_grad_ref[...], query)).astype(BF)
        for half in range(2):
            rows = pl.ds(pl.multiple_of(pair * LANES + half * head, head), head)
            own = slice(half * length, (half + 1) * length)
            dq_t_ref[rows, :] = dot(kt_ref[rows, :], score_grad_ref[own])
        return carry

    lax.fori_loop(0, HEADS // 2, pair_body, 0)
    query_grad = (dq_t_ref[...] * scale).T.astype(BF)
    key_grad = dk_ref[...]
    value_grad = dv_ref[...]
    turned = rows_ref[...].astype(BF).T
    other = memory_ref[...].astype(BF).T if cross else turned
    query_bias = total_of([column_sum(query_grad.astype(F32))])
    value_bias = total_of([column_sum(value_grad.astype(F32))])
    spare = jnp.zeros((3, width), F32)
    own = jnp.concatenate(
        [query_bias, value_bias, out_bias, gain_grad, shift_grad, spare], axis=0
    )
    if splits:
        enc_feed, self_attend, cross_attend, dec_feed = [other_small[...] for other_small in others]
        whole = small_rows(own, enc_feed, self_attend, cross_attend, dec_feed)
        table, room = outs[1][0], out_rooms[1]
        per = room.shape[0] * LANES // width
        for block in range(room.shape[0]):
            if block % per == 0:
                share = small_split(whole, block // per)
            room[table[block], QUAD // 2] = share
    else:
        small_out[...] = own
    matrix_put(outs[1], out_rooms[1], 0, dot(other, value_grad))
    store_start(outs[1], out_rooms[1], sems.at[1])
    matrix_put(outs[0], out_rooms[0], 0, dot(turned, query_grad))
    matrix_put(outs[0], out_rooms[0], 1, dot(other, key_grad))
    store_start(outs[0], out_rooms[0], sems.at[0])
    rows_back = rows_out[...] + dot_nt(query_grad, matrix_of(*where[0]))
    memory_back = dot_nt(key_grad, matrix_of(*where[1])) + dot_nt(value_grad, matrix_of(*where[2]))
    if cross:
        rows_out[...] = rows_back
        memory_out[...] = memory_back
        memory_out.put()
    else:
        rows_out[...] = rows_back + memory_back
    rows_out.put()
    for slot, part in enumerate(outs):
        store_wait(part, out_rooms[slot], sems.at[slot])


def small_rows(enc_attend, enc_feed, self_attend, cross_attend, dec_feed):
    return jnp.concatenate(
        [
            enc_attend[:5],
            enc_feed[:3],
            self_attend[:5],
            cross_attend[:5],
            dec_feed[:3],
            dec_feed[7:],
            dec_feed[7:],
            dec_feed[7:],
            enc_feed[3:7],
            dec_feed[3:7],
        ],
        axis=0,
    )


def gelu_parts(pre):
    square = pre * pre
    curve = jnp.tanh(ROOT_TWO_PI * pre * (1.0 + CUBIC * square))
    half = 0.5 * pre
    rise = 0.5 + 0.5 * curve
    bend = ROOT_TWO_PI * (1.0 + 3.0 * CUBIC * square)
    return pre * rise, rise + half * (1.0 - curve * curve) * bend


def feed_forward_steps(
    small, base, hidden_at, rows_ref, parts, up_ref, down_ref, active_ref, slope_ref, pre_ref, sum_ref
):
    rows = rows_ref[...].astype(BF)
    length = rows.shape[0]
    ready(small)

    def body(index, carry):
        pre_ref[...] = dot(rows, matrix_of(parts[0], up_ref, index))
        bias = small[pl.ds(hidden_at + index, 1)]

        def inner(chunk, carry):
            active, slope = gelu_parts(pre_ref[chunk] + bias)
            active_ref[index, chunk] = active.astype(BF)
            slope_ref[index, chunk] = slope
            return carry

        chunks(length, inner)
        for ref in (active_ref, slope_ref):
            if isinstance(ref, Output):
                ref.put(index)
        back = dot(active_ref[index], deep_of(parts[1], down_ref, index))
        sum_ref[...] += back
        return carry

    sum_ref[...] = jnp.zeros_like(sum_ref)
    lax.fori_loop(0, QUAD, body, 0)
    out_bias = small[base : base + 1]
    return lambda rows: rows_ref[rows] + (sum_ref[rows] + out_bias)


def feed_backward_steps(
    low_ref,
    rows_ref,
    parts,
    up_ref,
    down_ref,
    active_ref,
    slope_ref,
    dup_ref,
    ddown_ref,
    rows_out,
    small_out,
    back_ref,
    hidden_ref,
    outs,
    sems,
):
    low = low_ref[...]
    length, width = low.shape
    ready(active_ref, slope_ref)

    def deep_body(index, carry):
        deep_put(outs[1], ddown_ref, index, dot(active_ref[index].T, low))
        return carry

    lax.fori_loop(0, QUAD, deep_body, 0)
    store_start(outs[1], ddown_ref, sems.at[1])
    turned = rows_ref[...].astype(BF).T

    def body(index, carry):
        back_ref[...] = dot_nt(low, deep_of(parts[1], down_ref, index))

        def inner(chunk, total):
            hidden = (back_ref[chunk] * slope_ref[index, chunk]).astype(BF)
            hidden_ref[chunk] = hidden
            return total + column_sum(hidden.astype(F32))

        total = chunks(length, inner, jnp.zeros((8, width), F32))
        small_out[pl.ds(3 + index, 1)] = total_of([total])
        hidden = hidden_ref[...]
        matrix_put(outs[0], dup_ref, index, dot(turned, hidden))
        rows_out[...] += dot_nt(hidden, matrix_of(parts[0], up_ref, index))
        return carry

    lax.fori_loop(0, QUAD, body, 0)
    store_start(outs[0], dup_ref, sems.at[0])
    rows_out.put()


def load_feed(parts, rooms, sems):
    for slot, part in enumerate(parts):
        load_start(part, rooms[slot], sems.at[slot])


def wait_feed(parts, rooms, sems):
    for slot, part in enumerate(parts):
        load_wait(part, rooms[slot], sems.at[slot])


def end_feed(outs, rooms, sems):
    for slot, part in enumerate(outs):
        store_wait(part, rooms[slot], sems.at[slot])


def feed_outs(refs, tables):
    arrays = [refs.pop(0), refs.pop(0)]
    return [(tables[slot], arrays, slot * QUAD, QUAD) for slot in range(2)]


def feed_small(out_bias, gain_grad, shift_grad):
    spare = jnp.zeros((5, out_bias.shape[1]), F32)
    return jnp.concatenate([out_bias, gain_grad, shift_grad, spare], axis=0)


def feed_forward_kernel(layout, base, hidden_at, *refs):
    refs = list(refs)
    tables = [refs.pop(0), refs.pop(0)]
    small, rows_ref = refs.pop(0), refs.pop(0)
    parts = take_parts(refs, layout, tables)
    out_ref, hat_ref, rstd_ref, active_ref, slope_ref, up_ref, down_ref = refs[:7]
    pre_ref, sum_ref, sems = refs[7:]
    load_feed(parts, (up_ref, down_ref), sems)
    wait_feed(parts, (up_ref, down_ref), sems)
    pre_of = feed_forward_steps(
        small, base, hidden_at, rows_ref, parts, up_ref, down_ref, active_ref, slope_ref, pre_ref, sum_ref
    )
    gain, shift = small[base + 1 : base + 2], small[base + 2 : base + 3]
    norm_forward(pre_of, rows_ref.shape[0], gain, shift, out_ref, hat_ref, rstd_ref)


def feed_backward_kernel(layout, base, *refs):
    refs = list(refs)
    tables = [refs.pop(0), refs.pop(0)]
    out_tables = [refs.pop(0), refs.pop(0)]
    small, grad_ref, hat_ref, rstd_ref, rows_ref = [refs.pop(0) for _ in range(5)]
    active_ref, slope_ref = refs.pop(0), refs.pop(0)
    parts = take_parts(refs, layout, tables)
    rows_out, small_out = refs.pop(0), refs.pop(0)
    outs = feed_outs(refs, out_tables)
    up_ref, down_ref, dup_ref, ddown_ref, low_ref, back_ref, hidden_ref, sems, out_sems = refs
    load_feed(parts, (up_ref, down_ref), sems)
    gain_grad, shift_grad, out_bias = norm_backward(
        grad_ref, hat_ref, rstd_ref, small[base + 1 : base + 2], rows_out, low_ref
    )
    wait_feed(parts, (up_ref, down_ref), sems)
    small_out[...] = feed_small(out_bias, gain_grad, shift_grad)
    feed_backward_steps(
        low_ref,
        rows_ref,
        parts,
        up_ref,
        down_ref,
        active_ref,
        slope_ref,
        dup_ref,
        ddown_ref,
        rows_out,
        small_out,
        back_ref,
        hidden_ref,
        outs,
        out_sems,
    )
    end_feed(outs, (dup_ref, ddown_ref), out_sems)


def feed_both_kernel(layout, base, hidden_at, *refs):
    refs = list(refs)
    tables = [refs.pop(0), refs.pop(0)]
    out_tables = [refs.pop(0), refs.pop(0)]
    small, rows_ref, grad_ref = [refs.pop(0) for _ in range(3)]
    parts = take_parts(refs, layout, tables)
    out_ref, rows_out, small_out = [refs.pop(0) for _ in range(3)]
    outs = feed_outs(refs, out_tables)
    up_ref, down_ref, dup_ref, ddown_ref, low_ref, back_ref, hidden_ref, sum_ref = refs[:8]
    active_ref, slope_ref, hat_ref, rstd_ref, sems, out_sems = refs[8:]
    load_feed(parts, (up_ref, down_ref), sems)
    wait_feed(parts, (up_ref, down_ref), sems)
    pre_of = feed_forward_steps(
        small, base, hidden_at, rows_ref, parts, up_ref, down_ref, active_ref, slope_ref, back_ref, sum_ref
    )
    gain, shift = small[base + 1 : base + 2], small[base + 2 : base + 3]
    norm_forward(pre_of, rows_ref.shape[0], gain, shift, out_ref, hat_ref, rstd_ref)
    gain_grad, shift_grad, out_bias = norm_backward(
        grad_ref, hat_ref, rstd_ref, gain, rows_out, low_ref
    )
    small_out[...] = feed_small(out_bias, gain_grad, shift_grad)
    feed_backward_steps(
        low_ref,
        rows_ref,
        parts,
        up_ref,
        down_ref,
        active_ref,
        slope_ref,
        dup_ref,
        ddown_ref,
        rows_out,
        small_out,
        back_ref,
        hidden_ref,
        outs,
        out_sems,
    )
    end_feed(outs, (dup_ref, ddown_ref), out_sems)


def shaped(shape, dtype=F32):
    return jax.ShapeDtypeStruct(shape, dtype)


def call(
    kernel, scalars, inputs, others, outs, targets, scratch, flops, moved, limit=VMEM_BYTES
):
    rooms = [pltpu.VMEM(array.shape, array.dtype) for array in list(inputs) + list(outs)]
    return pl.pallas_call(
        functools.partial(
            staged_kernel, kernel, len(scalars), len(inputs), len(others), len(outs), len(targets)
        ),
        out_shape=list(outs) + list(targets),
        in_specs=[SMEM] * len(scalars) + [ANY] * (len(inputs) + len(others)),
        out_specs=[ANY] * (len(outs) + len(targets)),
        scratch_shapes=scratch + rooms + [pltpu.SemaphoreType.DMA((len(rooms),))],
        cost_estimate=pl.CostEstimate(flops=flops, bytes_accessed=moved, transcendentals=0),
        compiler_params=pltpu.CompilerParams(vmem_limit_bytes=limit),
    )(*scalars, *inputs, *others)


def layout_of(parts):
    return [(len(arrays), low, number) for _, arrays, low, number in parts]


def arrays_of(parts):
    return [array for part in parts for array in part[1]]


def most(parts):
    return max(len(part[1]) for part in parts)


def halves(width, number):
    return [shaped((width // BLOCK // 2, number, BLOCK, width), BF)] * 2


def attend_forward(segments, small, base, rows, memory, parts, causal):
    length, width = rows.shape
    cross = memory is not None
    joins = small is None
    scalars = [part[0] for part in parts]
    inputs = list(segments) + ([] if joins else [small]) + [rows] + ([memory] if cross else [])
    outs = [shaped((length, width), BF)] * 4 + [shaped((HEADS, length))]
    outs += [shaped((length, width)), shaped((length, LANES)), shaped((length, width))]
    outs += [shaped((SMALL_ROWS, width))] if joins else []
    scratch = [
        pltpu.VMEM((length, length), F32),
        pltpu.VMEM((2 * length, length), F32),
        pltpu.VMEM((2 * length, length), BF),
        pltpu.VMEM((2 * length, LANES), F32),
        pltpu.VMEM((2 * length, 2 * LANES), F32),
        pltpu.VMEM((length, width), F32),
        pltpu.VMEM((length, LANES), F32),
        pltpu.SemaphoreType.DMA((len(parts) + 1, most(parts))),
    ]
    scratch = part_rooms(width, [part[3] for part in parts]) + scratch
    scratch += part_rooms(width, [1]) if joins else []
    kernel = functools.partial(attend_forward_kernel, layout_of(parts), cross, causal, base, joins)
    flops = 8 * length * width * width + 16 * length * length * width
    return call(kernel, scalars, inputs, arrays_of(parts), outs, [], scratch, flops, 8_000_000)


def attend_backward(
    out_tables, segments, small, base, grad, kept, rows, memory, parts, causal, others
):
    length, width = rows.shape
    cross = memory is not None
    splits = others is not None
    q, k, v, o, lse, hat, rstd = kept[:7]
    scalars = [part[0] for part in parts] + list(out_tables)
    inputs = list(segments) + [small, grad, hat, rstd, rows]
    inputs += ([memory] if cross else []) + [q, k, v, o, lse] + list(others or ())
    outs = [shaped((length, width))] * (2 if cross else 1)
    outs += [] if splits else [shaped((8, width))]
    targets = halves(width, QUAD + (1 if splits else 0))
    scratch = [
        pltpu.VMEM((length, length), F32),
        pltpu.VMEM((length, width), BF),
        pltpu.VMEM((width, length), F32),
        pltpu.VMEM((length, width), BF),
        pltpu.VMEM((length, width), BF),
        pltpu.VMEM((width, length), BF),
        pltpu.VMEM((length, width), BF),
        pltpu.VMEM((2 * length, length), F32),
        pltpu.VMEM((2 * length, length), F32),
        pltpu.VMEM((2 * length, length), BF),
        pltpu.VMEM((2 * length, length), BF),
        pltpu.VMEM((BLOCK, length), F32),
        pltpu.SemaphoreType.DMA((3, 2)),
    ]
    numbers = [part[3] for part in parts] + [QUAD // 2, QUAD // 2 + (1 if splits else 0)]
    scratch = part_rooms(width, numbers) + scratch
    kernel = functools.partial(
        attend_backward_kernel, layout_of(parts), cross, causal, base, splits
    )
    flops = 16 * length * width * width + 40 * length * length * width
    arrays = arrays_of(parts)
    results = list(call(kernel, scalars, inputs, arrays, outs, targets, scratch, flops, 12_000_000))
    rows_grad = results.pop(0)
    memory_grad = results.pop(0) if cross else None
    small_grad = None if splits else results.pop(0)
    return rows_grad, memory_grad, small_grad, results


def part_rooms(width, numbers):
    return [pltpu.VMEM((width // BLOCK, number, BLOCK, width), BF) for number in numbers]


def feed_scratch(width, grads):
    return part_rooms(width, [QUAD] * (4 if grads else 2))


def feed_forward(small, base, hidden_at, rows, parts):
    length, width = rows.shape
    scalars = [part[0] for part in parts]
    outs = [shaped((length, width)), shaped((length, width)), shaped((length, LANES))]
    outs += [shaped((QUAD, length, width), BF), shaped((QUAD, length, width))]
    scratch = feed_scratch(width, False)
    scratch += [pltpu.VMEM((length, width), F32), pltpu.VMEM((length, width), F32)]
    scratch += [pltpu.SemaphoreType.DMA((2, most(parts)))]
    kernel = functools.partial(feed_forward_kernel, layout_of(parts), base, hidden_at)
    flops = 16 * length * width * width
    arrays = arrays_of(parts)
    return call(kernel, scalars, [small, rows], arrays, outs, [], scratch, flops, 10_000_000)


def feed_backward(out_tables, small, base, grad, kept, rows, parts):
    length, width = rows.shape
    hat, rstd, active, slope = kept[1:]
    scalars = [part[0] for part in parts] + list(out_tables)
    inputs = [small, grad, hat, rstd, rows, active, slope]
    outs = [shaped((length, width)), shaped((8, width))]
    targets = halves(width, 2 * QUAD)
    scratch = feed_scratch(width, True)
    scratch += [pltpu.VMEM((length, width), BF), pltpu.VMEM((length, width), F32)]
    scratch += [pltpu.VMEM((length, width), BF)]
    scratch += [pltpu.SemaphoreType.DMA((2, most(parts))), pltpu.SemaphoreType.DMA((2, 2))]
    kernel = functools.partial(feed_backward_kernel, layout_of(parts), base)
    flops = 32 * length * width * width
    arrays = arrays_of(parts)
    results = call(kernel, scalars, inputs, arrays, outs, targets, scratch, flops, 14_000_000)
    return results[0], results[1], results[2:4]


def feed_both(out_tables, small, base, hidden_at, rows, grad, parts):
    length, width = rows.shape
    scalars = [part[0] for part in parts] + list(out_tables)
    outs = [shaped((length, width)), shaped((length, width)), shaped((8, width))]
    targets = halves(width, 2 * QUAD)
    scratch = feed_scratch(width, True) + [
        pltpu.VMEM((length, width), BF),
        pltpu.VMEM((length, width), F32),
        pltpu.VMEM((length, width), BF),
        pltpu.VMEM((length, width), F32),
        pltpu.VMEM((QUAD, length, width), BF),
        pltpu.VMEM((QUAD, length, width), F32),
        pltpu.VMEM((length, width), F32),
        pltpu.VMEM((length, LANES), F32),
        pltpu.SemaphoreType.DMA((2, most(parts))),
        pltpu.SemaphoreType.DMA((2, 2)),
    ]
    kernel = functools.partial(feed_both_kernel, layout_of(parts), base, hidden_at)
    flops = 48 * length * width * width
    arrays = arrays_of(parts)
    results = call(kernel, scalars, [small, rows, grad], arrays, outs, targets, scratch, flops, 12_000_000)
    return results[0], results[1], results[2], results[3:5]


def first_kernel(
    at_ref,
    vector_ref,
    hidden_ref,
    square_ref,
    tall_ref,
    deep_ref,
    one_ref,
    two_ref,
    turn_ref,
    line_ref,
):
    at = at_ref[0]
    width = square_ref.shape[2]
    turn_ref[...] = jnp.zeros_like(turn_ref)
    lanes, rows = vector_ref.shape
    turn_ref[pl.ds(pl.multiple_of(at * lanes, lanes), lanes), :rows] = vector_ref[...]
    upright = turn_ref[...].T
    line_ref[...] = jnp.zeros_like(line_ref)
    layers, lanes = hidden_ref.shape
    per = LANES // lanes
    for layer in range(layers):
        row = jnp.concatenate([hidden_ref[layer : layer + 1]] * per, axis=1)
        lane = lax.broadcasted_iota(jnp.int32, row.shape, 1) // lanes
        row = jnp.where(lane == at % per, row, 0.0)
        line_ref[pl.ds(4 * layer + at // per, 1), :] = row
    columns = [upright[low : low + 8] for low in (0, 8, 16)] + [line_ref[...]]
    block = jnp.concatenate(columns, axis=1)
    small = jnp.concatenate([block, jnp.zeros_like(block)], axis=0)
    tall = []
    deep = []
    for layer in range(2):
        for index in range(QUAD):
            lanes = slice(index * width, (index + 1) * width)
            tall.append(tall_ref[layer, :, lanes])
            deep.append(deep_ref[layer, index * BLOCK : (index + 1) * BLOCK])
    square = [square_ref[index] for index in range(3 * QUAD)]
    cut = QUAD // 2
    groups = [
        square[:cut] + tall[:QUAD] + square[cut:QUAD] + [small] + deep[:QUAD],
        square[QUAD : 2 * QUAD] + tall[QUAD:] + square[2 * QUAD :] + deep[QUAD:],
    ]
    for out_ref, group in zip((one_ref, two_ref), groups):
        for slot, block in enumerate(group):
            out_ref[0, slot] = block.astype(BF)
        out_ref.put()


def first_arrays(at, square, tall, deep, vectors, hidden):
    width = square.shape[2]
    outs = [
        shaped((1, 3 * QUAD + 1, BLOCK, width), BF),
        shaped((1, 4 * QUAD, BLOCK, width), BF),
    ]
    scratch = [pltpu.VMEM((LANES, LANES), F32), pltpu.VMEM((8, LANES), F32)]
    inputs = [vectors.T, hidden, square, tall, deep]
    return call(first_kernel, [at], inputs, [], outs, [], scratch, 0, 4_000_000)


def last_kernel(plan, count, at_ref, *refs):
    masters, firsts, seconds = refs[:5], refs[5:10], refs[10:15]
    arrays, refs = refs[15 : 15 + count], refs[15 + count :]
    outs, refs = [refs[5 * kind : 5 * kind + 5] for kind in range(4)], refs[20:]
    buffers, turn_ref, line_ref, sems = refs
    at = at_ref[0]
    starts = []
    for width, pieces, _ in plan:
        for index, low in pieces:
            array = arrays[index]
            array = array if len(array.shape) == 3 else array.at[0]
            source = array.at[low : low + width]
            copy = pltpu.make_async_copy(source, buffers.at[len(starts), :width], sems.at[len(starts)])
            copy.start()
            starts.append(copy)

    def update(slot, where, gradient):
        results = adam_update(
            masters[slot][where],
            gradient,
            firsts[slot][where],
            seconds[slot][where],
            RATES[slot],
            DECAYS[slot],
        )
        for kind in range(4):
            outs[kind][slot][where] = results[kind]

    def small_update(gradient):
        turn_ref[...] = jnp.zeros_like(turn_ref)
        for column in range(3):
            lanes = slice(column * LANES, (column + 1) * LANES)
            turn_ref[8 * column : 8 * column + 8, :] = gradient[:8, lanes]
        turn_ref[...] = turn_ref[...].T
        lanes, rows = masters[3].shape
        share = turn_ref[pl.ds(pl.multiple_of(at * lanes, lanes), lanes), :][:, :rows]
        update(3, slice(None), share)
        line_ref[...] = gradient[:8, 3 * LANES :]
        layers, lanes = masters[4].shape
        per = LANES // lanes
        for layer in range(layers):
            row = line_ref[pl.ds(4 * layer + at // per, 1), :]
            share = row[:, :lanes]
            for part in range(1, per):
                other = row[:, part * lanes : (part + 1) * lanes]
                share = jnp.where(at % per == part, other, share)
            update(4, slice(layer, layer + 1), share)

    ready(*masters, *firsts, *seconds)

    def gradient_of(begin, number, sub):
        value = buffers[begin, sub].astype(F32)
        for index in range(1, number):
            value = value + buffers[begin + index, sub].astype(F32)
        return value

    begin = 0
    for slot, (width, pieces, targets) in enumerate(plan):
        for index in range(len(pieces)):
            starts[begin + index].wait()
        kind, first = targets
        count = 2 * (width // 2)

        def body(sub, carry, begin=begin, number=len(pieces), kind=kind, first=first):
            gradient = gradient_of(begin, number, sub)
            if kind == 0:
                update(0, first + sub, gradient)
            elif kind == 1:
                columns = gradient.shape[1]
                lanes = pl.ds(pl.multiple_of(sub * columns, columns), columns)
                update(1, (first, slice(None), lanes), gradient)
            else:
                rows = pl.ds(pl.multiple_of(sub * BLOCK, BLOCK), BLOCK)
                update(2, (first, rows), gradient)
            return carry

        lax.fori_loop(0, count, body, 0)
        if width > count:
            small_update(gradient_of(begin, len(pieces), count))
        begin += len(pieces)
        for kind in range(3):
            if [at for at, each in enumerate(plan) if each[2][0] == kind][-1] == slot:
                for each in outs:
                    each[kind].put()


def last_update(at, segments, masters, firsts, seconds):
    arrays = []
    plan = []
    for width, pieces, targets in segments:
        entry = []
        for array, low in pieces:
            found = [place for place, other in enumerate(arrays) if other is array]
            if not found:
                arrays.append(array)
            entry.append((found[0] if found else len(arrays) - 1, low))
        plan.append((width, entry, targets))
    params = [list(group) for group in (masters, firsts, seconds)]
    for group in params:
        group[3] = group[3].T
    flat = params[0] + params[1] + params[2]
    outs = [shaped(array.shape) for array in params[0]] * 3
    outs += [shaped(array.shape, BF) for array in params[0]]
    pieces = sum(len(entry[1]) for entry in plan)
    block = masters[0].shape[1:]
    scratch = [
        pltpu.VMEM((pieces, max(entry[0] for entry in plan)) + block, BF),
        pltpu.VMEM((LANES, LANES), F32),
        pltpu.VMEM((8, LANES), F32),
        pltpu.SemaphoreType.DMA((pieces,)),
    ]
    kernel = functools.partial(last_kernel, plan, len(arrays))
    results = call(
        kernel, [at], flat, arrays, outs, [], scratch, 0, 8_000_000, VMEM_BYTES // 2
    )
    results = list(results)
    for kind in range(4):
        results[5 * kind + 3] = results[5 * kind + 3].T
    return results


def tie(*arrays):
    return lax.optimization_barrier(arrays)


class Direct:
    def __init__(self, axis_sizes):
        outer, inner = axis_sizes
        self.count = outer * inner
        inner_bits = inner.bit_length() - 1
        bits = self.count.bit_length() - 1
        core = [inner_bits]
        across = list(range(inner_bits + 1, bits))
        up = [0]
        along = list(range(1, inner_bits))
        self.orders = {
            "a": core + across + up + along,
            "b": core + up + across + along,
        }
        self.place = lax.axis_index(AXES)

    def hop(self, array, bit):
        return lax.ppermute(array, AXES, [(at, at ^ (1 << bit)) for at in range(self.count)])

    def table(self, name):
        order = self.orders[name]
        apart = jnp.arange(self.count, dtype=jnp.int32) ^ self.place
        place = jnp.zeros_like(apart)
        for at, bit in enumerate(order):
            place = place | (((apart >> bit) & 1) << (len(order) - 1 - at))
        return place

    def arrive(self, array, name, step):
        return self.hop(array, self.orders[name][::-1][step])

    def finish(self, array, name):
        return [array, self.hop(array, self.orders[name][0])]


def grown(arrays, arrivals):
    return [jnp.concatenate(pair, axis=0) for pair in zip(arrays, arrivals)]


class Sum:
    def __init__(self, net, name, segments, done, blocks):
        self.net = net
        self.name = name
        self.segments = segments
        self.done = done
        self.blocks = blocks

    def bit(self):
        return self.net.orders[self.name][self.done]

    def split(self, names):
        return [
            Sum(self.net, name, [segment], self.done, self.blocks)
            for name, segment in zip(names, self.segments)
        ]


def core_hop(net, pair, widths):
    keep, send = pair
    arrived = net.hop(send, net.orders["a"][0])
    low = 0
    segments = []
    for width in widths:
        segments.append((width, [(keep, low), (arrived, low)]))
        low += width
    return Sum(net, "a", segments, 1, keep.shape[0])


def combine_kernel(plan, count, outputs, *refs):
    arrays, refs = refs[:count], refs[count:]
    outs, buffers, sems = refs[:outputs], refs[outputs:-1], refs[-1]
    starts = []
    for _, _, held, number, width, pieces in plan:
        begin = 0 if held is not None else number
        for index, low in pieces:
            array = arrays[index]
            if len(array.shape) == 3:
                source = array.at[low + begin * width : low + 2 * number * width]
            else:
                source = array.at[begin : 2 * number, low : low + width]
            copy = pltpu.make_async_copy(source, buffers[len(starts)], sems.at[len(starts)])
            copy.start()
            starts.append(copy)
    begin = 0
    for slot, first, held, number, width, pieces in plan:
        for index in range(begin, begin + len(pieces)):
            starts[index].wait()
        mine = buffers[begin : begin + len(pieces)]
        jobs = [(slot, first, 0)] if held is None else [(slot, first, number), (outputs - 1, held, 0)]
        for out, place, skip in jobs:

            def body(block, carry, out=out, place=place, skip=skip, width=width, mine=mine):
                value = None
                for buffer in mine:
                    flat = len(buffer.shape) == 3
                    at = block + skip
                    part = buffer[pl.ds(at * width, width)] if flat else buffer[at]
                    value = part.astype(F32) if value is None else value + part.astype(F32)
                outs[out][pl.ds(place + block * width, width)] = value.astype(BF)
                return carry

            lax.fori_loop(0, number, body, 0)
        begin += len(pieces)


class Round:
    def __init__(self, sums, *tokens, limit=VMEM_BYTES // 3):
        self.net = sums[0].net
        self.sums = sums
        self.bits = sorted({item.bit() for item in sums})
        arrays = []
        plan = []
        sizes = [0] * len(self.bits) + [0]
        self.places = []
        block = None
        for item in sums:
            slot = self.bits.index(item.bit())
            number = item.blocks // 2
            holds = item.done > 1
            places = []
            for width, pieces in item.segments:
                entry = []
                for array, low in pieces:
                    found = [at for at, other in enumerate(arrays) if other is array]
                    if not found:
                        arrays.append(array)
                    entry.append((found[0] if found else len(arrays) - 1, low))
                    block = array.shape[-2:]
                held = sizes[-1] if holds else None
                plan.append((slot, sizes[slot], held, number, width, entry))
                places.append((sizes[slot], held))
                sizes[slot] += number * width
                sizes[-1] += number * width if holds else 0
            self.places.append((slot, places))
        tied = list(tie(*arrays, *tokens))[: len(arrays)] if tokens else arrays
        scratch = []
        moved = 0
        for _, _, held, number, width, entry in plan:
            both = number if held is None else 2 * number
            moved += both * width * (len(entry) + 1) * 16384
            for index, _ in entry:
                flat = len(arrays[index].shape) == 3
                shape = (both * width,) if flat else (both, width)
                scratch.append(pltpu.VMEM(shape + block, BF))
        if not sizes[-1]:
            sizes.pop()
        self.sends = pl.pallas_call(
            functools.partial(combine_kernel, plan, len(tied), len(sizes)),
            out_shape=[shaped((size,) + block, BF) for size in sizes],
            in_specs=[ANY] * len(tied),
            out_specs=[VMEM] * len(sizes),
            scratch_shapes=scratch + [pltpu.SemaphoreType.DMA((len(scratch),))],
            cost_estimate=pl.CostEstimate(flops=0, bytes_accessed=moved, transcendentals=0),
            compiler_params=pltpu.CompilerParams(vmem_limit_bytes=limit),
        )(*tied)

    def before(self, *arrays):
        tied = tie(*arrays, *self.sends)
        self.sends = list(tied[len(arrays) :])
        return tied[: len(arrays)]

    def go(self):
        arrived = [self.net.hop(send, bit) for send, bit in zip(self.sends, self.bits)]
        for item, (slot, places) in zip(self.sums, self.places):
            made = []
            for (width, pieces), (place, held) in zip(item.segments, places):
                stay = pieces if held is None else [(self.sends[-1], held)]
                made.append((width, stay + [(arrived[slot], place)]))
            item.segments = made
            item.done += 1
            item.blocks //= 2
        return arrived


def adam_update(weight, gradient, first, second, rate, decay):
    first_new = BETA_ONE * first + (1.0 - BETA_ONE) * gradient
    second_new = BETA_TWO * second + (1.0 - BETA_TWO) * gradient * gradient
    first_hat = first_new / (1.0 - BETA_ONE**STEP)
    second_hat = second_new / (1.0 - BETA_TWO**STEP)
    weight_new = weight - rate * (first_hat / (jnp.sqrt(second_hat) + EPS_ADAM) + decay * weight)
    return (weight_new, first_new, second_new, weight_new.astype(BF))


def gather_small(vectors, hidden):
    whole = lax.all_gather(vectors.astype(BF), AXES, axis=1, tiled=True)
    deep = lax.all_gather(hidden.astype(BF), AXES, axis=1, tiled=True)
    whole = jnp.pad(whole, ((0, HIDDEN_ROW - whole.shape[0]), (0, 0)))
    return jnp.concatenate([whole, deep.reshape(-1, whole.shape[1])], axis=0).astype(F32)


def scatter_small(grads, vectors, hidden, place, count):
    whole = lax.psum(small_rows(*grads), AXES)
    rows, lanes = vectors.shape
    first = lax.dynamic_slice_in_dim(whole[:rows], place * lanes, lanes, axis=1)
    layers, lanes = hidden.shape
    deep = whole[HIDDEN_ROW:].reshape(layers, -1)
    return first, lax.dynamic_slice_in_dim(deep, place * lanes, lanes, axis=1)


def gather_whole(attention, up, down):
    width = attention.shape[2]
    number = width // BLOCK
    square = lax.all_gather(attention, AXES, axis=1, tiled=True)
    square = square.reshape(-1, QUAD, number, BLOCK, width).transpose(0, 2, 1, 3, 4)
    tall = lax.all_gather(up, AXES, axis=1, tiled=True)
    tall = tall.reshape(2, number, BLOCK, QUAD, width).transpose(0, 1, 3, 2, 4)
    deep = lax.all_gather(down, AXES, axis=1, tiled=True).reshape(2, number, QUAD, BLOCK, width)
    half = number // 2
    quads = [square[0], tall[0], deep[0], square[1], square[2], tall[1], deep[1]]
    return [(quad[:half], quad[half:]) for quad in quads]


def scatter_whole(quads):
    joined = [jnp.concatenate(pair, axis=0).astype(F32) for pair in quads]
    number, _, _, width = joined[0].shape
    square = jnp.stack([joined[0], joined[3], joined[4]])
    square = square.transpose(0, 2, 1, 3, 4).reshape(3 * QUAD, width, width)
    tall = jnp.stack([joined[1], joined[5]]).transpose(0, 1, 3, 2, 4)
    tall = tall.reshape(2, width, QUAD * width)
    deep = jnp.stack([joined[2], joined[6]]).reshape(2, QUAD * width, width)
    return [
        lax.psum_scatter(part, AXES, scatter_dimension=1, tiled=True)
        for part in (square, tall, deep)
    ]


def direct_step(pairs, source, target, grad, masters, firsts, seconds, axis_sizes):
    net = Direct(axis_sizes)
    source_pair, target_pair, cross_pair = pairs
    a, b = net.table("a"), net.table("b")
    cut = QUAD // 2
    at = (net.place % (net.count * LANES // source.shape[1])).astype(jnp.int32).reshape(1)

    one, rest = first_arrays(at, *masters)
    (one,) = grown([one], [net.arrive(one, "a", 0)])
    (one,) = grown([one], [net.arrive(one, "a", 1)])
    left, right = one[:, : cut + QUAD], one[:, cut + QUAD :]
    rest, left, right = tie(rest, left, right)
    for step in (2, 3):
        more = tie(
            net.arrive(left, "a", step),
            net.arrive(right, "b", step),
            net.arrive(rest, "a", step - 2),
        )
        left, right, rest = grown((left, right, rest), more)
    self_w, up_two = rest[:, :QUAD], rest[:, QUAD : 2 * QUAD]
    cross_w, down_two = rest[:, 2 * QUAD : 3 * QUAD], rest[:, 3 * QUAD :]
    more = tie(
        net.hop(left, net.orders["a"][0]),
        net.hop(right, net.orders["b"][0]),
        net.arrive(self_w, "a", 2),
        net.arrive(cross_w, "b", 2),
    )
    left, right = [left, more[0]], [right, more[1]]
    self_w, cross_w = grown((self_w, cross_w), more[2:])
    source, self_w, cross_w, up_two, down_two = tie(source, self_w, cross_w, up_two, down_two)
    more = [
        net.arrive(self_w, "a", 3),
        net.arrive(cross_w, "b", 3),
        net.arrive(up_two, "a", 2),
        net.arrive(down_two, "b", 2),
    ]
    enc_attend_w = [(a, left, 0, cut), (b, right, 0, cut)]
    enc_feed_w = [(a, left, cut, QUAD), (b, right, cut + 1, QUAD)]
    enc_kept = attend_forward(source_pair, None, 0, source, None, enc_attend_w, False)
    enc_mid, small = enc_kept[7], enc_kept[8]
    enc_feed_kept = feed_forward(small, 5, HIDDEN_ROW, enc_mid, enc_feed_w)
    memory = enc_feed_kept[0]
    up_two, down_two = grown((up_two, down_two), tie(*more[2:], memory)[:2])
    self_w, cross_w = grown((self_w, cross_w), tie(*more[:2], up_two, down_two)[:2])
    target, up_two, down_two, self_w, cross_w = tie(target, up_two, down_two, self_w, cross_w)
    more = [net.arrive(up_two, "a", 3), net.arrive(down_two, "b", 3)]
    self_w = [(a, net.finish(self_w, "a"), 0, QUAD)]
    cross_w = [(b, net.finish(cross_w, "b"), 0, QUAD)]
    self_kept = attend_forward(target_pair, small, 8, target, None, self_w, True)
    dec_one = self_kept[7]
    cross_kept = attend_forward(cross_pair, small, 13, dec_one, memory, cross_w, False)
    dec_two = cross_kept[7]
    up_two, down_two = grown((up_two, down_two), tie(*more, dec_two)[:2])
    dec_feed_w = [(a, net.finish(up_two, "a"), 0, QUAD), (b, net.finish(down_two, "b"), 0, QUAD)]
    result, two_grad, dec_feed_small, feed_two = feed_both(
        (a, b), small, 18, HIDDEN_ROW + QUAD, dec_two, grad, dec_feed_w
    )

    names = ("a", "b")
    feed_two = core_hop(net, feed_two, (QUAD, QUAD)).split(names)
    one_grad, memory_grad, cross_small, cross_q = attend_backward(
        (a, b), cross_pair, small, 13, two_grad, cross_kept, dec_one, memory, cross_w, False, None
    )
    send = Round(feed_two, cross_small)
    memory_grad, *cross_q = send.before(memory_grad, *cross_q)
    send.go()
    cross_s = core_hop(net, cross_q, (cut, cut)).split(names)
    mid_grad, enc_feed_small, feed_one = feed_backward(
        (a, b), small, 5, memory_grad, enc_feed_kept, enc_mid, enc_feed_w
    )
    send = Round(feed_two + cross_s, enc_feed_small)
    one_grad, *feed_one = send.before(one_grad, *feed_one)
    send.go()
    feed_one = core_hop(net, feed_one, (QUAD, QUAD)).split(names)
    target_grad, _, self_small, self_q = attend_backward(
        (a, b), target_pair, small, 8, one_grad, self_kept, target, None, self_w, True, None
    )
    send = Round(feed_two + cross_s + feed_one, self_small)
    mid_grad, *self_q = send.before(mid_grad, *self_q)
    send.go()
    self_s = core_hop(net, self_q, (cut, cut)).split(names)
    others = (enc_feed_small, self_small, cross_small, dec_feed_small)
    source_grad, _, _, enc_q = attend_backward(
        (a, b), source_pair, small, 0, mid_grad, enc_kept, source, None, enc_attend_w, False, others
    )
    send = Round(feed_two + cross_s + feed_one + self_s, source_grad)
    enc_q = send.before(*enc_q)
    last = send.go()
    enc_s = core_hop(net, enc_q, (cut, cut + 1)).split(names)
    while enc_s[0].blocks > 1:
        send = Round([item for item in cross_s + feed_one + self_s + enc_s if item.blocks > 1], *last)
        last = send.go()

    targets = [(0, 0), (0, cut), (0, QUAD), (0, QUAD + cut), (1, 0), (2, 0), (1, 1), (2, 1)]
    targets += [(0, 2 * QUAD), (0, 2 * QUAD + cut)]
    segments = [item.segments[0] for item in enc_s + self_s + feed_one + feed_two + cross_s]
    segments = [segment + (target,) for segment, target in zip(segments, targets)]
    updated = last_update(at, segments, masters, firsts, seconds)
    return (memory, result, source_grad, target_grad), updated


def whole_step(pairs, source, target, grad, masters, firsts, seconds, axis_sizes):
    attention, up, down = [master.astype(BF) for master in masters[:3]]
    vectors, hidden = masters[3:]
    source_pair, target_pair, cross_pair = pairs
    small = gather_small(vectors, hidden)
    quads = gather_whole(attention, up, down)
    table = jnp.arange(source.shape[1] // BLOCK, dtype=jnp.int32)
    two = (table, table)
    parts = [(table, list(quad), 0, QUAD) for quad in quads]
    enc_kept = attend_forward(source_pair, small, 0, source, None, parts[:1], False)
    enc_mid = enc_kept[7]
    enc_feed_kept = feed_forward(small, 5, HIDDEN_ROW, enc_mid, parts[1:3])
    memory = enc_feed_kept[0]
    self_kept = attend_forward(target_pair, small, 8, target, None, parts[3:4], True)
    dec_one = self_kept[7]
    cross_kept = attend_forward(cross_pair, small, 13, dec_one, memory, parts[4:5], False)
    dec_two = cross_kept[7]
    result, two_grad, dec_feed_small, feed_two = feed_both(
        two, small, 18, HIDDEN_ROW + QUAD, dec_two, grad, parts[5:7]
    )
    one_grad, memory_grad, cross_small, cross_q = attend_backward(
        two, cross_pair, small, 13, two_grad, cross_kept, dec_one, memory, parts[4:5], False, None
    )
    target_grad, _, self_small, self_q = attend_backward(
        two, target_pair, small, 8, one_grad, self_kept, target, None, parts[3:4], True, None
    )
    mid_grad, enc_feed_small, feed_one = feed_backward(
        two, small, 5, memory_grad, enc_feed_kept, enc_mid, parts[1:3]
    )
    source_grad, _, enc_small, enc_q = attend_backward(
        two, source_pair, small, 0, mid_grad, enc_kept, source, None, parts[:1], False, None
    )
    quads = [enc_q]
    quads += [[half[:, low : low + QUAD] for half in feed_one] for low in (0, QUAD)]
    quads += [self_q, cross_q]
    quads += [[half[:, low : low + QUAD] for half in feed_two] for low in (0, QUAD)]
    smalls = (enc_small, enc_feed_small, self_small, cross_small, dec_feed_small)
    count = axis_sizes[0] * axis_sizes[1]
    shares = scatter_small(smalls, vectors, hidden, lax.axis_index(AXES), count)
    grads = tuple(scatter_whole(quads)) + shares
    updated = [
        adam_update(
            masters[slot], grads[slot], firsts[slot], seconds[slot], RATES[slot], DECAYS[slot]
        )
        for slot in range(5)
    ]
    flat = [updated[slot][kind] for kind in range(4) for slot in range(5)]
    return (memory, result, source_grad, target_grad), flat


def per_device(
    axis_sizes,
    source_tokens,
    target_tokens,
    source_segments,
    target_segments,
    output_grad,
    attention_weight,
    up_weight,
    down_weight,
    vectors,
    hidden_bias,
    *moments,
):
    masters = (attention_weight, up_weight, down_weight, vectors, hidden_bias)
    firsts = moments[:5]
    seconds = moments[5:]
    width = source_tokens.shape[2]
    pairs = (
        (source_segments, source_segments),
        (target_segments, target_segments),
        (target_segments, source_segments),
    )
    direct = axis_sizes[0] * axis_sizes[1] * BLOCK == width
    tokens, updated = (direct_step if direct else whole_step)(
        pairs,
        source_tokens[0],
        target_tokens[0],
        output_grad[0],
        masters,
        firsts,
        seconds,
        axis_sizes,
    )
    return tuple(array[None] for array in tokens) + tuple(updated)


def solution(mesh):
    rows = P(AXES, None, None)
    line = P(AXES, None)
    matrix = P(None, AXES, None)
    vector = P(None, AXES)
    state = (matrix, matrix, matrix, vector, vector)
    return jax.shard_map(
        functools.partial(per_device, (mesh.shape["dp"], mesh.shape["fsdp"])),
        mesh=mesh,
        in_specs=(rows, rows, line, line, rows) + state * 3,
        out_specs=(rows,) * 4 + state * 4,
        check_vma=False,
    )
```

```python
import functools

import jax
import jax.numpy as jnp
from jax import lax
from jax.experimental import pallas as pl
from jax.experimental.pallas import tpu as pltpu
from jax.sharding import PartitionSpec as P

HEADS = 8
STEP = 10
EPS_NORM = 1e-05
EPS_ADAM = 1e-08
BETA_ONE = 0.9
BETA_TWO = 0.999
LOWEST = -1e30
RATES = (0.05, 0.05, 0.05, 0.3, 0.3)
DECAYS = (0.01, 0.01, 0.01, 0.0, 0.0)
AXES = ("dp", "fsdp")
QUAD = 4
BLOCK = 16
CHUNK = 64
LANES = 128
SMALL_ROWS = 32
VMEM_BYTES = 60 * 1024 * 1024
HIDDEN_ROW = 24
BF = jnp.bfloat16
F32 = jnp.float32
VMEM = pl.BlockSpec(memory_space=pltpu.VMEM)
SMEM = pl.BlockSpec(memory_space=pltpu.SMEM)
ANY = pl.BlockSpec(memory_space=pl.ANY)
ROOT_TWO_PI = 0.7978845608028654
CUBIC = 0.044715


def dot(left, right):
    return jnp.dot(left, right, preferred_element_type=F32)


def dot_nt(left, right):
    return lax.dot_general(left, right, (((1,), (1,)), ((), ())), preferred_element_type=F32)


class Input:
    def __init__(self, array, room, sem):
        self.room = room
        self.shape = room.shape
        self.copy = pltpu.make_async_copy(array, room, sem)
        self.copy.start()
        self.there = False

    def __getitem__(self, where):
        if not self.there:
            self.copy.wait()
            self.there = True
        return self.room[where]


class Output:
    def __init__(self, array, room, sem):
        self.array = array
        self.room = room
        self.shape = room.shape
        self.sem = sem
        self.left = False

    def __getitem__(self, where):
        return self.room[where]

    def __setitem__(self, where, value):
        self.room[where] = value

    def put(self, index=None):
        source = self.room if index is None else self.room.at[index]
        target = self.array if index is None else self.array.at[index]
        pltpu.make_async_copy(source, target, self.sem).start()
        self.left = True

    def finish(self):
        if not self.left:
            self.put()
        pltpu.make_async_copy(self.room, self.array, self.sem).wait()


def staged_kernel(kernel, scalars, inputs, others, outputs, targets, *refs):
    refs = list(refs)
    sems = refs.pop()
    count = inputs + outputs
    rooms = refs[len(refs) - count :]
    refs = refs[: len(refs) - count]
    at = scalars
    for slot in range(inputs):
        refs[at + slot] = Input(refs[at + slot], rooms[slot], sems.at[slot])
    at += inputs + others
    made = []
    for slot in range(inputs, count):
        place = at + slot - inputs
        refs[place] = Output(refs[place], rooms[slot], sems.at[slot])
        made.append(refs[place])
    kernel(*refs)
    for output in made:
        output.finish()


def load_start(part, place, sems):
    table, arrays, low, number = part
    at = 0
    for slot, array in enumerate(arrays):
        for index in range(array.shape[0]):
            source = array.at[index, low : low + number]
            pltpu.make_async_copy(source, place(table[at]), sems.at[slot]).start()
            at += 1


def load_wait(part, sems):
    table, arrays, low, number = part
    for slot, array in enumerate(arrays):
        whole = array.at[:, low : low + number]
        pltpu.make_async_copy(whole, whole, sems.at[slot]).wait()


def store_start(part, place, sems):
    table, arrays, low, number = part
    half = arrays[0].shape[0]
    for index in range(half):
        for slot in (1, 0):
            target = arrays[slot].at[index, low : low + number]
            source = place(table[slot * half + index])
            pltpu.make_async_copy(source, target, sems.at[slot]).start()


def row_place(scratch, low, high):
    def place(block):
        start = pl.multiple_of(block * BLOCK, BLOCK)
        return scratch.at[low:high, pl.ds(start, BLOCK), :]

    return place


def block_place(scratch):
    return lambda block: scratch.at[block]


def column_sum(values):
    rows, width = values.shape
    return jnp.sum(values.reshape(rows // 8, 8, width), axis=0)


def total_of(sums):
    return jnp.sum(functools.reduce(jnp.add, sums), axis=0, keepdims=True)


def norm_forward(pre_of, length, gain, shift, out_ref, hat_ref, rstd_ref):
    for at in range(0, length, CHUNK):
        rows = slice(at, at + CHUNK)
        pre = pre_of(rows)
        mean = jnp.mean(pre, axis=-1, keepdims=True)
        centred = pre - mean
        spread = jnp.mean(centred * centred, axis=-1, keepdims=True)
        rstd = lax.rsqrt(spread + EPS_NORM)
        hat = centred * rstd
        hat_ref[rows] = hat
        rstd_ref[rows] = jnp.broadcast_to(rstd, (CHUNK, LANES))
        out_ref[rows] = hat * gain + shift
    for ref in (hat_ref, rstd_ref, out_ref):
        if isinstance(ref, Output):
            ref.put()


def norm_backward(grad_ref, hat_ref, rstd_ref, gain, pre_out, low_out):
    length = grad_ref.shape[0]
    sums = ([], [], [])
    for at in range(0, length, CHUNK):
        rows = slice(at, at + CHUNK)
        grad = grad_ref[rows].astype(F32)
        hat = hat_ref[rows]
        sums[0].append(column_sum(grad * hat))
        sums[1].append(column_sum(grad))
        scaled = grad * gain
        one = jnp.mean(scaled, axis=-1, keepdims=True)
        two = jnp.mean(scaled * hat, axis=-1, keepdims=True)
        pre = rstd_ref[rows][:, :1] * (scaled - one - hat * two)
        low = pre.astype(BF)
        pre_out[rows] = pre
        low_out[rows] = low
        sums[2].append(column_sum(low.astype(F32)))
    return [total_of(each) for each in sums]


def lane_mask(rows):
    return lax.broadcasted_iota(jnp.int32, (rows, LANES), 1) < LANES // 2


def stacked_pair(block):
    first = lane_mask(block.shape[0])
    zero = jnp.zeros_like(block)
    return jnp.concatenate([jnp.where(first, block, zero), jnp.where(first, zero, block)], axis=0)


def merged_pair(stacked):
    rows = stacked.shape[0] // 2
    return jnp.where(lane_mask(rows), stacked[:rows], stacked[rows:])


def mask_fill(bias_ref, column_seg, row_seg, causal, transposed):
    length = bias_ref.shape[0]
    column = jnp.broadcast_to(column_seg, (LANES, length)).T
    for at in range(0, length, LANES):
        same = column == row_seg[:, at : at + LANES]
        if causal:
            down = lax.broadcasted_iota(jnp.int32, (length, LANES), 0)
            along = lax.broadcasted_iota(jnp.int32, (length, LANES), 1) + at
            order = (down <= along) if transposed else (along <= down)
            same = same & order
        bias_ref[:, at : at + LANES] = jnp.where(same, 0.0, LOWEST)


def take_parts(refs, layout, tables):
    parts = []
    for slot, (arrays, low, number) in enumerate(layout):
        parts.append((tables[slot], [refs.pop(0) for _ in range(arrays)], low, number))
    return parts


def small_part(part):
    table, arrays, low, number = part
    return table, arrays, low + number, 1


def small_join(blocks_ref):
    count = blocks_ref.shape[0]
    groups = blocks_ref.shape[3] // LANES
    per = count // groups
    vectors = []
    hidden = [[], []]
    for group in range(groups):
        total = blocks_ref[group * per, 0, :8].astype(F32)
        for at in range(group * per + 1, (group + 1) * per):
            total = total + blocks_ref[at, 0, :8].astype(F32)
        columns = [total[:, at : at + LANES] for at in range(0, 4 * LANES, LANES)]
        vectors.append(jnp.concatenate(columns[:3], axis=0))
        for layer in range(2):
            rows = [columns[3][4 * layer + at : 4 * layer + at + 1] for at in range(4)]
            hidden[layer].append(jnp.concatenate(rows, axis=1))
    return jnp.concatenate([jnp.concatenate(vectors, axis=1)] + hidden[0] + hidden[1], axis=0)


def small_split(whole, group):
    lanes = slice(group * LANES, (group + 1) * LANES)
    columns = [whole[at : at + 8, lanes] for at in (0, 8, 16)]
    rows = []
    for layer in range(2):
        row = whole[24 + 4 * layer + group : 25 + 4 * layer + group]
        rows += [row[:, at : at + LANES] for at in range(0, 4 * LANES, LANES)]
    columns.append(jnp.concatenate(rows, axis=0))
    block = jnp.concatenate(columns, axis=1)
    return jnp.concatenate([block, jnp.zeros_like(block)], axis=0).astype(BF)


def attend_forward_kernel(layout, cross, causal, base, joins, *refs):
    refs = list(refs)
    tables = [refs.pop(0) for _ in layout]
    query_seg = refs.pop(0)
    key_seg = refs.pop(0)
    small = None if joins else refs.pop(0)
    rows_ref = refs.pop(0)
    memory_ref = refs.pop(0) if cross else None
    parts = take_parts(refs, layout, tables)
    q_ref, k_ref, v_ref, o_ref, lse_ref, hat_ref, rstd_ref, out_ref = [refs.pop(0) for _ in range(8)]
    if joins:
        small = refs.pop(0)
        blocks_ref = refs.pop()
        extra = small_part(parts[-1])
    w_ref, bias_ref, scores_ref, exponent_ref, largest_ref, mixed_ref, attended_ref, sems = refs
    first = 0
    if joins:
        load_start(extra, lambda block: blocks_ref.at[block], sems.at[len(parts)])
    for slot, part in enumerate(parts):
        load_start(part, row_place(w_ref, first, first + part[3]), sems.at[slot])
        first += part[3]
    length, width = rows_ref.shape
    mask_fill(bias_ref, query_seg[...], key_seg[...], causal, False)
    rows = rows_ref[...].astype(BF)
    keys = memory_ref[...].astype(BF) if cross else rows
    if joins:
        load_wait(extra, sems.at[len(parts)])
        small[...] = small_join(blocks_ref)
        small.put()
    for slot, part in enumerate(parts):
        load_wait(part, sems.at[slot])
    scale = (width // HEADS) ** (-0.5)
    q_ref[...] = (dot(rows, w_ref[0]) + small[base : base + 1]).astype(BF) * jnp.asarray(scale, BF)
    k_ref[...] = dot(keys, w_ref[1]).astype(BF)
    v_ref[...] = (dot(keys, w_ref[2]) + small[base + 1 : base + 2]).astype(BF)
    for ref in (q_ref, k_ref, v_ref):
        ref.put()
    lane = lax.broadcasted_iota(jnp.int32, (LANES, LANES), 1)
    logs = [jnp.zeros((LANES, LANES), F32)] * (length // LANES)
    for pair in range(HEADS // 2):
        lanes = slice(pair * LANES, (pair + 1) * LANES)
        side = pair % 2
        scores_ref[side] = dot_nt(stacked_pair(q_ref[:, lanes]), k_ref[:, lanes])
        for at in range(0, 2 * length, CHUNK):
            chunk = slice(at, at + CHUNK)
            own = slice(at % length, at % length + CHUNK)
            reach = own.start // LANES * LANES + LANES if causal else length
            scores = scores_ref[side, chunk, :reach] + bias_ref[own, :reach]
            largest = jnp.max(scores, axis=-1, keepdims=True)
            exponent_ref[side, chunk, :reach] = jnp.exp(scores - largest).astype(BF)
            if reach < length:
                exponent_ref[side, chunk, reach:] = jnp.zeros((CHUNK, length - reach), BF)
            largest_ref[side, chunk] = jnp.broadcast_to(largest, (CHUNK, LANES))
        values = jnp.concatenate([v_ref[:, lanes], jnp.ones((length, LANES), BF)], axis=1)
        mixed_ref[side] = dot(exponent_ref[side], values)
        for slot, at in enumerate(range(0, length, LANES)):
            outs = []
            for half in range(2):
                chunk = slice(half * length + at, half * length + at + LANES)
                total = mixed_ref[side, chunk, LANES:]
                outs.append(mixed_ref[side, chunk, :LANES] / total)
                log_total = largest_ref[side, chunk] + jnp.log(total)
                logs[slot] = jnp.where(lane == 2 * pair + half, log_total, logs[slot])
            o_ref[at : at + LANES, lanes] = jnp.where(lane_mask(LANES), outs[0], outs[1]).astype(BF)
    for slot, at in enumerate(range(0, length, LANES)):
        lse_ref[:, at : at + LANES] = logs[slot].T[:HEADS]
    o_ref.put()
    lse_ref.put()
    attended_ref[...] = dot(o_ref[...], w_ref[3])
    out_bias = small[base + 2 : base + 3]
    norm_forward(
        lambda rows: rows_ref[rows].astype(F32) + (attended_ref[rows] + out_bias),
        length,
        small[base + 3 : base + 4],
        small[base + 4 : base + 5],
        out_ref,
        hat_ref,
        rstd_ref,
    )


def attend_backward_kernel(layout, cross, causal, base, splits, *refs):
    refs = list(refs)
    tables = [refs.pop(0) for _ in layout]
    out_tables = [refs.pop(0), refs.pop(0)]
    query_seg = refs.pop(0)
    key_seg = refs.pop(0)
    small = refs.pop(0)
    grad_ref = refs.pop(0)
    hat_ref, rstd_ref = refs.pop(0), refs.pop(0)
    rows_ref = refs.pop(0)
    memory_ref = refs.pop(0) if cross else None
    q_ref, k_ref, v_ref, o_ref, lse_ref = [refs.pop(0) for _ in range(5)]
    others = [refs.pop(0) for _ in range(4)] if splits else None
    parts = take_parts(refs, layout, tables)
    rows_out = refs.pop(0)
    memory_out = refs.pop(0) if cross else None
    small_out = None if splits else refs.pop(0)
    targets = [refs.pop(0), refs.pop(0)]
    outs = []
    for slot, table in enumerate(out_tables):
        outs.append((table, targets, slot * QUAD // 2, QUAD // 2))
    blocks_ref = refs.pop() if splits else None
    w_ref, dw_ref, bias_ref, dout_ref, dq_t_ref, dk_ref, dv_ref, kt_ref = refs[:8]
    low_ref, scores_ref, prob_grad_ref, prob_ref, score_grad_ref, sems = refs[8:]
    first = 0
    for slot, part in enumerate(parts):
        load_start(part, row_place(w_ref, first, first + part[3]), sems.at[slot])
        first += part[3]
    length, width = rows_ref.shape
    head = width // HEADS
    scale = head ** (-0.5)
    gain_grad, shift_grad, out_bias = norm_backward(
        grad_ref, hat_ref, rstd_ref, small[base + 3 : base + 4], rows_out, low_ref
    )
    mask_fill(bias_ref, key_seg[...], query_seg[...], causal, True)
    low = low_ref[...]
    for slot, part in enumerate(parts):
        load_wait(part, sems.at[slot])
    dout_ref[...] = dot_nt(low, w_ref[3]).astype(BF)
    dw_ref[3] = dot(o_ref[...].T, low).astype(BF)
    product = dout_ref[...].astype(F32) * o_ref[...].astype(F32)
    high = product.astype(BF)
    rest = (product - high.astype(F32)).astype(BF)
    picker = lax.broadcasted_iota(jnp.int32, (BLOCK, width), 1) // head
    picker = (picker == lax.broadcasted_iota(jnp.int32, (BLOCK, width), 0)).astype(BF)
    row_dots = dot_nt(picker, high) + dot_nt(picker, rest)
    kt_ref[...] = k_ref[...].T
    for pair in range(HEADS // 2):
        lanes = slice(pair * LANES, (pair + 1) * LANES)
        side = pair % 2
        query = q_ref[:, lanes]
        dout = dout_ref[:, lanes]
        scores_ref[side] = dot_nt(stacked_pair(k_ref[:, lanes]), query)
        prob_grad_ref[side] = dot_nt(stacked_pair(v_ref[:, lanes]), dout)
        for at in range(0, 2 * length, CHUNK):
            which = 2 * pair + at // length
            chunk = slice(at, at + CHUNK)
            own = slice(at % length, at % length + CHUNK)
            begin = own.start // LANES * LANES if causal else 0
            shift = bias_ref[own, begin:] - lse_ref[which : which + 1, begin:]
            prob = jnp.exp(scores_ref[side, chunk, begin:] + shift)
            prob_ref[side, chunk, begin:] = prob.astype(BF)
            centred = prob_grad_ref[side, chunk, begin:] - row_dots[which : which + 1, begin:]
            score_grad_ref[side, chunk, begin:] = (prob * centred).astype(BF)
            if begin:
                prob_ref[side, chunk, :begin] = jnp.zeros((CHUNK, begin), BF)
                score_grad_ref[side, chunk, :begin] = jnp.zeros((CHUNK, begin), BF)
        dv_ref[:, lanes] = merged_pair(dot(prob_ref[side], dout)).astype(BF)
        dk_ref[:, lanes] = merged_pair(dot(score_grad_ref[side], query)).astype(BF)
        for half in range(2):
            at = pair * LANES + half * head
            own = slice(half * length, (half + 1) * length)
            dq_t_ref[at : at + head, :] = dot(kt_ref[at : at + head, :], score_grad_ref[side, own])
    query_grad = (dq_t_ref[...] * scale).T.astype(BF)
    key_grad = dk_ref[...]
    value_grad = dv_ref[...]
    turned = rows_ref[...].astype(BF).T
    other = memory_ref[...].astype(BF).T if cross else turned
    dw_ref[2] = dot(other, value_grad).astype(BF)
    store_start(outs[1], row_place(dw_ref, QUAD // 2, QUAD), sems.at[1])
    dw_ref[0] = dot(turned, query_grad).astype(BF)
    dw_ref[1] = dot(other, key_grad).astype(BF)
    store_start(outs[0], row_place(dw_ref, 0, QUAD // 2), sems.at[0])
    rows_back = rows_out[...] + dot_nt(query_grad, w_ref[0])
    memory_back = dot_nt(key_grad, w_ref[1]) + dot_nt(value_grad, w_ref[2])
    if cross:
        rows_out[...] = rows_back
        memory_out[...] = memory_back
        memory_out.put()
    else:
        rows_out[...] = rows_back + memory_back
    rows_out.put()
    query_bias = total_of([column_sum(query_grad.astype(F32))])
    value_bias = total_of([column_sum(value_grad.astype(F32))])
    spare = jnp.zeros((3, width), F32)
    own = jnp.concatenate(
        [query_bias, value_bias, out_bias, gain_grad, shift_grad, spare], axis=0
    )
    if splits:
        enc_feed, self_attend, cross_attend, dec_feed = [other[...] for other in others]
        whole = small_rows(own, enc_feed, self_attend, cross_attend, dec_feed)
        groups = blocks_ref.shape[0]
        for group in range(groups):
            blocks_ref[group, 0] = small_split(whole, group)
        extra = small_part(outs[-1])
        per = 2 * extra[1][0].shape[0] // groups
        store_start(extra, lambda block: blocks_ref.at[block // per], sems.at[2])
        load_wait(extra, sems.at[2])
    else:
        small_out[...] = own
    for slot, part in enumerate(outs):
        load_wait(part, sems.at[slot])


def small_rows(enc_attend, enc_feed, self_attend, cross_attend, dec_feed):
    return jnp.concatenate(
        [
            enc_attend[:5],
            enc_feed[:3],
            self_attend[:5],
            cross_attend[:5],
            dec_feed[:3],
            dec_feed[7:],
            dec_feed[7:],
            dec_feed[7:],
            enc_feed[3:7],
            dec_feed[3:7],
        ],
        axis=0,
    )


def gelu_parts(pre):
    square = pre * pre
    curve = jnp.tanh(ROOT_TWO_PI * pre * (1.0 + CUBIC * square))
    half = 0.5 * pre
    rise = 0.5 + 0.5 * curve
    bend = ROOT_TWO_PI * (1.0 + 3.0 * CUBIC * square)
    return pre * rise, rise + half * (1.0 - curve * curve) * bend


def chunk_of(ref, index):
    number = ref.shape[0] // QUAD
    part = ref[index * number : (index + 1) * number]
    return part.reshape(number * ref.shape[1] * ref.shape[2], ref.shape[3])


def feed_forward_steps(small, base, hidden_at, rows_ref, up_ref, down_ref, active_ref, slope_ref, pre_ref, sum_ref):
    rows = rows_ref[...].astype(BF)
    length = rows.shape[0]
    for index in range(QUAD):
        at = hidden_at + index
        side = index % 2
        pre_ref[side] = dot(rows, up_ref[index])
        bias = small[at : at + 1]
        for at in range(0, length, CHUNK // 2):
            chunk = slice(at, at + CHUNK // 2)
            active, slope = gelu_parts(pre_ref[side, chunk] + bias)
            active_ref[index, chunk] = active.astype(BF)
            slope_ref[index, chunk] = slope
        for ref in (active_ref, slope_ref):
            if isinstance(ref, Output):
                ref.put(index)
    wide = jnp.concatenate([active_ref[index] for index in range(QUAD)], axis=1)
    number, _, _, width = down_ref.shape
    sum_ref[...] = dot(wide, down_ref[...].reshape(QUAD * width, width))
    out_bias = small[base : base + 1]
    return lambda rows: rows_ref[rows] + (sum_ref[rows] + out_bias)


def feed_backward_steps(
    pre_grad, low_ref, rows_ref, up_ref, down_ref, active_ref, slope_ref, dup_ref, ddown_ref, rows_out, back_ref, outs, sems
):
    low = low_ref[...]
    length = low.shape[0]
    number = ddown_ref.shape[0] // QUAD
    for index in range(QUAD):
        down_grad = dot(active_ref[index].T, low).astype(BF)
        ddown_ref[index * number : (index + 1) * number] = down_grad.reshape(
            (number,) + ddown_ref.shape[1:]
        )
    store_start(outs[1], block_place(ddown_ref), sems.at[1])
    turned = rows_ref[...].astype(BF).T
    hidden_grads = []
    hiddens = []
    for index in range(QUAD):
        side = index % 2
        back_ref[side] = dot_nt(low, chunk_of(down_ref, index))
        sums = []
        parts = []
        for at in range(0, length, CHUNK):
            chunk = slice(at, at + CHUNK)
            hidden = (back_ref[side, chunk] * slope_ref[index, chunk]).astype(BF)
            sums.append(column_sum(hidden.astype(F32)))
            parts.append(hidden)
        hidden = jnp.concatenate(parts, axis=0)
        hidden_grads.append(total_of(sums))
        dup_ref[index] = dot(turned, hidden).astype(BF)
        hiddens.append(hidden)
    store_start(outs[0], row_place(dup_ref, 0, QUAD), sems.at[0])
    total = pre_grad[...]
    for index in range(QUAD):
        total = total + dot_nt(hiddens[index], up_ref[index])
    rows_out[...] = total
    rows_out.put()
    return hidden_grads


def load_feed(parts, up_ref, down_ref, sems):
    load_start(parts[0], row_place(up_ref, 0, QUAD), sems.at[0])
    load_start(parts[1], block_place(down_ref), sems.at[1])


def wait_feed(parts, sems):
    for slot, part in enumerate(parts):
        load_wait(part, sems.at[slot])


def feed_outs(refs, tables):
    arrays = [refs.pop(0), refs.pop(0)]
    return [(tables[slot], arrays, slot * QUAD, QUAD) for slot in range(2)]


def feed_small(out_bias, gain_grad, shift_grad, hidden_grads):
    spare = jnp.zeros_like(out_bias)
    return jnp.concatenate([out_bias, gain_grad, shift_grad] + hidden_grads + [spare], axis=0)


def feed_forward_kernel(layout, base, hidden_at, *refs):
    refs = list(refs)
    tables = [refs.pop(0), refs.pop(0)]
    small, rows_ref = refs.pop(0), refs.pop(0)
    parts = take_parts(refs, layout, tables)
    out_ref, hat_ref, rstd_ref, active_ref, slope_ref, up_ref, down_ref = refs[:7]
    pre_ref, sum_ref, sems = refs[7:]
    load_feed(parts, up_ref, down_ref, sems)
    wait_feed(parts, sems)
    pre_of = feed_forward_steps(
        small, base, hidden_at, rows_ref, up_ref, down_ref, active_ref, slope_ref, pre_ref, sum_ref
    )
    gain, shift = small[base + 1 : base + 2], small[base + 2 : base + 3]
    norm_forward(pre_of, rows_ref.shape[0], gain, shift, out_ref, hat_ref, rstd_ref)


def feed_backward_kernel(layout, base, *refs):
    refs = list(refs)
    tables = [refs.pop(0), refs.pop(0)]
    out_tables = [refs.pop(0), refs.pop(0)]
    small, grad_ref, hat_ref, rstd_ref, rows_ref = [refs.pop(0) for _ in range(5)]
    active_ref, slope_ref = refs.pop(0), refs.pop(0)
    parts = take_parts(refs, layout, tables)
    rows_out, small_out = refs.pop(0), refs.pop(0)
    outs = feed_outs(refs, out_tables)
    up_ref, down_ref, dup_ref, ddown_ref, low_ref, back_ref, sems, out_sems = refs
    load_feed(parts, up_ref, down_ref, sems)
    gain_grad, shift_grad, out_bias = norm_backward(
        grad_ref, hat_ref, rstd_ref, small[base + 1 : base + 2], rows_out, low_ref
    )
    wait_feed(parts, sems)
    hidden_grads = feed_backward_steps(
        rows_out,
        low_ref,
        rows_ref,
        up_ref,
        down_ref,
        active_ref,
        slope_ref,
        dup_ref,
        ddown_ref,
        rows_out,
        back_ref,
        outs,
        out_sems,
    )
    small_out[...] = feed_small(out_bias, gain_grad, shift_grad, hidden_grads)
    wait_feed(outs, out_sems)


def feed_both_kernel(layout, base, hidden_at, *refs):
    refs = list(refs)
    tables = [refs.pop(0), refs.pop(0)]
    out_tables = [refs.pop(0), refs.pop(0)]
    small, rows_ref, grad_ref = [refs.pop(0) for _ in range(3)]
    parts = take_parts(refs, layout, tables)
    out_ref, rows_out, small_out = [refs.pop(0) for _ in range(3)]
    outs = feed_outs(refs, out_tables)
    up_ref, down_ref, dup_ref, ddown_ref, low_ref, back_ref, sum_ref = refs[:7]
    active_ref, slope_ref, hat_ref, rstd_ref, sems, out_sems = refs[7:]
    load_feed(parts, up_ref, down_ref, sems)
    wait_feed(parts, sems)
    pre_of = feed_forward_steps(
        small, base, hidden_at, rows_ref, up_ref, down_ref, active_ref, slope_ref, back_ref, sum_ref
    )
    gain, shift = small[base + 1 : base + 2], small[base + 2 : base + 3]
    norm_forward(pre_of, rows_ref.shape[0], gain, shift, out_ref, hat_ref, rstd_ref)
    gain_grad, shift_grad, out_bias = norm_backward(
        grad_ref, hat_ref, rstd_ref, gain, rows_out, low_ref
    )
    hidden_grads = feed_backward_steps(
        rows_out,
        low_ref,
        rows_ref,
        up_ref,
        down_ref,
        active_ref,
        slope_ref,
        dup_ref,
        ddown_ref,
        rows_out,
        back_ref,
        outs,
        out_sems,
    )
    small_out[...] = feed_small(out_bias, gain_grad, shift_grad, hidden_grads)
    wait_feed(outs, out_sems)


def shaped(shape, dtype=F32):
    return jax.ShapeDtypeStruct(shape, dtype)


def call(
    kernel, scalars, inputs, others, outs, targets, scratch, flops, moved, limit=VMEM_BYTES
):
    rooms = [pltpu.VMEM(array.shape, array.dtype) for array in list(inputs) + list(outs)]
    return pl.pallas_call(
        functools.partial(
            staged_kernel, kernel, len(scalars), len(inputs), len(others), len(outs), len(targets)
        ),
        out_shape=list(outs) + list(targets),
        in_specs=[SMEM] * len(scalars) + [ANY] * (len(inputs) + len(others)),
        out_specs=[ANY] * (len(outs) + len(targets)),
        scratch_shapes=scratch + rooms + [pltpu.SemaphoreType.DMA((len(rooms),))],
        cost_estimate=pl.CostEstimate(flops=flops, bytes_accessed=moved, transcendentals=0),
        compiler_params=pltpu.CompilerParams(vmem_limit_bytes=limit),
    )(*scalars, *inputs, *others)


def layout_of(parts):
    return [(len(arrays), low, number) for _, arrays, low, number in parts]


def arrays_of(parts):
    return [array for part in parts for array in part[1]]


def most(parts):
    return max(len(part[1]) for part in parts)


def halves(width, number):
    return [shaped((width // BLOCK // 2, number, BLOCK, width), BF)] * 2


def attend_forward(segments, small, base, rows, memory, parts, causal):
    length, width = rows.shape
    cross = memory is not None
    joins = small is None
    scalars = [part[0] for part in parts]
    inputs = list(segments) + ([] if joins else [small]) + [rows] + ([memory] if cross else [])
    outs = [shaped((length, width), BF)] * 4 + [shaped((HEADS, length))]
    outs += [shaped((length, width)), shaped((length, LANES)), shaped((length, width))]
    outs += [shaped((SMALL_ROWS, width))] if joins else []
    scratch = [
        pltpu.VMEM((QUAD, width, width), BF),
        pltpu.VMEM((length, length), F32),
        pltpu.VMEM((2, 2 * length, length), F32),
        pltpu.VMEM((2, 2 * length, length), BF),
        pltpu.VMEM((2, 2 * length, LANES), F32),
        pltpu.VMEM((2, 2 * length, 2 * LANES), F32),
        pltpu.VMEM((length, width), F32),
        pltpu.SemaphoreType.DMA((len(parts) + 1, most(parts))),
    ]
    scratch += [pltpu.VMEM((width // BLOCK, 1, BLOCK, width), BF)] if joins else []
    kernel = functools.partial(attend_forward_kernel, layout_of(parts), cross, causal, base, joins)
    flops = 8 * length * width * width + 16 * length * length * width
    return call(kernel, scalars, inputs, arrays_of(parts), outs, [], scratch, flops, 8_000_000)


def attend_backward(
    out_tables, segments, small, base, grad, kept, rows, memory, parts, causal, others
):
    length, width = rows.shape
    cross = memory is not None
    splits = others is not None
    q, k, v, o, lse, hat, rstd = kept[:7]
    scalars = [part[0] for part in parts] + list(out_tables)
    inputs = list(segments) + [small, grad, hat, rstd, rows]
    inputs += ([memory] if cross else []) + [q, k, v, o, lse] + list(others or ())
    outs = [shaped((length, width))] * (2 if cross else 1)
    outs += [] if splits else [shaped((8, width))]
    targets = halves(width, QUAD + (1 if splits else 0))
    scratch = [
        pltpu.VMEM((QUAD, width, width), BF),
        pltpu.VMEM((QUAD, width, width), BF),
        pltpu.VMEM((length, length), F32),
        pltpu.VMEM((length, width), BF),
        pltpu.VMEM((width, length), F32),
        pltpu.VMEM((length, width), BF),
        pltpu.VMEM((length, width), BF),
        pltpu.VMEM((width, length), BF),
        pltpu.VMEM((length, width), BF),
        pltpu.VMEM((2, 2 * length, length), F32),
        pltpu.VMEM((2, 2 * length, length), F32),
        pltpu.VMEM((2, 2 * length, length), BF),
        pltpu.VMEM((2, 2 * length, length), BF),
        pltpu.SemaphoreType.DMA((3, 2)),
    ]
    scratch += [pltpu.VMEM((width // LANES, 1, BLOCK, width), BF)] if splits else []
    kernel = functools.partial(
        attend_backward_kernel, layout_of(parts), cross, causal, base, splits
    )
    flops = 16 * length * width * width + 40 * length * length * width
    arrays = arrays_of(parts)
    results = list(call(kernel, scalars, inputs, arrays, outs, targets, scratch, flops, 12_000_000))
    rows_grad = results.pop(0)
    memory_grad = results.pop(0) if cross else None
    small_grad = None if splits else results.pop(0)
    return rows_grad, memory_grad, small_grad, results


def feed_scratch(width, grads):
    number = width // BLOCK
    once = [pltpu.VMEM((QUAD, width, width), BF), pltpu.VMEM((number, QUAD, BLOCK, width), BF)]
    return once * (2 if grads else 1)


def feed_forward(small, base, hidden_at, rows, parts):
    length, width = rows.shape
    scalars = [part[0] for part in parts]
    outs = [shaped((length, width)), shaped((length, width)), shaped((length, LANES))]
    outs += [shaped((QUAD, length, width), BF), shaped((QUAD, length, width))]
    scratch = feed_scratch(width, False)
    scratch += [pltpu.VMEM((2, length, width), F32), pltpu.VMEM((length, width), F32)]
    scratch += [pltpu.SemaphoreType.DMA((2, most(parts)))]
    kernel = functools.partial(feed_forward_kernel, layout_of(parts), base, hidden_at)
    flops = 16 * length * width * width
    arrays = arrays_of(parts)
    return call(kernel, scalars, [small, rows], arrays, outs, [], scratch, flops, 10_000_000)


def feed_backward(out_tables, small, base, grad, kept, rows, parts):
    length, width = rows.shape
    hat, rstd, active, slope = kept[1:]
    scalars = [part[0] for part in parts] + list(out_tables)
    inputs = [small, grad, hat, rstd, rows, active, slope]
    outs = [shaped((length, width)), shaped((8, width))]
    targets = halves(width, 2 * QUAD)
    scratch = feed_scratch(width, True)
    scratch += [pltpu.VMEM((length, width), BF), pltpu.VMEM((2, length, width), F32)]
    scratch += [pltpu.SemaphoreType.DMA((2, most(parts))), pltpu.SemaphoreType.DMA((2, 2))]
    kernel = functools.partial(feed_backward_kernel, layout_of(parts), base)
    flops = 32 * length * width * width
    arrays = arrays_of(parts)
    results = call(kernel, scalars, inputs, arrays, outs, targets, scratch, flops, 14_000_000)
    return results[0], results[1], results[2:4]


def feed_both(out_tables, small, base, hidden_at, rows, grad, parts):
    length, width = rows.shape
    scalars = [part[0] for part in parts] + list(out_tables)
    outs = [shaped((length, width)), shaped((length, width)), shaped((8, width))]
    targets = halves(width, 2 * QUAD)
    scratch = feed_scratch(width, True) + [
        pltpu.VMEM((length, width), BF),
        pltpu.VMEM((2, length, width), F32),
        pltpu.VMEM((length, width), F32),
        pltpu.VMEM((QUAD, length, width), BF),
        pltpu.VMEM((QUAD, length, width), F32),
        pltpu.VMEM((length, width), F32),
        pltpu.VMEM((length, LANES), F32),
        pltpu.SemaphoreType.DMA((2, most(parts))),
        pltpu.SemaphoreType.DMA((2, 2)),
    ]
    kernel = functools.partial(feed_both_kernel, layout_of(parts), base, hidden_at)
    flops = 48 * length * width * width
    arrays = arrays_of(parts)
    results = call(kernel, scalars, [small, rows, grad], arrays, outs, targets, scratch, flops, 12_000_000)
    return results[0], results[1], results[2], results[3:5]


def first_kernel(
    at_ref,
    vector_ref,
    hidden_ref,
    square_ref,
    tall_ref,
    deep_ref,
    one_ref,
    two_ref,
    three_ref,
    turn_ref,
    line_ref,
):
    at = at_ref[0]
    width = square_ref.shape[2]
    turn_ref[...] = jnp.zeros_like(turn_ref)
    lanes, rows = vector_ref.shape
    turn_ref[pl.ds(pl.multiple_of(at * lanes, lanes), lanes), :rows] = vector_ref[...]
    upright = turn_ref[...].T
    line_ref[...] = jnp.zeros_like(line_ref)
    layers, lanes = hidden_ref.shape
    per = LANES // lanes
    for layer in range(layers):
        row = jnp.concatenate([hidden_ref[layer : layer + 1]] * per, axis=1)
        lane = lax.broadcasted_iota(jnp.int32, row.shape, 1) // lanes
        row = jnp.where(lane == at % per, row, 0.0)
        line_ref[pl.ds(4 * layer + at // per, 1), :] = row
    columns = [upright[low : low + 8] for low in (0, 8, 16)] + [line_ref[...]]
    block = jnp.concatenate(columns, axis=1)
    small = jnp.concatenate([block, jnp.zeros_like(block)], axis=0)
    tall = []
    deep = []
    for layer in range(2):
        for index in range(QUAD):
            lanes = slice(index * width, (index + 1) * width)
            tall.append(tall_ref[layer, :, lanes])
            deep.append(deep_ref[layer, index * BLOCK : (index + 1) * BLOCK])
    square = [square_ref[index] for index in range(3 * QUAD)]
    cut = QUAD // 2
    groups = [
        square[:cut] + tall[:QUAD] + square[cut:QUAD] + [small] + deep[:QUAD],
        square[QUAD:],
        tall[QUAD:] + deep[QUAD:],
    ]
    for out_ref, group in zip((one_ref, two_ref, three_ref), groups):
        for slot, block in enumerate(group):
            out_ref[0, slot] = block.astype(BF)
        out_ref.put()


def first_arrays(at, square, tall, deep, vectors, hidden):
    width = square.shape[2]
    outs = [
        shaped((1, 3 * QUAD + 1, BLOCK, width), BF),
        shaped((1, 2 * QUAD, BLOCK, width), BF),
        shaped((1, 2 * QUAD, BLOCK, width), BF),
    ]
    scratch = [pltpu.VMEM((LANES, LANES), F32), pltpu.VMEM((8, LANES), F32)]
    inputs = [vectors.T, hidden, square, tall, deep]
    return call(first_kernel, [at], inputs, [], outs, [], scratch, 0, 4_000_000)


def last_kernel(plan, count, at_ref, *refs):
    masters, firsts, seconds = refs[:5], refs[5:10], refs[10:15]
    arrays, refs = refs[15 : 15 + count], refs[15 + count :]
    outs, refs = [refs[5 * kind : 5 * kind + 5] for kind in range(4)], refs[20:]
    buffers, turn_ref, line_ref, sems = refs
    at = at_ref[0]
    starts = []
    for width, pieces, _ in plan:
        for index, low in pieces:
            array = arrays[index]
            array = array if len(array.shape) == 3 else array.at[0]
            source = array.at[low : low + width]
            copy = pltpu.make_async_copy(source, buffers.at[len(starts), :width], sems.at[len(starts)])
            copy.start()
            starts.append(copy)

    def update(slot, where, gradient):
        results = adam_update(
            masters[slot][where],
            gradient,
            firsts[slot][where],
            seconds[slot][where],
            RATES[slot],
            DECAYS[slot],
        )
        for kind in range(4):
            outs[kind][slot][where] = results[kind]

    begin = 0
    left = len(plan)
    for width, pieces, targets in plan:
        for index in range(len(pieces)):
            starts[begin + index].wait()
        for sub, (slot, where) in enumerate(targets):
            gradient = buffers[begin, sub].astype(F32)
            for index in range(1, len(pieces)):
                gradient = gradient + buffers[begin + index, sub].astype(F32)
            if slot < 3:
                update(slot, where, gradient)
                continue
            turn_ref[...] = jnp.zeros_like(turn_ref)
            for column in range(3):
                lanes = slice(column * LANES, (column + 1) * LANES)
                turn_ref[8 * column : 8 * column + 8, :] = gradient[:8, lanes]
            turn_ref[...] = turn_ref[...].T
            lanes, rows = masters[3].shape
            share = turn_ref[pl.ds(pl.multiple_of(at * lanes, lanes), lanes), :][:, :rows]
            update(3, slice(None), share)
            line_ref[...] = gradient[:8, 3 * LANES :]
            layers, lanes = masters[4].shape
            per = LANES // lanes
            for layer in range(layers):
                row = line_ref[pl.ds(4 * layer + at // per, 1), :]
                share = row[:, :lanes]
                for part in range(1, per):
                    other = row[:, part * lanes : (part + 1) * lanes]
                    share = jnp.where(at % per == part, other, share)
                update(4, slice(layer, layer + 1), share)
        begin += len(pieces)
        left -= 1
        for slot in range(5):
            ends = [at for at, (_, _, each) in enumerate(plan) if any(to[0] in used(slot) for to in each)]
            if ends[-1] == len(plan) - 1 - left:
                for kind in range(4):
                    outs[kind][slot].put()


def used(slot):
    return (3,) if slot > 2 else (slot,)


def last_update(at, segments, masters, firsts, seconds):
    arrays = []
    plan = []
    for width, pieces, targets in segments:
        entry = []
        for array, low in pieces:
            found = [place for place, other in enumerate(arrays) if other is array]
            if not found:
                arrays.append(array)
            entry.append((found[0] if found else len(arrays) - 1, low))
        plan.append((width, entry, targets))
    params = [list(group) for group in (masters, firsts, seconds)]
    for group in params:
        group[3] = group[3].T
    flat = params[0] + params[1] + params[2]
    outs = [shaped(array.shape) for array in params[0]] * 3
    outs += [shaped(array.shape, BF) for array in params[0]]
    pieces = sum(len(entry[1]) for entry in plan)
    block = masters[0].shape[1:]
    scratch = [
        pltpu.VMEM((pieces, max(entry[0] for entry in plan)) + block, BF),
        pltpu.VMEM((LANES, LANES), F32),
        pltpu.VMEM((8, LANES), F32),
        pltpu.SemaphoreType.DMA((pieces,)),
    ]
    kernel = functools.partial(last_kernel, plan, len(arrays))
    results = call(
        kernel, [at], flat, arrays, outs, [], scratch, 0, 8_000_000, VMEM_BYTES // 2
    )
    results = list(results)
    for kind in range(4):
        results[5 * kind + 3] = results[5 * kind + 3].T
    return results


def tie(*arrays):
    return lax.optimization_barrier(arrays)


class Direct:
    def __init__(self, axis_sizes):
        outer, inner = axis_sizes
        self.count = outer * inner
        inner_bits = inner.bit_length() - 1
        bits = self.count.bit_length() - 1
        core = [inner_bits]
        across = list(range(inner_bits + 1, bits))
        up = [0]
        along = list(range(1, inner_bits))
        self.orders = {
            "a": core + across + up + along,
            "b": core + up + across + along,
            "c": core + along + across + up,
            "d": core + along + up + across,
        }
        self.place = lax.axis_index(AXES)

    def hop(self, array, bit):
        return lax.ppermute(array, AXES, [(at, at ^ (1 << bit)) for at in range(self.count)])

    def table(self, name):
        order = self.orders[name]
        index = jnp.arange(self.count, dtype=jnp.int32)
        block = jnp.zeros_like(index)
        for at, bit in enumerate(order):
            block = block | (((index >> (len(order) - 1 - at)) & 1) << bit)
        return block ^ self.place

    def arrive(self, array, name, step):
        return self.hop(array, self.orders[name][::-1][step])

    def finish(self, array, name):
        return [array, self.hop(array, self.orders[name][0])]


def grown(arrays, arrivals):
    return [jnp.concatenate(pair, axis=0) for pair in zip(arrays, arrivals)]


class Sum:
    def __init__(self, net, name, segments, done, blocks):
        self.net = net
        self.name = name
        self.segments = segments
        self.done = done
        self.blocks = blocks

    def bit(self):
        return self.net.orders[self.name][self.done]

    def split(self, names):
        return [
            Sum(self.net, name, [segment], self.done, self.blocks)
            for name, segment in zip(names, self.segments)
        ]


def core_hop(net, pair, widths):
    keep, send = pair
    arrived = net.hop(send, net.orders["a"][0])
    low = 0
    segments = []
    for width in widths:
        segments.append((width, [(keep, low), (arrived, low)]))
        low += width
    return Sum(net, "a", segments, 1, keep.shape[0])


def combine_kernel(plan, count, outputs, *refs):
    arrays, refs = refs[:count], refs[count:]
    outs, buffers, sems = refs[:outputs], refs[outputs:-1], refs[-1]
    starts = []
    for _, _, held, number, width, pieces in plan:
        begin = 0 if held is not None else number
        for index, low in pieces:
            array = arrays[index]
            if len(array.shape) == 3:
                source = array.at[low + begin * width : low + 2 * number * width]
            else:
                source = array.at[begin : 2 * number, low : low + width]
            copy = pltpu.make_async_copy(source, buffers[len(starts)], sems.at[len(starts)])
            copy.start()
            starts.append(copy)
    begin = 0
    for slot, first, held, number, width, pieces in plan:
        for index in range(begin, begin + len(pieces)):
            starts[index].wait()
        mine = buffers[begin : begin + len(pieces)]
        jobs = [(slot, first, 0)] if held is None else [(slot, first, number), (outputs - 1, held, 0)]
        for out, place, skip in jobs:

            def body(block, carry, out=out, place=place, skip=skip, width=width, mine=mine):
                value = None
                for buffer in mine:
                    flat = len(buffer.shape) == 3
                    at = block + skip
                    part = buffer[pl.ds(at * width, width)] if flat else buffer[at]
                    value = part.astype(F32) if value is None else value + part.astype(F32)
                outs[out][pl.ds(place + block * width, width)] = value.astype(BF)
                return carry

            lax.fori_loop(0, number, body, 0)
        begin += len(pieces)


class Round:
    def __init__(self, sums, *tokens, limit=VMEM_BYTES // 3):
        self.net = sums[0].net
        self.sums = sums
        self.bits = sorted({item.bit() for item in sums})
        arrays = []
        plan = []
        sizes = [0] * len(self.bits) + [0]
        self.places = []
        block = None
        for item in sums:
            slot = self.bits.index(item.bit())
            number = item.blocks // 2
            holds = item.done > 1
            places = []
            for width, pieces in item.segments:
                entry = []
                for array, low in pieces:
                    found = [at for at, other in enumerate(arrays) if other is array]
                    if not found:
                        arrays.append(array)
                    entry.append((found[0] if found else len(arrays) - 1, low))
                    block = array.shape[-2:]
                held = sizes[-1] if holds else None
                plan.append((slot, sizes[slot], held, number, width, entry))
                places.append((sizes[slot], held))
                sizes[slot] += number * width
                sizes[-1] += number * width if holds else 0
            self.places.append((slot, places))
        tied = list(tie(*arrays, *tokens))[: len(arrays)] if tokens else arrays
        scratch = []
        moved = 0
        for _, _, held, number, width, entry in plan:
            both = number if held is None else 2 * number
            moved += both * width * (len(entry) + 1) * 16384
            for index, _ in entry:
                flat = len(arrays[index].shape) == 3
                shape = (both * width,) if flat else (both, width)
                scratch.append(pltpu.VMEM(shape + block, BF))
        if not sizes[-1]:
            sizes.pop()
        self.sends = pl.pallas_call(
            functools.partial(combine_kernel, plan, len(tied), len(sizes)),
            out_shape=[shaped((size,) + block, BF) for size in sizes],
            in_specs=[ANY] * len(tied),
            out_specs=[VMEM] * len(sizes),
            scratch_shapes=scratch + [pltpu.SemaphoreType.DMA((len(scratch),))],
            cost_estimate=pl.CostEstimate(flops=0, bytes_accessed=moved, transcendentals=0),
            compiler_params=pltpu.CompilerParams(vmem_limit_bytes=limit),
        )(*tied)

    def before(self, *arrays):
        tied = tie(*arrays, *self.sends)
        self.sends = list(tied[len(arrays) :])
        return tied[: len(arrays)]

    def go(self):
        arrived = [self.net.hop(send, bit) for send, bit in zip(self.sends, self.bits)]
        for item, (slot, places) in zip(self.sums, self.places):
            made = []
            for (width, pieces), (place, held) in zip(item.segments, places):
                stay = pieces if held is None else [(self.sends[-1], held)]
                made.append((width, stay + [(arrived[slot], place)]))
            item.segments = made
            item.done += 1
            item.blocks //= 2
        return arrived


def adam_update(weight, gradient, first, second, rate, decay):
    first_new = BETA_ONE * first + (1.0 - BETA_ONE) * gradient
    second_new = BETA_TWO * second + (1.0 - BETA_TWO) * gradient * gradient
    first_hat = first_new / (1.0 - BETA_ONE**STEP)
    second_hat = second_new / (1.0 - BETA_TWO**STEP)
    weight_new = weight - rate * (first_hat / (jnp.sqrt(second_hat) + EPS_ADAM) + decay * weight)
    return (weight_new, first_new, second_new, weight_new.astype(BF))


def gather_small(vectors, hidden):
    whole = lax.all_gather(vectors.astype(BF), AXES, axis=1, tiled=True)
    deep = lax.all_gather(hidden.astype(BF), AXES, axis=1, tiled=True)
    whole = jnp.pad(whole, ((0, HIDDEN_ROW - whole.shape[0]), (0, 0)))
    return jnp.concatenate([whole, deep.reshape(-1, whole.shape[1])], axis=0).astype(F32)


def scatter_small(grads, vectors, hidden, place, count):
    whole = lax.psum(small_rows(*grads), AXES)
    rows, lanes = vectors.shape
    first = lax.dynamic_slice_in_dim(whole[:rows], place * lanes, lanes, axis=1)
    layers, lanes = hidden.shape
    deep = whole[HIDDEN_ROW:].reshape(layers, -1)
    return first, lax.dynamic_slice_in_dim(deep, place * lanes, lanes, axis=1)


def gather_whole(attention, up, down):
    width = attention.shape[2]
    number = width // BLOCK
    square = lax.all_gather(attention, AXES, axis=1, tiled=True)
    square = square.reshape(-1, QUAD, number, BLOCK, width).transpose(0, 2, 1, 3, 4)
    tall = lax.all_gather(up, AXES, axis=1, tiled=True)
    tall = tall.reshape(2, number, BLOCK, QUAD, width).transpose(0, 1, 3, 2, 4)
    deep = lax.all_gather(down, AXES, axis=1, tiled=True).reshape(2, number, QUAD, BLOCK, width)
    half = number // 2
    quads = [square[0], tall[0], deep[0], square[1], square[2], tall[1], deep[1]]
    return [(quad[:half], quad[half:]) for quad in quads]


def scatter_whole(quads):
    joined = [jnp.concatenate(pair, axis=0).astype(F32) for pair in quads]
    number, _, _, width = joined[0].shape
    square = jnp.stack([joined[0], joined[3], joined[4]])
    square = square.transpose(0, 2, 1, 3, 4).reshape(3 * QUAD, width, width)
    tall = jnp.stack([joined[1], joined[5]]).transpose(0, 1, 3, 2, 4)
    tall = tall.reshape(2, width, QUAD * width)
    deep = jnp.stack([joined[2], joined[6]]).reshape(2, QUAD * width, width)
    return [
        lax.psum_scatter(part, AXES, scatter_dimension=1, tiled=True)
        for part in (square, tall, deep)
    ]


def direct_step(pairs, source, target, grad, masters, firsts, seconds, axis_sizes):
    net = Direct(axis_sizes)
    source_pair, target_pair, cross_pair = pairs
    a, b = net.table("a"), net.table("b")
    cut = QUAD // 2
    at = (net.place % (net.count * LANES // source.shape[1])).astype(jnp.int32).reshape(1)

    one, two, three = first_arrays(at, *masters)
    up_two, down_two = three[:, :QUAD], three[:, QUAD:]
    for step in (0, 1):
        more = tie(
            net.arrive(one, "a", step),
            net.arrive(up_two, "c", step),
            net.arrive(down_two, "d", step),
        )
        one, up_two, down_two = grown((one, up_two, down_two), more)
    three = jnp.concatenate([up_two, down_two], axis=1)
    left, right = one[:, : cut + QUAD], one[:, cut + QUAD :]
    two, three, left, right = tie(two, three, left, right)
    left, right, two = grown(
        (left, right, two),
        tie(net.arrive(left, "a", 2), net.arrive(right, "b", 2), net.arrive(two, "a", 0)),
    )
    left, right, two, three = grown(
        (left, right, two, three),
        tie(
            net.arrive(left, "a", 3),
            net.arrive(right, "b", 3),
            net.arrive(two, "a", 1),
            net.arrive(three, "c", 2),
        ),
    )
    self_w, cross_w = two[:, :QUAD], two[:, QUAD:]
    more = tie(
        net.hop(left, net.orders["a"][0]),
        net.hop(right, net.orders["b"][0]),
        net.arrive(self_w, "a", 2),
        net.arrive(cross_w, "b", 2),
    )
    left, right = [left, more[0]], [right, more[1]]
    self_w, cross_w = grown((self_w, cross_w), more[2:])
    source, self_w, cross_w, three = tie(source, self_w, cross_w, three)
    more = [
        net.arrive(self_w, "a", 3),
        net.arrive(cross_w, "b", 3),
        net.arrive(three, "c", 3),
    ]
    enc_attend_w = [(a, left, 0, cut), (b, right, 0, cut)]
    enc_feed_w = [(a, left, cut, QUAD), (b, right, cut + 1, QUAD)]
    enc_kept = attend_forward(source_pair, None, 0, source, None, enc_attend_w, False)
    enc_mid, small = enc_kept[7], enc_kept[8]
    enc_feed_kept = feed_forward(small, 5, HIDDEN_ROW, enc_mid, enc_feed_w)
    memory = enc_feed_kept[0]
    self_w, cross_w = grown((self_w, cross_w), tie(*more[:2], memory)[:2])
    (three,) = grown([three], tie(more[2], self_w, cross_w)[:1])
    target, self_w, cross_w, three = tie(target, self_w, cross_w, three)
    self_w = [(a, net.finish(self_w, "a"), 0, QUAD)]
    cross_w = [(b, net.finish(cross_w, "b"), 0, QUAD)]
    self_kept = attend_forward(target_pair, small, 8, target, None, self_w, True)
    dec_one = self_kept[7]
    three = net.finish(three, "c")
    cross_kept = attend_forward(cross_pair, small, 13, dec_one, memory, cross_w, False)
    dec_two = cross_kept[7]
    dec_feed_w = [(net.table("c"), three, 0, QUAD), (net.table("d"), three, QUAD, QUAD)]
    result, two_grad, dec_feed_small, feed_two = feed_both(
        (a, b), small, 18, HIDDEN_ROW + QUAD, dec_two, grad, dec_feed_w
    )

    names = ("a", "b")
    feed_two = core_hop(net, feed_two, (QUAD, QUAD)).split(names)
    one_grad, memory_grad, cross_small, cross_q = attend_backward(
        (a, b), cross_pair, small, 13, two_grad, cross_kept, dec_one, memory, cross_w, False, None
    )
    send = Round(feed_two, cross_small)
    memory_grad, *cross_q = send.before(memory_grad, *cross_q)
    send.go()
    cross_s = core_hop(net, cross_q, (cut, cut)).split(names)
    mid_grad, enc_feed_small, feed_one = feed_backward(
        (a, b), small, 5, memory_grad, enc_feed_kept, enc_mid, enc_feed_w
    )
    send = Round(feed_two + cross_s, enc_feed_small)
    one_grad, *feed_one = send.before(one_grad, *feed_one)
    before = send.go()
    feed_one = core_hop(net, feed_one, (QUAD, QUAD)).split(names)
    target_grad, _, self_small, self_q = attend_backward(
        (a, b), target_pair, small, 8, one_grad, self_kept, target, None, self_w, True, None
    )
    send = Round(cross_s + feed_one, self_small, *before)
    mid_grad, *self_q = send.before(mid_grad, *self_q)
    send.go()
    self_s = core_hop(net, self_q, (cut, cut)).split(names)
    others = (enc_feed_small, self_small, cross_small, dec_feed_small)
    source_grad, _, _, enc_q = attend_backward(
        (a, b), source_pair, small, 0, mid_grad, enc_kept, source, None, enc_attend_w, False, others
    )
    send = Round(feed_two + cross_s + feed_one + self_s, source_grad)
    enc_q = send.before(*enc_q)
    last = send.go()
    enc_s = core_hop(net, enc_q, (cut, cut + 1)).split(names)
    for sums in (
        enc_s + self_s + feed_two + cross_s,
        enc_s + self_s + feed_one,
        enc_s + self_s + feed_one,
        enc_s,
    ):
        send = Round(sums, *last)
        last = send.go()

    square = [(0, index) for index in range(3 * QUAD)]
    tall, deep = [], []
    for layer in range(2):
        for index in range(QUAD):
            lanes = slice(index * source.shape[1], (index + 1) * source.shape[1])
            tall.append((1, (layer, slice(None), lanes)))
            deep.append((2, (layer, slice(index * BLOCK, (index + 1) * BLOCK))))
    targets = [square[:cut], square[cut:QUAD] + [(3, None)]]
    targets += [square[QUAD : QUAD + cut], square[QUAD + cut : 2 * QUAD], tall[:QUAD], deep[:QUAD]]
    targets += [tall[QUAD:], deep[QUAD:]]
    targets += [square[2 * QUAD : 2 * QUAD + cut], square[2 * QUAD + cut :]]
    segments = [item.segments[0] for item in enc_s + self_s + feed_one + feed_two + cross_s]
    segments = [segment + (target,) for segment, target in zip(segments, targets)]
    updated = last_update(at, segments, masters, firsts, seconds)
    return (memory, result, source_grad, target_grad), updated


def whole_step(pairs, source, target, grad, masters, firsts, seconds, axis_sizes):
    attention, up, down = [master.astype(BF) for master in masters[:3]]
    vectors, hidden = masters[3:]
    source_pair, target_pair, cross_pair = pairs
    small = gather_small(vectors, hidden)
    quads = gather_whole(attention, up, down)
    table = jnp.arange(source.shape[1] // BLOCK, dtype=jnp.int32)
    two = (table, table)
    parts = [(table, list(quad), 0, QUAD) for quad in quads]
    enc_kept = attend_forward(source_pair, small, 0, source, None, parts[:1], False)
    enc_mid = enc_kept[7]
    enc_feed_kept = feed_forward(small, 5, HIDDEN_ROW, enc_mid, parts[1:3])
    memory = enc_feed_kept[0]
    self_kept = attend_forward(target_pair, small, 8, target, None, parts[3:4], True)
    dec_one = self_kept[7]
    cross_kept = attend_forward(cross_pair, small, 13, dec_one, memory, parts[4:5], False)
    dec_two = cross_kept[7]
    result, two_grad, dec_feed_small, feed_two = feed_both(
        two, small, 18, HIDDEN_ROW + QUAD, dec_two, grad, parts[5:7]
    )
    one_grad, memory_grad, cross_small, cross_q = attend_backward(
        two, cross_pair, small, 13, two_grad, cross_kept, dec_one, memory, parts[4:5], False, None
    )
    target_grad, _, self_small, self_q = attend_backward(
        two, target_pair, small, 8, one_grad, self_kept, target, None, parts[3:4], True, None
    )
    mid_grad, enc_feed_small, feed_one = feed_backward(
        two, small, 5, memory_grad, enc_feed_kept, enc_mid, parts[1:3]
    )
    source_grad, _, enc_small, enc_q = attend_backward(
        two, source_pair, small, 0, mid_grad, enc_kept, source, None, parts[:1], False, None
    )
    quads = [enc_q]
    quads += [[half[:, low : low + QUAD] for half in feed_one] for low in (0, QUAD)]
    quads += [self_q, cross_q]
    quads += [[half[:, low : low + QUAD] for half in feed_two] for low in (0, QUAD)]
    smalls = (enc_small, enc_feed_small, self_small, cross_small, dec_feed_small)
    count = axis_sizes[0] * axis_sizes[1]
    shares = scatter_small(smalls, vectors, hidden, lax.axis_index(AXES), count)
    grads = tuple(scatter_whole(quads)) + shares
    updated = [
        adam_update(
            masters[slot], grads[slot], firsts[slot], seconds[slot], RATES[slot], DECAYS[slot]
        )
        for slot in range(5)
    ]
    flat = [updated[slot][kind] for kind in range(4) for slot in range(5)]
    return (memory, result, source_grad, target_grad), flat


def per_device(
    axis_sizes,
    source_tokens,
    target_tokens,
    source_segments,
    target_segments,
    output_grad,
    attention_weight,
    up_weight,
    down_weight,
    vectors,
    hidden_bias,
    *moments,
):
    masters = (attention_weight, up_weight, down_weight, vectors, hidden_bias)
    firsts = moments[:5]
    seconds = moments[5:]
    width = source_tokens.shape[2]
    pairs = (
        (source_segments, source_segments),
        (target_segments, target_segments),
        (target_segments, source_segments),
    )
    direct = axis_sizes[0] * axis_sizes[1] * BLOCK == width
    tokens, updated = (direct_step if direct else whole_step)(
        pairs,
        source_tokens[0],
        target_tokens[0],
        output_grad[0],
        masters,
        firsts,
        seconds,
        axis_sizes,
    )
    return tuple(array[None] for array in tokens) + tuple(updated)


def solution(mesh):
    rows = P(AXES, None, None)
    line = P(AXES, None)
    matrix = P(None, AXES, None)
    vector = P(None, AXES)
    state = (matrix, matrix, matrix, vector, vector)
    return jax.shard_map(
        functools.partial(per_device, (mesh.shape["dp"], mesh.shape["fsdp"])),
        mesh=mesh,
        in_specs=(rows, rows, line, line, rows) + state * 3,
        out_specs=(rows,) * 4 + state * 4,
        check_vma=False,
    )
```

```python
import functools

import jax
import jax.numpy as jnp
from jax import lax
from jax.experimental import pallas as pl
from jax.experimental.pallas import tpu as pltpu
from jax.sharding import PartitionSpec as P

HEADS = 8
STEP = 10
EPS_NORM = 1e-05
EPS_ADAM = 1e-08
BETA_ONE = 0.9
BETA_TWO = 0.999
LOWEST = -1e30
RATES = (0.05, 0.05, 0.05, 0.3, 0.3)
DECAYS = (0.01, 0.01, 0.01, 0.0, 0.0)
AXES = ("dp", "fsdp")
QUAD = 4
BLOCK = 16
CHUNK = 64
LANES = 128
SMALL_ROWS = 32
VMEM_BYTES = 60 * 1024 * 1024
HIDDEN_ROW = 24
BF = jnp.bfloat16
F32 = jnp.float32
VMEM = pl.BlockSpec(memory_space=pltpu.VMEM)
SMEM = pl.BlockSpec(memory_space=pltpu.SMEM)
ANY = pl.BlockSpec(memory_space=pl.ANY)
ROOT_TWO_PI = 0.7978845608028654
CUBIC = 0.044715


def dot(left, right):
    return jnp.dot(left, right, preferred_element_type=F32)


def dot_nt(left, right):
    return lax.dot_general(left, right, (((1,), (1,)), ((), ())), preferred_element_type=F32)


class Input:
    def __init__(self, array, room, sem):
        self.room = room
        self.shape = room.shape
        self.copy = pltpu.make_async_copy(array, room, sem)
        self.copy.start()
        self.there = False

    def __getitem__(self, where):
        if not self.there:
            self.copy.wait()
            self.there = True
        return self.room[where]


class Output:
    def __init__(self, array, room, sem):
        self.array = array
        self.room = room
        self.shape = room.shape
        self.sem = sem
        self.left = False

    def __getitem__(self, where):
        return self.room[where]

    def __setitem__(self, where, value):
        self.room[where] = value

    def put(self, index=None):
        source = self.room if index is None else self.room.at[index]
        target = self.array if index is None else self.array.at[index]
        pltpu.make_async_copy(source, target, self.sem).start()
        self.left = True

    def finish(self):
        if not self.left:
            self.put()
        pltpu.make_async_copy(self.room, self.array, self.sem).wait()


def staged_kernel(kernel, scalars, inputs, others, outputs, targets, *refs):
    refs = list(refs)
    sems = refs.pop()
    count = inputs + outputs
    rooms = refs[len(refs) - count :]
    refs = refs[: len(refs) - count]
    at = scalars
    for slot in range(inputs):
        refs[at + slot] = Input(refs[at + slot], rooms[slot], sems.at[slot])
    at += inputs + others
    made = []
    for slot in range(inputs, count):
        place = at + slot - inputs
        refs[place] = Output(refs[place], rooms[slot], sems.at[slot])
        made.append(refs[place])
    kernel(*refs)
    for output in made:
        output.finish()


def load_start(part, place, sems):
    table, arrays, low, number = part
    at = 0
    for slot, array in enumerate(arrays):
        for index in range(array.shape[0]):
            source = array.at[index, low : low + number]
            pltpu.make_async_copy(source, place(table[at]), sems.at[slot]).start()
            at += 1


def load_wait(part, sems):
    table, arrays, low, number = part
    for slot, array in enumerate(arrays):
        whole = array.at[:, low : low + number]
        pltpu.make_async_copy(whole, whole, sems.at[slot]).wait()


def store_start(part, place, sems):
    table, arrays, low, number = part
    half = arrays[0].shape[0]
    for index in range(half):
        for slot in (1, 0):
            target = arrays[slot].at[index, low : low + number]
            source = place(table[slot * half + index])
            pltpu.make_async_copy(source, target, sems.at[slot]).start()


def row_place(scratch, low, high):
    def place(block):
        start = pl.multiple_of(block * BLOCK, BLOCK)
        return scratch.at[low:high, pl.ds(start, BLOCK), :]

    return place


def block_place(scratch):
    return lambda block: scratch.at[block]


def column_sum(values):
    rows, width = values.shape
    return jnp.sum(values.reshape(rows // 8, 8, width), axis=0)


def total_of(sums):
    return jnp.sum(functools.reduce(jnp.add, sums), axis=0, keepdims=True)


def norm_forward(pre_of, length, gain, shift, out_ref, hat_ref, rstd_ref):
    for at in range(0, length, CHUNK):
        rows = slice(at, at + CHUNK)
        pre = pre_of(rows)
        mean = jnp.mean(pre, axis=-1, keepdims=True)
        centred = pre - mean
        spread = jnp.mean(centred * centred, axis=-1, keepdims=True)
        rstd = lax.rsqrt(spread + EPS_NORM)
        hat = centred * rstd
        hat_ref[rows] = hat
        rstd_ref[rows] = jnp.broadcast_to(rstd, (CHUNK, LANES))
        out_ref[rows] = hat * gain + shift
    for ref in (hat_ref, rstd_ref, out_ref):
        if isinstance(ref, Output):
            ref.put()


def norm_backward(grad_ref, hat_ref, rstd_ref, gain, pre_out, low_out):
    length = grad_ref.shape[0]
    sums = ([], [], [])
    for at in range(0, length, CHUNK):
        rows = slice(at, at + CHUNK)
        grad = grad_ref[rows].astype(F32)
        hat = hat_ref[rows]
        sums[0].append(column_sum(grad * hat))
        sums[1].append(column_sum(grad))
        scaled = grad * gain
        one = jnp.mean(scaled, axis=-1, keepdims=True)
        two = jnp.mean(scaled * hat, axis=-1, keepdims=True)
        pre = rstd_ref[rows][:, :1] * (scaled - one - hat * two)
        low = pre.astype(BF)
        pre_out[rows] = pre
        low_out[rows] = low
        sums[2].append(column_sum(low.astype(F32)))
    return [total_of(each) for each in sums]


def lane_mask(rows):
    return lax.broadcasted_iota(jnp.int32, (rows, LANES), 1) < LANES // 2


def stacked_pair(block):
    first = lane_mask(block.shape[0])
    zero = jnp.zeros_like(block)
    return jnp.concatenate([jnp.where(first, block, zero), jnp.where(first, zero, block)], axis=0)


def merged_pair(stacked):
    rows = stacked.shape[0] // 2
    return jnp.where(lane_mask(rows), stacked[:rows], stacked[rows:])


def mask_fill(bias_ref, column_seg, row_seg, causal, transposed):
    length = bias_ref.shape[0]
    column = jnp.broadcast_to(column_seg, (LANES, length)).T
    for at in range(0, length, LANES):
        same = column == row_seg[:, at : at + LANES]
        if causal:
            down = lax.broadcasted_iota(jnp.int32, (length, LANES), 0)
            along = lax.broadcasted_iota(jnp.int32, (length, LANES), 1) + at
            order = (down <= along) if transposed else (along <= down)
            same = same & order
        bias_ref[:, at : at + LANES] = jnp.where(same, 0.0, LOWEST)


def take_parts(refs, layout, tables):
    parts = []
    for slot, (arrays, low, number) in enumerate(layout):
        parts.append((tables[slot], [refs.pop(0) for _ in range(arrays)], low, number))
    return parts


def small_part(part):
    table, arrays, low, number = part
    return table, arrays, low + number, 1


def small_join(blocks_ref):
    count = blocks_ref.shape[0]
    groups = blocks_ref.shape[3] // LANES
    per = count // groups
    vectors = []
    hidden = [[], []]
    for group in range(groups):
        total = blocks_ref[group * per, 0, :8].astype(F32)
        for at in range(group * per + 1, (group + 1) * per):
            total = total + blocks_ref[at, 0, :8].astype(F32)
        columns = [total[:, at : at + LANES] for at in range(0, 4 * LANES, LANES)]
        vectors.append(jnp.concatenate(columns[:3], axis=0))
        for layer in range(2):
            rows = [columns[3][4 * layer + at : 4 * layer + at + 1] for at in range(4)]
            hidden[layer].append(jnp.concatenate(rows, axis=1))
    return jnp.concatenate([jnp.concatenate(vectors, axis=1)] + hidden[0] + hidden[1], axis=0)


def small_split(whole, group):
    lanes = slice(group * LANES, (group + 1) * LANES)
    columns = [whole[at : at + 8, lanes] for at in (0, 8, 16)]
    rows = []
    for layer in range(2):
        row = whole[24 + 4 * layer + group : 25 + 4 * layer + group]
        rows += [row[:, at : at + LANES] for at in range(0, 4 * LANES, LANES)]
    columns.append(jnp.concatenate(rows, axis=0))
    block = jnp.concatenate(columns, axis=1)
    return jnp.concatenate([block, jnp.zeros_like(block)], axis=0).astype(BF)


def attend_forward_kernel(layout, cross, causal, base, joins, *refs):
    refs = list(refs)
    tables = [refs.pop(0) for _ in layout]
    query_seg = refs.pop(0)
    key_seg = refs.pop(0)
    small = None if joins else refs.pop(0)
    rows_ref = refs.pop(0)
    memory_ref = refs.pop(0) if cross else None
    parts = take_parts(refs, layout, tables)
    q_ref, k_ref, v_ref, o_ref, lse_ref, hat_ref, rstd_ref, out_ref = [refs.pop(0) for _ in range(8)]
    if joins:
        small = refs.pop(0)
        blocks_ref = refs.pop()
        extra = small_part(parts[-1])
    w_ref, bias_ref, scores_ref, exponent_ref, largest_ref, mixed_ref, attended_ref, sems = refs
    first = 0
    if joins:
        load_start(extra, lambda block: blocks_ref.at[block], sems.at[len(parts)])
    for slot, part in enumerate(parts):
        load_start(part, row_place(w_ref, first, first + part[3]), sems.at[slot])
        first += part[3]
    length, width = rows_ref.shape
    mask_fill(bias_ref, query_seg[...], key_seg[...], causal, False)
    rows = rows_ref[...].astype(BF)
    keys = memory_ref[...].astype(BF) if cross else rows
    if joins:
        load_wait(extra, sems.at[len(parts)])
        small[...] = small_join(blocks_ref)
        small.put()
    for slot, part in enumerate(parts):
        load_wait(part, sems.at[slot])
    scale = (width // HEADS) ** (-0.5)
    q_ref[...] = (dot(rows, w_ref[0]) + small[base : base + 1]).astype(BF) * jnp.asarray(scale, BF)
    k_ref[...] = dot(keys, w_ref[1]).astype(BF)
    v_ref[...] = (dot(keys, w_ref[2]) + small[base + 1 : base + 2]).astype(BF)
    for ref in (q_ref, k_ref, v_ref):
        ref.put()
    lane = lax.broadcasted_iota(jnp.int32, (LANES, LANES), 1)
    logs = [jnp.zeros((LANES, LANES), F32)] * (length // LANES)
    for pair in range(HEADS // 2):
        lanes = slice(pair * LANES, (pair + 1) * LANES)
        side = pair % 2
        scores_ref[side] = dot_nt(stacked_pair(q_ref[:, lanes]), k_ref[:, lanes])
        for at in range(0, 2 * length, CHUNK):
            chunk = slice(at, at + CHUNK)
            own = slice(at % length, at % length + CHUNK)
            reach = own.start // LANES * LANES + LANES if causal else length
            scores = scores_ref[side, chunk, :reach] + bias_ref[own, :reach]
            largest = jnp.max(scores, axis=-1, keepdims=True)
            exponent_ref[side, chunk, :reach] = jnp.exp(scores - largest).astype(BF)
            if reach < length:
                exponent_ref[side, chunk, reach:] = jnp.zeros((CHUNK, length - reach), BF)
            largest_ref[side, chunk] = jnp.broadcast_to(largest, (CHUNK, LANES))
        values = jnp.concatenate([v_ref[:, lanes], jnp.ones((length, LANES), BF)], axis=1)
        mixed_ref[side] = dot(exponent_ref[side], values)
        for slot, at in enumerate(range(0, length, LANES)):
            outs = []
            for half in range(2):
                chunk = slice(half * length + at, half * length + at + LANES)
                total = mixed_ref[side, chunk, LANES:]
                outs.append(mixed_ref[side, chunk, :LANES] / total)
                log_total = largest_ref[side, chunk] + jnp.log(total)
                logs[slot] = jnp.where(lane == 2 * pair + half, log_total, logs[slot])
            o_ref[at : at + LANES, lanes] = jnp.where(lane_mask(LANES), outs[0], outs[1]).astype(BF)
    for slot, at in enumerate(range(0, length, LANES)):
        lse_ref[:, at : at + LANES] = logs[slot].T[:HEADS]
    o_ref.put()
    lse_ref.put()
    attended_ref[...] = dot(o_ref[...], w_ref[3])
    out_bias = small[base + 2 : base + 3]
    norm_forward(
        lambda rows: rows_ref[rows].astype(F32) + (attended_ref[rows] + out_bias),
        length,
        small[base + 3 : base + 4],
        small[base + 4 : base + 5],
        out_ref,
        hat_ref,
        rstd_ref,
    )


def attend_backward_kernel(layout, cross, causal, base, splits, *refs):
    refs = list(refs)
    tables = [refs.pop(0) for _ in layout]
    out_tables = [refs.pop(0), refs.pop(0)]
    query_seg = refs.pop(0)
    key_seg = refs.pop(0)
    small = refs.pop(0)
    grad_ref = refs.pop(0)
    hat_ref, rstd_ref = refs.pop(0), refs.pop(0)
    rows_ref = refs.pop(0)
    memory_ref = refs.pop(0) if cross else None
    q_ref, k_ref, v_ref, o_ref, lse_ref = [refs.pop(0) for _ in range(5)]
    others = [refs.pop(0) for _ in range(4)] if splits else None
    parts = take_parts(refs, layout, tables)
    rows_out = refs.pop(0)
    memory_out = refs.pop(0) if cross else None
    small_out = None if splits else refs.pop(0)
    targets = [refs.pop(0), refs.pop(0)]
    outs = []
    for slot, table in enumerate(out_tables):
        outs.append((table, targets, slot * QUAD // 2, QUAD // 2))
    blocks_ref = refs.pop() if splits else None
    w_ref, dw_ref, bias_ref, dout_ref, dq_t_ref, dk_ref, dv_ref, kt_ref = refs[:8]
    low_ref, scores_ref, prob_grad_ref, prob_ref, score_grad_ref, sems = refs[8:]
    first = 0
    for slot, part in enumerate(parts):
        load_start(part, row_place(w_ref, first, first + part[3]), sems.at[slot])
        first += part[3]
    length, width = rows_ref.shape
    head = width // HEADS
    scale = head ** (-0.5)
    gain_grad, shift_grad, out_bias = norm_backward(
        grad_ref, hat_ref, rstd_ref, small[base + 3 : base + 4], rows_out, low_ref
    )
    mask_fill(bias_ref, key_seg[...], query_seg[...], causal, True)
    low = low_ref[...]
    for slot, part in enumerate(parts):
        load_wait(part, sems.at[slot])
    dout_ref[...] = dot_nt(low, w_ref[3]).astype(BF)
    dw_ref[3] = dot(o_ref[...].T, low).astype(BF)
    product = dout_ref[...].astype(F32) * o_ref[...].astype(F32)
    high = product.astype(BF)
    rest = (product - high.astype(F32)).astype(BF)
    picker = lax.broadcasted_iota(jnp.int32, (BLOCK, width), 1) // head
    picker = (picker == lax.broadcasted_iota(jnp.int32, (BLOCK, width), 0)).astype(BF)
    row_dots = dot_nt(picker, high) + dot_nt(picker, rest)
    kt_ref[...] = k_ref[...].T
    for pair in range(HEADS // 2):
        lanes = slice(pair * LANES, (pair + 1) * LANES)
        side = pair % 2
        query = q_ref[:, lanes]
        dout = dout_ref[:, lanes]
        scores_ref[side] = dot_nt(stacked_pair(k_ref[:, lanes]), query)
        prob_grad_ref[side] = dot_nt(stacked_pair(v_ref[:, lanes]), dout)
        for at in range(0, 2 * length, CHUNK):
            which = 2 * pair + at // length
            chunk = slice(at, at + CHUNK)
            own = slice(at % length, at % length + CHUNK)
            begin = own.start // LANES * LANES if causal else 0
            shift = bias_ref[own, begin:] - lse_ref[which : which + 1, begin:]
            prob = jnp.exp(scores_ref[side, chunk, begin:] + shift)
            prob_ref[side, chunk, begin:] = prob.astype(BF)
            centred = prob_grad_ref[side, chunk, begin:] - row_dots[which : which + 1, begin:]
            score_grad_ref[side, chunk, begin:] = (prob * centred).astype(BF)
            if begin:
                prob_ref[side, chunk, :begin] = jnp.zeros((CHUNK, begin), BF)
                score_grad_ref[side, chunk, :begin] = jnp.zeros((CHUNK, begin), BF)
        dv_ref[:, lanes] = merged_pair(dot(prob_ref[side], dout)).astype(BF)
        dk_ref[:, lanes] = merged_pair(dot(score_grad_ref[side], query)).astype(BF)
        for half in range(2):
            at = pair * LANES + half * head
            own = slice(half * length, (half + 1) * length)
            dq_t_ref[at : at + head, :] = dot(kt_ref[at : at + head, :], score_grad_ref[side, own])
    query_grad = (dq_t_ref[...] * scale).T.astype(BF)
    key_grad = dk_ref[...]
    value_grad = dv_ref[...]
    turned = rows_ref[...].astype(BF).T
    other = memory_ref[...].astype(BF).T if cross else turned
    dw_ref[2] = dot(other, value_grad).astype(BF)
    store_start(outs[1], row_place(dw_ref, QUAD // 2, QUAD), sems.at[1])
    dw_ref[0] = dot(turned, query_grad).astype(BF)
    dw_ref[1] = dot(other, key_grad).astype(BF)
    store_start(outs[0], row_place(dw_ref, 0, QUAD // 2), sems.at[0])
    rows_back = rows_out[...] + dot_nt(query_grad, w_ref[0])
    memory_back = dot_nt(key_grad, w_ref[1]) + dot_nt(value_grad, w_ref[2])
    if cross:
        rows_out[...] = rows_back
        memory_out[...] = memory_back
        memory_out.put()
    else:
        rows_out[...] = rows_back + memory_back
    rows_out.put()
    query_bias = total_of([column_sum(query_grad.astype(F32))])
    value_bias = total_of([column_sum(value_grad.astype(F32))])
    spare = jnp.zeros((3, width), F32)
    own = jnp.concatenate(
        [query_bias, value_bias, out_bias, gain_grad, shift_grad, spare], axis=0
    )
    if splits:
        enc_feed, self_attend, cross_attend, dec_feed = [other[...] for other in others]
        whole = small_rows(own, enc_feed, self_attend, cross_attend, dec_feed)
        groups = blocks_ref.shape[0]
        for group in range(groups):
            blocks_ref[group, 0] = small_split(whole, group)
        extra = small_part(outs[-1])
        per = 2 * extra[1][0].shape[0] // groups
        store_start(extra, lambda block: blocks_ref.at[block // per], sems.at[2])
        load_wait(extra, sems.at[2])
    else:
        small_out[...] = own
    for slot, part in enumerate(outs):
        load_wait(part, sems.at[slot])


def small_rows(enc_attend, enc_feed, self_attend, cross_attend, dec_feed):
    return jnp.concatenate(
        [
            enc_attend[:5],
            enc_feed[:3],
            self_attend[:5],
            cross_attend[:5],
            dec_feed[:3],
            dec_feed[7:],
            dec_feed[7:],
            dec_feed[7:],
            enc_feed[3:7],
            dec_feed[3:7],
        ],
        axis=0,
    )


def gelu_parts(pre):
    square = pre * pre
    curve = jnp.tanh(ROOT_TWO_PI * pre * (1.0 + CUBIC * square))
    half = 0.5 * pre
    rise = 0.5 + 0.5 * curve
    bend = ROOT_TWO_PI * (1.0 + 3.0 * CUBIC * square)
    return pre * rise, rise + half * (1.0 - curve * curve) * bend


def chunk_of(ref, index):
    number = ref.shape[0] // QUAD
    part = ref[index * number : (index + 1) * number]
    return part.reshape(number * ref.shape[1] * ref.shape[2], ref.shape[3])


def feed_forward_steps(small, base, hidden_at, rows_ref, up_ref, down_ref, active_ref, slope_ref, pre_ref, sum_ref):
    rows = rows_ref[...].astype(BF)
    length = rows.shape[0]
    for index in range(QUAD):
        at = hidden_at + index
        side = index % 2
        pre_ref[side] = dot(rows, up_ref[index])
        bias = small[at : at + 1]
        for at in range(0, length, CHUNK // 2):
            chunk = slice(at, at + CHUNK // 2)
            active, slope = gelu_parts(pre_ref[side, chunk] + bias)
            active_ref[index, chunk] = active.astype(BF)
            slope_ref[index, chunk] = slope
        for ref in (active_ref, slope_ref):
            if isinstance(ref, Output):
                ref.put(index)
    wide = jnp.concatenate([active_ref[index] for index in range(QUAD)], axis=1)
    number, _, _, width = down_ref.shape
    sum_ref[...] = dot(wide, down_ref[...].reshape(QUAD * width, width))
    out_bias = small[base : base + 1]
    return lambda rows: rows_ref[rows] + (sum_ref[rows] + out_bias)


def feed_backward_steps(
    pre_grad, low_ref, rows_ref, up_ref, down_ref, active_ref, slope_ref, dup_ref, ddown_ref, rows_out, back_ref, outs, sems
):
    low = low_ref[...]
    length = low.shape[0]
    number = ddown_ref.shape[0] // QUAD
    for index in range(QUAD):
        down_grad = dot(active_ref[index].T, low).astype(BF)
        ddown_ref[index * number : (index + 1) * number] = down_grad.reshape(
            (number,) + ddown_ref.shape[1:]
        )
    store_start(outs[1], block_place(ddown_ref), sems.at[1])
    turned = rows_ref[...].astype(BF).T
    hidden_grads = []
    hiddens = []
    for index in range(QUAD):
        side = index % 2
        back_ref[side] = dot_nt(low, chunk_of(down_ref, index))
        sums = []
        parts = []
        for at in range(0, length, CHUNK):
            chunk = slice(at, at + CHUNK)
            hidden = (back_ref[side, chunk] * slope_ref[index, chunk]).astype(BF)
            sums.append(column_sum(hidden.astype(F32)))
            parts.append(hidden)
        hidden = jnp.concatenate(parts, axis=0)
        hidden_grads.append(total_of(sums))
        dup_ref[index] = dot(turned, hidden).astype(BF)
        hiddens.append(hidden)
    store_start(outs[0], row_place(dup_ref, 0, QUAD), sems.at[0])
    total = pre_grad[...]
    for index in range(QUAD):
        total = total + dot_nt(hiddens[index], up_ref[index])
    rows_out[...] = total
    rows_out.put()
    return hidden_grads


def load_feed(parts, up_ref, down_ref, sems):
    load_start(parts[0], row_place(up_ref, 0, QUAD), sems.at[0])
    load_start(parts[1], block_place(down_ref), sems.at[1])


def wait_feed(parts, sems):
    for slot, part in enumerate(parts):
        load_wait(part, sems.at[slot])


def feed_outs(refs, tables):
    arrays = [refs.pop(0), refs.pop(0)]
    return [(tables[slot], arrays, slot * QUAD, QUAD) for slot in range(2)]


def feed_small(out_bias, gain_grad, shift_grad, hidden_grads):
    spare = jnp.zeros_like(out_bias)
    return jnp.concatenate([out_bias, gain_grad, shift_grad] + hidden_grads + [spare], axis=0)


def feed_forward_kernel(layout, base, hidden_at, *refs):
    refs = list(refs)
    tables = [refs.pop(0), refs.pop(0)]
    small, rows_ref = refs.pop(0), refs.pop(0)
    parts = take_parts(refs, layout, tables)
    out_ref, hat_ref, rstd_ref, active_ref, slope_ref, up_ref, down_ref = refs[:7]
    pre_ref, sum_ref, sems = refs[7:]
    load_feed(parts, up_ref, down_ref, sems)
    wait_feed(parts, sems)
    pre_of = feed_forward_steps(
        small, base, hidden_at, rows_ref, up_ref, down_ref, active_ref, slope_ref, pre_ref, sum_ref
    )
    gain, shift = small[base + 1 : base + 2], small[base + 2 : base + 3]
    norm_forward(pre_of, rows_ref.shape[0], gain, shift, out_ref, hat_ref, rstd_ref)


def feed_backward_kernel(layout, base, *refs):
    refs = list(refs)
    tables = [refs.pop(0), refs.pop(0)]
    out_tables = [refs.pop(0), refs.pop(0)]
    small, grad_ref, hat_ref, rstd_ref, rows_ref = [refs.pop(0) for _ in range(5)]
    active_ref, slope_ref = refs.pop(0), refs.pop(0)
    parts = take_parts(refs, layout, tables)
    rows_out, small_out = refs.pop(0), refs.pop(0)
    outs = feed_outs(refs, out_tables)
    up_ref, down_ref, dup_ref, ddown_ref, low_ref, back_ref, sems, out_sems = refs
    load_feed(parts, up_ref, down_ref, sems)
    gain_grad, shift_grad, out_bias = norm_backward(
        grad_ref, hat_ref, rstd_ref, small[base + 1 : base + 2], rows_out, low_ref
    )
    wait_feed(parts, sems)
    hidden_grads = feed_backward_steps(
        rows_out,
        low_ref,
        rows_ref,
        up_ref,
        down_ref,
        active_ref,
        slope_ref,
        dup_ref,
        ddown_ref,
        rows_out,
        back_ref,
        outs,
        out_sems,
    )
    small_out[...] = feed_small(out_bias, gain_grad, shift_grad, hidden_grads)
    wait_feed(outs, out_sems)


def feed_both_kernel(layout, base, hidden_at, *refs):
    refs = list(refs)
    tables = [refs.pop(0), refs.pop(0)]
    out_tables = [refs.pop(0), refs.pop(0)]
    small, rows_ref, grad_ref = [refs.pop(0) for _ in range(3)]
    parts = take_parts(refs, layout, tables)
    out_ref, rows_out, small_out = [refs.pop(0) for _ in range(3)]
    outs = feed_outs(refs, out_tables)
    up_ref, down_ref, dup_ref, ddown_ref, low_ref, back_ref, sum_ref = refs[:7]
    active_ref, slope_ref, hat_ref, rstd_ref, sems, out_sems = refs[7:]
    load_feed(parts, up_ref, down_ref, sems)
    wait_feed(parts, sems)
    pre_of = feed_forward_steps(
        small, base, hidden_at, rows_ref, up_ref, down_ref, active_ref, slope_ref, back_ref, sum_ref
    )
    gain, shift = small[base + 1 : base + 2], small[base + 2 : base + 3]
    norm_forward(pre_of, rows_ref.shape[0], gain, shift, out_ref, hat_ref, rstd_ref)
    gain_grad, shift_grad, out_bias = norm_backward(
        grad_ref, hat_ref, rstd_ref, gain, rows_out, low_ref
    )
    hidden_grads = feed_backward_steps(
        rows_out,
        low_ref,
        rows_ref,
        up_ref,
        down_ref,
        active_ref,
        slope_ref,
        dup_ref,
        ddown_ref,
        rows_out,
        back_ref,
        outs,
        out_sems,
    )
    small_out[...] = feed_small(out_bias, gain_grad, shift_grad, hidden_grads)
    wait_feed(outs, out_sems)


def shaped(shape, dtype=F32):
    return jax.ShapeDtypeStruct(shape, dtype)


def call(
    kernel, scalars, inputs, others, outs, targets, scratch, flops, moved, limit=VMEM_BYTES
):
    rooms = [pltpu.VMEM(array.shape, array.dtype) for array in list(inputs) + list(outs)]
    return pl.pallas_call(
        functools.partial(
            staged_kernel, kernel, len(scalars), len(inputs), len(others), len(outs), len(targets)
        ),
        out_shape=list(outs) + list(targets),
        in_specs=[SMEM] * len(scalars) + [ANY] * (len(inputs) + len(others)),
        out_specs=[ANY] * (len(outs) + len(targets)),
        scratch_shapes=scratch + rooms + [pltpu.SemaphoreType.DMA((len(rooms),))],
        cost_estimate=pl.CostEstimate(flops=flops, bytes_accessed=moved, transcendentals=0),
        compiler_params=pltpu.CompilerParams(vmem_limit_bytes=limit),
    )(*scalars, *inputs, *others)


def layout_of(parts):
    return [(len(arrays), low, number) for _, arrays, low, number in parts]


def arrays_of(parts):
    return [array for part in parts for array in part[1]]


def most(parts):
    return max(len(part[1]) for part in parts)


def halves(width, number):
    return [shaped((width // BLOCK // 2, number, BLOCK, width), BF)] * 2


def attend_forward(segments, small, base, rows, memory, parts, causal):
    length, width = rows.shape
    cross = memory is not None
    joins = small is None
    scalars = [part[0] for part in parts]
    inputs = list(segments) + ([] if joins else [small]) + [rows] + ([memory] if cross else [])
    outs = [shaped((length, width), BF)] * 4 + [shaped((HEADS, length))]
    outs += [shaped((length, width)), shaped((length, LANES)), shaped((length, width))]
    outs += [shaped((SMALL_ROWS, width))] if joins else []
    scratch = [
        pltpu.VMEM((QUAD, width, width), BF),
        pltpu.VMEM((length, length), F32),
        pltpu.VMEM((2, 2 * length, length), F32),
        pltpu.VMEM((2, 2 * length, length), BF),
        pltpu.VMEM((2, 2 * length, LANES), F32),
        pltpu.VMEM((2, 2 * length, 2 * LANES), F32),
        pltpu.VMEM((length, width), F32),
        pltpu.SemaphoreType.DMA((len(parts) + 1, most(parts))),
    ]
    scratch += [pltpu.VMEM((width // BLOCK, 1, BLOCK, width), BF)] if joins else []
    kernel = functools.partial(attend_forward_kernel, layout_of(parts), cross, causal, base, joins)
    flops = 8 * length * width * width + 16 * length * length * width
    return call(kernel, scalars, inputs, arrays_of(parts), outs, [], scratch, flops, 8_000_000)


def attend_backward(
    out_tables, segments, small, base, grad, kept, rows, memory, parts, causal, others
):
    length, width = rows.shape
    cross = memory is not None
    splits = others is not None
    q, k, v, o, lse, hat, rstd = kept[:7]
    scalars = [part[0] for part in parts] + list(out_tables)
    inputs = list(segments) + [small, grad, hat, rstd, rows]
    inputs += ([memory] if cross else []) + [q, k, v, o, lse] + list(others or ())
    outs = [shaped((length, width))] * (2 if cross else 1)
    outs += [] if splits else [shaped((8, width))]
    targets = halves(width, QUAD + (1 if splits else 0))
    scratch = [
        pltpu.VMEM((QUAD, width, width), BF),
        pltpu.VMEM((QUAD, width, width), BF),
        pltpu.VMEM((length, length), F32),
        pltpu.VMEM((length, width), BF),
        pltpu.VMEM((width, length), F32),
        pltpu.VMEM((length, width), BF),
        pltpu.VMEM((length, width), BF),
        pltpu.VMEM((width, length), BF),
        pltpu.VMEM((length, width), BF),
        pltpu.VMEM((2, 2 * length, length), F32),
        pltpu.VMEM((2, 2 * length, length), F32),
        pltpu.VMEM((2, 2 * length, length), BF),
        pltpu.VMEM((2, 2 * length, length), BF),
        pltpu.SemaphoreType.DMA((3, 2)),
    ]
    scratch += [pltpu.VMEM((width // LANES, 1, BLOCK, width), BF)] if splits else []
    kernel = functools.partial(
        attend_backward_kernel, layout_of(parts), cross, causal, base, splits
    )
    flops = 16 * length * width * width + 40 * length * length * width
    arrays = arrays_of(parts)
    results = list(call(kernel, scalars, inputs, arrays, outs, targets, scratch, flops, 12_000_000))
    rows_grad = results.pop(0)
    memory_grad = results.pop(0) if cross else None
    small_grad = None if splits else results.pop(0)
    return rows_grad, memory_grad, small_grad, results


def feed_scratch(width, grads):
    number = width // BLOCK
    once = [pltpu.VMEM((QUAD, width, width), BF), pltpu.VMEM((number, QUAD, BLOCK, width), BF)]
    return once * (2 if grads else 1)


def feed_forward(small, base, hidden_at, rows, parts):
    length, width = rows.shape
    scalars = [part[0] for part in parts]
    outs = [shaped((length, width)), shaped((length, width)), shaped((length, LANES))]
    outs += [shaped((QUAD, length, width), BF), shaped((QUAD, length, width))]
    scratch = feed_scratch(width, False)
    scratch += [pltpu.VMEM((2, length, width), F32), pltpu.VMEM((length, width), F32)]
    scratch += [pltpu.SemaphoreType.DMA((2, most(parts)))]
    kernel = functools.partial(feed_forward_kernel, layout_of(parts), base, hidden_at)
    flops = 16 * length * width * width
    arrays = arrays_of(parts)
    return call(kernel, scalars, [small, rows], arrays, outs, [], scratch, flops, 10_000_000)


def feed_backward(out_tables, small, base, grad, kept, rows, parts):
    length, width = rows.shape
    hat, rstd, active, slope = kept[1:]
    scalars = [part[0] for part in parts] + list(out_tables)
    inputs = [small, grad, hat, rstd, rows, active, slope]
    outs = [shaped((length, width)), shaped((8, width))]
    targets = halves(width, 2 * QUAD)
    scratch = feed_scratch(width, True)
    scratch += [pltpu.VMEM((length, width), BF), pltpu.VMEM((2, length, width), F32)]
    scratch += [pltpu.SemaphoreType.DMA((2, most(parts))), pltpu.SemaphoreType.DMA((2, 2))]
    kernel = functools.partial(feed_backward_kernel, layout_of(parts), base)
    flops = 32 * length * width * width
    arrays = arrays_of(parts)
    results = call(kernel, scalars, inputs, arrays, outs, targets, scratch, flops, 14_000_000)
    return results[0], results[1], results[2:4]


def feed_both(out_tables, small, base, hidden_at, rows, grad, parts):
    length, width = rows.shape
    scalars = [part[0] for part in parts] + list(out_tables)
    outs = [shaped((length, width)), shaped((length, width)), shaped((8, width))]
    targets = halves(width, 2 * QUAD)
    scratch = feed_scratch(width, True) + [
        pltpu.VMEM((length, width), BF),
        pltpu.VMEM((2, length, width), F32),
        pltpu.VMEM((length, width), F32),
        pltpu.VMEM((QUAD, length, width), BF),
        pltpu.VMEM((QUAD, length, width), F32),
        pltpu.VMEM((length, width), F32),
        pltpu.VMEM((length, LANES), F32),
        pltpu.SemaphoreType.DMA((2, most(parts))),
        pltpu.SemaphoreType.DMA((2, 2)),
    ]
    kernel = functools.partial(feed_both_kernel, layout_of(parts), base, hidden_at)
    flops = 48 * length * width * width
    arrays = arrays_of(parts)
    results = call(kernel, scalars, [small, rows, grad], arrays, outs, targets, scratch, flops, 12_000_000)
    return results[0], results[1], results[2], results[3:5]


def first_kernel(
    at_ref,
    vector_ref,
    hidden_ref,
    square_ref,
    tall_ref,
    deep_ref,
    one_ref,
    two_ref,
    three_ref,
    turn_ref,
    line_ref,
):
    at = at_ref[0]
    width = square_ref.shape[2]
    turn_ref[...] = jnp.zeros_like(turn_ref)
    lanes, rows = vector_ref.shape
    turn_ref[pl.ds(pl.multiple_of(at * lanes, lanes), lanes), :rows] = vector_ref[...]
    upright = turn_ref[...].T
    line_ref[...] = jnp.zeros_like(line_ref)
    layers, lanes = hidden_ref.shape
    per = LANES // lanes
    for layer in range(layers):
        row = jnp.concatenate([hidden_ref[layer : layer + 1]] * per, axis=1)
        lane = lax.broadcasted_iota(jnp.int32, row.shape, 1) // lanes
        row = jnp.where(lane == at % per, row, 0.0)
        line_ref[pl.ds(4 * layer + at // per, 1), :] = row
    columns = [upright[low : low + 8] for low in (0, 8, 16)] + [line_ref[...]]
    block = jnp.concatenate(columns, axis=1)
    small = jnp.concatenate([block, jnp.zeros_like(block)], axis=0)
    tall = []
    deep = []
    for layer in range(2):
        for index in range(QUAD):
            lanes = slice(index * width, (index + 1) * width)
            tall.append(tall_ref[layer, :, lanes])
            deep.append(deep_ref[layer, index * BLOCK : (index + 1) * BLOCK])
    square = [square_ref[index] for index in range(3 * QUAD)]
    cut = QUAD // 2
    groups = [
        square[:cut] + tall[:QUAD] + square[cut:QUAD] + [small] + deep[:QUAD],
        square[QUAD:],
        tall[QUAD:] + deep[QUAD:],
    ]
    for out_ref, group in zip((one_ref, two_ref, three_ref), groups):
        for slot, block in enumerate(group):
            out_ref[0, slot] = block.astype(BF)
        out_ref.put()


def first_arrays(at, square, tall, deep, vectors, hidden):
    width = square.shape[2]
    outs = [
        shaped((1, 3 * QUAD + 1, BLOCK, width), BF),
        shaped((1, 2 * QUAD, BLOCK, width), BF),
        shaped((1, 2 * QUAD, BLOCK, width), BF),
    ]
    scratch = [pltpu.VMEM((LANES, LANES), F32), pltpu.VMEM((8, LANES), F32)]
    inputs = [vectors.T, hidden, square, tall, deep]
    return call(first_kernel, [at], inputs, [], outs, [], scratch, 0, 4_000_000)


def last_kernel(plan, count, at_ref, *refs):
    masters, firsts, seconds = refs[:5], refs[5:10], refs[10:15]
    arrays, refs = refs[15 : 15 + count], refs[15 + count :]
    outs, refs = [refs[5 * kind : 5 * kind + 5] for kind in range(4)], refs[20:]
    buffers, turn_ref, line_ref, sems = refs
    at = at_ref[0]
    starts = []
    for width, pieces, _ in plan:
        for index, low in pieces:
            array = arrays[index]
            array = array if len(array.shape) == 3 else array.at[0]
            source = array.at[low : low + width]
            copy = pltpu.make_async_copy(source, buffers.at[len(starts), :width], sems.at[len(starts)])
            copy.start()
            starts.append(copy)

    def update(slot, where, gradient):
        results = adam_update(
            masters[slot][where],
            gradient,
            firsts[slot][where],
            seconds[slot][where],
            RATES[slot],
            DECAYS[slot],
        )
        for kind in range(4):
            outs[kind][slot][where] = results[kind]

    begin = 0
    left = len(plan)
    for width, pieces, targets in plan:
        for index in range(len(pieces)):
            starts[begin + index].wait()
        for sub, (slot, where) in enumerate(targets):
            gradient = buffers[begin, sub].astype(F32)
            for index in range(1, len(pieces)):
                gradient = gradient + buffers[begin + index, sub].astype(F32)
            if slot < 3:
                update(slot, where, gradient)
                continue
            turn_ref[...] = jnp.zeros_like(turn_ref)
            for column in range(3):
                lanes = slice(column * LANES, (column + 1) * LANES)
                turn_ref[8 * column : 8 * column + 8, :] = gradient[:8, lanes]
            turn_ref[...] = turn_ref[...].T
            lanes, rows = masters[3].shape
            share = turn_ref[pl.ds(pl.multiple_of(at * lanes, lanes), lanes), :][:, :rows]
            update(3, slice(None), share)
            line_ref[...] = gradient[:8, 3 * LANES :]
            layers, lanes = masters[4].shape
            per = LANES // lanes
            for layer in range(layers):
                row = line_ref[pl.ds(4 * layer + at // per, 1), :]
                share = row[:, :lanes]
                for part in range(1, per):
                    other = row[:, part * lanes : (part + 1) * lanes]
                    share = jnp.where(at % per == part, other, share)
                update(4, slice(layer, layer + 1), share)
        begin += len(pieces)
        left -= 1
        for slot in range(5):
            ends = [at for at, (_, _, each) in enumerate(plan) if any(to[0] in used(slot) for to in each)]
            if ends[-1] == len(plan) - 1 - left:
                for kind in range(4):
                    outs[kind][slot].put()


def used(slot):
    return (3,) if slot > 2 else (slot,)


def last_update(at, segments, masters, firsts, seconds):
    arrays = []
    plan = []
    for width, pieces, targets in segments:
        entry = []
        for array, low in pieces:
            found = [place for place, other in enumerate(arrays) if other is array]
            if not found:
                arrays.append(array)
            entry.append((found[0] if found else len(arrays) - 1, low))
        plan.append((width, entry, targets))
    params = [list(group) for group in (masters, firsts, seconds)]
    for group in params:
        group[3] = group[3].T
    flat = params[0] + params[1] + params[2]
    outs = [shaped(array.shape) for array in params[0]] * 3
    outs += [shaped(array.shape, BF) for array in params[0]]
    pieces = sum(len(entry[1]) for entry in plan)
    block = masters[0].shape[1:]
    scratch = [
        pltpu.VMEM((pieces, max(entry[0] for entry in plan)) + block, BF),
        pltpu.VMEM((LANES, LANES), F32),
        pltpu.VMEM((8, LANES), F32),
        pltpu.SemaphoreType.DMA((pieces,)),
    ]
    kernel = functools.partial(last_kernel, plan, len(arrays))
    results = call(
        kernel, [at], flat, arrays, outs, [], scratch, 0, 8_000_000, VMEM_BYTES // 2
    )
    results = list(results)
    for kind in range(4):
        results[5 * kind + 3] = results[5 * kind + 3].T
    return results


def tie(*arrays):
    return lax.optimization_barrier(arrays)


class Direct:
    def __init__(self, axis_sizes):
        outer, inner = axis_sizes
        self.count = outer * inner
        inner_bits = inner.bit_length() - 1
        bits = self.count.bit_length() - 1
        core = [inner_bits]
        across = list(range(inner_bits + 1, bits))
        up = [0]
        along = list(range(1, inner_bits))
        self.orders = {
            "a": core + across + up + along,
            "b": core + up + across + along,
            "c": core + along + across + up,
            "d": core + along + up + across,
        }
        self.place = lax.axis_index(AXES)

    def hop(self, array, bit):
        return lax.ppermute(array, AXES, [(at, at ^ (1 << bit)) for at in range(self.count)])

    def table(self, name):
        order = self.orders[name]
        index = jnp.arange(self.count, dtype=jnp.int32)
        block = jnp.zeros_like(index)
        for at, bit in enumerate(order):
            block = block | (((index >> (len(order) - 1 - at)) & 1) << bit)
        return block ^ self.place

    def arrive(self, array, name, step):
        return self.hop(array, self.orders[name][::-1][step])

    def finish(self, array, name):
        return [array, self.hop(array, self.orders[name][0])]


def grown(arrays, arrivals):
    return [jnp.concatenate(pair, axis=0) for pair in zip(arrays, arrivals)]


class Sum:
    def __init__(self, net, name, segments, done, blocks):
        self.net = net
        self.name = name
        self.segments = segments
        self.done = done
        self.blocks = blocks

    def bit(self):
        return self.net.orders[self.name][self.done]

    def split(self, names):
        return [
            Sum(self.net, name, [segment], self.done, self.blocks)
            for name, segment in zip(names, self.segments)
        ]


def core_hop(net, pair, widths):
    keep, send = pair
    arrived = net.hop(send, net.orders["a"][0])
    low = 0
    segments = []
    for width in widths:
        segments.append((width, [(keep, low), (arrived, low)]))
        low += width
    return Sum(net, "a", segments, 1, keep.shape[0])


def combine_kernel(plan, count, outputs, *refs):
    arrays, refs = refs[:count], refs[count:]
    outs, buffers, sems = refs[:outputs], refs[outputs:-1], refs[-1]
    starts = []
    for _, _, held, number, width, pieces in plan:
        begin = 0 if held is not None else number
        for index, low in pieces:
            array = arrays[index]
            if len(array.shape) == 3:
                source = array.at[low + begin * width : low + 2 * number * width]
            else:
                source = array.at[begin : 2 * number, low : low + width]
            copy = pltpu.make_async_copy(source, buffers[len(starts)], sems.at[len(starts)])
            copy.start()
            starts.append(copy)
    begin = 0
    for slot, first, held, number, width, pieces in plan:
        for index in range(begin, begin + len(pieces)):
            starts[index].wait()
        mine = buffers[begin : begin + len(pieces)]
        jobs = [(slot, first, 0)] if held is None else [(slot, first, number), (outputs - 1, held, 0)]
        for out, place, skip in jobs:

            def body(block, carry, out=out, place=place, skip=skip, width=width, mine=mine):
                value = None
                for buffer in mine:
                    flat = len(buffer.shape) == 3
                    at = block + skip
                    part = buffer[pl.ds(at * width, width)] if flat else buffer[at]
                    value = part.astype(F32) if value is None else value + part.astype(F32)
                outs[out][pl.ds(place + block * width, width)] = value.astype(BF)
                return carry

            lax.fori_loop(0, number, body, 0)
        begin += len(pieces)


class Round:
    def __init__(self, sums, *tokens, limit=VMEM_BYTES // 3):
        self.net = sums[0].net
        self.sums = sums
        self.bits = sorted({item.bit() for item in sums})
        arrays = []
        plan = []
        sizes = [0] * len(self.bits) + [0]
        self.places = []
        block = None
        for item in sums:
            slot = self.bits.index(item.bit())
            number = item.blocks // 2
            holds = item.done > 1
            places = []
            for width, pieces in item.segments:
                entry = []
                for array, low in pieces:
                    found = [at for at, other in enumerate(arrays) if other is array]
                    if not found:
                        arrays.append(array)
                    entry.append((found[0] if found else len(arrays) - 1, low))
                    block = array.shape[-2:]
                held = sizes[-1] if holds else None
                plan.append((slot, sizes[slot], held, number, width, entry))
                places.append((sizes[slot], held))
                sizes[slot] += number * width
                sizes[-1] += number * width if holds else 0
            self.places.append((slot, places))
        tied = list(tie(*arrays, *tokens))[: len(arrays)] if tokens else arrays
        scratch = []
        moved = 0
        for _, _, held, number, width, entry in plan:
            both = number if held is None else 2 * number
            moved += both * width * (len(entry) + 1) * 16384
            for index, _ in entry:
                flat = len(arrays[index].shape) == 3
                shape = (both * width,) if flat else (both, width)
                scratch.append(pltpu.VMEM(shape + block, BF))
        if not sizes[-1]:
            sizes.pop()
        self.sends = pl.pallas_call(
            functools.partial(combine_kernel, plan, len(tied), len(sizes)),
            out_shape=[shaped((size,) + block, BF) for size in sizes],
            in_specs=[ANY] * len(tied),
            out_specs=[VMEM] * len(sizes),
            scratch_shapes=scratch + [pltpu.SemaphoreType.DMA((len(scratch),))],
            cost_estimate=pl.CostEstimate(flops=0, bytes_accessed=moved, transcendentals=0),
            compiler_params=pltpu.CompilerParams(vmem_limit_bytes=limit),
        )(*tied)

    def before(self, *arrays):
        tied = tie(*arrays, *self.sends)
        self.sends = list(tied[len(arrays) :])
        return tied[: len(arrays)]

    def go(self):
        arrived = [self.net.hop(send, bit) for send, bit in zip(self.sends, self.bits)]
        for item, (slot, places) in zip(self.sums, self.places):
            made = []
            for (width, pieces), (place, held) in zip(item.segments, places):
                stay = pieces if held is None else [(self.sends[-1], held)]
                made.append((width, stay + [(arrived[slot], place)]))
            item.segments = made
            item.done += 1
            item.blocks //= 2
        return arrived


def adam_update(weight, gradient, first, second, rate, decay):
    first_new = BETA_ONE * first + (1.0 - BETA_ONE) * gradient
    second_new = BETA_TWO * second + (1.0 - BETA_TWO) * gradient * gradient
    first_hat = first_new / (1.0 - BETA_ONE**STEP)
    second_hat = second_new / (1.0 - BETA_TWO**STEP)
    weight_new = weight - rate * (first_hat / (jnp.sqrt(second_hat) + EPS_ADAM) + decay * weight)
    return (weight_new, first_new, second_new, weight_new.astype(BF))


def gather_small(vectors, hidden):
    whole = lax.all_gather(vectors.astype(BF), AXES, axis=1, tiled=True)
    deep = lax.all_gather(hidden.astype(BF), AXES, axis=1, tiled=True)
    whole = jnp.pad(whole, ((0, HIDDEN_ROW - whole.shape[0]), (0, 0)))
    return jnp.concatenate([whole, deep.reshape(-1, whole.shape[1])], axis=0).astype(F32)


def scatter_small(grads, vectors, hidden, place, count):
    whole = lax.psum(small_rows(*grads), AXES)
    rows, lanes = vectors.shape
    first = lax.dynamic_slice_in_dim(whole[:rows], place * lanes, lanes, axis=1)
    layers, lanes = hidden.shape
    deep = whole[HIDDEN_ROW:].reshape(layers, -1)
    return first, lax.dynamic_slice_in_dim(deep, place * lanes, lanes, axis=1)


def gather_whole(attention, up, down):
    width = attention.shape[2]
    number = width // BLOCK
    square = lax.all_gather(attention, AXES, axis=1, tiled=True)
    square = square.reshape(-1, QUAD, number, BLOCK, width).transpose(0, 2, 1, 3, 4)
    tall = lax.all_gather(up, AXES, axis=1, tiled=True)
    tall = tall.reshape(2, number, BLOCK, QUAD, width).transpose(0, 1, 3, 2, 4)
    deep = lax.all_gather(down, AXES, axis=1, tiled=True).reshape(2, number, QUAD, BLOCK, width)
    half = number // 2
    quads = [square[0], tall[0], deep[0], square[1], square[2], tall[1], deep[1]]
    return [(quad[:half], quad[half:]) for quad in quads]


def scatter_whole(quads):
    joined = [jnp.concatenate(pair, axis=0).astype(F32) for pair in quads]
    number, _, _, width = joined[0].shape
    square = jnp.stack([joined[0], joined[3], joined[4]])
    square = square.transpose(0, 2, 1, 3, 4).reshape(3 * QUAD, width, width)
    tall = jnp.stack([joined[1], joined[5]]).transpose(0, 1, 3, 2, 4)
    tall = tall.reshape(2, width, QUAD * width)
    deep = jnp.stack([joined[2], joined[6]]).reshape(2, QUAD * width, width)
    return [
        lax.psum_scatter(part, AXES, scatter_dimension=1, tiled=True)
        for part in (square, tall, deep)
    ]


def direct_step(pairs, source, target, grad, masters, firsts, seconds, axis_sizes):
    net = Direct(axis_sizes)
    source_pair, target_pair, cross_pair = pairs
    a, b = net.table("a"), net.table("b")
    cut = QUAD // 2
    at = (net.place % (net.count * LANES // source.shape[1])).astype(jnp.int32).reshape(1)

    one, two, three = first_arrays(at, *masters)
    up_two, down_two = three[:, :QUAD], three[:, QUAD:]
    for step in (0, 1):
        more = tie(
            net.arrive(one, "a", step),
            net.arrive(up_two, "c", step),
            net.arrive(down_two, "d", step),
        )
        one, up_two, down_two = grown((one, up_two, down_two), more)
    three = jnp.concatenate([up_two, down_two], axis=1)
    left, right = one[:, : cut + QUAD], one[:, cut + QUAD :]
    two, three, left, right = tie(two, three, left, right)
    left, right, two = grown(
        (left, right, two),
        tie(net.arrive(left, "a", 2), net.arrive(right, "b", 2), net.arrive(two, "a", 0)),
    )
    left, right, two, three = grown(
        (left, right, two, three),
        tie(
            net.arrive(left, "a", 3),
            net.arrive(right, "b", 3),
            net.arrive(two, "a", 1),
            net.arrive(three, "c", 2),
        ),
    )
    self_w, cross_w = two[:, :QUAD], two[:, QUAD:]
    more = tie(
        net.hop(left, net.orders["a"][0]),
        net.hop(right, net.orders["b"][0]),
        net.arrive(self_w, "a", 2),
        net.arrive(cross_w, "b", 2),
    )
    left, right = [left, more[0]], [right, more[1]]
    self_w, cross_w = grown((self_w, cross_w), more[2:])
    source, self_w, cross_w, three = tie(source, self_w, cross_w, three)
    more = [
        net.arrive(self_w, "a", 3),
        net.arrive(cross_w, "b", 3),
        net.arrive(three, "c", 3),
    ]
    enc_attend_w = [(a, left, 0, cut), (b, right, 0, cut)]
    enc_feed_w = [(a, left, cut, QUAD), (b, right, cut + 1, QUAD)]
    enc_kept = attend_forward(source_pair, None, 0, source, None, enc_attend_w, False)
    enc_mid, small = enc_kept[7], enc_kept[8]
    enc_feed_kept = feed_forward(small, 5, HIDDEN_ROW, enc_mid, enc_feed_w)
    memory = enc_feed_kept[0]
    self_w, cross_w = grown((self_w, cross_w), tie(*more[:2], memory)[:2])
    (three,) = grown([three], tie(more[2], self_w, cross_w)[:1])
    target, self_w, cross_w, three = tie(target, self_w, cross_w, three)
    self_w, cross_w = net.finish(self_w, "a"), net.finish(cross_w, "b")
    three, self_w[1] = tie(three, self_w[1])
    three = net.finish(three, "c")
    self_w = [(a, self_w, 0, QUAD)]
    cross_w = [(b, cross_w, 0, QUAD)]
    self_kept = attend_forward(target_pair, small, 8, target, None, self_w, True)
    dec_one = self_kept[7]
    cross_kept = attend_forward(cross_pair, small, 13, dec_one, memory, cross_w, False)
    dec_two = cross_kept[7]
    dec_feed_w = [(net.table("c"), three, 0, QUAD), (net.table("d"), three, QUAD, QUAD)]
    result, two_grad, dec_feed_small, feed_two = feed_both(
        (a, b), small, 18, HIDDEN_ROW + QUAD, dec_two, grad, dec_feed_w
    )

    names = ("a", "b")
    feed_two = core_hop(net, feed_two, (QUAD, QUAD)).split(names)
    one_grad, memory_grad, cross_small, cross_q = attend_backward(
        (a, b), cross_pair, small, 13, two_grad, cross_kept, dec_one, memory, cross_w, False, None
    )
    send = Round(feed_two, cross_small)
    memory_grad, *cross_q = send.before(memory_grad, *cross_q)
    send.go()
    cross_s = core_hop(net, cross_q, (cut, cut)).split(names)
    mid_grad, enc_feed_small, feed_one = feed_backward(
        (a, b), small, 5, memory_grad, enc_feed_kept, enc_mid, enc_feed_w
    )
    send = Round(feed_two + cross_s, enc_feed_small)
    one_grad, *feed_one = send.before(one_grad, *feed_one)
    send.go()
    feed_one = core_hop(net, feed_one, (QUAD, QUAD)).split(names)
    target_grad, _, self_small, self_q = attend_backward(
        (a, b), target_pair, small, 8, one_grad, self_kept, target, None, self_w, True, None
    )
    send = Round(feed_two + cross_s + feed_one, self_small)
    mid_grad, *self_q = send.before(mid_grad, *self_q)
    send.go()
    self_s = core_hop(net, self_q, (cut, cut)).split(names)
    others = (enc_feed_small, self_small, cross_small, dec_feed_small)
    source_grad, _, _, enc_q = attend_backward(
        (a, b), source_pair, small, 0, mid_grad, enc_kept, source, None, enc_attend_w, False, others
    )
    send = Round(feed_two + cross_s + feed_one + self_s, source_grad)
    enc_q = send.before(*enc_q)
    last = send.go()
    enc_s = core_hop(net, enc_q, (cut, cut + 1)).split(names)
    while enc_s[0].blocks > 1:
        send = Round([item for item in cross_s + feed_one + self_s + enc_s if item.blocks > 1], *last)
        last = send.go()

    square = [(0, index) for index in range(3 * QUAD)]
    tall, deep = [], []
    for layer in range(2):
        for index in range(QUAD):
            lanes = slice(index * source.shape[1], (index + 1) * source.shape[1])
            tall.append((1, (layer, slice(None), lanes)))
            deep.append((2, (layer, slice(index * BLOCK, (index + 1) * BLOCK))))
    targets = [square[:cut], square[cut:QUAD] + [(3, None)]]
    targets += [square[QUAD : QUAD + cut], square[QUAD + cut : 2 * QUAD], tall[:QUAD], deep[:QUAD]]
    targets += [tall[QUAD:], deep[QUAD:]]
    targets += [square[2 * QUAD : 2 * QUAD + cut], square[2 * QUAD + cut :]]
    segments = [item.segments[0] for item in enc_s + self_s + feed_one + feed_two + cross_s]
    segments = [segment + (target,) for segment, target in zip(segments, targets)]
    updated = last_update(at, segments, masters, firsts, seconds)
    return (memory, result, source_grad, target_grad), updated


def whole_step(pairs, source, target, grad, masters, firsts, seconds, axis_sizes):
    attention, up, down = [master.astype(BF) for master in masters[:3]]
    vectors, hidden = masters[3:]
    source_pair, target_pair, cross_pair = pairs
    small = gather_small(vectors, hidden)
    quads = gather_whole(attention, up, down)
    table = jnp.arange(source.shape[1] // BLOCK, dtype=jnp.int32)
    two = (table, table)
    parts = [(table, list(quad), 0, QUAD) for quad in quads]
    enc_kept = attend_forward(source_pair, small, 0, source, None, parts[:1], False)
    enc_mid = enc_kept[7]
    enc_feed_kept = feed_forward(small, 5, HIDDEN_ROW, enc_mid, parts[1:3])
    memory = enc_feed_kept[0]
    self_kept = attend_forward(target_pair, small, 8, target, None, parts[3:4], True)
    dec_one = self_kept[7]
    cross_kept = attend_forward(cross_pair, small, 13, dec_one, memory, parts[4:5], False)
    dec_two = cross_kept[7]
    result, two_grad, dec_feed_small, feed_two = feed_both(
        two, small, 18, HIDDEN_ROW + QUAD, dec_two, grad, parts[5:7]
    )
    one_grad, memory_grad, cross_small, cross_q = attend_backward(
        two, cross_pair, small, 13, two_grad, cross_kept, dec_one, memory, parts[4:5], False, None
    )
    target_grad, _, self_small, self_q = attend_backward(
        two, target_pair, small, 8, one_grad, self_kept, target, None, parts[3:4], True, None
    )
    mid_grad, enc_feed_small, feed_one = feed_backward(
        two, small, 5, memory_grad, enc_feed_kept, enc_mid, parts[1:3]
    )
    source_grad, _, enc_small, enc_q = attend_backward(
        two, source_pair, small, 0, mid_grad, enc_kept, source, None, parts[:1], False, None
    )
    quads = [enc_q]
    quads += [[half[:, low : low + QUAD] for half in feed_one] for low in (0, QUAD)]
    quads += [self_q, cross_q]
    quads += [[half[:, low : low + QUAD] for half in feed_two] for low in (0, QUAD)]
    smalls = (enc_small, enc_feed_small, self_small, cross_small, dec_feed_small)
    count = axis_sizes[0] * axis_sizes[1]
    shares = scatter_small(smalls, vectors, hidden, lax.axis_index(AXES), count)
    grads = tuple(scatter_whole(quads)) + shares
    updated = [
        adam_update(
            masters[slot], grads[slot], firsts[slot], seconds[slot], RATES[slot], DECAYS[slot]
        )
        for slot in range(5)
    ]
    flat = [updated[slot][kind] for kind in range(4) for slot in range(5)]
    return (memory, result, source_grad, target_grad), flat


def per_device(
    axis_sizes,
    source_tokens,
    target_tokens,
    source_segments,
    target_segments,
    output_grad,
    attention_weight,
    up_weight,
    down_weight,
    vectors,
    hidden_bias,
    *moments,
):
    masters = (attention_weight, up_weight, down_weight, vectors, hidden_bias)
    firsts = moments[:5]
    seconds = moments[5:]
    width = source_tokens.shape[2]
    pairs = (
        (source_segments, source_segments),
        (target_segments, target_segments),
        (target_segments, source_segments),
    )
    direct = axis_sizes[0] * axis_sizes[1] * BLOCK == width
    tokens, updated = (direct_step if direct else whole_step)(
        pairs,
        source_tokens[0],
        target_tokens[0],
        output_grad[0],
        masters,
        firsts,
        seconds,
        axis_sizes,
    )
    return tuple(array[None] for array in tokens) + tuple(updated)


def solution(mesh):
    rows = P(AXES, None, None)
    line = P(AXES, None)
    matrix = P(None, AXES, None)
    vector = P(None, AXES)
    state = (matrix, matrix, matrix, vector, vector)
    return jax.shard_map(
        functools.partial(per_device, (mesh.shape["dp"], mesh.shape["fsdp"])),
        mesh=mesh,
        in_specs=(rows, rows, line, line, rows) + state * 3,
        out_specs=(rows,) * 4 + state * 4,
        check_vma=False,
    )
```

```python
import functools

import jax
import jax.numpy as jnp
from jax import lax
from jax.experimental import pallas as pl
from jax.experimental.pallas import tpu as pltpu
from jax.sharding import PartitionSpec as P

HEADS = 8
STEP = 10
EPS_NORM = 1e-05
EPS_ADAM = 1e-08
BETA_ONE = 0.9
BETA_TWO = 0.999
LOWEST = -1e30
RATES = (0.05, 0.05, 0.05, 0.3, 0.3)
DECAYS = (0.01, 0.01, 0.01, 0.0, 0.0)
AXES = ("dp", "fsdp")
QUAD = 4
BLOCK = 16
CHUNK = 64
LANES = 128
SMALL_ROWS = 32
VMEM_BYTES = 60 * 1024 * 1024
HIDDEN_ROW = 24
BF = jnp.bfloat16
F32 = jnp.float32
VMEM = pl.BlockSpec(memory_space=pltpu.VMEM)
SMEM = pl.BlockSpec(memory_space=pltpu.SMEM)
ANY = pl.BlockSpec(memory_space=pl.ANY)
ROOT_TWO_PI = 0.7978845608028654
CUBIC = 0.044715


def dot(left, right):
    return jnp.dot(left, right, preferred_element_type=F32)


def dot_nt(left, right):
    return lax.dot_general(left, right, (((1,), (1,)), ((), ())), preferred_element_type=F32)


class Input:
    def __init__(self, array, room, sem):
        self.room = room
        self.shape = room.shape
        self.copy = pltpu.make_async_copy(array, room, sem)
        self.copy.start()
        self.there = False

    def __getitem__(self, where):
        if not self.there:
            self.copy.wait()
            self.there = True
        return self.room[where]


class Output:
    def __init__(self, array, room, sem):
        self.array = array
        self.room = room
        self.shape = room.shape
        self.sem = sem
        self.left = False

    def __getitem__(self, where):
        return self.room[where]

    def __setitem__(self, where, value):
        self.room[where] = value

    def put(self, index=None):
        source = self.room if index is None else self.room.at[index]
        target = self.array if index is None else self.array.at[index]
        pltpu.make_async_copy(source, target, self.sem).start()
        self.left = True

    def finish(self):
        if not self.left:
            self.put()
        pltpu.make_async_copy(self.room, self.array, self.sem).wait()


def staged_kernel(kernel, scalars, inputs, others, outputs, targets, *refs):
    refs = list(refs)
    sems = refs.pop()
    count = inputs + outputs
    rooms = refs[len(refs) - count :]
    refs = refs[: len(refs) - count]
    at = scalars
    for slot in range(inputs):
        refs[at + slot] = Input(refs[at + slot], rooms[slot], sems.at[slot])
    at += inputs + others
    made = []
    for slot in range(inputs, count):
        place = at + slot - inputs
        refs[place] = Output(refs[place], rooms[slot], sems.at[slot])
        made.append(refs[place])
    kernel(*refs)
    for output in made:
        output.finish()


def load_start(part, place, sems):
    table, arrays, low, number = part
    at = 0
    for slot, array in enumerate(arrays):
        for index in range(array.shape[0]):
            source = array.at[index, low : low + number]
            pltpu.make_async_copy(source, place(table[at]), sems.at[slot]).start()
            at += 1


def load_wait(part, sems):
    table, arrays, low, number = part
    for slot, array in enumerate(arrays):
        whole = array.at[:, low : low + number]
        pltpu.make_async_copy(whole, whole, sems.at[slot]).wait()


def store_start(part, place, sems):
    table, arrays, low, number = part
    half = arrays[0].shape[0]
    for index in range(half):
        for slot in (1, 0):
            target = arrays[slot].at[index, low : low + number]
            source = place(table[slot * half + index])
            pltpu.make_async_copy(source, target, sems.at[slot]).start()


def row_place(scratch, low, high):
    def place(block):
        start = pl.multiple_of(block * BLOCK, BLOCK)
        return scratch.at[low:high, pl.ds(start, BLOCK), :]

    return place


def block_place(scratch):
    return lambda block: scratch.at[block]


def column_sum(values):
    rows, width = values.shape
    return jnp.sum(values.reshape(rows // 8, 8, width), axis=0)


def total_of(sums):
    return jnp.sum(functools.reduce(jnp.add, sums), axis=0, keepdims=True)


def norm_forward(pre_of, length, gain, shift, out_ref, hat_ref, rstd_ref):
    for at in range(0, length, CHUNK):
        rows = slice(at, at + CHUNK)
        pre = pre_of(rows)
        mean = jnp.mean(pre, axis=-1, keepdims=True)
        centred = pre - mean
        spread = jnp.mean(centred * centred, axis=-1, keepdims=True)
        rstd = lax.rsqrt(spread + EPS_NORM)
        hat = centred * rstd
        hat_ref[rows] = hat
        rstd_ref[rows] = jnp.broadcast_to(rstd, (CHUNK, LANES))
        out_ref[rows] = hat * gain + shift
    for ref in (hat_ref, rstd_ref, out_ref):
        if isinstance(ref, Output):
            ref.put()


def norm_backward(grad_ref, hat_ref, rstd_ref, gain, pre_out, low_out):
    length = grad_ref.shape[0]
    sums = ([], [], [])
    for at in range(0, length, CHUNK):
        rows = slice(at, at + CHUNK)
        grad = grad_ref[rows].astype(F32)
        hat = hat_ref[rows]
        sums[0].append(column_sum(grad * hat))
        sums[1].append(column_sum(grad))
        scaled = grad * gain
        one = jnp.mean(scaled, axis=-1, keepdims=True)
        two = jnp.mean(scaled * hat, axis=-1, keepdims=True)
        pre = rstd_ref[rows][:, :1] * (scaled - one - hat * two)
        low = pre.astype(BF)
        pre_out[rows] = pre
        low_out[rows] = low
        sums[2].append(column_sum(low.astype(F32)))
    return [total_of(each) for each in sums]


def lane_mask(rows):
    return lax.broadcasted_iota(jnp.int32, (rows, LANES), 1) < LANES // 2


def stacked_pair(block):
    first = lane_mask(block.shape[0])
    zero = jnp.zeros_like(block)
    return jnp.concatenate([jnp.where(first, block, zero), jnp.where(first, zero, block)], axis=0)


def merged_pair(stacked):
    rows = stacked.shape[0] // 2
    return jnp.where(lane_mask(rows), stacked[:rows], stacked[rows:])


def mask_fill(bias_ref, column_seg, row_seg, causal, transposed):
    length = bias_ref.shape[0]
    column = jnp.broadcast_to(column_seg, (LANES, length)).T
    for at in range(0, length, LANES):
        same = column == row_seg[:, at : at + LANES]
        if causal:
            down = lax.broadcasted_iota(jnp.int32, (length, LANES), 0)
            along = lax.broadcasted_iota(jnp.int32, (length, LANES), 1) + at
            order = (down <= along) if transposed else (along <= down)
            same = same & order
        bias_ref[:, at : at + LANES] = jnp.where(same, 0.0, LOWEST)


def take_parts(refs, layout, tables):
    parts = []
    for slot, (arrays, low, number) in enumerate(layout):
        parts.append((tables[slot], [refs.pop(0) for _ in range(arrays)], low, number))
    return parts


def small_part(part):
    table, arrays, low, number = part
    return table, arrays, low + number, 1


def small_join(blocks_ref):
    count = blocks_ref.shape[0]
    groups = blocks_ref.shape[3] // LANES
    per = count // groups
    vectors = []
    hidden = [[], []]
    for group in range(groups):
        total = blocks_ref[group * per, 0, :8].astype(F32)
        for at in range(group * per + 1, (group + 1) * per):
            total = total + blocks_ref[at, 0, :8].astype(F32)
        columns = [total[:, at : at + LANES] for at in range(0, 4 * LANES, LANES)]
        vectors.append(jnp.concatenate(columns[:3], axis=0))
        for layer in range(2):
            rows = [columns[3][4 * layer + at : 4 * layer + at + 1] for at in range(4)]
            hidden[layer].append(jnp.concatenate(rows, axis=1))
    return jnp.concatenate([jnp.concatenate(vectors, axis=1)] + hidden[0] + hidden[1], axis=0)


def small_split(whole, group):
    lanes = slice(group * LANES, (group + 1) * LANES)
    columns = [whole[at : at + 8, lanes] for at in (0, 8, 16)]
    rows = []
    for layer in range(2):
        row = whole[24 + 4 * layer + group : 25 + 4 * layer + group]
        rows += [row[:, at : at + LANES] for at in range(0, 4 * LANES, LANES)]
    columns.append(jnp.concatenate(rows, axis=0))
    block = jnp.concatenate(columns, axis=1)
    return jnp.concatenate([block, jnp.zeros_like(block)], axis=0).astype(BF)


def attend_forward_kernel(layout, cross, causal, base, joins, *refs):
    refs = list(refs)
    tables = [refs.pop(0) for _ in layout]
    query_seg = refs.pop(0)
    key_seg = refs.pop(0)
    small = None if joins else refs.pop(0)
    rows_ref = refs.pop(0)
    memory_ref = refs.pop(0) if cross else None
    parts = take_parts(refs, layout, tables)
    q_ref, k_ref, v_ref, o_ref, lse_ref, hat_ref, rstd_ref, out_ref = [refs.pop(0) for _ in range(8)]
    if joins:
        small = refs.pop(0)
        blocks_ref = refs.pop()
        extra = small_part(parts[-1])
    w_ref, bias_ref, scores_ref, exponent_ref, largest_ref, mixed_ref, attended_ref, sems = refs
    first = 0
    if joins:
        load_start(extra, lambda block: blocks_ref.at[block], sems.at[len(parts)])
    for slot, part in enumerate(parts):
        load_start(part, row_place(w_ref, first, first + part[3]), sems.at[slot])
        first += part[3]
    length, width = rows_ref.shape
    mask_fill(bias_ref, query_seg[...], key_seg[...], causal, False)
    rows = rows_ref[...].astype(BF)
    keys = memory_ref[...].astype(BF) if cross else rows
    if joins:
        load_wait(extra, sems.at[len(parts)])
        small[...] = small_join(blocks_ref)
        small.put()
    for slot, part in enumerate(parts):
        load_wait(part, sems.at[slot])
    scale = (width // HEADS) ** (-0.5)
    q_ref[...] = (dot(rows, w_ref[0]) + small[base : base + 1]).astype(BF) * jnp.asarray(scale, BF)
    k_ref[...] = dot(keys, w_ref[1]).astype(BF)
    v_ref[...] = (dot(keys, w_ref[2]) + small[base + 1 : base + 2]).astype(BF)
    for ref in (q_ref, k_ref, v_ref):
        ref.put()
    lane = lax.broadcasted_iota(jnp.int32, (LANES, LANES), 1)
    logs = [jnp.zeros((LANES, LANES), F32)] * (length // LANES)
    for pair in range(HEADS // 2):
        lanes = slice(pair * LANES, (pair + 1) * LANES)
        side = pair % 2
        scores_ref[side] = dot_nt(stacked_pair(q_ref[:, lanes]), k_ref[:, lanes])
        for at in range(0, 2 * length, CHUNK):
            chunk = slice(at, at + CHUNK)
            own = slice(at % length, at % length + CHUNK)
            reach = own.start // LANES * LANES + LANES if causal else length
            scores = scores_ref[side, chunk, :reach] + bias_ref[own, :reach]
            largest = jnp.max(scores, axis=-1, keepdims=True)
            exponent_ref[side, chunk, :reach] = jnp.exp(scores - largest).astype(BF)
            if reach < length:
                exponent_ref[side, chunk, reach:] = jnp.zeros((CHUNK, length - reach), BF)
            largest_ref[side, chunk] = jnp.broadcast_to(largest, (CHUNK, LANES))
        values = jnp.concatenate([v_ref[:, lanes], jnp.ones((length, LANES), BF)], axis=1)
        mixed_ref[side] = dot(exponent_ref[side], values)
        for slot, at in enumerate(range(0, length, LANES)):
            outs = []
            for half in range(2):
                chunk = slice(half * length + at, half * length + at + LANES)
                total = mixed_ref[side, chunk, LANES:]
                outs.append(mixed_ref[side, chunk, :LANES] / total)
                log_total = largest_ref[side, chunk] + jnp.log(total)
                logs[slot] = jnp.where(lane == 2 * pair + half, log_total, logs[slot])
            o_ref[at : at + LANES, lanes] = jnp.where(lane_mask(LANES), outs[0], outs[1]).astype(BF)
    for slot, at in enumerate(range(0, length, LANES)):
        lse_ref[:, at : at + LANES] = logs[slot].T[:HEADS]
    o_ref.put()
    lse_ref.put()
    attended_ref[...] = dot(o_ref[...], w_ref[3])
    out_bias = small[base + 2 : base + 3]
    norm_forward(
        lambda rows: rows_ref[rows].astype(F32) + (attended_ref[rows] + out_bias),
        length,
        small[base + 3 : base + 4],
        small[base + 4 : base + 5],
        out_ref,
        hat_ref,
        rstd_ref,
    )


def attend_backward_kernel(layout, cross, causal, base, splits, *refs):
    refs = list(refs)
    tables = [refs.pop(0) for _ in layout]
    out_tables = [refs.pop(0), refs.pop(0)]
    query_seg = refs.pop(0)
    key_seg = refs.pop(0)
    small = refs.pop(0)
    grad_ref = refs.pop(0)
    hat_ref, rstd_ref = refs.pop(0), refs.pop(0)
    rows_ref = refs.pop(0)
    memory_ref = refs.pop(0) if cross else None
    q_ref, k_ref, v_ref, o_ref, lse_ref = [refs.pop(0) for _ in range(5)]
    others = [refs.pop(0) for _ in range(4)] if splits else None
    parts = take_parts(refs, layout, tables)
    rows_out = refs.pop(0)
    memory_out = refs.pop(0) if cross else None
    small_out = None if splits else refs.pop(0)
    targets = [refs.pop(0), refs.pop(0)]
    outs = []
    for slot, table in enumerate(out_tables):
        outs.append((table, targets, slot * QUAD // 2, QUAD // 2))
    blocks_ref = refs.pop() if splits else None
    w_ref, dw_ref, bias_ref, dout_ref, dq_t_ref, dk_ref, dv_ref, kt_ref = refs[:8]
    low_ref, scores_ref, prob_grad_ref, prob_ref, score_grad_ref, sems = refs[8:]
    first = 0
    for slot, part in enumerate(parts):
        load_start(part, row_place(w_ref, first, first + part[3]), sems.at[slot])
        first += part[3]
    length, width = rows_ref.shape
    head = width // HEADS
    scale = head ** (-0.5)
    gain_grad, shift_grad, out_bias = norm_backward(
        grad_ref, hat_ref, rstd_ref, small[base + 3 : base + 4], rows_out, low_ref
    )
    mask_fill(bias_ref, key_seg[...], query_seg[...], causal, True)
    low = low_ref[...]
    for slot, part in enumerate(parts):
        load_wait(part, sems.at[slot])
    dout_ref[...] = dot_nt(low, w_ref[3]).astype(BF)
    dw_ref[3] = dot(o_ref[...].T, low).astype(BF)
    product = dout_ref[...].astype(F32) * o_ref[...].astype(F32)
    high = product.astype(BF)
    rest = (product - high.astype(F32)).astype(BF)
    picker = lax.broadcasted_iota(jnp.int32, (BLOCK, width), 1) // head
    picker = (picker == lax.broadcasted_iota(jnp.int32, (BLOCK, width), 0)).astype(BF)
    row_dots = dot_nt(picker, high) + dot_nt(picker, rest)
    kt_ref[...] = k_ref[...].T
    for pair in range(HEADS // 2):
        lanes = slice(pair * LANES, (pair + 1) * LANES)
        side = pair % 2
        query = q_ref[:, lanes]
        dout = dout_ref[:, lanes]
        scores_ref[side] = dot_nt(stacked_pair(k_ref[:, lanes]), query)
        prob_grad_ref[side] = dot_nt(stacked_pair(v_ref[:, lanes]), dout)
        for at in range(0, 2 * length, CHUNK):
            which = 2 * pair + at // length
            chunk = slice(at, at + CHUNK)
            own = slice(at % length, at % length + CHUNK)
            begin = own.start // LANES * LANES if causal else 0
            shift = bias_ref[own, begin:] - lse_ref[which : which + 1, begin:]
            prob = jnp.exp(scores_ref[side, chunk, begin:] + shift)
            prob_ref[side, chunk, begin:] = prob.astype(BF)
            centred = prob_grad_ref[side, chunk, begin:] - row_dots[which : which + 1, begin:]
            score_grad_ref[side, chunk, begin:] = (prob * centred).astype(BF)
            if begin:
                prob_ref[side, chunk, :begin] = jnp.zeros((CHUNK, begin), BF)
                score_grad_ref[side, chunk, :begin] = jnp.zeros((CHUNK, begin), BF)
        dv_ref[:, lanes] = merged_pair(dot(prob_ref[side], dout)).astype(BF)
        dk_ref[:, lanes] = merged_pair(dot(score_grad_ref[side], query)).astype(BF)
        for half in range(2):
            at = pair * LANES + half * head
            own = slice(half * length, (half + 1) * length)
            dq_t_ref[at : at + head, :] = dot(kt_ref[at : at + head, :], score_grad_ref[side, own])
    query_grad = (dq_t_ref[...] * scale).T.astype(BF)
    key_grad = dk_ref[...]
    value_grad = dv_ref[...]
    turned = rows_ref[...].astype(BF).T
    other = memory_ref[...].astype(BF).T if cross else turned
    dw_ref[2] = dot(other, value_grad).astype(BF)
    store_start(outs[1], row_place(dw_ref, QUAD // 2, QUAD), sems.at[1])
    dw_ref[0] = dot(turned, query_grad).astype(BF)
    dw_ref[1] = dot(other, key_grad).astype(BF)
    store_start(outs[0], row_place(dw_ref, 0, QUAD // 2), sems.at[0])
    rows_back = rows_out[...] + dot_nt(query_grad, w_ref[0])
    memory_back = dot_nt(key_grad, w_ref[1]) + dot_nt(value_grad, w_ref[2])
    if cross:
        rows_out[...] = rows_back
        memory_out[...] = memory_back
        memory_out.put()
    else:
        rows_out[...] = rows_back + memory_back
    rows_out.put()
    query_bias = total_of([column_sum(query_grad.astype(F32))])
    value_bias = total_of([column_sum(value_grad.astype(F32))])
    spare = jnp.zeros((3, width), F32)
    own = jnp.concatenate(
        [query_bias, value_bias, out_bias, gain_grad, shift_grad, spare], axis=0
    )
    if splits:
        enc_feed, self_attend, cross_attend, dec_feed = [other[...] for other in others]
        whole = small_rows(own, enc_feed, self_attend, cross_attend, dec_feed)
        groups = blocks_ref.shape[0]
        for group in range(groups):
            blocks_ref[group, 0] = small_split(whole, group)
        extra = small_part(outs[-1])
        per = 2 * extra[1][0].shape[0] // groups
        store_start(extra, lambda block: blocks_ref.at[block // per], sems.at[2])
        load_wait(extra, sems.at[2])
    else:
        small_out[...] = own
    for slot, part in enumerate(outs):
        load_wait(part, sems.at[slot])


def small_rows(enc_attend, enc_feed, self_attend, cross_attend, dec_feed):
    return jnp.concatenate(
        [
            enc_attend[:5],
            enc_feed[:3],
            self_attend[:5],
            cross_attend[:5],
            dec_feed[:3],
            dec_feed[7:],
            dec_feed[7:],
            dec_feed[7:],
            enc_feed[3:7],
            dec_feed[3:7],
        ],
        axis=0,
    )


def gelu_parts(pre):
    square = pre * pre
    curve = jnp.tanh(ROOT_TWO_PI * pre * (1.0 + CUBIC * square))
    half = 0.5 * pre
    rise = 0.5 + 0.5 * curve
    bend = ROOT_TWO_PI * (1.0 + 3.0 * CUBIC * square)
    return pre * rise, rise + half * (1.0 - curve * curve) * bend


def chunk_of(ref, index):
    number = ref.shape[0] // QUAD
    part = ref[index * number : (index + 1) * number]
    return part.reshape(number * ref.shape[1] * ref.shape[2], ref.shape[3])


def feed_forward_steps(small, base, hidden_at, rows_ref, up_ref, down_ref, active_ref, slope_ref, pre_ref, sum_ref):
    rows = rows_ref[...].astype(BF)
    length = rows.shape[0]
    for index in range(QUAD):
        at = hidden_at + index
        side = index % 2
        pre_ref[side] = dot(rows, up_ref[index])
        bias = small[at : at + 1]
        for at in range(0, length, CHUNK // 2):
            chunk = slice(at, at + CHUNK // 2)
            active, slope = gelu_parts(pre_ref[side, chunk] + bias)
            active_ref[index, chunk] = active.astype(BF)
            slope_ref[index, chunk] = slope
        for ref in (active_ref, slope_ref):
            if isinstance(ref, Output):
                ref.put(index)
    wide = jnp.concatenate([active_ref[index] for index in range(QUAD)], axis=1)
    number, _, _, width = down_ref.shape
    sum_ref[...] = dot(wide, down_ref[...].reshape(QUAD * width, width))
    out_bias = small[base : base + 1]
    return lambda rows: rows_ref[rows] + (sum_ref[rows] + out_bias)


def feed_backward_steps(
    pre_grad, low_ref, rows_ref, up_ref, down_ref, active_ref, slope_ref, dup_ref, ddown_ref, rows_out, back_ref, outs, sems
):
    low = low_ref[...]
    length = low.shape[0]
    number = ddown_ref.shape[0] // QUAD
    for index in range(QUAD):
        down_grad = dot(active_ref[index].T, low).astype(BF)
        ddown_ref[index * number : (index + 1) * number] = down_grad.reshape(
            (number,) + ddown_ref.shape[1:]
        )
    store_start(outs[1], block_place(ddown_ref), sems.at[1])
    turned = rows_ref[...].astype(BF).T
    hidden_grads = []
    hiddens = []
    for index in range(QUAD):
        side = index % 2
        back_ref[side] = dot_nt(low, chunk_of(down_ref, index))
        sums = []
        parts = []
        for at in range(0, length, CHUNK):
            chunk = slice(at, at + CHUNK)
            hidden = (back_ref[side, chunk] * slope_ref[index, chunk]).astype(BF)
            sums.append(column_sum(hidden.astype(F32)))
            parts.append(hidden)
        hidden = jnp.concatenate(parts, axis=0)
        hidden_grads.append(total_of(sums))
        dup_ref[index] = dot(turned, hidden).astype(BF)
        hiddens.append(hidden)
    store_start(outs[0], row_place(dup_ref, 0, QUAD), sems.at[0])
    total = pre_grad[...]
    for index in range(QUAD):
        total = total + dot_nt(hiddens[index], up_ref[index])
    rows_out[...] = total
    rows_out.put()
    return hidden_grads


def load_feed(parts, up_ref, down_ref, sems):
    load_start(parts[0], row_place(up_ref, 0, QUAD), sems.at[0])
    load_start(parts[1], block_place(down_ref), sems.at[1])


def wait_feed(parts, sems):
    for slot, part in enumerate(parts):
        load_wait(part, sems.at[slot])


def feed_outs(refs, tables):
    arrays = [refs.pop(0), refs.pop(0)]
    return [(tables[slot], arrays, slot * QUAD, QUAD) for slot in range(2)]


def feed_small(out_bias, gain_grad, shift_grad, hidden_grads):
    spare = jnp.zeros_like(out_bias)
    return jnp.concatenate([out_bias, gain_grad, shift_grad] + hidden_grads + [spare], axis=0)


def feed_forward_kernel(layout, base, hidden_at, *refs):
    refs = list(refs)
    tables = [refs.pop(0), refs.pop(0)]
    small, rows_ref = refs.pop(0), refs.pop(0)
    parts = take_parts(refs, layout, tables)
    out_ref, hat_ref, rstd_ref, active_ref, slope_ref, up_ref, down_ref = refs[:7]
    pre_ref, sum_ref, sems = refs[7:]
    load_feed(parts, up_ref, down_ref, sems)
    wait_feed(parts, sems)
    pre_of = feed_forward_steps(
        small, base, hidden_at, rows_ref, up_ref, down_ref, active_ref, slope_ref, pre_ref, sum_ref
    )
    gain, shift = small[base + 1 : base + 2], small[base + 2 : base + 3]
    norm_forward(pre_of, rows_ref.shape[0], gain, shift, out_ref, hat_ref, rstd_ref)


def feed_backward_kernel(layout, base, *refs):
    refs = list(refs)
    tables = [refs.pop(0), refs.pop(0)]
    out_tables = [refs.pop(0), refs.pop(0)]
    small, grad_ref, hat_ref, rstd_ref, rows_ref = [refs.pop(0) for _ in range(5)]
    active_ref, slope_ref = refs.pop(0), refs.pop(0)
    parts = take_parts(refs, layout, tables)
    rows_out, small_out = refs.pop(0), refs.pop(0)
    outs = feed_outs(refs, out_tables)
    up_ref, down_ref, dup_ref, ddown_ref, low_ref, back_ref, sems, out_sems = refs
    load_feed(parts, up_ref, down_ref, sems)
    gain_grad, shift_grad, out_bias = norm_backward(
        grad_ref, hat_ref, rstd_ref, small[base + 1 : base + 2], rows_out, low_ref
    )
    wait_feed(parts, sems)
    hidden_grads = feed_backward_steps(
        rows_out,
        low_ref,
        rows_ref,
        up_ref,
        down_ref,
        active_ref,
        slope_ref,
        dup_ref,
        ddown_ref,
        rows_out,
        back_ref,
        outs,
        out_sems,
    )
    small_out[...] = feed_small(out_bias, gain_grad, shift_grad, hidden_grads)
    wait_feed(outs, out_sems)


def feed_both_kernel(layout, base, hidden_at, *refs):
    refs = list(refs)
    tables = [refs.pop(0), refs.pop(0)]
    out_tables = [refs.pop(0), refs.pop(0)]
    small, rows_ref, grad_ref = [refs.pop(0) for _ in range(3)]
    parts = take_parts(refs, layout, tables)
    out_ref, rows_out, small_out = [refs.pop(0) for _ in range(3)]
    outs = feed_outs(refs, out_tables)
    up_ref, down_ref, dup_ref, ddown_ref, low_ref, back_ref, sum_ref = refs[:7]
    active_ref, slope_ref, hat_ref, rstd_ref, sems, out_sems = refs[7:]
    load_feed(parts, up_ref, down_ref, sems)
    wait_feed(parts, sems)
    pre_of = feed_forward_steps(
        small, base, hidden_at, rows_ref, up_ref, down_ref, active_ref, slope_ref, back_ref, sum_ref
    )
    gain, shift = small[base + 1 : base + 2], small[base + 2 : base + 3]
    norm_forward(pre_of, rows_ref.shape[0], gain, shift, out_ref, hat_ref, rstd_ref)
    gain_grad, shift_grad, out_bias = norm_backward(
        grad_ref, hat_ref, rstd_ref, gain, rows_out, low_ref
    )
    hidden_grads = feed_backward_steps(
        rows_out,
        low_ref,
        rows_ref,
        up_ref,
        down_ref,
        active_ref,
        slope_ref,
        dup_ref,
        ddown_ref,
        rows_out,
        back_ref,
        outs,
        out_sems,
    )
    small_out[...] = feed_small(out_bias, gain_grad, shift_grad, hidden_grads)
    wait_feed(outs, out_sems)


def shaped(shape, dtype=F32):
    return jax.ShapeDtypeStruct(shape, dtype)


def call(
    kernel, scalars, inputs, others, outs, targets, scratch, flops, moved, limit=VMEM_BYTES
):
    rooms = [pltpu.VMEM(array.shape, array.dtype) for array in list(inputs) + list(outs)]
    return pl.pallas_call(
        functools.partial(
            staged_kernel, kernel, len(scalars), len(inputs), len(others), len(outs), len(targets)
        ),
        out_shape=list(outs) + list(targets),
        in_specs=[SMEM] * len(scalars) + [ANY] * (len(inputs) + len(others)),
        out_specs=[ANY] * (len(outs) + len(targets)),
        scratch_shapes=scratch + rooms + [pltpu.SemaphoreType.DMA((len(rooms),))],
        cost_estimate=pl.CostEstimate(flops=flops, bytes_accessed=moved, transcendentals=0),
        compiler_params=pltpu.CompilerParams(vmem_limit_bytes=limit),
    )(*scalars, *inputs, *others)


def layout_of(parts):
    return [(len(arrays), low, number) for _, arrays, low, number in parts]


def arrays_of(parts):
    return [array for part in parts for array in part[1]]


def most(parts):
    return max(len(part[1]) for part in parts)


def halves(width, number):
    return [shaped((width // BLOCK // 2, number, BLOCK, width), BF)] * 2


def attend_forward(segments, small, base, rows, memory, parts, causal):
    length, width = rows.shape
    cross = memory is not None
    joins = small is None
    scalars = [part[0] for part in parts]
    inputs = list(segments) + ([] if joins else [small]) + [rows] + ([memory] if cross else [])
    outs = [shaped((length, width), BF)] * 4 + [shaped((HEADS, length))]
    outs += [shaped((length, width)), shaped((length, LANES)), shaped((length, width))]
    outs += [shaped((SMALL_ROWS, width))] if joins else []
    scratch = [
        pltpu.VMEM((QUAD, width, width), BF),
        pltpu.VMEM((length, length), F32),
        pltpu.VMEM((2, 2 * length, length), F32),
        pltpu.VMEM((2, 2 * length, length), BF),
        pltpu.VMEM((2, 2 * length, LANES), F32),
        pltpu.VMEM((2, 2 * length, 2 * LANES), F32),
        pltpu.VMEM((length, width), F32),
        pltpu.SemaphoreType.DMA((len(parts) + 1, most(parts))),
    ]
    scratch += [pltpu.VMEM((width // BLOCK, 1, BLOCK, width), BF)] if joins else []
    kernel = functools.partial(attend_forward_kernel, layout_of(parts), cross, causal, base, joins)
    flops = 8 * length * width * width + 16 * length * length * width
    return call(kernel, scalars, inputs, arrays_of(parts), outs, [], scratch, flops, 8_000_000)


def attend_backward(
    out_tables, segments, small, base, grad, kept, rows, memory, parts, causal, others
):
    length, width = rows.shape
    cross = memory is not None
    splits = others is not None
    q, k, v, o, lse, hat, rstd = kept[:7]
    scalars = [part[0] for part in parts] + list(out_tables)
    inputs = list(segments) + [small, grad, hat, rstd, rows]
    inputs += ([memory] if cross else []) + [q, k, v, o, lse] + list(others or ())
    outs = [shaped((length, width))] * (2 if cross else 1)
    outs += [] if splits else [shaped((8, width))]
    targets = halves(width, QUAD + (1 if splits else 0))
    scratch = [
        pltpu.VMEM((QUAD, width, width), BF),
        pltpu.VMEM((QUAD, width, width), BF),
        pltpu.VMEM((length, length), F32),
        pltpu.VMEM((length, width), BF),
        pltpu.VMEM((width, length), F32),
        pltpu.VMEM((length, width), BF),
        pltpu.VMEM((length, width), BF),
        pltpu.VMEM((width, length), BF),
        pltpu.VMEM((length, width), BF),
        pltpu.VMEM((2, 2 * length, length), F32),
        pltpu.VMEM((2, 2 * length, length), F32),
        pltpu.VMEM((2, 2 * length, length), BF),
        pltpu.VMEM((2, 2 * length, length), BF),
        pltpu.SemaphoreType.DMA((3, 2)),
    ]
    scratch += [pltpu.VMEM((width // LANES, 1, BLOCK, width), BF)] if splits else []
    kernel = functools.partial(
        attend_backward_kernel, layout_of(parts), cross, causal, base, splits
    )
    flops = 16 * length * width * width + 40 * length * length * width
    arrays = arrays_of(parts)
    results = list(call(kernel, scalars, inputs, arrays, outs, targets, scratch, flops, 12_000_000))
    rows_grad = results.pop(0)
    memory_grad = results.pop(0) if cross else None
    small_grad = None if splits else results.pop(0)
    return rows_grad, memory_grad, small_grad, results


def feed_scratch(width, grads):
    number = width // BLOCK
    once = [pltpu.VMEM((QUAD, width, width), BF), pltpu.VMEM((number, QUAD, BLOCK, width), BF)]
    return once * (2 if grads else 1)


def feed_forward(small, base, hidden_at, rows, parts):
    length, width = rows.shape
    scalars = [part[0] for part in parts]
    outs = [shaped((length, width)), shaped((length, width)), shaped((length, LANES))]
    outs += [shaped((QUAD, length, width), BF), shaped((QUAD, length, width))]
    scratch = feed_scratch(width, False)
    scratch += [pltpu.VMEM((2, length, width), F32), pltpu.VMEM((length, width), F32)]
    scratch += [pltpu.SemaphoreType.DMA((2, most(parts)))]
    kernel = functools.partial(feed_forward_kernel, layout_of(parts), base, hidden_at)
    flops = 16 * length * width * width
    arrays = arrays_of(parts)
    return call(kernel, scalars, [small, rows], arrays, outs, [], scratch, flops, 10_000_000)


def feed_backward(out_tables, small, base, grad, kept, rows, parts):
    length, width = rows.shape
    hat, rstd, active, slope = kept[1:]
    scalars = [part[0] for part in parts] + list(out_tables)
    inputs = [small, grad, hat, rstd, rows, active, slope]
    outs = [shaped((length, width)), shaped((8, width))]
    targets = halves(width, 2 * QUAD)
    scratch = feed_scratch(width, True)
    scratch += [pltpu.VMEM((length, width), BF), pltpu.VMEM((2, length, width), F32)]
    scratch += [pltpu.SemaphoreType.DMA((2, most(parts))), pltpu.SemaphoreType.DMA((2, 2))]
    kernel = functools.partial(feed_backward_kernel, layout_of(parts), base)
    flops = 32 * length * width * width
    arrays = arrays_of(parts)
    results = call(kernel, scalars, inputs, arrays, outs, targets, scratch, flops, 14_000_000)
    return results[0], results[1], results[2:4]


def feed_both(out_tables, small, base, hidden_at, rows, grad, parts):
    length, width = rows.shape
    scalars = [part[0] for part in parts] + list(out_tables)
    outs = [shaped((length, width)), shaped((length, width)), shaped((8, width))]
    targets = halves(width, 2 * QUAD)
    scratch = feed_scratch(width, True) + [
        pltpu.VMEM((length, width), BF),
        pltpu.VMEM((2, length, width), F32),
        pltpu.VMEM((length, width), F32),
        pltpu.VMEM((QUAD, length, width), BF),
        pltpu.VMEM((QUAD, length, width), F32),
        pltpu.VMEM((length, width), F32),
        pltpu.VMEM((length, LANES), F32),
        pltpu.SemaphoreType.DMA((2, most(parts))),
        pltpu.SemaphoreType.DMA((2, 2)),
    ]
    kernel = functools.partial(feed_both_kernel, layout_of(parts), base, hidden_at)
    flops = 48 * length * width * width
    arrays = arrays_of(parts)
    results = call(kernel, scalars, [small, rows, grad], arrays, outs, targets, scratch, flops, 12_000_000)
    return results[0], results[1], results[2], results[3:5]


def first_kernel(
    at_ref,
    vector_ref,
    hidden_ref,
    square_ref,
    tall_ref,
    deep_ref,
    one_ref,
    two_ref,
    three_ref,
    turn_ref,
    line_ref,
):
    at = at_ref[0]
    width = square_ref.shape[2]
    turn_ref[...] = jnp.zeros_like(turn_ref)
    lanes, rows = vector_ref.shape
    turn_ref[pl.ds(pl.multiple_of(at * lanes, lanes), lanes), :rows] = vector_ref[...]
    upright = turn_ref[...].T
    line_ref[...] = jnp.zeros_like(line_ref)
    layers, lanes = hidden_ref.shape
    per = LANES // lanes
    for layer in range(layers):
        row = jnp.concatenate([hidden_ref[layer : layer + 1]] * per, axis=1)
        lane = lax.broadcasted_iota(jnp.int32, row.shape, 1) // lanes
        row = jnp.where(lane == at % per, row, 0.0)
        line_ref[pl.ds(4 * layer + at // per, 1), :] = row
    columns = [upright[low : low + 8] for low in (0, 8, 16)] + [line_ref[...]]
    block = jnp.concatenate(columns, axis=1)
    small = jnp.concatenate([block, jnp.zeros_like(block)], axis=0)
    tall = []
    deep = []
    for layer in range(2):
        for index in range(QUAD):
            lanes = slice(index * width, (index + 1) * width)
            tall.append(tall_ref[layer, :, lanes])
            deep.append(deep_ref[layer, index * BLOCK : (index + 1) * BLOCK])
    square = [square_ref[index] for index in range(3 * QUAD)]
    cut = QUAD // 2
    groups = [
        square[:cut] + tall[:QUAD] + square[cut:QUAD] + [small] + deep[:QUAD],
        square[QUAD:],
        tall[QUAD:] + deep[QUAD:],
    ]
    for out_ref, group in zip((one_ref, two_ref, three_ref), groups):
        for slot, block in enumerate(group):
            out_ref[0, slot] = block.astype(BF)
        out_ref.put()


def first_arrays(at, square, tall, deep, vectors, hidden):
    width = square.shape[2]
    outs = [
        shaped((1, 3 * QUAD + 1, BLOCK, width), BF),
        shaped((1, 2 * QUAD, BLOCK, width), BF),
        shaped((1, 2 * QUAD, BLOCK, width), BF),
    ]
    scratch = [pltpu.VMEM((LANES, LANES), F32), pltpu.VMEM((8, LANES), F32)]
    inputs = [vectors.T, hidden, square, tall, deep]
    return call(first_kernel, [at], inputs, [], outs, [], scratch, 0, 4_000_000)


def last_kernel(plan, count, at_ref, *refs):
    masters, firsts, seconds = refs[:5], refs[5:10], refs[10:15]
    arrays, refs = refs[15 : 15 + count], refs[15 + count :]
    outs, refs = [refs[5 * kind : 5 * kind + 5] for kind in range(4)], refs[20:]
    buffers, turn_ref, line_ref, sems = refs
    at = at_ref[0]
    starts = []
    for width, pieces, _ in plan:
        for index, low in pieces:
            array = arrays[index]
            array = array if len(array.shape) == 3 else array.at[0]
            source = array.at[low : low + width]
            copy = pltpu.make_async_copy(source, buffers.at[len(starts), :width], sems.at[len(starts)])
            copy.start()
            starts.append(copy)

    def update(slot, where, gradient):
        results = adam_update(
            masters[slot][where],
            gradient,
            firsts[slot][where],
            seconds[slot][where],
            RATES[slot],
            DECAYS[slot],
        )
        for kind in range(4):
            outs[kind][slot][where] = results[kind]

    begin = 0
    left = len(plan)
    for width, pieces, targets in plan:
        for index in range(len(pieces)):
            starts[begin + index].wait()
        for sub, (slot, where) in enumerate(targets):
            gradient = buffers[begin, sub].astype(F32)
            for index in range(1, len(pieces)):
                gradient = gradient + buffers[begin + index, sub].astype(F32)
            if slot < 3:
                update(slot, where, gradient)
                continue
            turn_ref[...] = jnp.zeros_like(turn_ref)
            for column in range(3):
                lanes = slice(column * LANES, (column + 1) * LANES)
                turn_ref[8 * column : 8 * column + 8, :] = gradient[:8, lanes]
            turn_ref[...] = turn_ref[...].T
            lanes, rows = masters[3].shape
            share = turn_ref[pl.ds(pl.multiple_of(at * lanes, lanes), lanes), :][:, :rows]
            update(3, slice(None), share)
            line_ref[...] = gradient[:8, 3 * LANES :]
            layers, lanes = masters[4].shape
            per = LANES // lanes
            for layer in range(layers):
                row = line_ref[pl.ds(4 * layer + at // per, 1), :]
                share = row[:, :lanes]
                for part in range(1, per):
                    other = row[:, part * lanes : (part + 1) * lanes]
                    share = jnp.where(at % per == part, other, share)
                update(4, slice(layer, layer + 1), share)
        begin += len(pieces)
        left -= 1
        for slot in range(5):
            ends = [at for at, (_, _, each) in enumerate(plan) if any(to[0] in used(slot) for to in each)]
            if ends[-1] == len(plan) - 1 - left:
                for kind in range(4):
                    outs[kind][slot].put()


def used(slot):
    return (3,) if slot > 2 else (slot,)


def last_update(at, segments, masters, firsts, seconds):
    arrays = []
    plan = []
    for width, pieces, targets in segments:
        entry = []
        for array, low in pieces:
            found = [place for place, other in enumerate(arrays) if other is array]
            if not found:
                arrays.append(array)
            entry.append((found[0] if found else len(arrays) - 1, low))
        plan.append((width, entry, targets))
    params = [list(group) for group in (masters, firsts, seconds)]
    for group in params:
        group[3] = group[3].T
    flat = params[0] + params[1] + params[2]
    outs = [shaped(array.shape) for array in params[0]] * 3
    outs += [shaped(array.shape, BF) for array in params[0]]
    pieces = sum(len(entry[1]) for entry in plan)
    block = masters[0].shape[1:]
    scratch = [
        pltpu.VMEM((pieces, max(entry[0] for entry in plan)) + block, BF),
        pltpu.VMEM((LANES, LANES), F32),
        pltpu.VMEM((8, LANES), F32),
        pltpu.SemaphoreType.DMA((pieces,)),
    ]
    kernel = functools.partial(last_kernel, plan, len(arrays))
    results = call(
        kernel, [at], flat, arrays, outs, [], scratch, 0, 8_000_000, VMEM_BYTES // 2
    )
    results = list(results)
    for kind in range(4):
        results[5 * kind + 3] = results[5 * kind + 3].T
    return results


def tie(*arrays):
    return lax.optimization_barrier(arrays)


class Direct:
    def __init__(self, axis_sizes):
        outer, inner = axis_sizes
        self.count = outer * inner
        inner_bits = inner.bit_length() - 1
        bits = self.count.bit_length() - 1
        core = [inner_bits]
        across = list(range(inner_bits + 1, bits))
        up = [0]
        along = list(range(1, inner_bits))
        self.orders = {
            "a": core + across + up + along,
            "b": core + up + across + along,
            "c": core + along + across + up,
            "d": core + along + up + across,
        }
        self.place = lax.axis_index(AXES)

    def hop(self, array, bit):
        return lax.ppermute(array, AXES, [(at, at ^ (1 << bit)) for at in range(self.count)])

    def table(self, name):
        order = self.orders[name]
        index = jnp.arange(self.count, dtype=jnp.int32)
        block = jnp.zeros_like(index)
        for at, bit in enumerate(order):
            block = block | (((index >> (len(order) - 1 - at)) & 1) << bit)
        return block ^ self.place

    def arrive(self, array, name, step):
        return self.hop(array, self.orders[name][::-1][step])

    def finish(self, array, name):
        return [array, self.hop(array, self.orders[name][0])]


def grown(arrays, arrivals):
    return [jnp.concatenate(pair, axis=0) for pair in zip(arrays, arrivals)]


class Sum:
    def __init__(self, net, name, segments, done, blocks):
        self.net = net
        self.name = name
        self.segments = segments
        self.done = done
        self.blocks = blocks

    def bit(self):
        return self.net.orders[self.name][self.done]

    def split(self, names):
        return [
            Sum(self.net, name, [segment], self.done, self.blocks)
            for name, segment in zip(names, self.segments)
        ]


def core_hop(net, pair, widths):
    keep, send = pair
    arrived = net.hop(send, net.orders["a"][0])
    low = 0
    segments = []
    for width in widths:
        segments.append((width, [(keep, low), (arrived, low)]))
        low += width
    return Sum(net, "a", segments, 1, keep.shape[0])


def combine_kernel(plan, count, outputs, *refs):
    arrays, refs = refs[:count], refs[count:]
    outs, buffers, sems = refs[:outputs], refs[outputs:-1], refs[-1]
    starts = []
    for _, _, held, number, width, pieces in plan:
        begin = 0 if held is not None else number
        for index, low in pieces:
            array = arrays[index]
            if len(array.shape) == 3:
                source = array.at[low + begin * width : low + 2 * number * width]
            else:
                source = array.at[begin : 2 * number, low : low + width]
            copy = pltpu.make_async_copy(source, buffers[len(starts)], sems.at[len(starts)])
            copy.start()
            starts.append(copy)
    begin = 0
    for slot, first, held, number, width, pieces in plan:
        for index in range(begin, begin + len(pieces)):
            starts[index].wait()
        mine = buffers[begin : begin + len(pieces)]
        jobs = [(slot, first, 0)] if held is None else [(slot, first, number), (outputs - 1, held, 0)]
        for out, place, skip in jobs:

            for block in range(number):
                value = None
                for buffer in mine:
                    flat = len(buffer.shape) == 3
                    at = block + skip
                    part = buffer[at * width : (at + 1) * width] if flat else buffer[at]
                    value = part.astype(F32) if value is None else value + part.astype(F32)
                outs[out][place + block * width : place + (block + 1) * width] = value.astype(BF)
        begin += len(pieces)


class Round:
    def __init__(self, sums, *tokens, limit=VMEM_BYTES // 3):
        self.net = sums[0].net
        self.sums = sums
        self.bits = sorted({item.bit() for item in sums})
        arrays = []
        plan = []
        sizes = [0] * len(self.bits) + [0]
        self.places = []
        block = None
        for item in sums:
            slot = self.bits.index(item.bit())
            number = item.blocks // 2
            holds = item.done > 1
            places = []
            for width, pieces in item.segments:
                entry = []
                for array, low in pieces:
                    found = [at for at, other in enumerate(arrays) if other is array]
                    if not found:
                        arrays.append(array)
                    entry.append((found[0] if found else len(arrays) - 1, low))
                    block = array.shape[-2:]
                held = sizes[-1] if holds else None
                plan.append((slot, sizes[slot], held, number, width, entry))
                places.append((sizes[slot], held))
                sizes[slot] += number * width
                sizes[-1] += number * width if holds else 0
            self.places.append((slot, places))
        tied = list(tie(*arrays, *tokens))[: len(arrays)] if tokens else arrays
        scratch = []
        moved = 0
        for _, _, held, number, width, entry in plan:
            both = number if held is None else 2 * number
            moved += both * width * (len(entry) + 1) * 16384
            for index, _ in entry:
                flat = len(arrays[index].shape) == 3
                shape = (both * width,) if flat else (both, width)
                scratch.append(pltpu.VMEM(shape + block, BF))
        if not sizes[-1]:
            sizes.pop()
        self.sends = pl.pallas_call(
            functools.partial(combine_kernel, plan, len(tied), len(sizes)),
            out_shape=[shaped((size,) + block, BF) for size in sizes],
            in_specs=[ANY] * len(tied),
            out_specs=[VMEM] * len(sizes),
            scratch_shapes=scratch + [pltpu.SemaphoreType.DMA((len(scratch),))],
            cost_estimate=pl.CostEstimate(flops=0, bytes_accessed=moved, transcendentals=0),
            compiler_params=pltpu.CompilerParams(vmem_limit_bytes=limit),
        )(*tied)

    def before(self, *arrays):
        tied = tie(*arrays, *self.sends)
        self.sends = list(tied[len(arrays) :])
        return tied[: len(arrays)]

    def go(self):
        arrived = [self.net.hop(send, bit) for send, bit in zip(self.sends, self.bits)]
        for item, (slot, places) in zip(self.sums, self.places):
            made = []
            for (width, pieces), (place, held) in zip(item.segments, places):
                stay = pieces if held is None else [(self.sends[-1], held)]
                made.append((width, stay + [(arrived[slot], place)]))
            item.segments = made
            item.done += 1
            item.blocks //= 2
        return arrived


def adam_update(weight, gradient, first, second, rate, decay):
    first_new = BETA_ONE * first + (1.0 - BETA_ONE) * gradient
    second_new = BETA_TWO * second + (1.0 - BETA_TWO) * gradient * gradient
    first_hat = first_new / (1.0 - BETA_ONE**STEP)
    second_hat = second_new / (1.0 - BETA_TWO**STEP)
    weight_new = weight - rate * (first_hat / (jnp.sqrt(second_hat) + EPS_ADAM) + decay * weight)
    return (weight_new, first_new, second_new, weight_new.astype(BF))


def gather_small(vectors, hidden):
    whole = lax.all_gather(vectors.astype(BF), AXES, axis=1, tiled=True)
    deep = lax.all_gather(hidden.astype(BF), AXES, axis=1, tiled=True)
    whole = jnp.pad(whole, ((0, HIDDEN_ROW - whole.shape[0]), (0, 0)))
    return jnp.concatenate([whole, deep.reshape(-1, whole.shape[1])], axis=0).astype(F32)


def scatter_small(grads, vectors, hidden, place, count):
    whole = lax.psum(small_rows(*grads), AXES)
    rows, lanes = vectors.shape
    first = lax.dynamic_slice_in_dim(whole[:rows], place * lanes, lanes, axis=1)
    layers, lanes = hidden.shape
    deep = whole[HIDDEN_ROW:].reshape(layers, -1)
    return first, lax.dynamic_slice_in_dim(deep, place * lanes, lanes, axis=1)


def gather_whole(attention, up, down):
    width = attention.shape[2]
    number = width // BLOCK
    square = lax.all_gather(attention, AXES, axis=1, tiled=True)
    square = square.reshape(-1, QUAD, number, BLOCK, width).transpose(0, 2, 1, 3, 4)
    tall = lax.all_gather(up, AXES, axis=1, tiled=True)
    tall = tall.reshape(2, number, BLOCK, QUAD, width).transpose(0, 1, 3, 2, 4)
    deep = lax.all_gather(down, AXES, axis=1, tiled=True).reshape(2, number, QUAD, BLOCK, width)
    half = number // 2
    quads = [square[0], tall[0], deep[0], square[1], square[2], tall[1], deep[1]]
    return [(quad[:half], quad[half:]) for quad in quads]


def scatter_whole(quads):
    joined = [jnp.concatenate(pair, axis=0).astype(F32) for pair in quads]
    number, _, _, width = joined[0].shape
    square = jnp.stack([joined[0], joined[3], joined[4]])
    square = square.transpose(0, 2, 1, 3, 4).reshape(3 * QUAD, width, width)
    tall = jnp.stack([joined[1], joined[5]]).transpose(0, 1, 3, 2, 4)
    tall = tall.reshape(2, width, QUAD * width)
    deep = jnp.stack([joined[2], joined[6]]).reshape(2, QUAD * width, width)
    return [
        lax.psum_scatter(part, AXES, scatter_dimension=1, tiled=True)
        for part in (square, tall, deep)
    ]


def direct_step(pairs, source, target, grad, masters, firsts, seconds, axis_sizes):
    net = Direct(axis_sizes)
    source_pair, target_pair, cross_pair = pairs
    a, b = net.table("a"), net.table("b")
    cut = QUAD // 2
    at = (net.place % (net.count * LANES // source.shape[1])).astype(jnp.int32).reshape(1)

    one, two, three = first_arrays(at, *masters)
    up_two, down_two = three[:, :QUAD], three[:, QUAD:]
    for step in (0, 1):
        more = tie(
            net.arrive(one, "a", step),
            net.arrive(up_two, "c", step),
            net.arrive(down_two, "d", step),
        )
        one, up_two, down_two = grown((one, up_two, down_two), more)
    three = jnp.concatenate([up_two, down_two], axis=1)
    left, right = one[:, : cut + QUAD], one[:, cut + QUAD :]
    two, three, left, right = tie(two, three, left, right)
    left, right, two = grown(
        (left, right, two),
        tie(net.arrive(left, "a", 2), net.arrive(right, "b", 2), net.arrive(two, "a", 0)),
    )
    left, right, two, three = grown(
        (left, right, two, three),
        tie(
            net.arrive(left, "a", 3),
            net.arrive(right, "b", 3),
            net.arrive(two, "a", 1),
            net.arrive(three, "c", 2),
        ),
    )
    self_w, cross_w = two[:, :QUAD], two[:, QUAD:]
    more = tie(
        net.hop(left, net.orders["a"][0]),
        net.hop(right, net.orders["b"][0]),
        net.arrive(self_w, "a", 2),
        net.arrive(cross_w, "b", 2),
    )
    left, right = [left, more[0]], [right, more[1]]
    self_w, cross_w = grown((self_w, cross_w), more[2:])
    source, self_w, cross_w, three = tie(source, self_w, cross_w, three)
    more = [
        net.arrive(self_w, "a", 3),
        net.arrive(cross_w, "b", 3),
        net.arrive(three, "c", 3),
    ]
    enc_attend_w = [(a, left, 0, cut), (b, right, 0, cut)]
    enc_feed_w = [(a, left, cut, QUAD), (b, right, cut + 1, QUAD)]
    enc_kept = attend_forward(source_pair, None, 0, source, None, enc_attend_w, False)
    enc_mid, small = enc_kept[7], enc_kept[8]
    enc_feed_kept = feed_forward(small, 5, HIDDEN_ROW, enc_mid, enc_feed_w)
    memory = enc_feed_kept[0]
    self_w, cross_w = grown((self_w, cross_w), tie(*more[:2], memory)[:2])
    (three,) = grown([three], tie(more[2], self_w, cross_w)[:1])
    target, self_w, cross_w, three = tie(target, self_w, cross_w, three)
    self_w, cross_w = net.finish(self_w, "a"), net.finish(cross_w, "b")
    three, self_w[1] = tie(three, self_w[1])
    three = net.finish(three, "c")
    self_w = [(a, self_w, 0, QUAD)]
    cross_w = [(b, cross_w, 0, QUAD)]
    self_kept = attend_forward(target_pair, small, 8, target, None, self_w, True)
    dec_one = self_kept[7]
    cross_kept = attend_forward(cross_pair, small, 13, dec_one, memory, cross_w, False)
    dec_two = cross_kept[7]
    dec_feed_w = [(net.table("c"), three, 0, QUAD), (net.table("d"), three, QUAD, QUAD)]
    result, two_grad, dec_feed_small, feed_two = feed_both(
        (a, b), small, 18, HIDDEN_ROW + QUAD, dec_two, grad, dec_feed_w
    )

    names = ("a", "b")
    feed_two = core_hop(net, feed_two, (QUAD, QUAD)).split(names)
    one_grad, memory_grad, cross_small, cross_q = attend_backward(
        (a, b), cross_pair, small, 13, two_grad, cross_kept, dec_one, memory, cross_w, False, None
    )
    send = Round(feed_two, cross_small)
    memory_grad, *cross_q = send.before(memory_grad, *cross_q)
    send.go()
    cross_s = core_hop(net, cross_q, (cut, cut)).split(names)
    mid_grad, enc_feed_small, feed_one = feed_backward(
        (a, b), small, 5, memory_grad, enc_feed_kept, enc_mid, enc_feed_w
    )
    send = Round(feed_two + cross_s, enc_feed_small)
    one_grad, *feed_one = send.before(one_grad, *feed_one)
    send.go()
    feed_one = core_hop(net, feed_one, (QUAD, QUAD)).split(names)
    target_grad, _, self_small, self_q = attend_backward(
        (a, b), target_pair, small, 8, one_grad, self_kept, target, None, self_w, True, None
    )
    send = Round(feed_two + cross_s + feed_one, self_small)
    mid_grad, *self_q = send.before(mid_grad, *self_q)
    send.go()
    self_s = core_hop(net, self_q, (cut, cut)).split(names)
    others = (enc_feed_small, self_small, cross_small, dec_feed_small)
    source_grad, _, _, enc_q = attend_backward(
        (a, b), source_pair, small, 0, mid_grad, enc_kept, source, None, enc_attend_w, False, others
    )
    send = Round(feed_two + cross_s + feed_one + self_s, source_grad)
    enc_q = send.before(*enc_q)
    last = send.go()
    enc_s = core_hop(net, enc_q, (cut, cut + 1)).split(names)
    while enc_s[0].blocks > 1:
        send = Round([item for item in cross_s + feed_one + self_s + enc_s if item.blocks > 1], *last)
        last = send.go()

    square = [(0, index) for index in range(3 * QUAD)]
    tall, deep = [], []
    for layer in range(2):
        for index in range(QUAD):
            lanes = slice(index * source.shape[1], (index + 1) * source.shape[1])
            tall.append((1, (layer, slice(None), lanes)))
            deep.append((2, (layer, slice(index * BLOCK, (index + 1) * BLOCK))))
    targets = [square[:cut], square[cut:QUAD] + [(3, None)]]
    targets += [square[QUAD : QUAD + cut], square[QUAD + cut : 2 * QUAD], tall[:QUAD], deep[:QUAD]]
    targets += [tall[QUAD:], deep[QUAD:]]
    targets += [square[2 * QUAD : 2 * QUAD + cut], square[2 * QUAD + cut :]]
    segments = [item.segments[0] for item in enc_s + self_s + feed_one + feed_two + cross_s]
    segments = [segment + (target,) for segment, target in zip(segments, targets)]
    updated = last_update(at, segments, masters, firsts, seconds)
    return (memory, result, source_grad, target_grad), updated


def whole_step(pairs, source, target, grad, masters, firsts, seconds, axis_sizes):
    attention, up, down = [master.astype(BF) for master in masters[:3]]
    vectors, hidden = masters[3:]
    source_pair, target_pair, cross_pair = pairs
    small = gather_small(vectors, hidden)
    quads = gather_whole(attention, up, down)
    table = jnp.arange(source.shape[1] // BLOCK, dtype=jnp.int32)
    two = (table, table)
    parts = [(table, list(quad), 0, QUAD) for quad in quads]
    enc_kept = attend_forward(source_pair, small, 0, source, None, parts[:1], False)
    enc_mid = enc_kept[7]
    enc_feed_kept = feed_forward(small, 5, HIDDEN_ROW, enc_mid, parts[1:3])
    memory = enc_feed_kept[0]
    self_kept = attend_forward(target_pair, small, 8, target, None, parts[3:4], True)
    dec_one = self_kept[7]
    cross_kept = attend_forward(cross_pair, small, 13, dec_one, memory, parts[4:5], False)
    dec_two = cross_kept[7]
    result, two_grad, dec_feed_small, feed_two = feed_both(
        two, small, 18, HIDDEN_ROW + QUAD, dec_two, grad, parts[5:7]
    )
    one_grad, memory_grad, cross_small, cross_q = attend_backward(
        two, cross_pair, small, 13, two_grad, cross_kept, dec_one, memory, parts[4:5], False, None
    )
    target_grad, _, self_small, self_q = attend_backward(
        two, target_pair, small, 8, one_grad, self_kept, target, None, parts[3:4], True, None
    )
    mid_grad, enc_feed_small, feed_one = feed_backward(
        two, small, 5, memory_grad, enc_feed_kept, enc_mid, parts[1:3]
    )
    source_grad, _, enc_small, enc_q = attend_backward(
        two, source_pair, small, 0, mid_grad, enc_kept, source, None, parts[:1], False, None
    )
    quads = [enc_q]
    quads += [[half[:, low : low + QUAD] for half in feed_one] for low in (0, QUAD)]
    quads += [self_q, cross_q]
    quads += [[half[:, low : low + QUAD] for half in feed_two] for low in (0, QUAD)]
    smalls = (enc_small, enc_feed_small, self_small, cross_small, dec_feed_small)
    count = axis_sizes[0] * axis_sizes[1]
    shares = scatter_small(smalls, vectors, hidden, lax.axis_index(AXES), count)
    grads = tuple(scatter_whole(quads)) + shares
    updated = [
        adam_update(
            masters[slot], grads[slot], firsts[slot], seconds[slot], RATES[slot], DECAYS[slot]
        )
        for slot in range(5)
    ]
    flat = [updated[slot][kind] for kind in range(4) for slot in range(5)]
    return (memory, result, source_grad, target_grad), flat


def per_device(
    axis_sizes,
    source_tokens,
    target_tokens,
    source_segments,
    target_segments,
    output_grad,
    attention_weight,
    up_weight,
    down_weight,
    vectors,
    hidden_bias,
    *moments,
):
    masters = (attention_weight, up_weight, down_weight, vectors, hidden_bias)
    firsts = moments[:5]
    seconds = moments[5:]
    width = source_tokens.shape[2]
    pairs = (
        (source_segments, source_segments),
        (target_segments, target_segments),
        (target_segments, source_segments),
    )
    direct = axis_sizes[0] * axis_sizes[1] * BLOCK == width
    tokens, updated = (direct_step if direct else whole_step)(
        pairs,
        source_tokens[0],
        target_tokens[0],
        output_grad[0],
        masters,
        firsts,
        seconds,
        axis_sizes,
    )
    return tuple(array[None] for array in tokens) + tuple(updated)


def solution(mesh):
    rows = P(AXES, None, None)
    line = P(AXES, None)
    matrix = P(None, AXES, None)
    vector = P(None, AXES)
    state = (matrix, matrix, matrix, vector, vector)
    return jax.shard_map(
        functools.partial(per_device, (mesh.shape["dp"], mesh.shape["fsdp"])),
        mesh=mesh,
        in_specs=(rows, rows, line, line, rows) + state * 3,
        out_specs=(rows,) * 4 + state * 4,
        check_vma=False,
    )
```

```python
import functools

import jax
import jax.numpy as jnp
from jax import lax
from jax.experimental import pallas as pl
from jax.experimental.pallas import tpu as pltpu
from jax.sharding import PartitionSpec as P

HEADS = 8
STEP = 10
EPS_NORM = 1e-05
EPS_ADAM = 1e-08
BETA_ONE = 0.9
BETA_TWO = 0.999
LOWEST = -1e30
RATES = (0.05, 0.05, 0.05, 0.3, 0.3)
DECAYS = (0.01, 0.01, 0.01, 0.0, 0.0)
AXES = ("dp", "fsdp")
QUAD = 4
BLOCK = 16
CHUNK = 64
LANES = 128
SMALL_ROWS = 32
VMEM_BYTES = 60 * 1024 * 1024
HIDDEN_ROW = 24
BF = jnp.bfloat16
F32 = jnp.float32
VMEM = pl.BlockSpec(memory_space=pltpu.VMEM)
SMEM = pl.BlockSpec(memory_space=pltpu.SMEM)
ANY = pl.BlockSpec(memory_space=pl.ANY)
ROOT_TWO_PI = 0.7978845608028654
CUBIC = 0.044715


def dot(left, right):
    return jnp.dot(left, right, preferred_element_type=F32)


def dot_nt(left, right):
    return lax.dot_general(left, right, (((1,), (1,)), ((), ())), preferred_element_type=F32)


class Input:
    def __init__(self, array, room, sem):
        self.room = room
        self.shape = room.shape
        self.copy = pltpu.make_async_copy(array, room, sem)
        self.copy.start()
        self.there = False

    def __getitem__(self, where):
        if not self.there:
            self.copy.wait()
            self.there = True
        return self.room[where]


class Output:
    def __init__(self, array, room, sem):
        self.array = array
        self.room = room
        self.shape = room.shape
        self.sem = sem
        self.left = False

    def __getitem__(self, where):
        return self.room[where]

    def __setitem__(self, where, value):
        self.room[where] = value

    def put(self, index=None):
        source = self.room if index is None else self.room.at[index]
        target = self.array if index is None else self.array.at[index]
        pltpu.make_async_copy(source, target, self.sem).start()
        self.left = True

    def put_rows(self, rows):
        self.room, self.array = self.room.at[rows], self.array.at[rows]
        self.put()

    def finish(self):
        if not self.left:
            self.put()
        pltpu.make_async_copy(self.room, self.array, self.sem).wait()


def staged_kernel(kernel, scalars, inputs, others, outputs, targets, *refs):
    refs = list(refs)
    sems = refs.pop()
    count = inputs + outputs
    rooms = refs[len(refs) - count :]
    refs = refs[: len(refs) - count]
    at = scalars
    for slot in range(inputs):
        refs[at + slot] = Input(refs[at + slot], rooms[slot], sems.at[slot])
    at += inputs + others
    made = []
    for slot in range(inputs, count):
        place = at + slot - inputs
        refs[place] = Output(refs[place], rooms[slot], sems.at[slot])
        made.append(refs[place])
    kernel(*refs)
    for output in made:
        output.finish()


def load_start(part, place, sems):
    table, arrays, low, number = part
    at = 0
    for slot, array in enumerate(arrays):
        for index in range(array.shape[0]):
            source = array.at[index, low : low + number]
            pltpu.make_async_copy(source, place(table[at]), sems.at[slot]).start()
            at += 1


def load_wait(part, sems):
    table, arrays, low, number = part
    for slot, array in enumerate(arrays):
        whole = array.at[:, low : low + number]
        pltpu.make_async_copy(whole, whole, sems.at[slot]).wait()


def store_start(part, place, sems):
    table, arrays, low, number = part
    half = arrays[0].shape[0]
    for index in range(half):
        for slot in (1, 0):
            target = arrays[slot].at[index, low : low + number]
            source = place(table[slot * half + index])
            pltpu.make_async_copy(source, target, sems.at[slot]).start()


def row_place(scratch, low, high):
    def place(block):
        start = pl.multiple_of(block * BLOCK, BLOCK)
        return scratch.at[low:high, pl.ds(start, BLOCK), :]

    return place


def block_place(scratch):
    return lambda block: scratch.at[block]


def column_sum(values):
    rows, width = values.shape
    return jnp.sum(values.reshape(rows // 8, 8, width), axis=0)


def total_of(sums):
    return jnp.sum(functools.reduce(jnp.add, sums), axis=0, keepdims=True)


def norm_forward(pre_of, length, gain, shift, out_ref, hat_ref, rstd_ref):
    for at in range(0, length, CHUNK):
        rows = slice(at, at + CHUNK)
        pre = pre_of(rows)
        mean = jnp.mean(pre, axis=-1, keepdims=True)
        centred = pre - mean
        spread = jnp.mean(centred * centred, axis=-1, keepdims=True)
        rstd = lax.rsqrt(spread + EPS_NORM)
        hat = centred * rstd
        hat_ref[rows] = hat
        rstd_ref[rows] = jnp.broadcast_to(rstd, (CHUNK, LANES))
        out_ref[rows] = hat * gain + shift
    for ref in (hat_ref, rstd_ref, out_ref):
        if isinstance(ref, Output):
            ref.put()


def norm_backward(grad_ref, hat_ref, rstd_ref, gain, pre_out, low_out):
    length = grad_ref.shape[0]
    sums = ([], [], [])
    for at in range(0, length, CHUNK):
        rows = slice(at, at + CHUNK)
        grad = grad_ref[rows].astype(F32)
        hat = hat_ref[rows]
        sums[0].append(column_sum(grad * hat))
        sums[1].append(column_sum(grad))
        scaled = grad * gain
        one = jnp.mean(scaled, axis=-1, keepdims=True)
        two = jnp.mean(scaled * hat, axis=-1, keepdims=True)
        pre = rstd_ref[rows][:, :1] * (scaled - one - hat * two)
        low = pre.astype(BF)
        pre_out[rows] = pre
        low_out[rows] = low
        sums[2].append(column_sum(low.astype(F32)))
    return [total_of(each) for each in sums]


def lane_mask(rows):
    return lax.broadcasted_iota(jnp.int32, (rows, LANES), 1) < LANES // 2


def stacked_pair(block):
    first = lane_mask(block.shape[0])
    zero = jnp.zeros_like(block)
    return jnp.concatenate([jnp.where(first, block, zero), jnp.where(first, zero, block)], axis=0)


def merged_pair(stacked):
    rows = stacked.shape[0] // 2
    return jnp.where(lane_mask(rows), stacked[:rows], stacked[rows:])


def mask_fill(bias_ref, column_seg, row_seg, causal, transposed):
    length = bias_ref.shape[0]
    column = jnp.broadcast_to(column_seg, (LANES, length)).T
    for at in range(0, length, LANES):
        same = column == row_seg[:, at : at + LANES]
        if causal:
            down = lax.broadcasted_iota(jnp.int32, (length, LANES), 0)
            along = lax.broadcasted_iota(jnp.int32, (length, LANES), 1) + at
            order = (down <= along) if transposed else (along <= down)
            same = same & order
        bias_ref[:, at : at + LANES] = jnp.where(same, 0.0, LOWEST)


def take_parts(refs, layout, tables):
    parts = []
    for slot, (arrays, low, number) in enumerate(layout):
        parts.append((tables[slot], [refs.pop(0) for _ in range(arrays)], low, number))
    return parts


def small_part(part):
    table, arrays, low, number = part
    return table, arrays, low + number, 1


def small_join(blocks_ref):
    count = blocks_ref.shape[0]
    groups = blocks_ref.shape[3] // LANES
    per = count // groups
    vectors = []
    hidden = [[], []]
    for group in range(groups):
        total = blocks_ref[group * per, 0, :8].astype(F32)
        for at in range(group * per + 1, (group + 1) * per):
            total = total + blocks_ref[at, 0, :8].astype(F32)
        columns = [total[:, at : at + LANES] for at in range(0, 4 * LANES, LANES)]
        vectors.append(jnp.concatenate(columns[:3], axis=0))
        for layer in range(2):
            rows = [columns[3][4 * layer + at : 4 * layer + at + 1] for at in range(4)]
            hidden[layer].append(jnp.concatenate(rows, axis=1))
    return jnp.concatenate([jnp.concatenate(vectors, axis=1)] + hidden[0] + hidden[1], axis=0)


def small_split(whole, group):
    lanes = slice(group * LANES, (group + 1) * LANES)
    columns = [whole[at : at + 8, lanes] for at in (0, 8, 16)]
    rows = []
    for layer in range(2):
        row = whole[24 + 4 * layer + group : 25 + 4 * layer + group]
        rows += [row[:, at : at + LANES] for at in range(0, 4 * LANES, LANES)]
    columns.append(jnp.concatenate(rows, axis=0))
    block = jnp.concatenate(columns, axis=1)
    return jnp.concatenate([block, jnp.zeros_like(block)], axis=0).astype(BF)


def attend_forward_kernel(layout, cross, causal, base, joins, *refs):
    refs = list(refs)
    tables = [refs.pop(0) for _ in layout]
    query_seg = refs.pop(0)
    key_seg = refs.pop(0)
    small = None if joins else refs.pop(0)
    rows_ref = refs.pop(0)
    memory_ref = refs.pop(0) if cross else None
    parts = take_parts(refs, layout, tables)
    q_ref, k_ref, v_ref, o_ref, lse_ref, hat_ref, rstd_ref, out_ref = [refs.pop(0) for _ in range(8)]
    if joins:
        small = refs.pop(0)
        blocks_ref = refs.pop()
        extra = small_part(parts[-1])
    w_ref, bias_ref, scores_ref, exponent_ref, largest_ref, mixed_ref, attended_ref, sems = refs
    first = 0
    if joins:
        load_start(extra, lambda block: blocks_ref.at[block], sems.at[len(parts)])
    for slot, part in enumerate(parts):
        load_start(part, row_place(w_ref, first, first + part[3]), sems.at[slot])
        first += part[3]
    length, width = rows_ref.shape
    mask_fill(bias_ref, query_seg[...], key_seg[...], causal, False)
    rows = rows_ref[...].astype(BF)
    keys = memory_ref[...].astype(BF) if cross else rows
    if joins:
        load_wait(extra, sems.at[len(parts)])
        small[...] = small_join(blocks_ref)
        small.put()
    for slot, part in enumerate(parts):
        load_wait(part, sems.at[slot])
    scale = (width // HEADS) ** (-0.5)
    q_ref[...] = (dot(rows, w_ref[0]) + small[base : base + 1]).astype(BF) * jnp.asarray(scale, BF)
    k_ref[...] = dot(keys, w_ref[1]).astype(BF)
    v_ref[...] = (dot(keys, w_ref[2]) + small[base + 1 : base + 2]).astype(BF)
    for ref in (q_ref, k_ref, v_ref):
        ref.put()
    lane = lax.broadcasted_iota(jnp.int32, (LANES, LANES), 1)
    logs = [jnp.zeros((LANES, LANES), F32)] * (length // LANES)
    for pair in range(HEADS // 2):
        lanes = slice(pair * LANES, (pair + 1) * LANES)
        side = pair % 2
        scores_ref[side] = dot_nt(stacked_pair(q_ref[:, lanes]), k_ref[:, lanes])
        for at in range(0, 2 * length, CHUNK):
            chunk = slice(at, at + CHUNK)
            own = slice(at % length, at % length + CHUNK)
            reach = own.start // LANES * LANES + LANES if causal else length
            scores = scores_ref[side, chunk, :reach] + bias_ref[own, :reach]
            largest = jnp.max(scores, axis=-1, keepdims=True)
            exponent_ref[side, chunk, :reach] = jnp.exp(scores - largest).astype(BF)
            if reach < length:
                exponent_ref[side, chunk, reach:] = jnp.zeros((CHUNK, length - reach), BF)
            largest_ref[side, chunk] = jnp.broadcast_to(largest, (CHUNK, LANES))
        values = jnp.concatenate([v_ref[:, lanes], jnp.ones((length, LANES), BF)], axis=1)
        mixed_ref[side] = dot(exponent_ref[side], values)
        for slot, at in enumerate(range(0, length, LANES)):
            outs = []
            for half in range(2):
                chunk = slice(half * length + at, half * length + at + LANES)
                total = mixed_ref[side, chunk, LANES:]
                outs.append(mixed_ref[side, chunk, :LANES] / total)
                log_total = largest_ref[side, chunk] + jnp.log(total)
                logs[slot] = jnp.where(lane == 2 * pair + half, log_total, logs[slot])
            o_ref[at : at + LANES, lanes] = jnp.where(lane_mask(LANES), outs[0], outs[1]).astype(BF)
    for slot, at in enumerate(range(0, length, LANES)):
        lse_ref[:, at : at + LANES] = logs[slot].T[:HEADS]
    o_ref.put()
    lse_ref.put()
    attended_ref[...] = dot(o_ref[...], w_ref[3])
    out_bias = small[base + 2 : base + 3]
    norm_forward(
        lambda rows: rows_ref[rows].astype(F32) + (attended_ref[rows] + out_bias),
        length,
        small[base + 3 : base + 4],
        small[base + 4 : base + 5],
        out_ref,
        hat_ref,
        rstd_ref,
    )


def attend_backward_kernel(layout, cross, causal, base, splits, *refs):
    refs = list(refs)
    tables = [refs.pop(0) for _ in layout]
    out_tables = [refs.pop(0), refs.pop(0)]
    query_seg = refs.pop(0)
    key_seg = refs.pop(0)
    small = refs.pop(0)
    grad_ref = refs.pop(0)
    hat_ref, rstd_ref = refs.pop(0), refs.pop(0)
    rows_ref = refs.pop(0)
    memory_ref = refs.pop(0) if cross else None
    q_ref, k_ref, v_ref, o_ref, lse_ref = [refs.pop(0) for _ in range(5)]
    others = [refs.pop(0) for _ in range(4)] if splits else None
    parts = take_parts(refs, layout, tables)
    rows_out = refs.pop(0)
    memory_out = refs.pop(0) if cross else None
    small_out = None if splits else refs.pop(0)
    targets = [refs.pop(0), refs.pop(0)]
    outs = []
    for slot, table in enumerate(out_tables):
        outs.append((table, targets, slot * QUAD // 2, QUAD // 2))
    blocks_ref = refs.pop() if splits else None
    w_ref, dw_ref, bias_ref, dout_ref, dq_t_ref, dk_ref, dv_ref, kt_ref = refs[:8]
    low_ref, scores_ref, prob_grad_ref, prob_ref, score_grad_ref, sems = refs[8:]
    first = 0
    for slot, part in enumerate(parts):
        load_start(part, row_place(w_ref, first, first + part[3]), sems.at[slot])
        first += part[3]
    length, width = rows_ref.shape
    head = width // HEADS
    scale = head ** (-0.5)
    gain_grad, shift_grad, out_bias = norm_backward(
        grad_ref, hat_ref, rstd_ref, small[base + 3 : base + 4], rows_out, low_ref
    )
    mask_fill(bias_ref, key_seg[...], query_seg[...], causal, True)
    low = low_ref[...]
    for slot, part in enumerate(parts):
        load_wait(part, sems.at[slot])
    dout_ref[...] = dot_nt(low, w_ref[3]).astype(BF)
    dw_ref[3] = dot(o_ref[...].T, low).astype(BF)
    product = dout_ref[...].astype(F32) * o_ref[...].astype(F32)
    high = product.astype(BF)
    rest = (product - high.astype(F32)).astype(BF)
    picker = lax.broadcasted_iota(jnp.int32, (BLOCK, width), 1) // head
    picker = (picker == lax.broadcasted_iota(jnp.int32, (BLOCK, width), 0)).astype(BF)
    row_dots = dot_nt(picker, high) + dot_nt(picker, rest)
    kt_ref[...] = k_ref[...].T
    for pair in range(HEADS // 2):
        lanes = slice(pair * LANES, (pair + 1) * LANES)
        side = pair % 2
        query = q_ref[:, lanes]
        dout = dout_ref[:, lanes]
        scores_ref[side] = dot_nt(stacked_pair(k_ref[:, lanes]), query)
        prob_grad_ref[side] = dot_nt(stacked_pair(v_ref[:, lanes]), dout)
        for at in range(0, 2 * length, CHUNK):
            which = 2 * pair + at // length
            chunk = slice(at, at + CHUNK)
            own = slice(at % length, at % length + CHUNK)
            begin = own.start // LANES * LANES if causal else 0
            shift = bias_ref[own, begin:] - lse_ref[which : which + 1, begin:]
            prob = jnp.exp(scores_ref[side, chunk, begin:] + shift)
            prob_ref[side, chunk, begin:] = prob.astype(BF)
            centred = prob_grad_ref[side, chunk, begin:] - row_dots[which : which + 1, begin:]
            score_grad_ref[side, chunk, begin:] = (prob * centred).astype(BF)
            if begin:
                prob_ref[side, chunk, :begin] = jnp.zeros((CHUNK, begin), BF)
                score_grad_ref[side, chunk, :begin] = jnp.zeros((CHUNK, begin), BF)
        dv_ref[:, lanes] = merged_pair(dot(prob_ref[side], dout)).astype(BF)
        dk_ref[:, lanes] = merged_pair(dot(score_grad_ref[side], query)).astype(BF)
        for half in range(2):
            at = pair * LANES + half * head
            own = slice(half * length, (half + 1) * length)
            dq_t_ref[at : at + head, :] = dot(kt_ref[at : at + head, :], score_grad_ref[side, own])
    query_grad = (dq_t_ref[...] * scale).T.astype(BF)
    key_grad = dk_ref[...]
    value_grad = dv_ref[...]
    turned = rows_ref[...].astype(BF).T
    other = memory_ref[...].astype(BF).T if cross else turned
    dw_ref[2] = dot(other, value_grad).astype(BF)
    store_start(outs[1], row_place(dw_ref, QUAD // 2, QUAD), sems.at[1])
    dw_ref[0] = dot(turned, query_grad).astype(BF)
    dw_ref[1] = dot(other, key_grad).astype(BF)
    store_start(outs[0], row_place(dw_ref, 0, QUAD // 2), sems.at[0])
    rows_back = rows_out[...] + dot_nt(query_grad, w_ref[0])
    memory_back = dot_nt(key_grad, w_ref[1]) + dot_nt(value_grad, w_ref[2])
    if cross:
        rows_out[...] = rows_back
        memory_out[...] = memory_back
        memory_out.put()
    else:
        rows_out[...] = rows_back + memory_back
    rows_out.put()
    query_bias = total_of([column_sum(query_grad.astype(F32))])
    value_bias = total_of([column_sum(value_grad.astype(F32))])
    spare = jnp.zeros((3, width), F32)
    own = jnp.concatenate(
        [query_bias, value_bias, out_bias, gain_grad, shift_grad, spare], axis=0
    )
    if splits:
        enc_feed, self_attend, cross_attend, dec_feed = [other[...] for other in others]
        whole = small_rows(own, enc_feed, self_attend, cross_attend, dec_feed)
        groups = blocks_ref.shape[0]
        for group in range(groups):
            blocks_ref[group, 0] = small_split(whole, group)
        extra = small_part(outs[-1])
        per = 2 * extra[1][0].shape[0] // groups
        store_start(extra, lambda block: blocks_ref.at[block // per], sems.at[2])
        load_wait(extra, sems.at[2])
    else:
        small_out[...] = own
    for slot, part in enumerate(outs):
        load_wait(part, sems.at[slot])


def small_rows(enc_attend, enc_feed, self_attend, cross_attend, dec_feed):
    return jnp.concatenate(
        [
            enc_attend[:5],
            enc_feed[:3],
            self_attend[:5],
            cross_attend[:5],
            dec_feed[:3],
            dec_feed[7:],
            dec_feed[7:],
            dec_feed[7:],
            enc_feed[3:7],
            dec_feed[3:7],
        ],
        axis=0,
    )


def gelu_parts(pre):
    square = pre * pre
    curve = jnp.tanh(ROOT_TWO_PI * pre * (1.0 + CUBIC * square))
    half = 0.5 * pre
    rise = 0.5 + 0.5 * curve
    bend = ROOT_TWO_PI * (1.0 + 3.0 * CUBIC * square)
    return pre * rise, rise + half * (1.0 - curve * curve) * bend


def chunk_of(ref, index):
    number = ref.shape[0] // QUAD
    part = ref[index * number : (index + 1) * number]
    return part.reshape(number * ref.shape[1] * ref.shape[2], ref.shape[3])


def feed_forward_steps(small, base, hidden_at, rows_ref, up_ref, down_ref, active_ref, slope_ref, pre_ref, sum_ref):
    rows = rows_ref[...].astype(BF)
    length = rows.shape[0]
    for index in range(QUAD):
        at = hidden_at + index
        side = index % 2
        pre_ref[side] = dot(rows, up_ref[index])
        bias = small[at : at + 1]
        for at in range(0, length, CHUNK // 2):
            chunk = slice(at, at + CHUNK // 2)
            active, slope = gelu_parts(pre_ref[side, chunk] + bias)
            active_ref[index, chunk] = active.astype(BF)
            slope_ref[index, chunk] = slope
        for ref in (active_ref, slope_ref):
            if isinstance(ref, Output):
                ref.put(index)
    wide = jnp.concatenate([active_ref[index] for index in range(QUAD)], axis=1)
    number, _, _, width = down_ref.shape
    sum_ref[...] = dot(wide, down_ref[...].reshape(QUAD * width, width))
    out_bias = small[base : base + 1]
    return lambda rows: rows_ref[rows] + (sum_ref[rows] + out_bias)


def feed_backward_steps(
    pre_grad, low_ref, rows_ref, up_ref, down_ref, active_ref, slope_ref, dup_ref, ddown_ref, rows_out, back_ref, outs, sems
):
    low = low_ref[...]
    length = low.shape[0]
    number = ddown_ref.shape[0] // QUAD
    for index in range(QUAD):
        down_grad = dot(active_ref[index].T, low).astype(BF)
        ddown_ref[index * number : (index + 1) * number] = down_grad.reshape(
            (number,) + ddown_ref.shape[1:]
        )
    store_start(outs[1], block_place(ddown_ref), sems.at[1])
    turned = rows_ref[...].astype(BF).T
    hidden_grads = []
    hiddens = []
    for index in range(QUAD):
        side = index % 2
        back_ref[side] = dot_nt(low, chunk_of(down_ref, index))
        sums = []
        parts = []
        for at in range(0, length, CHUNK):
            chunk = slice(at, at + CHUNK)
            hidden = (back_ref[side, chunk] * slope_ref[index, chunk]).astype(BF)
            sums.append(column_sum(hidden.astype(F32)))
            parts.append(hidden)
        hidden = jnp.concatenate(parts, axis=0)
        hidden_grads.append(total_of(sums))
        dup_ref[index] = dot(turned, hidden).astype(BF)
        hiddens.append(hidden)
    store_start(outs[0], row_place(dup_ref, 0, QUAD), sems.at[0])
    total = pre_grad[...]
    for index in range(QUAD):
        total = total + dot_nt(hiddens[index], up_ref[index])
    rows_out[...] = total
    rows_out.put()
    return hidden_grads


def load_feed(parts, up_ref, down_ref, sems):
    load_start(parts[0], row_place(up_ref, 0, QUAD), sems.at[0])
    load_start(parts[1], block_place(down_ref), sems.at[1])


def wait_feed(parts, sems):
    for slot, part in enumerate(parts):
        load_wait(part, sems.at[slot])


def feed_outs(refs, tables):
    arrays = [refs.pop(0), refs.pop(0)]
    return [(tables[slot], arrays, slot * QUAD, QUAD) for slot in range(2)]


def feed_small(out_bias, gain_grad, shift_grad, hidden_grads):
    spare = jnp.zeros_like(out_bias)
    return jnp.concatenate([out_bias, gain_grad, shift_grad] + hidden_grads + [spare], axis=0)


def feed_forward_kernel(layout, base, hidden_at, *refs):
    refs = list(refs)
    tables = [refs.pop(0), refs.pop(0)]
    small, rows_ref = refs.pop(0), refs.pop(0)
    parts = take_parts(refs, layout, tables)
    out_ref, hat_ref, rstd_ref, active_ref, slope_ref, up_ref, down_ref = refs[:7]
    pre_ref, sum_ref, sems = refs[7:]
    load_feed(parts, up_ref, down_ref, sems)
    wait_feed(parts, sems)
    pre_of = feed_forward_steps(
        small, base, hidden_at, rows_ref, up_ref, down_ref, active_ref, slope_ref, pre_ref, sum_ref
    )
    gain, shift = small[base + 1 : base + 2], small[base + 2 : base + 3]
    norm_forward(pre_of, rows_ref.shape[0], gain, shift, out_ref, hat_ref, rstd_ref)


def feed_backward_kernel(layout, base, *refs):
    refs = list(refs)
    tables = [refs.pop(0), refs.pop(0)]
    out_tables = [refs.pop(0), refs.pop(0)]
    small, grad_ref, hat_ref, rstd_ref, rows_ref = [refs.pop(0) for _ in range(5)]
    active_ref, slope_ref = refs.pop(0), refs.pop(0)
    parts = take_parts(refs, layout, tables)
    rows_out, small_out = refs.pop(0), refs.pop(0)
    outs = feed_outs(refs, out_tables)
    up_ref, down_ref, dup_ref, ddown_ref, low_ref, back_ref, sems, out_sems = refs
    load_feed(parts, up_ref, down_ref, sems)
    gain_grad, shift_grad, out_bias = norm_backward(
        grad_ref, hat_ref, rstd_ref, small[base + 1 : base + 2], rows_out, low_ref
    )
    wait_feed(parts, sems)
    hidden_grads = feed_backward_steps(
        rows_out,
        low_ref,
        rows_ref,
        up_ref,
        down_ref,
        active_ref,
        slope_ref,
        dup_ref,
        ddown_ref,
        rows_out,
        back_ref,
        outs,
        out_sems,
    )
    small_out[...] = feed_small(out_bias, gain_grad, shift_grad, hidden_grads)
    wait_feed(outs, out_sems)


def feed_both_kernel(layout, base, hidden_at, *refs):
    refs = list(refs)
    tables = [refs.pop(0), refs.pop(0)]
    out_tables = [refs.pop(0), refs.pop(0)]
    small, rows_ref, grad_ref = [refs.pop(0) for _ in range(3)]
    parts = take_parts(refs, layout, tables)
    out_ref, rows_out, small_out = [refs.pop(0) for _ in range(3)]
    outs = feed_outs(refs, out_tables)
    up_ref, down_ref, dup_ref, ddown_ref, low_ref, back_ref, sum_ref = refs[:7]
    active_ref, slope_ref, hat_ref, rstd_ref, sems, out_sems = refs[7:]
    load_feed(parts, up_ref, down_ref, sems)
    wait_feed(parts, sems)
    pre_of = feed_forward_steps(
        small, base, hidden_at, rows_ref, up_ref, down_ref, active_ref, slope_ref, back_ref, sum_ref
    )
    gain, shift = small[base + 1 : base + 2], small[base + 2 : base + 3]
    norm_forward(pre_of, rows_ref.shape[0], gain, shift, out_ref, hat_ref, rstd_ref)
    gain_grad, shift_grad, out_bias = norm_backward(
        grad_ref, hat_ref, rstd_ref, gain, rows_out, low_ref
    )
    hidden_grads = feed_backward_steps(
        rows_out,
        low_ref,
        rows_ref,
        up_ref,
        down_ref,
        active_ref,
        slope_ref,
        dup_ref,
        ddown_ref,
        rows_out,
        back_ref,
        outs,
        out_sems,
    )
    small_out[...] = feed_small(out_bias, gain_grad, shift_grad, hidden_grads)
    wait_feed(outs, out_sems)


def shaped(shape, dtype=F32):
    return jax.ShapeDtypeStruct(shape, dtype)


def call(
    kernel, scalars, inputs, others, outs, targets, scratch, flops, moved, limit=VMEM_BYTES, held=0
):
    rooms = [pltpu.VMEM(array.shape, array.dtype) for array in list(inputs) + list(outs)]
    first = len(scalars) + len(inputs) + len(others) - held
    aliases = {first + slot: len(outs) + slot for slot in range(held)}
    return pl.pallas_call(
        functools.partial(
            staged_kernel, kernel, len(scalars), len(inputs), len(others), len(outs), len(targets)
        ),
        out_shape=list(outs) + list(targets),
        in_specs=[SMEM] * len(scalars) + [ANY] * (len(inputs) + len(others)),
        out_specs=[ANY] * (len(outs) + len(targets)),
        scratch_shapes=scratch + rooms + [pltpu.SemaphoreType.DMA((len(rooms),))],
        input_output_aliases=aliases,
        cost_estimate=pl.CostEstimate(flops=flops, bytes_accessed=moved, transcendentals=0),
        compiler_params=pltpu.CompilerParams(vmem_limit_bytes=limit),
    )(*scalars, *inputs, *others)


def layout_of(parts):
    return [(len(arrays), low, number) for _, arrays, low, number in parts]


def arrays_of(parts):
    return [array for part in parts for array in part[1]]


def most(parts):
    return max(len(part[1]) for part in parts)


def halves(width, number):
    return [shaped((width // BLOCK // 2, number, BLOCK, width), BF)] * 2


def attend_forward(segments, small, base, rows, memory, parts, causal):
    length, width = rows.shape
    cross = memory is not None
    joins = small is None
    scalars = [part[0] for part in parts]
    inputs = list(segments) + ([] if joins else [small]) + [rows] + ([memory] if cross else [])
    outs = [shaped((length, width), BF)] * 4 + [shaped((HEADS, length))]
    outs += [shaped((length, width)), shaped((length, LANES)), shaped((length, width))]
    outs += [shaped((SMALL_ROWS, width))] if joins else []
    scratch = [
        pltpu.VMEM((QUAD, width, width), BF),
        pltpu.VMEM((length, length), F32),
        pltpu.VMEM((2, 2 * length, length), F32),
        pltpu.VMEM((2, 2 * length, length), BF),
        pltpu.VMEM((2, 2 * length, LANES), F32),
        pltpu.VMEM((2, 2 * length, 2 * LANES), F32),
        pltpu.VMEM((length, width), F32),
        pltpu.SemaphoreType.DMA((len(parts) + 1, most(parts))),
    ]
    scratch += [pltpu.VMEM((width // BLOCK, 1, BLOCK, width), BF)] if joins else []
    kernel = functools.partial(attend_forward_kernel, layout_of(parts), cross, causal, base, joins)
    flops = 8 * length * width * width + 16 * length * length * width
    return call(kernel, scalars, inputs, arrays_of(parts), outs, [], scratch, flops, 8_000_000)


def attend_backward(
    out_tables, segments, small, base, grad, kept, rows, memory, parts, causal, others
):
    length, width = rows.shape
    cross = memory is not None
    splits = others is not None
    q, k, v, o, lse, hat, rstd = kept[:7]
    scalars = [part[0] for part in parts] + list(out_tables)
    inputs = list(segments) + [small, grad, hat, rstd, rows]
    inputs += ([memory] if cross else []) + [q, k, v, o, lse] + list(others or ())
    outs = [shaped((length, width))] * (2 if cross else 1)
    outs += [] if splits else [shaped((8, width))]
    targets = halves(width, QUAD + (1 if splits else 0))
    scratch = [
        pltpu.VMEM((QUAD, width, width), BF),
        pltpu.VMEM((QUAD, width, width), BF),
        pltpu.VMEM((length, length), F32),
        pltpu.VMEM((length, width), BF),
        pltpu.VMEM((width, length), F32),
        pltpu.VMEM((length, width), BF),
        pltpu.VMEM((length, width), BF),
        pltpu.VMEM((width, length), BF),
        pltpu.VMEM((length, width), BF),
        pltpu.VMEM((2, 2 * length, length), F32),
        pltpu.VMEM((2, 2 * length, length), F32),
        pltpu.VMEM((2, 2 * length, length), BF),
        pltpu.VMEM((2, 2 * length, length), BF),
        pltpu.SemaphoreType.DMA((3, 2)),
    ]
    scratch += [pltpu.VMEM((width // LANES, 1, BLOCK, width), BF)] if splits else []
    kernel = functools.partial(
        attend_backward_kernel, layout_of(parts), cross, causal, base, splits
    )
    flops = 16 * length * width * width + 40 * length * length * width
    arrays = arrays_of(parts)
    results = list(call(kernel, scalars, inputs, arrays, outs, targets, scratch, flops, 12_000_000))
    rows_grad = results.pop(0)
    memory_grad = results.pop(0) if cross else None
    small_grad = None if splits else results.pop(0)
    return rows_grad, memory_grad, small_grad, results


def feed_scratch(width, grads):
    number = width // BLOCK
    once = [pltpu.VMEM((QUAD, width, width), BF), pltpu.VMEM((number, QUAD, BLOCK, width), BF)]
    return once * (2 if grads else 1)


def feed_forward(small, base, hidden_at, rows, parts):
    length, width = rows.shape
    scalars = [part[0] for part in parts]
    outs = [shaped((length, width)), shaped((length, width)), shaped((length, LANES))]
    outs += [shaped((QUAD, length, width), BF), shaped((QUAD, length, width))]
    scratch = feed_scratch(width, False)
    scratch += [pltpu.VMEM((2, length, width), F32), pltpu.VMEM((length, width), F32)]
    scratch += [pltpu.SemaphoreType.DMA((2, most(parts)))]
    kernel = functools.partial(feed_forward_kernel, layout_of(parts), base, hidden_at)
    flops = 16 * length * width * width
    arrays = arrays_of(parts)
    return call(kernel, scalars, [small, rows], arrays, outs, [], scratch, flops, 10_000_000)


def feed_backward(out_tables, small, base, grad, kept, rows, parts):
    length, width = rows.shape
    hat, rstd, active, slope = kept[1:]
    scalars = [part[0] for part in parts] + list(out_tables)
    inputs = [small, grad, hat, rstd, rows, active, slope]
    outs = [shaped((length, width)), shaped((8, width))]
    targets = halves(width, 2 * QUAD)
    scratch = feed_scratch(width, True)
    scratch += [pltpu.VMEM((length, width), BF), pltpu.VMEM((2, length, width), F32)]
    scratch += [pltpu.SemaphoreType.DMA((2, most(parts))), pltpu.SemaphoreType.DMA((2, 2))]
    kernel = functools.partial(feed_backward_kernel, layout_of(parts), base)
    flops = 32 * length * width * width
    arrays = arrays_of(parts)
    results = call(kernel, scalars, inputs, arrays, outs, targets, scratch, flops, 14_000_000)
    return results[0], results[1], results[2:4]


def feed_both(out_tables, small, base, hidden_at, rows, grad, parts):
    length, width = rows.shape
    scalars = [part[0] for part in parts] + list(out_tables)
    outs = [shaped((length, width)), shaped((length, width)), shaped((8, width))]
    targets = halves(width, 2 * QUAD)
    scratch = feed_scratch(width, True) + [
        pltpu.VMEM((length, width), BF),
        pltpu.VMEM((2, length, width), F32),
        pltpu.VMEM((length, width), F32),
        pltpu.VMEM((QUAD, length, width), BF),
        pltpu.VMEM((QUAD, length, width), F32),
        pltpu.VMEM((length, width), F32),
        pltpu.VMEM((length, LANES), F32),
        pltpu.SemaphoreType.DMA((2, most(parts))),
        pltpu.SemaphoreType.DMA((2, 2)),
    ]
    kernel = functools.partial(feed_both_kernel, layout_of(parts), base, hidden_at)
    flops = 48 * length * width * width
    arrays = arrays_of(parts)
    results = call(kernel, scalars, [small, rows, grad], arrays, outs, targets, scratch, flops, 12_000_000)
    return results[0], results[1], results[2], results[3:5]


def first_kernel(
    at_ref,
    vector_ref,
    hidden_ref,
    square_ref,
    tall_ref,
    deep_ref,
    one_ref,
    two_ref,
    three_ref,
    turn_ref,
    line_ref,
):
    at = at_ref[0]
    width = square_ref.shape[2]
    turn_ref[...] = jnp.zeros_like(turn_ref)
    lanes, rows = vector_ref.shape
    turn_ref[pl.ds(pl.multiple_of(at * lanes, lanes), lanes), :rows] = vector_ref[...]
    upright = turn_ref[...].T
    line_ref[...] = jnp.zeros_like(line_ref)
    layers, lanes = hidden_ref.shape
    per = LANES // lanes
    for layer in range(layers):
        row = jnp.concatenate([hidden_ref[layer : layer + 1]] * per, axis=1)
        lane = lax.broadcasted_iota(jnp.int32, row.shape, 1) // lanes
        row = jnp.where(lane == at % per, row, 0.0)
        line_ref[pl.ds(4 * layer + at // per, 1), :] = row
    columns = [upright[low : low + 8] for low in (0, 8, 16)] + [line_ref[...]]
    block = jnp.concatenate(columns, axis=1)
    small = jnp.concatenate([block, jnp.zeros_like(block)], axis=0)
    tall = []
    deep = []
    for layer in range(2):
        for index in range(QUAD):
            lanes = slice(index * width, (index + 1) * width)
            tall.append(tall_ref[layer, :, lanes])
            deep.append(deep_ref[layer, index * BLOCK : (index + 1) * BLOCK])
    square = [square_ref[index] for index in range(3 * QUAD)]
    cut = QUAD // 2
    groups = [
        square[:cut] + tall[:QUAD] + square[cut:QUAD] + [small] + deep[:QUAD],
        square[QUAD:],
        tall[QUAD:] + deep[QUAD:],
    ]
    for out_ref, group in zip((one_ref, two_ref, three_ref), groups):
        for slot, block in enumerate(group):
            out_ref[0, slot] = block.astype(BF)
        out_ref.put()


def first_arrays(at, square, tall, deep, vectors, hidden):
    width = square.shape[2]
    outs = [
        shaped((1, 3 * QUAD + 1, BLOCK, width), BF),
        shaped((1, 2 * QUAD, BLOCK, width), BF),
        shaped((1, 2 * QUAD, BLOCK, width), BF),
    ]
    scratch = [pltpu.VMEM((LANES, LANES), F32), pltpu.VMEM((8, LANES), F32)]
    inputs = [vectors.T, hidden, square, tall, deep]
    return call(first_kernel, [at], inputs, [], outs, [], scratch, 0, 4_000_000)


def update_kernel(plan, count, slots, ends, at_ref, *refs):
    refs = list(refs)
    params = [dict(zip(slots, [refs.pop(0) for _ in slots])) for _ in range(3)]
    arrays = [refs.pop(0) for _ in range(count)]
    if ends:
        refs = refs[4:]
    staged = slots[1:] if ends else slots
    outs = [dict(zip(staged, [refs.pop(0) for _ in staged])) for _ in range(4)]
    if ends:
        targets = [refs.pop(0) for _ in range(4)]
        rooms = [refs.pop(0) for _ in range(4)]
        for kind in range(4):
            outs[kind][0] = rooms[kind]
    buffers, turn_ref, line_ref, sems = refs
    at = at_ref[0]
    starts = []
    for width, pieces, _ in plan:
        for index, low in pieces:
            array = arrays[index]
            array = array if len(array.shape) == 3 else array.at[0]
            source = array.at[low : low + width]
            copy = pltpu.make_async_copy(source, buffers.at[len(starts), :width], sems.at[len(starts)])
            copy.start()
            starts.append(copy)

    def update(slot, where, gradient):
        results = adam_update(
            params[0][slot][where],
            gradient,
            params[1][slot][where],
            params[2][slot][where],
            RATES[slot],
            DECAYS[slot],
        )
        for kind in range(4):
            outs[kind][slot][where] = results[kind]

    def update_small(gradient):
        turn_ref[...] = jnp.zeros_like(turn_ref)
        for column in range(3):
            lanes = slice(column * LANES, (column + 1) * LANES)
            turn_ref[8 * column : 8 * column + 8, :] = gradient[:8, lanes]
        turn_ref[...] = turn_ref[...].T
        lanes, rows = params[0][3].shape
        share = turn_ref[pl.ds(pl.multiple_of(at * lanes, lanes), lanes), :][:, :rows]
        update(3, slice(None), share)
        line_ref[...] = gradient[:8, 3 * LANES :]
        layers, lanes = params[0][4].shape
        per = LANES // lanes
        for layer in range(layers):
            row = line_ref[pl.ds(4 * layer + at // per, 1), :]
            share = row[:, :lanes]
            for part in range(1, per):
                other = row[:, part * lanes : (part + 1) * lanes]
                share = jnp.where(at % per == part, other, share)
            update(4, slice(layer, layer + 1), share)

    begin = 0
    for done, (width, pieces, targeted) in enumerate(plan):
        for index in range(len(pieces)):
            starts[begin + index].wait()
        for sub, (slot, where) in enumerate(targeted):
            gradient = buffers[begin, sub].astype(F32)
            for index in range(1, len(pieces)):
                gradient = gradient + buffers[begin + index, sub].astype(F32)
            if slot < 3:
                update(slot, where, gradient)
            else:
                update_small(gradient)
        begin += len(pieces)
        for slot in range(0 if ends else 3):
            with_slot = [at for at, each in enumerate(plan) if each[2][0][0] == slot]
            if with_slot[-1] == done:
                for kind in range(4):
                    if slot:
                        outs[kind][slot].put()
                    else:
                        outs[kind][slot].put_rows(slice(QUAD, 3 * QUAD))
    if ends:
        copies = []
        for kind in range(4):
            target = targets[kind].at[:QUAD]
            copies.append(pltpu.make_async_copy(rooms[kind], target, sems.at[kind]))
            copies[-1].start()
        for copy in copies:
            copy.wait()


def update_call(at, segments, slots, params, before):
    ends = before is not None
    arrays = []
    plan = []
    for width, pieces, targets in segments:
        entry = []
        for array, low in pieces:
            found = [place for place, other in enumerate(arrays) if other is array]
            if not found:
                arrays.append(array)
            entry.append((found[0] if found else len(arrays) - 1, low))
        plan.append((width, entry, targets))
    flat = [group[slot] for group in params for slot in slots]
    staged = [params[0][slot] for slot in (slots[1:] if ends else slots)]
    outs = [shaped(array.shape) for array in staged] * 3
    outs += [shaped(array.shape, BF) for array in staged]
    count = sum(len(entry[1]) for entry in plan)
    block = params[0][0].shape[1:]
    scratch = []
    if ends:
        scratch += [pltpu.VMEM((QUAD,) + block, F32)] * 3 + [pltpu.VMEM((QUAD,) + block, BF)]
    scratch += [
        pltpu.VMEM((count, max(entry[0] for entry in plan)) + block, BF),
        pltpu.VMEM((LANES, LANES), F32),
        pltpu.VMEM((8, LANES), F32),
        pltpu.SemaphoreType.DMA((count,)),
    ]
    kernel = functools.partial(update_kernel, plan, len(arrays), slots, ends)
    held = list(before) if ends else []
    targets = [shaped(array.shape, array.dtype) for array in held]
    return call(
        kernel,
        [at],
        flat,
        arrays + held,
        outs,
        targets,
        scratch,
        0,
        2_000_000 if ends else 8_000_000,
        VMEM_BYTES // 2,
        len(held),
    )


def last_update(at, early, late, masters, firsts, seconds):
    params = [list(group) for group in (masters, firsts, seconds)]
    for group in params:
        group[3] = group[3].T
    main = list(update_call(at, early, (0, 1, 2), params, None))
    rest = list(update_call(at, late, (0, 3, 4), params, [main[3 * kind] for kind in range(4)]))
    made = []
    for kind in range(4):
        made += [rest[8 + kind], main[3 * kind + 1], main[3 * kind + 2]]
        made += [rest[2 * kind].T, rest[2 * kind + 1]]
    return made


def tie(*arrays):
    return lax.optimization_barrier(arrays)


class Direct:
    def __init__(self, axis_sizes):
        outer, inner = axis_sizes
        self.count = outer * inner
        inner_bits = inner.bit_length() - 1
        bits = self.count.bit_length() - 1
        core = [inner_bits]
        across = list(range(inner_bits + 1, bits))
        up = [0]
        along = list(range(1, inner_bits))
        self.orders = {
            "a": core + across + up + along,
            "b": core + up + across + along,
            "c": core + along + across + up,
            "d": core + along + up + across,
        }
        self.place = lax.axis_index(AXES)

    def hop(self, array, bit):
        return lax.ppermute(array, AXES, [(at, at ^ (1 << bit)) for at in range(self.count)])

    def table(self, name):
        order = self.orders[name]
        index = jnp.arange(self.count, dtype=jnp.int32)
        block = jnp.zeros_like(index)
        for at, bit in enumerate(order):
            block = block | (((index >> (len(order) - 1 - at)) & 1) << bit)
        return block ^ self.place

    def arrive(self, array, name, step):
        return self.hop(array, self.orders[name][::-1][step])

    def finish(self, array, name):
        return [array, self.hop(array, self.orders[name][0])]


def grown(arrays, arrivals):
    return [jnp.concatenate(pair, axis=0) for pair in zip(arrays, arrivals)]


class Sum:
    def __init__(self, net, name, segments, done, blocks):
        self.net = net
        self.name = name
        self.segments = segments
        self.done = done
        self.blocks = blocks

    def bit(self):
        return self.net.orders[self.name][self.done]

    def split(self, names):
        return [
            Sum(self.net, name, [segment], self.done, self.blocks)
            for name, segment in zip(names, self.segments)
        ]


def core_hop(net, pair, widths):
    keep, send = pair
    arrived = net.hop(send, net.orders["a"][0])
    low = 0
    segments = []
    for width in widths:
        segments.append((width, [(keep, low), (arrived, low)]))
        low += width
    return Sum(net, "a", segments, 1, keep.shape[0])


def combine_kernel(plan, count, outputs, *refs):
    arrays, refs = refs[:count], refs[count:]
    outs, buffers, sems = refs[:outputs], refs[outputs:-1], refs[-1]
    starts = []
    for _, _, held, number, width, pieces in plan:
        begin = 0 if held is not None else number
        for index, low in pieces:
            array = arrays[index]
            if len(array.shape) == 3:
                source = array.at[low + begin * width : low + 2 * number * width]
            else:
                source = array.at[begin : 2 * number, low : low + width]
            copy = pltpu.make_async_copy(source, buffers[len(starts)], sems.at[len(starts)])
            copy.start()
            starts.append(copy)
    begin = 0
    for slot, first, held, number, width, pieces in plan:
        for index in range(begin, begin + len(pieces)):
            starts[index].wait()
        mine = buffers[begin : begin + len(pieces)]
        jobs = [(slot, first, 0)] if held is None else [(slot, first, number), (outputs - 1, held, 0)]
        for out, place, skip in jobs:

            for block in range(number):
                value = None
                for buffer in mine:
                    flat = len(buffer.shape) == 3
                    at = block + skip
                    part = buffer[at * width : (at + 1) * width] if flat else buffer[at]
                    value = part.astype(F32) if value is None else value + part.astype(F32)
                outs[out][place + block * width : place + (block + 1) * width] = value.astype(BF)
        begin += len(pieces)


class Round:
    def __init__(self, sums, *tokens, limit=VMEM_BYTES // 3):
        self.net = sums[0].net
        self.sums = sums
        self.bits = sorted({item.bit() for item in sums})
        arrays = []
        plan = []
        sizes = [0] * len(self.bits) + [0]
        self.places = []
        block = None
        for item in sums:
            slot = self.bits.index(item.bit())
            number = item.blocks // 2
            holds = item.done > 1
            places = []
            for width, pieces in item.segments:
                entry = []
                for array, low in pieces:
                    found = [at for at, other in enumerate(arrays) if other is array]
                    if not found:
                        arrays.append(array)
                    entry.append((found[0] if found else len(arrays) - 1, low))
                    block = array.shape[-2:]
                held = sizes[-1] if holds else None
                plan.append((slot, sizes[slot], held, number, width, entry))
                places.append((sizes[slot], held))
                sizes[slot] += number * width
                sizes[-1] += number * width if holds else 0
            self.places.append((slot, places))
        tied = list(tie(*arrays, *tokens))[: len(arrays)] if tokens else arrays
        scratch = []
        moved = 0
        for _, _, held, number, width, entry in plan:
            both = number if held is None else 2 * number
            moved += both * width * (len(entry) + 1) * 16384
            for index, _ in entry:
                flat = len(arrays[index].shape) == 3
                shape = (both * width,) if flat else (both, width)
                scratch.append(pltpu.VMEM(shape + block, BF))
        if not sizes[-1]:
            sizes.pop()
        self.sends = pl.pallas_call(
            functools.partial(combine_kernel, plan, len(tied), len(sizes)),
            out_shape=[shaped((size,) + block, BF) for size in sizes],
            in_specs=[ANY] * len(tied),
            out_specs=[VMEM] * len(sizes),
            scratch_shapes=scratch + [pltpu.SemaphoreType.DMA((len(scratch),))],
            cost_estimate=pl.CostEstimate(flops=0, bytes_accessed=moved, transcendentals=0),
            compiler_params=pltpu.CompilerParams(vmem_limit_bytes=limit),
        )(*tied)

    def before(self, *arrays):
        tied = tie(*arrays, *self.sends)
        self.sends = list(tied[len(arrays) :])
        return tied[: len(arrays)]

    def go(self):
        arrived = [self.net.hop(send, bit) for send, bit in zip(self.sends, self.bits)]
        for item, (slot, places) in zip(self.sums, self.places):
            made = []
            for (width, pieces), (place, held) in zip(item.segments, places):
                stay = pieces if held is None else [(self.sends[-1], held)]
                made.append((width, stay + [(arrived[slot], place)]))
            item.segments = made
            item.done += 1
            item.blocks //= 2
        return arrived


def adam_update(weight, gradient, first, second, rate, decay):
    first_new = BETA_ONE * first + (1.0 - BETA_ONE) * gradient
    second_new = BETA_TWO * second + (1.0 - BETA_TWO) * gradient * gradient
    first_hat = first_new / (1.0 - BETA_ONE**STEP)
    second_hat = second_new / (1.0 - BETA_TWO**STEP)
    weight_new = weight - rate * (first_hat / (jnp.sqrt(second_hat) + EPS_ADAM) + decay * weight)
    return (weight_new, first_new, second_new, weight_new.astype(BF))


def gather_small(vectors, hidden):
    whole = lax.all_gather(vectors.astype(BF), AXES, axis=1, tiled=True)
    deep = lax.all_gather(hidden.astype(BF), AXES, axis=1, tiled=True)
    whole = jnp.pad(whole, ((0, HIDDEN_ROW - whole.shape[0]), (0, 0)))
    return jnp.concatenate([whole, deep.reshape(-1, whole.shape[1])], axis=0).astype(F32)


def scatter_small(grads, vectors, hidden, place, count):
    whole = lax.psum(small_rows(*grads), AXES)
    rows, lanes = vectors.shape
    first = lax.dynamic_slice_in_dim(whole[:rows], place * lanes, lanes, axis=1)
    layers, lanes = hidden.shape
    deep = whole[HIDDEN_ROW:].reshape(layers, -1)
    return first, lax.dynamic_slice_in_dim(deep, place * lanes, lanes, axis=1)


def gather_whole(attention, up, down):
    width = attention.shape[2]
    number = width // BLOCK
    square = lax.all_gather(attention, AXES, axis=1, tiled=True)
    square = square.reshape(-1, QUAD, number, BLOCK, width).transpose(0, 2, 1, 3, 4)
    tall = lax.all_gather(up, AXES, axis=1, tiled=True)
    tall = tall.reshape(2, number, BLOCK, QUAD, width).transpose(0, 1, 3, 2, 4)
    deep = lax.all_gather(down, AXES, axis=1, tiled=True).reshape(2, number, QUAD, BLOCK, width)
    half = number // 2
    quads = [square[0], tall[0], deep[0], square[1], square[2], tall[1], deep[1]]
    return [(quad[:half], quad[half:]) for quad in quads]


def scatter_whole(quads):
    joined = [jnp.concatenate(pair, axis=0).astype(F32) for pair in quads]
    number, _, _, width = joined[0].shape
    square = jnp.stack([joined[0], joined[3], joined[4]])
    square = square.transpose(0, 2, 1, 3, 4).reshape(3 * QUAD, width, width)
    tall = jnp.stack([joined[1], joined[5]]).transpose(0, 1, 3, 2, 4)
    tall = tall.reshape(2, width, QUAD * width)
    deep = jnp.stack([joined[2], joined[6]]).reshape(2, QUAD * width, width)
    return [
        lax.psum_scatter(part, AXES, scatter_dimension=1, tiled=True)
        for part in (square, tall, deep)
    ]


def direct_step(pairs, source, target, grad, masters, firsts, seconds, axis_sizes):
    net = Direct(axis_sizes)
    source_pair, target_pair, cross_pair = pairs
    a, b = net.table("a"), net.table("b")
    cut = QUAD // 2
    at = (net.place % (net.count * LANES // source.shape[1])).astype(jnp.int32).reshape(1)

    one, two, three = first_arrays(at, *masters)
    up_two, down_two = three[:, :QUAD], three[:, QUAD:]
    for step in (0, 1):
        more = tie(
            net.arrive(one, "a", step),
            net.arrive(up_two, "c", step),
            net.arrive(down_two, "d", step),
        )
        one, up_two, down_two = grown((one, up_two, down_two), more)
    three = jnp.concatenate([up_two, down_two], axis=1)
    left, right = one[:, : cut + QUAD], one[:, cut + QUAD :]
    two, three, left, right = tie(two, three, left, right)
    left, right, two = grown(
        (left, right, two),
        tie(net.arrive(left, "a", 2), net.arrive(right, "b", 2), net.arrive(two, "a", 0)),
    )
    left, right, two, three = grown(
        (left, right, two, three),
        tie(
            net.arrive(left, "a", 3),
            net.arrive(right, "b", 3),
            net.arrive(two, "a", 1),
            net.arrive(three, "c", 2),
        ),
    )
    self_w, cross_w = two[:, :QUAD], two[:, QUAD:]
    more = tie(
        net.hop(left, net.orders["a"][0]),
        net.hop(right, net.orders["b"][0]),
        net.arrive(self_w, "a", 2),
        net.arrive(cross_w, "b", 2),
    )
    left, right = [left, more[0]], [right, more[1]]
    self_w, cross_w = grown((self_w, cross_w), more[2:])
    source, self_w, cross_w, three = tie(source, self_w, cross_w, three)
    more = [
        net.arrive(self_w, "a", 3),
        net.arrive(cross_w, "b", 3),
        net.arrive(three, "c", 3),
    ]
    enc_attend_w = [(a, left, 0, cut), (b, right, 0, cut)]
    enc_feed_w = [(a, left, cut, QUAD), (b, right, cut + 1, QUAD)]
    enc_kept = attend_forward(source_pair, None, 0, source, None, enc_attend_w, False)
    enc_mid, small = enc_kept[7], enc_kept[8]
    enc_feed_kept = feed_forward(small, 5, HIDDEN_ROW, enc_mid, enc_feed_w)
    memory = enc_feed_kept[0]
    self_w, cross_w = grown((self_w, cross_w), tie(*more[:2], memory)[:2])
    (three,) = grown([three], tie(more[2], self_w, cross_w)[:1])
    target, self_w, cross_w, three = tie(target, self_w, cross_w, three)
    self_w, cross_w = net.finish(self_w, "a"), net.finish(cross_w, "b")
    three, self_w[1] = tie(three, self_w[1])
    three = net.finish(three, "c")
    self_w = [(a, self_w, 0, QUAD)]
    cross_w = [(b, cross_w, 0, QUAD)]
    self_kept = attend_forward(target_pair, small, 8, target, None, self_w, True)
    dec_one = self_kept[7]
    cross_kept = attend_forward(cross_pair, small, 13, dec_one, memory, cross_w, False)
    dec_two = cross_kept[7]
    dec_feed_w = [(net.table("c"), three, 0, QUAD), (net.table("d"), three, QUAD, QUAD)]
    result, two_grad, dec_feed_small, feed_two = feed_both(
        (a, b), small, 18, HIDDEN_ROW + QUAD, dec_two, grad, dec_feed_w
    )

    names = ("a", "b")
    feed_two = core_hop(net, feed_two, (QUAD, QUAD)).split(names)
    one_grad, memory_grad, cross_small, cross_q = attend_backward(
        (a, b), cross_pair, small, 13, two_grad, cross_kept, dec_one, memory, cross_w, False, None
    )
    send = Round(feed_two, cross_small)
    memory_grad, *cross_q = send.before(memory_grad, *cross_q)
    send.go()
    cross_s = core_hop(net, cross_q, (cut, cut)).split(names)
    mid_grad, enc_feed_small, feed_one = feed_backward(
        (a, b), small, 5, memory_grad, enc_feed_kept, enc_mid, enc_feed_w
    )
    send = Round(feed_two + cross_s, enc_feed_small)
    one_grad, *feed_one = send.before(one_grad, *feed_one)
    send.go()
    feed_one = core_hop(net, feed_one, (QUAD, QUAD)).split(names)
    target_grad, _, self_small, self_q = attend_backward(
        (a, b), target_pair, small, 8, one_grad, self_kept, target, None, self_w, True, None
    )
    send = Round(feed_two + cross_s + feed_one, self_small)
    mid_grad, *self_q = send.before(mid_grad, *self_q)
    send.go()
    self_s = core_hop(net, self_q, (cut, cut)).split(names)
    others = (enc_feed_small, self_small, cross_small, dec_feed_small)
    source_grad, _, _, enc_q = attend_backward(
        (a, b), source_pair, small, 0, mid_grad, enc_kept, source, None, enc_attend_w, False, others
    )
    send = Round(feed_two + cross_s + feed_one + self_s, source_grad)
    enc_q = send.before(*enc_q)
    last = send.go()
    enc_s = core_hop(net, enc_q, (cut, cut + 1)).split(names)
    while enc_s[0].blocks > 1:
        send = Round([item for item in cross_s + feed_one + self_s + enc_s if item.blocks > 1], *last)
        last = send.go()

    square = [(0, index) for index in range(3 * QUAD)]
    tall, deep = [], []
    for layer in range(2):
        for index in range(QUAD):
            lanes = slice(index * source.shape[1], (index + 1) * source.shape[1])
            tall.append((1, (layer, slice(None), lanes)))
            deep.append((2, (layer, slice(index * BLOCK, (index + 1) * BLOCK))))
    targets = [square[:cut], square[cut:QUAD] + [(3, None)]]
    targets += [square[QUAD : QUAD + cut], square[QUAD + cut : 2 * QUAD], tall[:QUAD], deep[:QUAD]]
    targets += [tall[QUAD:], deep[QUAD:]]
    targets += [square[2 * QUAD : 2 * QUAD + cut], square[2 * QUAD + cut :]]
    segments = [item.segments[0] for item in enc_s + self_s + feed_one + feed_two + cross_s]
    segments = [segment + (target,) for segment, target in zip(segments, targets)]
    updated = last_update(at, segments[2:], segments[:2], masters, firsts, seconds)
    return (memory, result, source_grad, target_grad), updated


def whole_step(pairs, source, target, grad, masters, firsts, seconds, axis_sizes):
    attention, up, down = [master.astype(BF) for master in masters[:3]]
    vectors, hidden = masters[3:]
    source_pair, target_pair, cross_pair = pairs
    small = gather_small(vectors, hidden)
    quads = gather_whole(attention, up, down)
    table = jnp.arange(source.shape[1] // BLOCK, dtype=jnp.int32)
    two = (table, table)
    parts = [(table, list(quad), 0, QUAD) for quad in quads]
    enc_kept = attend_forward(source_pair, small, 0, source, None, parts[:1], False)
    enc_mid = enc_kept[7]
    enc_feed_kept = feed_forward(small, 5, HIDDEN_ROW, enc_mid, parts[1:3])
    memory = enc_feed_kept[0]
    self_kept = attend_forward(target_pair, small, 8, target, None, parts[3:4], True)
    dec_one = self_kept[7]
    cross_kept = attend_forward(cross_pair, small, 13, dec_one, memory, parts[4:5], False)
    dec_two = cross_kept[7]
    result, two_grad, dec_feed_small, feed_two = feed_both(
        two, small, 18, HIDDEN_ROW + QUAD, dec_two, grad, parts[5:7]
    )
    one_grad, memory_grad, cross_small, cross_q = attend_backward(
        two, cross_pair, small, 13, two_grad, cross_kept, dec_one, memory, parts[4:5], False, None
    )
    target_grad, _, self_small, self_q = attend_backward(
        two, target_pair, small, 8, one_grad, self_kept, target, None, parts[3:4], True, None
    )
    mid_grad, enc_feed_small, feed_one = feed_backward(
        two, small, 5, memory_grad, enc_feed_kept, enc_mid, parts[1:3]
    )
    source_grad, _, enc_small, enc_q = attend_backward(
        two, source_pair, small, 0, mid_grad, enc_kept, source, None, parts[:1], False, None
    )
    quads = [enc_q]
    quads += [[half[:, low : low + QUAD] for half in feed_one] for low in (0, QUAD)]
    quads += [self_q, cross_q]
    quads += [[half[:, low : low + QUAD] for half in feed_two] for low in (0, QUAD)]
    smalls = (enc_small, enc_feed_small, self_small, cross_small, dec_feed_small)
    count = axis_sizes[0] * axis_sizes[1]
    shares = scatter_small(smalls, vectors, hidden, lax.axis_index(AXES), count)
    grads = tuple(scatter_whole(quads)) + shares
    updated = [
        adam_update(
            masters[slot], grads[slot], firsts[slot], seconds[slot], RATES[slot], DECAYS[slot]
        )
        for slot in range(5)
    ]
    flat = [updated[slot][kind] for kind in range(4) for slot in range(5)]
    return (memory, result, source_grad, target_grad), flat


def per_device(
    axis_sizes,
    source_tokens,
    target_tokens,
    source_segments,
    target_segments,
    output_grad,
    attention_weight,
    up_weight,
    down_weight,
    vectors,
    hidden_bias,
    *moments,
):
    masters = (attention_weight, up_weight, down_weight, vectors, hidden_bias)
    firsts = moments[:5]
    seconds = moments[5:]
    width = source_tokens.shape[2]
    pairs = (
        (source_segments, source_segments),
        (target_segments, target_segments),
        (target_segments, source_segments),
    )
    direct = axis_sizes[0] * axis_sizes[1] * BLOCK == width
    tokens, updated = (direct_step if direct else whole_step)(
        pairs,
        source_tokens[0],
        target_tokens[0],
        output_grad[0],
        masters,
        firsts,
        seconds,
        axis_sizes,
    )
    return tuple(array[None] for array in tokens) + tuple(updated)


def solution(mesh):
    rows = P(AXES, None, None)
    line = P(AXES, None)
    matrix = P(None, AXES, None)
    vector = P(None, AXES)
    state = (matrix, matrix, matrix, vector, vector)
    return jax.shard_map(
        functools.partial(per_device, (mesh.shape["dp"], mesh.shape["fsdp"])),
        mesh=mesh,
        in_specs=(rows, rows, line, line, rows) + state * 3,
        out_specs=(rows,) * 4 + state * 4,
        check_vma=False,
    )
```
